32 devices in a mesh: dp: 8 (over z, y), seq: 4 (over x, core).
Axes of the slice: x: 2, y: 2, z: 4, core: 2. Of those that a mesh axis runs over, the one named last changes fastest.
Arguments:
- long_input: bfloat16 [8, 2048, 768], P('dp', 'seq'), may hold values from -6 to 6
- global_input: bfloat16 [8, 230, 768], P('dp'), may hold values from -6 to 6
- lengths: int32 [8], P('dp'), may hold values from 1024 to 2048, as said below
- w_query: bfloat16 [768, 768], replicated, may hold values from -0.21875 to 0.21875
- b_query: float32 [768], replicated, may hold values from -1.25 to 1.25
- w_key: bfloat16 [768, 768], replicated, may hold values from -0.21875 to 0.21875
- w_value: bfloat16 [768, 768], replicated, may hold values from -0.21875 to 0.21875
- b_value: float32 [768], replicated, may hold values from -1.25 to 1.25
- w_out: bfloat16 [768, 768], replicated, may hold values from -6 to 6
- b_out: float32 [768], replicated, may hold values from -1.25 to 1.25
- w_inner: bfloat16 [768, 3072], replicated, may hold values from -0.21875 to 0.21875
- b_inner: float32 [3072], replicated, may hold values from -1.25 to 1.25
- w_outer: bfloat16 [3072, 768], replicated, may hold values from -0.109375 to 0.109375
- b_outer: float32 [768], replicated, may hold values from -1.25 to 1.25
- norm1_gain: float32 [768], replicated, may hold values from 0.5 to 1.5
- norm1_shift: float32 [768], replicated, may hold values from -1.25 to 1.25
- norm2_gain: float32 [768], replicated, may hold values from 0.5 to 1.5
- norm2_shift: float32 [768], replicated, may hold values from -1.25 to 1.25
- rel_table: float32 [169, 12], replicated, may hold values from -6 to 6
- long_cotangent: bfloat16 [8, 2048, 768], P('dp', 'seq'), may hold values from -6 to 6
- global_cotangent: bfloat16 [8, 230, 768], P('dp'), may hold values from -6 to 6
Outputs:
- long_output: bfloat16 [8, 2048, 768], P('dp', 'seq')
- global_output: bfloat16 [8, 230, 768], P('dp')
- long_grad: float32 [8, 2048, 768], P('dp', 'seq')
- global_grad: float32 [8, 230, 768], P('dp')
- grad_w_query: float32 [768, 768], P(('dp', 'seq'))
- grad_b_query: float32 [768], P(('dp', 'seq'))
- grad_w_key: float32 [768, 768], P(('dp', 'seq'))
- grad_w_value: float32 [768, 768], P(('dp', 'seq'))
- grad_b_value: float32 [768], P(('dp', 'seq'))
- grad_w_out: float32 [768, 768], P(('dp', 'seq'))
- grad_b_out: float32 [768], P(('dp', 'seq'))
- grad_w_inner: float32 [768, 3072], P(('dp', 'seq'))
- grad_b_inner: float32 [3072], P(('dp', 'seq'))
- grad_w_outer: float32 [3072, 768], P(('dp', 'seq'))
- grad_b_outer: float32 [768], P(('dp', 'seq'))
- grad_norm1_gain: float32 [768], P(('dp', 'seq'))
- grad_norm1_shift: float32 [768], P(('dp', 'seq'))
- grad_norm2_gain: float32 [768], P(('dp', 'seq'))
- grad_norm2_shift: float32 [768], P(('dp', 'seq'))
- grad_rel_table: float32 [169, 12], replicated
The draws below stay inside these ranges and needn't reach their ends.
Inputs may be any that keep to these rules, and one draw needn't show every extreme that they name: `lengths`: true long-token count of each document, whose long slots from it up to 2048 are padding; some document has all 2048 slots valid.
All inputs are finite; a program needn't handle non-finite values.
Results may differ from the reference program's by a relative error of at most 0.015.
Values may be sent and summed in bfloat16 or wider, within the bound.
A program may use at most 256 MiB of HBM per device.

```python
import jax
import jax.numpy as jnp
from jax import lax

D = 768
HEADS = 12
HD = 64
FF = 3072
R = 84
LABELS = 169
G = 230
QB = 512
BLK = 512
MINLEN = 1024
DOCS = 8
NL = 2048
N_SEQ = 4


def draw_lengths(key, part):
    key = jax.random.fold_in(key, 11)
    key_draw, key_pick = jax.random.split(key)
    sampled = jax.random.randint(key_draw, (DOCS,), MINLEN, N_SEQ * BLK + 1)
    chosen = jax.random.randint(key_pick, (), 0, DOCS)
    return jnp.where(jnp.arange(DOCS) == chosen, N_SEQ * BLK, sampled).astype(jnp.int32)


def levels(stream_key, shape, cuts, low, largest):
    level = 1.0
    for position, blocks in cuts:
        steps = jax.random.uniform(jax.random.fold_in(jax.random.fold_in(stream_key, 6), position), (blocks,), jnp.float32, low / len(cuts), largest / len(cuts))
        level = level * jnp.repeat(jnp.exp(steps), shape[position] // blocks).reshape((-1,) + (1,) * (len(shape) - 1 - position))
    return level


def gaussian(key, extent, spread, limit, shards=(), held_as=jnp.bfloat16):
    entries = jax.random.normal(key, extent, jnp.float32) * spread
    if len(shards) > 0:
        entries = levels(key, extent, shards, -0.22, 0.18) * entries
    return jnp.clip(entries, min=-limit, max=limit).astype(held_as)


def setup_inputs(seed: int = 0) -> dict:
    streams_of = jax.random.split(jax.random.key(seed), 22)
    long_input = gaussian(streams_of[0], (DOCS, NL, D), 1.0, 6.0, ((0, 8), (1, 4)))
    global_input = gaussian(streams_of[1], (DOCS, G, D), 1.0, 6.0, ((0, 8),))
    lengths = draw_lengths(jax.random.fold_in(streams_of[21], 71), 0)
    w_query = gaussian(streams_of[3], (D, D), D ** -0.5, 0.21875)
    b_query = gaussian(streams_of[4], (D,), 0.2, 1.25, (), jnp.float32)
    w_key = gaussian(streams_of[5], (D, D), D ** -0.5, 0.21875)
    w_value = gaussian(streams_of[6], (D, D), D ** -0.5, 0.21875)
    b_value = gaussian(streams_of[7], (D,), 0.2, 1.25, (), jnp.float32)
    w_out = gaussian(streams_of[8], (D, D), (max(1, D // (2 * R + 1 + G))) ** -0.5, 6.0)
    b_out = gaussian(streams_of[9], (D,), 0.2, 1.25, (), jnp.float32)
    w_inner = gaussian(streams_of[10], (D, FF), D ** -0.5, 0.21875)
    b_inner = gaussian(streams_of[11], (FF,), 0.2, 1.25, (), jnp.float32)
    w_outer = gaussian(streams_of[12], (FF, D), FF ** -0.5, 0.109375)
    b_outer = gaussian(streams_of[13], (D,), 0.2, 1.25, (), jnp.float32)
    norm1_gain = jnp.clip(1.0 + 0.1 * jax.random.normal(streams_of[14], (D,), jnp.float32), 0.5, 1.5)
    norm1_shift = gaussian(streams_of[15], (D,), 0.2, 1.25, (), jnp.float32)
    norm2_gain = jnp.clip(1.0 + 0.1 * jax.random.normal(streams_of[16], (D,), jnp.float32), 0.5, 1.5)
    norm2_shift = gaussian(streams_of[17], (D,), 0.2, 1.25, (), jnp.float32)
    rel_table = gaussian(streams_of[18], (LABELS, HEADS), 1.0, 6.0, (), jnp.float32)
    long_cotangent = gaussian(streams_of[19], (DOCS, NL, D), 1.0, 6.0, ((0, 8), (1, 4)))
    global_cotangent = gaussian(streams_of[20], (DOCS, G, D), 1.0, 6.0, ((0, 8),))
    return dict(long_input=long_input, global_input=global_input, lengths=lengths, w_query=w_query, b_query=b_query, w_key=w_key, w_value=w_value, b_value=b_value, w_out=w_out, b_out=b_out, w_inner=w_inner, b_inner=b_inner, w_outer=w_outer, b_outer=b_outer, norm1_gain=norm1_gain, norm1_shift=norm1_shift, norm2_gain=norm2_gain, norm2_shift=norm2_shift, rel_table=rel_table, long_cotangent=long_cotangent, global_cotangent=global_cotangent)


EPSILON = 1e-05
MASKED = -1e+30
PRECISE = lax.Precision.HIGHEST

@jax.custom_vjp
def low(v):
    return lax.optimization_barrier(v.astype(jnp.bfloat16)).astype(jnp.float32)

@jax.custom_vjp
def low_back(v):
    return v

def low_keep(v):
    return (low(v), None)

def low_pass(kept, grad):
    return (grad,)

def back_keep(v):
    return (v, None)

def back_low(kept, grad):
    return (low(grad),)
low.defvjp(low_keep, low_pass)
low_back.defvjp(back_keep, back_low)

def norm_apply(values, gain, shift):
    average = lax.optimization_barrier(jnp.mean(values, -1, keepdims=True))
    centred = values - average
    variance = lax.optimization_barrier(jnp.mean(centred * centred, -1, keepdims=True))
    return centred * lax.rsqrt(variance + EPSILON) * gain + shift

def matmul(left, right):
    return jnp.dot(left, right, precision=PRECISE)

def split_heads(matrix):
    return matrix.reshape(matrix.shape[0], -1, HD)

def scores_of(queries, keys):
    return jnp.einsum('qhd,khd->hqk', split_heads(queries), split_heads(keys), precision=PRECISE)

def apply_probs(probabilities, values):
    mixed_rows = jnp.einsum('hqk,khd->qhd', probabilities, split_heads(values), precision=PRECISE)
    return mixed_rows.reshape(mixed_rows.shape[0], -1)

def spread_diag(diag_values, width):
    row_count = diag_values.shape[-2]
    lead = [(0, 0)] * (diag_values.ndim - 1)
    padded = jnp.pad(diag_values, lead + [(0, width + 1 - diag_values.shape[-1])])
    flattened = padded.reshape(diag_values.shape[:-2] + (row_count * (width + 1),))
    return flattened[..., :row_count * width].reshape(diag_values.shape[:-2] + (row_count, width))

def smooth_gate(values):
    return jax.nn.gelu(values, approximate=True)

def document(weights, long_x, glob_x, doc_len):
    w_query, b_query, w_key, w_value, b_value, w_out, b_out, w_inner, b_inner, w_outer, b_outer, gain_one, shift_one, gain_two, shift_two, table = weights
    long_len = long_x.shape[0]
    score_scale = HD ** (-0.5)
    whole_x = jnp.concatenate([long_x, glob_x], 0)
    normed = low(norm_apply(whole_x, gain_one, shift_one))
    queries = low(low_back(matmul(normed, w_query) + b_query))
    keys = low(low_back(matmul(normed, w_key)))
    values = low(low_back(matmul(normed, w_value) + b_value))
    long_q, glob_q = (queries[:long_len], queries[long_len:])
    long_k, glob_k = (keys[:long_len], keys[long_len:])
    long_v, glob_v = (values[:long_len], values[long_len:])
    positions = jnp.arange(long_len, dtype=jnp.int32)
    row_valid = positions < doc_len
    ext_key = jnp.pad(long_k, ((R, R), (0, 0)))
    ext_value = jnp.pad(long_v, ((R, R), (0, 0)))
    key_pos = jnp.arange(long_len + 2 * R, dtype=jnp.int32) - R
    key_valid = (key_pos >= 0) & (key_pos < doc_len)
    label_count = 2 * R + 1
    window = QB + 2 * R
    head_count = table.shape[1]
    band_bias = spread_diag(jnp.broadcast_to(table.T[:, None, :], (head_count, QB, label_count)), window)
    band_mask = spread_diag(jnp.ones((QB, label_count), jnp.float32), window) > 0.5

    def block_fn(block_index):
        row_start = block_index * QB
        query_blk = lax.dynamic_slice_in_dim(long_q, row_start, QB)
        key_win = lax.dynamic_slice_in_dim(ext_key, row_start, window)
        value_win = lax.dynamic_slice_in_dim(ext_value, row_start, window)
        valid_win = lax.dynamic_slice_in_dim(key_valid, row_start, window)
        keep_mask = band_mask[None] & valid_win[None, None, :]
        band_scores = jnp.where(keep_mask, low_back(score_scale * scores_of(query_blk, key_win)) + band_bias, MASKED)
        glob_scores = low_back(score_scale * scores_of(query_blk, glob_k))
        row_max = jnp.maximum(lax.optimization_barrier(jnp.max(band_scores, -1)), lax.optimization_barrier(jnp.max(glob_scores, -1)))
        band_exp = jnp.where(keep_mask, jnp.exp(band_scores - row_max[..., None]), 0.0)
        glob_exp = jnp.exp(glob_scores - row_max[..., None])
        denominator = lax.optimization_barrier(jnp.sum(band_exp, -1)) + lax.optimization_barrier(jnp.sum(glob_exp, -1))
        return apply_probs(low(band_exp / denominator[..., None]), value_win) + apply_probs(low(glob_exp / denominator[..., None]), glob_v)
    block_count = long_len // QB
    long_attn = lax.map(jax.checkpoint(block_fn), jnp.arange(block_count, dtype=jnp.int32))
    long_attn = long_attn.reshape(long_len, -1)
    far_scores = jnp.where(row_valid[None, None, :], low_back(score_scale * scores_of(glob_q, long_k)), MASKED)
    near_scores = low_back(score_scale * scores_of(glob_q, glob_k))
    row_max = jnp.maximum(lax.optimization_barrier(jnp.max(far_scores, -1)), lax.optimization_barrier(jnp.max(near_scores, -1)))
    far_exp = jnp.where(row_valid[None, None, :], jnp.exp(far_scores - row_max[..., None]), 0.0)
    near_exp = jnp.exp(near_scores - row_max[..., None])
    denominator = lax.optimization_barrier(jnp.sum(far_exp, -1)) + lax.optimization_barrier(jnp.sum(near_exp, -1))
    glob_attn = apply_probs(low(far_exp / denominator[..., None]), long_v) + apply_probs(low(near_exp / denominator[..., None]), glob_v)
    attention = low(low_back(jnp.concatenate([long_attn, glob_attn], 0)))
    residual_mid = whole_x + low_back(matmul(attention, w_out)) + b_out
    normed_two = low(norm_apply(residual_mid, gain_two, shift_two))
    hidden_pre = low_back(matmul(normed_two, w_inner)) + b_inner
    activated = low(smooth_gate(hidden_pre))
    result = residual_mid + low_back(matmul(activated, w_outer)) + b_outer
    long_result = jnp.where(row_valid[:, None], result[:long_len], 0.0)
    return (long_result, result[long_len:])

def reference(long_input, global_input, lengths, w_query, b_query, w_key, w_value, b_value, w_out, b_out, w_inner, b_inner, w_outer, b_outer, norm1_gain, norm1_shift, norm2_gain, norm2_shift, rel_table, long_cotangent, global_cotangent):
    params = tuple((member.astype(jnp.float32) for member in (w_query, b_query, w_key, w_value, b_value, w_out, b_out, w_inner, b_inner, w_outer, b_outer, norm1_gain, norm1_shift, norm2_gain, norm2_shift, rel_table)))

    def forward(long_all, glob_all, *weights):

        def per_doc(pieces):
            long_x, glob_x, doc_len = pieces
            return document(weights, long_x, glob_x, doc_len)
        return lax.map(jax.checkpoint(per_doc), (long_all, glob_all, lengths))
    outputs, pullback = jax.vjp(forward, long_input.astype(jnp.float32), global_input.astype(jnp.float32), *params)
    grads = pullback((long_cotangent.astype(jnp.float32), global_cotangent.astype(jnp.float32)))
    return (outputs[0].astype(jnp.bfloat16), outputs[1].astype(jnp.bfloat16), grads[0], grads[1], grads[2], grads[3], grads[4], grads[5], grads[6], grads[7], grads[8], grads[9], grads[10], grads[11], grads[12], grads[13], grads[14], grads[15], grads[16], grads[17])
```

```python
import functools

import jax
import jax.numpy as jnp
from jax import lax
from jax.experimental import pallas as pl
from jax.experimental.pallas import tpu as pltpu
from jax.sharding import PartitionSpec as P

HD = 64
R = 84
HALO = 128
GP = 256
SUB = 128
EPSILON = 1e-05
MASKED = -1e30
F32 = jnp.float32
BF16 = jnp.bfloat16


def norm_forward(values, gain, shift):
    average = jnp.mean(values, -1, keepdims=True)
    centred = values - average
    variance = jnp.mean(centred * centred, -1, keepdims=True)
    inverse = lax.rsqrt(variance + EPSILON)
    normed = centred * inverse
    return (normed * gain + shift, normed, inverse)


def norm_backward(grad_rows, normed, inverse, gain):
    scaled = grad_rows * gain
    grad_in = inverse * (
        scaled
        - jnp.mean(scaled, -1, keepdims=True)
        - normed * jnp.mean(scaled * normed, -1, keepdims=True)
    )
    return (grad_in, jnp.sum(grad_rows * normed, 0), jnp.sum(grad_rows, 0))


def smooth_gate(values):
    return jax.nn.gelu(values, approximate=True)


def dot_t(left, right):
    return lax.dot_general(left, right, (((1,), (1,)), ((), ())), preferred_element_type=F32)


def dot_n(left, right):
    return lax.dot_general(left, right, (((1,), (0,)), ((), ())), preferred_element_type=F32)


def t_dot(left, right):
    return lax.dot_general(left, right, (((0,), (0,)), ((), ())), preferred_element_type=F32)


def band_bias(table_row, rows, width):
    spread = jnp.broadcast_to(table_row, (rows, width))
    return pltpu.roll(spread, 0, 1, stride=1, stride_axis=0)


def diagonal_sums(rows):
    height, width = rows.shape
    while height > 8:
        height //= 2
        rows = rows[:height] + pltpu.roll(rows[height:], width - height, 1)
    row = lax.broadcasted_iota(jnp.int32, rows.shape, 0)
    for bit in (1, 2, 4):
        rows = jnp.where((row & bit) != 0, pltpu.roll(rows, width - bit, 1), rows)
    return jnp.sum(rows, 0, keepdims=True)


def valid_bias(meta_ref, block, start, width):
    doc_len, seq_index = meta_ref[0], meta_ref[1]
    key_pos = (
        seq_index * block - HALO + start + lax.broadcasted_iota(jnp.int32, (1, width), 1)
    )
    return jnp.where((key_pos >= 0) & (key_pos < doc_len), 0.0, MASKED)


def glob_bias(first, width, count):
    return jnp.where(
        first + lax.broadcasted_iota(jnp.int32, (1, width), 1) < count, 0.0, MASKED
    )


def attend_kernel(dims, meta_ref, tab_ref, q_ref, kx_ref, vx_ref, kg_ref, vg_ref, o_ref, l_ref):
    block, count, quarter = dims
    window = SUB + 2 * HALO
    low_lanes = lax.broadcasted_iota(jnp.int32, (1, 2 * HD), 1) < HD
    scale = HD ** (-0.5)
    kg, vg = kg_ref[...], vg_ref[...]
    every_glob = glob_bias(0, GP, count)
    biases = [band_bias(tab_ref[0, head : head + 1], SUB, window) for head in range(2)]

    def own_half(head, value):
        lanes = low_lanes if head == 0 else ~low_lanes
        return jnp.where(lanes, value, jnp.zeros_like(value))

    for sub in range(block // SUB):
        rows = slice(sub * SUB, (sub + 1) * SUB)
        keys = slice(sub * SUB, sub * SUB + window)
        valid = valid_bias(meta_ref, block, sub * SUB, window)
        query = q_ref[rows] * jnp.asarray(scale, BF16)
        outs = []
        for head in range(2):
            own = own_half(head, query)
            band = dot_t(own, kx_ref[keys]) + (biases[head] + valid)
            glob = dot_t(own, kg) + every_glob
            top = jnp.maximum(
                jnp.max(band, -1, keepdims=True), jnp.max(glob, -1, keepdims=True)
            )
            band_exp = jnp.exp(band - top)
            glob_exp = jnp.exp(glob - top)
            total = jnp.sum(band_exp, -1, keepdims=True) + jnp.sum(glob_exp, -1, keepdims=True)
            mixed = dot_n(band_exp.astype(BF16), vx_ref[keys]) + dot_n(glob_exp.astype(BF16), vg)
            outs.append(mixed / total)
            l_ref[0, rows, head : head + 1] = top + jnp.log(total)
        o_ref[rows] = jnp.where(low_lanes, outs[0], outs[1]).astype(BF16)

    first = meta_ref[1] * quarter
    own_rows = pl.ds(pl.multiple_of(first, quarter), quarter)
    kq, vq = kg_ref[own_rows], vg_ref[own_rows]
    own_keys = slice(HALO, HALO + block)
    valid = valid_bias(meta_ref, block, HALO, block)
    some_glob = glob_bias(first, quarter, count)
    rows = slice(block, block + GP)
    query = q_ref[rows] * jnp.asarray(scale, BF16)
    outs = []
    for head in range(2):
        own = own_half(head, query)
        far = dot_t(own, kx_ref[own_keys]) + valid
        near = dot_t(own, kq) + some_glob
        top = jnp.maximum(jnp.max(far, -1, keepdims=True), jnp.max(near, -1, keepdims=True))
        far_exp = jnp.exp(far - top)
        near_exp = jnp.exp(near - top)
        total = jnp.sum(far_exp, -1, keepdims=True) + jnp.sum(near_exp, -1, keepdims=True)
        mixed = dot_n(far_exp.astype(BF16), vx_ref[own_keys]) + dot_n(near_exp.astype(BF16), vq)
        outs.append(mixed / total)
        l_ref[0, rows, head : head + 1] = top + jnp.log(total)
    o_ref[rows] = jnp.where(low_lanes, outs[0], outs[1]).astype(BF16)


def attend_back_kernel(
    dims,
    meta_ref,
    tab_ref,
    q_ref,
    kx_ref,
    vx_ref,
    kg_ref,
    vg_ref,
    o_ref,
    do_ref,
    dog_ref,
    l_ref,
    lg_ref,
    dq_ref,
    dkx_ref,
    dvx_ref,
    dkg_ref,
    dvg_ref,
    dtab_ref,
    dkg_acc,
    dvg_acc,
):
    block, count, quarter = dims
    window = SUB + 2 * HALO
    low_lanes = lax.broadcasted_iota(jnp.int32, (1, 2 * HD), 1) < HD
    scale = HD ** (-0.5)
    kg, vg = kg_ref[...], vg_ref[...]
    every_glob = glob_bias(0, GP, count)
    biases = [band_bias(tab_ref[0, head : head + 1], SUB, window) for head in range(2)]

    def own_half(head, value):
        lanes = low_lanes if head == 0 else ~low_lanes
        return jnp.where(lanes, value, jnp.zeros_like(value))

    first = meta_ref[1] * quarter
    own_rows = pl.ds(pl.multiple_of(first, quarter), quarter)
    own_keys = slice(HALO, HALO + block)

    dkx_ref[...] = jnp.zeros_like(dkx_ref)
    dvx_ref[...] = jnp.zeros_like(dvx_ref)
    dkg_acc[...] = jnp.zeros_like(dkg_acc)
    dvg_acc[...] = jnp.zeros_like(dvg_acc)
    kq, vq = kg_ref[own_rows], vg_ref[own_rows]
    valid = valid_bias(meta_ref, block, HALO, block)
    some_glob = glob_bias(first, quarter, count)
    query = q_ref[block:] * jnp.asarray(scale, BF16)
    grad_o = dog_ref[...]
    outs, kept = [], []
    for head in range(2):
        own, dog = own_half(head, query), own_half(head, grad_o)
        norm = lg_ref[0, :, head : head + 1]
        delta = lg_ref[0, :, 2 + head : 3 + head]
        far = jnp.exp(dot_t(own, kx_ref[own_keys]) + valid - norm)
        near = jnp.exp(dot_t(own, kq) + some_glob - norm)
        far_ds = (far * (dot_t(dog, vx_ref[own_keys]) - delta)).astype(BF16)
        near_ds = (near * (dot_t(dog, vq) - delta)).astype(BF16)
        outs.append(dot_n(far_ds, kx_ref[own_keys]) + dot_n(near_ds, kq))
        kept.append((own, dog, far.astype(BF16), near.astype(BF16), far_ds, near_ds))
    own, dog, far, near, far_ds, near_ds = (jnp.concatenate(pair, 0) for pair in zip(*kept))
    dq_ref[block:] = (jnp.where(low_lanes, outs[0], outs[1]) * scale).astype(BF16)
    dkx_ref[own_keys] = t_dot(far_ds, own)
    dvx_ref[own_keys] = t_dot(far, dog)
    dkg_acc[own_rows] = t_dot(near_ds, own)
    dvg_acc[own_rows] = t_dot(near, dog)

    table_sum = [jnp.zeros((SUB, window), F32) for _ in range(2)]
    for sub in range(block // SUB):
        rows = slice(sub * SUB, (sub + 1) * SUB)
        keys = slice(sub * SUB, sub * SUB + window)
        valid = valid_bias(meta_ref, block, sub * SUB, window)
        query = q_ref[rows] * jnp.asarray(scale, BF16)
        grad_o = do_ref[rows]
        both = grad_o.astype(F32) * o_ref[rows].astype(F32)
        outs, kept = [], []
        for head in range(2):
            own, dol = own_half(head, query), own_half(head, grad_o)
            norm = l_ref[0, rows, head : head + 1]
            delta = jnp.sum(own_half(head, both), -1, keepdims=True)
            band = jnp.exp(dot_t(own, kx_ref[keys]) + (biases[head] + valid) - norm)
            glob = jnp.exp(dot_t(own, kg) + every_glob - norm)
            band_ds = band * (dot_t(dol, vx_ref[keys]) - delta)
            table_sum[head] += band_ds
            band_ds = band_ds.astype(BF16)
            glob_ds = (glob * (dot_t(dol, vg) - delta)).astype(BF16)
            outs.append(dot_n(band_ds, kx_ref[keys]) + dot_n(glob_ds, kg))
            kept.append((own, dol, band.astype(BF16), glob.astype(BF16), band_ds, glob_ds))
        own, dol, band, glob, band_ds, glob_ds = (
            jnp.concatenate(pair, 0) for pair in zip(*kept)
        )
        dq_ref[rows] = (jnp.where(low_lanes, outs[0], outs[1]) * scale).astype(BF16)
        dkx_ref[keys] += t_dot(band_ds, own)
        dvx_ref[keys] += t_dot(band, dol)
        dkg_acc[...] += t_dot(glob_ds, own)
        dvg_acc[...] += t_dot(glob, dol)
    dkg_ref[...] = dkg_acc[...].astype(BF16)
    dvg_ref[...] = dvg_acc[...].astype(BF16)
    for head in range(2):
        dtab_ref[0, head : head + 1] = diagonal_sums(table_sum[head])


def columns(rows):
    return pl.BlockSpec((rows, 2 * HD), lambda pair: (0, pair))


def per_pair(*dims):
    return pl.BlockSpec((1,) + dims, lambda pair: (pair,) + (0,) * len(dims))


def attend(dims, meta, table, q, kx, vx, kg, vg):
    block = dims[0]
    pairs, width = table.shape[0], q.shape[1]
    window = table.shape[2]
    ext = block + 2 * HALO
    return pl.pallas_call(
        functools.partial(attend_kernel, dims),
        grid=(pairs,),
        in_specs=[
            pl.BlockSpec(memory_space=pltpu.SMEM),
            per_pair(2, window),
            columns(block + GP),
            columns(ext),
            columns(ext),
            columns(GP),
            columns(GP),
        ],
        out_specs=[columns(block + GP), per_pair(block + GP, 2)],
        out_shape=[
            jax.ShapeDtypeStruct((block + GP, width), BF16),
            jax.ShapeDtypeStruct((pairs, block + GP, 2), F32),
        ],
        compiler_params=pltpu.CompilerParams(vmem_limit_bytes=48 * 2**20),
        name="attend",
    )(meta, table, q, kx, vx, kg, vg)


def attend_back(dims, meta, table, q, kx, vx, kg, vg, o, do, dog, l, lg):
    block = dims[0]
    pairs, width = table.shape[0], q.shape[1]
    window = table.shape[2]
    ext = block + 2 * HALO
    return pl.pallas_call(
        functools.partial(attend_back_kernel, dims),
        grid=(pairs,),
        in_specs=[
            pl.BlockSpec(memory_space=pltpu.SMEM),
            per_pair(2, window),
            columns(block + GP),
            columns(ext),
            columns(ext),
            columns(GP),
            columns(GP),
            columns(block),
            columns(block),
            columns(GP),
            per_pair(block, 2),
            per_pair(GP, 4),
        ],
        out_specs=[
            columns(block + GP),
            columns(ext),
            columns(ext),
            columns(GP),
            columns(GP),
            per_pair(2, window),
        ],
        out_shape=[
            jax.ShapeDtypeStruct((block + GP, width), BF16),
            jax.ShapeDtypeStruct((ext, width), F32),
            jax.ShapeDtypeStruct((ext, width), F32),
            jax.ShapeDtypeStruct((GP, width), BF16),
            jax.ShapeDtypeStruct((GP, width), BF16),
            jax.ShapeDtypeStruct((pairs, 2, window), F32),
        ],
        scratch_shapes=[pltpu.VMEM((GP, 2 * HD), F32), pltpu.VMEM((GP, 2 * HD), F32)],
        compiler_params=pltpu.CompilerParams(vmem_limit_bytes=48 * 2**20),
        name="attend_back",
    )(meta, table, q, kx, vx, kg, vg, o, do, dog, l, lg)


def passed_along(value, axis, steps):
    count = lax.axis_size(axis)
    first, last = (max(0, -steps), min(count, count - steps))
    return lax.ppermute(value, axis, [(source, source + steps) for source in range(first, last)])


def matmul(left, right):
    return jnp.dot(left, right, preferred_element_type=F32)


def rows_dot(left, right):
    return jnp.einsum("rd,re->de", left, right, preferred_element_type=F32)


def back_dot(left, right):
    return lax.dot_general(left, right, (((1,), (1,)), ((), ())), preferred_element_type=F32)


def on_device(
    long_input,
    global_input,
    lengths,
    w_query,
    b_query,
    w_key,
    w_value,
    b_value,
    w_out,
    b_out,
    w_inner,
    b_inner,
    w_outer,
    b_outer,
    norm1_gain,
    norm1_shift,
    norm2_gain,
    norm2_shift,
    rel_table,
    long_cotangent,
    global_cotangent,
):
    seq_count = lax.axis_size("seq")
    data_count = lax.axis_size("dp")
    seq_index = lax.axis_index("seq")
    block = long_input.shape[1]
    count = global_input.shape[1]
    width = long_input.shape[2]
    heads = rel_table.shape[1]
    pairs = heads // 2
    labels = 2 * R + 1
    quarter = GP // seq_count
    dims = (block, count, quarter)
    doc_len = lengths[0]
    row_valid = (seq_index * block + jnp.arange(block, dtype=jnp.int32)) < doc_len
    meta = jnp.stack([doc_len, seq_index]).astype(jnp.int32)
    window = SUB + 2 * HALO
    table = jnp.pad(
        rel_table.T,
        ((0, 0), (HALO - R, window - labels - HALO + R)),
        constant_values=MASKED,
    ).reshape(pairs, 2, window)

    glob_x = jnp.pad(global_input[0], ((0, GP - count), (0, 0)))
    glob_dy = jnp.pad(global_cotangent[0], ((0, GP - count), (0, 0)))
    own_glob = lambda a: lax.dynamic_slice_in_dim(a, seq_index * quarter, quarter, 0)
    all_x = jnp.concatenate([long_input[0], glob_x], 0).astype(F32)
    own_x = jnp.concatenate([long_input[0], own_glob(glob_x)], 0).astype(F32)
    normed = norm_forward(all_x, norm1_gain, norm1_shift)[0].astype(BF16)
    keys = matmul(normed, w_key).astype(BF16)
    values = (matmul(normed, w_value) + b_value).astype(BF16)
    queries = (matmul(normed, w_query) + b_query).astype(BF16)

    def extended(rows):
        below = passed_along(rows[block - HALO : block], "seq", 1)
        above = passed_along(rows[:HALO], "seq", -1)
        return jnp.concatenate([below, rows[:block], above], 0)

    kx, vx = extended(keys), extended(values)
    kg, vg = keys[block:], values[block:]
    attended, norms = attend(dims, meta, table, queries, kx, vx, kg, vg)

    def to_owner(part):
        return lax.all_to_all(
            part.reshape(seq_count, quarter, -1), "seq", split_axis=0, concat_axis=0, tiled=True
        )

    part_o = to_owner(attended[block:]).astype(F32).reshape(seq_count, quarter, heads, HD)
    part_l = to_owner(norms[:, block:].transpose(1, 0, 2).reshape(GP, heads))
    top = jnp.max(part_l, 0)
    glob_l = top + jnp.log(jnp.sum(jnp.exp(part_l - top), 0))
    glob_o = jnp.sum(part_o * jnp.exp(part_l - glob_l)[..., None], 0).reshape(quarter, width)
    attn_low = jnp.concatenate([attended[:block], glob_o.astype(BF16)], 0)

    residual_mid = own_x + matmul(attn_low, w_out) + b_out
    normed_two, hat_two, inv_two = norm_forward(residual_mid, norm2_gain, norm2_shift)
    normed_two_low = normed_two.astype(BF16)
    hidden_pre = matmul(normed_two_low, w_inner) + b_inner
    activated, gelu_back = jax.vjp(smooth_gate, hidden_pre)
    activated_low = activated.astype(BF16)
    result = residual_mid + matmul(activated_low, w_outer) + b_outer
    long_result = jnp.where(row_valid[:, None], result[:block], 0.0).astype(BF16)
    grad_y_low = jnp.concatenate(
        [
            jnp.where(row_valid[:, None], long_cotangent[0], jnp.zeros_like(long_cotangent[0])),
            own_glob(glob_dy),
        ],
        0,
    )
    grad_y = grad_y_low.astype(F32)
    grad_b_outer = jnp.sum(grad_y, 0)
    grad_w_outer = rows_dot(activated_low, grad_y_low)
    (grad_hidden,) = gelu_back(back_dot(grad_y_low, w_outer))
    grad_b_inner = jnp.sum(grad_hidden, 0)
    hidden_low = grad_hidden.astype(BF16)
    grad_w_inner = rows_dot(normed_two_low, hidden_low)
    grad_from_two, grad_gain_two, grad_shift_two = norm_backward(
        back_dot(hidden_low, w_inner), hat_two, inv_two, norm2_gain
    )
    grad_mid = grad_y + grad_from_two
    grad_b_out = jnp.sum(grad_mid, 0)
    grad_mid_low = grad_mid.astype(BF16)
    grad_w_out = rows_dot(attn_low, grad_mid_low)
    grad_attn = back_dot(grad_mid_low, w_out).astype(BF16)

    glob_do = grad_attn[block:]
    glob_delta = jnp.sum((glob_do.astype(F32) * glob_o).reshape(quarter, heads, HD), -1)
    every_do = lax.all_gather(glob_do, "seq", axis=0, tiled=True)
    every_ld = lax.all_gather(
        jnp.concatenate(
            [glob_l.reshape(quarter, pairs, 2), glob_delta.reshape(quarter, pairs, 2)], -1
        ),
        "seq",
        axis=0,
        tiled=True,
    ).transpose(1, 0, 2)
    dq, dkx, dvx, dkg, dvg, dtab = attend_back(
        dims,
        meta,
        table,
        queries,
        kx,
        vx,
        kg,
        vg,
        attended[:block],
        grad_attn[:block],
        every_do,
        norms[:, :block],
        every_ld,
    )
    glob_sum = lax.psum_scatter(
        jnp.concatenate([dq[block:], dkg, dvg], 1), "seq", scatter_dimension=0, tiled=True
    )

    def joined(ext):
        from_above = passed_along(ext[:HALO].astype(BF16), "seq", -1).astype(F32)
        from_below = passed_along(ext[HALO + block :].astype(BF16), "seq", 1).astype(F32)
        own = ext[HALO : HALO + block]
        return jnp.concatenate(
            [
                own[:HALO] + from_below,
                own[HALO : block - HALO],
                own[block - HALO :] + from_above,
            ],
            0,
        ).astype(BF16)

    query_low = jnp.concatenate([dq[:block], glob_sum[:, :width]], 0)
    key_low = jnp.concatenate([joined(dkx), glob_sum[:, width : 2 * width]], 0)
    value_low = jnp.concatenate([joined(dvx), glob_sum[:, 2 * width :]], 0)
    own_normed, hat_one, inv_one = norm_forward(own_x, norm1_gain, norm1_shift)
    own_normed = own_normed.astype(BF16)
    grad_b_query = jnp.sum(query_low.astype(F32), 0)
    grad_b_value = jnp.sum(value_low.astype(F32), 0)
    grad_w_query = rows_dot(own_normed, query_low)
    grad_w_key = rows_dot(own_normed, key_low)
    grad_w_value = rows_dot(own_normed, value_low)
    grad_normed_one = (
        back_dot(query_low, w_query) + back_dot(key_low, w_key) + back_dot(value_low, w_value)
    )
    grad_from_one, grad_gain_one, grad_shift_one = norm_backward(
        grad_normed_one, hat_one, inv_one, norm1_gain
    )
    grad_x = grad_mid + grad_from_one

    def summed(part):
        return lax.psum_scatter(
            part.astype(BF16), ("dp", "seq"), scatter_dimension=0, tiled=True
        ).astype(F32)

    devices = data_count * seq_count
    piece = width // devices
    vectors = (
        grad_b_query,
        grad_b_value,
        grad_b_out,
        grad_b_inner,
        grad_b_outer,
        grad_gain_one,
        grad_shift_one,
        grad_gain_two,
        grad_shift_two,
    )
    small = summed(jnp.concatenate([v.reshape(devices, -1) for v in vectors], 1))[0]
    pieces, at = [], 0
    for vector in vectors:
        length = vector.shape[0] // devices
        pieces.append(small[at : at + length])
        at += length
    g_b_query, g_b_value, g_b_out, g_b_inner, g_b_outer, g_g1, g_s1, g_g2, g_s2 = pieces
    turned = dtab.reshape(heads, window)[:, HALO - R : HALO - R + labels]
    table_total = lax.psum(turned.T, ("dp", "seq"))
    glob_out = lax.all_gather(result[block:].astype(BF16), "seq", axis=0, tiled=True)[:count]
    glob_grad = lax.all_gather(grad_x[block:], "seq", axis=0, tiled=True)[:count]
    return (
        long_result[None],
        glob_out[None],
        grad_x[:block][None],
        glob_grad[None],
        summed(grad_w_query),
        g_b_query,
        summed(grad_w_key),
        summed(grad_w_value),
        g_b_value,
        summed(grad_w_out),
        g_b_out,
        summed(grad_w_inner),
        g_b_inner,
        summed(grad_w_outer),
        g_b_outer,
        g_g1,
        g_s1,
        g_g2,
        g_s2,
        table_total,
    )


def solution(mesh):
    rows, whole = P("dp", "seq", None), P("dp", None, None)
    matrix, vector = P(("dp", "seq"), None), P(("dp", "seq"))
    return jax.shard_map(
        on_device,
        mesh=mesh,
        in_specs=(rows, whole, P("dp")) + (P(),) * 16 + (rows, whole),
        out_specs=(
            rows,
            whole,
            rows,
            whole,
            matrix,
            vector,
            matrix,
            matrix,
            vector,
            matrix,
            vector,
            matrix,
            vector,
            matrix,
            vector,
            vector,
            vector,
            vector,
            vector,
            P(),
        ),
        check_vma=False,
    )
```

```python
import functools

import jax
import jax.numpy as jnp
from jax import lax
from jax.experimental import pallas as pl
from jax.experimental.pallas import tpu as pltpu
from jax.sharding import PartitionSpec as P

HD = 64
R = 84
HALO = 128
GP = 256
SUB = 128
EPSILON = 1e-05
MASKED = -1e30
F32 = jnp.float32
BF16 = jnp.bfloat16


def norm_forward(values, gain, shift):
    average = jnp.mean(values, -1, keepdims=True)
    centred = values - average
    variance = jnp.mean(centred * centred, -1, keepdims=True)
    inverse = lax.rsqrt(variance + EPSILON)
    normed = centred * inverse
    return (normed * gain + shift, normed, inverse)


def norm_backward(grad_rows, normed, inverse, gain):
    scaled = grad_rows * gain
    grad_in = inverse * (
        scaled
        - jnp.mean(scaled, -1, keepdims=True)
        - normed * jnp.mean(scaled * normed, -1, keepdims=True)
    )
    return (grad_in, jnp.sum(grad_rows * normed, 0), jnp.sum(grad_rows, 0))


def smooth_gate(values):
    return jax.nn.gelu(values, approximate=True)


def dot_t(left, right):
    return lax.dot_general(left, right, (((1,), (1,)), ((), ())), preferred_element_type=F32)


def dot_n(left, right):
    return lax.dot_general(left, right, (((1,), (0,)), ((), ())), preferred_element_type=F32)


def t_dot(left, right):
    return lax.dot_general(left, right, (((0,), (0,)), ((), ())), preferred_element_type=F32)


def band_bias(table_row, rows, width):
    spread = jnp.broadcast_to(table_row, (rows, width))
    return pltpu.roll(spread, 0, 1, stride=1, stride_axis=0)


def diagonal_sums(rows):
    height, width = rows.shape
    while height > 8:
        height //= 2
        rows = rows[:height] + pltpu.roll(rows[height:], width - height, 1)
    row = lax.broadcasted_iota(jnp.int32, rows.shape, 0)
    for bit in (1, 2, 4):
        rows = jnp.where((row & bit) != 0, pltpu.roll(rows, width - bit, 1), rows)
    return jnp.sum(rows, 0, keepdims=True)


def valid_bias(meta_ref, block, start, width):
    doc_len, seq_index = meta_ref[0], meta_ref[1]
    key_pos = (
        seq_index * block - HALO + start + lax.broadcasted_iota(jnp.int32, (1, width), 1)
    )
    return jnp.where((key_pos >= 0) & (key_pos < doc_len), 0.0, MASKED)


def glob_bias(first, width, count):
    return jnp.where(
        first + lax.broadcasted_iota(jnp.int32, (1, width), 1) < count, 0.0, MASKED
    )


def attend_kernel(dims, meta_ref, tab_ref, q_ref, kx_ref, vx_ref, kg_ref, vg_ref, o_ref, l_ref):
    block, count, quarter = dims
    window = SUB + 2 * HALO
    low_lanes = lax.broadcasted_iota(jnp.int32, (1, 2 * HD), 1) < HD
    scale = HD ** (-0.5)
    kg, vg = kg_ref[...], vg_ref[...]
    every_glob = glob_bias(0, GP, count)
    biases = [band_bias(tab_ref[0, head : head + 1], SUB, window) for head in range(2)]

    def own_half(head, value):
        lanes = low_lanes if head == 0 else ~low_lanes
        return jnp.where(lanes, value, jnp.zeros_like(value))

    for sub in range(block // SUB):
        rows = slice(sub * SUB, (sub + 1) * SUB)
        keys = slice(sub * SUB, sub * SUB + window)
        valid = valid_bias(meta_ref, block, sub * SUB, window)
        query = q_ref[rows] * jnp.asarray(scale, BF16)
        outs = []
        for head in range(2):
            own = own_half(head, query)
            band = dot_t(own, kx_ref[keys]) + (biases[head] + valid)
            glob = dot_t(own, kg) + every_glob
            top = jnp.maximum(
                jnp.max(band, -1, keepdims=True), jnp.max(glob, -1, keepdims=True)
            )
            band_exp = jnp.exp(band - top)
            glob_exp = jnp.exp(glob - top)
            total = jnp.sum(band_exp, -1, keepdims=True) + jnp.sum(glob_exp, -1, keepdims=True)
            mixed = dot_n(band_exp.astype(BF16), vx_ref[keys]) + dot_n(glob_exp.astype(BF16), vg)
            outs.append(mixed / total)
            l_ref[0, rows, head : head + 1] = top + jnp.log(total)
        o_ref[rows] = jnp.where(low_lanes, outs[0], outs[1]).astype(BF16)

    first = meta_ref[1] * quarter
    own_rows = pl.ds(pl.multiple_of(first, quarter), quarter)
    kq, vq = kg_ref[own_rows], vg_ref[own_rows]
    own_keys = slice(HALO, HALO + block)
    valid = valid_bias(meta_ref, block, HALO, block)
    some_glob = glob_bias(first, quarter, count)
    rows = slice(block, block + GP)
    query = q_ref[rows] * jnp.asarray(scale, BF16)
    outs = []
    for head in range(2):
        own = own_half(head, query)
        far = dot_t(own, kx_ref[own_keys]) + valid
        near = dot_t(own, kq) + some_glob
        top = jnp.maximum(jnp.max(far, -1, keepdims=True), jnp.max(near, -1, keepdims=True))
        far_exp = jnp.exp(far - top)
        near_exp = jnp.exp(near - top)
        total = jnp.sum(far_exp, -1, keepdims=True) + jnp.sum(near_exp, -1, keepdims=True)
        mixed = dot_n(far_exp.astype(BF16), vx_ref[own_keys]) + dot_n(near_exp.astype(BF16), vq)
        outs.append(mixed / total)
        l_ref[0, rows, head : head + 1] = top + jnp.log(total)
    o_ref[rows] = jnp.where(low_lanes, outs[0], outs[1]).astype(BF16)


def attend_back_kernel(
    dims,
    meta_ref,
    tab_ref,
    q_ref,
    kx_ref,
    vx_ref,
    kg_ref,
    vg_ref,
    o_ref,
    do_ref,
    dog_ref,
    l_ref,
    lg_ref,
    dq_ref,
    dkx_ref,
    dvx_ref,
    dkg_ref,
    dvg_ref,
    dtab_ref,
    dkg_acc,
    dvg_acc,
):
    block, count, quarter = dims
    window = SUB + 2 * HALO
    low_lanes = lax.broadcasted_iota(jnp.int32, (1, 2 * HD), 1) < HD
    scale = HD ** (-0.5)
    kg, vg = kg_ref[...], vg_ref[...]
    every_glob = glob_bias(0, GP, count)
    biases = [band_bias(tab_ref[0, head : head + 1], SUB, window) for head in range(2)]

    def own_half(head, value):
        lanes = low_lanes if head == 0 else ~low_lanes
        return jnp.where(lanes, value, jnp.zeros_like(value))

    first = meta_ref[1] * quarter
    own_rows = pl.ds(pl.multiple_of(first, quarter), quarter)
    own_keys = slice(HALO, HALO + block)

    dkx_ref[...] = jnp.zeros_like(dkx_ref)
    dvx_ref[...] = jnp.zeros_like(dvx_ref)
    dkg_acc[...] = jnp.zeros_like(dkg_acc)
    dvg_acc[...] = jnp.zeros_like(dvg_acc)
    kq, vq = kg_ref[own_rows], vg_ref[own_rows]
    valid = valid_bias(meta_ref, block, HALO, block)
    some_glob = glob_bias(first, quarter, count)
    query = q_ref[block:] * jnp.asarray(scale, BF16)
    grad_o = dog_ref[...]
    outs, kept = [], []
    for head in range(2):
        own, dog = own_half(head, query), own_half(head, grad_o)
        norm = lg_ref[0, :, head : head + 1]
        delta = lg_ref[0, :, 2 + head : 3 + head]
        far = jnp.exp(dot_t(own, kx_ref[own_keys]) + valid - norm)
        near = jnp.exp(dot_t(own, kq) + some_glob - norm)
        far_ds = (far * (dot_t(dog, vx_ref[own_keys]) - delta)).astype(BF16)
        near_ds = (near * (dot_t(dog, vq) - delta)).astype(BF16)
        outs.append(dot_n(far_ds, kx_ref[own_keys]) + dot_n(near_ds, kq))
        kept.append((own, dog, far.astype(BF16), near.astype(BF16), far_ds, near_ds))
    own, dog, far, near, far_ds, near_ds = (jnp.concatenate(pair, 0) for pair in zip(*kept))
    dq_ref[block:] = (jnp.where(low_lanes, outs[0], outs[1]) * scale).astype(BF16)
    dkx_ref[own_keys] = t_dot(far_ds, own)
    dvx_ref[own_keys] = t_dot(far, dog)
    dkg_acc[own_rows] = t_dot(near_ds, own)
    dvg_acc[own_rows] = t_dot(near, dog)

    table_sum = [jnp.zeros((SUB, window), F32) for _ in range(2)]
    for sub in range(block // SUB):
        rows = slice(sub * SUB, (sub + 1) * SUB)
        keys = slice(sub * SUB, sub * SUB + window)
        valid = valid_bias(meta_ref, block, sub * SUB, window)
        query = q_ref[rows] * jnp.asarray(scale, BF16)
        grad_o = do_ref[rows]
        both = grad_o.astype(F32) * o_ref[rows].astype(F32)
        outs, kept = [], []
        for head in range(2):
            own, dol = own_half(head, query), own_half(head, grad_o)
            norm = l_ref[0, rows, head : head + 1]
            delta = jnp.sum(own_half(head, both), -1, keepdims=True)
            band = jnp.exp(dot_t(own, kx_ref[keys]) + (biases[head] + valid) - norm)
            glob = jnp.exp(dot_t(own, kg) + every_glob - norm)
            band_ds = band * (dot_t(dol, vx_ref[keys]) - delta)
            table_sum[head] += band_ds
            band_ds = band_ds.astype(BF16)
            glob_ds = (glob * (dot_t(dol, vg) - delta)).astype(BF16)
            outs.append(dot_n(band_ds, kx_ref[keys]) + dot_n(glob_ds, kg))
            kept.append((own, dol, band.astype(BF16), glob.astype(BF16), band_ds, glob_ds))
        own, dol, band, glob, band_ds, glob_ds = (
            jnp.concatenate(pair, 0) for pair in zip(*kept)
        )
        dq_ref[rows] = (jnp.where(low_lanes, outs[0], outs[1]) * scale).astype(BF16)
        dkx_ref[keys] += t_dot(band_ds, own)
        dvx_ref[keys] += t_dot(band, dol)
        dkg_acc[...] += t_dot(glob_ds, own)
        dvg_acc[...] += t_dot(glob, dol)
    dkg_ref[...] = dkg_acc[...].astype(BF16)
    dvg_ref[...] = dvg_acc[...].astype(BF16)
    for head in range(2):
        dtab_ref[0, head : head + 1] = diagonal_sums(table_sum[head])


def columns(rows):
    return pl.BlockSpec((rows, 2 * HD), lambda pair: (0, pair))


def per_pair(*dims):
    return pl.BlockSpec((1,) + dims, lambda pair: (pair,) + (0,) * len(dims))


def attend(dims, meta, table, q, kx, vx, kg, vg):
    block = dims[0]
    pairs, width = table.shape[0], q.shape[1]
    window = table.shape[2]
    ext = block + 2 * HALO
    return pl.pallas_call(
        functools.partial(attend_kernel, dims),
        grid=(pairs,),
        in_specs=[
            pl.BlockSpec(memory_space=pltpu.SMEM),
            per_pair(2, window),
            columns(block + GP),
            columns(ext),
            columns(ext),
            columns(GP),
            columns(GP),
        ],
        out_specs=[columns(block + GP), per_pair(block + GP, 2)],
        out_shape=[
            jax.ShapeDtypeStruct((block + GP, width), BF16),
            jax.ShapeDtypeStruct((pairs, block + GP, 2), F32),
        ],
        compiler_params=pltpu.CompilerParams(vmem_limit_bytes=48 * 2**20),
        name="attend",
    )(meta, table, q, kx, vx, kg, vg)


def attend_back(dims, meta, table, q, kx, vx, kg, vg, o, do, dog, l, lg):
    block = dims[0]
    pairs, width = table.shape[0], q.shape[1]
    window = table.shape[2]
    ext = block + 2 * HALO
    return pl.pallas_call(
        functools.partial(attend_back_kernel, dims),
        grid=(pairs,),
        in_specs=[
            pl.BlockSpec(memory_space=pltpu.SMEM),
            per_pair(2, window),
            columns(block + GP),
            columns(ext),
            columns(ext),
            columns(GP),
            columns(GP),
            columns(block),
            columns(block),
            columns(GP),
            per_pair(block, 2),
            per_pair(GP, 4),
        ],
        out_specs=[
            columns(block + GP),
            columns(ext),
            columns(ext),
            columns(GP),
            columns(GP),
            per_pair(2, window),
        ],
        out_shape=[
            jax.ShapeDtypeStruct((block + GP, width), BF16),
            jax.ShapeDtypeStruct((ext, width), F32),
            jax.ShapeDtypeStruct((ext, width), F32),
            jax.ShapeDtypeStruct((GP, width), BF16),
            jax.ShapeDtypeStruct((GP, width), BF16),
            jax.ShapeDtypeStruct((pairs, 2, window), F32),
        ],
        scratch_shapes=[pltpu.VMEM((GP, 2 * HD), F32), pltpu.VMEM((GP, 2 * HD), F32)],
        compiler_params=pltpu.CompilerParams(vmem_limit_bytes=48 * 2**20),
        name="attend_back",
    )(meta, table, q, kx, vx, kg, vg, o, do, dog, l, lg)


class Reducer:
    SCRATCH = 4

    def __init__(self, mesh_ids, rows, pieces, mine, from_core, from_one, from_two, from_z, sems):
        self.ids = mesh_ids
        half = (rows // 2 + 15) // 16 * 16
        self.halves = (slice(0, half), slice(half, rows))
        self.pieces, self.mine = pieces, mine
        self.from_core, self.from_one, self.from_two, self.from_z = (
            from_core,
            from_one,
            from_two,
            from_z,
        )
        self.local, self.sends, self.recvs = sems

    @staticmethod
    def scratch(rows, width):
        half = (rows // 2 + 15) // 16 * 16
        return [
            pltpu.VMEM((4, 2, 2, rows, width), BF16),
            pltpu.VMEM((4, 2, 2, rows, width), BF16),
            pltpu.VMEM((4, 2, rows, width), BF16),
            pltpu.VMEM((4, rows, width), BF16),
            pltpu.VMEM((3, rows, width), BF16),
            pltpu.SemaphoreType.DMA((4,)),
            pltpu.SemaphoreType.DMA((6, 4)),
            pltpu.SemaphoreType.DMA((6, 4)),
        ]

    def partners(self):
        z, y, x, core = self.ids
        dp, seq = z * 2 + y, x * 2 + core
        near = [(dp, x * 2 + 1 - core), (dp, (1 - x) * 2 + core), (z * 2 + 1 - y, seq)]
        return near + [(lax.rem(z + step, 4) * 2 + y, seq) for step in (1, 2, 3)]

    def target(self, chunk):
        return lax.rem(self.ids[0] + 1 + chunk, 4)

    def remote(self, source, dest, kind, chunk, partner):
        return pltpu.make_async_remote_copy(
            src_ref=source,
            dst_ref=dest,
            send_sem=self.sends.at[kind, chunk],
            recv_sem=self.recvs.at[kind, chunk],
            device_id=self.partners()[partner],
            device_id_type=pl.DeviceIdType.MESH,
        )

    def own_copy(self, chunk):
        z, y, x, core = self.ids
        to = self.target(chunk)
        return pltpu.make_async_copy(
            self.pieces.at[core, to], self.mine.at[to], self.local.at[chunk]
        )

    def core_copy(self, chunk):
        z, y, x, core = self.ids
        to = self.target(chunk)
        return self.remote(self.pieces.at[1 - core, to], self.from_core.at[to], 0, chunk, 0)

    def first_copies(self, chunk):
        z, y, x, core = self.ids
        to = self.target(chunk)
        one, two = self.halves
        return (
            self.remote(
                self.mine.at[to, :, 1 - x, one], self.from_one.at[to, :, one], 1, chunk, 1
            ),
            self.remote(
                self.mine.at[to, 1 - y, :, two], self.from_one.at[to, :, two], 2, chunk, 2
            ),
        )

    def second_copies(self, chunk):
        z, y, x, core = self.ids
        to = self.target(chunk)
        one, two = self.halves
        return (
            self.remote(
                self.mine.at[to, 1 - y, x, one], self.from_two.at[to, one], 3, chunk, 2
            ),
            self.remote(
                self.mine.at[to, y, 1 - x, two], self.from_two.at[to, two], 4, chunk, 1
            ),
        )

    def last_copy(self, chunk):
        z, y, x, core = self.ids
        return self.remote(
            self.mine.at[self.target(chunk), y, x], self.from_z.at[chunk], 5, chunk, 3 + chunk
        )

    def start(self):
        for chunk in range(4):
            self.core_copy(chunk).start()
            self.own_copy(chunk).start()

    def step(self, number):
        z, y, x, core = self.ids
        one, two = self.halves
        chunk = number
        if 0 <= chunk < 4:
            to = self.target(chunk)
            self.own_copy(chunk).wait()
            self.core_copy(chunk).wait_recv()

            def add(index, carry):
                at = (to, lax.div(index, 2), lax.rem(index, 2))
                self.mine[at] = (
                    self.mine[at].astype(F32) + self.from_core[at].astype(F32)
                ).astype(BF16)
                return carry

            lax.fori_loop(0, 4, add, 0)
            for copy in self.first_copies(chunk):
                copy.start()
        chunk = number - 1
        if 0 <= chunk < 4:
            to = self.target(chunk)
            for copy in self.first_copies(chunk):
                copy.wait_recv()

            def add(index, carry):
                for at, rows in (((to, index, x), one), ((to, y, index), two)):
                    self.mine[at + (rows,)] = (
                        self.mine[at + (rows,)].astype(F32)
                        + self.from_one[to, index, rows].astype(F32)
                    ).astype(BF16)
                return carry

            lax.fori_loop(0, 2, add, 0)
            for copy in self.second_copies(chunk):
                copy.start()
        chunk = number - 2
        if 0 <= chunk < 4:
            to = self.target(chunk)
            for copy in self.second_copies(chunk):
                copy.wait_recv()
            if chunk < 3:
                self.mine[to, y, x] = (
                    self.mine[to, y, x].astype(F32) + self.from_two[to].astype(F32)
                ).astype(BF16)
                self.last_copy(chunk).start()

    def finish(self, out):
        z, y, x, core = self.ids
        total = self.mine[z, y, x].astype(F32) + self.from_two[z].astype(F32)
        for chunk in range(3):
            self.last_copy(chunk).wait_recv()
            total += self.from_z[chunk].astype(F32)
        out[...] = total
        for chunk in range(4):
            self.core_copy(chunk).wait_send()
            for copy in self.first_copies(chunk) + self.second_copies(chunk):
                copy.wait_send()
            if chunk < 3:
                self.last_copy(chunk).wait_send()

    STEPS = 6


def mesh_ids():
    dp, seq = lax.axis_index("dp"), lax.axis_index("seq")
    return lax.div(dp, 2), lax.rem(dp, 2), lax.div(seq, 2), lax.rem(seq, 2)


def meet(devices):
    barrier = pltpu.get_barrier_semaphore()
    for device in devices:
        pl.semaphore_signal(barrier, inc=1, device_id=device, device_id_type=pl.DeviceIdType.MESH)
    pl.semaphore_wait(barrier, len(devices))


def reduce_kernel(rows, pieces_ref, out_ref, *scratch):
    reducer = Reducer(mesh_ids(), rows, pieces_ref, *scratch[:5], scratch[5:])
    meet(reducer.partners())
    reducer.start()
    for number in range(Reducer.STEPS):
        reducer.step(number)
    reducer.finish(out_ref)


def reduce_pieces(pieces, collective_id):
    rows, width = pieces.shape[-2:]
    return pl.pallas_call(
        functools.partial(reduce_kernel, rows),
        in_specs=[pl.BlockSpec(memory_space=pl.ANY)],
        out_specs=pl.BlockSpec(memory_space=pltpu.VMEM),
        out_shape=jax.ShapeDtypeStruct((rows, width), F32),
        scratch_shapes=Reducer.scratch(rows, width),
        compiler_params=pltpu.CompilerParams(
            collective_id=collective_id, has_side_effects=True, vmem_limit_bytes=40 * 2**20
        ),
        name="reduce_pieces",
    )(pieces)


def summed_over_devices(parts, width, collective_id):
    data_count, seq_count = lax.axis_size("dp"), lax.axis_size("seq")
    if (data_count, seq_count) != (8, 4):
        return lax.psum_scatter(
            parts.astype(BF16), ("dp", "seq"), scatter_dimension=0, tiled=True
        )[0].astype(F32)
    rows = parts.shape[1]
    ordered = parts.reshape(4, 2, 2, 2, rows, width).transpose(3, 0, 1, 2, 4, 5)
    return reduce_pieces(ordered.astype(BF16), collective_id)


def passed_along(value, axis, steps):
    count = lax.axis_size(axis)
    first, last = (max(0, -steps), min(count, count - steps))
    return lax.ppermute(value, axis, [(source, source + steps) for source in range(first, last)])


def matmul(left, right):
    return jnp.dot(left, right, preferred_element_type=F32)


def rows_dot(left, right):
    return jnp.einsum("rd,re->de", left, right, preferred_element_type=F32)


def back_dot(left, right):
    return lax.dot_general(left, right, (((1,), (1,)), ((), ())), preferred_element_type=F32)


def on_device(
    long_input,
    global_input,
    lengths,
    w_query,
    b_query,
    w_key,
    w_value,
    b_value,
    w_out,
    b_out,
    w_inner,
    b_inner,
    w_outer,
    b_outer,
    norm1_gain,
    norm1_shift,
    norm2_gain,
    norm2_shift,
    rel_table,
    long_cotangent,
    global_cotangent,
):
    seq_count = lax.axis_size("seq")
    data_count = lax.axis_size("dp")
    seq_index = lax.axis_index("seq")
    block = long_input.shape[1]
    count = global_input.shape[1]
    width = long_input.shape[2]
    heads = rel_table.shape[1]
    pairs = heads // 2
    labels = 2 * R + 1
    quarter = GP // seq_count
    dims = (block, count, quarter)
    doc_len = lengths[0]
    row_valid = (seq_index * block + jnp.arange(block, dtype=jnp.int32)) < doc_len
    meta = jnp.stack([doc_len, seq_index]).astype(jnp.int32)
    window = SUB + 2 * HALO
    table = jnp.pad(
        rel_table.T,
        ((0, 0), (HALO - R, window - labels - HALO + R)),
        constant_values=MASKED,
    ).reshape(pairs, 2, window)

    glob_x = jnp.pad(global_input[0], ((0, GP - count), (0, 0)))
    glob_dy = jnp.pad(global_cotangent[0], ((0, GP - count), (0, 0)))
    own_glob = lambda a: lax.dynamic_slice_in_dim(a, seq_index * quarter, quarter, 0)
    all_x = jnp.concatenate([long_input[0], glob_x], 0).astype(F32)
    own_x = jnp.concatenate([long_input[0], own_glob(glob_x)], 0).astype(F32)
    normed = norm_forward(all_x, norm1_gain, norm1_shift)[0].astype(BF16)
    keys = matmul(normed, w_key).astype(BF16)
    values = (matmul(normed, w_value) + b_value).astype(BF16)
    queries = (matmul(normed, w_query) + b_query).astype(BF16)

    def extended(rows):
        below = passed_along(rows[block - HALO : block], "seq", 1)
        above = passed_along(rows[:HALO], "seq", -1)
        return jnp.concatenate([below, rows[:block], above], 0)

    kx, vx = extended(keys), extended(values)
    kg, vg = keys[block:], values[block:]
    attended, norms = attend(dims, meta, table, queries, kx, vx, kg, vg)

    def to_owner(part):
        return lax.all_to_all(
            part.reshape(seq_count, quarter, -1), "seq", split_axis=0, concat_axis=0, tiled=True
        )

    part_o = to_owner(attended[block:]).astype(F32).reshape(seq_count, quarter, heads, HD)
    part_l = to_owner(norms[:, block:].transpose(1, 0, 2).reshape(GP, heads))
    top = jnp.max(part_l, 0)
    glob_l = top + jnp.log(jnp.sum(jnp.exp(part_l - top), 0))
    glob_o = jnp.sum(part_o * jnp.exp(part_l - glob_l)[..., None], 0).reshape(quarter, width)
    attn_low = jnp.concatenate([attended[:block], glob_o.astype(BF16)], 0)

    residual_mid = own_x + matmul(attn_low, w_out) + b_out
    normed_two, hat_two, inv_two = norm_forward(residual_mid, norm2_gain, norm2_shift)
    normed_two_low = normed_two.astype(BF16)
    hidden_pre = matmul(normed_two_low, w_inner) + b_inner
    activated, gelu_back = jax.vjp(smooth_gate, hidden_pre)
    activated_low = activated.astype(BF16)
    result = residual_mid + matmul(activated_low, w_outer) + b_outer
    long_result = jnp.where(row_valid[:, None], result[:block], 0.0).astype(BF16)
    grad_y_low = jnp.concatenate(
        [
            jnp.where(row_valid[:, None], long_cotangent[0], jnp.zeros_like(long_cotangent[0])),
            own_glob(glob_dy),
        ],
        0,
    )
    grad_y = grad_y_low.astype(F32)
    grad_b_outer = jnp.sum(grad_y, 0)
    grad_w_outer = rows_dot(activated_low, grad_y_low)
    (grad_hidden,) = gelu_back(back_dot(grad_y_low, w_outer))
    grad_b_inner = jnp.sum(grad_hidden, 0)
    hidden_low = grad_hidden.astype(BF16)
    grad_w_inner = rows_dot(normed_two_low, hidden_low)
    grad_from_two, grad_gain_two, grad_shift_two = norm_backward(
        back_dot(hidden_low, w_inner), hat_two, inv_two, norm2_gain
    )
    grad_mid = grad_y + grad_from_two
    grad_b_out = jnp.sum(grad_mid, 0)
    grad_mid_low = grad_mid.astype(BF16)
    grad_w_out = rows_dot(attn_low, grad_mid_low)
    grad_attn = back_dot(grad_mid_low, w_out).astype(BF16)

    glob_do = grad_attn[block:]
    glob_delta = jnp.sum((glob_do.astype(F32) * glob_o).reshape(quarter, heads, HD), -1)
    every_do = lax.all_gather(glob_do, "seq", axis=0, tiled=True)
    every_ld = lax.all_gather(
        jnp.concatenate(
            [glob_l.reshape(quarter, pairs, 2), glob_delta.reshape(quarter, pairs, 2)], -1
        ),
        "seq",
        axis=0,
        tiled=True,
    ).transpose(1, 0, 2)
    dq, dkx, dvx, dkg, dvg, dtab = attend_back(
        dims,
        meta,
        table,
        queries,
        kx,
        vx,
        kg,
        vg,
        attended[:block],
        grad_attn[:block],
        every_do,
        norms[:, :block],
        every_ld,
    )
    glob_sum = lax.psum_scatter(
        jnp.concatenate([dq[block:], dkg, dvg], 1), "seq", scatter_dimension=0, tiled=True
    )

    def joined(ext):
        from_above = passed_along(ext[:HALO].astype(BF16), "seq", -1).astype(F32)
        from_below = passed_along(ext[HALO + block :].astype(BF16), "seq", 1).astype(F32)
        own = ext[HALO : HALO + block]
        return jnp.concatenate(
            [
                own[:HALO] + from_below,
                own[HALO : block - HALO],
                own[block - HALO :] + from_above,
            ],
            0,
        ).astype(BF16)

    query_low = jnp.concatenate([dq[:block], glob_sum[:, :width]], 0)
    key_low = jnp.concatenate([joined(dkx), glob_sum[:, width : 2 * width]], 0)
    value_low = jnp.concatenate([joined(dvx), glob_sum[:, 2 * width :]], 0)
    own_normed, hat_one, inv_one = norm_forward(own_x, norm1_gain, norm1_shift)
    own_normed = own_normed.astype(BF16)
    grad_b_query = jnp.sum(query_low.astype(F32), 0)
    grad_b_value = jnp.sum(value_low.astype(F32), 0)
    grad_w_query = rows_dot(own_normed, query_low)
    grad_w_key = rows_dot(own_normed, key_low)
    grad_w_value = rows_dot(own_normed, value_low)
    grad_normed_one = (
        back_dot(query_low, w_query) + back_dot(key_low, w_key) + back_dot(value_low, w_value)
    )
    grad_from_one, grad_gain_one, grad_shift_one = norm_backward(
        grad_normed_one, hat_one, inv_one, norm1_gain
    )
    grad_x = grad_mid + grad_from_one

    devices = data_count * seq_count
    piece = width // devices
    by_device = lambda grad: grad.reshape(devices, -1, width)

    def wide(grad):
        blocks = grad.reshape(devices, piece, -1, width)
        return blocks.transpose(0, 2, 1, 3).reshape(devices, -1, width)

    inner_rows = wide(grad_w_inner).shape[1]
    early = summed_over_devices(
        jnp.concatenate([by_device(grad_w_outer), wide(grad_w_inner)], 1), width, 1
    )
    g_outer = early[:-inner_rows]
    g_inner = early[-inner_rows:].reshape(-1, piece, width).transpose(1, 0, 2)
    vectors = (
        grad_b_query,
        grad_b_value,
        grad_b_out,
        grad_b_inner,
        grad_b_outer,
        grad_gain_one,
        grad_shift_one,
        grad_gain_two,
        grad_shift_two,
    )
    small = jnp.concatenate([v.reshape(devices, -1) for v in vectors], 1)
    small = jnp.pad(small, ((0, 0), (0, width - small.shape[1])))
    small = jnp.pad(small[:, None], ((0, 0), (0, 15), (0, 0)))
    late = summed_over_devices(
        jnp.concatenate(
            [by_device(g) for g in (grad_w_query, grad_w_key, grad_w_value, grad_w_out)]
            + [small],
            1,
        ),
        width,
        2,
    )
    pieces, at = [], 0
    for vector in vectors:
        length = vector.shape[0] // devices
        pieces.append(late[4 * piece, at : at + length])
        at += length
    g_b_query, g_b_value, g_b_out, g_b_inner, g_b_outer, g_g1, g_s1, g_g2, g_s2 = pieces
    g_query, g_key, g_value, g_out = (late[i * piece : (i + 1) * piece] for i in range(4))
    turned = dtab.reshape(heads, window)[:, HALO - R : HALO - R + labels]
    table_total = lax.psum(turned.T, ("dp", "seq"))
    glob_out = lax.all_gather(result[block:].astype(BF16), "seq", axis=0, tiled=True)[:count]
    glob_grad = lax.all_gather(grad_x[block:], "seq", axis=0, tiled=True)[:count]
    return (
        long_result[None],
        glob_out[None],
        grad_x[:block][None],
        glob_grad[None],
        g_query,
        g_b_query,
        g_key,
        g_value,
        g_b_value,
        g_out,
        g_b_out,
        g_inner.reshape(piece, -1),
        g_b_inner,
        g_outer,
        g_b_outer,
        g_g1,
        g_s1,
        g_g2,
        g_s2,
        table_total,
    )


def solution(mesh):
    rows, whole = P("dp", "seq", None), P("dp", None, None)
    matrix, vector = P(("dp", "seq"), None), P(("dp", "seq"))
    return jax.shard_map(
        on_device,
        mesh=mesh,
        in_specs=(rows, whole, P("dp")) + (P(),) * 16 + (rows, whole),
        out_specs=(
            rows,
            whole,
            rows,
            whole,
            matrix,
            vector,
            matrix,
            matrix,
            vector,
            matrix,
            vector,
            matrix,
            vector,
            matrix,
            vector,
            vector,
            vector,
            vector,
            vector,
            P(),
        ),
        check_vma=False,
    )
```

```python
import functools
from typing import NamedTuple

import jax
import jax.numpy as jnp
from jax import lax
from jax.experimental import pallas as pl
from jax.experimental.pallas import tpu as pltpu
from jax.sharding import PartitionSpec as P

HD = 64
R = 84
PAIR = 2 * HD
HALO = 128
REACH = 96
GP = 256
SUB = 256
WINDOW = SUB + 2 * HALO
EPSILON = 1e-05
MASKED = -1e30
F32 = jnp.float32
BF16 = jnp.bfloat16


def norm_forward(values, gain, shift):
    average = jnp.mean(values, -1, keepdims=True)
    centred = values - average
    variance = jnp.mean(centred * centred, -1, keepdims=True)
    inverse = lax.rsqrt(variance + EPSILON)
    normed = centred * inverse
    return (normed * gain + shift, normed, inverse)


def norm_backward(grad_rows, normed, inverse, gain):
    scaled = grad_rows * gain
    grad_in = inverse * (
        scaled
        - jnp.mean(scaled, -1, keepdims=True)
        - normed * jnp.mean(scaled * normed, -1, keepdims=True)
    )
    return (grad_in, jnp.sum(grad_rows * normed, 0), jnp.sum(grad_rows, 0))


def smooth_gate(values):
    return jax.nn.gelu(values, approximate=True)


def dot_t(left, right):
    return lax.dot_general(left, right, (((1,), (1,)), ((), ())), preferred_element_type=F32)


def dot_n(left, right):
    return lax.dot_general(left, right, (((1,), (0,)), ((), ())), preferred_element_type=F32)


def t_dot(left, right):
    return lax.dot_general(left, right, (((0,), (0,)), ((), ())), preferred_element_type=F32)


def band_bias(table_row):
    spread = jnp.broadcast_to(table_row, (SUB, WINDOW))
    return pltpu.roll(spread, 0, 1, stride=1, stride_axis=0)


def diagonal_sums(rows):
    height, width = rows.shape
    while height > 8:
        height //= 2
        rows = rows[:height] + pltpu.roll(rows[height:], width - height, 1)
    row = lax.broadcasted_iota(jnp.int32, rows.shape, 0)
    for bit in (1, 2, 4):
        rows = jnp.where((row & bit) != 0, pltpu.roll(rows, width - bit, 1), rows)
    return jnp.sum(rows, 0, keepdims=True)


def lane_index():
    return lax.broadcasted_iota(jnp.int32, (1, PAIR), 1)


def own_half(head, value):
    low_lanes = lane_index() < HD
    return jnp.where(low_lanes if head == 0 else ~low_lanes, value, jnp.zeros_like(value))


def other_lane(head):
    return HD * (1 - head)


def with_lanes(head, value, columns):
    wide = own_half(head, value.astype(F32))
    lane = lane_index()
    for offset, column in enumerate(columns):
        wide = jnp.where(lane == other_lane(head) + offset, column, wide)
    return wide.astype(BF16)


def in_three(column):
    high = column.astype(BF16).astype(F32)
    middle = (column - high).astype(BF16).astype(F32)
    return (high, middle, column - high - middle)


def key_bias(first, rows, end):
    position = first + lax.broadcasted_iota(jnp.int32, (rows, 1), 0)
    return jnp.where((position >= 0) & (position < end), 0.0, MASKED)


def pick_column(rows, index):
    return jnp.sum(jnp.where(lane_index() == index, rows, 0.0), -1, keepdims=True)


def key_side(head, keys, bias):
    return with_lanes(head, keys, (bias, 1.0, 1.0, 1.0))


def value_side(head, values):
    return with_lanes(head, values, (1.0, 1.0, 1.0))


def softmax_rows(parts, value_parts, head):
    top = functools.reduce(
        jnp.maximum, [jnp.max(part, -1, keepdims=True) for part in parts]
    )
    mixed = sum(
        dot_n(jnp.exp(part - top).astype(BF16), values)
        for part, values in zip(parts, value_parts)
    )
    at = other_lane(head)
    total = mixed[:, at : at + 1]
    return mixed / total, top + jnp.log(total)


def attend_kernel(dims, meta_ref, tab_ref, q_ref, kx_ref, vx_ref, kg_ref, vg_ref, o_ref, l_ref):
    block, count, quarter = dims
    doc_len, seq_index = meta_ref[0], meta_ref[1]
    scale = jnp.asarray(HD ** (-0.5), BF16)
    long_bias = key_bias(seq_index * block - HALO, block + 2 * HALO, doc_len)
    glob_bias = key_bias(0, GP, count)
    own_rows = pl.ds(pl.multiple_of(seq_index * quarter, quarter), quarter)
    own_bias = key_bias(seq_index * quarter, quarter, count)
    own_keys = slice(HALO, HALO + block)
    query = q_ref[...] * scale
    outs, norms = [], []
    for head in range(2):
        q = with_lanes(head, query, (1.0,))
        kx = with_lanes(head, kx_ref[...], (long_bias,))
        kg = with_lanes(head, kg_ref[...], (glob_bias,))
        kq = with_lanes(head, kg_ref[own_rows], (own_bias,))
        vx, vg = (with_lanes(head, ref[...], (1.0,)) for ref in (vx_ref, vg_ref))
        vq = with_lanes(head, vg_ref[own_rows], (1.0,))
        bias = band_bias(tab_ref[0, head : head + 1])
        rows_out = []
        for start in range(0, block, SUB):
            rows, keys = slice(start, start + SUB), slice(start, start + WINDOW)
            rows_out.append(
                softmax_rows(
                    [dot_t(q[rows], kx[keys]) + bias, dot_t(q[rows], kg)], [vx[keys], vg], head
                )
            )
        rows_out.append(
            softmax_rows(
                [dot_t(q[block:], kx[own_keys]), dot_t(q[block:], kq)], [vx[own_keys], vq], head
            )
        )
        outs.append(jnp.concatenate([out for out, _ in rows_out], 0))
        norms.append(jnp.concatenate([norm for _, norm in rows_out], 0))
    low_lanes = lane_index() < HD
    o_ref[...] = jnp.where(low_lanes, outs[0], outs[1]).astype(BF16)
    for head in range(2):
        l_ref[0, :, head : head + 1] = norms[head]


def columns(rows):
    return pl.BlockSpec((rows, PAIR), lambda pair: (0, pair))


def per_pair(*dims):
    return pl.BlockSpec((1,) + dims, lambda pair: (pair,) + (0,) * len(dims))


def attend(dims, meta, table, q, kx, vx, kg, vg):
    block = dims[0]
    pairs, width = table.shape[0], q.shape[1]
    ext = block + 2 * HALO
    return pl.pallas_call(
        functools.partial(attend_kernel, dims),
        grid=(pairs,),
        in_specs=[
            pl.BlockSpec(memory_space=pltpu.SMEM),
            per_pair(2, WINDOW),
            columns(block + GP),
            columns(ext),
            columns(ext),
            columns(GP),
            columns(GP),
        ],
        out_specs=[columns(block + GP), per_pair(block + GP, 2)],
        out_shape=[
            jax.ShapeDtypeStruct((block + GP, width), BF16),
            jax.ShapeDtypeStruct((pairs, block + GP, 2), F32),
        ],
        compiler_params=pltpu.CompilerParams(vmem_limit_bytes=48 * 2**20),
        name="attend",
    )(meta, table, q, kx, vx, kg, vg)


class Reducer:
    def __init__(self, mesh_ids, rows, pieces, mine, from_core, from_one, from_two, from_z, sems):
        self.ids = mesh_ids
        half = (rows // 2 + 15) // 16 * 16
        self.halves = (slice(0, half), slice(half, rows))
        self.pieces, self.mine = pieces, mine
        self.from_core, self.from_one, self.from_two, self.from_z = (
            from_core,
            from_one,
            from_two,
            from_z,
        )
        self.local, self.sends, self.recvs = sems

    @staticmethod
    def scratch(rows, width):
        half = (rows // 2 + 15) // 16 * 16
        return [
            pltpu.VMEM((4, 2, 2, rows, width), BF16),
            pltpu.VMEM((4, 2, 2, rows, width), BF16),
            pltpu.VMEM((4, 2, rows, width), BF16),
            pltpu.VMEM((4, rows, width), BF16),
            pltpu.VMEM((3, rows, width), BF16),
            pltpu.SemaphoreType.DMA((4,)),
            pltpu.SemaphoreType.DMA((6, 4)),
            pltpu.SemaphoreType.DMA((6, 4)),
        ]

    def partners(self):
        z, y, x, core = self.ids
        dp, seq = z * 2 + y, x * 2 + core
        near = [(dp, x * 2 + 1 - core), (dp, (1 - x) * 2 + core), (z * 2 + 1 - y, seq)]
        return near + [(lax.rem(z + step, 4) * 2 + y, seq) for step in (1, 2, 3)]

    def target(self, chunk):
        return lax.rem(self.ids[0] + 1 + chunk, 4)

    def remote(self, source, dest, kind, chunk, partner):
        return pltpu.make_async_remote_copy(
            src_ref=source,
            dst_ref=dest,
            send_sem=self.sends.at[kind, chunk],
            recv_sem=self.recvs.at[kind, chunk],
            device_id=self.partners()[partner],
            device_id_type=pl.DeviceIdType.MESH,
        )

    def own_copy(self, chunk):
        z, y, x, core = self.ids
        to = self.target(chunk)
        return pltpu.make_async_copy(
            self.pieces.at[core, to], self.mine.at[to], self.local.at[chunk]
        )

    def core_copy(self, chunk):
        z, y, x, core = self.ids
        to = self.target(chunk)
        return self.remote(self.pieces.at[1 - core, to], self.from_core.at[to], 0, chunk, 0)

    def first_copies(self, chunk):
        z, y, x, core = self.ids
        to = self.target(chunk)
        one, two = self.halves
        return (
            self.remote(
                self.mine.at[to, :, 1 - x, one], self.from_one.at[to, :, one], 1, chunk, 1
            ),
            self.remote(
                self.mine.at[to, 1 - y, :, two], self.from_one.at[to, :, two], 2, chunk, 2
            ),
        )

    def second_copies(self, chunk):
        z, y, x, core = self.ids
        to = self.target(chunk)
        one, two = self.halves
        return (
            self.remote(
                self.mine.at[to, 1 - y, x, one], self.from_two.at[to, one], 3, chunk, 2
            ),
            self.remote(
                self.mine.at[to, y, 1 - x, two], self.from_two.at[to, two], 4, chunk, 1
            ),
        )

    def last_copy(self, chunk):
        z, y, x, core = self.ids
        return self.remote(
            self.mine.at[self.target(chunk), y, x], self.from_z.at[chunk], 5, chunk, 3 + chunk
        )

    def start(self):
        for chunk in range(4):
            self.core_copy(chunk).start()
            self.own_copy(chunk).start()

    def add_core(self, chunk):
        to = self.target(chunk)
        self.own_copy(chunk).wait()
        self.core_copy(chunk).wait_recv()

        def add(index, carry):
            at = (to, lax.div(index, 2), lax.rem(index, 2))
            self.mine[at] = (self.mine[at].astype(F32) + self.from_core[at].astype(F32)).astype(
                BF16
            )
            return carry

        lax.fori_loop(0, 4, add, 0)
        for copy in self.first_copies(chunk):
            copy.start()

    def add_first(self, chunk):
        z, y, x, core = self.ids
        one, two = self.halves
        to = self.target(chunk)
        for copy in self.first_copies(chunk):
            copy.wait_recv()

        def add(index, carry):
            for at, rows in (((to, index, x), one), ((to, y, index), two)):
                self.mine[at + (rows,)] = (
                    self.mine[at + (rows,)].astype(F32)
                    + self.from_one[to, index, rows].astype(F32)
                ).astype(BF16)
            return carry

        lax.fori_loop(0, 2, add, 0)
        for copy in self.second_copies(chunk):
            copy.start()

    def add_second(self, chunk):
        z, y, x, core = self.ids
        to = self.target(chunk)
        for copy in self.second_copies(chunk):
            copy.wait_recv()
        if chunk < 3:
            self.mine[to, y, x] = (
                self.mine[to, y, x].astype(F32) + self.from_two[to].astype(F32)
            ).astype(BF16)
            self.last_copy(chunk).start()

    def finish(self, out):
        z, y, x, core = self.ids
        total = self.mine[z, y, x].astype(F32) + self.from_two[z].astype(F32)
        for chunk in range(3):
            self.last_copy(chunk).wait_recv()
            total += self.from_z[chunk].astype(F32)
        out[...] = total
        for chunk in range(4):
            self.core_copy(chunk).wait_send()
            for copy in self.first_copies(chunk) + self.second_copies(chunk):
                copy.wait_send()
            if chunk < 3:
                self.last_copy(chunk).wait_send()


def mesh_ids():
    dp, seq = lax.axis_index("dp"), lax.axis_index("seq")
    return lax.div(dp, 2), lax.rem(dp, 2), lax.div(seq, 2), lax.rem(seq, 2)


def meet(devices):
    barrier = pltpu.get_barrier_semaphore()
    for device in devices:
        pl.semaphore_signal(barrier, inc=1, device_id=device, device_id_type=pl.DeviceIdType.MESH)
    pl.semaphore_wait(barrier, len(devices))


EARLY_PLAN = (
    (1, "add_core", 0),
    (2, "add_core", 1),
    (3, "add_core", 2),
    (4, "add_core", 3),
    (5, "add_first", 0),
    (8, "add_first", 1),
    (9, "add_second", 0),
    (11, "add_first", 2),
    (11, "add_second", 1),
    (11, "add_first", 3),
    (11, "add_second", 2),
    (11, "add_second", 3),
)
LATE_PLAN = (
    ("add_core", 0),
    ("add_core", 1),
    ("add_first", 0),
    ("add_core", 2),
    ("add_first", 1),
    ("add_second", 0),
    ("add_core", 3),
    ("add_first", 2),
    ("add_second", 1),
    ("add_first", 3),
    ("add_second", 2),
    ("add_second", 3),
)


def late_kernel(rows, pieces_ref, table_ref, out_ref, total_ref, *scratch):
    reducer = Reducer(mesh_ids(), rows, pieces_ref, *scratch[:5], scratch[5:8])
    kept, arrived, sends, recvs = scratch[8:]
    z, y, x, core = mesh_ids()
    dp, seq = lax.axis_index("dp"), lax.axis_index("seq")
    flip_low = z + 1 - 2 * lax.rem(z, 2)
    flip_high = lax.rem(z + 2, 4)
    partners = (
        (dp, x * 2 + 1 - core),
        (dp, (1 - x) * 2 + core),
        (z * 2 + 1 - y, seq),
        (flip_low * 2 + y, seq),
        (flip_high * 2 + y, seq),
    )

    def table_copy(stage):
        return pltpu.make_async_remote_copy(
            src_ref=kept.at[stage],
            dst_ref=arrived.at[stage],
            send_sem=sends.at[stage],
            recv_sem=recvs.at[stage],
            device_id=partners[stage],
            device_id_type=pl.DeviceIdType.MESH,
        )

    meet(reducer.partners())
    reducer.start()
    kept[0] = table_ref[...]
    table_copy(0).start()
    for number, (act, chunk) in enumerate(LATE_PLAN):
        getattr(reducer, act)(chunk)
        if number % 2 == 1:
            stage = number // 2
            if stage < 5:
                table_copy(stage).wait_recv()
                kept[stage + 1] = kept[stage] + arrived[stage]
            if stage < 4:
                table_copy(stage + 1).start()
    total_ref[...] = kept[5]
    reducer.finish(out_ref)
    for stage in range(5):
        table_copy(stage).wait_send()


def reduce_late(pieces, table):
    rows, width = pieces.shape[-2:]
    whole = pl.BlockSpec(memory_space=pltpu.VMEM)
    return pl.pallas_call(
        functools.partial(late_kernel, rows),
        in_specs=[pl.BlockSpec(memory_space=pl.ANY), whole],
        out_specs=[whole, whole],
        out_shape=[
            jax.ShapeDtypeStruct((rows, width), F32),
            jax.ShapeDtypeStruct(table.shape, F32),
        ],
        scratch_shapes=Reducer.scratch(rows, width)
        + [
            pltpu.VMEM((6,) + table.shape, F32),
            pltpu.VMEM((5,) + table.shape, F32),
            pltpu.SemaphoreType.DMA((5,)),
            pltpu.SemaphoreType.DMA((5,)),
        ],
        compiler_params=pltpu.CompilerParams(
            collective_id=2, has_side_effects=True, vmem_limit_bytes=40 * 2**20
        ),
        name="reduce_late",
    )(pieces, table)


def has_plan():
    return (lax.axis_size("dp"), lax.axis_size("seq")) == (8, 4)


def by_core(parts):
    return parts.astype(BF16).reshape((4, 2, 2, 2) + parts.shape[1:]).transpose(3, 0, 1, 2, 4, 5)


def scattered(parts):
    return lax.psum_scatter(
        parts.astype(BF16), ("dp", "seq"), scatter_dimension=0, tiled=True
    )[0].astype(F32)


class BackSizes(NamedTuple):
    block: int
    count: int
    quarter: int
    seq_count: int
    pairs: int
    early_rows: int


def seq_device(steps, seq_count):
    return (lax.axis_index("dp"), lax.rem(lax.axis_index("seq") + steps + seq_count, seq_count))


def back_kernel(
    sizes,
    len_ref,
    tab_ref,
    q_ref,
    kx_ref,
    vx_ref,
    kg_ref,
    vg_ref,
    o_ref,
    do_ref,
    l_ref,
    doq_ref,
    ldq_ref,
    *rest,
):
    block, count, quarter, seq_count, pairs, early_rows = sizes
    reduces = early_rows > 0
    if reduces:
        pieces_ref, rest = rest[0], rest[1:]
    dq_ref, dk_ref, dv_ref, dtab_ref, *rest = rest
    if reduces:
        early_ref, rest = rest[0], rest[1:]
    (
        dkx,
        dvx,
        dkg,
        dvg,
        glob_send,
        glob_recv,
        halo_send,
        halo_recv,
        dog_all,
        ld_all,
        every_sends,
        every_recvs,
        glob_sends,
        glob_recvs,
        halo_sends,
        halo_recvs,
        *rest,
    ) = rest
    number = pl.program_id(0)
    pair = lax.rem(number, pairs)
    seq_index = lax.axis_index("seq")
    reducer = Reducer(mesh_ids(), early_rows, pieces_ref, *rest[:5], rest[5:]) if reduces else None
    scale = HD ** (-0.5)
    low_lanes = lane_index() < HD
    own_keys = slice(HALO, HALO + block)
    own_rows = pl.ds(pl.multiple_of(seq_index * quarter, quarter), quarter)
    lanes_of = lambda at: pl.ds(pl.multiple_of(at * PAIR, PAIR), PAIR)

    def every_copies():
        for step in range(1, seq_count):
            for kind, (source, dest) in enumerate(((doq_ref, dog_all), (ldq_ref, ld_all))):
                yield pltpu.make_async_remote_copy(
                    src_ref=source,
                    dst_ref=dest.at[seq_index],
                    send_sem=every_sends.at[kind, step - 1],
                    recv_sem=every_recvs.at[kind, step - 1],
                    device_id=seq_device(step, seq_count),
                    device_id_type=pl.DeviceIdType.MESH,
                )

    def glob_copies(at):
        for step in range(1, seq_count):
            device = seq_device(step, seq_count)
            yield pltpu.make_async_remote_copy(
                src_ref=glob_send.at[device[1], at],
                dst_ref=glob_recv.at[step - 1, at],
                send_sem=glob_sends.at[step - 1, at],
                recv_sem=glob_recvs.at[step - 1, at],
                device_id=device,
                device_id_type=pl.DeviceIdType.MESH,
            )

    def halo_copy(direction):
        return pltpu.make_async_remote_copy(
            src_ref=halo_send.at[direction],
            dst_ref=halo_recv.at[direction],
            send_sem=halo_sends.at[direction],
            recv_sem=halo_recvs.at[direction],
            device_id=seq_device(2 * direction - 1, seq_count),
            device_id_type=pl.DeviceIdType.MESH,
        )

    has_low, has_high = seq_index > 0, seq_index < seq_count - 1
    sends_to = (has_low, has_high)
    gets_from = (has_high, has_low)

    @pl.when(number == 0)
    def _():
        others = [seq_device(step, seq_count) for step in range(1, seq_count)]
        meet(others + (reducer.partners()[2:] if reduces else []))
        for copy in every_copies():
            copy.start()
        if reduces:
            reducer.start()
        dog_all[seq_index] = doq_ref[...]
        ld_all[seq_index] = ldq_ref[...]

    if reduces:
        for at, act, chunk in EARLY_PLAN:

            @pl.when(number == at)
            def _(act=act, chunk=chunk):
                getattr(reducer, act)(chunk)

    @pl.when(number < pairs)
    def _():
        long_bias = key_bias(seq_index * block - HALO, block + 2 * HALO, len_ref[0])
        glob_bias = key_bias(0, GP, count)
        query = q_ref[:block] * jnp.asarray(scale, BF16)
        grad_o = do_ref[...]
        both = grad_o.astype(F32) * o_ref[...].astype(F32)
        heads = []
        for head in range(2):
            norm = in_three(-pick_column(l_ref[...], 2 * pair + head))
            delta = in_three(-jnp.sum(own_half(head, both), -1, keepdims=True))
            heads.append(
                dict(
                    q=own_half(head, query),
                    do=own_half(head, grad_o),
                    qa=with_lanes(head, query, (1.0,) + norm),
                    doa=with_lanes(head, grad_o, delta),
                    kxa=key_side(head, kx_ref[...], long_bias),
                    vxa=value_side(head, vx_ref[...]),
                    kga=key_side(head, kg_ref[...], glob_bias),
                    vga=value_side(head, vg_ref[...]),
                    bias=band_bias(tab_ref[0, head : head + 1]),
                )
            )
        dkx[pair] = jnp.zeros_like(dkx[pair])
        dvx[pair] = jnp.zeros_like(dvx[pair])
        table_sums = [0.0, 0.0]
        grads_q = []
        for start in range(0, block, SUB):
            rows, keys = slice(start, start + SUB), slice(start, start + WINDOW)
            outs, probs, grads = [], [], []
            for head, own in enumerate(heads):
                band = jnp.exp(dot_t(own["qa"][rows], own["kxa"][keys]) + own["bias"])
                band_ds = band * dot_t(own["doa"][rows], own["vxa"][keys])
                table_sums[head] += band_ds
                glob = jnp.exp(dot_t(own["qa"][rows], own["kga"]))
                glob_ds = (glob * dot_t(own["doa"][rows], own["vga"])).astype(BF16)
                band_ds = band_ds.astype(BF16)
                outs.append(dot_n(band_ds, kx_ref[keys]) + dot_n(glob_ds, kg_ref[...]))
                probs.append((band.astype(BF16), glob.astype(BF16)))
                grads.append((band_ds, glob_ds))
            grads_q.append(jnp.where(low_lanes, outs[0], outs[1]))
            own_q = jnp.concatenate([own["q"][rows] for own in heads], 0)
            own_do = jnp.concatenate([own["do"][rows] for own in heads], 0)
            band, glob = (jnp.concatenate(part, 0) for part in zip(*probs))
            band_ds, glob_ds = (jnp.concatenate(part, 0) for part in zip(*grads))
            dkx[pair, keys] += t_dot(band_ds, own_q)
            dvx[pair, keys] += t_dot(band, own_do)
            more_k, more_v = t_dot(glob_ds, own_q), t_dot(glob, own_do)
            dkg[pair] = more_k if start == 0 else dkg[pair] + more_k
            dvg[pair] = more_v if start == 0 else dvg[pair] + more_v
        dq_ref[:block, lanes_of(pair)] = (jnp.concatenate(grads_q, 0) * scale).astype(BF16)
        for head in range(2):
            dtab_ref[pair, head : head + 1] = diagonal_sums(table_sums[head])

    @pl.when(number == pairs)
    def _():
        for kind, total in enumerate((dkx, dvx)):
            for direction, first in enumerate((HALO - REACH, HALO + block)):
                halo_send[direction, kind] = total[:, first : first + REACH].astype(BF16)
        for direction in range(2):

            @pl.when(sends_to[direction])
            def _(direction=direction):
                halo_copy(direction).start()

        for copy in every_copies():
            copy.wait_recv()

    @pl.when(number >= pairs)
    def _():
        long_bias = key_bias(seq_index * block, block, len_ref[0])
        near_bias = key_bias(seq_index * quarter, quarter, count)
        query = q_ref[block:] * jnp.asarray(scale, BF16)
        grad_o = dog_all[:, :, lanes_of(pair)].reshape(GP, PAIR)
        stats = ld_all[...].reshape(GP, PAIR)
        far_k, far_v = kx_ref[own_keys], vx_ref[own_keys]
        near_k, near_v = kg_ref[own_rows], vg_ref[own_rows]
        outs, kept = [], []
        for head in range(2):
            norm = in_three(-pick_column(stats, 2 * pair + head))
            delta = in_three(-pick_column(stats, HD + 2 * pair + head))
            qa = with_lanes(head, query, (1.0,) + norm)
            doa = with_lanes(head, grad_o, delta)
            far = jnp.exp(dot_t(qa, key_side(head, far_k, long_bias)))
            near = jnp.exp(dot_t(qa, key_side(head, near_k, near_bias)))
            far_ds = (far * dot_t(doa, value_side(head, far_v))).astype(BF16)
            near_ds = (near * dot_t(doa, value_side(head, near_v))).astype(BF16)
            outs.append(dot_n(far_ds, far_k) + dot_n(near_ds, near_k))
            kept.append(
                (
                    own_half(head, query),
                    own_half(head, grad_o),
                    far.astype(BF16),
                    near.astype(BF16),
                    far_ds,
                    near_ds,
                )
            )
        own_q, own_do, far, near, far_ds, near_ds = (
            jnp.concatenate(part, 0) for part in zip(*kept)
        )
        dkx[pair, own_keys] += t_dot(far_ds, own_q)
        dvx[pair, own_keys] += t_dot(far, own_do)
        dkg[pair, own_rows] += t_dot(near_ds, own_q)
        dvg[pair, own_rows] += t_dot(near, own_do)
        glob_dq = jnp.where(low_lanes, outs[0], outs[1]) * scale
        for at, grad in enumerate((glob_dq, dkg[pair], dvg[pair])):
            glob_send[:, pair, :, at * PAIR : (at + 1) * PAIR] = grad.astype(BF16).reshape(
                seq_count, quarter, PAIR
            )
        for copy in glob_copies(pair):
            copy.start()

    @pl.when(number == 2 * pairs - 1)
    def _():
        for direction in range(2):

            @pl.when(gets_from[direction])
            def _(direction=direction):
                halo_copy(direction).wait_recv()

            @pl.when(jnp.logical_not(gets_from[direction]))
            def _(direction=direction):
                halo_recv[direction] = jnp.zeros_like(halo_recv[direction])

        for at in range(pairs):
            lanes = slice(at * PAIR, (at + 1) * PAIR)
            for kind, (total, out) in enumerate(((dkx, dk_ref), (dvx, dv_ref))):
                first, last = HALO + REACH, HALO + block - REACH
                out[:REACH, lanes] = (
                    total[at, HALO:first] + halo_recv[1, kind, at].astype(F32)
                ).astype(BF16)
                out[REACH : block - REACH, lanes] = total[at, first:last].astype(BF16)
                out[block - REACH : block, lanes] = (
                    total[at, last : HALO + block] + halo_recv[0, kind, at].astype(F32)
                ).astype(BF16)
        for at in range(pairs):
            lanes = slice(at * PAIR, (at + 1) * PAIR)
            total = glob_send[seq_index, at].astype(F32)
            for step, copy in enumerate(glob_copies(at)):
                copy.wait_recv()
                total += glob_recv[step, at].astype(F32)
            for kind, out in enumerate((dq_ref, dk_ref, dv_ref)):
                out[block:, lanes] = total[:, kind * PAIR : (kind + 1) * PAIR].astype(BF16)
        for at in range(pairs):
            for copy in glob_copies(at):
                copy.wait_send()
        for copy in every_copies():
            copy.wait_send()
        for direction in range(2):

            @pl.when(sends_to[direction])
            def _(direction=direction):
                halo_copy(direction).wait_send()

        if reduces:
            reducer.finish(early_ref)


def attend_back(sizes, doc_len, table, q, kx, vx, kg, vg, o, do, l, doq, ldq, pieces=None):
    block, count, quarter, seq_count, pairs, early_rows = sizes
    width = q.shape[1]
    ext = block + 2 * HALO
    cols = lambda rows: pl.BlockSpec((rows, PAIR), lambda i: (0, lax.rem(i, pairs)))
    whole = pl.BlockSpec(memory_space=pltpu.VMEM)
    shape = jax.ShapeDtypeStruct
    in_specs = [
        pl.BlockSpec(memory_space=pltpu.SMEM),
        pl.BlockSpec((1, 2, WINDOW), lambda i: (lax.rem(i, pairs), 0, 0)),
        cols(block + GP),
        cols(ext),
        cols(ext),
        cols(GP),
        cols(GP),
        cols(block),
        cols(block),
        whole,
        whole,
        whole,
    ]
    rows = block + quarter
    outs = [shape((rows, width), BF16)] * 3 + [shape((pairs, 2, WINDOW), F32)]
    others = seq_count - 1
    scratch = [
        pltpu.VMEM((pairs, ext, PAIR), F32),
        pltpu.VMEM((pairs, ext, PAIR), F32),
        pltpu.VMEM((pairs, GP, PAIR), F32),
        pltpu.VMEM((pairs, GP, PAIR), F32),
        pltpu.VMEM((seq_count, pairs, quarter, 3 * PAIR), BF16),
        pltpu.VMEM((others, pairs, quarter, 3 * PAIR), BF16),
        pltpu.VMEM((2, 2, pairs, REACH, PAIR), BF16),
        pltpu.VMEM((2, 2, pairs, REACH, PAIR), BF16),
        pltpu.VMEM((seq_count, quarter, width), BF16),
        pltpu.VMEM((seq_count, quarter, PAIR), F32),
        pltpu.SemaphoreType.DMA((2, others)),
        pltpu.SemaphoreType.DMA((2, others)),
        pltpu.SemaphoreType.DMA((others, pairs)),
        pltpu.SemaphoreType.DMA((others, pairs)),
        pltpu.SemaphoreType.DMA((2,)),
        pltpu.SemaphoreType.DMA((2,)),
    ]
    args = [doc_len, table, q, kx, vx, kg, vg, o, do, l, doq, ldq]
    if early_rows:
        in_specs.append(pl.BlockSpec(memory_space=pl.ANY))
        outs.append(shape((early_rows, width), F32))
        scratch += Reducer.scratch(early_rows, width)
        args.append(pieces)
    return pl.pallas_call(
        functools.partial(back_kernel, sizes),
        grid=(2 * pairs,),
        in_specs=in_specs,
        out_specs=[whole] * len(outs),
        out_shape=outs,
        scratch_shapes=scratch,
        compiler_params=pltpu.CompilerParams(
            collective_id=1, has_side_effects=True, vmem_limit_bytes=60 * 2**20
        ),
        name="attend_back",
    )(*args)


def passed_along(value, axis, steps):
    count = lax.axis_size(axis)
    first, last = (max(0, -steps), min(count, count - steps))
    return lax.ppermute(value, axis, [(source, source + steps) for source in range(first, last)])


def matmul(left, right):
    return jnp.dot(left, right, preferred_element_type=F32)


def rows_dot(left, right):
    return jnp.einsum("rd,re->de", left, right, preferred_element_type=F32)


def back_dot(left, right):
    return lax.dot_general(left, right, (((1,), (1,)), ((), ())), preferred_element_type=F32)


def on_device(
    long_input,
    global_input,
    lengths,
    w_query,
    b_query,
    w_key,
    w_value,
    b_value,
    w_out,
    b_out,
    w_inner,
    b_inner,
    w_outer,
    b_outer,
    norm1_gain,
    norm1_shift,
    norm2_gain,
    norm2_shift,
    rel_table,
    long_cotangent,
    global_cotangent,
):
    seq_count = lax.axis_size("seq")
    data_count = lax.axis_size("dp")
    seq_index = lax.axis_index("seq")
    block = long_input.shape[1]
    count = global_input.shape[1]
    width = long_input.shape[2]
    heads = rel_table.shape[1]
    pairs = heads // 2
    labels = 2 * R + 1
    quarter = GP // seq_count
    dims = (block, count, quarter)
    doc_len = lengths[0]
    row_valid = (seq_index * block + jnp.arange(block, dtype=jnp.int32)) < doc_len
    meta = jnp.stack([doc_len, seq_index]).astype(jnp.int32)
    table = jnp.pad(
        rel_table.T,
        ((0, 0), (HALO - R, WINDOW - labels - HALO + R)),
        constant_values=MASKED,
    ).reshape(pairs, 2, WINDOW)

    glob_x = jnp.pad(global_input[0], ((0, GP - count), (0, 0)))
    glob_dy = jnp.pad(global_cotangent[0], ((0, GP - count), (0, 0)))
    own_glob = lambda a: lax.dynamic_slice_in_dim(a, seq_index * quarter, quarter, 0)
    all_x = jnp.concatenate([long_input[0], glob_x], 0).astype(F32)
    own_x = jnp.concatenate([long_input[0], own_glob(glob_x)], 0).astype(F32)
    normed = norm_forward(all_x, norm1_gain, norm1_shift)[0].astype(BF16)
    keys = matmul(normed, w_key).astype(BF16)
    values = (matmul(normed, w_value) + b_value).astype(BF16)
    queries = (matmul(normed, w_query) + b_query).astype(BF16)

    def extended(rows):
        below = passed_along(rows[block - HALO : block], "seq", 1)
        above = passed_along(rows[:HALO], "seq", -1)
        return jnp.concatenate([below, rows[:block], above], 0)

    kx, vx = extended(keys), extended(values)
    kg, vg = keys[block:], values[block:]
    attended, norms = attend(dims, meta, table, queries, kx, vx, kg, vg)

    def to_owner(part):
        return lax.all_to_all(
            part.reshape(seq_count, quarter, -1), "seq", split_axis=0, concat_axis=0, tiled=True
        )

    part_o = to_owner(attended[block:]).astype(F32).reshape(seq_count, quarter, heads, HD)
    part_l = to_owner(norms[:, block:].transpose(1, 0, 2).reshape(GP, heads))
    top = jnp.max(part_l, 0)
    glob_l = top + jnp.log(jnp.sum(jnp.exp(part_l - top), 0))
    glob_o = jnp.sum(part_o * jnp.exp(part_l - glob_l)[..., None], 0).reshape(quarter, width)
    attn_low = jnp.concatenate([attended[:block], glob_o.astype(BF16)], 0)

    residual_mid = own_x + matmul(attn_low, w_out) + b_out
    normed_two, hat_two, inv_two = norm_forward(residual_mid, norm2_gain, norm2_shift)
    normed_two_low = normed_two.astype(BF16)
    hidden_pre = matmul(normed_two_low, w_inner) + b_inner
    activated, gelu_back = jax.vjp(smooth_gate, hidden_pre)
    activated_low = activated.astype(BF16)
    result = residual_mid + matmul(activated_low, w_outer) + b_outer
    long_result = jnp.where(row_valid[:, None], result[:block], 0.0).astype(BF16)
    grad_y_low = jnp.concatenate(
        [
            jnp.where(row_valid[:, None], long_cotangent[0], jnp.zeros_like(long_cotangent[0])),
            own_glob(glob_dy),
        ],
        0,
    )
    grad_y = grad_y_low.astype(F32)
    grad_b_outer = jnp.sum(grad_y, 0)
    grad_w_outer = rows_dot(activated_low, grad_y_low)
    (grad_hidden,) = gelu_back(back_dot(grad_y_low, w_outer))
    grad_b_inner = jnp.sum(grad_hidden, 0)
    hidden_low = grad_hidden.astype(BF16)
    grad_w_inner = rows_dot(normed_two_low, hidden_low)
    grad_from_two, grad_gain_two, grad_shift_two = norm_backward(
        back_dot(hidden_low, w_inner), hat_two, inv_two, norm2_gain
    )
    grad_mid = grad_y + grad_from_two
    grad_b_out = jnp.sum(grad_mid, 0)
    grad_mid_low = grad_mid.astype(BF16)
    grad_w_out = rows_dot(attn_low, grad_mid_low)
    grad_attn = back_dot(grad_mid_low, w_out).astype(BF16)

    glob_do = grad_attn[block:]
    glob_delta = jnp.sum((glob_do.astype(F32) * glob_o).reshape(quarter, heads, HD), -1)
    stats = jnp.zeros((quarter, PAIR), F32)
    stats = stats.at[:, :heads].set(glob_l).at[:, HD : HD + heads].set(glob_delta)
    long_l = jnp.pad(
        norms[:, :block].transpose(1, 0, 2).reshape(block, heads), ((0, 0), (0, PAIR - heads))
    )
    devices = data_count * seq_count
    piece = width // devices
    by_device = lambda grad: grad.reshape(devices, -1, width)

    def wide(grad):
        blocks = grad.reshape(devices, piece, -1, width)
        return blocks.transpose(0, 2, 1, 3).reshape(devices, -1, width)

    inner_rows = wide(grad_w_inner).shape[1]
    early_parts = jnp.concatenate([by_device(grad_w_outer), wide(grad_w_inner)], 1)
    planned = has_plan()
    sizes = BackSizes(
        block, count, quarter, seq_count, pairs, early_parts.shape[1] if planned else 0
    )
    query_low, key_low, value_low, dtab, *early = attend_back(
        sizes,
        lengths,
        table,
        queries,
        kx,
        vx,
        kg,
        vg,
        attended[:block],
        grad_attn[:block],
        long_l,
        glob_do,
        stats,
        *([by_core(early_parts)] if planned else []),
    )
    early = early[0] if planned else scattered(early_parts)
    own_normed, hat_one, inv_one = norm_forward(own_x, norm1_gain, norm1_shift)
    own_normed = own_normed.astype(BF16)
    grad_b_query = jnp.sum(query_low.astype(F32), 0)
    grad_b_value = jnp.sum(value_low.astype(F32), 0)
    grad_w_query = rows_dot(own_normed, query_low)
    grad_w_key = rows_dot(own_normed, key_low)
    grad_w_value = rows_dot(own_normed, value_low)
    grad_normed_one = (
        back_dot(query_low, w_query) + back_dot(key_low, w_key) + back_dot(value_low, w_value)
    )
    grad_from_one, grad_gain_one, grad_shift_one = norm_backward(
        grad_normed_one, hat_one, inv_one, norm1_gain
    )
    grad_x = grad_mid + grad_from_one

    g_outer = early[:-inner_rows]
    g_inner = early[-inner_rows:].reshape(-1, piece, width).transpose(1, 0, 2)
    vectors = (
        grad_b_query,
        grad_b_value,
        grad_b_out,
        grad_b_inner,
        grad_b_outer,
        grad_gain_one,
        grad_shift_one,
        grad_gain_two,
        grad_shift_two,
    )
    small = jnp.concatenate([v.reshape(devices, -1) for v in vectors], 1)
    small = jnp.pad(small, ((0, 0), (0, width - small.shape[1])))
    small = jnp.pad(small[:, None], ((0, 0), (0, 15), (0, 0)))
    late_parts = jnp.concatenate(
        [by_device(g) for g in (grad_w_query, grad_w_key, grad_w_value, grad_w_out)] + [small], 1
    )
    table_part = dtab.reshape(heads, WINDOW)
    if planned:
        late, table_total = reduce_late(by_core(late_parts), table_part)
    else:
        late, table_total = scattered(late_parts), lax.psum(table_part, ("dp", "seq"))
    table_total = table_total[:, HALO - R : HALO - R + labels].T
    pieces, at = [], 0
    for vector in vectors:
        length = vector.shape[0] // devices
        pieces.append(late[4 * piece, at : at + length])
        at += length
    g_b_query, g_b_value, g_b_out, g_b_inner, g_b_outer, g_g1, g_s1, g_g2, g_s2 = pieces
    g_query, g_key, g_value, g_out = (late[i * piece : (i + 1) * piece] for i in range(4))
    glob_out = lax.all_gather(result[block:].astype(BF16), "seq", axis=0, tiled=True)[:count]
    glob_grad = lax.all_gather(grad_x[block:], "seq", axis=0, tiled=True)[:count]
    return (
        long_result[None],
        glob_out[None],
        grad_x[:block][None],
        glob_grad[None],
        g_query,
        g_b_query,
        g_key,
        g_value,
        g_b_value,
        g_out,
        g_b_out,
        g_inner.reshape(piece, -1),
        g_b_inner,
        g_outer,
        g_b_outer,
        g_g1,
        g_s1,
        g_g2,
        g_s2,
        table_total,
    )


def solution(mesh):
    rows, whole = P("dp", "seq", None), P("dp", None, None)
    matrix, vector = P(("dp", "seq"), None), P(("dp", "seq"))
    return jax.shard_map(
        on_device,
        mesh=mesh,
        in_specs=(rows, whole, P("dp")) + (P(),) * 16 + (rows, whole),
        out_specs=(
            rows,
            whole,
            rows,
            whole,
            matrix,
            vector,
            matrix,
            matrix,
            vector,
            matrix,
            vector,
            matrix,
            vector,
            matrix,
            vector,
            vector,
            vector,
            vector,
            vector,
            P(),
        ),
        check_vma=False,
    )
```

```python
import functools
from typing import NamedTuple

import jax
import jax.numpy as jnp
from jax import lax
from jax.experimental import pallas as pl
from jax.experimental.pallas import tpu as pltpu
from jax.sharding import PartitionSpec as P

HD = 64
R = 84
PAIR = 2 * HD
HALO = 128
REACH = 96
GP = 256
SUB = 256
WINDOW = SUB + 2 * HALO
EPSILON = 1e-05
MASKED = -1e30
F32 = jnp.float32
BF16 = jnp.bfloat16


def norm_forward(values, gain, shift):
    average = jnp.mean(values, -1, keepdims=True)
    centred = values - average
    variance = jnp.mean(centred * centred, -1, keepdims=True)
    inverse = lax.rsqrt(variance + EPSILON)
    normed = centred * inverse
    return (normed * gain + shift, normed, inverse)


def norm_backward(grad_rows, normed, inverse, gain):
    scaled = grad_rows * gain
    grad_in = inverse * (
        scaled
        - jnp.mean(scaled, -1, keepdims=True)
        - normed * jnp.mean(scaled * normed, -1, keepdims=True)
    )
    return (grad_in, jnp.sum(grad_rows * normed, 0), jnp.sum(grad_rows, 0))


def smooth_gate(values):
    return jax.nn.gelu(values, approximate=True)


def dot_t(left, right):
    return lax.dot_general(left, right, (((1,), (1,)), ((), ())), preferred_element_type=F32)


def dot_n(left, right):
    return lax.dot_general(left, right, (((1,), (0,)), ((), ())), preferred_element_type=F32)


def t_dot(left, right):
    return lax.dot_general(left, right, (((0,), (0,)), ((), ())), preferred_element_type=F32)


def band_bias(table_row):
    spread = jnp.broadcast_to(table_row, (SUB, WINDOW))
    return pltpu.roll(spread, 0, 1, stride=1, stride_axis=0)


def diagonal_sums(rows):
    height, width = rows.shape
    while height > 8:
        height //= 2
        rows = rows[:height] + pltpu.roll(rows[height:], width - height, 1)
    row = lax.broadcasted_iota(jnp.int32, rows.shape, 0)
    for bit in (1, 2, 4):
        rows = jnp.where((row & bit) != 0, pltpu.roll(rows, width - bit, 1), rows)
    return jnp.sum(rows, 0, keepdims=True)


def lane_index():
    return lax.broadcasted_iota(jnp.int32, (1, PAIR), 1)


def own_half(head, value):
    low_lanes = lane_index() < HD
    return jnp.where(low_lanes if head == 0 else ~low_lanes, value, jnp.zeros_like(value))


def other_lane(head):
    return HD * (1 - head)


def with_lanes(head, value, columns):
    wide = own_half(head, value.astype(F32))
    lane = lane_index()
    for offset, column in enumerate(columns):
        wide = jnp.where(lane == other_lane(head) + offset, column, wide)
    return wide.astype(BF16)


def in_three(column):
    high = column.astype(BF16).astype(F32)
    middle = (column - high).astype(BF16).astype(F32)
    return (high, middle, column - high - middle)


def key_bias(first, rows, end):
    position = first + lax.broadcasted_iota(jnp.int32, (rows, 1), 0)
    return jnp.where((position >= 0) & (position < end), 0.0, MASKED)


def pick_column(rows, index):
    return jnp.sum(jnp.where(lane_index() == index, rows, 0.0), -1, keepdims=True)


def key_side(head, keys, bias):
    return with_lanes(head, keys, (bias, 1.0, 1.0, 1.0))


def value_side(head, values):
    return with_lanes(head, values, (1.0, 1.0, 1.0))


def softmax_rows(parts, value_parts, head):
    top = functools.reduce(
        jnp.maximum, [jnp.max(part, -1, keepdims=True) for part in parts]
    )
    mixed = sum(
        dot_n(jnp.exp(part - top).astype(BF16), values)
        for part, values in zip(parts, value_parts)
    )
    at = other_lane(head)
    total = mixed[:, at : at + 1]
    return mixed / total, top + jnp.log(total)


def seq_device(steps, seq_count):
    return (lax.axis_index("dp"), lax.rem(lax.axis_index("seq") + steps + seq_count, seq_count))


def row_norm(rows):
    centred = rows - jnp.mean(rows, -1, keepdims=True)
    inverse = lax.rsqrt(jnp.mean(centred * centred, -1, keepdims=True) + EPSILON)
    return centred * inverse, inverse


def put_column(ref, rows, index, column):
    ref[rows] = jnp.where(lane_index() == index, column, ref[rows])


def lanes_of(at):
    return pl.ds(pl.multiple_of(at * PAIR, PAIR), PAIR)


class Sizes(NamedTuple):
    block: int
    count: int
    quarter: int
    seq_count: int
    pairs: int


def attend_kernel(
    sizes,
    len_ref,
    tab_ref,
    long_ref,
    glob_ref,
    wq_ref,
    wk_ref,
    wv_ref,
    bq_ref,
    bv_ref,
    gain_ref,
    shift_ref,
    q_ref,
    kx_ref,
    vx_ref,
    kg_ref,
    vg_ref,
    o_ref,
    l_ref,
    lq_ref,
    part_o,
    part_l,
    from_o,
    from_l,
    halo_sends,
    halo_recvs,
    part_sends,
    part_recvs,
):
    block, count, quarter, seq_count, pairs = sizes
    ext = block + 2 * HALO
    seq_index = lax.axis_index("seq")
    scale = jnp.asarray(HD ** (-0.5), BF16)
    low_lanes = lane_index() < HD
    own_keys = slice(HALO, HALO + block)
    own_rows = pl.ds(pl.multiple_of(seq_index * quarter, quarter), quarter)
    neighbours = (seq_index > 0, seq_index < seq_count - 1)
    barrier = pltpu.get_barrier_semaphore()
    for step in range(1, seq_count):
        pl.semaphore_signal(
            barrier,
            inc=1,
            device_id=seq_device(step, seq_count),
            device_id_type=pl.DeviceIdType.MESH,
        )

    def halo_copies(direction):
        source = HALO if direction == 0 else HALO + block - REACH
        dest = HALO + block if direction == 0 else HALO - REACH
        for kind, ref in enumerate((kx_ref, vx_ref)):
            yield pltpu.make_async_remote_copy(
                src_ref=ref.at[source : source + REACH],
                dst_ref=ref.at[dest : dest + REACH],
                send_sem=halo_sends.at[direction, kind],
                recv_sem=halo_recvs.at[direction, kind],
                device_id=seq_device(2 * direction - 1, seq_count),
                device_id_type=pl.DeviceIdType.MESH,
            )

    def part_copies():
        for step in range(1, seq_count):
            device = seq_device(step, seq_count)
            rows = pl.ds(pl.multiple_of(device[1] * quarter, quarter), quarter)
            for kind, (source, dest) in enumerate(((part_o, from_o), (part_l, from_l))):
                yield step, kind, pltpu.make_async_remote_copy(
                    src_ref=source.at[rows],
                    dst_ref=dest.at[step - 1],
                    send_sem=part_sends.at[kind, step - 1],
                    recv_sem=part_recvs.at[kind, step - 1],
                    device_id=device,
                    device_id_type=pl.DeviceIdType.MESH,
                )

    gain, shift = gain_ref[...], shift_ref[...]
    normed_long = (row_norm(long_ref[...].astype(F32))[0] * gain + shift).astype(BF16)
    kx_ref[own_keys] = dot_n(normed_long, wk_ref[...]).astype(BF16)
    vx_ref[own_keys] = (dot_n(normed_long, wv_ref[...]) + bv_ref[...]).astype(BF16)
    pl.semaphore_wait(barrier, seq_count - 1)
    for direction, first in enumerate((HALO - REACH, HALO + block)):

        @pl.when(neighbours[direction])
        def _(direction=direction):
            for copy in halo_copies(direction):
                copy.start()

        outer = slice(0, first) if direction == 0 else slice(first + REACH, ext)
        for ref in (kx_ref, vx_ref):
            ref[outer] = jnp.zeros((HALO - REACH, ref.shape[1]), BF16)

        @pl.when(jnp.logical_not(neighbours[direction]))
        def _(first=first):
            for ref in (kx_ref, vx_ref):
                ref[first : first + REACH] = jnp.zeros((REACH, ref.shape[1]), BF16)

    normed_glob = (row_norm(glob_ref[...].astype(F32))[0] * gain + shift).astype(BF16)
    kg_ref[...] = dot_n(normed_glob, wk_ref[...]).astype(BF16)
    vg_ref[...] = (dot_n(normed_glob, wv_ref[...]) + bv_ref[...]).astype(BF16)
    q_ref[block:] = (dot_n(normed_glob, wq_ref[...]) + bq_ref[...]).astype(BF16)
    q_ref[:block] = (dot_n(normed_long, wq_ref[...]) + bq_ref[...]).astype(BF16)
    part_l[...] = jnp.zeros_like(part_l)
    l_ref[...] = jnp.zeros_like(l_ref)

    def glob_pair(pair, carry):
        lanes = lanes_of(pair)
        far_bias = key_bias(seq_index * block, block, len_ref[0])
        near_bias = key_bias(seq_index * quarter, quarter, count)
        query = q_ref[block:, lanes] * scale
        outs = []
        for head in range(2):
            q = with_lanes(head, query, (1.0,))
            far = dot_t(q, with_lanes(head, kx_ref[own_keys, lanes], (far_bias,)))
            near = dot_t(q, with_lanes(head, kg_ref[own_rows, lanes], (near_bias,)))
            out, norm = softmax_rows(
                [far, near],
                [
                    with_lanes(head, vx_ref[own_keys, lanes], (1.0,)),
                    with_lanes(head, vg_ref[own_rows, lanes], (1.0,)),
                ],
                head,
            )
            outs.append(out)
            put_column(part_l, slice(None), 2 * pair + head, norm)
        part_o[:, lanes] = jnp.where(low_lanes, outs[0], outs[1]).astype(BF16)
        return carry

    lax.fori_loop(0, pairs, glob_pair, 0)
    for _, _, copy in part_copies():
        copy.start()
    for direction in range(2):

        @pl.when(neighbours[1 - direction])
        def _(direction=direction):
            for copy in halo_copies(direction):
                copy.wait_recv()

    def long_pair(pair, carry):
        lanes = lanes_of(pair)
        long_bias = key_bias(seq_index * block - HALO, ext, len_ref[0])
        glob_bias = key_bias(0, GP, count)
        query = q_ref[:block, lanes] * scale
        outs = []
        for head in range(2):
            q = with_lanes(head, query, (1.0,))
            kx = with_lanes(head, kx_ref[:, lanes], (long_bias,))
            kg = with_lanes(head, kg_ref[:, lanes], (glob_bias,))
            vx, vg = (with_lanes(head, ref[:, lanes], (1.0,)) for ref in (vx_ref, vg_ref))
            bias = band_bias(tab_ref[pair, head : head + 1])
            mixed = []
            for start in range(0, block, SUB):
                rows, keys = slice(start, start + SUB), slice(start, start + WINDOW)
                out, norm = softmax_rows(
                    [dot_t(q[rows], kx[keys]) + bias, dot_t(q[rows], kg)], [vx[keys], vg], head
                )
                mixed.append(out)
                put_column(l_ref, rows, 2 * pair + head, norm)
            outs.append(jnp.concatenate(mixed, 0))
        o_ref[:block, lanes] = jnp.where(low_lanes, outs[0], outs[1]).astype(BF16)
        return carry

    lax.fori_loop(0, pairs, long_pair, 0)
    for _, _, copy in part_copies():
        copy.wait_recv()
    norms = [part_l[own_rows]] + [from_l[step] for step in range(seq_count - 1)]
    outs = [part_o[own_rows]] + [from_o[step] for step in range(seq_count - 1)]
    top = functools.reduce(jnp.maximum, norms)
    shares = [jnp.exp(norm - top) for norm in norms]
    total = sum(shares)
    lq_ref[...] = top + jnp.log(total)
    shares = [share / total for share in shares]
    for at in range(pairs):
        lanes = slice(at * PAIR, (at + 1) * PAIR)
        mixed = 0.0
        for share, out in zip(shares, outs):
            spread = jnp.where(
                low_lanes, share[:, 2 * at : 2 * at + 1], share[:, 2 * at + 1 : 2 * at + 2]
            )
            mixed += spread * out[:, lanes].astype(F32)
        o_ref[block:, lanes] = mixed.astype(BF16)
    for _, _, copy in part_copies():
        copy.wait_send()
    for direction in range(2):

        @pl.when(neighbours[direction])
        def _(direction=direction):
            for copy in halo_copies(direction):
                copy.wait_send()


def attend(sizes, doc_len, table, long_x, glob_x, *weights):
    block, count, quarter, seq_count, pairs = sizes
    width = long_x.shape[1]
    ext = block + 2 * HALO
    whole = pl.BlockSpec(memory_space=pltpu.VMEM)
    shape = jax.ShapeDtypeStruct
    others = seq_count - 1
    return pl.pallas_call(
        functools.partial(attend_kernel, sizes),
        in_specs=[pl.BlockSpec(memory_space=pltpu.SMEM)] + [whole] * 10,
        out_specs=[whole] * 8,
        out_shape=[
            shape((block + GP, width), BF16),
            shape((ext, width), BF16),
            shape((ext, width), BF16),
            shape((GP, width), BF16),
            shape((GP, width), BF16),
            shape((block + quarter, width), BF16),
            shape((block, PAIR), F32),
            shape((quarter, PAIR), F32),
        ],
        scratch_shapes=[
            pltpu.VMEM((GP, width), BF16),
            pltpu.VMEM((GP, PAIR), F32),
            pltpu.VMEM((others, quarter, width), BF16),
            pltpu.VMEM((others, quarter, PAIR), F32),
            pltpu.SemaphoreType.DMA((2, 2)),
            pltpu.SemaphoreType.DMA((2, 2)),
            pltpu.SemaphoreType.DMA((2, others)),
            pltpu.SemaphoreType.DMA((2, others)),
        ],
        compiler_params=pltpu.CompilerParams(
            collective_id=3, has_side_effects=True, vmem_limit_bytes=56 * 2**20
        ),
        name="attend",
    )(doc_len, table, long_x, glob_x, *weights)


class Reducer:
    def __init__(self, mesh_ids, rows, pieces, mine, from_core, from_one, from_two, from_z, sems):
        self.ids = mesh_ids
        half = (rows // 2 + 15) // 16 * 16
        self.halves = (slice(0, half), slice(half, rows))
        self.pieces, self.mine = pieces, mine
        self.from_core, self.from_one, self.from_two, self.from_z = (
            from_core,
            from_one,
            from_two,
            from_z,
        )
        self.local, self.sends, self.recvs = sems

    @staticmethod
    def scratch(rows, width):
        half = (rows // 2 + 15) // 16 * 16
        return [
            pltpu.VMEM((4, 2, 2, rows, width), BF16),
            pltpu.VMEM((4, 2, 2, rows, width), BF16),
            pltpu.VMEM((4, 2, rows, width), BF16),
            pltpu.VMEM((4, rows, width), BF16),
            pltpu.VMEM((3, rows, width), BF16),
            pltpu.SemaphoreType.DMA((4,)),
            pltpu.SemaphoreType.DMA((6, 4)),
            pltpu.SemaphoreType.DMA((6, 4)),
        ]

    def partners(self):
        z, y, x, core = self.ids
        dp, seq = z * 2 + y, x * 2 + core
        near = [(dp, x * 2 + 1 - core), (dp, (1 - x) * 2 + core), (z * 2 + 1 - y, seq)]
        return near + [(lax.rem(z + step, 4) * 2 + y, seq) for step in (1, 2, 3)]

    def target(self, chunk):
        return lax.rem(self.ids[0] + 1 + chunk, 4)

    def remote(self, source, dest, kind, chunk, partner):
        return pltpu.make_async_remote_copy(
            src_ref=source,
            dst_ref=dest,
            send_sem=self.sends.at[kind, chunk],
            recv_sem=self.recvs.at[kind, chunk],
            device_id=self.partners()[partner],
            device_id_type=pl.DeviceIdType.MESH,
        )

    def own_copy(self, chunk):
        z, y, x, core = self.ids
        to = self.target(chunk)
        return pltpu.make_async_copy(
            self.pieces.at[core, to], self.mine.at[to], self.local.at[chunk]
        )

    def core_copy(self, chunk):
        z, y, x, core = self.ids
        to = self.target(chunk)
        return self.remote(self.pieces.at[1 - core, to], self.from_core.at[to], 0, chunk, 0)

    def first_copies(self, chunk):
        z, y, x, core = self.ids
        to = self.target(chunk)
        one, two = self.halves
        return (
            self.remote(
                self.mine.at[to, :, 1 - x, one], self.from_one.at[to, :, one], 1, chunk, 1
            ),
            self.remote(
                self.mine.at[to, 1 - y, :, two], self.from_one.at[to, :, two], 2, chunk, 2
            ),
        )

    def second_copies(self, chunk):
        z, y, x, core = self.ids
        to = self.target(chunk)
        one, two = self.halves
        return (
            self.remote(
                self.mine.at[to, 1 - y, x, one], self.from_two.at[to, one], 3, chunk, 2
            ),
            self.remote(
                self.mine.at[to, y, 1 - x, two], self.from_two.at[to, two], 4, chunk, 1
            ),
        )

    def last_copy(self, chunk):
        z, y, x, core = self.ids
        return self.remote(
            self.mine.at[self.target(chunk), y, x], self.from_z.at[chunk], 5, chunk, 3 + chunk
        )

    def start(self):
        for chunk in range(4):
            self.core_copy(chunk).start()
            self.own_copy(chunk).start()

    def add_core(self, chunk):
        to = self.target(chunk)
        self.own_copy(chunk).wait()
        self.core_copy(chunk).wait_recv()

        def add(index, carry):
            at = (to, lax.div(index, 2), lax.rem(index, 2))
            self.mine[at] = (self.mine[at].astype(F32) + self.from_core[at].astype(F32)).astype(
                BF16
            )
            return carry

        lax.fori_loop(0, 4, add, 0)
        for copy in self.first_copies(chunk):
            copy.start()

    def add_first(self, chunk):
        z, y, x, core = self.ids
        one, two = self.halves
        to = self.target(chunk)
        for copy in self.first_copies(chunk):
            copy.wait_recv()

        def add(index, carry):
            for at, rows in (((to, index, x), one), ((to, y, index), two)):
                self.mine[at + (rows,)] = (
                    self.mine[at + (rows,)].astype(F32)
                    + self.from_one[to, index, rows].astype(F32)
                ).astype(BF16)
            return carry

        lax.fori_loop(0, 2, add, 0)
        for copy in self.second_copies(chunk):
            copy.start()

    def add_second(self, chunk):
        z, y, x, core = self.ids
        to = self.target(chunk)
        for copy in self.second_copies(chunk):
            copy.wait_recv()
        if chunk < 3:
            self.mine[to, y, x] = (
                self.mine[to, y, x].astype(F32) + self.from_two[to].astype(F32)
            ).astype(BF16)
            self.last_copy(chunk).start()

    def finish(self, out):
        z, y, x, core = self.ids
        total = self.mine[z, y, x].astype(F32) + self.from_two[z].astype(F32)
        for chunk in range(3):
            self.last_copy(chunk).wait_recv()
            total += self.from_z[chunk].astype(F32)
        out[...] = total
        for chunk in range(4):
            self.core_copy(chunk).wait_send()
            for copy in self.first_copies(chunk) + self.second_copies(chunk):
                copy.wait_send()
            if chunk < 3:
                self.last_copy(chunk).wait_send()


def mesh_ids():
    dp, seq = lax.axis_index("dp"), lax.axis_index("seq")
    return lax.div(dp, 2), lax.rem(dp, 2), lax.div(seq, 2), lax.rem(seq, 2)


def meet(devices):
    barrier = pltpu.get_barrier_semaphore()
    for device in devices:
        pl.semaphore_signal(barrier, inc=1, device_id=device, device_id_type=pl.DeviceIdType.MESH)
    pl.semaphore_wait(barrier, len(devices))


EARLY_PLAN = (
    (1, "add_core", 0),
    (2, "add_core", 1),
    (3, "add_core", 2),
    (4, "add_core", 3),
    (5, "add_first", 0),
    (8, "add_first", 1),
    (9, "add_second", 0),
    (11, "add_first", 2),
    (11, "add_second", 1),
    (11, "add_first", 3),
    (11, "add_second", 2),
    (11, "add_second", 3),
)
LATE_PLAN = (
    ("add_core", 0),
    ("add_core", 1),
    ("add_first", 0),
    ("add_core", 2),
    ("add_first", 1),
    ("add_second", 0),
    ("add_core", 3),
    ("add_first", 2),
    ("add_second", 1),
    ("add_first", 3),
    ("add_second", 2),
    ("add_second", 3),
)


def late_kernel(rows, pieces_ref, table_ref, out_ref, total_ref, *scratch):
    reducer = Reducer(mesh_ids(), rows, pieces_ref, *scratch[:5], scratch[5:8])
    kept, arrived, sends, recvs = scratch[8:]
    z, y, x, core = mesh_ids()
    dp, seq = lax.axis_index("dp"), lax.axis_index("seq")
    flip_low = z + 1 - 2 * lax.rem(z, 2)
    flip_high = lax.rem(z + 2, 4)
    partners = (
        (dp, x * 2 + 1 - core),
        (dp, (1 - x) * 2 + core),
        (z * 2 + 1 - y, seq),
        (flip_low * 2 + y, seq),
        (flip_high * 2 + y, seq),
    )

    def table_copy(stage):
        return pltpu.make_async_remote_copy(
            src_ref=kept.at[stage],
            dst_ref=arrived.at[stage],
            send_sem=sends.at[stage],
            recv_sem=recvs.at[stage],
            device_id=partners[stage],
            device_id_type=pl.DeviceIdType.MESH,
        )

    meet(reducer.partners())
    reducer.start()
    kept[0] = table_ref[...]
    table_copy(0).start()
    for number, (act, chunk) in enumerate(LATE_PLAN):
        getattr(reducer, act)(chunk)
        if number % 2 == 1:
            stage = number // 2
            if stage < 5:
                table_copy(stage).wait_recv()
                kept[stage + 1] = kept[stage] + arrived[stage]
            if stage < 4:
                table_copy(stage + 1).start()
    total_ref[...] = kept[5]
    reducer.finish(out_ref)
    for stage in range(5):
        table_copy(stage).wait_send()


def reduce_late(pieces, table):
    rows, width = pieces.shape[-2:]
    whole = pl.BlockSpec(memory_space=pltpu.VMEM)
    return pl.pallas_call(
        functools.partial(late_kernel, rows),
        in_specs=[pl.BlockSpec(memory_space=pl.ANY), whole],
        out_specs=[whole, whole],
        out_shape=[
            jax.ShapeDtypeStruct((rows, width), F32),
            jax.ShapeDtypeStruct(table.shape, F32),
        ],
        scratch_shapes=Reducer.scratch(rows, width)
        + [
            pltpu.VMEM((6,) + table.shape, F32),
            pltpu.VMEM((5,) + table.shape, F32),
            pltpu.SemaphoreType.DMA((5,)),
            pltpu.SemaphoreType.DMA((5,)),
        ],
        compiler_params=pltpu.CompilerParams(
            collective_id=2, has_side_effects=True, vmem_limit_bytes=40 * 2**20
        ),
        name="reduce_late",
    )(pieces, table)


def has_plan():
    return (lax.axis_size("dp"), lax.axis_size("seq")) == (8, 4)


def by_core(parts):
    return parts.astype(BF16).reshape((4, 2, 2, 2) + parts.shape[1:]).transpose(3, 0, 1, 2, 4, 5)


def scattered(parts):
    return lax.psum_scatter(
        parts.astype(BF16), ("dp", "seq"), scatter_dimension=0, tiled=True
    )[0].astype(F32)


class BackSizes(NamedTuple):
    block: int
    count: int
    quarter: int
    seq_count: int
    pairs: int
    early_rows: int


def back_kernel(
    sizes,
    len_ref,
    tab_ref,
    q_ref,
    kx_ref,
    vx_ref,
    kg_ref,
    vg_ref,
    o_ref,
    do_ref,
    l_ref,
    doq_ref,
    ldq_ref,
    *rest,
):
    block, count, quarter, seq_count, pairs, early_rows = sizes
    reduces = early_rows > 0
    if reduces:
        pieces_ref, rest = rest[0], rest[1:]
    dq_ref, dk_ref, dv_ref, dtab_ref, *rest = rest
    if reduces:
        early_ref, rest = rest[0], rest[1:]
    (
        dkx,
        dvx,
        dkg,
        dvg,
        glob_send,
        glob_recv,
        halo_send,
        halo_recv,
        dog_all,
        ld_all,
        every_sends,
        every_recvs,
        glob_sends,
        glob_recvs,
        halo_sends,
        halo_recvs,
        *rest,
    ) = rest
    number = pl.program_id(0)
    pair = lax.rem(number, pairs)
    seq_index = lax.axis_index("seq")
    reducer = Reducer(mesh_ids(), early_rows, pieces_ref, *rest[:5], rest[5:]) if reduces else None
    scale = HD ** (-0.5)
    low_lanes = lane_index() < HD
    own_keys = slice(HALO, HALO + block)
    own_rows = pl.ds(pl.multiple_of(seq_index * quarter, quarter), quarter)

    def every_copies():
        for step in range(1, seq_count):
            for kind, (source, dest) in enumerate(((doq_ref, dog_all), (ldq_ref, ld_all))):
                yield pltpu.make_async_remote_copy(
                    src_ref=source,
                    dst_ref=dest.at[seq_index],
                    send_sem=every_sends.at[kind, step - 1],
                    recv_sem=every_recvs.at[kind, step - 1],
                    device_id=seq_device(step, seq_count),
                    device_id_type=pl.DeviceIdType.MESH,
                )

    def glob_copies(at):
        for step in range(1, seq_count):
            device = seq_device(step, seq_count)
            yield pltpu.make_async_remote_copy(
                src_ref=glob_send.at[device[1], at],
                dst_ref=glob_recv.at[step - 1, at],
                send_sem=glob_sends.at[step - 1, at],
                recv_sem=glob_recvs.at[step - 1, at],
                device_id=device,
                device_id_type=pl.DeviceIdType.MESH,
            )

    def halo_copy(direction):
        return pltpu.make_async_remote_copy(
            src_ref=halo_send.at[direction],
            dst_ref=halo_recv.at[direction],
            send_sem=halo_sends.at[direction],
            recv_sem=halo_recvs.at[direction],
            device_id=seq_device(2 * direction - 1, seq_count),
            device_id_type=pl.DeviceIdType.MESH,
        )

    has_low, has_high = seq_index > 0, seq_index < seq_count - 1
    sends_to = (has_low, has_high)
    gets_from = (has_high, has_low)

    @pl.when(number == 0)
    def _():
        others = [seq_device(step, seq_count) for step in range(1, seq_count)]
        meet(others + (reducer.partners()[2:] if reduces else []))
        for copy in every_copies():
            copy.start()
        if reduces:
            reducer.start()
        dog_all[seq_index] = doq_ref[...]
        ld_all[seq_index] = ldq_ref[...]

    if reduces:
        for at, act, chunk in EARLY_PLAN:

            @pl.when(number == at)
            def _(act=act, chunk=chunk):
                getattr(reducer, act)(chunk)

    @pl.when(number < pairs)
    def _():
        long_bias = key_bias(seq_index * block - HALO, block + 2 * HALO, len_ref[0])
        glob_bias = key_bias(0, GP, count)
        query = q_ref[:block] * jnp.asarray(scale, BF16)
        grad_o = do_ref[...]
        both = grad_o.astype(F32) * o_ref[...].astype(F32)
        heads = []
        for head in range(2):
            norm = in_three(-pick_column(l_ref[...], 2 * pair + head))
            delta = in_three(-jnp.sum(own_half(head, both), -1, keepdims=True))
            heads.append(
                dict(
                    q=own_half(head, query),
                    do=own_half(head, grad_o),
                    qa=with_lanes(head, query, (1.0,) + norm),
                    doa=with_lanes(head, grad_o, delta),
                    kxa=key_side(head, kx_ref[...], long_bias),
                    vxa=value_side(head, vx_ref[...]),
                    kga=key_side(head, kg_ref[...], glob_bias),
                    vga=value_side(head, vg_ref[...]),
                    bias=band_bias(tab_ref[0, head : head + 1]),
                )
            )
        dkx[pair] = jnp.zeros_like(dkx[pair])
        dvx[pair] = jnp.zeros_like(dvx[pair])
        table_sums = [0.0, 0.0]
        grads_q = []
        for start in range(0, block, SUB):
            rows, keys = slice(start, start + SUB), slice(start, start + WINDOW)
            outs, probs, grads = [], [], []
            for head, own in enumerate(heads):
                band = jnp.exp(dot_t(own["qa"][rows], own["kxa"][keys]) + own["bias"])
                band_ds = band * dot_t(own["doa"][rows], own["vxa"][keys])
                table_sums[head] += band_ds
                glob = jnp.exp(dot_t(own["qa"][rows], own["kga"]))
                glob_ds = (glob * dot_t(own["doa"][rows], own["vga"])).astype(BF16)
                band_ds = band_ds.astype(BF16)
                outs.append(dot_n(band_ds, kx_ref[keys]) + dot_n(glob_ds, kg_ref[...]))
                probs.append((band.astype(BF16), glob.astype(BF16)))
                grads.append((band_ds, glob_ds))
            grads_q.append(jnp.where(low_lanes, outs[0], outs[1]))
            own_q = jnp.concatenate([own["q"][rows] for own in heads], 0)
            own_do = jnp.concatenate([own["do"][rows] for own in heads], 0)
            band, glob = (jnp.concatenate(part, 0) for part in zip(*probs))
            band_ds, glob_ds = (jnp.concatenate(part, 0) for part in zip(*grads))
            dkx[pair, keys] += t_dot(band_ds, own_q)
            dvx[pair, keys] += t_dot(band, own_do)
            more_k, more_v = t_dot(glob_ds, own_q), t_dot(glob, own_do)
            dkg[pair] = more_k if start == 0 else dkg[pair] + more_k
            dvg[pair] = more_v if start == 0 else dvg[pair] + more_v
        dq_ref[:block, lanes_of(pair)] = (jnp.concatenate(grads_q, 0) * scale).astype(BF16)
        for head in range(2):
            dtab_ref[pair, head : head + 1] = diagonal_sums(table_sums[head])

    @pl.when(number == pairs)
    def _():
        for kind, total in enumerate((dkx, dvx)):
            for direction, first in enumerate((HALO - REACH, HALO + block)):
                halo_send[direction, kind] = total[:, first : first + REACH].astype(BF16)
        for direction in range(2):

            @pl.when(sends_to[direction])
            def _(direction=direction):
                halo_copy(direction).start()

        for copy in every_copies():
            copy.wait_recv()

    @pl.when(number >= pairs)
    def _():
        long_bias = key_bias(seq_index * block, block, len_ref[0])
        near_bias = key_bias(seq_index * quarter, quarter, count)
        query = q_ref[block:] * jnp.asarray(scale, BF16)
        grad_o = dog_all[:, :, lanes_of(pair)].reshape(GP, PAIR)
        stats = ld_all[...].reshape(GP, PAIR)
        far_k, far_v = kx_ref[own_keys], vx_ref[own_keys]
        near_k, near_v = kg_ref[own_rows], vg_ref[own_rows]
        outs, kept = [], []
        for head in range(2):
            norm = in_three(-pick_column(stats, 2 * pair + head))
            delta = in_three(-pick_column(stats, HD + 2 * pair + head))
            qa = with_lanes(head, query, (1.0,) + norm)
            doa = with_lanes(head, grad_o, delta)
            far = jnp.exp(dot_t(qa, key_side(head, far_k, long_bias)))
            near = jnp.exp(dot_t(qa, key_side(head, near_k, near_bias)))
            far_ds = (far * dot_t(doa, value_side(head, far_v))).astype(BF16)
            near_ds = (near * dot_t(doa, value_side(head, near_v))).astype(BF16)
            outs.append(dot_n(far_ds, far_k) + dot_n(near_ds, near_k))
            kept.append(
                (
                    own_half(head, query),
                    own_half(head, grad_o),
                    far.astype(BF16),
                    near.astype(BF16),
                    far_ds,
                    near_ds,
                )
            )
        own_q, own_do, far, near, far_ds, near_ds = (
            jnp.concatenate(part, 0) for part in zip(*kept)
        )
        dkx[pair, own_keys] += t_dot(far_ds, own_q)
        dvx[pair, own_keys] += t_dot(far, own_do)
        dkg[pair, own_rows] += t_dot(near_ds, own_q)
        dvg[pair, own_rows] += t_dot(near, own_do)
        glob_dq = jnp.where(low_lanes, outs[0], outs[1]) * scale
        for at, grad in enumerate((glob_dq, dkg[pair], dvg[pair])):
            glob_send[:, pair, :, at * PAIR : (at + 1) * PAIR] = grad.astype(BF16).reshape(
                seq_count, quarter, PAIR
            )
        for copy in glob_copies(pair):
            copy.start()

    @pl.when(number == 2 * pairs - 1)
    def _():
        for direction in range(2):

            @pl.when(gets_from[direction])
            def _(direction=direction):
                halo_copy(direction).wait_recv()

            @pl.when(jnp.logical_not(gets_from[direction]))
            def _(direction=direction):
                halo_recv[direction] = jnp.zeros_like(halo_recv[direction])

        for at in range(pairs):
            lanes = slice(at * PAIR, (at + 1) * PAIR)
            for kind, (total, out) in enumerate(((dkx, dk_ref), (dvx, dv_ref))):
                first, last = HALO + REACH, HALO + block - REACH
                out[:REACH, lanes] = (
                    total[at, HALO:first] + halo_recv[1, kind, at].astype(F32)
                ).astype(BF16)
                out[REACH : block - REACH, lanes] = total[at, first:last].astype(BF16)
                out[block - REACH : block, lanes] = (
                    total[at, last : HALO + block] + halo_recv[0, kind, at].astype(F32)
                ).astype(BF16)
        for at in range(pairs):
            lanes = slice(at * PAIR, (at + 1) * PAIR)
            total = glob_send[seq_index, at].astype(F32)
            for step, copy in enumerate(glob_copies(at)):
                copy.wait_recv()
                total += glob_recv[step, at].astype(F32)
            for kind, out in enumerate((dq_ref, dk_ref, dv_ref)):
                out[block:, lanes] = total[:, kind * PAIR : (kind + 1) * PAIR].astype(BF16)
        for at in range(pairs):
            for copy in glob_copies(at):
                copy.wait_send()
        for copy in every_copies():
            copy.wait_send()
        for direction in range(2):

            @pl.when(sends_to[direction])
            def _(direction=direction):
                halo_copy(direction).wait_send()

        if reduces:
            reducer.finish(early_ref)


def attend_back(sizes, doc_len, table, q, kx, vx, kg, vg, o, do, l, doq, ldq, pieces=None):
    block, count, quarter, seq_count, pairs, early_rows = sizes
    width = q.shape[1]
    ext = block + 2 * HALO
    cols = lambda rows: pl.BlockSpec((rows, PAIR), lambda i: (0, lax.rem(i, pairs)))
    whole = pl.BlockSpec(memory_space=pltpu.VMEM)
    shape = jax.ShapeDtypeStruct
    in_specs = [
        pl.BlockSpec(memory_space=pltpu.SMEM),
        pl.BlockSpec((1, 2, WINDOW), lambda i: (lax.rem(i, pairs), 0, 0)),
        cols(block + GP),
        cols(ext),
        cols(ext),
        cols(GP),
        cols(GP),
        cols(block),
        cols(block),
        whole,
        whole,
        whole,
    ]
    rows = block + quarter
    outs = [shape((rows, width), BF16)] * 3 + [shape((pairs, 2, WINDOW), F32)]
    others = seq_count - 1
    scratch = [
        pltpu.VMEM((pairs, ext, PAIR), F32),
        pltpu.VMEM((pairs, ext, PAIR), F32),
        pltpu.VMEM((pairs, GP, PAIR), F32),
        pltpu.VMEM((pairs, GP, PAIR), F32),
        pltpu.VMEM((seq_count, pairs, quarter, 3 * PAIR), BF16),
        pltpu.VMEM((others, pairs, quarter, 3 * PAIR), BF16),
        pltpu.VMEM((2, 2, pairs, REACH, PAIR), BF16),
        pltpu.VMEM((2, 2, pairs, REACH, PAIR), BF16),
        pltpu.VMEM((seq_count, quarter, width), BF16),
        pltpu.VMEM((seq_count, quarter, PAIR), F32),
        pltpu.SemaphoreType.DMA((2, others)),
        pltpu.SemaphoreType.DMA((2, others)),
        pltpu.SemaphoreType.DMA((others, pairs)),
        pltpu.SemaphoreType.DMA((others, pairs)),
        pltpu.SemaphoreType.DMA((2,)),
        pltpu.SemaphoreType.DMA((2,)),
    ]
    args = [doc_len, table, q, kx, vx, kg, vg, o, do, l, doq, ldq]
    if early_rows:
        in_specs.append(pl.BlockSpec(memory_space=pl.ANY))
        outs.append(shape((early_rows, width), F32))
        scratch += Reducer.scratch(early_rows, width)
        args.append(pieces)
    return pl.pallas_call(
        functools.partial(back_kernel, sizes),
        grid=(2 * pairs,),
        in_specs=in_specs,
        out_specs=[whole] * len(outs),
        out_shape=outs,
        scratch_shapes=scratch,
        compiler_params=pltpu.CompilerParams(
            collective_id=1, has_side_effects=True, vmem_limit_bytes=60 * 2**20
        ),
        name="attend_back",
    )(*args)


def matmul(left, right):
    return jnp.dot(left, right, preferred_element_type=F32)


def rows_dot(left, right):
    return jnp.einsum("rd,re->de", left, right, preferred_element_type=F32)


def back_dot(left, right):
    return lax.dot_general(left, right, (((1,), (1,)), ((), ())), preferred_element_type=F32)


def on_device(
    long_input,
    global_input,
    lengths,
    w_query,
    b_query,
    w_key,
    w_value,
    b_value,
    w_out,
    b_out,
    w_inner,
    b_inner,
    w_outer,
    b_outer,
    norm1_gain,
    norm1_shift,
    norm2_gain,
    norm2_shift,
    rel_table,
    long_cotangent,
    global_cotangent,
):
    seq_count = lax.axis_size("seq")
    data_count = lax.axis_size("dp")
    seq_index = lax.axis_index("seq")
    block = long_input.shape[1]
    count = global_input.shape[1]
    width = long_input.shape[2]
    heads = rel_table.shape[1]
    pairs = heads // 2
    labels = 2 * R + 1
    quarter = GP // seq_count
    sizes = Sizes(block, count, quarter, seq_count, pairs)
    row_valid = (seq_index * block + jnp.arange(block, dtype=jnp.int32)) < lengths[0]
    table = jnp.pad(
        rel_table.T,
        ((0, 0), (HALO - R, WINDOW - labels - HALO + R)),
        constant_values=MASKED,
    ).reshape(pairs, 2, WINDOW)

    glob_x = jnp.pad(global_input[0], ((0, GP - count), (0, 0)))
    glob_dy = jnp.pad(global_cotangent[0], ((0, GP - count), (0, 0)))
    own_glob = lambda a: lax.dynamic_slice_in_dim(a, seq_index * quarter, quarter, 0)
    own_x = jnp.concatenate([long_input[0], own_glob(glob_x)], 0).astype(F32)
    queries, kx, vx, kg, vg, attn_low, long_l, glob_l = attend(
        sizes,
        lengths,
        table,
        long_input[0],
        glob_x,
        w_query,
        w_key,
        w_value,
        b_query[None],
        b_value[None],
        norm1_gain[None],
        norm1_shift[None],
    )

    residual_mid = own_x + matmul(attn_low, w_out) + b_out
    normed_two, hat_two, inv_two = norm_forward(residual_mid, norm2_gain, norm2_shift)
    normed_two_low = normed_two.astype(BF16)
    hidden_pre = matmul(normed_two_low, w_inner) + b_inner
    activated, gelu_back = jax.vjp(smooth_gate, hidden_pre)
    activated_low = activated.astype(BF16)
    result = residual_mid + matmul(activated_low, w_outer) + b_outer
    long_result = jnp.where(row_valid[:, None], result[:block], 0.0).astype(BF16)
    grad_y_low = jnp.concatenate(
        [
            jnp.where(row_valid[:, None], long_cotangent[0], jnp.zeros_like(long_cotangent[0])),
            own_glob(glob_dy),
        ],
        0,
    )
    grad_y = grad_y_low.astype(F32)
    grad_b_outer = jnp.sum(grad_y, 0)
    grad_w_outer = rows_dot(activated_low, grad_y_low)
    (grad_hidden,) = gelu_back(back_dot(grad_y_low, w_outer))
    grad_b_inner = jnp.sum(grad_hidden, 0)
    hidden_low = grad_hidden.astype(BF16)
    grad_w_inner = rows_dot(normed_two_low, hidden_low)
    grad_from_two, grad_gain_two, grad_shift_two = norm_backward(
        back_dot(hidden_low, w_inner), hat_two, inv_two, norm2_gain
    )
    grad_mid = grad_y + grad_from_two
    grad_b_out = jnp.sum(grad_mid, 0)
    grad_mid_low = grad_mid.astype(BF16)
    grad_w_out = rows_dot(attn_low, grad_mid_low)
    grad_attn = back_dot(grad_mid_low, w_out).astype(BF16)

    glob_do = grad_attn[block:]
    glob_o = attn_low[block:].astype(F32)
    glob_delta = jnp.sum((glob_do.astype(F32) * glob_o).reshape(quarter, heads, HD), -1)
    stats = jnp.concatenate(
        [glob_l[:, :HD], jnp.pad(glob_delta, ((0, 0), (0, HD - heads)))], 1
    )
    devices = data_count * seq_count
    piece = width // devices
    by_device = lambda grad: grad.reshape(devices, -1, width)

    def wide(grad):
        blocks = grad.reshape(devices, piece, -1, width)
        return blocks.transpose(0, 2, 1, 3).reshape(devices, -1, width)

    inner_rows = wide(grad_w_inner).shape[1]
    early_parts = jnp.concatenate([by_device(grad_w_outer), wide(grad_w_inner)], 1)
    planned = has_plan()
    sizes = BackSizes(
        block, count, quarter, seq_count, pairs, early_parts.shape[1] if planned else 0
    )
    query_low, key_low, value_low, dtab, *early = attend_back(
        sizes,
        lengths,
        table,
        queries,
        kx,
        vx,
        kg,
        vg,
        attn_low[:block],
        grad_attn[:block],
        long_l,
        glob_do,
        stats,
        *([by_core(early_parts)] if planned else []),
    )
    early = early[0] if planned else scattered(early_parts)
    own_normed, hat_one, inv_one = norm_forward(own_x, norm1_gain, norm1_shift)
    own_normed = own_normed.astype(BF16)
    grad_b_query = jnp.sum(query_low.astype(F32), 0)
    grad_b_value = jnp.sum(value_low.astype(F32), 0)
    grad_w_query = rows_dot(own_normed, query_low)
    grad_w_key = rows_dot(own_normed, key_low)
    grad_w_value = rows_dot(own_normed, value_low)
    grad_normed_one = (
        back_dot(query_low, w_query) + back_dot(key_low, w_key) + back_dot(value_low, w_value)
    )
    grad_from_one, grad_gain_one, grad_shift_one = norm_backward(
        grad_normed_one, hat_one, inv_one, norm1_gain
    )
    grad_x = grad_mid + grad_from_one

    g_outer = early[:-inner_rows]
    g_inner = early[-inner_rows:].reshape(-1, piece, width).transpose(1, 0, 2)
    vectors = (
        grad_b_query,
        grad_b_value,
        grad_b_out,
        grad_b_inner,
        grad_b_outer,
        grad_gain_one,
        grad_shift_one,
        grad_gain_two,
        grad_shift_two,
    )
    small = jnp.concatenate([v.reshape(devices, -1) for v in vectors], 1)
    small = jnp.pad(small, ((0, 0), (0, width - small.shape[1])))
    small = jnp.pad(small[:, None], ((0, 0), (0, 15), (0, 0)))
    late_parts = jnp.concatenate(
        [by_device(g) for g in (grad_w_query, grad_w_key, grad_w_value, grad_w_out)] + [small], 1
    )
    table_part = dtab.reshape(heads, WINDOW)
    if planned:
        late, table_total = reduce_late(by_core(late_parts), table_part)
    else:
        late, table_total = scattered(late_parts), lax.psum(table_part, ("dp", "seq"))
    table_total = table_total[:, HALO - R : HALO - R + labels].T
    pieces, at = [], 0
    for vector in vectors:
        length = vector.shape[0] // devices
        pieces.append(late[4 * piece, at : at + length])
        at += length
    g_b_query, g_b_value, g_b_out, g_b_inner, g_b_outer, g_g1, g_s1, g_g2, g_s2 = pieces
    g_query, g_key, g_value, g_out = (late[i * piece : (i + 1) * piece] for i in range(4))
    glob_out = lax.all_gather(result[block:].astype(BF16), "seq", axis=0, tiled=True)[:count]
    glob_grad = lax.all_gather(grad_x[block:], "seq", axis=0, tiled=True)[:count]
    return (
        long_result[None],
        glob_out[None],
        grad_x[:block][None],
        glob_grad[None],
        g_query,
        g_b_query,
        g_key,
        g_value,
        g_b_value,
        g_out,
        g_b_out,
        g_inner.reshape(piece, -1),
        g_b_inner,
        g_outer,
        g_b_outer,
        g_g1,
        g_s1,
        g_g2,
        g_s2,
        table_total,
    )


def solution(mesh):
    rows, whole = P("dp", "seq", None), P("dp", None, None)
    matrix, vector = P(("dp", "seq"), None), P(("dp", "seq"))
    return jax.shard_map(
        on_device,
        mesh=mesh,
        in_specs=(rows, whole, P("dp")) + (P(),) * 16 + (rows, whole),
        out_specs=(
            rows,
            whole,
            rows,
            whole,
            matrix,
            vector,
            matrix,
            matrix,
            vector,
            matrix,
            vector,
            matrix,
            vector,
            matrix,
            vector,
            vector,
            vector,
            vector,
            vector,
            P(),
        ),
        check_vma=False,
    )
```

```python
import functools
from typing import NamedTuple

import jax
import jax.numpy as jnp
from jax import lax
from jax.experimental import pallas as pl
from jax.experimental.pallas import tpu as pltpu
from jax.sharding import PartitionSpec as P

HD = 64
R = 84
PAIR = 2 * HD
HALO = 128
REACH = 96
GP = 256
SUB = 256
WINDOW = SUB + 2 * HALO
EPSILON = 1e-05
MASKED = -1e30
F32 = jnp.float32
BF16 = jnp.bfloat16


def norm_forward(values, gain, shift):
    average = jnp.mean(values, -1, keepdims=True)
    centred = values - average
    variance = jnp.mean(centred * centred, -1, keepdims=True)
    inverse = lax.rsqrt(variance + EPSILON)
    normed = centred * inverse
    return (normed * gain + shift, normed, inverse)


def norm_backward(grad_rows, normed, inverse, gain):
    scaled = grad_rows * gain
    grad_in = inverse * (
        scaled
        - jnp.mean(scaled, -1, keepdims=True)
        - normed * jnp.mean(scaled * normed, -1, keepdims=True)
    )
    return (grad_in, jnp.sum(grad_rows * normed, 0), jnp.sum(grad_rows, 0))


def smooth_gate(values):
    return jax.nn.gelu(values, approximate=True)


def dot_t(left, right):
    return lax.dot_general(left, right, (((1,), (1,)), ((), ())), preferred_element_type=F32)


def dot_n(left, right):
    return lax.dot_general(left, right, (((1,), (0,)), ((), ())), preferred_element_type=F32)


def t_dot(left, right):
    return lax.dot_general(left, right, (((0,), (0,)), ((), ())), preferred_element_type=F32)


def band_bias(table_row):
    spread = jnp.broadcast_to(table_row, (SUB, WINDOW))
    return pltpu.roll(spread, 0, 1, stride=1, stride_axis=0)


def diagonal_sums(rows):
    height, width = rows.shape
    while height > 8:
        height //= 2
        rows = rows[:height] + pltpu.roll(rows[height:], width - height, 1)
    row = lax.broadcasted_iota(jnp.int32, rows.shape, 0)
    for bit in (1, 2, 4):
        rows = jnp.where((row & bit) != 0, pltpu.roll(rows, width - bit, 1), rows)
    return jnp.sum(rows, 0, keepdims=True)


def lane_index():
    return lax.broadcasted_iota(jnp.int32, (1, PAIR), 1)


def own_half(head, value):
    low_lanes = lane_index() < HD
    return jnp.where(low_lanes if head == 0 else ~low_lanes, value, jnp.zeros_like(value))


def other_lane(head):
    return HD * (1 - head)


def with_lanes(head, value, columns):
    wide = own_half(head, value.astype(F32))
    lane = lane_index()
    for offset, column in enumerate(columns):
        wide = jnp.where(lane == other_lane(head) + offset, column, wide)
    return wide.astype(BF16)


def in_three(column):
    high = column.astype(BF16).astype(F32)
    middle = (column - high).astype(BF16).astype(F32)
    return (high, middle, column - high - middle)


def key_bias(first, rows, end):
    position = first + lax.broadcasted_iota(jnp.int32, (rows, 1), 0)
    return jnp.where((position >= 0) & (position < end), 0.0, MASKED)


def pick_column(rows, index):
    return jnp.sum(jnp.where(lane_index() == index, rows, 0.0), -1, keepdims=True)


def key_side(head, keys, bias):
    return with_lanes(head, keys, (bias, 1.0, 1.0, 1.0))


def value_side(head, values):
    return with_lanes(head, values, (1.0, 1.0, 1.0))


def softmax_rows(parts, value_parts, head):
    top = functools.reduce(
        jnp.maximum, [jnp.max(part, -1, keepdims=True) for part in parts]
    )
    mixed = sum(
        dot_n(jnp.exp(part - top).astype(BF16), values)
        for part, values in zip(parts, value_parts)
    )
    at = other_lane(head)
    total = mixed[:, at : at + 1]
    return mixed / total, top + jnp.log(total)


def seq_device(steps, seq_count):
    return (lax.axis_index("dp"), lax.rem(lax.axis_index("seq") + steps + seq_count, seq_count))


def row_norm(rows):
    centred = rows - jnp.mean(rows, -1, keepdims=True)
    inverse = lax.rsqrt(jnp.mean(centred * centred, -1, keepdims=True) + EPSILON)
    return centred * inverse, inverse


def put_column(ref, rows, index, column):
    ref[rows] = jnp.where(lane_index() == index, column, ref[rows])


def lanes_of(at):
    return pl.ds(pl.multiple_of(at * PAIR, PAIR), PAIR)


class Sizes(NamedTuple):
    block: int
    count: int
    quarter: int
    seq_count: int
    pairs: int


def attend_kernel(
    sizes,
    len_ref,
    tab_ref,
    long_ref,
    glob_ref,
    wq_ref,
    wk_ref,
    wv_ref,
    bq_ref,
    bv_ref,
    gain_ref,
    shift_ref,
    q_ref,
    kx_ref,
    vx_ref,
    kg_ref,
    vg_ref,
    o_ref,
    l_ref,
    lq_ref,
    part_o,
    part_l,
    from_o,
    from_l,
    halo_sends,
    halo_recvs,
    part_sends,
    part_recvs,
):
    block, count, quarter, seq_count, pairs = sizes
    ext = block + 2 * HALO
    seq_index = lax.axis_index("seq")
    scale = jnp.asarray(HD ** (-0.5), BF16)
    low_lanes = lane_index() < HD
    own_keys = slice(HALO, HALO + block)
    own_rows = pl.ds(pl.multiple_of(seq_index * quarter, quarter), quarter)
    neighbours = (seq_index > 0, seq_index < seq_count - 1)
    barrier = pltpu.get_barrier_semaphore()
    for step in range(1, seq_count):
        pl.semaphore_signal(
            barrier,
            inc=1,
            device_id=seq_device(step, seq_count),
            device_id_type=pl.DeviceIdType.MESH,
        )

    def halo_copies(direction):
        source = HALO if direction == 0 else HALO + block - REACH
        dest = HALO + block if direction == 0 else HALO - REACH
        for kind, ref in enumerate((kx_ref, vx_ref)):
            yield pltpu.make_async_remote_copy(
                src_ref=ref.at[source : source + REACH],
                dst_ref=ref.at[dest : dest + REACH],
                send_sem=halo_sends.at[direction, kind],
                recv_sem=halo_recvs.at[direction, kind],
                device_id=seq_device(2 * direction - 1, seq_count),
                device_id_type=pl.DeviceIdType.MESH,
            )

    def part_copies():
        for step in range(1, seq_count):
            device = seq_device(step, seq_count)
            rows = pl.ds(pl.multiple_of(device[1] * quarter, quarter), quarter)
            for kind, (source, dest) in enumerate(((part_o, from_o), (part_l, from_l))):
                yield step, kind, pltpu.make_async_remote_copy(
                    src_ref=source.at[rows],
                    dst_ref=dest.at[step - 1],
                    send_sem=part_sends.at[kind, step - 1],
                    recv_sem=part_recvs.at[kind, step - 1],
                    device_id=device,
                    device_id_type=pl.DeviceIdType.MESH,
                )

    gain, shift = gain_ref[...], shift_ref[...]
    normed_long = (row_norm(long_ref[...].astype(F32))[0] * gain + shift).astype(BF16)
    kx_ref[own_keys] = dot_n(normed_long, wk_ref[...]).astype(BF16)
    vx_ref[own_keys] = (dot_n(normed_long, wv_ref[...]) + bv_ref[...]).astype(BF16)
    pl.semaphore_wait(barrier, seq_count - 1)
    for direction, first in enumerate((HALO - REACH, HALO + block)):

        @pl.when(neighbours[direction])
        def _(direction=direction):
            for copy in halo_copies(direction):
                copy.start()

        outer = slice(0, first) if direction == 0 else slice(first + REACH, ext)
        for ref in (kx_ref, vx_ref):
            ref[outer] = jnp.zeros((HALO - REACH, ref.shape[1]), BF16)

        @pl.when(jnp.logical_not(neighbours[direction]))
        def _(first=first):
            for ref in (kx_ref, vx_ref):
                ref[first : first + REACH] = jnp.zeros((REACH, ref.shape[1]), BF16)

    normed_glob = (row_norm(glob_ref[...].astype(F32))[0] * gain + shift).astype(BF16)
    kg_ref[...] = dot_n(normed_glob, wk_ref[...]).astype(BF16)
    vg_ref[...] = (dot_n(normed_glob, wv_ref[...]) + bv_ref[...]).astype(BF16)
    q_ref[block:] = (dot_n(normed_glob, wq_ref[...]) + bq_ref[...]).astype(BF16)
    q_ref[:block] = (dot_n(normed_long, wq_ref[...]) + bq_ref[...]).astype(BF16)
    part_l[...] = jnp.zeros_like(part_l)
    l_ref[...] = jnp.zeros_like(l_ref)

    def glob_pair(pair, carry):
        lanes = lanes_of(pair)
        far_bias = key_bias(seq_index * block, block, len_ref[0])
        near_bias = key_bias(seq_index * quarter, quarter, count)
        query = q_ref[block:, lanes] * scale
        outs = []
        for head in range(2):
            q = with_lanes(head, query, (1.0,))
            far = dot_t(q, with_lanes(head, kx_ref[own_keys, lanes], (far_bias,)))
            near = dot_t(q, with_lanes(head, kg_ref[own_rows, lanes], (near_bias,)))
            out, norm = softmax_rows(
                [far, near],
                [
                    with_lanes(head, vx_ref[own_keys, lanes], (1.0,)),
                    with_lanes(head, vg_ref[own_rows, lanes], (1.0,)),
                ],
                head,
            )
            outs.append(out)
            put_column(part_l, slice(None), 2 * pair + head, norm)
        part_o[:, lanes] = jnp.where(low_lanes, outs[0], outs[1]).astype(BF16)
        return carry

    lax.fori_loop(0, pairs, glob_pair, 0)
    for _, _, copy in part_copies():
        copy.start()
    for direction in range(2):

        @pl.when(neighbours[1 - direction])
        def _(direction=direction):
            for copy in halo_copies(direction):
                copy.wait_recv()

    def long_pair(pair, carry):
        lanes = lanes_of(pair)
        long_bias = key_bias(seq_index * block - HALO, ext, len_ref[0])
        glob_bias = key_bias(0, GP, count)
        query = q_ref[:block, lanes] * scale
        outs = []
        for head in range(2):
            q = with_lanes(head, query, (1.0,))
            kx = with_lanes(head, kx_ref[:, lanes], (long_bias,))
            kg = with_lanes(head, kg_ref[:, lanes], (glob_bias,))
            vx, vg = (with_lanes(head, ref[:, lanes], (1.0,)) for ref in (vx_ref, vg_ref))
            bias = band_bias(tab_ref[pair, head : head + 1])
            mixed = []
            for start in range(0, block, SUB):
                rows, keys = slice(start, start + SUB), slice(start, start + WINDOW)
                out, norm = softmax_rows(
                    [dot_t(q[rows], kx[keys]) + bias, dot_t(q[rows], kg)], [vx[keys], vg], head
                )
                mixed.append(out)
                put_column(l_ref, rows, 2 * pair + head, norm)
            outs.append(jnp.concatenate(mixed, 0))
        o_ref[:block, lanes] = jnp.where(low_lanes, outs[0], outs[1]).astype(BF16)
        return carry

    lax.fori_loop(0, pairs, long_pair, 0)
    for _, _, copy in part_copies():
        copy.wait_recv()
    norms = [part_l[own_rows]] + [from_l[step] for step in range(seq_count - 1)]
    outs = [part_o[own_rows]] + [from_o[step] for step in range(seq_count - 1)]
    top = functools.reduce(jnp.maximum, norms)
    shares = [jnp.exp(norm - top) for norm in norms]
    total = sum(shares)
    lq_ref[...] = top + jnp.log(total)
    shares = [share / total for share in shares]
    for at in range(pairs):
        lanes = slice(at * PAIR, (at + 1) * PAIR)
        mixed = 0.0
        for share, out in zip(shares, outs):
            spread = jnp.where(
                low_lanes, share[:, 2 * at : 2 * at + 1], share[:, 2 * at + 1 : 2 * at + 2]
            )
            mixed += spread * out[:, lanes].astype(F32)
        o_ref[block:, lanes] = mixed.astype(BF16)
    for _, _, copy in part_copies():
        copy.wait_send()
    for direction in range(2):

        @pl.when(neighbours[direction])
        def _(direction=direction):
            for copy in halo_copies(direction):
                copy.wait_send()


def attend(sizes, doc_len, table, long_x, glob_x, *weights):
    block, count, quarter, seq_count, pairs = sizes
    width = long_x.shape[1]
    ext = block + 2 * HALO
    whole = pl.BlockSpec(memory_space=pltpu.VMEM)
    shape = jax.ShapeDtypeStruct
    others = seq_count - 1
    return pl.pallas_call(
        functools.partial(attend_kernel, sizes),
        in_specs=[pl.BlockSpec(memory_space=pltpu.SMEM)] + [whole] * 10,
        out_specs=[whole] * 8,
        out_shape=[
            shape((block + GP, width), BF16),
            shape((ext, width), BF16),
            shape((ext, width), BF16),
            shape((GP, width), BF16),
            shape((GP, width), BF16),
            shape((block + quarter, width), BF16),
            shape((block, PAIR), F32),
            shape((quarter, PAIR), F32),
        ],
        scratch_shapes=[
            pltpu.VMEM((GP, width), BF16),
            pltpu.VMEM((GP, PAIR), F32),
            pltpu.VMEM((others, quarter, width), BF16),
            pltpu.VMEM((others, quarter, PAIR), F32),
            pltpu.SemaphoreType.DMA((2, 2)),
            pltpu.SemaphoreType.DMA((2, 2)),
            pltpu.SemaphoreType.DMA((2, others)),
            pltpu.SemaphoreType.DMA((2, others)),
        ],
        compiler_params=pltpu.CompilerParams(
            collective_id=3, has_side_effects=True, vmem_limit_bytes=56 * 2**20
        ),
        name="attend",
    )(doc_len, table, long_x, glob_x, *weights)


class Reducer:
    def __init__(self, rows, scratch, pieces=None, outgoing=None):
        self.ids = mesh_ids()
        half = (rows // 2 + 15) // 16 * 16
        self.halves = (slice(0, half), slice(half, rows))
        self.pieces, self.outgoing = pieces, outgoing
        self.mine, self.from_core, self.from_one, self.from_two, self.from_z = scratch[:5]
        self.local, self.sends, self.recvs = scratch[5:]

    @staticmethod
    def scratch(rows, width):
        return [
            pltpu.VMEM((4, 2, 2, rows, width), BF16),
            pltpu.VMEM((4, 2, 2, rows, width), BF16),
            pltpu.VMEM((4, 2, rows, width), BF16),
            pltpu.VMEM((4, rows, width), BF16),
            pltpu.VMEM((3, rows, width), BF16),
            pltpu.SemaphoreType.DMA((4,)),
            pltpu.SemaphoreType.DMA((6, 4)),
            pltpu.SemaphoreType.DMA((6, 4)),
        ]

    def partners(self):
        z, y, x, core = self.ids
        dp, seq = z * 2 + y, x * 2 + core
        near = [(dp, x * 2 + 1 - core), (dp, (1 - x) * 2 + core), (z * 2 + 1 - y, seq)]
        return near + [(lax.rem(z + step, 4) * 2 + y, seq) for step in (1, 2, 3)]

    def target(self, chunk):
        return chunk if self.pieces is None else lax.rem(self.ids[0] + 1 + chunk, 4)

    def remote(self, source, dest, kind, send_at, recv_at, device):
        return pltpu.make_async_remote_copy(
            src_ref=source,
            dst_ref=dest,
            send_sem=self.sends.at[kind, send_at],
            recv_sem=self.recvs.at[kind, recv_at],
            device_id=device,
            device_id_type=pl.DeviceIdType.MESH,
        )

    def own_copy(self, chunk):
        core, to = self.ids[3], self.target(chunk)
        return pltpu.make_async_copy(
            self.pieces.at[core, to], self.mine.at[to], self.local.at[chunk]
        )

    def core_copy(self, chunk):
        core, to = self.ids[3], self.target(chunk)
        source = self.outgoing.at[to] if self.pieces is None else self.pieces.at[1 - core, to]
        return self.remote(source, self.from_core.at[to], 0, chunk, chunk, self.partners()[0])

    def first_copies(self, chunk):
        z, y, x, core = self.ids
        to = self.target(chunk)
        one, two = self.halves
        near = self.partners()
        return (
            self.remote(
                self.mine.at[to, :, 1 - x, one],
                self.from_one.at[to, :, one],
                1,
                chunk,
                chunk,
                near[1],
            ),
            self.remote(
                self.mine.at[to, 1 - y, :, two],
                self.from_one.at[to, :, two],
                2,
                chunk,
                chunk,
                near[2],
            ),
        )

    def second_copies(self, chunk):
        z, y, x, core = self.ids
        to = self.target(chunk)
        one, two = self.halves
        near = self.partners()
        return (
            self.remote(
                self.mine.at[to, 1 - y, x, one],
                self.from_two.at[to, one],
                3,
                chunk,
                chunk,
                near[2],
            ),
            self.remote(
                self.mine.at[to, y, 1 - x, two],
                self.from_two.at[to, two],
                4,
                chunk,
                chunk,
                near[1],
            ),
        )

    def last_copy(self, chunk):
        z, y, x, core = self.ids
        to = self.target(chunk)
        slot = lax.rem(z - to + 4, 4) - 1
        return self.remote(
            self.mine.at[to, y, x],
            self.from_z.at[slot],
            5,
            chunk,
            slot,
            (to * 2 + y, x * 2 + core),
        )

    def arrival(self, slot):
        z, y, x, core = self.ids
        return self.remote(
            self.mine.at[z, y, x], self.from_z.at[slot], 5, slot, slot, self.partners()[3]
        )

    def leaves(self, chunk):
        return chunk < 3 if self.pieces is not None else self.target(chunk) != self.ids[0]

    def start(self, chunk):
        self.core_copy(chunk).start()
        if self.pieces is not None:
            self.own_copy(chunk).start()

    def add_core(self, chunk):
        to = self.target(chunk)
        if self.pieces is not None:
            self.own_copy(chunk).wait()
        self.core_copy(chunk).wait_recv()

        def add(index, carry):
            at = (to, lax.div(index, 2), lax.rem(index, 2))
            self.mine[at] = (self.mine[at].astype(F32) + self.from_core[at].astype(F32)).astype(
                BF16
            )
            return carry

        lax.fori_loop(0, 4, add, 0)
        for copy in self.first_copies(chunk):
            copy.start()

    def add_first(self, chunk):
        z, y, x, core = self.ids
        one, two = self.halves
        to = self.target(chunk)
        for copy in self.first_copies(chunk):
            copy.wait_recv()

        def add(index, carry):
            for at, rows in (((to, index, x), one), ((to, y, index), two)):
                self.mine[at + (rows,)] = (
                    self.mine[at + (rows,)].astype(F32)
                    + self.from_one[to, index, rows].astype(F32)
                ).astype(BF16)
            return carry

        lax.fori_loop(0, 2, add, 0)
        for copy in self.second_copies(chunk):
            copy.start()

    def add_second(self, chunk):
        z, y, x, core = self.ids
        to = self.target(chunk)
        for copy in self.second_copies(chunk):
            copy.wait_recv()

        @pl.when(self.leaves(chunk))
        def _():
            self.mine[to, y, x] = (
                self.mine[to, y, x].astype(F32) + self.from_two[to].astype(F32)
            ).astype(BF16)
            self.last_copy(chunk).start()

    def finish(self, out):
        z, y, x, core = self.ids
        total = self.mine[z, y, x].astype(F32) + self.from_two[z].astype(F32)
        for slot in range(3):
            self.arrival(slot).wait_recv()
            total += self.from_z[slot].astype(F32)
        out[...] = total
        for chunk in range(4):
            self.core_copy(chunk).wait_send()
            for copy in self.first_copies(chunk) + self.second_copies(chunk):
                copy.wait_send()

            @pl.when(self.leaves(chunk))
            def _(chunk=chunk):
                self.last_copy(chunk).wait_send()


def mesh_ids():
    dp, seq = lax.axis_index("dp"), lax.axis_index("seq")
    return lax.div(dp, 2), lax.rem(dp, 2), lax.div(seq, 2), lax.rem(seq, 2)


def meet(devices):
    barrier = pltpu.get_barrier_semaphore()
    for device in devices:
        pl.semaphore_signal(barrier, inc=1, device_id=device, device_id_type=pl.DeviceIdType.MESH)
    pl.semaphore_wait(barrier, len(devices))


EARLY_PLAN = (
    (2, "add_core", 0),
    (3, "add_core", 1),
    (4, "add_core", 2),
    (5, "add_core", 3),
    (7, "add_first", 0),
    (8, "add_first", 1),
    (9, "add_second", 0),
    (10, "add_first", 2),
    (10, "add_second", 1),
    (11, "add_first", 3),
    (12, "add_second", 2),
    (12, "add_second", 3),
)
LATE_PLAN = (
    ("add_core", 0),
    ("add_core", 1),
    ("add_first", 0),
    ("add_core", 2),
    ("add_first", 1),
    ("add_second", 0),
    ("add_core", 3),
    ("add_first", 2),
    ("add_second", 1),
    ("add_first", 3),
    ("add_second", 2),
    ("add_second", 3),
)


def late_kernel(rows, pieces_ref, table_ref, out_ref, total_ref, *scratch):
    reducer = Reducer(rows, scratch[:8], pieces=pieces_ref)
    kept, arrived, sends, recvs = scratch[8:]
    z, y, x, core = mesh_ids()
    dp, seq = lax.axis_index("dp"), lax.axis_index("seq")
    flip_low = z + 1 - 2 * lax.rem(z, 2)
    flip_high = lax.rem(z + 2, 4)
    partners = (
        (dp, x * 2 + 1 - core),
        (dp, (1 - x) * 2 + core),
        (z * 2 + 1 - y, seq),
        (flip_low * 2 + y, seq),
        (flip_high * 2 + y, seq),
    )

    def table_copy(stage):
        return pltpu.make_async_remote_copy(
            src_ref=kept.at[stage],
            dst_ref=arrived.at[stage],
            send_sem=sends.at[stage],
            recv_sem=recvs.at[stage],
            device_id=partners[stage],
            device_id_type=pl.DeviceIdType.MESH,
        )

    meet(reducer.partners())
    for chunk in range(4):
        reducer.start(chunk)
    kept[0] = table_ref[...]
    table_copy(0).start()
    for number, (act, chunk) in enumerate(LATE_PLAN):
        getattr(reducer, act)(chunk)
        if number % 2 == 1:
            stage = number // 2
            if stage < 5:
                table_copy(stage).wait_recv()
                kept[stage + 1] = kept[stage] + arrived[stage]
            if stage < 4:
                table_copy(stage + 1).start()
    total_ref[...] = kept[5]
    reducer.finish(out_ref)
    for stage in range(5):
        table_copy(stage).wait_send()


def reduce_late(pieces, table):
    rows, width = pieces.shape[-2:]
    whole = pl.BlockSpec(memory_space=pltpu.VMEM)
    return pl.pallas_call(
        functools.partial(late_kernel, rows),
        in_specs=[pl.BlockSpec(memory_space=pl.ANY), whole],
        out_specs=[whole, whole],
        out_shape=[
            jax.ShapeDtypeStruct((rows, width), F32),
            jax.ShapeDtypeStruct(table.shape, F32),
        ],
        scratch_shapes=Reducer.scratch(rows, width)
        + [
            pltpu.VMEM((6,) + table.shape, F32),
            pltpu.VMEM((5,) + table.shape, F32),
            pltpu.SemaphoreType.DMA((5,)),
            pltpu.SemaphoreType.DMA((5,)),
        ],
        compiler_params=pltpu.CompilerParams(
            collective_id=2, has_side_effects=True, vmem_limit_bytes=40 * 2**20
        ),
        name="reduce_late",
    )(pieces, table)


def has_plan():
    return (lax.axis_size("dp"), lax.axis_size("seq")) == (8, 4)


def by_core(parts):
    return parts.astype(BF16).reshape((4, 2, 2, 2) + parts.shape[1:]).transpose(3, 0, 1, 2, 4, 5)


GELU_A = 0.7978845608028654
GELU_B = 0.044715


def gate_both(u):
    square = u * u
    turned = jnp.tanh(GELU_A * u * (1.0 + GELU_B * square))
    half = 0.5 * (1.0 + turned)
    slope = half + 0.5 * u * (1.0 - turned * turned) * (
        GELU_A * (1.0 + 3.0 * GELU_B * square)
    )
    return u * half, slope


def column_sum(rows):
    return jnp.sum(rows, 0, keepdims=True)


def ffn_kernel(
    sizes,
    planned,
    len_ref,
    attn_ref,
    long_ref,
    glob_ref,
    dlong_ref,
    dglob_ref,
    lq_ref,
    wo_ref,
    bo_ref,
    gain_ref,
    shift_ref,
    wi_ref,
    bi_ref,
    wr_ref,
    br_ref,
    long_out,
    glob_out,
    dmid_ref,
    do_ref,
    dog_ref,
    ldg_ref,
    *rest,
):
    block, count, quarter, seq_count, pairs = sizes
    if planned:
        pieces_ref, sum_ref, *rest = rest
    else:
        g_outer_ref, g_inner_ref, g_out_ref, vec_ref, *rest = rest
    (
        mid,
        y_sum,
        df_sum,
        normed,
        normed_t,
        dy,
        vectors,
        every_do,
        every_ld,
        every_out,
        gather_sends,
        gather_recvs,
        *rest,
    ) = rest
    if planned:
        even, odd, outgoing, *rest = rest
        reducer = Reducer(outgoing.shape[-2], rest, outgoing=outgoing)
    chunk = pl.program_id(0)
    seq_index = lax.axis_index("seq")
    own_rows = pl.ds(pl.multiple_of(seq_index * quarter, quarter), quarter)
    width = mid.shape[1]

    def gathers():
        for step in range(1, seq_count):
            for kind, every in enumerate((every_do, every_ld, every_out)):
                yield kind, pltpu.make_async_remote_copy(
                    src_ref=every.at[own_rows],
                    dst_ref=every.at[own_rows],
                    send_sem=gather_sends.at[kind, step - 1],
                    recv_sem=gather_recvs.at[kind, step - 1],
                    device_id=seq_device(step, seq_count),
                    device_id_type=pl.DeviceIdType.MESH,
                )

    @pl.when(chunk == 0)
    def _():
        others = [seq_device(step, seq_count) for step in range(1, seq_count)]
        meet(others + (reducer.partners()[2:] if planned else []))
        projected = dot_n(attn_ref[...], wo_ref[...]) + bo_ref[...]
        mid[:block] = long_ref[...].astype(F32) + projected[:block]
        mid[block:] = glob_ref[own_rows].astype(F32) + projected[block:]
        hat, _ = row_norm(mid[...])
        normed[...] = (hat * gain_ref[...] + shift_ref[...]).astype(BF16)
        normed_t[...] = normed[...].T
        y_sum[...] = mid[...] + br_ref[...]
        df_sum[...] = jnp.zeros_like(df_sum)
        position = seq_index * block + lax.broadcasted_iota(jnp.int32, (block, 1), 0)
        dy[:block] = jnp.where(
            position < len_ref[0], dlong_ref[...].astype(F32), 0.0
        ).astype(BF16)
        dy[block:] = dglob_ref[own_rows]
        vectors[1:2] = column_sum(dy[...].astype(F32))

    if planned:
        for now, act, at in OUTER_PLAN:

            @pl.when(chunk == now)
            def _(act=act, at=at):
                getattr(reducer, act)(at)

    active, slope = gate_both(dot_n(normed[...], wi_ref[...]) + bi_ref[...])
    active = active.astype(BF16)
    g_outer = t_dot(active, dy[...])
    if planned:
        core = reducer.ids[3]
        rows = g_outer.shape[0] // 8
        for part in range(4):
            for side in range(2):
                at = (2 * part + side) * rows
                value = g_outer[at : at + rows].astype(BF16)

                @pl.when(core == side)
                def _(part=part, value=value):
                    reducer.mine[chunk, part // 2, part % 2] = value

                @pl.when(core != side)
                def _(part=part, value=value):
                    outgoing[chunk, part // 2, part % 2] = value

        reducer.start(chunk)
    else:
        g_outer_ref[...] = g_outer.astype(BF16)
    y_sum[...] += dot_n(active, wr_ref[...])
    hidden = dot_t(dy[...], wr_ref[...]) * slope
    for at in range(4):

        @pl.when(chunk == at)
        def _(at=at):
            vectors[4 + at : 5 + at] = column_sum(hidden)

    hidden = hidden.astype(BF16)
    df_sum[...] += dot_t(hidden, wi_ref[...])
    g_inner = dot_n(normed_t[...], hidden)
    if planned:
        piece = width // 32
        for now in range(4):

            @pl.when(chunk == now)
            def _(now=now):
                (even, odd)[now % 2][...] = g_inner
                if now % 2 == 1:

                    def pack(at, carry):
                        rows = pl.ds(pl.multiple_of(at * piece, 8), piece)
                        where = (
                            lax.rem(at, 2),
                            lax.div(at, 8),
                            lax.rem(lax.div(at, 4), 2),
                            lax.rem(lax.div(at, 2), 2),
                        )
                        pieces_ref[where + (slice(now // 2 * 48, now // 2 * 48 + 48),)] = (
                            jnp.concatenate([even[rows], odd[rows]], 0).astype(BF16)
                        )
                        return carry

                    lax.fori_loop(0, 32, pack, 0)
    else:
        g_inner_ref[...] = g_inner.astype(BF16)

    @pl.when(chunk == 3)
    def _():
        position = seq_index * block + lax.broadcasted_iota(jnp.int32, (block, 1), 0)
        long_out[...] = jnp.where(position < len_ref[0], y_sum[:block], 0.0).astype(BF16)
        every_out[own_rows] = y_sum[block:].astype(BF16)
        hat, inverse = row_norm(mid[...])
        df = df_sum[...]
        vectors[2:3] = column_sum(df * hat)
        vectors[3:4] = column_sum(df)
        scaled = df * gain_ref[...]
        dmid = dy[...].astype(F32) + inverse * (
            scaled
            - jnp.mean(scaled, -1, keepdims=True)
            - hat * jnp.mean(scaled * hat, -1, keepdims=True)
        )
        dmid_ref[...] = dmid
        vectors[0:1] = column_sum(dmid)
        low = dmid.astype(BF16)
        grad_o = dot_t(low, wo_ref[...]).astype(BF16)
        do_ref[...] = grad_o
        every_do[own_rows] = grad_o[block:]
        both = grad_o[block:].astype(F32) * attn_ref[block:].astype(F32)
        stats = lq_ref[...]
        for head in range(2 * pairs):
            lanes = slice(head // 2 * PAIR, head // 2 * PAIR + PAIR)
            delta = jnp.sum(own_half(head % 2, both[:, lanes]), -1, keepdims=True)
            stats = jnp.where(lane_index() == HD + head, delta, stats)
        every_ld[own_rows] = stats
        for _, copy in gathers():
            copy.start()
        g_out = t_dot(attn_ref[...], low)
        if planned:
            even[...] = g_out
            piece = width // 32

            def pack(at, carry):
                rows = pl.ds(pl.multiple_of(at * piece, 8), piece)
                where = (
                    lax.rem(at, 2),
                    lax.div(at, 8),
                    lax.rem(lax.div(at, 4), 2),
                    lax.rem(lax.div(at, 2), 2),
                )
                pieces_ref[where + (slice(96, 128),)] = jnp.concatenate(
                    [even[rows], vectors[...]], 0
                ).astype(BF16)
                return carry

            lax.fori_loop(0, 32, pack, 0)
            for now, act, at in OUTER_PLAN:
                if now == 4:
                    getattr(reducer, act)(at)
            reducer.finish(sum_ref)
        else:
            g_out_ref[...] = g_out.astype(BF16)
            vec_ref[...] = vectors[...]
        for _, copy in gathers():
            copy.wait_recv()
        dog_ref[...] = every_do[...]
        ldg_ref[...] = every_ld[...]
        glob_out[...] = every_out[...]
        for _, copy in gathers():
            copy.wait_send()


OUTER_PLAN = (
    (1, "add_core", 0),
    (2, "add_first", 0),
    (2, "add_core", 1),
    (3, "add_second", 0),
    (3, "add_first", 1),
    (3, "add_core", 2),
    (4, "add_core", 3),
    (4, "add_second", 1),
    (4, "add_first", 2),
    (4, "add_second", 2),
    (4, "add_first", 3),
    (4, "add_second", 3),
)


def feed_forward(sizes, planned, doc_len, attn, long_x, glob_x, dlong, dglob, lq, *weights):
    block, count, quarter, seq_count, pairs = sizes
    wo, bo, gain, shift, wi, bi, wr, br = weights
    width, hidden = wi.shape
    chunk = hidden // 4
    rows = block + quarter
    whole = pl.BlockSpec(memory_space=pltpu.VMEM)
    shape = jax.ShapeDtypeStruct
    in_specs = [pl.BlockSpec(memory_space=pltpu.SMEM)] + [whole] * 10
    in_specs += [
        pl.BlockSpec((width, chunk), lambda c: (0, c)),
        pl.BlockSpec((1, chunk), lambda c: (0, c)),
        pl.BlockSpec((chunk, width), lambda c: (c, 0)),
        whole,
    ]
    outs = [
        shape((block, width), BF16),
        shape((GP, width), BF16),
        shape((rows, width), F32),
        shape((rows, width), BF16),
        shape((GP, width), BF16),
        shape((GP, PAIR), F32),
    ]
    out_specs = [whole] * 6
    others = seq_count - 1
    scratch = [
        pltpu.VMEM((rows, width), F32),
        pltpu.VMEM((rows, width), F32),
        pltpu.VMEM((rows, width), F32),
        pltpu.VMEM((rows, width), BF16),
        pltpu.VMEM((width, rows), BF16),
        pltpu.VMEM((rows, width), BF16),
        pltpu.VMEM((8, width), F32),
        pltpu.VMEM((GP, width), BF16),
        pltpu.VMEM((GP, PAIR), F32),
        pltpu.VMEM((GP, width), BF16),
        pltpu.SemaphoreType.DMA((3, others)),
        pltpu.SemaphoreType.DMA((3, others)),
    ]
    if planned:
        part = hidden // 32
        outs += [shape((2, 4, 2, 2, part + width // 32 + 8, width), BF16), shape((part, width), F32)]
        out_specs += [whole] * 2
        scratch += [
            pltpu.VMEM((width, chunk), F32),
            pltpu.VMEM((width, chunk), F32),
            pltpu.VMEM((4, 2, 2, part, width), BF16),
        ] + Reducer.scratch(part, width)
    else:
        outs += [
            shape((hidden, width), BF16),
            shape((width, hidden), BF16),
            shape((width, width), BF16),
            shape((8, width), F32),
        ]
        out_specs += [
            pl.BlockSpec((chunk, width), lambda c: (c, 0)),
            pl.BlockSpec((width, chunk), lambda c: (0, c)),
            whole,
            whole,
        ]
    return pl.pallas_call(
        functools.partial(ffn_kernel, sizes, planned),
        grid=(4,),
        in_specs=in_specs,
        out_specs=out_specs,
        out_shape=outs,
        scratch_shapes=scratch,
        compiler_params=pltpu.CompilerParams(
            collective_id=4, has_side_effects=True, vmem_limit_bytes=62 * 2**20
        ),
        name="feed_forward",
    )(doc_len, attn, long_x, glob_x, dlong, dglob, lq, wo, bo, gain, shift, wi, bi, wr, br)


def back_kernel(
    sizes,
    early_rows,
    len_ref,
    tab_ref,
    q_ref,
    kx_ref,
    vx_ref,
    kg_ref,
    vg_ref,
    o_ref,
    do_ref,
    l_ref,
    dog_ref,
    ldg_ref,
    *rest,
):
    block, count, quarter, seq_count, pairs = sizes
    reduces = early_rows > 0
    if reduces:
        pieces_ref, rest = rest[0], rest[1:]
    dq_ref, dk_ref, dv_ref, dtab_ref, *rest = rest
    if reduces:
        early_ref, rest = rest[0], rest[1:]
    (
        dkx,
        dvx,
        dkg,
        dvg,
        q_send,
        q_recv,
        kv_send,
        kv_recv,
        halo_send,
        halo_recv,
        glob_sends,
        glob_recvs,
        halo_sends,
        halo_recvs,
        *rest,
    ) = rest
    number = pl.program_id(0)
    pair = lax.rem(number, pairs)
    seq_index = lax.axis_index("seq")
    reducer = Reducer(early_rows, rest, pieces=pieces_ref) if reduces else None
    scale = HD ** (-0.5)
    low_lanes = lane_index() < HD
    own_keys = slice(HALO, HALO + block)
    own_rows = pl.ds(pl.multiple_of(seq_index * quarter, quarter), quarter)

    def glob_copies(kind, at):
        source, dest = ((q_send, q_recv), (kv_send, kv_recv))[kind]
        for step in range(1, seq_count):
            device = seq_device(step, seq_count)
            yield pltpu.make_async_remote_copy(
                src_ref=source.at[device[1], at],
                dst_ref=dest.at[step - 1, at],
                send_sem=glob_sends.at[kind, step - 1, at],
                recv_sem=glob_recvs.at[kind, step - 1, at],
                device_id=device,
                device_id_type=pl.DeviceIdType.MESH,
            )

    def halo_copy(direction, at):
        return pltpu.make_async_remote_copy(
            src_ref=halo_send.at[direction, at],
            dst_ref=halo_recv.at[direction, at],
            send_sem=halo_sends.at[direction, at],
            recv_sem=halo_recvs.at[direction, at],
            device_id=seq_device(2 * direction - 1, seq_count),
            device_id_type=pl.DeviceIdType.MESH,
        )

    has_low, has_high = seq_index > 0, seq_index < seq_count - 1
    sends_to = (has_low, has_high)
    gets_from = (has_high, has_low)

    def close_pair(at):
        lanes = lanes_of(at)
        for direction in range(2):

            @pl.when(gets_from[direction])
            def _(direction=direction):
                halo_copy(direction, at).wait_recv()

        for kind, (total, out) in enumerate(((dkx, dk_ref), (dvx, dv_ref))):
            first, last = HALO + REACH, HALO + block - REACH
            out[:REACH, lanes] = (
                total[at, HALO:first] + halo_recv[1, at, kind].astype(F32)
            ).astype(BF16)
            out[REACH : block - REACH, lanes] = total[at, first:last].astype(BF16)
            out[block - REACH : block, lanes] = (
                total[at, last : HALO + block] + halo_recv[0, at, kind].astype(F32)
            ).astype(BF16)
        sums = []
        for kind, (source, dest) in enumerate(((q_send, q_recv), (kv_send, kv_recv))):
            total = source[seq_index, at].astype(F32)
            for step, copy in enumerate(glob_copies(kind, at)):
                copy.wait_recv()
                total += dest[step, at].astype(F32)
            sums.append(total.astype(BF16))
        dq_ref[block:, lanes] = sums[0]
        dk_ref[block:, lanes] = sums[1][:, :PAIR]
        dv_ref[block:, lanes] = sums[1][:, PAIR:]

    def run_plan(now):
        for at, act, chunk in EARLY_PLAN:
            if now == at:
                getattr(reducer, act)(chunk)

    @pl.when(number == 0)
    def _():
        others = [seq_device(step, seq_count) for step in range(1, seq_count)]
        meet(others + (reducer.partners()[2:] if reduces else []))
        if reduces:
            for chunk in range(4):
                reducer.start(chunk)
        for direction in range(2):

            @pl.when(jnp.logical_not(gets_from[direction]))
            def _(direction=direction):
                halo_recv[direction] = jnp.zeros_like(halo_recv[direction])

    if reduces:
        for now in range(1, 2 * pairs):
            if any(at == now for at, _, _ in EARLY_PLAN):

                @pl.when(number == now)
                def _(now=now):
                    run_plan(now)

    @pl.when(number < pairs)
    def _():
        long_bias = key_bias(seq_index * block, block, len_ref[0])
        near_bias = key_bias(seq_index * quarter, quarter, count)
        query = q_ref[block:] * jnp.asarray(scale, BF16)
        grad_o = dog_ref[...]
        far_k, far_v = kx_ref[own_keys], vx_ref[own_keys]
        near_k, near_v = kg_ref[own_rows], vg_ref[own_rows]
        outs, kept = [], []
        for head in range(2):
            norm = in_three(-pick_column(ldg_ref[...], 2 * pair + head))
            delta = in_three(-pick_column(ldg_ref[...], HD + 2 * pair + head))
            qa = with_lanes(head, query, (1.0,) + norm)
            doa = with_lanes(head, grad_o, delta)
            far = jnp.exp(dot_t(qa, key_side(head, far_k, long_bias)))
            near = jnp.exp(dot_t(qa, key_side(head, near_k, near_bias)))
            far_ds = (far * dot_t(doa, value_side(head, far_v))).astype(BF16)
            near_ds = (near * dot_t(doa, value_side(head, near_v))).astype(BF16)
            outs.append(dot_n(far_ds, far_k) + dot_n(near_ds, near_k))
            kept.append(
                (
                    own_half(head, query),
                    own_half(head, grad_o),
                    far.astype(BF16),
                    near.astype(BF16),
                    far_ds,
                    near_ds,
                )
            )
        own_q, own_do, far, near, far_ds, near_ds = (
            jnp.concatenate(part, 0) for part in zip(*kept)
        )
        for total, edge in ((dkx, own_keys), (dvx, own_keys)):
            total[pair, :HALO] = jnp.zeros((HALO, PAIR), F32)
            total[pair, HALO + block :] = jnp.zeros((HALO, PAIR), F32)
        dkx[pair, own_keys] = t_dot(far_ds, own_q)
        dvx[pair, own_keys] = t_dot(far, own_do)
        dkg[pair] = jnp.zeros((GP, PAIR), F32)
        dvg[pair] = jnp.zeros((GP, PAIR), F32)
        dkg[pair, own_rows] = t_dot(near_ds, own_q)
        dvg[pair, own_rows] = t_dot(near, own_do)
        glob_dq = (jnp.where(low_lanes, outs[0], outs[1]) * scale).astype(BF16)
        q_send[:, pair] = glob_dq.reshape(seq_count, quarter, PAIR)
        for copy in glob_copies(0, pair):
            copy.start()

    @pl.when(number >= pairs)
    def _():
        long_bias = key_bias(seq_index * block - HALO, block + 2 * HALO, len_ref[0])
        glob_bias = key_bias(0, GP, count)
        query = q_ref[:block] * jnp.asarray(scale, BF16)
        grad_o = do_ref[...]
        both = grad_o.astype(F32) * o_ref[...].astype(F32)
        heads = []
        for head in range(2):
            norm = in_three(-pick_column(l_ref[...], 2 * pair + head))
            delta = in_three(-jnp.sum(own_half(head, both), -1, keepdims=True))
            heads.append(
                dict(
                    q=own_half(head, query),
                    do=own_half(head, grad_o),
                    qa=with_lanes(head, query, (1.0,) + norm),
                    doa=with_lanes(head, grad_o, delta),
                    kxa=key_side(head, kx_ref[...], long_bias),
                    vxa=value_side(head, vx_ref[...]),
                    kga=key_side(head, kg_ref[...], glob_bias),
                    vga=value_side(head, vg_ref[...]),
                    bias=band_bias(tab_ref[0, head : head + 1]),
                )
            )
        table_sums = [0.0, 0.0]
        grads_q = []
        for start in range(0, block, SUB):
            rows, keys = slice(start, start + SUB), slice(start, start + WINDOW)
            outs, probs, grads = [], [], []
            for head, own in enumerate(heads):
                band = jnp.exp(dot_t(own["qa"][rows], own["kxa"][keys]) + own["bias"])
                band_ds = band * dot_t(own["doa"][rows], own["vxa"][keys])
                table_sums[head] += band_ds
                glob = jnp.exp(dot_t(own["qa"][rows], own["kga"]))
                glob_ds = (glob * dot_t(own["doa"][rows], own["vga"])).astype(BF16)
                band_ds = band_ds.astype(BF16)
                outs.append(dot_n(band_ds, kx_ref[keys]) + dot_n(glob_ds, kg_ref[...]))
                probs.append((band.astype(BF16), glob.astype(BF16)))
                grads.append((band_ds, glob_ds))
            grads_q.append(jnp.where(low_lanes, outs[0], outs[1]))
            own_q = jnp.concatenate([own["q"][rows] for own in heads], 0)
            own_do = jnp.concatenate([own["do"][rows] for own in heads], 0)
            band, glob = (jnp.concatenate(part, 0) for part in zip(*probs))
            band_ds, glob_ds = (jnp.concatenate(part, 0) for part in zip(*grads))
            dkx[pair, keys] += t_dot(band_ds, own_q)
            dvx[pair, keys] += t_dot(band, own_do)
            dkg[pair] += t_dot(glob_ds, own_q)
            dvg[pair] += t_dot(glob, own_do)
        for kind, total in enumerate((dkg, dvg)):
            kv_send[:, pair, :, kind * PAIR : (kind + 1) * PAIR] = (
                total[pair].astype(BF16).reshape(seq_count, quarter, PAIR)
            )
        for copy in glob_copies(1, pair):
            copy.start()
        for kind, total in enumerate((dkx, dvx)):
            for direction, first in enumerate((HALO - REACH, HALO + block)):
                halo_send[direction, pair, kind] = total[pair, first : first + REACH].astype(BF16)
        for direction in range(2):

            @pl.when(sends_to[direction])
            def _(direction=direction):
                halo_copy(direction, pair).start()

        dq_ref[:block, lanes_of(pair)] = (jnp.concatenate(grads_q, 0) * scale).astype(BF16)
        for head in range(2):
            dtab_ref[pair, head : head + 1] = diagonal_sums(table_sums[head])

    @pl.when(number > pairs)
    def _():
        close_pair(pair - 1)

    @pl.when(number == 2 * pairs - 1)
    def _():
        if reduces:
            run_plan(2 * pairs)
        close_pair(pairs - 1)
        for at in range(pairs):
            for kind in range(2):
                for copy in glob_copies(kind, at):
                    copy.wait_send()
            for direction in range(2):

                @pl.when(sends_to[direction])
                def _(direction=direction, at=at):
                    halo_copy(direction, at).wait_send()

        if reduces:
            reducer.finish(early_ref)


def attend_back(sizes, doc_len, table, q, kx, vx, kg, vg, o, do, l, dog, ldg, pieces=None):
    block, count, quarter, seq_count, pairs = sizes
    width = q.shape[1]
    early_rows = 0 if pieces is None else pieces.shape[-2]
    ext = block + 2 * HALO
    cols = lambda rows: pl.BlockSpec((rows, PAIR), lambda i: (0, lax.rem(i, pairs)))
    whole = pl.BlockSpec(memory_space=pltpu.VMEM)
    shape = jax.ShapeDtypeStruct
    in_specs = [
        pl.BlockSpec(memory_space=pltpu.SMEM),
        pl.BlockSpec((1, 2, WINDOW), lambda i: (lax.rem(i, pairs), 0, 0)),
        cols(block + GP),
        cols(ext),
        cols(ext),
        cols(GP),
        cols(GP),
        cols(block),
        cols(block),
        whole,
        cols(GP),
        whole,
    ]
    rows = block + quarter
    outs = [shape((rows, width), BF16)] * 3 + [shape((pairs, 2, WINDOW), F32)]
    others = seq_count - 1
    scratch = [
        pltpu.VMEM((pairs, ext, PAIR), F32),
        pltpu.VMEM((pairs, ext, PAIR), F32),
        pltpu.VMEM((pairs, GP, PAIR), F32),
        pltpu.VMEM((pairs, GP, PAIR), F32),
        pltpu.VMEM((seq_count, pairs, quarter, PAIR), BF16),
        pltpu.VMEM((others, pairs, quarter, PAIR), BF16),
        pltpu.VMEM((seq_count, pairs, quarter, 2 * PAIR), BF16),
        pltpu.VMEM((others, pairs, quarter, 2 * PAIR), BF16),
        pltpu.VMEM((2, pairs, 2, REACH, PAIR), BF16),
        pltpu.VMEM((2, pairs, 2, REACH, PAIR), BF16),
        pltpu.SemaphoreType.DMA((2, others, pairs)),
        pltpu.SemaphoreType.DMA((2, others, pairs)),
        pltpu.SemaphoreType.DMA((2, pairs)),
        pltpu.SemaphoreType.DMA((2, pairs)),
    ]
    args = [doc_len, table, q, kx, vx, kg, vg, o, do, l, dog, ldg]
    if early_rows:
        in_specs.append(pl.BlockSpec(memory_space=pl.ANY))
        outs.append(shape((early_rows, width), F32))
        scratch += Reducer.scratch(early_rows, width)
        args.append(pieces)
    return pl.pallas_call(
        functools.partial(back_kernel, sizes, early_rows),
        grid=(2 * pairs,),
        in_specs=in_specs,
        out_specs=[whole] * len(outs),
        out_shape=outs,
        scratch_shapes=scratch,
        compiler_params=pltpu.CompilerParams(
            collective_id=1, has_side_effects=True, vmem_limit_bytes=60 * 2**20
        ),
        name="attend_back",
    )(*args)


def matmul(left, right):
    return jnp.dot(left, right, preferred_element_type=F32)


def rows_dot(left, right):
    return jnp.einsum("rd,re->de", left, right, preferred_element_type=F32)


def back_dot(left, right):
    return lax.dot_general(left, right, (((1,), (1,)), ((), ())), preferred_element_type=F32)


def on_device(
    long_input,
    global_input,
    lengths,
    w_query,
    b_query,
    w_key,
    w_value,
    b_value,
    w_out,
    b_out,
    w_inner,
    b_inner,
    w_outer,
    b_outer,
    norm1_gain,
    norm1_shift,
    norm2_gain,
    norm2_shift,
    rel_table,
    long_cotangent,
    global_cotangent,
):
    seq_count = lax.axis_size("seq")
    data_count = lax.axis_size("dp")
    seq_index = lax.axis_index("seq")
    block = long_input.shape[1]
    count = global_input.shape[1]
    width = long_input.shape[2]
    heads = rel_table.shape[1]
    pairs = heads // 2
    labels = 2 * R + 1
    quarter = GP // seq_count
    sizes = Sizes(block, count, quarter, seq_count, pairs)
    table = jnp.pad(
        rel_table.T,
        ((0, 0), (HALO - R, WINDOW - labels - HALO + R)),
        constant_values=MASKED,
    ).reshape(pairs, 2, WINDOW)

    glob_x = jnp.pad(global_input[0], ((0, GP - count), (0, 0)))
    glob_dy = jnp.pad(global_cotangent[0], ((0, GP - count), (0, 0)))
    own_glob = lambda a: lax.dynamic_slice_in_dim(a, seq_index * quarter, quarter, 0)
    row = lambda vector: vector.reshape(1, -1)
    queries, kx, vx, kg, vg, attn_low, long_l, glob_l = attend(
        sizes,
        lengths,
        table,
        long_input[0],
        glob_x,
        w_query,
        w_key,
        w_value,
        row(b_query),
        row(b_value),
        row(norm1_gain),
        row(norm1_shift),
    )

    planned = has_plan()
    long_result, glob_out, grad_mid, grad_attn, every_do, every_ld, *gradients = feed_forward(
        sizes,
        planned,
        lengths,
        attn_low,
        long_input[0],
        glob_x,
        long_cotangent[0],
        glob_dy,
        glob_l,
        w_out,
        row(b_out),
        row(norm2_gain),
        row(norm2_shift),
        w_inner,
        row(b_inner),
        w_outer,
        row(b_outer),
    )
    query_low, key_low, value_low, dtab, *early = attend_back(
        sizes,
        lengths,
        table,
        queries,
        kx,
        vx,
        kg,
        vg,
        attn_low,
        grad_attn,
        long_l,
        every_do,
        every_ld,
        *(gradients[:1] if planned else []),
    )
    devices = data_count * seq_count
    piece = width // devices
    by_device = lambda grad: grad.reshape(devices, -1, width)
    own_part = lambda vector: lax.dynamic_slice_in_dim(
        vector,
        (lax.axis_index("dp") * seq_count + seq_index) * (vector.shape[0] // devices),
        vector.shape[0] // devices,
    )
    own_x = jnp.concatenate([long_input[0], own_glob(glob_x)], 0).astype(F32)
    own_normed, hat_one, inv_one = norm_forward(own_x, norm1_gain, norm1_shift)
    own_normed = own_normed.astype(BF16)
    grad_b_query = jnp.sum(query_low.astype(F32), 0)
    grad_b_value = jnp.sum(value_low.astype(F32), 0)
    grad_w_query = rows_dot(own_normed, query_low)
    grad_w_key = rows_dot(own_normed, key_low)
    grad_w_value = rows_dot(own_normed, value_low)
    grad_normed_one = (
        back_dot(query_low, w_query) + back_dot(key_low, w_key) + back_dot(value_low, w_value)
    )
    grad_from_one, grad_gain_one, grad_shift_one = norm_backward(
        grad_normed_one, hat_one, inv_one, norm1_gain
    )
    grad_x = grad_mid + grad_from_one

    vectors = jnp.stack([grad_b_query, grad_b_value, grad_gain_one, grad_shift_one])
    grads = (grad_w_query, grad_w_key, grad_w_value)
    table_part = dtab.reshape(heads, WINDOW)
    if planned:
        g_outer, early = gradients[1], early[0]
        g_inner = early[: 4 * piece].reshape(4, piece, width).transpose(1, 0, 2)
        g_inner = g_inner.reshape(piece, -1)
        g_out, early_vectors = early[4 * piece : 5 * piece], early[5 * piece :]
        extra = jnp.broadcast_to(jnp.pad(vectors, ((0, 4), (0, 0))), (devices, 8, width))
        late, table_total = reduce_late(
            by_core(jnp.concatenate([by_device(g) for g in grads] + [extra], 1)), table_part
        )
        g_query, g_key, g_value = (late[i * piece : (i + 1) * piece] for i in range(3))
        vectors = late[3 * piece :]
    else:
        g_outer, g_inner, g_out, early_vectors = gradients
        g_outer, g_inner, g_out, g_query, g_key, g_value = (
            lax.psum_scatter(g.astype(BF16), ("dp", "seq"), scatter_dimension=0, tiled=True).astype(
                F32
            )
            for g in (g_outer, g_inner, g_out) + grads
        )
        early_vectors, vectors, table_total = lax.psum(
            (early_vectors, vectors, table_part), ("dp", "seq")
        )
    g_b_query, g_b_value, g_g1, g_s1 = (own_part(vectors[i]) for i in range(4))
    g_b_out, g_b_outer, g_g2, g_s2 = (own_part(early_vectors[i]) for i in range(4))
    g_b_inner = own_part(early_vectors[4:].reshape(-1))
    table_total = table_total[:, HALO - R : HALO - R + labels].T
    glob_grad = lax.all_gather(grad_x[block:], "seq", axis=0, tiled=True)[:count]
    return (
        long_result[None],
        glob_out[:count][None],
        grad_x[:block][None],
        glob_grad[None],
        g_query,
        g_b_query,
        g_key,
        g_value,
        g_b_value,
        g_out,
        g_b_out,
        g_inner,
        g_b_inner,
        g_outer,
        g_b_outer,
        g_g1,
        g_s1,
        g_g2,
        g_s2,
        table_total,
    )


def solution(mesh):
    rows, whole = P("dp", "seq", None), P("dp", None, None)
    matrix, vector = P(("dp", "seq"), None), P(("dp", "seq"))
    return jax.shard_map(
        on_device,
        mesh=mesh,
        in_specs=(rows, whole, P("dp")) + (P(),) * 16 + (rows, whole),
        out_specs=(
            rows,
            whole,
            rows,
            whole,
            matrix,
            vector,
            matrix,
            matrix,
            vector,
            matrix,
            vector,
            matrix,
            vector,
            matrix,
            vector,
            vector,
            vector,
            vector,
            vector,
            P(),
        ),
        check_vma=False,
    )
```

```python
import functools
from typing import NamedTuple

import jax
import jax.numpy as jnp
from jax import lax
from jax.experimental import pallas as pl
from jax.experimental.pallas import tpu as pltpu
from jax.sharding import PartitionSpec as P

HD = 64
R = 84
PAIR = 2 * HD
HALO = 128
REACH = 96
GP = 256
SUB = 256
WINDOW = SUB + 2 * HALO
EPSILON = 1e-05
MASKED = -1e30
F32 = jnp.float32
BF16 = jnp.bfloat16


def dot_t(left, right):
    return lax.dot_general(left, right, (((1,), (1,)), ((), ())), preferred_element_type=F32)


def dot_n(left, right):
    return lax.dot_general(left, right, (((1,), (0,)), ((), ())), preferred_element_type=F32)


def t_dot(left, right):
    return lax.dot_general(left, right, (((0,), (0,)), ((), ())), preferred_element_type=F32)


def band_bias(table_row):
    spread = jnp.broadcast_to(table_row, (SUB, WINDOW))
    return pltpu.roll(spread, 0, 1, stride=1, stride_axis=0)


def diagonal_sums(rows):
    height, width = rows.shape
    while height > 8:
        height //= 2
        rows = rows[:height] + pltpu.roll(rows[height:], width - height, 1)
    row = lax.broadcasted_iota(jnp.int32, rows.shape, 0)
    for bit in (1, 2, 4):
        rows = jnp.where((row & bit) != 0, pltpu.roll(rows, width - bit, 1), rows)
    return jnp.sum(rows, 0, keepdims=True)


def lane_index():
    return lax.broadcasted_iota(jnp.int32, (1, PAIR), 1)


def own_half(head, value):
    low_lanes = lane_index() < HD
    return jnp.where(low_lanes if head == 0 else ~low_lanes, value, jnp.zeros_like(value))


def other_lane(head):
    return HD * (1 - head)


def with_lanes(head, value, columns):
    wide = own_half(head, value.astype(F32))
    lane = lane_index()
    for offset, column in enumerate(columns):
        wide = jnp.where(lane == other_lane(head) + offset, column, wide)
    return wide.astype(BF16)


def in_three(column):
    high = column.astype(BF16).astype(F32)
    middle = (column - high).astype(BF16).astype(F32)
    return (high, middle, column - high - middle)


def key_bias(first, rows, end):
    position = first + lax.broadcasted_iota(jnp.int32, (rows, 1), 0)
    return jnp.where((position >= 0) & (position < end), 0.0, MASKED)


def pick_column(rows, index):
    return jnp.sum(jnp.where(lane_index() == index, rows, 0.0), -1, keepdims=True)


def key_side(head, keys, bias):
    return with_lanes(head, keys, (bias, 1.0, 1.0, 1.0))


def value_side(head, values):
    return with_lanes(head, values, (1.0, 1.0, 1.0))


def softmax_rows(parts, value_parts, head):
    top = functools.reduce(
        jnp.maximum, [jnp.max(part, -1, keepdims=True) for part in parts]
    )
    mixed = sum(
        dot_n(jnp.exp(part - top).astype(BF16), values)
        for part, values in zip(parts, value_parts)
    )
    at = other_lane(head)
    total = mixed[:, at : at + 1]
    return mixed / total, top + jnp.log(total)


def seq_device(steps, seq_count):
    return (lax.axis_index("dp"), lax.rem(lax.axis_index("seq") + steps + seq_count, seq_count))


def row_norm(rows):
    centred = rows - jnp.mean(rows, -1, keepdims=True)
    inverse = lax.rsqrt(jnp.mean(centred * centred, -1, keepdims=True) + EPSILON)
    return centred * inverse, inverse


def put_column(ref, rows, index, column):
    ref[rows] = jnp.where(lane_index() == index, column, ref[rows])


def lanes_of(at):
    return pl.ds(pl.multiple_of(at * PAIR, PAIR), PAIR)


class Sizes(NamedTuple):
    block: int
    count: int
    quarter: int
    seq_count: int
    pairs: int


def attend_kernel(
    sizes,
    len_ref,
    tab_ref,
    long_ref,
    glob_ref,
    wq_ref,
    wk_ref,
    wv_ref,
    bq_ref,
    bv_ref,
    gain_ref,
    shift_ref,
    q_ref,
    kx_ref,
    vx_ref,
    kg_ref,
    vg_ref,
    o_ref,
    l_ref,
    lq_ref,
    part_o,
    part_l,
    from_o,
    from_l,
    halo_sends,
    halo_recvs,
    part_sends,
    part_recvs,
):
    block, count, quarter, seq_count, pairs = sizes
    ext = block + 2 * HALO
    seq_index = lax.axis_index("seq")
    scale = jnp.asarray(HD ** (-0.5), BF16)
    low_lanes = lane_index() < HD
    own_keys = slice(HALO, HALO + block)
    own_rows = pl.ds(pl.multiple_of(seq_index * quarter, quarter), quarter)
    neighbours = (seq_index > 0, seq_index < seq_count - 1)
    barrier = pltpu.get_barrier_semaphore()
    for step in range(1, seq_count):
        pl.semaphore_signal(
            barrier,
            inc=1,
            device_id=seq_device(step, seq_count),
            device_id_type=pl.DeviceIdType.MESH,
        )

    def halo_copies(direction):
        source = HALO if direction == 0 else HALO + block - REACH
        dest = HALO + block if direction == 0 else HALO - REACH
        for kind, ref in enumerate((kx_ref, vx_ref)):
            yield pltpu.make_async_remote_copy(
                src_ref=ref.at[source : source + REACH],
                dst_ref=ref.at[dest : dest + REACH],
                send_sem=halo_sends.at[direction, kind],
                recv_sem=halo_recvs.at[direction, kind],
                device_id=seq_device(2 * direction - 1, seq_count),
                device_id_type=pl.DeviceIdType.MESH,
            )

    def part_copies():
        for step in range(1, seq_count):
            device = seq_device(step, seq_count)
            rows = pl.ds(pl.multiple_of(device[1] * quarter, quarter), quarter)
            for kind, (source, dest) in enumerate(((part_o, from_o), (part_l, from_l))):
                yield step, kind, pltpu.make_async_remote_copy(
                    src_ref=source.at[rows],
                    dst_ref=dest.at[step - 1],
                    send_sem=part_sends.at[kind, step - 1],
                    recv_sem=part_recvs.at[kind, step - 1],
                    device_id=device,
                    device_id_type=pl.DeviceIdType.MESH,
                )

    gain, shift = gain_ref[...], shift_ref[...]
    normed_long = (row_norm(long_ref[...].astype(F32))[0] * gain + shift).astype(BF16)
    kx_ref[own_keys] = dot_n(normed_long, wk_ref[...]).astype(BF16)
    vx_ref[own_keys] = (dot_n(normed_long, wv_ref[...]) + bv_ref[...]).astype(BF16)
    pl.semaphore_wait(barrier, seq_count - 1)
    for direction, first in enumerate((HALO - REACH, HALO + block)):

        @pl.when(neighbours[direction])
        def _(direction=direction):
            for copy in halo_copies(direction):
                copy.start()

        outer = slice(0, first) if direction == 0 else slice(first + REACH, ext)
        for ref in (kx_ref, vx_ref):
            ref[outer] = jnp.zeros((HALO - REACH, ref.shape[1]), BF16)

        @pl.when(jnp.logical_not(neighbours[direction]))
        def _(first=first):
            for ref in (kx_ref, vx_ref):
                ref[first : first + REACH] = jnp.zeros((REACH, ref.shape[1]), BF16)

    normed_glob = (row_norm(glob_ref[...].astype(F32))[0] * gain + shift).astype(BF16)
    kg_ref[...] = dot_n(normed_glob, wk_ref[...]).astype(BF16)
    vg_ref[...] = (dot_n(normed_glob, wv_ref[...]) + bv_ref[...]).astype(BF16)
    q_ref[block:] = (dot_n(normed_glob, wq_ref[...]) + bq_ref[...]).astype(BF16)
    q_ref[:block] = (dot_n(normed_long, wq_ref[...]) + bq_ref[...]).astype(BF16)
    part_l[...] = jnp.zeros_like(part_l)
    l_ref[...] = jnp.zeros_like(l_ref)

    def glob_pair(pair, carry):
        lanes = lanes_of(pair)
        far_bias = key_bias(seq_index * block, block, len_ref[0])
        near_bias = key_bias(seq_index * quarter, quarter, count)
        query = q_ref[block:, lanes] * scale
        outs = []
        for head in range(2):
            q = with_lanes(head, query, (1.0,))
            far = dot_t(q, with_lanes(head, kx_ref[own_keys, lanes], (far_bias,)))
            near = dot_t(q, with_lanes(head, kg_ref[own_rows, lanes], (near_bias,)))
            out, norm = softmax_rows(
                [far, near],
                [
                    with_lanes(head, vx_ref[own_keys, lanes], (1.0,)),
                    with_lanes(head, vg_ref[own_rows, lanes], (1.0,)),
                ],
                head,
            )
            outs.append(out)
            put_column(part_l, slice(None), 2 * pair + head, norm)
        part_o[:, lanes] = jnp.where(low_lanes, outs[0], outs[1]).astype(BF16)
        return carry

    lax.fori_loop(0, pairs, glob_pair, 0)
    for _, _, copy in part_copies():
        copy.start()
    for direction in range(2):

        @pl.when(neighbours[1 - direction])
        def _(direction=direction):
            for copy in halo_copies(direction):
                copy.wait_recv()

    def long_pair(pair, carry):
        lanes = lanes_of(pair)
        long_bias = key_bias(seq_index * block - HALO, ext, len_ref[0])
        glob_bias = key_bias(0, GP, count)
        query = q_ref[:block, lanes] * scale
        outs = []
        for head in range(2):
            q = with_lanes(head, query, (1.0,))
            kx = with_lanes(head, kx_ref[:, lanes], (long_bias,))
            kg = with_lanes(head, kg_ref[:, lanes], (glob_bias,))
            vx, vg = (with_lanes(head, ref[:, lanes], (1.0,)) for ref in (vx_ref, vg_ref))
            bias = band_bias(tab_ref[pair, head : head + 1])
            mixed = []
            for start in range(0, block, SUB):
                rows, keys = slice(start, start + SUB), slice(start, start + WINDOW)
                out, norm = softmax_rows(
                    [dot_t(q[rows], kx[keys]) + bias, dot_t(q[rows], kg)], [vx[keys], vg], head
                )
                mixed.append(out)
                put_column(l_ref, rows, 2 * pair + head, norm)
            outs.append(jnp.concatenate(mixed, 0))
        o_ref[:block, lanes] = jnp.where(low_lanes, outs[0], outs[1]).astype(BF16)
        return carry

    lax.fori_loop(0, pairs, long_pair, 0)
    for _, _, copy in part_copies():
        copy.wait_recv()
    norms = [part_l[own_rows]] + [from_l[step] for step in range(seq_count - 1)]
    outs = [part_o[own_rows]] + [from_o[step] for step in range(seq_count - 1)]
    top = functools.reduce(jnp.maximum, norms)
    shares = [jnp.exp(norm - top) for norm in norms]
    total = sum(shares)
    lq_ref[...] = top + jnp.log(total)
    shares = [share / total for share in shares]
    for at in range(pairs):
        lanes = slice(at * PAIR, (at + 1) * PAIR)
        mixed = 0.0
        for share, out in zip(shares, outs):
            spread = jnp.where(
                low_lanes, share[:, 2 * at : 2 * at + 1], share[:, 2 * at + 1 : 2 * at + 2]
            )
            mixed += spread * out[:, lanes].astype(F32)
        o_ref[block:, lanes] = mixed.astype(BF16)
    for _, _, copy in part_copies():
        copy.wait_send()
    for direction in range(2):

        @pl.when(neighbours[direction])
        def _(direction=direction):
            for copy in halo_copies(direction):
                copy.wait_send()


def attend(sizes, doc_len, table, long_x, glob_x, *weights):
    block, count, quarter, seq_count, pairs = sizes
    width = long_x.shape[1]
    ext = block + 2 * HALO
    whole = pl.BlockSpec(memory_space=pltpu.VMEM)
    shape = jax.ShapeDtypeStruct
    others = seq_count - 1
    return pl.pallas_call(
        functools.partial(attend_kernel, sizes),
        in_specs=[pl.BlockSpec(memory_space=pltpu.SMEM)] + [whole] * 10,
        out_specs=[whole] * 8,
        out_shape=[
            shape((block + GP, width), BF16),
            shape((ext, width), BF16),
            shape((ext, width), BF16),
            shape((GP, width), BF16),
            shape((GP, width), BF16),
            shape((block + quarter, width), BF16),
            shape((block, PAIR), F32),
            shape((quarter, PAIR), F32),
        ],
        scratch_shapes=[
            pltpu.VMEM((GP, width), BF16),
            pltpu.VMEM((GP, PAIR), F32),
            pltpu.VMEM((others, quarter, width), BF16),
            pltpu.VMEM((others, quarter, PAIR), F32),
            pltpu.SemaphoreType.DMA((2, 2)),
            pltpu.SemaphoreType.DMA((2, 2)),
            pltpu.SemaphoreType.DMA((2, others)),
            pltpu.SemaphoreType.DMA((2, others)),
        ],
        compiler_params=pltpu.CompilerParams(
            collective_id=3, has_side_effects=True, vmem_limit_bytes=56 * 2**20
        ),
        name="attend",
    )(doc_len, table, long_x, glob_x, *weights)


class Reducer:
    def __init__(self, rows, split, scratch, pieces=None, outgoing=None, in_order=False):
        self.ids = mesh_ids()
        self.halves = (slice(0, split), slice(split, rows))
        self.in_order = in_order
        self.pieces, self.outgoing = pieces, outgoing
        self.mine, self.from_core, self.from_one, self.from_two, self.from_z = scratch[:5]
        self.local, self.sends, self.recvs = scratch[5:]

    @staticmethod
    def scratch(rows, width):
        return [
            pltpu.VMEM((4, 2, 2, rows, width), BF16),
            pltpu.VMEM((4, 2, 2, rows, width), BF16),
            pltpu.VMEM((4, 2, rows, width), BF16),
            pltpu.VMEM((4, rows, width), BF16),
            pltpu.VMEM((3, rows, width), BF16),
            pltpu.SemaphoreType.DMA((4,)),
            pltpu.SemaphoreType.DMA((6, 4)),
            pltpu.SemaphoreType.DMA((6, 4)),
        ]

    def partners(self):
        z, y, x, core = self.ids
        dp, seq = z * 2 + y, x * 2 + core
        near = [(dp, x * 2 + 1 - core), (dp, (1 - x) * 2 + core), (z * 2 + 1 - y, seq)]
        return near + [(lax.rem(z + step, 4) * 2 + y, seq) for step in (1, 2, 3)]

    def target(self, chunk):
        return chunk if self.in_order else lax.rem(self.ids[0] + 1 + chunk, 4)

    def remote(self, source, dest, kind, send_at, recv_at, device):
        return pltpu.make_async_remote_copy(
            src_ref=source,
            dst_ref=dest,
            send_sem=self.sends.at[kind, send_at],
            recv_sem=self.recvs.at[kind, recv_at],
            device_id=device,
            device_id_type=pl.DeviceIdType.MESH,
        )

    def own_copy(self, chunk):
        core, to = self.ids[3], self.target(chunk)
        return pltpu.make_async_copy(
            self.pieces.at[core, to], self.mine.at[to], self.local.at[chunk]
        )

    def core_copy(self, chunk):
        core, to = self.ids[3], self.target(chunk)
        source = self.outgoing.at[to] if self.pieces is None else self.pieces.at[1 - core, to]
        return self.remote(source, self.from_core.at[to], 0, chunk, chunk, self.partners()[0])

    def first_copies(self, chunk):
        z, y, x, core = self.ids
        to = self.target(chunk)
        one, two = self.halves
        near = self.partners()
        return (
            self.remote(
                self.mine.at[to, :, 1 - x, one],
                self.from_one.at[to, :, one],
                1,
                chunk,
                chunk,
                near[1],
            ),
            self.remote(
                self.mine.at[to, 1 - y, :, two],
                self.from_one.at[to, :, two],
                2,
                chunk,
                chunk,
                near[2],
            ),
        )

    def second_copies(self, chunk):
        z, y, x, core = self.ids
        to = self.target(chunk)
        one, two = self.halves
        near = self.partners()
        return (
            self.remote(
                self.mine.at[to, 1 - y, x, one],
                self.from_two.at[to, one],
                3,
                chunk,
                chunk,
                near[2],
            ),
            self.remote(
                self.mine.at[to, y, 1 - x, two],
                self.from_two.at[to, two],
                4,
                chunk,
                chunk,
                near[1],
            ),
        )

    def last_copy(self, chunk):
        z, y, x, core = self.ids
        to = self.target(chunk)
        slot = lax.rem(z - to + 4, 4) - 1
        return self.remote(
            self.mine.at[to, y, x],
            self.from_z.at[slot],
            5,
            chunk,
            slot,
            (to * 2 + y, x * 2 + core),
        )

    def arrival(self, slot):
        z, y, x, core = self.ids
        return self.remote(
            self.mine.at[z, y, x], self.from_z.at[slot], 5, slot, slot, self.partners()[3]
        )

    def leaves(self, chunk):
        return self.target(chunk) != self.ids[0]

    def fill(self, to, y, x, value_of):
        core = self.ids[3]
        self.mine[to, y, x] = value_of(core).astype(BF16)
        self.outgoing[to, y, x] = value_of(1 - core).astype(BF16)

    def start(self, chunk):
        self.core_copy(chunk).start()
        if self.pieces is not None:
            self.own_copy(chunk).start()

    def add_core(self, chunk):
        to = self.target(chunk)
        if self.pieces is not None:
            self.own_copy(chunk).wait()
        self.core_copy(chunk).wait_recv()

        def add(index, carry):
            at = (to, lax.div(index, 2), lax.rem(index, 2))
            self.mine[at] = (self.mine[at].astype(F32) + self.from_core[at].astype(F32)).astype(
                BF16
            )
            return carry

        lax.fori_loop(0, 4, add, 0)
        for copy in self.first_copies(chunk):
            copy.start()

    def add_first(self, chunk):
        z, y, x, core = self.ids
        one, two = self.halves
        to = self.target(chunk)
        for copy in self.first_copies(chunk):
            copy.wait_recv()

        def add(index, carry):
            for at, rows in (((to, index, x), one), ((to, y, index), two)):
                self.mine[at + (rows,)] = (
                    self.mine[at + (rows,)].astype(F32)
                    + self.from_one[to, index, rows].astype(F32)
                ).astype(BF16)
            return carry

        lax.fori_loop(0, 2, add, 0)
        for copy in self.second_copies(chunk):
            copy.start()

    def add_second(self, chunk):
        z, y, x, core = self.ids
        to = self.target(chunk)
        for copy in self.second_copies(chunk):
            copy.wait_recv()

        @pl.when(self.leaves(chunk))
        def _():
            self.mine[to, y, x] = (
                self.mine[to, y, x].astype(F32) + self.from_two[to].astype(F32)
            ).astype(BF16)
            self.last_copy(chunk).start()

    def finish(self, out):
        z, y, x, core = self.ids
        total = self.mine[z, y, x].astype(F32) + self.from_two[z].astype(F32)
        for slot in range(3):
            self.arrival(slot).wait_recv()
            total += self.from_z[slot].astype(F32)
        out[...] = total
        for chunk in range(4):
            self.core_copy(chunk).wait_send()
            for copy in self.first_copies(chunk) + self.second_copies(chunk):
                copy.wait_send()

            @pl.when(self.leaves(chunk))
            def _(chunk=chunk):
                self.last_copy(chunk).wait_send()


def mesh_ids():
    dp, seq = lax.axis_index("dp"), lax.axis_index("seq")
    return lax.div(dp, 2), lax.rem(dp, 2), lax.div(seq, 2), lax.rem(seq, 2)


def meet(devices):
    barrier = pltpu.get_barrier_semaphore()
    for device in devices:
        pl.semaphore_signal(barrier, inc=1, device_id=device, device_id_type=pl.DeviceIdType.MESH)
    pl.semaphore_wait(barrier, len(devices))


EARLY_PLAN = (
    (2, "add_core", 0),
    (3, "add_core", 1),
    (4, "add_core", 2),
    (5, "add_core", 3),
    (7, "add_first", 0),
    (8, "add_first", 1),
    (9, "add_second", 0),
    (9, "add_first", 2),
    (10, "add_second", 1),
    (10, "add_first", 3),
    (11, "add_second", 2),
    (12, "add_second", 3),
)


def late_kernel(
    sizes,
    planned,
    long_ref,
    glob_ref,
    dq_ref,
    dk_ref,
    dv_ref,
    dmid_ref,
    wq_ref,
    wk_ref,
    wv_ref,
    gain_ref,
    shift_ref,
    table_ref,
    long_out,
    glob_out,
    *rest,
):
    block, count, quarter, seq_count, pairs = sizes
    rows = block + quarter
    width = long_ref.shape[1]
    if planned:
        late_ref, total_ref, *rest = rest
    else:
        gq_ref, gk_ref, gv_ref, total_ref, *rest = rest
    normed_t, every, gather_sends, gather_recvs, *rest = rest
    seq_index = lax.axis_index("seq")
    own_rows = pl.ds(pl.multiple_of(seq_index * quarter, quarter), quarter)
    others = [seq_device(step, seq_count) for step in range(1, seq_count)]

    def gathers():
        for step, device in enumerate(others):
            yield pltpu.make_async_remote_copy(
                src_ref=every.at[own_rows],
                dst_ref=every.at[own_rows],
                send_sem=gather_sends.at[step],
                recv_sem=gather_recvs.at[step],
                device_id=device,
                device_id_type=pl.DeviceIdType.MESH,
            )

    if planned:
        work, outgoing, kept, arrived, table_sends, table_recvs, *rest = rest
        reducer = Reducer(outgoing.shape[-2], 32, rest, outgoing=outgoing)
        z, y, x, core = mesh_ids()
        partners = reducer.partners()[:3] + [
            ((z + 1 - 2 * lax.rem(z, 2)) * 2 + y, lax.axis_index("seq")),
            (lax.rem(z + 2, 4) * 2 + y, lax.axis_index("seq")),
        ]

        def table_copy(stage):
            return pltpu.make_async_remote_copy(
                src_ref=kept.at[stage],
                dst_ref=arrived.at[stage],
                send_sem=table_sends.at[stage],
                recv_sem=table_recvs.at[stage],
                device_id=partners[stage],
                device_id_type=pl.DeviceIdType.MESH,
            )

        def table_step(stage):
            table_copy(stage).wait_recv()
            kept[stage + 1] = kept[stage] + arrived[stage]
            if stage < 4:
                table_copy(stage + 1).start()

    meet(others + (reducer.partners()[2:] if planned else []))
    everything = jnp.concatenate([long_ref[...], glob_ref[own_rows]], 0).astype(F32)
    hat, inverse = row_norm(everything)
    normed_t[...] = (hat * gain_ref[...] + shift_ref[...]).astype(BF16).T
    if planned:
        piece = width // 32
        blank = jnp.zeros((8, width), F32)
        for chunk in range(4):
            to = reducer.target(chunk)
            some = normed_t[pl.ds(pl.multiple_of(to * 8 * piece, 64), 8 * piece)]
            for kind, ref in enumerate((dq_ref, dk_ref, dv_ref)):
                work[kind] = dot_n(some, ref[...])
            for at in range(4):

                def value_of(side, at=at):
                    part = pl.ds(pl.multiple_of((2 * at + side) * piece, 8), piece)
                    return jnp.concatenate([work[kind, part] for kind in range(3)] + [blank], 0)

                reducer.fill(to, at // 2, at % 2, value_of)
            reducer.start(chunk)
            if chunk > 0:
                reducer.add_core(chunk - 1)
        grads = dot_t(dq_ref[...], wq_ref[...])
        reducer.add_core(3)
        grads += dot_t(dk_ref[...], wk_ref[...]) + dot_t(dv_ref[...], wv_ref[...])
        reducer.add_first(0)
    else:
        for ref, out in ((dq_ref, gq_ref), (dk_ref, gk_ref), (dv_ref, gv_ref)):
            out[...] = dot_n(normed_t[...], ref[...]).astype(BF16)
        grads = (
            dot_t(dq_ref[...], wq_ref[...])
            + dot_t(dk_ref[...], wk_ref[...])
            + dot_t(dv_ref[...], wv_ref[...])
        )
    scaled = grads * gain_ref[...]
    total = dmid_ref[...] + inverse * (
        scaled
        - jnp.mean(scaled, -1, keepdims=True)
        - hat * jnp.mean(scaled * hat, -1, keepdims=True)
    )
    every[own_rows] = total[block:].astype(BF16)
    for copy in gathers():
        copy.start()
    long_out[...] = total[:block]
    sums = [
        column_sum(part)
        for part in (dq_ref[...].astype(F32), dv_ref[...].astype(F32), grads * hat, grads)
    ]
    heads = 2 * pairs
    first = kept.at[0] if planned else total_ref
    first[...] = jnp.zeros(first.shape, F32)
    first[:heads, :WINDOW] = table_ref[...]
    for at, vector in enumerate(sums):
        first[heads + at : heads + at + 1] = vector
    if planned:
        table_copy(0).start()
        for number, (act, chunk) in enumerate(LATE_TAIL):
            getattr(reducer, act)(chunk)
            if number < 5:
                table_step(number)
        total_ref[...] = kept[5]
        reducer.finish(late_ref)
        for stage in range(5):
            table_copy(stage).wait_send()
    for copy in gathers():
        copy.wait_recv()
    glob_out[...] = every[...].astype(F32)
    for copy in gathers():
        copy.wait_send()


LATE_TAIL = (
    ("add_first", 1),
    ("add_second", 0),
    ("add_first", 2),
    ("add_second", 1),
    ("add_first", 3),
    ("add_second", 2),
    ("add_second", 3),
)


def last_part(sizes, planned, long_x, glob_x, dq, dk, dv, dmid, wq, wk, wv, gain, shift, table):
    block, count, quarter, seq_count, pairs = sizes
    rows, width = dq.shape
    others = seq_count - 1
    whole = pl.BlockSpec(memory_space=pltpu.VMEM)
    shape = jax.ShapeDtypeStruct
    sums = shape(((2 * pairs + 4 + 7) // 8 * 8, width), F32)
    outs = [shape((block, width), F32), shape((GP, width), F32)]
    scratch = [
        pltpu.VMEM((width, rows), BF16),
        pltpu.VMEM((GP, width), BF16),
        pltpu.SemaphoreType.DMA((others,)),
        pltpu.SemaphoreType.DMA((others,)),
    ]
    if planned:
        piece = width // 32
        part = 3 * piece + 8
        outs += [shape((part, width), F32), sums]
        scratch += [
            pltpu.VMEM((3, 8 * piece, width), F32),
            pltpu.VMEM((4, 2, 2, part, width), BF16),
            pltpu.VMEM((6,) + sums.shape, F32),
            pltpu.VMEM((5,) + sums.shape, F32),
            pltpu.SemaphoreType.DMA((5,)),
            pltpu.SemaphoreType.DMA((5,)),
        ] + Reducer.scratch(part, width)
    else:
        outs += [shape((width, width), BF16)] * 3 + [sums]
    return pl.pallas_call(
        functools.partial(late_kernel, sizes, planned),
        in_specs=[whole] * 12,
        out_specs=[whole] * len(outs),
        out_shape=outs,
        scratch_shapes=scratch,
        compiler_params=pltpu.CompilerParams(
            collective_id=2, has_side_effects=True, vmem_limit_bytes=60 * 2**20
        ),
        name="last_part",
    )(long_x, glob_x, dq, dk, dv, dmid, wq, wk, wv, gain, shift, table)


def has_plan():
    return (lax.axis_size("dp"), lax.axis_size("seq")) == (8, 4)


GELU_A = 0.7978845608028654
GELU_B = 0.044715


def gate_both(u):
    square = u * u
    turned = jnp.tanh(GELU_A * u * (1.0 + GELU_B * square))
    half = 0.5 * (1.0 + turned)
    slope = half + 0.5 * u * (1.0 - turned * turned) * (
        GELU_A * (1.0 + 3.0 * GELU_B * square)
    )
    return u * half, slope


def column_sum(rows):
    return jnp.sum(rows, 0, keepdims=True)


def ffn_kernel(
    sizes,
    planned,
    len_ref,
    attn_ref,
    long_ref,
    glob_ref,
    dlong_ref,
    dglob_ref,
    lq_ref,
    wo_ref,
    bo_ref,
    gain_ref,
    shift_ref,
    wi_ref,
    bi_ref,
    wr_ref,
    br_ref,
    long_out,
    glob_out,
    dmid_ref,
    do_ref,
    dog_ref,
    ldg_ref,
    *rest,
):
    block, count, quarter, seq_count, pairs = sizes
    if planned:
        pieces_ref, outer_ref, inner_ref, *rest = rest
    else:
        g_outer_ref, g_inner_ref, g_out_ref, vec_ref, *rest = rest
    (
        mid,
        rows_sum,
        slopes,
        normed,
        normed_t,
        dy,
        vectors,
        every_do,
        every_ld,
        every_out,
        gather_sends,
        gather_recvs,
        *rest,
    ) = rest
    if planned:
        even, odd, outer_out, inner_out, *rest = rest
        outer = Reducer(outer_out.shape[-2], 48, rest[:8], outgoing=outer_out, in_order=True)
        inner = Reducer(inner_out.shape[-2], 16, rest[8:], outgoing=inner_out)
    step = pl.program_id(0)
    chunk = lax.rem(step, 4)
    seq_index = lax.axis_index("seq")
    own_rows = pl.ds(pl.multiple_of(seq_index * quarter, quarter), quarter)
    width = mid.shape[1]
    piece = width // 32

    def gathers(kinds):
        for seq_step in range(1, seq_count):
            for kind in kinds:
                every = (every_do, every_ld, every_out)[kind]
                yield pltpu.make_async_remote_copy(
                    src_ref=every.at[own_rows],
                    dst_ref=every.at[own_rows],
                    send_sem=gather_sends.at[kind, seq_step - 1],
                    recv_sem=gather_recvs.at[kind, seq_step - 1],
                    device_id=seq_device(seq_step, seq_count),
                    device_id_type=pl.DeviceIdType.MESH,
                )

    @pl.when(step == 0)
    def _():
        others = [seq_device(seq_step, seq_count) for seq_step in range(1, seq_count)]
        meet(others + (outer.partners()[2:] if planned else []))
        projected = dot_n(attn_ref[...], wo_ref[...]) + bo_ref[...]
        mid[:block] = long_ref[...].astype(F32) + projected[:block]
        mid[block:] = glob_ref[own_rows].astype(F32) + projected[block:]
        hat, _ = row_norm(mid[...])
        normed[...] = (hat * gain_ref[...] + shift_ref[...]).astype(BF16)
        normed_t[...] = normed[...].T
        rows_sum[...] = mid[...] + br_ref[...]
        position = seq_index * block + lax.broadcasted_iota(jnp.int32, (block, 1), 0)
        dy[:block] = jnp.where(
            position < len_ref[0], dlong_ref[...].astype(F32), 0.0
        ).astype(BF16)
        dy[block:] = dglob_ref[own_rows]
        vectors[1:2] = column_sum(dy[...].astype(F32))

    def act(plan, reducer, now):
        for at, name, part in plan:
            if at == now:
                getattr(reducer, name)(part)

    if planned:
        for now in range(1, 8):

            @pl.when(step == now)
            def _(now=now):
                act(OUTER_PLAN, outer, now)
                act(INNER_PLAN, inner, now)

    @pl.when(step < 4)
    def _():
        active, slope = gate_both(dot_n(normed[...], wi_ref[...]) + bi_ref[...])
        slopes[chunk] = slope
        active = active.astype(BF16)
        g_outer = t_dot(active, dy[...])
        if planned:
            even[...] = g_outer
            for at in range(4):

                def value_of(side, at=at):
                    return even[pl.ds(pl.multiple_of((2 * at + side) * 4 * piece, 32), 4 * piece)]

                outer.fill(chunk, at // 2, at % 2, value_of)
            outer.start(chunk)
        else:
            g_outer_ref[...] = g_outer.astype(BF16)
        rows_sum[...] += dot_n(active, wr_ref[...])

    @pl.when(step == 4)
    def _():
        position = seq_index * block + lax.broadcasted_iota(jnp.int32, (block, 1), 0)
        every_out[own_rows] = rows_sum[block:].astype(BF16)
        for copy in gathers((2,)):
            copy.start()
        long_out[...] = jnp.where(position < len_ref[0], rows_sum[:block], 0.0).astype(BF16)
        rows_sum[...] = jnp.zeros_like(rows_sum)

    @pl.when(step >= 4)
    def _():
        hidden = dot_t(dy[...], wr_ref[...]) * slopes[chunk]
        for at in range(4):

            @pl.when(chunk == at)
            def _(at=at):
                vectors[4 + at : 5 + at] = column_sum(hidden)

        hidden = hidden.astype(BF16)
        rows_sum[...] += dot_t(hidden, wi_ref[...])
        g_inner = dot_n(normed_t[...], hidden)
        if planned:
            for now in range(4):

                @pl.when(chunk == now)
                def _(now=now):
                    (even, odd)[now % 2][...] = g_inner
                    if now % 2 == 0:
                        return

                    def pack(at, carry):
                        where = (lax.div(at, 4), lax.rem(lax.div(at, 2), 2), lax.rem(at, 2))

                        def value_of(side):
                            part = pl.ds(pl.multiple_of((2 * at + side) * piece, 8), piece)
                            return jnp.concatenate([even[part], odd[part]], 0)

                        if now == 1:
                            inner.fill(*where, value_of)
                        else:
                            for side in range(2):
                                pieces_ref[(side,) + where + (slice(0, 2 * piece),)] = value_of(
                                    side
                                ).astype(BF16)
                        return carry

                    lax.fori_loop(0, 16, pack, 0)
                    if now == 1:
                        for part in range(4):
                            inner.start(part)
        else:
            g_inner_ref[...] = g_inner.astype(BF16)

    def norm_back(rows):
        hat, inverse = row_norm(mid[rows])
        df = rows_sum[rows]
        scaled = df * gain_ref[...]
        dmid = dy[rows].astype(F32) + inverse * (
            scaled
            - jnp.mean(scaled, -1, keepdims=True)
            - hat * jnp.mean(scaled * hat, -1, keepdims=True)
        )
        dmid_ref[rows] = dmid
        low = dmid.astype(BF16)
        grad_o = dot_t(low, wo_ref[...]).astype(BF16)
        do_ref[rows] = grad_o
        return [column_sum(dmid), column_sum(df * hat), column_sum(df)], low, grad_o

    @pl.when(step == 7)
    def _():
        glob_sums, glob_low, grad_o = norm_back(slice(block, block + quarter))
        every_do[own_rows] = grad_o
        both = grad_o.astype(F32) * attn_ref[block:].astype(F32)
        stats = lq_ref[...]
        for head in range(2 * pairs):
            lanes = slice(head // 2 * PAIR, head // 2 * PAIR + PAIR)
            delta = jnp.sum(own_half(head % 2, both[:, lanes]), -1, keepdims=True)
            stats = jnp.where(lane_index() == HD + head, delta, stats)
        every_ld[own_rows] = stats
        for copy in gathers((0, 1)):
            copy.start()
        if planned:
            act(INNER_PLAN, inner, 8)
        long_sums, long_low, _ = norm_back(slice(0, block))
        for at, one, two in zip((0, 2, 3), long_sums, glob_sums):
            vectors[at : at + 1] = one + two
        if planned:
            act(INNER_PLAN, inner, 9)
        g_out = t_dot(attn_ref[...], jnp.concatenate([long_low, glob_low], 0))
        if planned:
            even[...] = g_out

            def pack(at, carry):
                for side in range(2):
                    part = pl.ds(pl.multiple_of((2 * at + side) * piece, 8), piece)
                    where = (side, lax.div(at, 4), lax.rem(lax.div(at, 2), 2), lax.rem(at, 2))
                    pieces_ref[where + (slice(2 * piece, 3 * piece + 8),)] = jnp.concatenate(
                        [even[part], vectors[...]], 0
                    ).astype(BF16)
                return carry

            lax.fori_loop(0, 16, pack, 0)
            act(INNER_PLAN, inner, 10)
            outer.finish(outer_ref)
            inner.finish(inner_ref)
        else:
            g_out_ref[...] = g_out.astype(BF16)
            vec_ref[...] = vectors[...]
        for copy in gathers((0, 1, 2)):
            copy.wait_recv()
        dog_ref[...] = every_do[...]
        ldg_ref[...] = every_ld[...]
        glob_out[...] = every_out[...]
        for copy in gathers((0, 1, 2)):
            copy.wait_send()


OUTER_PLAN = (
    (1, "add_core", 0),
    (2, "add_core", 1),
    (2, "add_first", 0),
    (3, "add_core", 2),
    (3, "add_first", 1),
    (3, "add_second", 0),
    (4, "add_core", 3),
    (4, "add_first", 2),
    (4, "add_second", 1),
    (5, "add_first", 3),
    (5, "add_second", 2),
    (6, "add_second", 3),
)
INNER_PLAN = (
    (7, "add_core", 0),
    (7, "add_core", 1),
    (7, "add_core", 2),
    (7, "add_core", 3),
    (8, "add_first", 0),
    (9, "add_first", 1),
    (9, "add_second", 0),
    (10, "add_first", 2),
    (10, "add_second", 1),
    (10, "add_first", 3),
    (10, "add_second", 2),
    (10, "add_second", 3),
)


def feed_forward(sizes, planned, doc_len, attn, long_x, glob_x, dlong, dglob, lq, *weights):
    block, count, quarter, seq_count, pairs = sizes
    wo, bo, gain, shift, wi, bi, wr, br = weights
    width, hidden = wi.shape
    chunk = hidden // 4
    rows = block + quarter
    whole = pl.BlockSpec(memory_space=pltpu.VMEM)
    shape = jax.ShapeDtypeStruct
    in_specs = [pl.BlockSpec(memory_space=pltpu.SMEM)] + [whole] * 10
    in_specs += [
        pl.BlockSpec((width, chunk), lambda c: (0, lax.rem(c, 4))),
        pl.BlockSpec((1, chunk), lambda c: (0, lax.rem(c, 4))),
        pl.BlockSpec((chunk, width), lambda c: (lax.rem(c, 4), 0)),
        whole,
    ]
    outs = [
        shape((block, width), BF16),
        shape((GP, width), BF16),
        shape((rows, width), F32),
        shape((rows, width), BF16),
        shape((GP, width), BF16),
        shape((GP, PAIR), F32),
    ]
    out_specs = [whole] * 6
    others = seq_count - 1
    scratch = [
        pltpu.VMEM((rows, width), F32),
        pltpu.VMEM((rows, width), F32),
        pltpu.VMEM((4, rows, chunk), F32),
        pltpu.VMEM((rows, width), BF16),
        pltpu.VMEM((width, rows), BF16),
        pltpu.VMEM((rows, width), BF16),
        pltpu.VMEM((8, width), F32),
        pltpu.VMEM((GP, width), BF16),
        pltpu.VMEM((GP, PAIR), F32),
        pltpu.VMEM((GP, width), BF16),
        pltpu.SemaphoreType.DMA((3, others)),
        pltpu.SemaphoreType.DMA((3, others)),
    ]
    if planned:
        part, piece = hidden // 32, width // 32
        outs += [
            shape((2, 4, 2, 2, 3 * piece + 8, width), BF16),
            shape((part, width), F32),
            shape((2 * piece, width), F32),
        ]
        out_specs += [whole] * 3
        scratch += [
            pltpu.VMEM((width, chunk), F32),
            pltpu.VMEM((width, chunk), F32),
            pltpu.VMEM((4, 2, 2, part, width), BF16),
            pltpu.VMEM((4, 2, 2, 2 * piece, width), BF16),
        ]
        scratch += Reducer.scratch(part, width) + Reducer.scratch(2 * piece, width)
    else:
        outs += [
            shape((hidden, width), BF16),
            shape((width, hidden), BF16),
            shape((width, width), BF16),
            shape((8, width), F32),
        ]
        out_specs += [
            pl.BlockSpec((chunk, width), lambda c: (lax.min(c, 3), 0)),
            pl.BlockSpec((width, chunk), lambda c: (0, lax.max(c - 4, 0))),
            whole,
            whole,
        ]
    return pl.pallas_call(
        functools.partial(ffn_kernel, sizes, planned),
        grid=(8,),
        in_specs=in_specs,
        out_specs=out_specs,
        out_shape=outs,
        scratch_shapes=scratch,
        compiler_params=pltpu.CompilerParams(
            collective_id=4, has_side_effects=True, vmem_limit_bytes=62 * 2**20
        ),
        name="feed_forward",
    )(doc_len, attn, long_x, glob_x, dlong, dglob, lq, wo, bo, gain, shift, wi, bi, wr, br)


def back_kernel(
    sizes,
    early_rows,
    len_ref,
    tab_ref,
    q_ref,
    kx_ref,
    vx_ref,
    kg_ref,
    vg_ref,
    o_ref,
    do_ref,
    l_ref,
    dog_ref,
    ldg_ref,
    *rest,
):
    block, count, quarter, seq_count, pairs = sizes
    reduces = early_rows > 0
    if reduces:
        pieces_ref, rest = rest[0], rest[1:]
    dq_ref, dk_ref, dv_ref, dtab_ref, *rest = rest
    if reduces:
        early_ref, rest = rest[0], rest[1:]
    (
        dkx,
        dvx,
        dkg,
        dvg,
        q_send,
        q_recv,
        kv_send,
        kv_recv,
        halo_send,
        halo_recv,
        glob_sends,
        glob_recvs,
        halo_sends,
        halo_recvs,
        *rest,
    ) = rest
    number = pl.program_id(0)
    pair = lax.rem(number, pairs)
    seq_index = lax.axis_index("seq")
    reducer = Reducer(early_rows, 16, rest, pieces=pieces_ref) if reduces else None
    scale = HD ** (-0.5)
    low_lanes = lane_index() < HD
    own_keys = slice(HALO, HALO + block)
    own_rows = pl.ds(pl.multiple_of(seq_index * quarter, quarter), quarter)

    def glob_copies(kind, at):
        source, dest = ((q_send, q_recv), (kv_send, kv_recv))[kind]
        for step in range(1, seq_count):
            device = seq_device(step, seq_count)
            yield pltpu.make_async_remote_copy(
                src_ref=source.at[device[1], at],
                dst_ref=dest.at[step - 1, at],
                send_sem=glob_sends.at[kind, step - 1, at],
                recv_sem=glob_recvs.at[kind, step - 1, at],
                device_id=device,
                device_id_type=pl.DeviceIdType.MESH,
            )

    def halo_copy(direction, at):
        return pltpu.make_async_remote_copy(
            src_ref=halo_send.at[direction, at],
            dst_ref=halo_recv.at[direction, at],
            send_sem=halo_sends.at[direction, at],
            recv_sem=halo_recvs.at[direction, at],
            device_id=seq_device(2 * direction - 1, seq_count),
            device_id_type=pl.DeviceIdType.MESH,
        )

    has_low, has_high = seq_index > 0, seq_index < seq_count - 1
    sends_to = (has_low, has_high)
    gets_from = (has_high, has_low)

    def close_pair(at):
        lanes = lanes_of(at)
        for direction in range(2):

            @pl.when(gets_from[direction])
            def _(direction=direction):
                halo_copy(direction, at).wait_recv()

        for kind, (total, out) in enumerate(((dkx, dk_ref), (dvx, dv_ref))):
            first, last = HALO + REACH, HALO + block - REACH
            out[:REACH, lanes] = (
                total[at, HALO:first] + halo_recv[1, at, kind].astype(F32)
            ).astype(BF16)
            out[REACH : block - REACH, lanes] = total[at, first:last].astype(BF16)
            out[block - REACH : block, lanes] = (
                total[at, last : HALO + block] + halo_recv[0, at, kind].astype(F32)
            ).astype(BF16)
        sums = []
        for kind, (source, dest) in enumerate(((q_send, q_recv), (kv_send, kv_recv))):
            total = source[seq_index, at].astype(F32)
            for step, copy in enumerate(glob_copies(kind, at)):
                copy.wait_recv()
                total += dest[step, at].astype(F32)
            sums.append(total.astype(BF16))
        dq_ref[block:, lanes] = sums[0]
        dk_ref[block:, lanes] = sums[1][:, :PAIR]
        dv_ref[block:, lanes] = sums[1][:, PAIR:]

    def run_plan(now):
        for at, act, chunk in EARLY_PLAN:
            if now == at:
                getattr(reducer, act)(chunk)

    @pl.when(number == 0)
    def _():
        others = [seq_device(step, seq_count) for step in range(1, seq_count)]
        meet(others + (reducer.partners()[2:] if reduces else []))
        if reduces:
            for chunk in range(4):
                reducer.start(chunk)
        for direction in range(2):

            @pl.when(jnp.logical_not(gets_from[direction]))
            def _(direction=direction):
                halo_recv[direction] = jnp.zeros_like(halo_recv[direction])

    if reduces:
        for now in range(1, 2 * pairs):
            if any(at == now for at, _, _ in EARLY_PLAN):

                @pl.when(number == now)
                def _(now=now):
                    run_plan(now)

    @pl.when(number < pairs)
    def _():
        long_bias = key_bias(seq_index * block, block, len_ref[0])
        near_bias = key_bias(seq_index * quarter, quarter, count)
        query = q_ref[block:] * jnp.asarray(scale, BF16)
        grad_o = dog_ref[...]
        far_k, far_v = kx_ref[own_keys], vx_ref[own_keys]
        near_k, near_v = kg_ref[own_rows], vg_ref[own_rows]
        outs, kept = [], []
        for head in range(2):
            norm = in_three(-pick_column(ldg_ref[...], 2 * pair + head))
            delta = in_three(-pick_column(ldg_ref[...], HD + 2 * pair + head))
            qa = with_lanes(head, query, (1.0,) + norm)
            doa = with_lanes(head, grad_o, delta)
            far = jnp.exp(dot_t(qa, key_side(head, far_k, long_bias)))
            near = jnp.exp(dot_t(qa, key_side(head, near_k, near_bias)))
            far_ds = (far * dot_t(doa, value_side(head, far_v))).astype(BF16)
            near_ds = (near * dot_t(doa, value_side(head, near_v))).astype(BF16)
            outs.append(dot_n(far_ds, far_k) + dot_n(near_ds, near_k))
            kept.append(
                (
                    own_half(head, query),
                    own_half(head, grad_o),
                    far.astype(BF16),
                    near.astype(BF16),
                    far_ds,
                    near_ds,
                )
            )
        own_q, own_do, far, near, far_ds, near_ds = (
            jnp.concatenate(part, 0) for part in zip(*kept)
        )
        for total, edge in ((dkx, own_keys), (dvx, own_keys)):
            total[pair, :HALO] = jnp.zeros((HALO, PAIR), F32)
            total[pair, HALO + block :] = jnp.zeros((HALO, PAIR), F32)
        dkx[pair, own_keys] = t_dot(far_ds, own_q)
        dvx[pair, own_keys] = t_dot(far, own_do)
        dkg[pair] = jnp.zeros((GP, PAIR), F32)
        dvg[pair] = jnp.zeros((GP, PAIR), F32)
        dkg[pair, own_rows] = t_dot(near_ds, own_q)
        dvg[pair, own_rows] = t_dot(near, own_do)
        glob_dq = (jnp.where(low_lanes, outs[0], outs[1]) * scale).astype(BF16)
        q_send[:, pair] = glob_dq.reshape(seq_count, quarter, PAIR)
        for copy in glob_copies(0, pair):
            copy.start()

    @pl.when(number >= pairs)
    def _():
        long_bias = key_bias(seq_index * block - HALO, block + 2 * HALO, len_ref[0])
        glob_bias = key_bias(0, GP, count)
        query = q_ref[:block] * jnp.asarray(scale, BF16)
        grad_o = do_ref[...]
        both = grad_o.astype(F32) * o_ref[...].astype(F32)
        heads = []
        for head in range(2):
            norm = in_three(-pick_column(l_ref[...], 2 * pair + head))
            delta = in_three(-jnp.sum(own_half(head, both), -1, keepdims=True))
            heads.append(
                dict(
                    q=own_half(head, query),
                    do=own_half(head, grad_o),
                    qa=with_lanes(head, query, (1.0,) + norm),
                    doa=with_lanes(head, grad_o, delta),
                    kxa=key_side(head, kx_ref[...], long_bias),
                    vxa=value_side(head, vx_ref[...]),
                    kga=key_side(head, kg_ref[...], glob_bias),
                    vga=value_side(head, vg_ref[...]),
                    bias=band_bias(tab_ref[0, head : head + 1]),
                )
            )
        table_sums = [0.0, 0.0]
        grads_q = []
        for start in range(0, block, SUB):
            rows, keys = slice(start, start + SUB), slice(start, start + WINDOW)
            outs, probs, grads = [], [], []
            for head, own in enumerate(heads):
                band = jnp.exp(dot_t(own["qa"][rows], own["kxa"][keys]) + own["bias"])
                band_ds = band * dot_t(own["doa"][rows], own["vxa"][keys])
                table_sums[head] += band_ds
                glob = jnp.exp(dot_t(own["qa"][rows], own["kga"]))
                glob_ds = (glob * dot_t(own["doa"][rows], own["vga"])).astype(BF16)
                band_ds = band_ds.astype(BF16)
                outs.append(dot_n(band_ds, kx_ref[keys]) + dot_n(glob_ds, kg_ref[...]))
                probs.append((band.astype(BF16), glob.astype(BF16)))
                grads.append((band_ds, glob_ds))
            grads_q.append(jnp.where(low_lanes, outs[0], outs[1]))
            own_q = jnp.concatenate([own["q"][rows] for own in heads], 0)
            own_do = jnp.concatenate([own["do"][rows] for own in heads], 0)
            band, glob = (jnp.concatenate(part, 0) for part in zip(*probs))
            band_ds, glob_ds = (jnp.concatenate(part, 0) for part in zip(*grads))
            dkx[pair, keys] += t_dot(band_ds, own_q)
            dvx[pair, keys] += t_dot(band, own_do)
            dkg[pair] += t_dot(glob_ds, own_q)
            dvg[pair] += t_dot(glob, own_do)
        for kind, total in enumerate((dkg, dvg)):
            kv_send[:, pair, :, kind * PAIR : (kind + 1) * PAIR] = (
                total[pair].astype(BF16).reshape(seq_count, quarter, PAIR)
            )
        for copy in glob_copies(1, pair):
            copy.start()
        for kind, total in enumerate((dkx, dvx)):
            for direction, first in enumerate((HALO - REACH, HALO + block)):
                halo_send[direction, pair, kind] = total[pair, first : first + REACH].astype(BF16)
        for direction in range(2):

            @pl.when(sends_to[direction])
            def _(direction=direction):
                halo_copy(direction, pair).start()

        dq_ref[:block, lanes_of(pair)] = (jnp.concatenate(grads_q, 0) * scale).astype(BF16)
        for head in range(2):
            dtab_ref[pair, head : head + 1] = diagonal_sums(table_sums[head])

    @pl.when(number > pairs)
    def _():
        close_pair(pair - 1)

    @pl.when(number == 2 * pairs - 1)
    def _():
        if reduces:
            run_plan(2 * pairs)
        close_pair(pairs - 1)
        for at in range(pairs):
            for kind in range(2):
                for copy in glob_copies(kind, at):
                    copy.wait_send()
            for direction in range(2):

                @pl.when(sends_to[direction])
                def _(direction=direction, at=at):
                    halo_copy(direction, at).wait_send()

        if reduces:
            reducer.finish(early_ref)


def attend_back(sizes, doc_len, table, q, kx, vx, kg, vg, o, do, l, dog, ldg, pieces=None):
    block, count, quarter, seq_count, pairs = sizes
    width = q.shape[1]
    early_rows = 0 if pieces is None else pieces.shape[-2]
    ext = block + 2 * HALO
    cols = lambda rows: pl.BlockSpec((rows, PAIR), lambda i: (0, lax.rem(i, pairs)))
    whole = pl.BlockSpec(memory_space=pltpu.VMEM)
    shape = jax.ShapeDtypeStruct
    in_specs = [
        pl.BlockSpec(memory_space=pltpu.SMEM),
        pl.BlockSpec((1, 2, WINDOW), lambda i: (lax.rem(i, pairs), 0, 0)),
        cols(block + GP),
        cols(ext),
        cols(ext),
        cols(GP),
        cols(GP),
        cols(block),
        cols(block),
        whole,
        cols(GP),
        whole,
    ]
    rows = block + quarter
    outs = [shape((rows, width), BF16)] * 3 + [shape((pairs, 2, WINDOW), F32)]
    others = seq_count - 1
    scratch = [
        pltpu.VMEM((pairs, ext, PAIR), F32),
        pltpu.VMEM((pairs, ext, PAIR), F32),
        pltpu.VMEM((pairs, GP, PAIR), F32),
        pltpu.VMEM((pairs, GP, PAIR), F32),
        pltpu.VMEM((seq_count, pairs, quarter, PAIR), BF16),
        pltpu.VMEM((others, pairs, quarter, PAIR), BF16),
        pltpu.VMEM((seq_count, pairs, quarter, 2 * PAIR), BF16),
        pltpu.VMEM((others, pairs, quarter, 2 * PAIR), BF16),
        pltpu.VMEM((2, pairs, 2, REACH, PAIR), BF16),
        pltpu.VMEM((2, pairs, 2, REACH, PAIR), BF16),
        pltpu.SemaphoreType.DMA((2, others, pairs)),
        pltpu.SemaphoreType.DMA((2, others, pairs)),
        pltpu.SemaphoreType.DMA((2, pairs)),
        pltpu.SemaphoreType.DMA((2, pairs)),
    ]
    args = [doc_len, table, q, kx, vx, kg, vg, o, do, l, dog, ldg]
    if early_rows:
        in_specs.append(pl.BlockSpec(memory_space=pl.ANY))
        outs.append(shape((early_rows, width), F32))
        scratch += Reducer.scratch(early_rows, width)
        args.append(pieces)
    return pl.pallas_call(
        functools.partial(back_kernel, sizes, early_rows),
        grid=(2 * pairs,),
        in_specs=in_specs,
        out_specs=[whole] * len(outs),
        out_shape=outs,
        scratch_shapes=scratch,
        compiler_params=pltpu.CompilerParams(
            collective_id=1, has_side_effects=True, vmem_limit_bytes=60 * 2**20
        ),
        name="attend_back",
    )(*args)


def on_device(
    long_input,
    global_input,
    lengths,
    w_query,
    b_query,
    w_key,
    w_value,
    b_value,
    w_out,
    b_out,
    w_inner,
    b_inner,
    w_outer,
    b_outer,
    norm1_gain,
    norm1_shift,
    norm2_gain,
    norm2_shift,
    rel_table,
    long_cotangent,
    global_cotangent,
):
    seq_count = lax.axis_size("seq")
    data_count = lax.axis_size("dp")
    seq_index = lax.axis_index("seq")
    block = long_input.shape[1]
    count = global_input.shape[1]
    width = long_input.shape[2]
    heads = rel_table.shape[1]
    pairs = heads // 2
    labels = 2 * R + 1
    quarter = GP // seq_count
    sizes = Sizes(block, count, quarter, seq_count, pairs)
    table = jnp.pad(
        rel_table.T,
        ((0, 0), (HALO - R, WINDOW - labels - HALO + R)),
        constant_values=MASKED,
    ).reshape(pairs, 2, WINDOW)

    glob_x = jnp.pad(global_input[0], ((0, GP - count), (0, 0)))
    glob_dy = jnp.pad(global_cotangent[0], ((0, GP - count), (0, 0)))
    row = lambda vector: vector.reshape(1, -1)
    queries, kx, vx, kg, vg, attn_low, long_l, glob_l = attend(
        sizes,
        lengths,
        table,
        long_input[0],
        glob_x,
        w_query,
        w_key,
        w_value,
        row(b_query),
        row(b_value),
        row(norm1_gain),
        row(norm1_shift),
    )

    planned = has_plan()
    long_result, glob_out, grad_mid, grad_attn, every_do, every_ld, *gradients = feed_forward(
        sizes,
        planned,
        lengths,
        attn_low,
        long_input[0],
        glob_x,
        long_cotangent[0],
        glob_dy,
        glob_l,
        w_out,
        row(b_out),
        row(norm2_gain),
        row(norm2_shift),
        w_inner,
        row(b_inner),
        w_outer,
        row(b_outer),
    )
    query_low, key_low, value_low, dtab, *early = attend_back(
        sizes,
        lengths,
        table,
        queries,
        kx,
        vx,
        kg,
        vg,
        attn_low,
        grad_attn,
        long_l,
        every_do,
        every_ld,
        *(gradients[:1] if planned else []),
    )
    devices = data_count * seq_count
    piece = width // devices
    own_part = lambda vector: lax.dynamic_slice_in_dim(
        vector,
        (lax.axis_index("dp") * seq_count + seq_index) * (vector.shape[0] // devices),
        vector.shape[0] // devices,
    )
    long_grad, glob_grad, *late, sums = last_part(
        sizes,
        planned,
        long_input[0],
        glob_x,
        query_low,
        key_low,
        value_low,
        grad_mid,
        w_query,
        w_key,
        w_value,
        row(norm1_gain),
        row(norm1_shift),
        dtab.reshape(heads, WINDOW),
    )
    if planned:
        _, g_outer, inner_one = gradients
        early, late = early[0], late[0]
        g_inner = jnp.concatenate([inner_one, early[: 2 * piece]], 0)
        g_inner = g_inner.reshape(4, piece, width).transpose(1, 0, 2).reshape(piece, -1)
        g_out, early_vectors = early[2 * piece : 3 * piece], early[3 * piece :]
        g_query, g_key, g_value = (late[i * piece : (i + 1) * piece] for i in range(3))
    else:
        g_outer, g_inner, g_out, early_vectors = gradients
        g_outer, g_inner, g_out, g_query, g_key, g_value = (
            lax.psum_scatter(g.astype(BF16), ("dp", "seq"), scatter_dimension=0, tiled=True).astype(
                F32
            )
            for g in (g_outer, g_inner, g_out, *late)
        )
        early_vectors, sums = lax.psum((early_vectors, sums), ("dp", "seq"))
    vectors, table_total = sums[heads:], sums[:heads]
    g_b_query, g_b_value, g_g1, g_s1 = (own_part(vectors[i]) for i in range(4))
    g_b_out, g_b_outer, g_g2, g_s2 = (own_part(early_vectors[i]) for i in range(4))
    g_b_inner = own_part(early_vectors[4:].reshape(-1))
    table_total = table_total[:, HALO - R : HALO - R + labels].T
    return (
        long_result[None],
        glob_out[:count][None],
        long_grad[None],
        glob_grad[:count][None],
        g_query,
        g_b_query,
        g_key,
        g_value,
        g_b_value,
        g_out,
        g_b_out,
        g_inner,
        g_b_inner,
        g_outer,
        g_b_outer,
        g_g1,
        g_s1,
        g_g2,
        g_s2,
        table_total,
    )


def solution(mesh):
    rows, whole = P("dp", "seq", None), P("dp", None, None)
    matrix, vector = P(("dp", "seq"), None), P(("dp", "seq"))
    return jax.shard_map(
        on_device,
        mesh=mesh,
        in_specs=(rows, whole, P("dp")) + (P(),) * 16 + (rows, whole),
        out_specs=(
            rows,
            whole,
            rows,
            whole,
            matrix,
            vector,
            matrix,
            matrix,
            vector,
            matrix,
            vector,
            matrix,
            vector,
            matrix,
            vector,
            vector,
            vector,
            vector,
            vector,
            P(),
        ),
        check_vma=False,
    )
```

```python
import functools
from typing import NamedTuple

import jax
import jax.numpy as jnp
from jax import lax
from jax.experimental import pallas as pl
from jax.experimental.pallas import tpu as pltpu
from jax.sharding import PartitionSpec as P

HD = 64
R = 84
PAIR = 2 * HD
HALO = 128
REACH = 96
GP = 256
SUB = 256
WINDOW = SUB + 2 * HALO
EPSILON = 1e-05
MASKED = -1e30
F32 = jnp.float32
BF16 = jnp.bfloat16


def dot_t(left, right):
    return lax.dot_general(left, right, (((1,), (1,)), ((), ())), preferred_element_type=F32)


def dot_n(left, right):
    return lax.dot_general(left, right, (((1,), (0,)), ((), ())), preferred_element_type=F32)


def t_dot(left, right):
    return lax.dot_general(left, right, (((0,), (0,)), ((), ())), preferred_element_type=F32)


def band_bias(table_row):
    spread = jnp.broadcast_to(table_row, (SUB, WINDOW))
    return pltpu.roll(spread, 0, 1, stride=1, stride_axis=0)


def diagonal_sums(rows):
    height, width = rows.shape
    while height > 8:
        height //= 2
        rows = rows[:height] + pltpu.roll(rows[height:], width - height, 1)
    row = lax.broadcasted_iota(jnp.int32, rows.shape, 0)
    for bit in (1, 2, 4):
        rows = jnp.where((row & bit) != 0, pltpu.roll(rows, width - bit, 1), rows)
    return jnp.sum(rows, 0, keepdims=True)


def lane_index():
    return lax.broadcasted_iota(jnp.int32, (1, PAIR), 1)


def own_half(head, value):
    low_lanes = lane_index() < HD
    return jnp.where(low_lanes if head == 0 else ~low_lanes, value, jnp.zeros_like(value))


def other_lane(head):
    return HD * (1 - head)


def with_lanes(head, value, columns):
    wide = own_half(head, value.astype(F32))
    lane = lane_index()
    for offset, column in enumerate(columns):
        wide = jnp.where(lane == other_lane(head) + offset, column, wide)
    return wide.astype(BF16)


def in_three(column):
    high = column.astype(BF16).astype(F32)
    middle = (column - high).astype(BF16).astype(F32)
    return (high, middle, column - high - middle)


def key_bias(first, rows, end):
    position = first + lax.broadcasted_iota(jnp.int32, (rows, 1), 0)
    return jnp.where((position >= 0) & (position < end), 0.0, MASKED)


def pick_column(rows, index):
    return jnp.sum(jnp.where(lane_index() == index, rows, 0.0), -1, keepdims=True)


def key_side(head, keys, bias):
    return with_lanes(head, keys, (bias, 1.0, 1.0, 1.0))


def value_side(head, values):
    return with_lanes(head, values, (1.0, 1.0, 1.0))


def softmax_rows(parts, value_parts, head):
    top = functools.reduce(
        jnp.maximum, [jnp.max(part, -1, keepdims=True) for part in parts]
    )
    mixed = sum(
        dot_n(jnp.exp(part - top).astype(BF16), values)
        for part, values in zip(parts, value_parts)
    )
    at = other_lane(head)
    total = mixed[:, at : at + 1]
    return mixed / total, top + jnp.log(total)


def seq_device(steps, seq_count):
    return (lax.axis_index("dp"), lax.rem(lax.axis_index("seq") + steps + seq_count, seq_count))


def row_norm(rows):
    centred = rows - jnp.mean(rows, -1, keepdims=True)
    inverse = lax.rsqrt(jnp.mean(centred * centred, -1, keepdims=True) + EPSILON)
    return centred * inverse, inverse


def put_column(ref, rows, index, column):
    ref[rows] = jnp.where(lane_index() == index, column, ref[rows])


def lanes_of(at):
    return pl.ds(pl.multiple_of(at * PAIR, PAIR), PAIR)


class Sizes(NamedTuple):
    block: int
    count: int
    quarter: int
    seq_count: int
    pairs: int


def attend_kernel(
    sizes,
    len_ref,
    rel_ref,
    long_ref,
    raw_ref,
    wq_ref,
    wk_ref,
    wv_ref,
    bq_ref,
    bv_ref,
    gain_ref,
    shift_ref,
    q_ref,
    kx_ref,
    vx_ref,
    kg_ref,
    vg_ref,
    o_ref,
    l_ref,
    lq_ref,
    glob_ref,
    tab_ref,
    spread,
    wide,
    part_o,
    part_l,
    from_o,
    from_l,
    halo_sends,
    halo_recvs,
    part_sends,
    part_recvs,
):
    block, count, quarter, seq_count, pairs = sizes
    ext = block + 2 * HALO
    seq_index = lax.axis_index("seq")
    scale = jnp.asarray(HD ** (-0.5), BF16)
    low_lanes = lane_index() < HD
    own_keys = slice(HALO, HALO + block)
    own_rows = pl.ds(pl.multiple_of(seq_index * quarter, quarter), quarter)
    neighbours = (seq_index > 0, seq_index < seq_count - 1)
    barrier = pltpu.get_barrier_semaphore()
    for step in range(1, seq_count):
        pl.semaphore_signal(
            barrier,
            inc=1,
            device_id=seq_device(step, seq_count),
            device_id_type=pl.DeviceIdType.MESH,
        )

    def halo_copies(direction):
        source = HALO if direction == 0 else HALO + block - REACH
        dest = HALO + block if direction == 0 else HALO - REACH
        for kind, ref in enumerate((kx_ref, vx_ref)):
            yield pltpu.make_async_remote_copy(
                src_ref=ref.at[source : source + REACH],
                dst_ref=ref.at[dest : dest + REACH],
                send_sem=halo_sends.at[direction, kind],
                recv_sem=halo_recvs.at[direction, kind],
                device_id=seq_device(2 * direction - 1, seq_count),
                device_id_type=pl.DeviceIdType.MESH,
            )

    def part_copies():
        for step in range(1, seq_count):
            device = seq_device(step, seq_count)
            rows = pl.ds(pl.multiple_of(device[1] * quarter, quarter), quarter)
            for kind, (source, dest) in enumerate(((part_o, from_o), (part_l, from_l))):
                yield step, kind, pltpu.make_async_remote_copy(
                    src_ref=source.at[rows],
                    dst_ref=dest.at[step - 1],
                    send_sem=part_sends.at[kind, step - 1],
                    recv_sem=part_recvs.at[kind, step - 1],
                    device_id=device,
                    device_id_type=pl.DeviceIdType.MESH,
                )

    gain, shift = gain_ref[...], shift_ref[...]
    labels, heads = rel_ref.shape
    spread[...] = jnp.full(spread.shape, MASKED, F32)
    spread[:labels, :heads] = rel_ref[...]
    turned = pltpu.roll(spread[...].T, HALO - R, 1)
    for pair in range(pairs):
        tab_ref[pair] = turned[2 * pair : 2 * pair + 2]
    normed_long = (row_norm(long_ref[...].astype(F32))[0] * gain + shift).astype(BF16)
    kx_ref[own_keys] = dot_n(normed_long, wk_ref[...]).astype(BF16)
    vx_ref[own_keys] = (dot_n(normed_long, wv_ref[...]) + bv_ref[...]).astype(BF16)
    pl.semaphore_wait(barrier, seq_count - 1)
    for direction, first in enumerate((HALO - REACH, HALO + block)):

        @pl.when(neighbours[direction])
        def _(direction=direction):
            for copy in halo_copies(direction):
                copy.start()

        outer = slice(0, first) if direction == 0 else slice(first + REACH, ext)
        for ref in (kx_ref, vx_ref):
            ref[outer] = jnp.zeros((HALO - REACH, ref.shape[1]), BF16)

        @pl.when(jnp.logical_not(neighbours[direction]))
        def _(first=first):
            for ref in (kx_ref, vx_ref):
                ref[first : first + REACH] = jnp.zeros((REACH, ref.shape[1]), BF16)

    wide[...] = jnp.zeros_like(wide)
    wide[:count] = raw_ref[...].astype(F32)
    glob_ref[...] = wide[...].astype(BF16)
    normed_glob = (row_norm(wide[...])[0] * gain + shift).astype(BF16)
    kg_ref[...] = dot_n(normed_glob, wk_ref[...]).astype(BF16)
    vg_ref[...] = (dot_n(normed_glob, wv_ref[...]) + bv_ref[...]).astype(BF16)
    q_ref[block:] = (dot_n(normed_glob, wq_ref[...]) + bq_ref[...]).astype(BF16)
    q_ref[:block] = (dot_n(normed_long, wq_ref[...]) + bq_ref[...]).astype(BF16)
    part_l[...] = jnp.zeros_like(part_l)
    l_ref[...] = jnp.zeros_like(l_ref)

    def glob_pair(pair, carry):
        lanes = lanes_of(pair)
        far_bias = key_bias(seq_index * block, block, len_ref[0])
        near_bias = key_bias(seq_index * quarter, quarter, count)
        query = q_ref[block:, lanes] * scale
        outs = []
        for head in range(2):
            q = with_lanes(head, query, (1.0,))
            far = dot_t(q, with_lanes(head, kx_ref[own_keys, lanes], (far_bias,)))
            near = dot_t(q, with_lanes(head, kg_ref[own_rows, lanes], (near_bias,)))
            out, norm = softmax_rows(
                [far, near],
                [
                    with_lanes(head, vx_ref[own_keys, lanes], (1.0,)),
                    with_lanes(head, vg_ref[own_rows, lanes], (1.0,)),
                ],
                head,
            )
            outs.append(out)
            put_column(part_l, slice(None), 2 * pair + head, norm)
        part_o[:, lanes] = jnp.where(low_lanes, outs[0], outs[1]).astype(BF16)
        return carry

    lax.fori_loop(0, pairs, glob_pair, 0)
    for _, _, copy in part_copies():
        copy.start()
    for direction in range(2):

        @pl.when(neighbours[1 - direction])
        def _(direction=direction):
            for copy in halo_copies(direction):
                copy.wait_recv()

    def long_pair(pair, carry):
        lanes = lanes_of(pair)
        long_bias = key_bias(seq_index * block - HALO, ext, len_ref[0])
        glob_bias = key_bias(0, GP, count)
        query = q_ref[:block, lanes] * scale
        outs = []
        for head in range(2):
            q = with_lanes(head, query, (1.0,))
            kx = with_lanes(head, kx_ref[:, lanes], (long_bias,))
            kg = with_lanes(head, kg_ref[:, lanes], (glob_bias,))
            vx, vg = (with_lanes(head, ref[:, lanes], (1.0,)) for ref in (vx_ref, vg_ref))
            bias = band_bias(tab_ref[pair, head : head + 1])
            mixed = []
            for start in range(0, block, SUB):
                rows, keys = slice(start, start + SUB), slice(start, start + WINDOW)
                out, norm = softmax_rows(
                    [dot_t(q[rows], kx[keys]) + bias, dot_t(q[rows], kg)], [vx[keys], vg], head
                )
                mixed.append(out)
                put_column(l_ref, rows, 2 * pair + head, norm)
            outs.append(jnp.concatenate(mixed, 0))
        o_ref[:block, lanes] = jnp.where(low_lanes, outs[0], outs[1]).astype(BF16)
        return carry

    lax.fori_loop(0, pairs, long_pair, 0)
    for _, _, copy in part_copies():
        copy.wait_recv()
    norms = [part_l[own_rows]] + [from_l[step] for step in range(seq_count - 1)]
    outs = [part_o[own_rows]] + [from_o[step] for step in range(seq_count - 1)]
    top = functools.reduce(jnp.maximum, norms)
    shares = [jnp.exp(norm - top) for norm in norms]
    total = sum(shares)
    lq_ref[...] = top + jnp.log(total)
    shares = [share / total for share in shares]
    for at in range(pairs):
        lanes = slice(at * PAIR, (at + 1) * PAIR)
        mixed = 0.0
        for share, out in zip(shares, outs):
            spread = jnp.where(
                low_lanes, share[:, 2 * at : 2 * at + 1], share[:, 2 * at + 1 : 2 * at + 2]
            )
            mixed += spread * out[:, lanes].astype(F32)
        o_ref[block:, lanes] = mixed.astype(BF16)
    for _, _, copy in part_copies():
        copy.wait_send()
    for direction in range(2):

        @pl.when(neighbours[direction])
        def _(direction=direction):
            for copy in halo_copies(direction):
                copy.wait_send()


def attend(sizes, doc_len, rel_table, long_x, glob_x, *weights):
    block, count, quarter, seq_count, pairs = sizes
    width = long_x.shape[1]
    ext = block + 2 * HALO
    whole = pl.BlockSpec(memory_space=pltpu.VMEM)
    shape = jax.ShapeDtypeStruct
    others = seq_count - 1
    return pl.pallas_call(
        functools.partial(attend_kernel, sizes),
        in_specs=[pl.BlockSpec(memory_space=pltpu.SMEM)] + [whole] * 10,
        out_specs=[whole] * 10,
        out_shape=[
            shape((block + GP, width), BF16),
            shape((ext, width), BF16),
            shape((ext, width), BF16),
            shape((GP, width), BF16),
            shape((GP, width), BF16),
            shape((block + quarter, width), BF16),
            shape((block, PAIR), F32),
            shape((quarter, PAIR), F32),
            shape((GP, width), BF16),
            shape((pairs, 2, WINDOW), F32),
        ],
        scratch_shapes=[
            pltpu.VMEM((WINDOW, PAIR), F32),
            pltpu.VMEM((GP, width), F32),
            pltpu.VMEM((GP, width), BF16),
            pltpu.VMEM((GP, PAIR), F32),
            pltpu.VMEM((others, quarter, width), BF16),
            pltpu.VMEM((others, quarter, PAIR), F32),
            pltpu.SemaphoreType.DMA((2, 2)),
            pltpu.SemaphoreType.DMA((2, 2)),
            pltpu.SemaphoreType.DMA((2, others)),
            pltpu.SemaphoreType.DMA((2, others)),
        ],
        compiler_params=pltpu.CompilerParams(
            collective_id=3, has_side_effects=True, vmem_limit_bytes=56 * 2**20
        ),
        name="attend",
    )(doc_len, rel_table, long_x, glob_x, *weights)


class Reducer:
    def __init__(self, rows, split, scratch, pieces=None, order=None):
        self.ids = mesh_ids()
        self.order = order
        self.halves = (slice(0, split), slice(split, rows))
        held, self.from_core, self.from_one, self.from_two, self.from_z = scratch[:5]
        self.local, self.sends, self.recvs = scratch[5:]
        self.pieces, self.held = pieces, held
        self.mine = held.at[self.ids[3]] if pieces is None else held.at[0]

    @staticmethod
    def scratch(rows, width, sides):
        return [
            pltpu.VMEM((sides, 4, 2, 2, rows, width), BF16),
            pltpu.VMEM((4, 2, 2, rows, width), BF16),
            pltpu.VMEM((4, 2, rows, width), BF16),
            pltpu.VMEM((4, rows, width), BF16),
            pltpu.VMEM((3, rows, width), BF16),
            pltpu.SemaphoreType.DMA((4,)),
            pltpu.SemaphoreType.DMA((6, 4)),
            pltpu.SemaphoreType.DMA((6, 4)),
        ]

    def partners(self):
        z, y, x, core = self.ids
        dp, seq = z * 2 + y, x * 2 + core
        near = [(dp, x * 2 + 1 - core), (dp, (1 - x) * 2 + core), (z * 2 + 1 - y, seq)]
        return near + [(lax.rem(z + step, 4) * 2 + y, seq) for step in (1, 2, 3)]

    def target(self, chunk):
        return self.order(chunk) if self.order else lax.rem(self.ids[0] + 1 + chunk, 4)

    def remote(self, source, dest, kind, send_at, recv_at, device):
        return pltpu.make_async_remote_copy(
            src_ref=source,
            dst_ref=dest,
            send_sem=self.sends.at[kind, send_at],
            recv_sem=self.recvs.at[kind, recv_at],
            device_id=device,
            device_id_type=pl.DeviceIdType.MESH,
        )

    def own_copy(self, chunk):
        core, to = self.ids[3], self.target(chunk)
        return pltpu.make_async_copy(
            self.pieces.at[core, to], self.mine.at[to], self.local.at[chunk]
        )

    def core_copy(self, chunk):
        core, to = self.ids[3], self.target(chunk)
        source = (self.held if self.pieces is None else self.pieces).at[1 - core, to]
        return self.remote(source, self.from_core.at[to], 0, chunk, chunk, self.partners()[0])

    def first_copies(self, chunk):
        z, y, x, core = self.ids
        to = self.target(chunk)
        one, two = self.halves
        near = self.partners()
        return (
            self.remote(
                self.mine.at[to, :, 1 - x, one],
                self.from_one.at[to, :, one],
                1,
                chunk,
                chunk,
                near[1],
            ),
            self.remote(
                self.mine.at[to, 1 - y, :, two],
                self.from_one.at[to, :, two],
                2,
                chunk,
                chunk,
                near[2],
            ),
        )

    def second_copies(self, chunk):
        z, y, x, core = self.ids
        to = self.target(chunk)
        one, two = self.halves
        near = self.partners()
        return (
            self.remote(
                self.mine.at[to, 1 - y, x, one],
                self.from_two.at[to, one],
                3,
                chunk,
                chunk,
                near[2],
            ),
            self.remote(
                self.mine.at[to, y, 1 - x, two],
                self.from_two.at[to, two],
                4,
                chunk,
                chunk,
                near[1],
            ),
        )

    def last_copy(self, chunk):
        z, y, x, core = self.ids
        to = self.target(chunk)
        slot = lax.rem(z - to + 4, 4) - 1
        return self.remote(
            self.mine.at[to, y, x],
            self.from_z.at[slot],
            5,
            chunk,
            slot,
            (to * 2 + y, x * 2 + core),
        )

    def arrival(self, slot):
        z, y, x, core = self.ids
        return self.remote(
            self.mine.at[z, y, x], self.from_z.at[slot], 5, slot, slot, self.partners()[3]
        )

    def leaves(self, chunk):
        return self.target(chunk) != self.ids[0]

    def fill(self, to, at, value):
        self.held[at % 2, to, at // 4, at // 2 % 2] = value.astype(BF16)

    def start(self, chunk):
        self.core_copy(chunk).start()
        if self.pieces is not None:
            self.own_copy(chunk).start()

    def add_core(self, chunk):
        to = self.target(chunk)
        if self.pieces is not None:
            self.own_copy(chunk).wait()
        self.core_copy(chunk).wait_recv()

        def add(index, carry):
            at = (to, lax.div(index, 2), lax.rem(index, 2))
            self.mine[at] = self.mine[at] + self.from_core[at]
            return carry

        lax.fori_loop(0, 4, add, 0)
        for copy in self.first_copies(chunk):
            copy.start()

    def add_first(self, chunk):
        z, y, x, core = self.ids
        one, two = self.halves
        to = self.target(chunk)
        for copy in self.first_copies(chunk):
            copy.wait_recv()

        def add(index, carry):
            for at, rows in (((to, index, x), one), ((to, y, index), two)):
                self.mine[at + (rows,)] = self.mine[at + (rows,)] + self.from_one[to, index, rows]
            return carry

        lax.fori_loop(0, 2, add, 0)
        for copy in self.second_copies(chunk):
            copy.start()

    def add_second(self, chunk):
        z, y, x, core = self.ids
        to = self.target(chunk)
        for copy in self.second_copies(chunk):
            copy.wait_recv()

        @pl.when(self.leaves(chunk))
        def _():
            self.mine[to, y, x] = self.mine[to, y, x] + self.from_two[to]
            self.last_copy(chunk).start()

    def finish(self, out):
        z, y, x, core = self.ids
        total = self.mine[z, y, x].astype(F32) + self.from_two[z].astype(F32)
        for slot in range(3):
            self.arrival(slot).wait_recv()
            total += self.from_z[slot].astype(F32)
        out[...] = total
        for chunk in range(4):
            self.core_copy(chunk).wait_send()
            for copy in self.first_copies(chunk) + self.second_copies(chunk):
                copy.wait_send()

            @pl.when(self.leaves(chunk))
            def _(chunk=chunk):
                self.last_copy(chunk).wait_send()


def mesh_ids():
    dp, seq = lax.axis_index("dp"), lax.axis_index("seq")
    return lax.div(dp, 2), lax.rem(dp, 2), lax.div(seq, 2), lax.rem(seq, 2)


def meet(devices):
    barrier = pltpu.get_barrier_semaphore()
    for device in devices:
        pl.semaphore_signal(barrier, inc=1, device_id=device, device_id_type=pl.DeviceIdType.MESH)
    pl.semaphore_wait(barrier, len(devices))


EARLY_PLAN = (
    (2, "add_core", 0),
    (3, "add_core", 1),
    (4, "add_core", 2),
    (5, "add_core", 3),
    (7, "add_first", 0),
    (8, "add_first", 1),
    (9, "add_second", 0),
    (9, "add_first", 2),
    (10, "add_second", 1),
    (10, "add_first", 3),
    (11, "add_second", 2),
    (12, "add_second", 3),
)


def late_kernel(
    sizes,
    planned,
    long_ref,
    glob_ref,
    dq_ref,
    dk_ref,
    dv_ref,
    dmid_ref,
    wq_ref,
    wk_ref,
    wv_ref,
    gain_ref,
    shift_ref,
    table_ref,
    long_out,
    glob_out,
    *rest,
):
    block, count, quarter, seq_count, pairs = sizes
    rows = block + quarter
    width = long_ref.shape[1]
    if planned:
        late_ref, total_ref, *rest = rest
    else:
        gq_ref, gk_ref, gv_ref, total_ref, *rest = rest
    normed_t, every, gather_sends, gather_recvs, *rest = rest
    seq_index = lax.axis_index("seq")
    own_rows = pl.ds(pl.multiple_of(seq_index * quarter, quarter), quarter)
    others = [seq_device(step, seq_count) for step in range(1, seq_count)]

    def gathers():
        for step, device in enumerate(others):
            yield pltpu.make_async_remote_copy(
                src_ref=every.at[own_rows],
                dst_ref=every.at[own_rows],
                send_sem=gather_sends.at[step],
                recv_sem=gather_recvs.at[step],
                device_id=device,
                device_id_type=pl.DeviceIdType.MESH,
            )

    if planned:
        kept, arrived, table_sends, table_recvs, *rest = rest
        reducer = Reducer(rest[0].shape[-2], 32, rest)
        z, y, x, core = mesh_ids()
        partners = reducer.partners()[:3] + [
            ((z + 1 - 2 * lax.rem(z, 2)) * 2 + y, lax.axis_index("seq")),
            (lax.rem(z + 2, 4) * 2 + y, lax.axis_index("seq")),
        ]

        def table_copy(stage):
            return pltpu.make_async_remote_copy(
                src_ref=kept.at[stage],
                dst_ref=arrived.at[stage],
                send_sem=table_sends.at[stage],
                recv_sem=table_recvs.at[stage],
                device_id=partners[stage],
                device_id_type=pl.DeviceIdType.MESH,
            )

        def table_step(stage):
            table_copy(stage).wait_recv()
            kept[stage + 1] = kept[stage] + arrived[stage]
            if stage < 4:
                table_copy(stage + 1).start()

    meet(others + (reducer.partners()[2:] if planned else []))
    everything = jnp.concatenate([long_ref[...], glob_ref[own_rows]], 0).astype(F32)
    hat, inverse = row_norm(everything)
    normed_t[...] = (hat * gain_ref[...] + shift_ref[...]).astype(BF16).T
    if planned:
        piece = width // 32
        blank = jnp.zeros((8, width), F32)
        def weight_rows(chunk):
            to = reducer.target(chunk)
            some = normed_t[pl.ds(pl.multiple_of(to * 8 * piece, 64), 8 * piece)]
            parts = [dot_n(some, ref[...]) for ref in (dq_ref, dk_ref, dv_ref)]
            for at in range(8):
                rows_at = slice(at * piece, (at + 1) * piece)
                reducer.fill(
                    to, at, jnp.concatenate([part[rows_at] for part in parts] + [blank], 0)
                )
            reducer.start(chunk)

        weight_rows(0)
        weight_rows(1)
        reducer.add_core(0)
        weight_rows(2)
        reducer.add_core(1)
        weight_rows(3)
        grads = dot_t(dq_ref[...], wq_ref[...])
        reducer.add_first(0)
        reducer.add_core(2)
        grads += dot_t(dk_ref[...], wk_ref[...]) + dot_t(dv_ref[...], wv_ref[...])
        reducer.add_first(1)
        reducer.add_core(3)
        reducer.add_second(0)
    else:
        for ref, out in ((dq_ref, gq_ref), (dk_ref, gk_ref), (dv_ref, gv_ref)):
            out[...] = dot_n(normed_t[...], ref[...]).astype(BF16)
        grads = (
            dot_t(dq_ref[...], wq_ref[...])
            + dot_t(dk_ref[...], wk_ref[...])
            + dot_t(dv_ref[...], wv_ref[...])
        )
    scaled = grads * gain_ref[...]
    total = dmid_ref[...] + inverse * (
        scaled
        - jnp.mean(scaled, -1, keepdims=True)
        - hat * jnp.mean(scaled * hat, -1, keepdims=True)
    )
    every[own_rows] = total[block:].astype(BF16)
    for copy in gathers():
        copy.start()
    long_out[...] = total[:block]
    sums = [
        column_sum(part)
        for part in (dq_ref[...].astype(F32), dv_ref[...].astype(F32), grads * hat, grads)
    ]
    heads = 2 * pairs
    first = kept.at[0] if planned else total_ref
    first[...] = jnp.zeros(first.shape, F32)
    for pair in range(pairs):
        first[2 * pair : 2 * pair + 2, :WINDOW] = table_ref[pair]
    for at, vector in enumerate(sums):
        first[heads + at : heads + at + 1] = vector
    if planned:
        table_copy(0).start()
        for number, (act, chunk) in enumerate(LATE_TAIL):
            getattr(reducer, act)(chunk)
            table_step(number)
        total_ref[...] = kept[5]
        reducer.finish(late_ref)
        for stage in range(5):
            table_copy(stage).wait_send()
    for copy in gathers():
        copy.wait_recv()
    glob_out[...] = every[:count].astype(F32)
    for copy in gathers():
        copy.wait_send()


LATE_TAIL = (
    ("add_first", 2),
    ("add_second", 1),
    ("add_first", 3),
    ("add_second", 2),
    ("add_second", 3),
)


def last_part(sizes, planned, long_x, glob_x, dq, dk, dv, dmid, wq, wk, wv, gain, shift, table):
    block, count, quarter, seq_count, pairs = sizes
    rows, width = dq.shape
    others = seq_count - 1
    whole = pl.BlockSpec(memory_space=pltpu.VMEM)
    shape = jax.ShapeDtypeStruct
    sums = shape(((2 * pairs + 4 + 7) // 8 * 8, width), F32)
    outs = [shape((block, width), F32), shape((count, width), F32)]
    scratch = [
        pltpu.VMEM((width, rows), BF16),
        pltpu.VMEM((GP, width), BF16),
        pltpu.SemaphoreType.DMA((others,)),
        pltpu.SemaphoreType.DMA((others,)),
    ]
    if planned:
        piece = width // 32
        part = 3 * piece + 8
        outs += [shape((part, width), F32), sums]
        scratch += [
            pltpu.VMEM((6,) + sums.shape, F32),
            pltpu.VMEM((5,) + sums.shape, F32),
            pltpu.SemaphoreType.DMA((5,)),
            pltpu.SemaphoreType.DMA((5,)),
        ] + Reducer.scratch(part, width, 2)
    else:
        outs += [shape((width, width), BF16)] * 3 + [sums]
    return pl.pallas_call(
        functools.partial(late_kernel, sizes, planned),
        in_specs=[whole] * 12,
        out_specs=[whole] * len(outs),
        out_shape=outs,
        scratch_shapes=scratch,
        compiler_params=pltpu.CompilerParams(
            collective_id=2, has_side_effects=True, vmem_limit_bytes=60 * 2**20
        ),
        name="last_part",
    )(long_x, glob_x, dq, dk, dv, dmid, wq, wk, wv, gain, shift, table)


def small_kernel(heads, early_ref, late_ref, outer_ref, inner_ref, sums_ref, *outs):
    g_query, g_key, g_value, g_out, g_inner, g_outer, *vectors, table = outs
    device = lax.axis_index("dp") * lax.axis_size("seq") + lax.axis_index("seq")
    piece, width = g_query.shape
    for at, out in enumerate((g_query, g_key, g_value)):
        out[...] = late_ref[at * piece : (at + 1) * piece]
    g_out[...] = early_ref[2 * piece : 3 * piece]
    g_outer[...] = outer_ref[...]
    for source, first, chunk in (
        (inner_ref, 0, 0),
        (inner_ref, piece, 3),
        (early_ref, 0, 1),
        (early_ref, piece, 2),
    ):
        g_inner[:, chunk * width : (chunk + 1) * width] = source[first : first + piece]

    def entries(row, at, length):
        return pltpu.roll(row, width - at * length, 1)[0, :length]

    b_query, b_value, b_out, b_outer, gain_one, shift_one, gain_two, shift_two, b_inner = vectors
    for at, out in enumerate((b_query, b_value, gain_one, shift_one)):
        out[...] = entries(sums_ref[heads + at : heads + at + 1], device, piece)
    for at, out in enumerate((b_out, b_outer, gain_two, shift_two)):
        row = 3 * piece + at
        out[...] = entries(early_ref[row : row + 1], device, piece)
    row = pl.ds(3 * piece + 4 + lax.div(device, 8), 1)
    b_inner[...] = entries(early_ref[row], lax.rem(device, 8), 4 * piece)
    labels = table.shape[0]
    turned = pltpu.roll(sums_ref[:, :WINDOW], WINDOW - HALO + R, 1).T
    table[...] = turned[:labels, :heads]


def small_results(heads, early, late, outer, inner, sums):
    width = early.shape[1]
    piece = width // 32
    shape = jax.ShapeDtypeStruct
    whole = pl.BlockSpec(memory_space=pltpu.VMEM)
    outs = [shape((piece, width), F32)] * 4
    outs += [shape((piece, 4 * width), F32), shape((4 * piece, width), F32)]
    outs += [shape((piece,), F32)] * 8 + [shape((4 * piece,), F32)]
    outs += [shape((2 * R + 1, heads), F32)]
    return pl.pallas_call(
        functools.partial(small_kernel, heads),
        in_specs=[whole] * 5,
        out_specs=[whole] * len(outs),
        out_shape=outs,
        name="small_results",
    )(early, late, outer, inner, sums)


def has_plan():
    return (lax.axis_size("dp"), lax.axis_size("seq")) == (8, 4)


GELU_A = 0.7978845608028654
GELU_B = 0.044715


def gate_both(u):
    square = u * u
    turned = jnp.tanh(GELU_A * u * (1.0 + GELU_B * square))
    half = 0.5 * (1.0 + turned)
    slope = half + 0.5 * u * (1.0 - turned * turned) * (
        GELU_A * (1.0 + 3.0 * GELU_B * square)
    )
    return u * half, slope


def column_sum(rows):
    return jnp.sum(rows, 0, keepdims=True)


def ffn_kernel(
    sizes,
    planned,
    len_ref,
    attn_ref,
    long_ref,
    glob_ref,
    dlong_ref,
    dglob_ref,
    lq_ref,
    wo_ref,
    bo_ref,
    gain_ref,
    shift_ref,
    wi_ref,
    bi_ref,
    wr_ref,
    br_ref,
    long_out,
    glob_out,
    dmid_ref,
    do_ref,
    dog_ref,
    ldg_ref,
    *rest,
):
    block, count, quarter, seq_count, pairs = sizes
    if planned:
        pieces_ref, outer_ref, inner_ref, *rest = rest
    else:
        g_outer_ref, g_inner_ref, g_out_ref, vec_ref, *rest = rest
    (
        mid,
        y_sum,
        df_sum,
        normed,
        normed_t,
        dy,
        vectors,
        biases,
        every_do,
        every_ld,
        every_out,
        gather_sends,
        gather_recvs,
        *rest,
    ) = rest
    if planned:
        even, *rest = rest
        outer = Reducer(rest[0].shape[-2], 48, rest[:8], order=chunk_of)
        inner = Reducer(rest[8].shape[-2], 16, rest[8:])
    step = pl.program_id(0)
    chunk = chunk_of(step)
    seq_index = lax.axis_index("seq")
    own_rows = pl.ds(pl.multiple_of(seq_index * quarter, quarter), quarter)
    width = mid.shape[1]
    piece = width // 32

    def gathers(kinds):
        for seq_step in range(1, seq_count):
            for kind in kinds:
                every = (every_do, every_ld, every_out)[kind]
                yield pltpu.make_async_remote_copy(
                    src_ref=every.at[own_rows],
                    dst_ref=every.at[own_rows],
                    send_sem=gather_sends.at[kind, seq_step - 1],
                    recv_sem=gather_recvs.at[kind, seq_step - 1],
                    device_id=seq_device(seq_step, seq_count),
                    device_id_type=pl.DeviceIdType.MESH,
                )

    def act(now):
        if planned:
            for at, reducer, name, part in FFN_PLAN:
                if at == now:
                    getattr((outer, inner)[reducer], name)(part)

    def act_in_step(point):
        if planned:
            for now in range(4):
                if any(at == (now, point) for at, _, _, _ in FFN_PLAN):

                    @pl.when(step == now)
                    def _(now=now):
                        act((now, point))

    @pl.when(step == 0)
    def _():
        others = [seq_device(seq_step, seq_count) for seq_step in range(1, seq_count)]
        meet(others + (outer.partners()[2:] if planned else []))
        projected = dot_n(attn_ref[...], wo_ref[...]) + bo_ref[...]
        mid[:block] = long_ref[...].astype(F32) + projected[:block]
        mid[block:] = glob_ref[own_rows].astype(F32) + projected[block:]
        hat, _ = row_norm(mid[...])
        normed[...] = (hat * gain_ref[...] + shift_ref[...]).astype(BF16)
        normed_t[...] = normed[...].T
        position = seq_index * block + lax.broadcasted_iota(jnp.int32, (block, 1), 0)
        dy[:block] = jnp.where(
            position < len_ref[0], dlong_ref[...].astype(F32), 0.0
        ).astype(BF16)
        y_sum[:GP] = jnp.zeros((GP, width), F32)
        y_sum[:count] = dglob_ref[...].astype(F32)
        dy[block:] = y_sum[own_rows].astype(BF16)
        vectors[1:2] = column_sum(dy[...].astype(F32))
        y_sum[...] = mid[...] + br_ref[...]
        df_sum[...] = jnp.zeros_like(df_sum)
        for at in range(4):
            biases[at] = bi_ref[at * width : (at + 1) * width].reshape(1, width)

    act_in_step(0)
    active, slope = gate_both(dot_n(normed[...], wi_ref[...]) + biases[chunk])
    active = active.astype(BF16)
    g_outer = t_dot(active, dy[...])
    if planned:
        for at in range(8):
            outer.fill(chunk, at, g_outer[at * 4 * piece : (at + 1) * 4 * piece])
        outer.start(step)
    else:
        g_outer_ref[...] = g_outer.astype(BF16)
    y_sum[...] += dot_n(active, wr_ref[...])
    hidden = dot_t(dy[...], wr_ref[...]) * slope
    for at in range(4):

        @pl.when(chunk == at)
        def _(at=at):
            vectors[4 + at : 5 + at] = column_sum(hidden)

    hidden = hidden.astype(BF16)
    act_in_step(1)
    df_sum[...] += dot_t(hidden, wi_ref[...])
    g_inner = dot_n(normed_t[...], hidden)
    if planned:

        @pl.when(lax.rem(step, 2) == 0)
        def _():
            even[...] = g_inner

        def halves(at):
            part = slice(at * piece, (at + 1) * piece)
            return jnp.concatenate([even[part], g_inner[part]], 0)

        @pl.when(step == 1)
        def _():
            for at in range(32):
                inner.fill(at // 8, at % 8, halves(at))
            for part in range(4):
                inner.start(part)

        @pl.when(step == 3)
        def _():
            for at in range(32):
                pieces_ref[at % 2, at // 8, at // 4 % 2, at // 2 % 2, : 2 * piece] = halves(
                    at
                ).astype(BF16)

    else:
        g_inner_ref[...] = g_inner.astype(BF16)

    def norm_back(rows):
        hat, inverse = row_norm(mid[rows])
        df = df_sum[rows]
        scaled = df * gain_ref[...]
        dmid = dy[rows].astype(F32) + inverse * (
            scaled
            - jnp.mean(scaled, -1, keepdims=True)
            - hat * jnp.mean(scaled * hat, -1, keepdims=True)
        )
        dmid_ref[rows] = dmid
        low = dmid.astype(BF16)
        grad_o = dot_t(low, wo_ref[...]).astype(BF16)
        do_ref[rows] = grad_o
        return [column_sum(dmid), column_sum(df * hat), column_sum(df)], low, grad_o

    @pl.when(step == 3)
    def _():
        glob_sums, glob_low, grad_o = norm_back(slice(block, block + quarter))
        every_do[own_rows] = grad_o
        both = grad_o.astype(F32) * attn_ref[block:].astype(F32)
        stats = lq_ref[...]
        for head in range(2 * pairs):
            lanes = slice(head // 2 * PAIR, head // 2 * PAIR + PAIR)
            delta = jnp.sum(own_half(head % 2, both[:, lanes]), -1, keepdims=True)
            stats = jnp.where(lane_index() == HD + head, delta, stats)
        every_ld[own_rows] = stats
        every_out[own_rows] = y_sum[block:].astype(BF16)
        for copy in gathers((0, 1, 2)):
            copy.start()
        act((4, 0))
        position = seq_index * block + lax.broadcasted_iota(jnp.int32, (block, 1), 0)
        long_out[...] = jnp.where(position < len_ref[0], y_sum[:block], 0.0).astype(BF16)
        long_sums, long_low, _ = norm_back(slice(0, block))
        for at, one, two in zip((0, 2, 3), long_sums, glob_sums):
            vectors[at : at + 1] = one + two
        act((4, 1))
        g_out = t_dot(attn_ref[...], jnp.concatenate([long_low, glob_low], 0))
        if planned:
            for at in range(32):
                pieces_ref[at % 2, at // 8, at // 4 % 2, at // 2 % 2, 2 * piece :] = (
                    jnp.concatenate(
                        [g_out[at * piece : (at + 1) * piece], vectors[...]], 0
                    ).astype(BF16)
                )
            act((4, 2))
            outer.finish(outer_ref)
            inner.finish(inner_ref)
        else:
            g_out_ref[...] = g_out.astype(BF16)
            vec_ref[...] = vectors[...]
        for copy in gathers((0, 1, 2)):
            copy.wait_recv()
        dog_ref[...] = every_do[...]
        ldg_ref[...] = every_ld[...]
        glob_out[...] = every_out[:count]
        for copy in gathers((0, 1, 2)):
            copy.wait_send()


OUTER, INNER = 0, 1
FFN_PLAN = (
    ((1, 0), OUTER, "add_core", 0),
    ((2, 0), OUTER, "add_first", 0),
    ((2, 0), OUTER, "add_core", 1),
    ((2, 1), OUTER, "add_second", 0),
    ((2, 1), INNER, "add_core", 0),
    ((2, 1), INNER, "add_core", 1),
    ((2, 1), INNER, "add_core", 2),
    ((2, 1), INNER, "add_core", 3),
    ((3, 0), OUTER, "add_first", 1),
    ((3, 0), OUTER, "add_core", 2),
    ((3, 1), OUTER, "add_second", 1),
    ((3, 1), INNER, "add_first", 0),
    ((3, 1), INNER, "add_first", 1),
    ((4, 0), OUTER, "add_core", 3),
    ((4, 0), OUTER, "add_first", 2),
    ((4, 0), INNER, "add_second", 0),
    ((4, 0), INNER, "add_first", 2),
    ((4, 0), INNER, "add_second", 1),
    ((4, 0), INNER, "add_first", 3),
    ((4, 1), OUTER, "add_second", 2),
    ((4, 1), OUTER, "add_first", 3),
    ((4, 1), INNER, "add_second", 2),
    ((4, 2), OUTER, "add_second", 3),
    ((4, 2), INNER, "add_second", 3),
)


def chunk_of(step):
    return jnp.where(step == 0, 0, jnp.where(step == 1, 3, step - 1))


def feed_forward(sizes, planned, doc_len, attn, long_x, glob_x, dlong, dglob, lq, *weights):
    block, count, quarter, seq_count, pairs = sizes
    wo, bo, gain, shift, wi, bi, wr, br = weights
    width, hidden = wi.shape
    chunk = hidden // 4
    rows = block + quarter
    whole = pl.BlockSpec(memory_space=pltpu.VMEM)
    shape = jax.ShapeDtypeStruct
    in_specs = [pl.BlockSpec(memory_space=pltpu.SMEM)] + [whole] * 10
    in_specs += [
        pl.BlockSpec((width, chunk), lambda c: (0, chunk_of(c))),
        whole,
        pl.BlockSpec((chunk, width), lambda c: (chunk_of(c), 0)),
        whole,
    ]
    outs = [
        shape((block, width), BF16),
        shape((count, width), BF16),
        shape((rows, width), F32),
        shape((rows, width), BF16),
        shape((GP, width), BF16),
        shape((GP, PAIR), F32),
    ]
    out_specs = [whole] * 6
    others = seq_count - 1
    scratch = [
        pltpu.VMEM((rows, width), F32),
        pltpu.VMEM((rows, width), F32),
        pltpu.VMEM((rows, width), F32),
        pltpu.VMEM((rows, width), BF16),
        pltpu.VMEM((width, rows), BF16),
        pltpu.VMEM((rows, width), BF16),
        pltpu.VMEM((8, width), F32),
        pltpu.VMEM((4, 1, chunk), F32),
        pltpu.VMEM((GP, width), BF16),
        pltpu.VMEM((GP, PAIR), F32),
        pltpu.VMEM((GP, width), BF16),
        pltpu.SemaphoreType.DMA((3, others)),
        pltpu.SemaphoreType.DMA((3, others)),
    ]
    if planned:
        part, piece = hidden // 32, width // 32
        outs += [
            shape((2, 4, 2, 2, 3 * piece + 8, width), BF16),
            shape((part, width), F32),
            shape((2 * piece, width), F32),
        ]
        out_specs += [whole] * 3
        scratch += [
            pltpu.VMEM((width, chunk), F32),
        ]
        scratch += Reducer.scratch(part, width, 2) + Reducer.scratch(2 * piece, width, 2)
    else:
        outs += [
            shape((hidden, width), BF16),
            shape((width, hidden), BF16),
            shape((width, width), BF16),
            shape((8, width), F32),
        ]
        out_specs += [
            pl.BlockSpec((chunk, width), lambda c: (chunk_of(c), 0)),
            pl.BlockSpec((width, chunk), lambda c: (0, chunk_of(c))),
            whole,
            whole,
        ]
    return pl.pallas_call(
        functools.partial(ffn_kernel, sizes, planned),
        grid=(4,),
        in_specs=in_specs,
        out_specs=out_specs,
        out_shape=outs,
        scratch_shapes=scratch,
        compiler_params=pltpu.CompilerParams(
            collective_id=4, has_side_effects=True, vmem_limit_bytes=62 * 2**20
        ),
        name="feed_forward",
    )(doc_len, attn, long_x, glob_x, dlong, dglob, lq, wo, bo, gain, shift, wi, bi, wr, br)


def back_kernel(
    sizes,
    early_rows,
    len_ref,
    tab_ref,
    q_ref,
    kx_ref,
    vx_ref,
    kg_ref,
    vg_ref,
    o_ref,
    do_ref,
    l_ref,
    dog_ref,
    ldg_ref,
    *rest,
):
    block, count, quarter, seq_count, pairs = sizes
    reduces = early_rows > 0
    if reduces:
        pieces_ref, rest = rest[0], rest[1:]
    dq_ref, dk_ref, dv_ref, dtab_ref, *rest = rest
    if reduces:
        early_ref, rest = rest[0], rest[1:]
    (
        dkx,
        dvx,
        dkg,
        dvg,
        q_send,
        q_recv,
        kv_send,
        kv_recv,
        halo_send,
        halo_recv,
        glob_sends,
        glob_recvs,
        halo_sends,
        halo_recvs,
        *rest,
    ) = rest
    number = pl.program_id(0)
    pair = lax.rem(number, pairs)
    seq_index = lax.axis_index("seq")
    reducer = Reducer(early_rows, 16, rest, pieces=pieces_ref) if reduces else None
    scale = HD ** (-0.5)
    low_lanes = lane_index() < HD
    own_keys = slice(HALO, HALO + block)
    own_rows = pl.ds(pl.multiple_of(seq_index * quarter, quarter), quarter)

    def glob_copies(kind, at):
        source, dest = ((q_send, q_recv), (kv_send, kv_recv))[kind]
        for step in range(1, seq_count):
            device = seq_device(step, seq_count)
            yield pltpu.make_async_remote_copy(
                src_ref=source.at[device[1], at],
                dst_ref=dest.at[step - 1, at],
                send_sem=glob_sends.at[kind, step - 1, at],
                recv_sem=glob_recvs.at[kind, step - 1, at],
                device_id=device,
                device_id_type=pl.DeviceIdType.MESH,
            )

    def halo_copy(direction, at):
        return pltpu.make_async_remote_copy(
            src_ref=halo_send.at[direction, at],
            dst_ref=halo_recv.at[direction, at],
            send_sem=halo_sends.at[direction, at],
            recv_sem=halo_recvs.at[direction, at],
            device_id=seq_device(2 * direction - 1, seq_count),
            device_id_type=pl.DeviceIdType.MESH,
        )

    has_low, has_high = seq_index > 0, seq_index < seq_count - 1
    sends_to = (has_low, has_high)
    gets_from = (has_high, has_low)

    def close_pair(at):
        lanes = lanes_of(at)
        for direction in range(2):

            @pl.when(gets_from[direction])
            def _(direction=direction):
                halo_copy(direction, at).wait_recv()

        for kind, (total, out) in enumerate(((dkx, dk_ref), (dvx, dv_ref))):
            first, last = HALO + REACH, HALO + block - REACH
            out[:REACH, lanes] = (
                total[at, HALO:first] + halo_recv[1, at, kind].astype(F32)
            ).astype(BF16)
            out[REACH : block - REACH, lanes] = total[at, first:last].astype(BF16)
            out[block - REACH : block, lanes] = (
                total[at, last : HALO + block] + halo_recv[0, at, kind].astype(F32)
            ).astype(BF16)
        sums = []
        for kind, (source, dest) in enumerate(((q_send, q_recv), (kv_send, kv_recv))):
            total = source[seq_index, at].astype(F32)
            for step, copy in enumerate(glob_copies(kind, at)):
                copy.wait_recv()
                total += dest[step, at].astype(F32)
            sums.append(total.astype(BF16))
        dq_ref[block:, lanes] = sums[0]
        dk_ref[block:, lanes] = sums[1][:, :PAIR]
        dv_ref[block:, lanes] = sums[1][:, PAIR:]

    def run_plan(now):
        for at, act, chunk in EARLY_PLAN:
            if now == at:
                getattr(reducer, act)(chunk)

    @pl.when(number == 0)
    def _():
        others = [seq_device(step, seq_count) for step in range(1, seq_count)]
        meet(others + (reducer.partners()[2:] if reduces else []))
        if reduces:
            for chunk in range(4):
                reducer.start(chunk)
        for direction in range(2):

            @pl.when(jnp.logical_not(gets_from[direction]))
            def _(direction=direction):
                halo_recv[direction] = jnp.zeros_like(halo_recv[direction])

    if reduces:
        for now in range(1, 2 * pairs):
            if any(at == now for at, _, _ in EARLY_PLAN):

                @pl.when(number == now)
                def _(now=now):
                    run_plan(now)

    @pl.when(number < pairs)
    def _():
        long_bias = key_bias(seq_index * block, block, len_ref[0])
        near_bias = key_bias(seq_index * quarter, quarter, count)
        query = q_ref[block:] * jnp.asarray(scale, BF16)
        grad_o = dog_ref[...]
        far_k, far_v = kx_ref[own_keys], vx_ref[own_keys]
        near_k, near_v = kg_ref[own_rows], vg_ref[own_rows]
        outs, kept = [], []
        for head in range(2):
            norm = in_three(-pick_column(ldg_ref[...], 2 * pair + head))
            delta = in_three(-pick_column(ldg_ref[...], HD + 2 * pair + head))
            qa = with_lanes(head, query, (1.0,) + norm)
            doa = with_lanes(head, grad_o, delta)
            far = jnp.exp(dot_t(qa, key_side(head, far_k, long_bias)))
            near = jnp.exp(dot_t(qa, key_side(head, near_k, near_bias)))
            far_ds = (far * dot_t(doa, value_side(head, far_v))).astype(BF16)
            near_ds = (near * dot_t(doa, value_side(head, near_v))).astype(BF16)
            outs.append(dot_n(far_ds, far_k) + dot_n(near_ds, near_k))
            kept.append(
                (
                    own_half(head, query),
                    own_half(head, grad_o),
                    far.astype(BF16),
                    near.astype(BF16),
                    far_ds,
                    near_ds,
                )
            )
        own_q, own_do, far, near, far_ds, near_ds = (
            jnp.concatenate(part, 0) for part in zip(*kept)
        )
        for total, edge in ((dkx, own_keys), (dvx, own_keys)):
            total[pair, :HALO] = jnp.zeros((HALO, PAIR), F32)
            total[pair, HALO + block :] = jnp.zeros((HALO, PAIR), F32)
        dkx[pair, own_keys] = t_dot(far_ds, own_q)
        dvx[pair, own_keys] = t_dot(far, own_do)
        dkg[pair] = jnp.zeros((GP, PAIR), F32)
        dvg[pair] = jnp.zeros((GP, PAIR), F32)
        dkg[pair, own_rows] = t_dot(near_ds, own_q)
        dvg[pair, own_rows] = t_dot(near, own_do)
        glob_dq = (jnp.where(low_lanes, outs[0], outs[1]) * scale).astype(BF16)
        q_send[:, pair] = glob_dq.reshape(seq_count, quarter, PAIR)
        for copy in glob_copies(0, pair):
            copy.start()

    @pl.when(number >= pairs)
    def _():
        long_bias = key_bias(seq_index * block - HALO, block + 2 * HALO, len_ref[0])
        glob_bias = key_bias(0, GP, count)
        query = q_ref[:block] * jnp.asarray(scale, BF16)
        grad_o = do_ref[...]
        both = grad_o.astype(F32) * o_ref[...].astype(F32)
        heads = []
        for head in range(2):
            norm = in_three(-pick_column(l_ref[...], 2 * pair + head))
            delta = in_three(-jnp.sum(own_half(head, both), -1, keepdims=True))
            heads.append(
                dict(
                    q=own_half(head, query),
                    do=own_half(head, grad_o),
                    qa=with_lanes(head, query, (1.0,) + norm),
                    doa=with_lanes(head, grad_o, delta),
                    kxa=key_side(head, kx_ref[...], long_bias),
                    vxa=value_side(head, vx_ref[...]),
                    kga=key_side(head, kg_ref[...], glob_bias),
                    vga=value_side(head, vg_ref[...]),
                    bias=band_bias(tab_ref[0, head : head + 1]),
                )
            )
        table_sums = [0.0, 0.0]
        grads_q = []
        for start in range(0, block, SUB):
            rows, keys = slice(start, start + SUB), slice(start, start + WINDOW)
            outs, probs, grads = [], [], []
            for head, own in enumerate(heads):
                band = jnp.exp(dot_t(own["qa"][rows], own["kxa"][keys]) + own["bias"])
                band_ds = band * dot_t(own["doa"][rows], own["vxa"][keys])
                table_sums[head] += band_ds
                glob = jnp.exp(dot_t(own["qa"][rows], own["kga"]))
                glob_ds = (glob * dot_t(own["doa"][rows], own["vga"])).astype(BF16)
                band_ds = band_ds.astype(BF16)
                outs.append(dot_n(band_ds, kx_ref[keys]) + dot_n(glob_ds, kg_ref[...]))
                probs.append((band.astype(BF16), glob.astype(BF16)))
                grads.append((band_ds, glob_ds))
            grads_q.append(jnp.where(low_lanes, outs[0], outs[1]))
            own_q = jnp.concatenate([own["q"][rows] for own in heads], 0)
            own_do = jnp.concatenate([own["do"][rows] for own in heads], 0)
            band, glob = (jnp.concatenate(part, 0) for part in zip(*probs))
            band_ds, glob_ds = (jnp.concatenate(part, 0) for part in zip(*grads))
            dkx[pair, keys] += t_dot(band_ds, own_q)
            dvx[pair, keys] += t_dot(band, own_do)
            dkg[pair] += t_dot(glob_ds, own_q)
            dvg[pair] += t_dot(glob, own_do)
        for kind, total in enumerate((dkg, dvg)):
            kv_send[:, pair, :, kind * PAIR : (kind + 1) * PAIR] = (
                total[pair].astype(BF16).reshape(seq_count, quarter, PAIR)
            )
        for copy in glob_copies(1, pair):
            copy.start()
        for kind, total in enumerate((dkx, dvx)):
            for direction, first in enumerate((HALO - REACH, HALO + block)):
                halo_send[direction, pair, kind] = total[pair, first : first + REACH].astype(BF16)
        for direction in range(2):

            @pl.when(sends_to[direction])
            def _(direction=direction):
                halo_copy(direction, pair).start()

        dq_ref[:block, lanes_of(pair)] = (jnp.concatenate(grads_q, 0) * scale).astype(BF16)
        for head in range(2):
            dtab_ref[pair, head : head + 1] = diagonal_sums(table_sums[head])

    @pl.when(number > pairs)
    def _():
        close_pair(pair - 1)

    @pl.when(number == 2 * pairs - 1)
    def _():
        if reduces:
            run_plan(2 * pairs)
        close_pair(pairs - 1)
        for at in range(pairs):
            for kind in range(2):
                for copy in glob_copies(kind, at):
                    copy.wait_send()
            for direction in range(2):

                @pl.when(sends_to[direction])
                def _(direction=direction, at=at):
                    halo_copy(direction, at).wait_send()

        if reduces:
            reducer.finish(early_ref)


def attend_back(sizes, doc_len, table, q, kx, vx, kg, vg, o, do, l, dog, ldg, pieces=None):
    block, count, quarter, seq_count, pairs = sizes
    width = q.shape[1]
    early_rows = 0 if pieces is None else pieces.shape[-2]
    ext = block + 2 * HALO
    cols = lambda rows: pl.BlockSpec((rows, PAIR), lambda i: (0, lax.rem(i, pairs)))
    whole = pl.BlockSpec(memory_space=pltpu.VMEM)
    shape = jax.ShapeDtypeStruct
    in_specs = [
        pl.BlockSpec(memory_space=pltpu.SMEM),
        pl.BlockSpec((1, 2, WINDOW), lambda i: (lax.rem(i, pairs), 0, 0)),
        cols(block + GP),
        cols(ext),
        cols(ext),
        cols(GP),
        cols(GP),
        cols(block),
        cols(block),
        whole,
        cols(GP),
        whole,
    ]
    rows = block + quarter
    outs = [shape((rows, width), BF16)] * 3 + [shape((pairs, 2, WINDOW), F32)]
    others = seq_count - 1
    scratch = [
        pltpu.VMEM((pairs, ext, PAIR), F32),
        pltpu.VMEM((pairs, ext, PAIR), F32),
        pltpu.VMEM((pairs, GP, PAIR), F32),
        pltpu.VMEM((pairs, GP, PAIR), F32),
        pltpu.VMEM((seq_count, pairs, quarter, PAIR), BF16),
        pltpu.VMEM((others, pairs, quarter, PAIR), BF16),
        pltpu.VMEM((seq_count, pairs, quarter, 2 * PAIR), BF16),
        pltpu.VMEM((others, pairs, quarter, 2 * PAIR), BF16),
        pltpu.VMEM((2, pairs, 2, REACH, PAIR), BF16),
        pltpu.VMEM((2, pairs, 2, REACH, PAIR), BF16),
        pltpu.SemaphoreType.DMA((2, others, pairs)),
        pltpu.SemaphoreType.DMA((2, others, pairs)),
        pltpu.SemaphoreType.DMA((2, pairs)),
        pltpu.SemaphoreType.DMA((2, pairs)),
    ]
    args = [doc_len, table, q, kx, vx, kg, vg, o, do, l, dog, ldg]
    if early_rows:
        in_specs.append(pl.BlockSpec(memory_space=pl.ANY))
        outs.append(shape((early_rows, width), F32))
        scratch += Reducer.scratch(early_rows, width, 1)
        args.append(pieces)
    return pl.pallas_call(
        functools.partial(back_kernel, sizes, early_rows),
        grid=(2 * pairs,),
        in_specs=in_specs,
        out_specs=[whole] * len(outs),
        out_shape=outs,
        scratch_shapes=scratch,
        compiler_params=pltpu.CompilerParams(
            collective_id=1, has_side_effects=True, vmem_limit_bytes=60 * 2**20
        ),
        name="attend_back",
    )(*args)


def on_device(
    long_input,
    global_input,
    lengths,
    w_query,
    b_query,
    w_key,
    w_value,
    b_value,
    w_out,
    b_out,
    w_inner,
    b_inner,
    w_outer,
    b_outer,
    norm1_gain,
    norm1_shift,
    norm2_gain,
    norm2_shift,
    rel_table,
    long_cotangent,
    global_cotangent,
):
    seq_count = lax.axis_size("seq")
    data_count = lax.axis_size("dp")
    seq_index = lax.axis_index("seq")
    block = long_input.shape[1]
    count = global_input.shape[1]
    width = long_input.shape[2]
    heads = rel_table.shape[1]
    pairs = heads // 2
    labels = 2 * R + 1
    quarter = GP // seq_count
    sizes = Sizes(block, count, quarter, seq_count, pairs)
    queries, kx, vx, kg, vg, attn_low, long_l, glob_l, glob_x, table = attend(
        sizes,
        lengths,
        rel_table,
        long_input[0],
        global_input[0],
        w_query,
        w_key,
        w_value,
        b_query,
        b_value,
        norm1_gain,
        norm1_shift,
    )
    planned = has_plan()
    long_result, glob_out, grad_mid, grad_attn, every_do, every_ld, *gradients = feed_forward(
        sizes,
        planned,
        lengths,
        attn_low,
        long_input[0],
        glob_x,
        long_cotangent[0],
        global_cotangent[0],
        glob_l,
        w_out,
        b_out,
        norm2_gain,
        norm2_shift,
        w_inner,
        b_inner,
        w_outer,
        b_outer,
    )
    query_low, key_low, value_low, dtab, *early = attend_back(
        sizes,
        lengths,
        table,
        queries,
        kx,
        vx,
        kg,
        vg,
        attn_low,
        grad_attn,
        long_l,
        every_do,
        every_ld,
        *(gradients[:1] if planned else []),
    )
    long_grad, glob_grad, *late, sums = last_part(
        sizes,
        planned,
        long_input[0],
        glob_x,
        query_low,
        key_low,
        value_low,
        grad_mid,
        w_query,
        w_key,
        w_value,
        norm1_gain,
        norm1_shift,
        dtab,
    )
    if planned:
        (
            g_query,
            g_key,
            g_value,
            g_out,
            g_inner,
            g_outer,
            g_b_query,
            g_b_value,
            g_b_out,
            g_b_outer,
            g_g1,
            g_s1,
            g_g2,
            g_s2,
            g_b_inner,
            table_total,
        ) = small_results(heads, early[0], late[0], gradients[1], gradients[2], sums)
    else:
        devices = data_count * seq_count
        own_part = lambda vector: lax.dynamic_slice_in_dim(
            vector,
            (lax.axis_index("dp") * seq_count + seq_index) * (vector.shape[0] // devices),
            vector.shape[0] // devices,
        )
        g_outer, g_inner, g_out, vectors = gradients
        g_outer, g_inner, g_out, g_query, g_key, g_value = (
            lax.psum_scatter(g.astype(BF16), ("dp", "seq"), scatter_dimension=0, tiled=True).astype(
                F32
            )
            for g in (g_outer, g_inner, g_out, *late)
        )
        vectors, sums = lax.psum((vectors, sums), ("dp", "seq"))
        g_b_query, g_b_value, g_g1, g_s1 = (own_part(sums[heads + i]) for i in range(4))
        g_b_out, g_b_outer, g_g2, g_s2 = (own_part(vectors[i]) for i in range(4))
        g_b_inner = own_part(vectors[4:].reshape(-1))
        table_total = sums[:heads, HALO - R : HALO - R + labels].T
    return (
        long_result[None],
        glob_out[None],
        long_grad[None],
        glob_grad[None],
        g_query,
        g_b_query,
        g_key,
        g_value,
        g_b_value,
        g_out,
        g_b_out,
        g_inner,
        g_b_inner,
        g_outer,
        g_b_outer,
        g_g1,
        g_s1,
        g_g2,
        g_s2,
        table_total,
    )


def solution(mesh):
    rows, whole = P("dp", "seq", None), P("dp", None, None)
    matrix, vector = P(("dp", "seq"), None), P(("dp", "seq"))
    return jax.shard_map(
        on_device,
        mesh=mesh,
        in_specs=(rows, whole, P("dp")) + (P(),) * 16 + (rows, whole),
        out_specs=(
            rows,
            whole,
            rows,
            whole,
            matrix,
            vector,
            matrix,
            matrix,
            vector,
            matrix,
            vector,
            matrix,
            vector,
            matrix,
            vector,
            vector,
            vector,
            vector,
            vector,
            P(),
        ),
        check_vma=False,
    )
```

```python
import functools
from typing import NamedTuple

import jax
import jax.numpy as jnp
from jax import lax
from jax.experimental import pallas as pl
from jax.experimental.pallas import tpu as pltpu
from jax.sharding import PartitionSpec as P

HD = 64
R = 84
PAIR = 2 * HD
HALO = 128
REACH = 96
GP = 256
SUB = 256
WINDOW = SUB + 2 * HALO
EPSILON = 1e-05
MASKED = -1e30
F32 = jnp.float32
BF16 = jnp.bfloat16


def dot_t(left, right):
    return lax.dot_general(left, right, (((1,), (1,)), ((), ())), preferred_element_type=F32)


def dot_n(left, right):
    return lax.dot_general(left, right, (((1,), (0,)), ((), ())), preferred_element_type=F32)


def t_dot(left, right):
    return lax.dot_general(left, right, (((0,), (0,)), ((), ())), preferred_element_type=F32)


def band_bias(table_row):
    spread = jnp.broadcast_to(table_row, (SUB, WINDOW))
    return pltpu.roll(spread, 0, 1, stride=1, stride_axis=0)


def diagonal_sums(rows):
    height, width = rows.shape
    while height > 8:
        height //= 2
        rows = rows[:height] + pltpu.roll(rows[height:], width - height, 1)
    row = lax.broadcasted_iota(jnp.int32, rows.shape, 0)
    for bit in (1, 2, 4):
        rows = jnp.where((row & bit) != 0, pltpu.roll(rows, width - bit, 1), rows)
    return jnp.sum(rows, 0, keepdims=True)


def lane_index():
    return lax.broadcasted_iota(jnp.int32, (1, PAIR), 1)


def own_half(head, value):
    low_lanes = lane_index() < HD
    return jnp.where(low_lanes if head == 0 else ~low_lanes, value, jnp.zeros_like(value))


def other_lane(head):
    return HD * (1 - head)


def with_lanes(head, value, columns):
    wide = own_half(head, value.astype(F32))
    lane = lane_index()
    for offset, column in enumerate(columns):
        wide = jnp.where(lane == other_lane(head) + offset, column, wide)
    return wide.astype(BF16)


def in_three(column):
    high = column.astype(BF16).astype(F32)
    middle = (column - high).astype(BF16).astype(F32)
    return (high, middle, column - high - middle)


def key_bias(first, rows, end):
    position = first + lax.broadcasted_iota(jnp.int32, (rows, 1), 0)
    return jnp.where((position >= 0) & (position < end), 0.0, MASKED)


def pick_column(rows, index):
    return jnp.sum(jnp.where(lane_index() == index, rows, 0.0), -1, keepdims=True)


def key_side(head, keys, bias):
    return with_lanes(head, keys, (bias, 1.0, 1.0, 1.0))


def value_side(head, values):
    return with_lanes(head, values, (1.0, 1.0, 1.0))


def softmax_rows(parts, value_parts, head):
    top = functools.reduce(
        jnp.maximum, [jnp.max(part, -1, keepdims=True) for part in parts]
    )
    mixed = sum(
        dot_n(jnp.exp(part - top).astype(BF16), values)
        for part, values in zip(parts, value_parts)
    )
    at = other_lane(head)
    total = mixed[:, at : at + 1]
    return mixed / total, top + jnp.log(total)


def seq_device(steps, seq_count):
    return (lax.axis_index("dp"), lax.rem(lax.axis_index("seq") + steps + seq_count, seq_count))


def row_norm(rows):
    centred = rows - jnp.mean(rows, -1, keepdims=True)
    inverse = lax.rsqrt(jnp.mean(centred * centred, -1, keepdims=True) + EPSILON)
    return centred * inverse, inverse


def put_column(ref, rows, index, column):
    ref[rows] = jnp.where(lane_index() == index, column, ref[rows])


def lanes_of(at):
    return pl.ds(pl.multiple_of(at * PAIR, PAIR), PAIR)


class Sizes(NamedTuple):
    block: int
    count: int
    quarter: int
    seq_count: int
    pairs: int


def attend_kernel(
    sizes,
    len_ref,
    rel_ref,
    long_ref,
    raw_ref,
    wq_ref,
    wk_ref,
    wv_ref,
    bq_ref,
    bv_ref,
    gain_ref,
    shift_ref,
    q_ref,
    kx_ref,
    vx_ref,
    kg_ref,
    vg_ref,
    o_ref,
    l_ref,
    lq_ref,
    glob_ref,
    tab_ref,
    spread,
    wide,
    part_o,
    part_l,
    from_o,
    from_l,
    halo_sends,
    halo_recvs,
    part_sends,
    part_recvs,
):
    block, count, quarter, seq_count, pairs = sizes
    ext = block + 2 * HALO
    seq_index = lax.axis_index("seq")
    scale = jnp.asarray(HD ** (-0.5), BF16)
    low_lanes = lane_index() < HD
    own_keys = slice(HALO, HALO + block)
    own_rows = pl.ds(pl.multiple_of(seq_index * quarter, quarter), quarter)
    neighbours = (seq_index > 0, seq_index < seq_count - 1)
    barrier = pltpu.get_barrier_semaphore()
    for step in range(1, seq_count):
        pl.semaphore_signal(
            barrier,
            inc=1,
            device_id=seq_device(step, seq_count),
            device_id_type=pl.DeviceIdType.MESH,
        )

    def halo_copies(direction):
        source = HALO if direction == 0 else HALO + block - REACH
        dest = HALO + block if direction == 0 else HALO - REACH
        for kind, ref in enumerate((kx_ref, vx_ref)):
            yield pltpu.make_async_remote_copy(
                src_ref=ref.at[source : source + REACH],
                dst_ref=ref.at[dest : dest + REACH],
                send_sem=halo_sends.at[direction, kind],
                recv_sem=halo_recvs.at[direction, kind],
                device_id=seq_device(2 * direction - 1, seq_count),
                device_id_type=pl.DeviceIdType.MESH,
            )

    def part_copies():
        for step in range(1, seq_count):
            device = seq_device(step, seq_count)
            rows = pl.ds(pl.multiple_of(device[1] * quarter, quarter), quarter)
            for kind, (source, dest) in enumerate(((part_o, from_o), (part_l, from_l))):
                yield step, kind, pltpu.make_async_remote_copy(
                    src_ref=source.at[rows],
                    dst_ref=dest.at[step - 1],
                    send_sem=part_sends.at[kind, step - 1],
                    recv_sem=part_recvs.at[kind, step - 1],
                    device_id=device,
                    device_id_type=pl.DeviceIdType.MESH,
                )

    gain, shift = gain_ref[...], shift_ref[...]
    labels, heads = rel_ref.shape
    spread[...] = jnp.full(spread.shape, MASKED, F32)
    spread[:labels, :heads] = rel_ref[...]
    turned = pltpu.roll(spread[...].T, HALO - R, 1)
    for pair in range(pairs):
        tab_ref[pair] = turned[2 * pair : 2 * pair + 2]
    normed_long = (row_norm(long_ref[...].astype(F32))[0] * gain + shift).astype(BF16)
    kx_ref[own_keys] = dot_n(normed_long, wk_ref[...]).astype(BF16)
    vx_ref[own_keys] = (dot_n(normed_long, wv_ref[...]) + bv_ref[...]).astype(BF16)
    pl.semaphore_wait(barrier, seq_count - 1)
    for direction, first in enumerate((HALO - REACH, HALO + block)):

        @pl.when(neighbours[direction])
        def _(direction=direction):
            for copy in halo_copies(direction):
                copy.start()

        outer = slice(0, first) if direction == 0 else slice(first + REACH, ext)
        for ref in (kx_ref, vx_ref):
            ref[outer] = jnp.zeros((HALO - REACH, ref.shape[1]), BF16)

        @pl.when(jnp.logical_not(neighbours[direction]))
        def _(first=first):
            for ref in (kx_ref, vx_ref):
                ref[first : first + REACH] = jnp.zeros((REACH, ref.shape[1]), BF16)

    wide[...] = jnp.zeros_like(wide)
    wide[:count] = raw_ref[...].astype(F32)
    glob_ref[...] = wide[...].astype(BF16)
    normed_glob = (row_norm(wide[...])[0] * gain + shift).astype(BF16)
    kg_ref[...] = dot_n(normed_glob, wk_ref[...]).astype(BF16)
    vg_ref[...] = (dot_n(normed_glob, wv_ref[...]) + bv_ref[...]).astype(BF16)
    q_ref[block:] = (dot_n(normed_glob, wq_ref[...]) + bq_ref[...]).astype(BF16)
    q_ref[:block] = (dot_n(normed_long, wq_ref[...]) + bq_ref[...]).astype(BF16)
    part_l[...] = jnp.zeros_like(part_l)
    l_ref[...] = jnp.zeros_like(l_ref)

    def glob_pair(pair, carry):
        lanes = lanes_of(pair)
        far_bias = key_bias(seq_index * block, block, len_ref[0])
        near_bias = key_bias(seq_index * quarter, quarter, count)
        query = q_ref[block:, lanes] * scale
        outs = []
        for head in range(2):
            q = with_lanes(head, query, (1.0,))
            far = dot_t(q, with_lanes(head, kx_ref[own_keys, lanes], (far_bias,)))
            near = dot_t(q, with_lanes(head, kg_ref[own_rows, lanes], (near_bias,)))
            out, norm = softmax_rows(
                [far, near],
                [
                    with_lanes(head, vx_ref[own_keys, lanes], (1.0,)),
                    with_lanes(head, vg_ref[own_rows, lanes], (1.0,)),
                ],
                head,
            )
            outs.append(out)
            put_column(part_l, slice(None), 2 * pair + head, norm)
        part_o[:, lanes] = jnp.where(low_lanes, outs[0], outs[1]).astype(BF16)
        return carry

    lax.fori_loop(0, pairs, glob_pair, 0)
    for _, _, copy in part_copies():
        copy.start()
    for direction in range(2):

        @pl.when(neighbours[1 - direction])
        def _(direction=direction):
            for copy in halo_copies(direction):
                copy.wait_recv()

    def long_pair(pair, carry):
        lanes = lanes_of(pair)
        long_bias = key_bias(seq_index * block - HALO, ext, len_ref[0])
        glob_bias = key_bias(0, GP, count)
        query = q_ref[:block, lanes] * scale
        outs = []
        for head in range(2):
            q = with_lanes(head, query, (1.0,))
            kx = with_lanes(head, kx_ref[:, lanes], (long_bias,))
            kg = with_lanes(head, kg_ref[:, lanes], (glob_bias,))
            vx, vg = (with_lanes(head, ref[:, lanes], (1.0,)) for ref in (vx_ref, vg_ref))
            bias = band_bias(tab_ref[pair, head : head + 1])
            mixed = []
            for start in range(0, block, SUB):
                rows, keys = slice(start, start + SUB), slice(start, start + WINDOW)
                out, norm = softmax_rows(
                    [dot_t(q[rows], kx[keys]) + bias, dot_t(q[rows], kg)], [vx[keys], vg], head
                )
                mixed.append(out)
                put_column(l_ref, rows, 2 * pair + head, norm)
            outs.append(jnp.concatenate(mixed, 0))
        o_ref[:block, lanes] = jnp.where(low_lanes, outs[0], outs[1]).astype(BF16)
        return carry

    lax.fori_loop(0, pairs, long_pair, 0)
    for _, _, copy in part_copies():
        copy.wait_recv()
    norms = [part_l[own_rows]] + [from_l[step] for step in range(seq_count - 1)]
    outs = [part_o[own_rows]] + [from_o[step] for step in range(seq_count - 1)]
    top = functools.reduce(jnp.maximum, norms)
    shares = [jnp.exp(norm - top) for norm in norms]
    total = sum(shares)
    lq_ref[...] = top + jnp.log(total)
    shares = [share / total for share in shares]
    for at in range(pairs):
        lanes = slice(at * PAIR, (at + 1) * PAIR)
        mixed = 0.0
        for share, out in zip(shares, outs):
            spread = jnp.where(
                low_lanes, share[:, 2 * at : 2 * at + 1], share[:, 2 * at + 1 : 2 * at + 2]
            )
            mixed += spread * out[:, lanes].astype(F32)
        o_ref[block:, lanes] = mixed.astype(BF16)
    for _, _, copy in part_copies():
        copy.wait_send()
    for direction in range(2):

        @pl.when(neighbours[direction])
        def _(direction=direction):
            for copy in halo_copies(direction):
                copy.wait_send()


def attend(sizes, doc_len, rel_table, long_x, glob_x, *weights):
    block, count, quarter, seq_count, pairs = sizes
    width = long_x.shape[1]
    ext = block + 2 * HALO
    whole = pl.BlockSpec(memory_space=pltpu.VMEM)
    shape = jax.ShapeDtypeStruct
    others = seq_count - 1
    return pl.pallas_call(
        functools.partial(attend_kernel, sizes),
        in_specs=[pl.BlockSpec(memory_space=pltpu.SMEM)] + [whole] * 10,
        out_specs=[whole] * 10,
        out_shape=[
            shape((block + GP, width), BF16),
            shape((ext, width), BF16),
            shape((ext, width), BF16),
            shape((GP, width), BF16),
            shape((GP, width), BF16),
            shape((block + quarter, width), BF16),
            shape((block, PAIR), F32),
            shape((quarter, PAIR), F32),
            shape((GP, width), BF16),
            shape((pairs, 2, WINDOW), F32),
        ],
        scratch_shapes=[
            pltpu.VMEM((WINDOW, PAIR), F32),
            pltpu.VMEM((GP, width), F32),
            pltpu.VMEM((GP, width), BF16),
            pltpu.VMEM((GP, PAIR), F32),
            pltpu.VMEM((others, quarter, width), BF16),
            pltpu.VMEM((others, quarter, PAIR), F32),
            pltpu.SemaphoreType.DMA((2, 2)),
            pltpu.SemaphoreType.DMA((2, 2)),
            pltpu.SemaphoreType.DMA((2, others)),
            pltpu.SemaphoreType.DMA((2, others)),
        ],
        compiler_params=pltpu.CompilerParams(
            collective_id=3, has_side_effects=True, vmem_limit_bytes=56 * 2**20
        ),
        name="attend",
    )(doc_len, rel_table, long_x, glob_x, *weights)


class Reducer:
    def __init__(self, rows, split, scratch, pieces=None, order=None, parts=None):
        self.ids = mesh_ids()
        self.parts = parts
        self.order = order
        self.halves = (slice(0, split), slice(split, rows))
        held, self.from_core, self.from_one, self.from_two = scratch[:4]
        self.local, self.sends, self.recvs = scratch[4:7]
        if parts is None:
            self.from_z, self.z_sends, self.z_recvs = scratch[7:]
        self.pieces, self.held = pieces, held
        self.mine = held.at[self.ids[3]] if pieces is None else held.at[0]

    @staticmethod
    def scratch(rows, width, sides, with_z=False):
        buffers = [
            pltpu.VMEM((sides, 4, 2, 2, rows, width), BF16),
            pltpu.VMEM((4, 2, 2, rows, width), BF16),
            pltpu.VMEM((4, 2, rows, width), BF16),
            pltpu.VMEM((4, rows, width), BF16),
            pltpu.SemaphoreType.DMA((4,)),
            pltpu.SemaphoreType.DMA((5, 4)),
            pltpu.SemaphoreType.DMA((5, 4)),
        ]
        if with_z:
            buffers += [
                pltpu.VMEM((3, rows, width), BF16),
                pltpu.SemaphoreType.DMA((4,)),
                pltpu.SemaphoreType.DMA((3,)),
            ]
        return buffers

    def partners(self):
        z, y, x, core = self.ids
        dp, seq = z * 2 + y, x * 2 + core
        near = [(dp, x * 2 + 1 - core), (dp, (1 - x) * 2 + core), (z * 2 + 1 - y, seq)]
        return near + [(lax.rem(z + step, 4) * 2 + y, seq) for step in (1, 2, 3)]

    def target(self, chunk):
        return self.order(chunk) if self.order else lax.rem(self.ids[0] + 1 + chunk, 4)

    def remote(self, source, dest, kind, send_at, recv_at, device):
        return pltpu.make_async_remote_copy(
            src_ref=source,
            dst_ref=dest,
            send_sem=self.sends.at[kind, send_at],
            recv_sem=self.recvs.at[kind, recv_at],
            device_id=device,
            device_id_type=pl.DeviceIdType.MESH,
        )

    def own_copy(self, chunk):
        core, to = self.ids[3], self.target(chunk)
        return pltpu.make_async_copy(
            self.pieces.at[core, to], self.mine.at[to], self.local.at[chunk]
        )

    def core_copy(self, chunk):
        core, to = self.ids[3], self.target(chunk)
        source = (self.held if self.pieces is None else self.pieces).at[1 - core, to]
        return self.remote(source, self.from_core.at[to], 0, chunk, chunk, self.partners()[0])

    def first_copies(self, chunk):
        z, y, x, core = self.ids
        to = self.target(chunk)
        one, two = self.halves
        near = self.partners()
        return (
            self.remote(
                self.mine.at[to, :, 1 - x, one],
                self.from_one.at[to, :, one],
                1,
                chunk,
                chunk,
                near[1],
            ),
            self.remote(
                self.mine.at[to, 1 - y, :, two],
                self.from_one.at[to, :, two],
                2,
                chunk,
                chunk,
                near[2],
            ),
        )

    def second_copies(self, chunk):
        z, y, x, core = self.ids
        to = self.target(chunk)
        one, two = self.halves
        near = self.partners()
        return (
            self.remote(
                self.mine.at[to, 1 - y, x, one],
                self.from_two.at[to, one],
                3,
                chunk,
                chunk,
                near[2],
            ),
            self.remote(
                self.mine.at[to, y, 1 - x, two],
                self.from_two.at[to, two],
                4,
                chunk,
                chunk,
                near[1],
            ),
        )

    def last_copy(self, chunk):
        z, y, x, core = self.ids
        to = self.target(chunk)
        slot = lax.rem(z - to + 4, 4) - 1
        return pltpu.make_async_remote_copy(
            src_ref=self.mine.at[to, y, x],
            dst_ref=self.from_z.at[slot],
            send_sem=self.z_sends.at[chunk],
            recv_sem=self.z_recvs.at[slot],
            device_id=(to * 2 + y, x * 2 + core),
            device_id_type=pl.DeviceIdType.MESH,
        )

    def arrival(self, slot):
        z, y, x, core = self.ids
        return pltpu.make_async_remote_copy(
            src_ref=self.mine.at[z, y, x],
            dst_ref=self.from_z.at[slot],
            send_sem=self.z_sends.at[slot],
            recv_sem=self.z_recvs.at[slot],
            device_id=self.partners()[3],
            device_id_type=pl.DeviceIdType.MESH,
        )

    def leaves(self, chunk):
        return self.target(chunk) != self.ids[0]

    def fill(self, to, at, value):
        self.held[at % 2, to, at // 4, at // 2 % 2] = value.astype(BF16)

    def start(self, chunk):
        self.core_copy(chunk).start()
        if self.pieces is not None:
            self.own_copy(chunk).start()

    def add_core(self, chunk):
        to = self.target(chunk)
        if self.pieces is not None:
            self.own_copy(chunk).wait()
        self.core_copy(chunk).wait_recv()

        def add(index, carry):
            at = (to, lax.div(index, 2), lax.rem(index, 2))
            self.mine[at] = self.mine[at] + self.from_core[at]
            return carry

        lax.fori_loop(0, 4, add, 0)
        for copy in self.first_copies(chunk):
            copy.start()

    def add_first(self, chunk):
        z, y, x, core = self.ids
        one, two = self.halves
        to = self.target(chunk)
        for copy in self.first_copies(chunk):
            copy.wait_recv()

        def add(index, carry):
            for at, rows in (((to, index, x), one), ((to, y, index), two)):
                self.mine[at + (rows,)] = self.mine[at + (rows,)] + self.from_one[to, index, rows]
            return carry

        lax.fori_loop(0, 2, add, 0)
        for copy in self.second_copies(chunk):
            copy.start()

    def add_second(self, chunk):
        z, y, x, core = self.ids
        to = self.target(chunk)
        for copy in self.second_copies(chunk):
            copy.wait_recv()
        if self.parts is not None:
            self.parts[to] = self.mine[to, y, x] + self.from_two[to]
            return

        @pl.when(self.leaves(chunk))
        def _():
            self.mine[to, y, x] = self.mine[to, y, x] + self.from_two[to]
            self.last_copy(chunk).start()

    def finish(self, out=None):
        z, y, x, core = self.ids
        if self.parts is None:
            total = self.mine[z, y, x].astype(F32) + self.from_two[z].astype(F32)
            for slot in range(3):
                self.arrival(slot).wait_recv()
                total += self.from_z[slot].astype(F32)
            out[...] = total
        for chunk in range(4):
            self.core_copy(chunk).wait_send()
            for copy in self.first_copies(chunk) + self.second_copies(chunk):
                copy.wait_send()
            if self.parts is None:

                @pl.when(self.leaves(chunk))
                def _(chunk=chunk):
                    self.last_copy(chunk).wait_send()


class ZSum:
    def __init__(self, parts, scratch):
        self.ids = mesh_ids()
        self.parts = parts
        self.own, self.from_z, self.local, self.sends, self.recvs = scratch

    @staticmethod
    def scratch(rows, width):
        return [
            pltpu.VMEM((rows, width), BF16),
            pltpu.VMEM((3, rows, width), BF16),
            pltpu.SemaphoreType.DMA,
            pltpu.SemaphoreType.DMA((3,)),
            pltpu.SemaphoreType.DMA((3,)),
        ]

    def own_copy(self):
        return pltpu.make_async_copy(self.parts.at[self.ids[0]], self.own, self.local)

    def copies(self):
        z, y, x, core = self.ids
        for slot in range(3):
            to = lax.rem(z + 3 - slot, 4)
            yield pltpu.make_async_remote_copy(
                src_ref=self.parts.at[to],
                dst_ref=self.from_z.at[slot],
                send_sem=self.sends.at[slot],
                recv_sem=self.recvs.at[slot],
                device_id=(to * 2 + y, x * 2 + core),
                device_id_type=pl.DeviceIdType.MESH,
            )

    def start(self):
        self.own_copy().start()
        for copy in self.copies():
            copy.start()

    def finish(self, out):
        self.own_copy().wait()
        total = self.own[...].astype(F32)
        for slot, copy in enumerate(self.copies()):
            copy.wait_recv()
            total += self.from_z[slot].astype(F32)
        out[...] = total
        for copy in self.copies():
            copy.wait_send()


def mesh_ids():
    dp, seq = lax.axis_index("dp"), lax.axis_index("seq")
    return lax.div(dp, 2), lax.rem(dp, 2), lax.div(seq, 2), lax.rem(seq, 2)


def meet(devices):
    barrier = pltpu.get_barrier_semaphore()
    for device in devices:
        pl.semaphore_signal(barrier, inc=1, device_id=device, device_id_type=pl.DeviceIdType.MESH)
    pl.semaphore_wait(barrier, len(devices))


EARLY_PLAN = (
    (2, "add_core", 0),
    (3, "add_core", 1),
    (4, "add_core", 2),
    (5, "add_core", 3),
    (7, "add_first", 0),
    (8, "add_first", 1),
    (9, "add_second", 0),
    (9, "add_first", 2),
    (10, "add_second", 1),
    (10, "add_first", 3),
    (11, "add_second", 2),
    (12, "add_second", 3),
)


def late_kernel(
    sizes,
    planned,
    long_ref,
    glob_ref,
    dq_ref,
    dk_ref,
    dv_ref,
    dmid_ref,
    wq_ref,
    wk_ref,
    wv_ref,
    gain_ref,
    shift_ref,
    table_ref,
    *rest,
):
    block, count, quarter, seq_count, pairs = sizes
    rows = block + quarter
    width = long_ref.shape[1]
    if planned:
        early_parts, long_out, glob_out, late_ref, total_ref, early_ref, *rest = rest
    else:
        long_out, glob_out, gq_ref, gk_ref, gv_ref, total_ref, *rest = rest
    normed_t, every, gather_sends, gather_recvs, *rest = rest
    seq_index = lax.axis_index("seq")
    own_rows = pl.ds(pl.multiple_of(seq_index * quarter, quarter), quarter)
    others = [seq_device(step, seq_count) for step in range(1, seq_count)]

    def gathers():
        for step, device in enumerate(others):
            yield pltpu.make_async_remote_copy(
                src_ref=every.at[own_rows],
                dst_ref=every.at[own_rows],
                send_sem=gather_sends.at[step],
                recv_sem=gather_recvs.at[step],
                device_id=device,
                device_id_type=pl.DeviceIdType.MESH,
            )

    if planned:
        kept, arrived, table_sends, table_recvs, *rest = rest
        z_sum = ZSum(early_parts, rest[:5])
        reducer = Reducer(rest[5].shape[-2], 32, rest[5:])
        z, y, x, core = mesh_ids()
        partners = reducer.partners()[:3] + [
            ((z + 1 - 2 * lax.rem(z, 2)) * 2 + y, lax.axis_index("seq")),
            (lax.rem(z + 2, 4) * 2 + y, lax.axis_index("seq")),
        ]

        def table_copy(stage):
            return pltpu.make_async_remote_copy(
                src_ref=kept.at[stage],
                dst_ref=arrived.at[stage],
                send_sem=table_sends.at[stage],
                recv_sem=table_recvs.at[stage],
                device_id=partners[stage],
                device_id_type=pl.DeviceIdType.MESH,
            )

        def table_step(stage):
            table_copy(stage).wait_recv()
            kept[stage + 1] = kept[stage] + arrived[stage]
            if stage < 4:
                table_copy(stage + 1).start()

    meet(others + (reducer.partners()[2:] if planned else []))
    if planned:
        z_sum.start()
    everything = jnp.concatenate([long_ref[...], glob_ref[own_rows]], 0).astype(F32)
    hat, inverse = row_norm(everything)
    normed_t[...] = (hat * gain_ref[...] + shift_ref[...]).astype(BF16).T
    if planned:
        piece = width // 32
        blank = jnp.zeros((8, width), F32)
        def weight_rows(chunk):
            to = reducer.target(chunk)
            some = normed_t[pl.ds(pl.multiple_of(to * 8 * piece, 64), 8 * piece)]
            parts = [dot_n(some, ref[...]) for ref in (dq_ref, dk_ref, dv_ref)]
            for at in range(8):
                rows_at = slice(at * piece, (at + 1) * piece)
                reducer.fill(
                    to, at, jnp.concatenate([part[rows_at] for part in parts] + [blank], 0)
                )
            reducer.start(chunk)

        weight_rows(0)
        weight_rows(1)
        reducer.add_core(0)
        weight_rows(2)
        reducer.add_core(1)
        weight_rows(3)
        grads = dot_t(dq_ref[...], wq_ref[...])
        reducer.add_first(0)
        reducer.add_core(2)
        grads += dot_t(dk_ref[...], wk_ref[...]) + dot_t(dv_ref[...], wv_ref[...])
        reducer.add_first(1)
        reducer.add_core(3)
        reducer.add_second(0)
    else:
        for ref, out in ((dq_ref, gq_ref), (dk_ref, gk_ref), (dv_ref, gv_ref)):
            out[...] = dot_n(normed_t[...], ref[...]).astype(BF16)
        grads = (
            dot_t(dq_ref[...], wq_ref[...])
            + dot_t(dk_ref[...], wk_ref[...])
            + dot_t(dv_ref[...], wv_ref[...])
        )
    scaled = grads * gain_ref[...]
    total = dmid_ref[...] + inverse * (
        scaled
        - jnp.mean(scaled, -1, keepdims=True)
        - hat * jnp.mean(scaled * hat, -1, keepdims=True)
    )
    every[own_rows] = total[block:].astype(BF16)
    for copy in gathers():
        copy.start()
    long_out[...] = total[:block]
    sums = [
        column_sum(part)
        for part in (dq_ref[...].astype(F32), dv_ref[...].astype(F32), grads * hat, grads)
    ]
    heads = 2 * pairs
    first = kept.at[0] if planned else total_ref
    first[...] = jnp.zeros(first.shape, F32)
    for pair in range(pairs):
        first[2 * pair : 2 * pair + 2, :WINDOW] = table_ref[pair]
    for at, vector in enumerate(sums):
        first[heads + at : heads + at + 1] = vector
    if planned:
        table_copy(0).start()
        for number, (act, chunk) in enumerate(LATE_TAIL):
            getattr(reducer, act)(chunk)
            table_step(number)
        total_ref[...] = kept[5]
        z_sum.finish(early_ref)
        reducer.finish(late_ref)
        for stage in range(5):
            table_copy(stage).wait_send()
    for copy in gathers():
        copy.wait_recv()
    glob_out[...] = every[:count].astype(F32)
    for copy in gathers():
        copy.wait_send()


LATE_TAIL = (
    ("add_first", 2),
    ("add_second", 1),
    ("add_first", 3),
    ("add_second", 2),
    ("add_second", 3),
)


def last_part(sizes, planned, long_x, glob_x, dq, dk, dv, dmid, *weights):
    block, count, quarter, seq_count, pairs = sizes
    rows, width = dq.shape
    others = seq_count - 1
    whole = pl.BlockSpec(memory_space=pltpu.VMEM)
    shape = jax.ShapeDtypeStruct
    sums = shape(((2 * pairs + 4 + 7) // 8 * 8, width), F32)
    outs = [shape((block, width), F32), shape((count, width), F32)]
    scratch = [
        pltpu.VMEM((width, rows), BF16),
        pltpu.VMEM((GP, width), BF16),
        pltpu.SemaphoreType.DMA((others,)),
        pltpu.SemaphoreType.DMA((others,)),
    ]
    if planned:
        piece = width // 32
        part = 3 * piece + 8
        early = weights[-1].shape[1:]
        outs += [shape((part, width), F32), sums, shape(early, F32)]
        scratch += [
            pltpu.VMEM((6,) + sums.shape, F32),
            pltpu.VMEM((5,) + sums.shape, F32),
            pltpu.SemaphoreType.DMA((5,)),
            pltpu.SemaphoreType.DMA((5,)),
        ]
        scratch += ZSum.scratch(*early) + Reducer.scratch(part, width, 2, with_z=True)
    else:
        outs += [shape((width, width), BF16)] * 3 + [sums]
    return pl.pallas_call(
        functools.partial(late_kernel, sizes, planned),
        in_specs=[whole] * 12 + [pl.BlockSpec(memory_space=pl.ANY)] * planned,
        out_specs=[whole] * len(outs),
        out_shape=outs,
        scratch_shapes=scratch,
        compiler_params=pltpu.CompilerParams(
            collective_id=2, has_side_effects=True, vmem_limit_bytes=60 * 2**20
        ),
        name="last_part",
    )(long_x, glob_x, dq, dk, dv, dmid, *weights)


def small_kernel(heads, early_ref, late_ref, outer_ref, inner_ref, sums_ref, *rest):
    *refs, sems = rest
    big = len(refs) - 16
    outs = refs[big // 2 : big // 2 + 16]
    copies = [
        pltpu.make_async_copy(source, dest, sems.at[at])
        for at, (source, dest) in enumerate(zip(refs, refs[big // 2 + 16 :]))
    ]
    for copy in copies:
        copy.start()
    g_query, g_key, g_value, g_out, g_inner, g_outer, *vectors, table = outs
    device = lax.axis_index("dp") * lax.axis_size("seq") + lax.axis_index("seq")
    piece, width = g_query.shape
    for at, out in enumerate((g_query, g_key, g_value)):
        out[...] = late_ref[at * piece : (at + 1) * piece]
    g_out[...] = early_ref[2 * piece : 3 * piece]
    g_outer[...] = outer_ref[...]
    for source, first, chunk in (
        (inner_ref, 0, 0),
        (inner_ref, piece, 3),
        (early_ref, 0, 1),
        (early_ref, piece, 2),
    ):
        g_inner[:, chunk * width : (chunk + 1) * width] = source[first : first + piece]

    def entries(row, at, length):
        return pltpu.roll(row, width - at * length, 1)[0, :length]

    b_query, b_value, b_out, b_outer, gain_one, shift_one, gain_two, shift_two, b_inner = vectors
    for at, out in enumerate((b_query, b_value, gain_one, shift_one)):
        out[...] = entries(sums_ref[heads + at : heads + at + 1], device, piece)
    for at, out in enumerate((b_out, b_outer, gain_two, shift_two)):
        row = 3 * piece + at
        out[...] = entries(early_ref[row : row + 1], device, piece)
    row = pl.ds(3 * piece + 4 + lax.div(device, 8), 1)
    b_inner[...] = entries(early_ref[row], lax.rem(device, 8), 4 * piece)
    labels = table.shape[0]
    turned = pltpu.roll(sums_ref[:, :WINDOW], WINDOW - HALO + R, 1).T
    table[...] = turned[:labels, :heads]
    for copy in copies:
        copy.wait()


def small_results(heads, early, late, outer, inner, sums, *big):
    width = early.shape[1]
    piece = width // 32
    shape = jax.ShapeDtypeStruct
    whole = pl.BlockSpec(memory_space=pltpu.VMEM)
    outs = [shape((piece, width), F32)] * 4
    outs += [shape((piece, 4 * width), F32), shape((4 * piece, width), F32)]
    outs += [shape((piece,), F32)] * 8 + [shape((4 * piece,), F32)]
    outs += [shape((2 * R + 1, heads), F32)]
    there = [pl.BlockSpec(memory_space=pl.ANY)] * len(big)
    return pl.pallas_call(
        functools.partial(small_kernel, heads),
        in_specs=[whole] * 5 + there,
        out_specs=[whole] * len(outs) + there,
        out_shape=outs + [shape(part.shape, part.dtype) for part in big],
        scratch_shapes=[pltpu.SemaphoreType.DMA((len(big),))],
        name="small_results",
    )(early, late, outer, inner, sums, *big)


def has_plan():
    return (lax.axis_size("dp"), lax.axis_size("seq")) == (8, 4)


GELU_A = 0.7978845608028654
GELU_B = 0.044715


def gate_both(u):
    square = u * u
    turned = jnp.tanh(GELU_A * u * (1.0 + GELU_B * square))
    half = 0.5 * (1.0 + turned)
    slope = half + 0.5 * u * (1.0 - turned * turned) * (
        GELU_A * (1.0 + 3.0 * GELU_B * square)
    )
    return u * half, slope


def column_sum(rows):
    return jnp.sum(rows, 0, keepdims=True)


def ffn_kernel(
    sizes,
    planned,
    len_ref,
    attn_ref,
    long_ref,
    glob_ref,
    dlong_ref,
    dglob_ref,
    lq_ref,
    wo_ref,
    bo_ref,
    gain_ref,
    shift_ref,
    wi_ref,
    bi_ref,
    wr_ref,
    br_ref,
    long_out,
    glob_out,
    dmid_ref,
    do_ref,
    dog_ref,
    ldg_ref,
    *rest,
):
    block, count, quarter, seq_count, pairs = sizes
    if planned:
        pieces_ref, outer_ref, inner_ref, *rest = rest
    else:
        g_outer_ref, g_inner_ref, g_out_ref, vec_ref, *rest = rest
    (
        mid,
        y_sum,
        df_sum,
        normed,
        normed_t,
        dy,
        vectors,
        biases,
        every_do,
        every_ld,
        gather_sends,
        gather_recvs,
        *rest,
    ) = rest
    if planned:
        even, *rest = rest
        outer = Reducer(rest[0].shape[-2], 48, rest[:7], order=chunk_of, parts=outer_ref)
        inner = Reducer(rest[7].shape[-2], 16, rest[7:], parts=inner_ref)
    step = pl.program_id(0)
    chunk = chunk_of(step)
    seq_index = lax.axis_index("seq")
    own_rows = pl.ds(pl.multiple_of(seq_index * quarter, quarter), quarter)
    width = mid.shape[1]
    piece = width // 32

    def rows_of(device):
        return pl.ds(pl.multiple_of(device[1] * quarter, quarter), quarter)

    def gather(owner, device, at):
        for kind, every in enumerate((every_do, every_ld)):
            yield pltpu.make_async_remote_copy(
                src_ref=every.at[rows_of(owner)],
                dst_ref=every.at[rows_of(owner)],
                send_sem=gather_sends.at[kind, at],
                recv_sem=gather_recvs.at[kind, at],
                device_id=device,
                device_id_type=pl.DeviceIdType.MESH,
            )

    me = seq_device(0, seq_count)
    if planned:
        sibling, across = outer.partners()[:2]
        first_gathers = [(me, across, 0), (me, sibling, 1)]
        second_gathers = [(across, sibling, 2)]
    else:
        first_gathers = [
            (me, seq_device(at + 1, seq_count), at) for at in range(seq_count - 1)
        ]
        second_gathers = []

    def act(now):
        if planned:
            for at, reducer, name, part in FFN_PLAN:
                if at == now:
                    getattr((outer, inner)[reducer], name)(part)

    def act_in_step(point):
        if planned:
            for now in range(4):
                if any(at == (now, point) for at, _, _, _ in FFN_PLAN):

                    @pl.when(step == now)
                    def _(now=now):
                        act((now, point))

    @pl.when(step == 0)
    def _():
        others = [seq_device(seq_step, seq_count) for seq_step in range(1, seq_count)]
        meet(others + (outer.partners()[2:] if planned else []))
        projected = dot_n(attn_ref[...], wo_ref[...]) + bo_ref[...]
        mid[:block] = long_ref[...].astype(F32) + projected[:block]
        mid[block:] = glob_ref[own_rows].astype(F32) + projected[block:]
        hat, _ = row_norm(mid[...])
        normed[...] = (hat * gain_ref[...] + shift_ref[...]).astype(BF16)
        normed_t[...] = normed[...].T
        position = seq_index * block + lax.broadcasted_iota(jnp.int32, (block, 1), 0)
        dy[:block] = jnp.where(
            position < len_ref[0], dlong_ref[...].astype(F32), 0.0
        ).astype(BF16)
        y_sum[:GP] = jnp.zeros((GP, width), F32)
        y_sum[:count] = dglob_ref[...].astype(F32)
        dy[block:] = y_sum[own_rows].astype(BF16)
        vectors[1:2] = column_sum(dy[...].astype(F32))
        y_sum[...] = mid[...] + br_ref[...]
        df_sum[...] = jnp.zeros_like(df_sum)
        for at in range(4):
            biases[at] = bi_ref[at * width : (at + 1) * width].reshape(1, width)

    act_in_step(0)
    active, slope = gate_both(dot_n(normed[...], wi_ref[...]) + biases[chunk])
    active = active.astype(BF16)
    g_outer = t_dot(active, dy[...])
    if planned:
        for at in range(8):
            outer.fill(chunk, at, g_outer[at * 4 * piece : (at + 1) * 4 * piece])
        outer.start(step)
    else:
        g_outer_ref[...] = g_outer.astype(BF16)
    y_sum[...] += dot_n(active, wr_ref[...])
    hidden = dot_t(dy[...], wr_ref[...]) * slope
    for at in range(4):

        @pl.when(chunk == at)
        def _(at=at):
            vectors[4 + at : 5 + at] = column_sum(hidden)

    hidden = hidden.astype(BF16)
    act_in_step(1)
    df_sum[...] += dot_t(hidden, wi_ref[...])
    g_inner = dot_n(normed_t[...], hidden)
    if planned:

        @pl.when(lax.rem(step, 2) == 0)
        def _():
            even[...] = g_inner

        def halves(at):
            part = slice(at * piece, (at + 1) * piece)
            return jnp.concatenate([even[part], g_inner[part]], 0)

        @pl.when(step == 1)
        def _():
            for at in range(32):
                inner.fill(at // 8, at % 8, halves(at))
            for part in range(4):
                inner.start(part)

        @pl.when(step == 3)
        def _():
            for at in range(32):
                pieces_ref[at % 2, at // 8, at // 4 % 2, at // 2 % 2, : 2 * piece] = halves(
                    at
                ).astype(BF16)

    else:
        g_inner_ref[...] = g_inner.astype(BF16)

    def norm_back(rows):
        hat, inverse = row_norm(mid[rows])
        df = df_sum[rows]
        scaled = df * gain_ref[...]
        dmid = dy[rows].astype(F32) + inverse * (
            scaled
            - jnp.mean(scaled, -1, keepdims=True)
            - hat * jnp.mean(scaled * hat, -1, keepdims=True)
        )
        dmid_ref[rows] = dmid
        low = dmid.astype(BF16)
        grad_o = dot_t(low, wo_ref[...]).astype(BF16)
        do_ref[rows] = grad_o
        return [column_sum(dmid), column_sum(df * hat), column_sum(df)], low, grad_o

    @pl.when(step == 3)
    def _():
        glob_sums, glob_low, grad_o = norm_back(slice(block, block + quarter))
        every_do[own_rows] = grad_o
        both = grad_o.astype(F32) * attn_ref[block:].astype(F32)
        stats = lq_ref[...]
        for head in range(2 * pairs):
            lanes = slice(head // 2 * PAIR, head // 2 * PAIR + PAIR)
            delta = jnp.sum(own_half(head % 2, both[:, lanes]), -1, keepdims=True)
            stats = jnp.where(lane_index() == HD + head, delta, stats)
        every_ld[own_rows] = stats
        for part in first_gathers:
            for copy in gather(*part):
                copy.start()
        glob_out[...] = y_sum[block:].astype(BF16)
        act((4, 0))
        position = seq_index * block + lax.broadcasted_iota(jnp.int32, (block, 1), 0)
        long_out[...] = jnp.where(position < len_ref[0], y_sum[:block], 0.0).astype(BF16)
        long_sums, long_low, _ = norm_back(slice(0, block))
        for at, one, two in zip((0, 2, 3), long_sums, glob_sums):
            vectors[at : at + 1] = one + two
        if planned:
            for copy in gather(*first_gathers[0]):
                copy.wait_recv()
            for copy in gather(*second_gathers[0]):
                copy.start()
        act((4, 1))
        g_out = t_dot(attn_ref[...], jnp.concatenate([long_low, glob_low], 0))
        if planned:
            for at in range(32):
                pieces_ref[at % 2, at // 8, at // 4 % 2, at // 2 % 2, 2 * piece :] = (
                    jnp.concatenate(
                        [g_out[at * piece : (at + 1) * piece], vectors[...]], 0
                    ).astype(BF16)
                )
            act((4, 2))
            outer.finish()
            inner.finish()
        else:
            g_out_ref[...] = g_out.astype(BF16)
            vec_ref[...] = vectors[...]
        for part in (first_gathers[1:] if planned else first_gathers) + second_gathers:
            for copy in gather(*part):
                copy.wait_recv()
        dog_ref[...] = every_do[...]
        ldg_ref[...] = every_ld[...]
        for part in first_gathers + second_gathers:
            for copy in gather(*part):
                copy.wait_send()


OUTER, INNER = 0, 1
FFN_PLAN = (
    ((1, 0), OUTER, "add_core", 0),
    ((2, 0), OUTER, "add_first", 0),
    ((2, 0), OUTER, "add_core", 1),
    ((2, 1), OUTER, "add_second", 0),
    ((2, 1), INNER, "add_core", 0),
    ((2, 1), INNER, "add_core", 1),
    ((2, 1), INNER, "add_core", 2),
    ((2, 1), INNER, "add_core", 3),
    ((3, 0), OUTER, "add_first", 1),
    ((3, 0), OUTER, "add_core", 2),
    ((3, 1), OUTER, "add_second", 1),
    ((3, 1), INNER, "add_first", 0),
    ((3, 1), INNER, "add_first", 1),
    ((4, 0), OUTER, "add_core", 3),
    ((4, 0), OUTER, "add_first", 2),
    ((4, 0), INNER, "add_second", 0),
    ((4, 0), INNER, "add_first", 2),
    ((4, 0), INNER, "add_second", 1),
    ((4, 0), INNER, "add_first", 3),
    ((4, 1), OUTER, "add_second", 2),
    ((4, 1), OUTER, "add_first", 3),
    ((4, 1), INNER, "add_second", 2),
    ((4, 2), OUTER, "add_second", 3),
    ((4, 2), INNER, "add_second", 3),
)


def chunk_of(step):
    return jnp.where(step == 0, 0, jnp.where(step == 1, 3, step - 1))


def feed_forward(sizes, planned, doc_len, attn, long_x, glob_x, dlong, dglob, lq, *weights):
    block, count, quarter, seq_count, pairs = sizes
    wo, bo, gain, shift, wi, bi, wr, br = weights
    width, hidden = wi.shape
    chunk = hidden // 4
    rows = block + quarter
    whole = pl.BlockSpec(memory_space=pltpu.VMEM)
    shape = jax.ShapeDtypeStruct
    in_specs = [pl.BlockSpec(memory_space=pltpu.SMEM)] + [whole] * 10
    in_specs += [
        pl.BlockSpec((width, chunk), lambda c: (0, chunk_of(c))),
        whole,
        pl.BlockSpec((chunk, width), lambda c: (chunk_of(c), 0)),
        whole,
    ]
    outs = [
        shape((block, width), BF16),
        shape((quarter, width), BF16),
        shape((rows, width), F32),
        shape((rows, width), BF16),
        shape((GP, width), BF16),
        shape((GP, PAIR), F32),
    ]
    out_specs = [whole] * 6
    others = seq_count - 1
    scratch = [
        pltpu.VMEM((rows, width), F32),
        pltpu.VMEM((rows, width), F32),
        pltpu.VMEM((rows, width), F32),
        pltpu.VMEM((rows, width), BF16),
        pltpu.VMEM((width, rows), BF16),
        pltpu.VMEM((rows, width), BF16),
        pltpu.VMEM((8, width), F32),
        pltpu.VMEM((4, 1, chunk), F32),
        pltpu.VMEM((GP, width), BF16),
        pltpu.VMEM((GP, PAIR), F32),
        pltpu.SemaphoreType.DMA((2, others)),
        pltpu.SemaphoreType.DMA((2, others)),
    ]
    if planned:
        part, piece = hidden // 32, width // 32
        outs += [
            shape((2, 4, 2, 2, 3 * piece + 8, width), BF16),
            shape((4, part, width), BF16),
            shape((4, 2 * piece, width), BF16),
        ]
        out_specs += [whole] * 3
        scratch += [
            pltpu.VMEM((width, chunk), F32),
        ]
        scratch += Reducer.scratch(part, width, 2) + Reducer.scratch(2 * piece, width, 2)
    else:
        outs += [
            shape((hidden, width), BF16),
            shape((width, hidden), BF16),
            shape((width, width), BF16),
            shape((8, width), F32),
        ]
        out_specs += [
            pl.BlockSpec((chunk, width), lambda c: (chunk_of(c), 0)),
            pl.BlockSpec((width, chunk), lambda c: (0, chunk_of(c))),
            whole,
            whole,
        ]
    return pl.pallas_call(
        functools.partial(ffn_kernel, sizes, planned),
        grid=(4,),
        in_specs=in_specs,
        out_specs=out_specs,
        out_shape=outs,
        scratch_shapes=scratch,
        compiler_params=pltpu.CompilerParams(
            collective_id=4, has_side_effects=True, vmem_limit_bytes=62 * 2**20
        ),
        name="feed_forward",
    )(doc_len, attn, long_x, glob_x, dlong, dglob, lq, wo, bo, gain, shift, wi, bi, wr, br)


def back_kernel(
    sizes,
    early_rows,
    len_ref,
    tab_ref,
    q_ref,
    kx_ref,
    vx_ref,
    kg_ref,
    vg_ref,
    o_ref,
    do_ref,
    l_ref,
    dog_ref,
    ldg_ref,
    yq_ref,
    *rest,
):
    block, count, quarter, seq_count, pairs = sizes
    reduces = early_rows > 0
    if reduces:
        pieces_ref, outer_parts, inner_parts, *rest = rest
    dq_ref, dk_ref, dv_ref, dtab_ref, glob_out, *rest = rest
    if reduces:
        early_parts, outer_ref, inner_ref, *rest = rest
    (
        dkx,
        dvx,
        dkg,
        dvg,
        q_send,
        q_recv,
        kv_send,
        kv_recv,
        halo_send,
        halo_recv,
        glob_sends,
        glob_recvs,
        halo_sends,
        halo_recvs,
        every,
        gather_sends,
        gather_recvs,
        *rest,
    ) = rest
    number = pl.program_id(0)
    pair = lax.rem(number, pairs)
    seq_index = lax.axis_index("seq")
    if reduces:
        reducer = Reducer(early_rows, 16, rest[:7], pieces=pieces_ref, parts=early_parts)
        z_sums = (
            (ZSum(outer_parts, rest[7:12]), outer_ref),
            (ZSum(inner_parts, rest[12:]), inner_ref),
        )
    scale = HD ** (-0.5)
    low_lanes = lane_index() < HD
    own_keys = slice(HALO, HALO + block)
    own_rows = pl.ds(pl.multiple_of(seq_index * quarter, quarter), quarter)

    def glob_copies(kind, at):
        source, dest = ((q_send, q_recv), (kv_send, kv_recv))[kind]
        for step in range(1, seq_count):
            device = seq_device(step, seq_count)
            yield pltpu.make_async_remote_copy(
                src_ref=source.at[device[1], at],
                dst_ref=dest.at[step - 1, at],
                send_sem=glob_sends.at[kind, step - 1, at],
                recv_sem=glob_recvs.at[kind, step - 1, at],
                device_id=device,
                device_id_type=pl.DeviceIdType.MESH,
            )

    def gathers():
        for step in range(1, seq_count):
            yield pltpu.make_async_remote_copy(
                src_ref=every.at[own_rows],
                dst_ref=every.at[own_rows],
                send_sem=gather_sends.at[step - 1],
                recv_sem=gather_recvs.at[step - 1],
                device_id=seq_device(step, seq_count),
                device_id_type=pl.DeviceIdType.MESH,
            )

    def halo_copy(direction, at):
        return pltpu.make_async_remote_copy(
            src_ref=halo_send.at[direction, at],
            dst_ref=halo_recv.at[direction, at],
            send_sem=halo_sends.at[direction, at],
            recv_sem=halo_recvs.at[direction, at],
            device_id=seq_device(2 * direction - 1, seq_count),
            device_id_type=pl.DeviceIdType.MESH,
        )

    has_low, has_high = seq_index > 0, seq_index < seq_count - 1
    sends_to = (has_low, has_high)
    gets_from = (has_high, has_low)

    def close_pair(at):
        lanes = lanes_of(at)
        for direction in range(2):

            @pl.when(gets_from[direction])
            def _(direction=direction):
                halo_copy(direction, at).wait_recv()

        for kind, (total, out) in enumerate(((dkx, dk_ref), (dvx, dv_ref))):
            first, last = HALO + REACH, HALO + block - REACH
            out[:REACH, lanes] = (
                total[at, HALO:first] + halo_recv[1, at, kind].astype(F32)
            ).astype(BF16)
            out[REACH : block - REACH, lanes] = total[at, first:last].astype(BF16)
            out[block - REACH : block, lanes] = (
                total[at, last : HALO + block] + halo_recv[0, at, kind].astype(F32)
            ).astype(BF16)
        sums = []
        for kind, (source, dest) in enumerate(((q_send, q_recv), (kv_send, kv_recv))):
            total = source[seq_index, at].astype(F32)
            for step, copy in enumerate(glob_copies(kind, at)):
                copy.wait_recv()
                total += dest[step, at].astype(F32)
            sums.append(total.astype(BF16))
        dq_ref[block:, lanes] = sums[0]
        dk_ref[block:, lanes] = sums[1][:, :PAIR]
        dv_ref[block:, lanes] = sums[1][:, PAIR:]

    def run_plan(now):
        for at, act, chunk in EARLY_PLAN:
            if now == at:
                getattr(reducer, act)(chunk)

    @pl.when(number == 0)
    def _():
        others = [seq_device(step, seq_count) for step in range(1, seq_count)]
        meet(others + (reducer.partners()[2:] if reduces else []))
        if reduces:
            for chunk in range(4):
                reducer.start(chunk)
            for z_sum, _ in z_sums:
                z_sum.start()
        every[own_rows] = yq_ref[...]
        for copy in gathers():
            copy.start()
        for direction in range(2):

            @pl.when(jnp.logical_not(gets_from[direction]))
            def _(direction=direction):
                halo_recv[direction] = jnp.zeros_like(halo_recv[direction])

    if reduces:
        for now in range(1, 2 * pairs):
            if any(at == now for at, _, _ in EARLY_PLAN):

                @pl.when(number == now)
                def _(now=now):
                    run_plan(now)

    @pl.when(number < pairs)
    def _():
        long_bias = key_bias(seq_index * block, block, len_ref[0])
        near_bias = key_bias(seq_index * quarter, quarter, count)
        query = q_ref[block:] * jnp.asarray(scale, BF16)
        grad_o = dog_ref[...]
        far_k, far_v = kx_ref[own_keys], vx_ref[own_keys]
        near_k, near_v = kg_ref[own_rows], vg_ref[own_rows]
        outs, kept = [], []
        for head in range(2):
            norm = in_three(-pick_column(ldg_ref[...], 2 * pair + head))
            delta = in_three(-pick_column(ldg_ref[...], HD + 2 * pair + head))
            qa = with_lanes(head, query, (1.0,) + norm)
            doa = with_lanes(head, grad_o, delta)
            far = jnp.exp(dot_t(qa, key_side(head, far_k, long_bias)))
            near = jnp.exp(dot_t(qa, key_side(head, near_k, near_bias)))
            far_ds = (far * dot_t(doa, value_side(head, far_v))).astype(BF16)
            near_ds = (near * dot_t(doa, value_side(head, near_v))).astype(BF16)
            outs.append(dot_n(far_ds, far_k) + dot_n(near_ds, near_k))
            kept.append(
                (
                    own_half(head, query),
                    own_half(head, grad_o),
                    far.astype(BF16),
                    near.astype(BF16),
                    far_ds,
                    near_ds,
                )
            )
        own_q, own_do, far, near, far_ds, near_ds = (
            jnp.concatenate(part, 0) for part in zip(*kept)
        )
        for total, edge in ((dkx, own_keys), (dvx, own_keys)):
            total[pair, :HALO] = jnp.zeros((HALO, PAIR), F32)
            total[pair, HALO + block :] = jnp.zeros((HALO, PAIR), F32)
        dkx[pair, own_keys] = t_dot(far_ds, own_q)
        dvx[pair, own_keys] = t_dot(far, own_do)
        dkg[pair] = jnp.zeros((GP, PAIR), F32)
        dvg[pair] = jnp.zeros((GP, PAIR), F32)
        dkg[pair, own_rows] = t_dot(near_ds, own_q)
        dvg[pair, own_rows] = t_dot(near, own_do)
        glob_dq = (jnp.where(low_lanes, outs[0], outs[1]) * scale).astype(BF16)
        q_send[:, pair] = glob_dq.reshape(seq_count, quarter, PAIR)
        for copy in glob_copies(0, pair):
            copy.start()

    @pl.when(number >= pairs)
    def _():
        long_bias = key_bias(seq_index * block - HALO, block + 2 * HALO, len_ref[0])
        glob_bias = key_bias(0, GP, count)
        query = q_ref[:block] * jnp.asarray(scale, BF16)
        grad_o = do_ref[...]
        both = grad_o.astype(F32) * o_ref[...].astype(F32)
        heads = []
        for head in range(2):
            norm = in_three(-pick_column(l_ref[...], 2 * pair + head))
            delta = in_three(-jnp.sum(own_half(head, both), -1, keepdims=True))
            heads.append(
                dict(
                    q=own_half(head, query),
                    do=own_half(head, grad_o),
                    qa=with_lanes(head, query, (1.0,) + norm),
                    doa=with_lanes(head, grad_o, delta),
                    kxa=key_side(head, kx_ref[...], long_bias),
                    vxa=value_side(head, vx_ref[...]),
                    kga=key_side(head, kg_ref[...], glob_bias),
                    vga=value_side(head, vg_ref[...]),
                    bias=band_bias(tab_ref[0, head : head + 1]),
                )
            )
        table_sums = [0.0, 0.0]
        grads_q = []
        for start in range(0, block, SUB):
            rows, keys = slice(start, start + SUB), slice(start, start + WINDOW)
            outs, probs, grads = [], [], []
            for head, own in enumerate(heads):
                band = jnp.exp(dot_t(own["qa"][rows], own["kxa"][keys]) + own["bias"])
                band_ds = band * dot_t(own["doa"][rows], own["vxa"][keys])
                table_sums[head] += band_ds
                glob = jnp.exp(dot_t(own["qa"][rows], own["kga"]))
                glob_ds = (glob * dot_t(own["doa"][rows], own["vga"])).astype(BF16)
                band_ds = band_ds.astype(BF16)
                outs.append(dot_n(band_ds, kx_ref[keys]) + dot_n(glob_ds, kg_ref[...]))
                probs.append((band.astype(BF16), glob.astype(BF16)))
                grads.append((band_ds, glob_ds))
            grads_q.append(jnp.where(low_lanes, outs[0], outs[1]))
            own_q = jnp.concatenate([own["q"][rows] for own in heads], 0)
            own_do = jnp.concatenate([own["do"][rows] for own in heads], 0)
            band, glob = (jnp.concatenate(part, 0) for part in zip(*probs))
            band_ds, glob_ds = (jnp.concatenate(part, 0) for part in zip(*grads))
            dkx[pair, keys] += t_dot(band_ds, own_q)
            dvx[pair, keys] += t_dot(band, own_do)
            dkg[pair] += t_dot(glob_ds, own_q)
            dvg[pair] += t_dot(glob, own_do)
        for kind, total in enumerate((dkg, dvg)):
            kv_send[:, pair, :, kind * PAIR : (kind + 1) * PAIR] = (
                total[pair].astype(BF16).reshape(seq_count, quarter, PAIR)
            )
        for copy in glob_copies(1, pair):
            copy.start()
        for kind, total in enumerate((dkx, dvx)):
            for direction, first in enumerate((HALO - REACH, HALO + block)):
                halo_send[direction, pair, kind] = total[pair, first : first + REACH].astype(BF16)
        for direction in range(2):

            @pl.when(sends_to[direction])
            def _(direction=direction):
                halo_copy(direction, pair).start()

        dq_ref[:block, lanes_of(pair)] = (jnp.concatenate(grads_q, 0) * scale).astype(BF16)
        for head in range(2):
            dtab_ref[pair, head : head + 1] = diagonal_sums(table_sums[head])

    @pl.when(number > pairs)
    def _():
        close_pair(pair - 1)

    @pl.when(number == 2 * pairs - 1)
    def _():
        if reduces:
            run_plan(2 * pairs)
        close_pair(pairs - 1)
        for at in range(pairs):
            for kind in range(2):
                for copy in glob_copies(kind, at):
                    copy.wait_send()
            for direction in range(2):

                @pl.when(sends_to[direction])
                def _(direction=direction, at=at):
                    halo_copy(direction, at).wait_send()

        for copy in gathers():
            copy.wait_recv()
        glob_out[...] = every[:count]
        for copy in gathers():
            copy.wait_send()
        if reduces:
            reducer.finish()
            for z_sum, out in z_sums:
                z_sum.finish(out)


def attend_back(sizes, doc_len, table, q, kx, vx, kg, vg, o, do, l, dog, ldg, yq, *sums):
    block, count, quarter, seq_count, pairs = sizes
    width = q.shape[1]
    early_rows = sums[0].shape[-2] if sums else 0
    ext = block + 2 * HALO
    cols = lambda rows: pl.BlockSpec((rows, PAIR), lambda i: (0, lax.rem(i, pairs)))
    whole = pl.BlockSpec(memory_space=pltpu.VMEM)
    shape = jax.ShapeDtypeStruct
    in_specs = [
        pl.BlockSpec(memory_space=pltpu.SMEM),
        pl.BlockSpec((1, 2, WINDOW), lambda i: (lax.rem(i, pairs), 0, 0)),
        cols(block + GP),
        cols(ext),
        cols(ext),
        cols(GP),
        cols(GP),
        cols(block),
        cols(block),
        whole,
        cols(GP),
        whole,
        whole,
    ]
    rows = block + quarter
    outs = [shape((rows, width), BF16)] * 3 + [shape((pairs, 2, WINDOW), F32)]
    outs.append(shape((count, width), BF16))
    others = seq_count - 1
    scratch = [
        pltpu.VMEM((pairs, ext, PAIR), F32),
        pltpu.VMEM((pairs, ext, PAIR), F32),
        pltpu.VMEM((pairs, GP, PAIR), F32),
        pltpu.VMEM((pairs, GP, PAIR), F32),
        pltpu.VMEM((seq_count, pairs, quarter, PAIR), BF16),
        pltpu.VMEM((others, pairs, quarter, PAIR), BF16),
        pltpu.VMEM((seq_count, pairs, quarter, 2 * PAIR), BF16),
        pltpu.VMEM((others, pairs, quarter, 2 * PAIR), BF16),
        pltpu.VMEM((2, pairs, 2, REACH, PAIR), BF16),
        pltpu.VMEM((2, pairs, 2, REACH, PAIR), BF16),
        pltpu.SemaphoreType.DMA((2, others, pairs)),
        pltpu.SemaphoreType.DMA((2, others, pairs)),
        pltpu.SemaphoreType.DMA((2, pairs)),
        pltpu.SemaphoreType.DMA((2, pairs)),
        pltpu.VMEM((GP, width), BF16),
        pltpu.SemaphoreType.DMA((others,)),
        pltpu.SemaphoreType.DMA((others,)),
    ]
    args = [doc_len, table, q, kx, vx, kg, vg, o, do, l, dog, ldg, yq, *sums]
    if early_rows:
        in_specs += [pl.BlockSpec(memory_space=pl.ANY)] * 3
        outs.append(shape((4, early_rows, width), BF16))
        scratch += Reducer.scratch(early_rows, width, 1)
        for parts in sums[1:]:
            outs.append(shape(parts.shape[1:], F32))
            scratch += ZSum.scratch(*parts.shape[1:])
    return pl.pallas_call(
        functools.partial(back_kernel, sizes, early_rows),
        grid=(2 * pairs,),
        in_specs=in_specs,
        out_specs=[whole] * len(outs),
        out_shape=outs,
        scratch_shapes=scratch,
        compiler_params=pltpu.CompilerParams(
            collective_id=1, has_side_effects=True, vmem_limit_bytes=60 * 2**20
        ),
        name="attend_back",
    )(*args)


def on_device(
    long_input,
    global_input,
    lengths,
    w_query,
    b_query,
    w_key,
    w_value,
    b_value,
    w_out,
    b_out,
    w_inner,
    b_inner,
    w_outer,
    b_outer,
    norm1_gain,
    norm1_shift,
    norm2_gain,
    norm2_shift,
    rel_table,
    long_cotangent,
    global_cotangent,
):
    seq_count = lax.axis_size("seq")
    data_count = lax.axis_size("dp")
    seq_index = lax.axis_index("seq")
    block = long_input.shape[1]
    count = global_input.shape[1]
    width = long_input.shape[2]
    heads = rel_table.shape[1]
    pairs = heads // 2
    labels = 2 * R + 1
    quarter = GP // seq_count
    sizes = Sizes(block, count, quarter, seq_count, pairs)
    queries, kx, vx, kg, vg, attn_low, long_l, glob_l, glob_x, table = attend(
        sizes,
        lengths,
        rel_table,
        long_input[0],
        global_input[0],
        w_query,
        w_key,
        w_value,
        b_query,
        b_value,
        norm1_gain,
        norm1_shift,
    )
    planned = has_plan()
    long_result, own_out, grad_mid, grad_attn, every_do, every_ld, *gradients = feed_forward(
        sizes,
        planned,
        lengths,
        attn_low,
        long_input[0],
        glob_x,
        long_cotangent[0],
        global_cotangent[0],
        glob_l,
        w_out,
        b_out,
        norm2_gain,
        norm2_shift,
        w_inner,
        b_inner,
        w_outer,
        b_outer,
    )
    query_low, key_low, value_low, dtab, glob_out, *early = attend_back(
        sizes,
        lengths,
        table,
        queries,
        kx,
        vx,
        kg,
        vg,
        attn_low,
        grad_attn,
        long_l,
        every_do,
        every_ld,
        own_out,
        *(gradients if planned else []),
    )
    long_grad, glob_grad, *late = last_part(
        sizes,
        planned,
        long_input[0],
        glob_x,
        query_low,
        key_low,
        value_low,
        grad_mid,
        w_query,
        w_key,
        w_value,
        norm1_gain,
        norm1_shift,
        dtab,
        *early[:1],
    )
    if planned:
        (
            g_query,
            g_key,
            g_value,
            g_out,
            g_inner,
            g_outer,
            g_b_query,
            g_b_value,
            g_b_out,
            g_b_outer,
            g_g1,
            g_s1,
            g_g2,
            g_s2,
            g_b_inner,
            table_total,
            long_grad,
            long_result,
        ) = small_results(
            heads, late[2], late[0], early[1], early[2], late[1], long_grad, long_result
        )
    else:
        devices = data_count * seq_count
        own_part = lambda vector: lax.dynamic_slice_in_dim(
            vector,
            (lax.axis_index("dp") * seq_count + seq_index) * (vector.shape[0] // devices),
            vector.shape[0] // devices,
        )
        g_outer, g_inner, g_out, vectors = gradients
        g_outer, g_inner, g_out, g_query, g_key, g_value = (
            lax.psum_scatter(g.astype(BF16), ("dp", "seq"), scatter_dimension=0, tiled=True).astype(
                F32
            )
            for g in (g_outer, g_inner, g_out, *late[:3])
        )
        vectors, sums = lax.psum((vectors, late[3]), ("dp", "seq"))
        g_b_query, g_b_value, g_g1, g_s1 = (own_part(sums[heads + i]) for i in range(4))
        g_b_out, g_b_outer, g_g2, g_s2 = (own_part(vectors[i]) for i in range(4))
        g_b_inner = own_part(vectors[4:].reshape(-1))
        table_total = sums[:heads, HALO - R : HALO - R + labels].T
    return (
        long_result[None],
        glob_out[None],
        long_grad[None],
        glob_grad[None],
        g_query,
        g_b_query,
        g_key,
        g_value,
        g_b_value,
        g_out,
        g_b_out,
        g_inner,
        g_b_inner,
        g_outer,
        g_b_outer,
        g_g1,
        g_s1,
        g_g2,
        g_s2,
        table_total,
    )


def solution(mesh):
    rows, whole = P("dp", "seq", None), P("dp", None, None)
    matrix, vector = P(("dp", "seq"), None), P(("dp", "seq"))
    return jax.shard_map(
        on_device,
        mesh=mesh,
        in_specs=(rows, whole, P("dp")) + (P(),) * 16 + (rows, whole),
        out_specs=(
            rows,
            whole,
            rows,
            whole,
            matrix,
            vector,
            matrix,
            matrix,
            vector,
            matrix,
            vector,
            matrix,
            vector,
            matrix,
            vector,
            vector,
            vector,
            vector,
            vector,
            P(),
        ),
        check_vma=False,
    )
```

```python
import functools
from typing import NamedTuple

import jax
import jax.numpy as jnp
from jax import lax
from jax.experimental import pallas as pl
from jax.experimental.pallas import tpu as pltpu
from jax.sharding import PartitionSpec as P

HD = 64
R = 84
PAIR = 2 * HD
HALO = 128
REACH = 96
GP = 256
SUB = 256
WINDOW = SUB + 2 * HALO
EPSILON = 1e-05
MASKED = -1e30
F32 = jnp.float32
BF16 = jnp.bfloat16


def dot_t(left, right):
    return lax.dot_general(left, right, (((1,), (1,)), ((), ())), preferred_element_type=F32)


def dot_n(left, right):
    return lax.dot_general(left, right, (((1,), (0,)), ((), ())), preferred_element_type=F32)


def t_dot(left, right):
    return lax.dot_general(left, right, (((0,), (0,)), ((), ())), preferred_element_type=F32)


def band_bias(table_row):
    spread = jnp.broadcast_to(table_row, (SUB, WINDOW))
    return pltpu.roll(spread, 0, 1, stride=1, stride_axis=0)


def diagonal_sums(rows):
    height, width = rows.shape
    while height > 8:
        height //= 2
        rows = rows[:height] + pltpu.roll(rows[height:], width - height, 1)
    row = lax.broadcasted_iota(jnp.int32, rows.shape, 0)
    for bit in (1, 2, 4):
        rows = jnp.where((row & bit) != 0, pltpu.roll(rows, width - bit, 1), rows)
    return jnp.sum(rows, 0, keepdims=True)


def lane_index():
    return lax.broadcasted_iota(jnp.int32, (1, PAIR), 1)


def own_half(head, value):
    low_lanes = lane_index() < HD
    return jnp.where(low_lanes if head == 0 else ~low_lanes, value, jnp.zeros_like(value))


def other_lane(head):
    return HD * (1 - head)


def with_lanes(head, value, columns):
    wide = own_half(head, value.astype(F32))
    lane = lane_index()
    for offset, column in enumerate(columns):
        wide = jnp.where(lane == other_lane(head) + offset, column, wide)
    return wide.astype(BF16)


def in_three(column):
    high = column.astype(BF16).astype(F32)
    middle = (column - high).astype(BF16).astype(F32)
    return (high, middle, column - high - middle)


def key_bias(first, rows, end):
    position = first + lax.broadcasted_iota(jnp.int32, (rows, 1), 0)
    return jnp.where((position >= 0) & (position < end), 0.0, MASKED)


def pick_column(rows, index):
    return jnp.sum(jnp.where(lane_index() == index, rows, 0.0), -1, keepdims=True)


def key_side(head, keys, bias):
    return with_lanes(head, keys, (bias, 1.0, 1.0, 1.0))


def value_side(head, values):
    return with_lanes(head, values, (1.0, 1.0, 1.0))


def softmax_rows(parts, value_parts, head):
    top = functools.reduce(
        jnp.maximum, [jnp.max(part, -1, keepdims=True) for part in parts]
    )
    mixed = sum(
        dot_n(jnp.exp(part - top).astype(BF16), values)
        for part, values in zip(parts, value_parts)
    )
    at = other_lane(head)
    total = mixed[:, at : at + 1]
    return mixed / total, top + jnp.log(total)


def seq_device(steps, seq_count):
    return (lax.axis_index("dp"), lax.rem(lax.axis_index("seq") + steps + seq_count, seq_count))


def row_norm(rows):
    centred = rows - jnp.mean(rows, -1, keepdims=True)
    inverse = lax.rsqrt(jnp.mean(centred * centred, -1, keepdims=True) + EPSILON)
    return centred * inverse, inverse


def put_column(ref, rows, index, column):
    ref[rows] = jnp.where(lane_index() == index, column, ref[rows])


def lanes_of(at):
    return pl.ds(pl.multiple_of(at * PAIR, PAIR), PAIR)


class Sizes(NamedTuple):
    block: int
    count: int
    quarter: int
    seq_count: int
    pairs: int


def attend_kernel(
    sizes,
    len_ref,
    rel_ref,
    long_ref,
    raw_ref,
    wq_ref,
    wk_ref,
    wv_ref,
    bq_ref,
    bv_ref,
    gain_ref,
    shift_ref,
    q_ref,
    kx_ref,
    vx_ref,
    kg_ref,
    vg_ref,
    o_ref,
    l_ref,
    lq_ref,
    glob_ref,
    tab_ref,
    spread,
    wide,
    part_o,
    part_l,
    from_o,
    from_l,
    halo_sends,
    halo_recvs,
    part_sends,
    part_recvs,
):
    block, count, quarter, seq_count, pairs = sizes
    ext = block + 2 * HALO
    seq_index = lax.axis_index("seq")
    scale = jnp.asarray(HD ** (-0.5), BF16)
    low_lanes = lane_index() < HD
    own_keys = slice(HALO, HALO + block)
    own_rows = pl.ds(pl.multiple_of(seq_index * quarter, quarter), quarter)
    neighbours = (seq_index > 0, seq_index < seq_count - 1)
    barrier = pltpu.get_barrier_semaphore()
    for step in range(1, seq_count):
        pl.semaphore_signal(
            barrier,
            inc=1,
            device_id=seq_device(step, seq_count),
            device_id_type=pl.DeviceIdType.MESH,
        )

    def halo_copies(direction):
        source = HALO if direction == 0 else HALO + block - REACH
        dest = HALO + block if direction == 0 else HALO - REACH
        for kind, ref in enumerate((kx_ref, vx_ref)):
            yield pltpu.make_async_remote_copy(
                src_ref=ref.at[source : source + REACH],
                dst_ref=ref.at[dest : dest + REACH],
                send_sem=halo_sends.at[direction, kind],
                recv_sem=halo_recvs.at[direction, kind],
                device_id=seq_device(2 * direction - 1, seq_count),
                device_id_type=pl.DeviceIdType.MESH,
            )

    def part_copies():
        for step in range(1, seq_count):
            device = seq_device(step, seq_count)
            rows = pl.ds(pl.multiple_of(device[1] * quarter, quarter), quarter)
            for kind, (source, dest) in enumerate(((part_o, from_o), (part_l, from_l))):
                yield step, kind, pltpu.make_async_remote_copy(
                    src_ref=source.at[rows],
                    dst_ref=dest.at[step - 1],
                    send_sem=part_sends.at[kind, step - 1],
                    recv_sem=part_recvs.at[kind, step - 1],
                    device_id=device,
                    device_id_type=pl.DeviceIdType.MESH,
                )

    gain, shift = gain_ref[...], shift_ref[...]
    labels, heads = rel_ref.shape
    spread[...] = jnp.full(spread.shape, MASKED, F32)
    spread[:labels, :heads] = rel_ref[...]
    turned = pltpu.roll(spread[...].T, HALO - R, 1)
    for pair in range(pairs):
        tab_ref[pair] = turned[2 * pair : 2 * pair + 2]
    normed_long = (row_norm(long_ref[...].astype(F32))[0] * gain + shift).astype(BF16)
    kx_ref[own_keys] = dot_n(normed_long, wk_ref[...]).astype(BF16)
    vx_ref[own_keys] = (dot_n(normed_long, wv_ref[...]) + bv_ref[...]).astype(BF16)
    pl.semaphore_wait(barrier, seq_count - 1)
    for direction, first in enumerate((HALO - REACH, HALO + block)):

        @pl.when(neighbours[direction])
        def _(direction=direction):
            for copy in halo_copies(direction):
                copy.start()

        outer = slice(0, first) if direction == 0 else slice(first + REACH, ext)
        for ref in (kx_ref, vx_ref):
            ref[outer] = jnp.zeros((HALO - REACH, ref.shape[1]), BF16)

        @pl.when(jnp.logical_not(neighbours[direction]))
        def _(first=first):
            for ref in (kx_ref, vx_ref):
                ref[first : first + REACH] = jnp.zeros((REACH, ref.shape[1]), BF16)

    wide[...] = jnp.zeros_like(wide)
    wide[:count] = raw_ref[...].astype(F32)
    glob_ref[...] = wide[...].astype(BF16)
    normed_glob = (row_norm(wide[...])[0] * gain + shift).astype(BF16)
    kg_ref[...] = dot_n(normed_glob, wk_ref[...]).astype(BF16)
    vg_ref[...] = (dot_n(normed_glob, wv_ref[...]) + bv_ref[...]).astype(BF16)
    q_ref[block:] = (dot_n(normed_glob, wq_ref[...]) + bq_ref[...]).astype(BF16)
    q_ref[:block] = (dot_n(normed_long, wq_ref[...]) + bq_ref[...]).astype(BF16)
    part_l[...] = jnp.zeros_like(part_l)
    l_ref[...] = jnp.zeros_like(l_ref)

    def glob_pair(pair, carry):
        lanes = lanes_of(pair)
        far_bias = key_bias(seq_index * block, block, len_ref[0])
        near_bias = key_bias(seq_index * quarter, quarter, count)
        query = q_ref[block:, lanes] * scale
        outs = []
        for head in range(2):
            q = with_lanes(head, query, (1.0,))
            far = dot_t(q, with_lanes(head, kx_ref[own_keys, lanes], (far_bias,)))
            near = dot_t(q, with_lanes(head, kg_ref[own_rows, lanes], (near_bias,)))
            out, norm = softmax_rows(
                [far, near],
                [
                    with_lanes(head, vx_ref[own_keys, lanes], (1.0,)),
                    with_lanes(head, vg_ref[own_rows, lanes], (1.0,)),
                ],
                head,
            )
            outs.append(out)
            put_column(part_l, slice(None), 2 * pair + head, norm)
        part_o[:, lanes] = jnp.where(low_lanes, outs[0], outs[1]).astype(BF16)
        return carry

    lax.fori_loop(0, pairs, glob_pair, 0)
    for _, _, copy in part_copies():
        copy.start()
    for direction in range(2):

        @pl.when(neighbours[1 - direction])
        def _(direction=direction):
            for copy in halo_copies(direction):
                copy.wait_recv()

    def long_pair(pair, carry):
        lanes = lanes_of(pair)
        long_bias = key_bias(seq_index * block - HALO, ext, len_ref[0])
        glob_bias = key_bias(0, GP, count)
        query = q_ref[:block, lanes] * scale
        outs = []
        for head in range(2):
            q = with_lanes(head, query, (1.0,))
            kx = with_lanes(head, kx_ref[:, lanes], (long_bias,))
            kg = with_lanes(head, kg_ref[:, lanes], (glob_bias,))
            vx, vg = (with_lanes(head, ref[:, lanes], (1.0,)) for ref in (vx_ref, vg_ref))
            bias = band_bias(tab_ref[pair, head : head + 1])
            mixed = []
            for start in range(0, block, SUB):
                rows, keys = slice(start, start + SUB), slice(start, start + WINDOW)
                out, norm = softmax_rows(
                    [dot_t(q[rows], kx[keys]) + bias, dot_t(q[rows], kg)], [vx[keys], vg], head
                )
                mixed.append(out)
                put_column(l_ref, rows, 2 * pair + head, norm)
            outs.append(jnp.concatenate(mixed, 0))
        o_ref[:block, lanes] = jnp.where(low_lanes, outs[0], outs[1]).astype(BF16)
        return carry

    lax.fori_loop(0, pairs, long_pair, 0)
    for _, _, copy in part_copies():
        copy.wait_recv()
    norms = [part_l[own_rows]] + [from_l[step] for step in range(seq_count - 1)]
    outs = [part_o[own_rows]] + [from_o[step] for step in range(seq_count - 1)]
    top = functools.reduce(jnp.maximum, norms)
    shares = [jnp.exp(norm - top) for norm in norms]
    total = sum(shares)
    lq_ref[...] = top + jnp.log(total)
    shares = [share / total for share in shares]
    for at in range(pairs):
        lanes = slice(at * PAIR, (at + 1) * PAIR)
        mixed = 0.0
        for share, out in zip(shares, outs):
            spread = jnp.where(
                low_lanes, share[:, 2 * at : 2 * at + 1], share[:, 2 * at + 1 : 2 * at + 2]
            )
            mixed += spread * out[:, lanes].astype(F32)
        o_ref[block:, lanes] = mixed.astype(BF16)
    for _, _, copy in part_copies():
        copy.wait_send()
    for direction in range(2):

        @pl.when(neighbours[direction])
        def _(direction=direction):
            for copy in halo_copies(direction):
                copy.wait_send()


def attend(sizes, doc_len, rel_table, long_x, glob_x, *weights):
    block, count, quarter, seq_count, pairs = sizes
    width = long_x.shape[1]
    ext = block + 2 * HALO
    whole = pl.BlockSpec(memory_space=pltpu.VMEM)
    shape = jax.ShapeDtypeStruct
    others = seq_count - 1
    return pl.pallas_call(
        functools.partial(attend_kernel, sizes),
        in_specs=[pl.BlockSpec(memory_space=pltpu.SMEM)] + [whole] * 10,
        out_specs=[whole] * 10,
        out_shape=[
            shape((block + GP, width), BF16),
            shape((ext, width), BF16),
            shape((ext, width), BF16),
            shape((GP, width), BF16),
            shape((GP, width), BF16),
            shape((block + quarter, width), BF16),
            shape((block, PAIR), F32),
            shape((quarter, PAIR), F32),
            shape((GP, width), BF16),
            shape((pairs, 2, WINDOW), F32),
        ],
        scratch_shapes=[
            pltpu.VMEM((WINDOW, PAIR), F32),
            pltpu.VMEM((GP, width), F32),
            pltpu.VMEM((GP, width), BF16),
            pltpu.VMEM((GP, PAIR), F32),
            pltpu.VMEM((others, quarter, width), BF16),
            pltpu.VMEM((others, quarter, PAIR), F32),
            pltpu.SemaphoreType.DMA((2, 2)),
            pltpu.SemaphoreType.DMA((2, 2)),
            pltpu.SemaphoreType.DMA((2, others)),
            pltpu.SemaphoreType.DMA((2, others)),
        ],
        compiler_params=pltpu.CompilerParams(
            collective_id=3, has_side_effects=True, vmem_limit_bytes=56 * 2**20
        ),
        name="attend",
    )(doc_len, rel_table, long_x, glob_x, *weights)


class Reducer:
    def __init__(self, rows, split, scratch, pieces=None, order=None, parts=None):
        self.ids = mesh_ids()
        self.parts = parts
        self.order = order
        self.halves = (slice(0, split), slice(split, rows))
        held, self.from_core, self.from_one, self.from_two = scratch[:4]
        self.local, self.sends, self.recvs = scratch[4:7]
        if parts is None:
            self.from_z, self.z_sends, self.z_recvs = scratch[7:]
        self.pieces, self.held = pieces, held
        self.mine = held.at[self.ids[3]] if pieces is None else held.at[0]

    @staticmethod
    def scratch(rows, width, sides, with_z=False):
        buffers = [
            pltpu.VMEM((sides, 4, 2, 2, rows, width), BF16),
            pltpu.VMEM((4, 2, 2, rows, width), BF16),
            pltpu.VMEM((4, 2, rows, width), BF16),
            pltpu.VMEM((4, rows, width), BF16),
            pltpu.SemaphoreType.DMA((4,)),
            pltpu.SemaphoreType.DMA((5, 4)),
            pltpu.SemaphoreType.DMA((5, 4)),
        ]
        if with_z:
            buffers += [
                pltpu.VMEM((3, rows, width), BF16),
                pltpu.SemaphoreType.DMA((4,)),
                pltpu.SemaphoreType.DMA((3,)),
            ]
        return buffers

    def partners(self):
        z, y, x, core = self.ids
        dp, seq = z * 2 + y, x * 2 + core
        near = [(dp, x * 2 + 1 - core), (dp, (1 - x) * 2 + core), (z * 2 + 1 - y, seq)]
        return near + [(lax.rem(z + step, 4) * 2 + y, seq) for step in (1, 2, 3)]

    def target(self, chunk):
        return self.order(chunk) if self.order else lax.rem(self.ids[0] + 1 + chunk, 4)

    def remote(self, source, dest, kind, send_at, recv_at, device):
        return pltpu.make_async_remote_copy(
            src_ref=source,
            dst_ref=dest,
            send_sem=self.sends.at[kind, send_at],
            recv_sem=self.recvs.at[kind, recv_at],
            device_id=device,
            device_id_type=pl.DeviceIdType.MESH,
        )

    def own_copy(self, chunk):
        core, to = self.ids[3], self.target(chunk)
        return pltpu.make_async_copy(
            self.pieces.at[core, to], self.mine.at[to], self.local.at[chunk]
        )

    def core_copy(self, chunk):
        core, to = self.ids[3], self.target(chunk)
        source = (self.held if self.pieces is None else self.pieces).at[1 - core, to]
        return self.remote(source, self.from_core.at[to], 0, chunk, chunk, self.partners()[0])

    def first_copies(self, chunk):
        z, y, x, core = self.ids
        to = self.target(chunk)
        one, two = self.halves
        near = self.partners()
        return (
            self.remote(
                self.mine.at[to, :, 1 - x, one],
                self.from_one.at[to, :, one],
                1,
                chunk,
                chunk,
                near[1],
            ),
            self.remote(
                self.mine.at[to, 1 - y, :, two],
                self.from_one.at[to, :, two],
                2,
                chunk,
                chunk,
                near[2],
            ),
        )

    def second_copies(self, chunk):
        z, y, x, core = self.ids
        to = self.target(chunk)
        one, two = self.halves
        near = self.partners()
        return (
            self.remote(
                self.mine.at[to, 1 - y, x, one],
                self.from_two.at[to, one],
                3,
                chunk,
                chunk,
                near[2],
            ),
            self.remote(
                self.mine.at[to, y, 1 - x, two],
                self.from_two.at[to, two],
                4,
                chunk,
                chunk,
                near[1],
            ),
        )

    def last_copy(self, chunk):
        z, y, x, core = self.ids
        to = self.target(chunk)
        slot = lax.rem(z - to + 4, 4) - 1
        return pltpu.make_async_remote_copy(
            src_ref=self.mine.at[to, y, x],
            dst_ref=self.from_z.at[slot],
            send_sem=self.z_sends.at[chunk],
            recv_sem=self.z_recvs.at[slot],
            device_id=(to * 2 + y, x * 2 + core),
            device_id_type=pl.DeviceIdType.MESH,
        )

    def arrival(self, slot):
        z, y, x, core = self.ids
        return pltpu.make_async_remote_copy(
            src_ref=self.mine.at[z, y, x],
            dst_ref=self.from_z.at[slot],
            send_sem=self.z_sends.at[slot],
            recv_sem=self.z_recvs.at[slot],
            device_id=self.partners()[3],
            device_id_type=pl.DeviceIdType.MESH,
        )

    def leaves(self, chunk):
        return self.target(chunk) != self.ids[0]

    def fill(self, to, at, value):
        self.held[at % 2, to, at // 4, at // 2 % 2] = value.astype(BF16)

    def start(self, chunk):
        self.core_copy(chunk).start()
        if self.pieces is not None:
            self.own_copy(chunk).start()

    def add_core(self, chunk):
        to = self.target(chunk)
        if self.pieces is not None:
            self.own_copy(chunk).wait()
        self.core_copy(chunk).wait_recv()

        def add(index, carry):
            at = (to, lax.div(index, 2), lax.rem(index, 2))
            self.mine[at] = self.mine[at] + self.from_core[at]
            return carry

        lax.fori_loop(0, 4, add, 0)
        for copy in self.first_copies(chunk):
            copy.start()

    def add_first(self, chunk):
        z, y, x, core = self.ids
        one, two = self.halves
        to = self.target(chunk)
        for copy in self.first_copies(chunk):
            copy.wait_recv()

        def add(index, carry):
            for at, rows in (((to, index, x), one), ((to, y, index), two)):
                self.mine[at + (rows,)] = self.mine[at + (rows,)] + self.from_one[to, index, rows]
            return carry

        lax.fori_loop(0, 2, add, 0)
        for copy in self.second_copies(chunk):
            copy.start()

    def add_second(self, chunk):
        z, y, x, core = self.ids
        to = self.target(chunk)
        for copy in self.second_copies(chunk):
            copy.wait_recv()
        if self.parts is not None:
            self.parts[to] = self.mine[to, y, x] + self.from_two[to]
            return

        @pl.when(self.leaves(chunk))
        def _():
            self.mine[to, y, x] = self.mine[to, y, x] + self.from_two[to]
            self.last_copy(chunk).start()

    def finish(self, out=None):
        z, y, x, core = self.ids
        if self.parts is None:
            total = self.mine[z, y, x].astype(F32) + self.from_two[z].astype(F32)
            for slot in range(3):
                self.arrival(slot).wait_recv()
                total += self.from_z[slot].astype(F32)
            out[...] = total
        for chunk in range(4):
            self.core_copy(chunk).wait_send()
            for copy in self.first_copies(chunk) + self.second_copies(chunk):
                copy.wait_send()
            if self.parts is None:

                @pl.when(self.leaves(chunk))
                def _(chunk=chunk):
                    self.last_copy(chunk).wait_send()


class ZSum:
    def __init__(self, parts, scratch):
        self.ids = mesh_ids()
        self.parts = parts
        self.own, self.from_z, self.local, self.sends, self.recvs = scratch

    @staticmethod
    def scratch(rows, width):
        return [
            pltpu.VMEM((rows, width), BF16),
            pltpu.VMEM((3, rows, width), BF16),
            pltpu.SemaphoreType.DMA,
            pltpu.SemaphoreType.DMA((3,)),
            pltpu.SemaphoreType.DMA((3,)),
        ]

    def own_copy(self):
        return pltpu.make_async_copy(self.parts.at[self.ids[0]], self.own, self.local)

    def copies(self):
        z, y, x, core = self.ids
        for slot in range(3):
            to = lax.rem(z + 3 - slot, 4)
            yield pltpu.make_async_remote_copy(
                src_ref=self.parts.at[to],
                dst_ref=self.from_z.at[slot],
                send_sem=self.sends.at[slot],
                recv_sem=self.recvs.at[slot],
                device_id=(to * 2 + y, x * 2 + core),
                device_id_type=pl.DeviceIdType.MESH,
            )

    def start(self):
        self.own_copy().start()
        for copy in self.copies():
            copy.start()

    def finish(self, out):
        self.own_copy().wait()
        total = self.own[...].astype(F32)
        for slot, copy in enumerate(self.copies()):
            copy.wait_recv()
            total += self.from_z[slot].astype(F32)
        out[...] = total
        for copy in self.copies():
            copy.wait_send()


class EverySum:
    def __init__(self, scratch):
        self.kept, self.arrived, self.from_z, self.sends, self.recvs = scratch
        z, y, x, core = mesh_ids()
        seq = x * 2 + core
        self.z = z
        self.pairs = (
            (z * 2 + y, x * 2 + 1 - core),
            (z * 2 + y, (1 - x) * 2 + core),
            (z * 2 + 1 - y, seq),
        )
        self.along_z = [(lax.rem(z + step, 4) * 2 + y, seq) for step in (1, 2, 3)]

    @staticmethod
    def scratch(rows, width):
        return [
            pltpu.VMEM((3, rows, width), F32),
            pltpu.VMEM((3, rows, width), F32),
            pltpu.VMEM((4, rows, width), F32),
            pltpu.SemaphoreType.DMA((6,)),
            pltpu.SemaphoreType.DMA((6,)),
        ]

    def copy(self, stage):
        return pltpu.make_async_remote_copy(
            src_ref=self.kept.at[stage],
            dst_ref=self.arrived.at[stage],
            send_sem=self.sends.at[stage],
            recv_sem=self.recvs.at[stage],
            device_id=self.pairs[stage],
            device_id_type=pl.DeviceIdType.MESH,
        )

    def z_copies(self):
        for at, device in enumerate(self.along_z):
            yield pltpu.make_async_remote_copy(
                src_ref=self.from_z.at[self.z],
                dst_ref=self.from_z.at[self.z],
                send_sem=self.sends.at[3 + at],
                recv_sem=self.recvs.at[3 + at],
                device_id=device,
                device_id_type=pl.DeviceIdType.MESH,
            )

    def step(self, stage):
        if stage > 0:
            self.copy(stage - 1).wait_recv()
            total = self.kept[stage - 1] + self.arrived[stage - 1]
            if stage < 3:
                self.kept[stage] = total
            else:
                self.from_z[self.z] = total
        if stage < 3:
            self.copy(stage).start()
        else:
            for copy in self.z_copies():
                copy.start()

    def finish(self, out):
        for copy in self.z_copies():
            copy.wait_recv()
        out[...] = (self.from_z[0] + self.from_z[1]) + (self.from_z[2] + self.from_z[3])
        for copy in [self.copy(stage) for stage in range(3)] + list(self.z_copies()):
            copy.wait_send()


def mesh_ids():
    dp, seq = lax.axis_index("dp"), lax.axis_index("seq")
    return lax.div(dp, 2), lax.rem(dp, 2), lax.div(seq, 2), lax.rem(seq, 2)


def meet(devices):
    barrier = pltpu.get_barrier_semaphore()
    for device in devices:
        pl.semaphore_signal(barrier, inc=1, device_id=device, device_id_type=pl.DeviceIdType.MESH)
    pl.semaphore_wait(barrier, len(devices))


EARLY_PLAN = (
    (2, "add_core", 0),
    (3, "add_core", 1),
    (4, "add_core", 2),
    (5, "add_core", 3),
    (7, "add_first", 0),
    (8, "add_first", 1),
    (9, "add_second", 0),
    (9, "add_first", 2),
    (10, "add_second", 1),
    (10, "add_first", 3),
    (11, "add_second", 2),
    (12, "add_second", 3),
)


def late_kernel(
    sizes,
    planned,
    long_ref,
    glob_ref,
    dq_ref,
    dk_ref,
    dv_ref,
    dmid_ref,
    wq_ref,
    wk_ref,
    wv_ref,
    gain_ref,
    shift_ref,
    table_ref,
    *rest,
):
    block, count, quarter, seq_count, pairs = sizes
    rows = block + quarter
    width = long_ref.shape[1]
    if planned:
        early_parts, long_out, glob_out, late_ref, total_ref, scale_ref, early_ref, *rest = rest
    else:
        long_out, glob_out, gq_ref, gk_ref, gv_ref, total_ref, scale_ref, *rest = rest
    normed_t, every, gather_sends, gather_recvs, *rest = rest
    seq_index = lax.axis_index("seq")
    own_rows = pl.ds(pl.multiple_of(seq_index * quarter, quarter), quarter)
    others = [seq_device(step, seq_count) for step in range(1, seq_count)]

    def gathers():
        for step, device in enumerate(others):
            yield pltpu.make_async_remote_copy(
                src_ref=every.at[own_rows],
                dst_ref=every.at[own_rows],
                send_sem=gather_sends.at[step],
                recv_sem=gather_recvs.at[step],
                device_id=device,
                device_id_type=pl.DeviceIdType.MESH,
            )

    if planned:
        first_sum, second_sum = EverySum(rest[:5]), EverySum(rest[5:10])
        z_sum = ZSum(early_parts, rest[10:15])
        reducer = Reducer(rest[15].shape[-2], 32, rest[15:])

    meet(others + (reducer.partners()[2:] if planned else []))
    heads = 2 * pairs
    first = first_sum.kept.at[0] if planned else total_ref
    first[...] = jnp.zeros(first.shape, F32)
    for pair in range(pairs):
        first[2 * pair : 2 * pair + 2, :WINDOW] = table_ref[pair]
    for at, ref in enumerate((dq_ref, dv_ref)):
        first[heads + at : heads + at + 1] = column_sum(ref[...].astype(F32))
    if planned:
        first_sum.step(0)
        z_sum.start()
    everything = jnp.concatenate([long_ref[...], glob_ref[own_rows]], 0).astype(F32)
    hat, inverse = row_norm(everything)
    normed_t[...] = (hat * gain_ref[...] + shift_ref[...]).astype(BF16).T
    if planned:
        piece = width // 32
        blank = jnp.zeros((8, width), F32)
        def weight_rows(chunk):
            to = reducer.target(chunk)
            some = normed_t[pl.ds(pl.multiple_of(to * 8 * piece, 64), 8 * piece)]
            parts = [dot_n(some, ref[...]) for ref in (dq_ref, dk_ref, dv_ref)]
            for at in range(8):
                rows_at = slice(at * piece, (at + 1) * piece)
                reducer.fill(
                    to, at, jnp.concatenate([part[rows_at] for part in parts] + [blank], 0)
                )
            reducer.start(chunk)

        weight_rows(0)
        first_sum.step(1)
        weight_rows(1)
        reducer.add_core(0)
        weight_rows(2)
        first_sum.step(2)
        reducer.add_core(1)
        weight_rows(3)
        grads = dot_t(dq_ref[...], wq_ref[...])
        first_sum.step(3)
        reducer.add_first(0)
        reducer.add_core(2)
        grads += dot_t(dk_ref[...], wk_ref[...]) + dot_t(dv_ref[...], wv_ref[...])
        reducer.add_first(1)
        reducer.add_core(3)
        reducer.add_second(0)
    else:
        for ref, out in ((dq_ref, gq_ref), (dk_ref, gk_ref), (dv_ref, gv_ref)):
            out[...] = dot_n(normed_t[...], ref[...]).astype(BF16)
        grads = (
            dot_t(dq_ref[...], wq_ref[...])
            + dot_t(dk_ref[...], wk_ref[...])
            + dot_t(dv_ref[...], wv_ref[...])
        )
    scaled = grads * gain_ref[...]
    total = dmid_ref[...] + inverse * (
        scaled
        - jnp.mean(scaled, -1, keepdims=True)
        - hat * jnp.mean(scaled * hat, -1, keepdims=True)
    )
    every[own_rows] = total[block:].astype(BF16)
    for copy in gathers():
        copy.start()
    long_out[...] = total[:block]
    second = second_sum.kept.at[0] if planned else scale_ref
    second[...] = jnp.zeros(second.shape, F32)
    second[0:1] = column_sum(grads * hat)
    second[1:2] = column_sum(grads)
    if planned:
        second_sum.step(0)
        first_sum.finish(total_ref)
        reducer.add_first(2)
        second_sum.step(1)
        reducer.add_second(1)
        reducer.add_first(3)
        reducer.add_second(2)
        second_sum.step(2)
        reducer.add_second(3)
        second_sum.step(3)
        z_sum.finish(early_ref)
        reducer.finish(late_ref)
        second_sum.finish(scale_ref)
    for copy in gathers():
        copy.wait_recv()
    glob_out[...] = every[:count].astype(F32)
    for copy in gathers():
        copy.wait_send()


def last_part(sizes, planned, long_x, glob_x, dq, dk, dv, dmid, *weights):
    block, count, quarter, seq_count, pairs = sizes
    rows, width = dq.shape
    others = seq_count - 1
    whole = pl.BlockSpec(memory_space=pltpu.VMEM)
    shape = jax.ShapeDtypeStruct
    sums = [shape(((2 * pairs + 2 + 7) // 8 * 8, width), F32), shape((8, width), F32)]
    outs = [shape((block, width), F32), shape((count, width), F32)]
    scratch = [
        pltpu.VMEM((width, rows), BF16),
        pltpu.VMEM((GP, width), BF16),
        pltpu.SemaphoreType.DMA((others,)),
        pltpu.SemaphoreType.DMA((others,)),
    ]
    if planned:
        piece = width // 32
        part = 3 * piece + 8
        early = weights[-1].shape[1:]
        outs += [shape((part, width), F32), *sums, shape(early, F32)]
        for part_sums in sums:
            scratch += EverySum.scratch(*part_sums.shape)
        scratch += ZSum.scratch(*early) + Reducer.scratch(part, width, 2, with_z=True)
    else:
        outs += [shape((width, width), BF16)] * 3 + sums
    return pl.pallas_call(
        functools.partial(late_kernel, sizes, planned),
        in_specs=[whole] * 12 + [pl.BlockSpec(memory_space=pl.ANY)] * planned,
        out_specs=[whole] * len(outs),
        out_shape=outs,
        scratch_shapes=scratch,
        compiler_params=pltpu.CompilerParams(
            collective_id=2, has_side_effects=True, vmem_limit_bytes=60 * 2**20
        ),
        name="last_part",
    )(long_x, glob_x, dq, dk, dv, dmid, *weights)


def small_kernel(heads, early_ref, late_ref, outer_ref, inner_ref, sums_ref, scale_ref, *outs):
    g_query, g_key, g_value, g_out, g_inner, g_outer, *vectors, table = outs
    device = lax.axis_index("dp") * lax.axis_size("seq") + lax.axis_index("seq")
    piece, width = g_query.shape
    for at, out in enumerate((g_query, g_key, g_value)):
        out[...] = late_ref[at * piece : (at + 1) * piece]
    g_out[...] = early_ref[2 * piece : 3 * piece]
    g_outer[...] = outer_ref[...]
    for source, first, chunk in (
        (inner_ref, 0, 0),
        (inner_ref, piece, 3),
        (early_ref, 0, 1),
        (early_ref, piece, 2),
    ):
        g_inner[:, chunk * width : (chunk + 1) * width] = source[first : first + piece]

    def entries(row, at, length):
        return pltpu.roll(row, width - at * length, 1)[0, :length]

    b_query, b_value, b_out, b_outer, gain_one, shift_one, gain_two, shift_two, b_inner = vectors
    for at, out in enumerate((b_query, b_value)):
        out[...] = entries(sums_ref[heads + at : heads + at + 1], device, piece)
    for at, out in enumerate((gain_one, shift_one)):
        out[...] = entries(scale_ref[at : at + 1], device, piece)
    for at, out in enumerate((b_out, b_outer, gain_two, shift_two)):
        row = 3 * piece + at
        out[...] = entries(early_ref[row : row + 1], device, piece)
    row = pl.ds(3 * piece + 4 + lax.div(device, 8), 1)
    b_inner[...] = entries(early_ref[row], lax.rem(device, 8), 4 * piece)
    labels = table.shape[0]
    turned = pltpu.roll(sums_ref[:, :WINDOW], WINDOW - HALO + R, 1).T
    table[...] = turned[:labels, :heads]


def small_results(heads, early, late, outer, inner, sums, scales):
    width = early.shape[1]
    piece = width // 32
    shape = jax.ShapeDtypeStruct
    whole = pl.BlockSpec(memory_space=pltpu.VMEM)
    outs = [shape((piece, width), F32)] * 4
    outs += [shape((piece, 4 * width), F32), shape((4 * piece, width), F32)]
    outs += [shape((piece,), F32)] * 8 + [shape((4 * piece,), F32)]
    outs += [shape((2 * R + 1, heads), F32)]
    return pl.pallas_call(
        functools.partial(small_kernel, heads),
        in_specs=[whole] * 6,
        out_specs=[whole] * len(outs),
        out_shape=outs,
        name="small_results",
    )(early, late, outer, inner, sums, scales)


def has_plan():
    return (lax.axis_size("dp"), lax.axis_size("seq")) == (8, 4)


GELU_A = 0.7978845608028654
GELU_B = 0.044715


def gate_both(u):
    square = u * u
    turned = jnp.tanh(GELU_A * u * (1.0 + GELU_B * square))
    half = 0.5 * (1.0 + turned)
    slope = half + 0.5 * u * (1.0 - turned * turned) * (
        GELU_A * (1.0 + 3.0 * GELU_B * square)
    )
    return u * half, slope


def column_sum(rows):
    return jnp.sum(rows, 0, keepdims=True)


def ffn_kernel(
    sizes,
    planned,
    len_ref,
    attn_ref,
    long_ref,
    glob_ref,
    dlong_ref,
    dglob_ref,
    lq_ref,
    wo_ref,
    bo_ref,
    gain_ref,
    shift_ref,
    wi_ref,
    bi_ref,
    wr_ref,
    br_ref,
    long_out,
    glob_out,
    dmid_ref,
    do_ref,
    dog_ref,
    ldg_ref,
    *rest,
):
    block, count, quarter, seq_count, pairs = sizes
    if planned:
        pieces_ref, outer_ref, inner_ref, *rest = rest
    else:
        g_outer_ref, g_inner_ref, g_out_ref, vec_ref, *rest = rest
    (
        mid,
        y_sum,
        df_sum,
        normed,
        normed_t,
        dy,
        vectors,
        biases,
        every_do,
        every_ld,
        gather_sends,
        gather_recvs,
        *rest,
    ) = rest
    if planned:
        even, *rest = rest
        outer = Reducer(rest[0].shape[-2], 48, rest[:7], order=chunk_of, parts=outer_ref)
        inner = Reducer(rest[7].shape[-2], 16, rest[7:], parts=inner_ref)
    step = pl.program_id(0)
    chunk = chunk_of(step)
    seq_index = lax.axis_index("seq")
    own_rows = pl.ds(pl.multiple_of(seq_index * quarter, quarter), quarter)
    width = mid.shape[1]
    piece = width // 32

    def rows_of(device):
        return pl.ds(pl.multiple_of(device[1] * quarter, quarter), quarter)

    def gather(owner, device, at):
        for kind, every in enumerate((every_do, every_ld)):
            yield pltpu.make_async_remote_copy(
                src_ref=every.at[rows_of(owner)],
                dst_ref=every.at[rows_of(owner)],
                send_sem=gather_sends.at[kind, at],
                recv_sem=gather_recvs.at[kind, at],
                device_id=device,
                device_id_type=pl.DeviceIdType.MESH,
            )

    me = seq_device(0, seq_count)
    if planned:
        sibling, across = outer.partners()[:2]
        first_gathers = [(me, across, 0), (me, sibling, 1)]
        second_gathers = [(across, sibling, 2)]
    else:
        first_gathers = [
            (me, seq_device(at + 1, seq_count), at) for at in range(seq_count - 1)
        ]
        second_gathers = []

    def act(now):
        if planned:
            for at, reducer, name, part in FFN_PLAN:
                if at == now:
                    getattr((outer, inner)[reducer], name)(part)

    def act_in_step(point):
        if planned:
            for now in range(4):
                if any(at == (now, point) for at, _, _, _ in FFN_PLAN):

                    @pl.when(step == now)
                    def _(now=now):
                        act((now, point))

    @pl.when(step == 0)
    def _():
        others = [seq_device(seq_step, seq_count) for seq_step in range(1, seq_count)]
        meet(others + (outer.partners()[2:] if planned else []))
        projected = dot_n(attn_ref[...], wo_ref[...]) + bo_ref[...]
        mid[:block] = long_ref[...].astype(F32) + projected[:block]
        mid[block:] = glob_ref[own_rows].astype(F32) + projected[block:]
        hat, _ = row_norm(mid[...])
        normed[...] = (hat * gain_ref[...] + shift_ref[...]).astype(BF16)
        normed_t[...] = normed[...].T
        position = seq_index * block + lax.broadcasted_iota(jnp.int32, (block, 1), 0)
        dy[:block] = jnp.where(
            position < len_ref[0], dlong_ref[...].astype(F32), 0.0
        ).astype(BF16)
        y_sum[:GP] = jnp.zeros((GP, width), F32)
        y_sum[:count] = dglob_ref[...].astype(F32)
        dy[block:] = y_sum[own_rows].astype(BF16)
        vectors[1:2] = column_sum(dy[...].astype(F32))
        y_sum[...] = mid[...] + br_ref[...]
        df_sum[...] = jnp.zeros_like(df_sum)
        for at in range(4):
            biases[at] = bi_ref[at * width : (at + 1) * width].reshape(1, width)

    act_in_step(0)
    active, slope = gate_both(dot_n(normed[...], wi_ref[...]) + biases[chunk])
    active = active.astype(BF16)
    g_outer = t_dot(active, dy[...])
    if planned:
        for at in range(8):
            outer.fill(chunk, at, g_outer[at * 4 * piece : (at + 1) * 4 * piece])
        outer.start(step)
    else:
        g_outer_ref[...] = g_outer.astype(BF16)
    y_sum[...] += dot_n(active, wr_ref[...])
    hidden = dot_t(dy[...], wr_ref[...]) * slope
    for at in range(4):

        @pl.when(chunk == at)
        def _(at=at):
            vectors[4 + at : 5 + at] = column_sum(hidden)

    hidden = hidden.astype(BF16)
    act_in_step(1)
    df_sum[...] += dot_t(hidden, wi_ref[...])
    g_inner = dot_n(normed_t[...], hidden)
    if planned:

        @pl.when(lax.rem(step, 2) == 0)
        def _():
            even[...] = g_inner

        def halves(at):
            part = slice(at * piece, (at + 1) * piece)
            return jnp.concatenate([even[part], g_inner[part]], 0)

        @pl.when(step == 1)
        def _():
            for at in range(32):
                inner.fill(at // 8, at % 8, halves(at))
            for part in range(4):
                inner.start(part)

        @pl.when(step == 3)
        def _():
            for at in range(32):
                pieces_ref[at % 2, at // 8, at // 4 % 2, at // 2 % 2, : 2 * piece] = halves(
                    at
                ).astype(BF16)

    else:
        g_inner_ref[...] = g_inner.astype(BF16)

    def norm_back(rows):
        hat, inverse = row_norm(mid[rows])
        df = df_sum[rows]
        scaled = df * gain_ref[...]
        dmid = dy[rows].astype(F32) + inverse * (
            scaled
            - jnp.mean(scaled, -1, keepdims=True)
            - hat * jnp.mean(scaled * hat, -1, keepdims=True)
        )
        dmid_ref[rows] = dmid
        low = dmid.astype(BF16)
        grad_o = dot_t(low, wo_ref[...]).astype(BF16)
        do_ref[rows] = grad_o
        return [column_sum(dmid), column_sum(df * hat), column_sum(df)], low, grad_o

    @pl.when(step == 3)
    def _():
        glob_sums, glob_low, grad_o = norm_back(slice(block, block + quarter))
        every_do[own_rows] = grad_o
        both = grad_o.astype(F32) * attn_ref[block:].astype(F32)
        stats = lq_ref[...]
        for head in range(2 * pairs):
            lanes = slice(head // 2 * PAIR, head // 2 * PAIR + PAIR)
            delta = jnp.sum(own_half(head % 2, both[:, lanes]), -1, keepdims=True)
            stats = jnp.where(lane_index() == HD + head, delta, stats)
        every_ld[own_rows] = stats
        for part in first_gathers:
            for copy in gather(*part):
                copy.start()
        glob_out[...] = y_sum[block:].astype(BF16)
        act((4, 0))
        position = seq_index * block + lax.broadcasted_iota(jnp.int32, (block, 1), 0)
        long_out[...] = jnp.where(position < len_ref[0], y_sum[:block], 0.0).astype(BF16)
        long_sums, long_low, _ = norm_back(slice(0, block))
        for at, one, two in zip((0, 2, 3), long_sums, glob_sums):
            vectors[at : at + 1] = one + two
        if planned:
            for copy in gather(*first_gathers[0]):
                copy.wait_recv()
            for copy in gather(*second_gathers[0]):
                copy.start()
        act((4, 1))
        g_out = t_dot(attn_ref[...], jnp.concatenate([long_low, glob_low], 0))
        if planned:
            for at in range(32):
                pieces_ref[at % 2, at // 8, at // 4 % 2, at // 2 % 2, 2 * piece :] = (
                    jnp.concatenate(
                        [g_out[at * piece : (at + 1) * piece], vectors[...]], 0
                    ).astype(BF16)
                )
            act((4, 2))
            outer.finish()
            inner.finish()
        else:
            g_out_ref[...] = g_out.astype(BF16)
            vec_ref[...] = vectors[...]
        for part in (first_gathers[1:] if planned else first_gathers) + second_gathers:
            for copy in gather(*part):
                copy.wait_recv()
        dog_ref[...] = every_do[...]
        ldg_ref[...] = every_ld[...]
        for part in first_gathers + second_gathers:
            for copy in gather(*part):
                copy.wait_send()


OUTER, INNER = 0, 1
FFN_PLAN = (
    ((1, 0), OUTER, "add_core", 0),
    ((2, 0), OUTER, "add_core", 1),
    ((2, 0), OUTER, "add_first", 0),
    ((2, 1), INNER, "add_core", 0),
    ((2, 1), INNER, "add_core", 1),
    ((2, 1), INNER, "add_core", 2),
    ((2, 1), INNER, "add_core", 3),
    ((3, 0), OUTER, "add_first", 1),
    ((3, 0), OUTER, "add_second", 0),
    ((3, 0), OUTER, "add_core", 2),
    ((4, 0), OUTER, "add_core", 3),
    ((4, 0), INNER, "add_first", 0),
    ((4, 0), INNER, "add_first", 1),
    ((4, 0), OUTER, "add_first", 2),
    ((4, 0), OUTER, "add_second", 1),
    ((4, 1), INNER, "add_first", 2),
    ((4, 1), INNER, "add_first", 3),
    ((4, 1), INNER, "add_second", 0),
    ((4, 1), INNER, "add_second", 1),
    ((4, 2), OUTER, "add_first", 3),
    ((4, 2), OUTER, "add_second", 2),
    ((4, 2), INNER, "add_second", 2),
    ((4, 2), INNER, "add_second", 3),
    ((4, 2), OUTER, "add_second", 3),
)


def chunk_of(step):
    return jnp.where(step == 0, 0, jnp.where(step == 1, 3, step - 1))


def feed_forward(sizes, planned, doc_len, attn, long_x, glob_x, dlong, dglob, lq, *weights):
    block, count, quarter, seq_count, pairs = sizes
    wo, bo, gain, shift, wi, bi, wr, br = weights
    width, hidden = wi.shape
    chunk = hidden // 4
    rows = block + quarter
    whole = pl.BlockSpec(memory_space=pltpu.VMEM)
    shape = jax.ShapeDtypeStruct
    in_specs = [pl.BlockSpec(memory_space=pltpu.SMEM)] + [whole] * 10
    in_specs += [
        pl.BlockSpec((width, chunk), lambda c: (0, chunk_of(c))),
        whole,
        pl.BlockSpec((chunk, width), lambda c: (chunk_of(c), 0)),
        whole,
    ]
    outs = [
        shape((block, width), BF16),
        shape((quarter, width), BF16),
        shape((rows, width), F32),
        shape((rows, width), BF16),
        shape((GP, width), BF16),
        shape((GP, PAIR), F32),
    ]
    out_specs = [whole] * 6
    others = seq_count - 1
    scratch = [
        pltpu.VMEM((rows, width), F32),
        pltpu.VMEM((rows, width), F32),
        pltpu.VMEM((rows, width), F32),
        pltpu.VMEM((rows, width), BF16),
        pltpu.VMEM((width, rows), BF16),
        pltpu.VMEM((rows, width), BF16),
        pltpu.VMEM((8, width), F32),
        pltpu.VMEM((4, 1, chunk), F32),
        pltpu.VMEM((GP, width), BF16),
        pltpu.VMEM((GP, PAIR), F32),
        pltpu.SemaphoreType.DMA((2, others)),
        pltpu.SemaphoreType.DMA((2, others)),
    ]
    if planned:
        part, piece = hidden // 32, width // 32
        outs += [
            shape((2, 4, 2, 2, 3 * piece + 8, width), BF16),
            shape((4, part, width), BF16),
            shape((4, 2 * piece, width), BF16),
        ]
        out_specs += [whole] * 3
        scratch += [
            pltpu.VMEM((width, chunk), F32),
        ]
        scratch += Reducer.scratch(part, width, 2) + Reducer.scratch(2 * piece, width, 2)
    else:
        outs += [
            shape((hidden, width), BF16),
            shape((width, hidden), BF16),
            shape((width, width), BF16),
            shape((8, width), F32),
        ]
        out_specs += [
            pl.BlockSpec((chunk, width), lambda c: (chunk_of(c), 0)),
            pl.BlockSpec((width, chunk), lambda c: (0, chunk_of(c))),
            whole,
            whole,
        ]
    return pl.pallas_call(
        functools.partial(ffn_kernel, sizes, planned),
        grid=(4,),
        in_specs=in_specs,
        out_specs=out_specs,
        out_shape=outs,
        scratch_shapes=scratch,
        compiler_params=pltpu.CompilerParams(
            collective_id=4, has_side_effects=True, vmem_limit_bytes=62 * 2**20
        ),
        name="feed_forward",
    )(doc_len, attn, long_x, glob_x, dlong, dglob, lq, wo, bo, gain, shift, wi, bi, wr, br)


def back_kernel(
    sizes,
    early_rows,
    len_ref,
    tab_ref,
    q_ref,
    kx_ref,
    vx_ref,
    kg_ref,
    vg_ref,
    o_ref,
    do_ref,
    l_ref,
    dog_ref,
    ldg_ref,
    yq_ref,
    *rest,
):
    block, count, quarter, seq_count, pairs = sizes
    reduces = early_rows > 0
    if reduces:
        pieces_ref, outer_parts, inner_parts, *rest = rest
    dq_ref, dk_ref, dv_ref, dtab_ref, glob_out, *rest = rest
    if reduces:
        early_parts, outer_ref, inner_ref, *rest = rest
    (
        dkx,
        dvx,
        dkg,
        dvg,
        q_send,
        q_recv,
        kv_send,
        kv_recv,
        halo_send,
        halo_recv,
        glob_sends,
        glob_recvs,
        halo_sends,
        halo_recvs,
        every,
        gather_sends,
        gather_recvs,
        *rest,
    ) = rest
    number = pl.program_id(0)
    pair = lax.rem(number, pairs)
    seq_index = lax.axis_index("seq")
    if reduces:
        reducer = Reducer(early_rows, 16, rest[:7], pieces=pieces_ref, parts=early_parts)
        z_sums = (
            (ZSum(outer_parts, rest[7:12]), outer_ref),
            (ZSum(inner_parts, rest[12:]), inner_ref),
        )
    scale = HD ** (-0.5)
    low_lanes = lane_index() < HD
    own_keys = slice(HALO, HALO + block)
    own_rows = pl.ds(pl.multiple_of(seq_index * quarter, quarter), quarter)

    def glob_copies(kind, at):
        source, dest = ((q_send, q_recv), (kv_send, kv_recv))[kind]
        for step in range(1, seq_count):
            device = seq_device(step, seq_count)
            yield pltpu.make_async_remote_copy(
                src_ref=source.at[device[1], at],
                dst_ref=dest.at[step - 1, at],
                send_sem=glob_sends.at[kind, step - 1, at],
                recv_sem=glob_recvs.at[kind, step - 1, at],
                device_id=device,
                device_id_type=pl.DeviceIdType.MESH,
            )

    def gathers():
        for step in range(1, seq_count):
            yield pltpu.make_async_remote_copy(
                src_ref=every.at[own_rows],
                dst_ref=every.at[own_rows],
                send_sem=gather_sends.at[step - 1],
                recv_sem=gather_recvs.at[step - 1],
                device_id=seq_device(step, seq_count),
                device_id_type=pl.DeviceIdType.MESH,
            )

    def halo_copy(direction, at):
        return pltpu.make_async_remote_copy(
            src_ref=halo_send.at[direction, at],
            dst_ref=halo_recv.at[direction, at],
            send_sem=halo_sends.at[direction, at],
            recv_sem=halo_recvs.at[direction, at],
            device_id=seq_device(2 * direction - 1, seq_count),
            device_id_type=pl.DeviceIdType.MESH,
        )

    has_low, has_high = seq_index > 0, seq_index < seq_count - 1
    sends_to = (has_low, has_high)
    gets_from = (has_high, has_low)

    def close_pair(at):
        lanes = lanes_of(at)
        for direction in range(2):

            @pl.when(gets_from[direction])
            def _(direction=direction):
                halo_copy(direction, at).wait_recv()

        for kind, (total, out) in enumerate(((dkx, dk_ref), (dvx, dv_ref))):
            first, last = HALO + REACH, HALO + block - REACH
            out[:REACH, lanes] = (
                total[at, HALO:first] + halo_recv[1, at, kind].astype(F32)
            ).astype(BF16)
            out[REACH : block - REACH, lanes] = total[at, first:last].astype(BF16)
            out[block - REACH : block, lanes] = (
                total[at, last : HALO + block] + halo_recv[0, at, kind].astype(F32)
            ).astype(BF16)
        sums = []
        for kind, (source, dest) in enumerate(((q_send, q_recv), (kv_send, kv_recv))):
            total = source[seq_index, at].astype(F32)
            for step, copy in enumerate(glob_copies(kind, at)):
                copy.wait_recv()
                total += dest[step, at].astype(F32)
            sums.append(total.astype(BF16))
        dq_ref[block:, lanes] = sums[0]
        dk_ref[block:, lanes] = sums[1][:, :PAIR]
        dv_ref[block:, lanes] = sums[1][:, PAIR:]

    def run_plan(now):
        for at, act, chunk in EARLY_PLAN:
            if now == at:
                getattr(reducer, act)(chunk)

    @pl.when(number == 0)
    def _():
        others = [seq_device(step, seq_count) for step in range(1, seq_count)]
        meet(others + (reducer.partners()[2:] if reduces else []))
        if reduces:
            for chunk in range(4):
                reducer.start(chunk)
            for z_sum, _ in z_sums:
                z_sum.start()
        every[own_rows] = yq_ref[...]
        for copy in gathers():
            copy.start()
        for direction in range(2):

            @pl.when(jnp.logical_not(gets_from[direction]))
            def _(direction=direction):
                halo_recv[direction] = jnp.zeros_like(halo_recv[direction])

    if reduces:
        for now in range(1, 2 * pairs):
            if any(at == now for at, _, _ in EARLY_PLAN):

                @pl.when(number == now)
                def _(now=now):
                    run_plan(now)

    @pl.when(number < pairs)
    def _():
        long_bias = key_bias(seq_index * block, block, len_ref[0])
        near_bias = key_bias(seq_index * quarter, quarter, count)
        query = q_ref[block:] * jnp.asarray(scale, BF16)
        grad_o = dog_ref[...]
        far_k, far_v = kx_ref[own_keys], vx_ref[own_keys]
        near_k, near_v = kg_ref[own_rows], vg_ref[own_rows]
        outs, kept = [], []
        for head in range(2):
            norm = in_three(-pick_column(ldg_ref[...], 2 * pair + head))
            delta = in_three(-pick_column(ldg_ref[...], HD + 2 * pair + head))
            qa = with_lanes(head, query, (1.0,) + norm)
            doa = with_lanes(head, grad_o, delta)
            far = jnp.exp(dot_t(qa, key_side(head, far_k, long_bias)))
            near = jnp.exp(dot_t(qa, key_side(head, near_k, near_bias)))
            far_ds = (far * dot_t(doa, value_side(head, far_v))).astype(BF16)
            near_ds = (near * dot_t(doa, value_side(head, near_v))).astype(BF16)
            outs.append(dot_n(far_ds, far_k) + dot_n(near_ds, near_k))
            kept.append(
                (
                    own_half(head, query),
                    own_half(head, grad_o),
                    far.astype(BF16),
                    near.astype(BF16),
                    far_ds,
                    near_ds,
                )
            )
        own_q, own_do, far, near, far_ds, near_ds = (
            jnp.concatenate(part, 0) for part in zip(*kept)
        )
        for total, edge in ((dkx, own_keys), (dvx, own_keys)):
            total[pair, :HALO] = jnp.zeros((HALO, PAIR), F32)
            total[pair, HALO + block :] = jnp.zeros((HALO, PAIR), F32)
        dkx[pair, own_keys] = t_dot(far_ds, own_q)
        dvx[pair, own_keys] = t_dot(far, own_do)
        dkg[pair] = jnp.zeros((GP, PAIR), F32)
        dvg[pair] = jnp.zeros((GP, PAIR), F32)
        dkg[pair, own_rows] = t_dot(near_ds, own_q)
        dvg[pair, own_rows] = t_dot(near, own_do)
        glob_dq = (jnp.where(low_lanes, outs[0], outs[1]) * scale).astype(BF16)
        q_send[:, pair] = glob_dq.reshape(seq_count, quarter, PAIR)
        for copy in glob_copies(0, pair):
            copy.start()

    @pl.when(number >= pairs)
    def _():
        long_bias = key_bias(seq_index * block - HALO, block + 2 * HALO, len_ref[0])
        glob_bias = key_bias(0, GP, count)
        query = q_ref[:block] * jnp.asarray(scale, BF16)
        grad_o = do_ref[...]
        both = grad_o.astype(F32) * o_ref[...].astype(F32)
        heads = []
        for head in range(2):
            norm = in_three(-pick_column(l_ref[...], 2 * pair + head))
            delta = in_three(-jnp.sum(own_half(head, both), -1, keepdims=True))
            heads.append(
                dict(
                    q=own_half(head, query),
                    do=own_half(head, grad_o),
                    qa=with_lanes(head, query, (1.0,) + norm),
                    doa=with_lanes(head, grad_o, delta),
                    kxa=key_side(head, kx_ref[...], long_bias),
                    vxa=value_side(head, vx_ref[...]),
                    kga=key_side(head, kg_ref[...], glob_bias),
                    vga=value_side(head, vg_ref[...]),
                    bias=band_bias(tab_ref[0, head : head + 1]),
                )
            )
        table_sums = [0.0, 0.0]
        grads_q = []
        for start in range(0, block, SUB):
            rows, keys = slice(start, start + SUB), slice(start, start + WINDOW)
            outs, probs, grads = [], [], []
            for head, own in enumerate(heads):
                band = jnp.exp(dot_t(own["qa"][rows], own["kxa"][keys]) + own["bias"])
                band_ds = band * dot_t(own["doa"][rows], own["vxa"][keys])
                table_sums[head] += band_ds
                glob = jnp.exp(dot_t(own["qa"][rows], own["kga"]))
                glob_ds = (glob * dot_t(own["doa"][rows], own["vga"])).astype(BF16)
                band_ds = band_ds.astype(BF16)
                outs.append(dot_n(band_ds, kx_ref[keys]) + dot_n(glob_ds, kg_ref[...]))
                probs.append((band.astype(BF16), glob.astype(BF16)))
                grads.append((band_ds, glob_ds))
            grads_q.append(jnp.where(low_lanes, outs[0], outs[1]))
            own_q = jnp.concatenate([own["q"][rows] for own in heads], 0)
            own_do = jnp.concatenate([own["do"][rows] for own in heads], 0)
            band, glob = (jnp.concatenate(part, 0) for part in zip(*probs))
            band_ds, glob_ds = (jnp.concatenate(part, 0) for part in zip(*grads))
            dkx[pair, keys] += t_dot(band_ds, own_q)
            dvx[pair, keys] += t_dot(band, own_do)
            dkg[pair] += t_dot(glob_ds, own_q)
            dvg[pair] += t_dot(glob, own_do)
        for kind, total in enumerate((dkg, dvg)):
            kv_send[:, pair, :, kind * PAIR : (kind + 1) * PAIR] = (
                total[pair].astype(BF16).reshape(seq_count, quarter, PAIR)
            )
        for copy in glob_copies(1, pair):
            copy.start()
        for kind, total in enumerate((dkx, dvx)):
            for direction, first in enumerate((HALO - REACH, HALO + block)):
                halo_send[direction, pair, kind] = total[pair, first : first + REACH].astype(BF16)
        for direction in range(2):

            @pl.when(sends_to[direction])
            def _(direction=direction):
                halo_copy(direction, pair).start()

        dq_ref[:block, lanes_of(pair)] = (jnp.concatenate(grads_q, 0) * scale).astype(BF16)
        for head in range(2):
            dtab_ref[pair, head : head + 1] = diagonal_sums(table_sums[head])

    @pl.when(number > pairs)
    def _():
        close_pair(pair - 1)

    @pl.when(number == 2 * pairs - 1)
    def _():
        if reduces:
            run_plan(2 * pairs)
        close_pair(pairs - 1)
        for at in range(pairs):
            for kind in range(2):
                for copy in glob_copies(kind, at):
                    copy.wait_send()
            for direction in range(2):

                @pl.when(sends_to[direction])
                def _(direction=direction, at=at):
                    halo_copy(direction, at).wait_send()

        for copy in gathers():
            copy.wait_recv()
        glob_out[...] = every[:count]
        for copy in gathers():
            copy.wait_send()
        if reduces:
            reducer.finish()
            for z_sum, out in z_sums:
                z_sum.finish(out)


def attend_back(sizes, doc_len, table, q, kx, vx, kg, vg, o, do, l, dog, ldg, yq, *sums):
    block, count, quarter, seq_count, pairs = sizes
    width = q.shape[1]
    early_rows = sums[0].shape[-2] if sums else 0
    ext = block + 2 * HALO
    cols = lambda rows: pl.BlockSpec((rows, PAIR), lambda i: (0, lax.rem(i, pairs)))
    whole = pl.BlockSpec(memory_space=pltpu.VMEM)
    shape = jax.ShapeDtypeStruct
    in_specs = [
        pl.BlockSpec(memory_space=pltpu.SMEM),
        pl.BlockSpec((1, 2, WINDOW), lambda i: (lax.rem(i, pairs), 0, 0)),
        cols(block + GP),
        cols(ext),
        cols(ext),
        cols(GP),
        cols(GP),
        cols(block),
        cols(block),
        whole,
        cols(GP),
        whole,
        whole,
    ]
    rows = block + quarter
    outs = [shape((rows, width), BF16)] * 3 + [shape((pairs, 2, WINDOW), F32)]
    outs.append(shape((count, width), BF16))
    others = seq_count - 1
    scratch = [
        pltpu.VMEM((pairs, ext, PAIR), F32),
        pltpu.VMEM((pairs, ext, PAIR), F32),
        pltpu.VMEM((pairs, GP, PAIR), F32),
        pltpu.VMEM((pairs, GP, PAIR), F32),
        pltpu.VMEM((seq_count, pairs, quarter, PAIR), BF16),
        pltpu.VMEM((others, pairs, quarter, PAIR), BF16),
        pltpu.VMEM((seq_count, pairs, quarter, 2 * PAIR), BF16),
        pltpu.VMEM((others, pairs, quarter, 2 * PAIR), BF16),
        pltpu.VMEM((2, pairs, 2, REACH, PAIR), BF16),
        pltpu.VMEM((2, pairs, 2, REACH, PAIR), BF16),
        pltpu.SemaphoreType.DMA((2, others, pairs)),
        pltpu.SemaphoreType.DMA((2, others, pairs)),
        pltpu.SemaphoreType.DMA((2, pairs)),
        pltpu.SemaphoreType.DMA((2, pairs)),
        pltpu.VMEM((GP, width), BF16),
        pltpu.SemaphoreType.DMA((others,)),
        pltpu.SemaphoreType.DMA((others,)),
    ]
    args = [doc_len, table, q, kx, vx, kg, vg, o, do, l, dog, ldg, yq, *sums]
    if early_rows:
        in_specs += [pl.BlockSpec(memory_space=pl.ANY)] * 3
        outs.append(shape((4, early_rows, width), BF16))
        scratch += Reducer.scratch(early_rows, width, 1)
        for parts in sums[1:]:
            outs.append(shape(parts.shape[1:], F32))
            scratch += ZSum.scratch(*parts.shape[1:])
    return pl.pallas_call(
        functools.partial(back_kernel, sizes, early_rows),
        grid=(2 * pairs,),
        in_specs=in_specs,
        out_specs=[whole] * len(outs),
        out_shape=outs,
        scratch_shapes=scratch,
        compiler_params=pltpu.CompilerParams(
            collective_id=1, has_side_effects=True, vmem_limit_bytes=60 * 2**20
        ),
        name="attend_back",
    )(*args)


def on_device(
    long_input,
    global_input,
    lengths,
    w_query,
    b_query,
    w_key,
    w_value,
    b_value,
    w_out,
    b_out,
    w_inner,
    b_inner,
    w_outer,
    b_outer,
    norm1_gain,
    norm1_shift,
    norm2_gain,
    norm2_shift,
    rel_table,
    long_cotangent,
    global_cotangent,
):
    seq_count = lax.axis_size("seq")
    data_count = lax.axis_size("dp")
    seq_index = lax.axis_index("seq")
    block = long_input.shape[1]
    count = global_input.shape[1]
    width = long_input.shape[2]
    heads = rel_table.shape[1]
    pairs = heads // 2
    labels = 2 * R + 1
    quarter = GP // seq_count
    sizes = Sizes(block, count, quarter, seq_count, pairs)
    queries, kx, vx, kg, vg, attn_low, long_l, glob_l, glob_x, table = attend(
        sizes,
        lengths,
        rel_table,
        long_input[0],
        global_input[0],
        w_query,
        w_key,
        w_value,
        b_query,
        b_value,
        norm1_gain,
        norm1_shift,
    )
    planned = has_plan()
    long_result, own_out, grad_mid, grad_attn, every_do, every_ld, *gradients = feed_forward(
        sizes,
        planned,
        lengths,
        attn_low,
        long_input[0],
        glob_x,
        long_cotangent[0],
        global_cotangent[0],
        glob_l,
        w_out,
        b_out,
        norm2_gain,
        norm2_shift,
        w_inner,
        b_inner,
        w_outer,
        b_outer,
    )
    query_low, key_low, value_low, dtab, glob_out, *early = attend_back(
        sizes,
        lengths,
        table,
        queries,
        kx,
        vx,
        kg,
        vg,
        attn_low,
        grad_attn,
        long_l,
        every_do,
        every_ld,
        own_out,
        *(gradients if planned else []),
    )
    long_grad, glob_grad, *late = last_part(
        sizes,
        planned,
        long_input[0],
        glob_x,
        query_low,
        key_low,
        value_low,
        grad_mid,
        w_query,
        w_key,
        w_value,
        norm1_gain,
        norm1_shift,
        dtab,
        *early[:1],
    )
    if planned:
        (
            g_query,
            g_key,
            g_value,
            g_out,
            g_inner,
            g_outer,
            g_b_query,
            g_b_value,
            g_b_out,
            g_b_outer,
            g_g1,
            g_s1,
            g_g2,
            g_s2,
            g_b_inner,
            table_total,
        ) = small_results(heads, late[3], late[0], early[1], early[2], late[1], late[2])
    else:
        devices = data_count * seq_count
        own_part = lambda vector: lax.dynamic_slice_in_dim(
            vector,
            (lax.axis_index("dp") * seq_count + seq_index) * (vector.shape[0] // devices),
            vector.shape[0] // devices,
        )
        g_outer, g_inner, g_out, vectors = gradients
        g_outer, g_inner, g_out, g_query, g_key, g_value = (
            lax.psum_scatter(g.astype(BF16), ("dp", "seq"), scatter_dimension=0, tiled=True).astype(
                F32
            )
            for g in (g_outer, g_inner, g_out, *late[:3])
        )
        vectors, sums, scales = lax.psum((vectors, *late[3:]), ("dp", "seq"))
        g_b_query, g_b_value = (own_part(sums[heads + i]) for i in range(2))
        g_g1, g_s1 = (own_part(scales[i]) for i in range(2))
        g_b_out, g_b_outer, g_g2, g_s2 = (own_part(vectors[i]) for i in range(4))
        g_b_inner = own_part(vectors[4:].reshape(-1))
        table_total = sums[:heads, HALO - R : HALO - R + labels].T
    return (
        long_result[None],
        glob_out[None],
        long_grad[None],
        glob_grad[None],
        g_query,
        g_b_query,
        g_key,
        g_value,
        g_b_value,
        g_out,
        g_b_out,
        g_inner,
        g_b_inner,
        g_outer,
        g_b_outer,
        g_g1,
        g_s1,
        g_g2,
        g_s2,
        table_total,
    )


def solution(mesh):
    rows, whole = P("dp", "seq", None), P("dp", None, None)
    matrix, vector = P(("dp", "seq"), None), P(("dp", "seq"))
    return jax.shard_map(
        on_device,
        mesh=mesh,
        in_specs=(rows, whole, P("dp")) + (P(),) * 16 + (rows, whole),
        out_specs=(
            rows,
            whole,
            rows,
            whole,
            matrix,
            vector,
            matrix,
            matrix,
            vector,
            matrix,
            vector,
            matrix,
            vector,
            matrix,
            vector,
            vector,
            vector,
            vector,
            vector,
            P(),
        ),
        check_vma=False,
    )
```

```python
import functools
from typing import NamedTuple

import jax
import jax.numpy as jnp
from jax import lax
from jax.experimental import pallas as pl
from jax.experimental.pallas import tpu as pltpu
from jax.sharding import PartitionSpec as P

HD = 64
R = 84
PAIR = 2 * HD
HALO = 128
REACH = 96
GP = 256
SUB = 256
WINDOW = SUB + 2 * HALO
EPSILON = 1e-05
MASKED = -1e30
F32 = jnp.float32
BF16 = jnp.bfloat16


def dot_t(left, right):
    return lax.dot_general(left, right, (((1,), (1,)), ((), ())), preferred_element_type=F32)


def dot_n(left, right):
    return lax.dot_general(left, right, (((1,), (0,)), ((), ())), preferred_element_type=F32)


def t_dot(left, right):
    return lax.dot_general(left, right, (((0,), (0,)), ((), ())), preferred_element_type=F32)


def band_bias(table_row):
    spread = jnp.broadcast_to(table_row, (SUB, WINDOW))
    return pltpu.roll(spread, 0, 1, stride=1, stride_axis=0)


def diagonal_sums(rows):
    height, width = rows.shape
    while height > 8:
        height //= 2
        rows = rows[:height] + pltpu.roll(rows[height:], width - height, 1)
    row = lax.broadcasted_iota(jnp.int32, rows.shape, 0)
    for bit in (1, 2, 4):
        rows = jnp.where((row & bit) != 0, pltpu.roll(rows, width - bit, 1), rows)
    return jnp.sum(rows, 0, keepdims=True)


def lane_index():
    return lax.broadcasted_iota(jnp.int32, (1, PAIR), 1)


def own_half(head, value):
    low_lanes = lane_index() < HD
    return jnp.where(low_lanes if head == 0 else ~low_lanes, value, jnp.zeros_like(value))


def other_lane(head):
    return HD * (1 - head)


def with_lanes(head, value, columns):
    wide = own_half(head, value.astype(F32))
    lane = lane_index()
    for offset, column in enumerate(columns):
        wide = jnp.where(lane == other_lane(head) + offset, column, wide)
    return wide.astype(BF16)


def in_three(column):
    high = column.astype(BF16).astype(F32)
    middle = (column - high).astype(BF16).astype(F32)
    return (high, middle, column - high - middle)


def key_bias(first, rows, end):
    position = first + lax.broadcasted_iota(jnp.int32, (rows, 1), 0)
    return jnp.where((position >= 0) & (position < end), 0.0, MASKED)


def pick_column(rows, index):
    return jnp.sum(jnp.where(lane_index() == index, rows, 0.0), -1, keepdims=True)


def key_side(head, keys, bias):
    return with_lanes(head, keys, (bias, 1.0, 1.0, 1.0))


def value_side(head, values):
    return with_lanes(head, values, (1.0, 1.0, 1.0))


def softmax_rows(parts, value_parts, head):
    top = functools.reduce(
        jnp.maximum, [jnp.max(part, -1, keepdims=True) for part in parts]
    )
    mixed = sum(
        dot_n(jnp.exp(part - top).astype(BF16), values)
        for part, values in zip(parts, value_parts)
    )
    at = other_lane(head)
    total = mixed[:, at : at + 1]
    return mixed / total, top + jnp.log(total)


def seq_device(steps, seq_count):
    return (lax.axis_index("dp"), lax.rem(lax.axis_index("seq") + steps + seq_count, seq_count))


def row_norm(rows):
    centred = rows - jnp.mean(rows, -1, keepdims=True)
    inverse = lax.rsqrt(jnp.mean(centred * centred, -1, keepdims=True) + EPSILON)
    return centred * inverse, inverse


def put_column(ref, rows, index, column):
    ref[rows] = jnp.where(lane_index() == index, column, ref[rows])


def lanes_of(at):
    return pl.ds(pl.multiple_of(at * PAIR, PAIR), PAIR)


class Sizes(NamedTuple):
    block: int
    count: int
    quarter: int
    seq_count: int
    pairs: int


def attend_kernel(
    sizes,
    len_ref,
    rel_ref,
    long_ref,
    raw_ref,
    wq_ref,
    wk_ref,
    wv_ref,
    bq_ref,
    bv_ref,
    gain_ref,
    shift_ref,
    q_ref,
    kx_ref,
    vx_ref,
    kg_ref,
    vg_ref,
    o_ref,
    l_ref,
    lq_ref,
    glob_ref,
    tab_ref,
    spread,
    wide,
    part_o,
    part_l,
    from_o,
    from_l,
    halo_sends,
    halo_recvs,
    part_sends,
    part_recvs,
):
    block, count, quarter, seq_count, pairs = sizes
    ext = block + 2 * HALO
    seq_index = lax.axis_index("seq")
    scale = jnp.asarray(HD ** (-0.5), BF16)
    low_lanes = lane_index() < HD
    own_keys = slice(HALO, HALO + block)
    own_rows = pl.ds(pl.multiple_of(seq_index * quarter, quarter), quarter)
    neighbours = (seq_index > 0, seq_index < seq_count - 1)
    barrier = pltpu.get_barrier_semaphore()
    for step in range(1, seq_count):
        pl.semaphore_signal(
            barrier,
            inc=1,
            device_id=seq_device(step, seq_count),
            device_id_type=pl.DeviceIdType.MESH,
        )

    def halo_copies(direction):
        source = HALO if direction == 0 else HALO + block - REACH
        dest = HALO + block if direction == 0 else HALO - REACH
        for kind, ref in enumerate((kx_ref, vx_ref)):
            yield pltpu.make_async_remote_copy(
                src_ref=ref.at[source : source + REACH],
                dst_ref=ref.at[dest : dest + REACH],
                send_sem=halo_sends.at[direction, kind],
                recv_sem=halo_recvs.at[direction, kind],
                device_id=seq_device(2 * direction - 1, seq_count),
                device_id_type=pl.DeviceIdType.MESH,
            )

    def part_copies():
        for step in range(1, seq_count):
            device = seq_device(step, seq_count)
            rows = pl.ds(pl.multiple_of(device[1] * quarter, quarter), quarter)
            for kind, (source, dest) in enumerate(((part_o, from_o), (part_l, from_l))):
                yield step, kind, pltpu.make_async_remote_copy(
                    src_ref=source.at[rows],
                    dst_ref=dest.at[step - 1],
                    send_sem=part_sends.at[kind, step - 1],
                    recv_sem=part_recvs.at[kind, step - 1],
                    device_id=device,
                    device_id_type=pl.DeviceIdType.MESH,
                )

    gain, shift = gain_ref[...], shift_ref[...]
    heads, labels = rel_ref.shape
    spread[...] = jnp.full(spread.shape, MASKED, F32)
    spread[:heads, :labels] = rel_ref[...]
    turned = pltpu.roll(spread[...], HALO - R, 1)
    for pair in range(pairs):
        tab_ref[pair] = turned[2 * pair : 2 * pair + 2]
    normed_long = (row_norm(long_ref[...].astype(F32))[0] * gain + shift).astype(BF16)
    kx_ref[own_keys] = dot_n(normed_long, wk_ref[...]).astype(BF16)
    vx_ref[own_keys] = (dot_n(normed_long, wv_ref[...]) + bv_ref[...]).astype(BF16)
    pl.semaphore_wait(barrier, seq_count - 1)
    for direction, first in enumerate((HALO - REACH, HALO + block)):

        @pl.when(neighbours[direction])
        def _(direction=direction):
            for copy in halo_copies(direction):
                copy.start()

        outer = slice(0, first) if direction == 0 else slice(first + REACH, ext)
        for ref in (kx_ref, vx_ref):
            ref[outer] = jnp.zeros((HALO - REACH, ref.shape[1]), BF16)

        @pl.when(jnp.logical_not(neighbours[direction]))
        def _(first=first):
            for ref in (kx_ref, vx_ref):
                ref[first : first + REACH] = jnp.zeros((REACH, ref.shape[1]), BF16)

    wide[...] = jnp.zeros_like(wide)
    wide[:count] = raw_ref[...].astype(F32)
    glob_ref[...] = wide[...].astype(BF16)
    normed_glob = (row_norm(wide[...])[0] * gain + shift).astype(BF16)
    kg_ref[...] = dot_n(normed_glob, wk_ref[...]).astype(BF16)
    vg_ref[...] = (dot_n(normed_glob, wv_ref[...]) + bv_ref[...]).astype(BF16)
    q_ref[block:] = (dot_n(normed_glob, wq_ref[...]) + bq_ref[...]).astype(BF16)
    q_ref[:block] = (dot_n(normed_long, wq_ref[...]) + bq_ref[...]).astype(BF16)
    part_l[...] = jnp.zeros_like(part_l)
    l_ref[...] = jnp.zeros_like(l_ref)

    def glob_pair(pair, carry):
        lanes = lanes_of(pair)
        far_bias = key_bias(seq_index * block, block, len_ref[0])
        near_bias = key_bias(seq_index * quarter, quarter, count)
        query = q_ref[block:, lanes] * scale
        outs = []
        for head in range(2):
            q = with_lanes(head, query, (1.0,))
            far = dot_t(q, with_lanes(head, kx_ref[own_keys, lanes], (far_bias,)))
            near = dot_t(q, with_lanes(head, kg_ref[own_rows, lanes], (near_bias,)))
            out, norm = softmax_rows(
                [far, near],
                [
                    with_lanes(head, vx_ref[own_keys, lanes], (1.0,)),
                    with_lanes(head, vg_ref[own_rows, lanes], (1.0,)),
                ],
                head,
            )
            outs.append(out)
            put_column(part_l, slice(None), 2 * pair + head, norm)
        part_o[:, lanes] = jnp.where(low_lanes, outs[0], outs[1]).astype(BF16)
        return carry

    lax.fori_loop(0, pairs, glob_pair, 0, unroll=2)
    for _, _, copy in part_copies():
        copy.start()
    for direction in range(2):

        @pl.when(neighbours[1 - direction])
        def _(direction=direction):
            for copy in halo_copies(direction):
                copy.wait_recv()

    def long_pair(pair, carry):
        lanes = lanes_of(pair)
        long_bias = key_bias(seq_index * block - HALO, ext, len_ref[0])
        glob_bias = key_bias(0, GP, count)
        query = q_ref[:block, lanes] * scale
        outs = []
        for head in range(2):
            q = with_lanes(head, query, (1.0,))
            kx = with_lanes(head, kx_ref[:, lanes], (long_bias,))
            kg = with_lanes(head, kg_ref[:, lanes], (glob_bias,))
            vx, vg = (with_lanes(head, ref[:, lanes], (1.0,)) for ref in (vx_ref, vg_ref))
            bias = band_bias(tab_ref[pair, head : head + 1])
            mixed = []
            for start in range(0, block, SUB):
                rows, keys = slice(start, start + SUB), slice(start, start + WINDOW)
                out, norm = softmax_rows(
                    [dot_t(q[rows], kx[keys]) + bias, dot_t(q[rows], kg)], [vx[keys], vg], head
                )
                mixed.append(out)
                put_column(l_ref, rows, 2 * pair + head, norm)
            outs.append(jnp.concatenate(mixed, 0))
        o_ref[:block, lanes] = jnp.where(low_lanes, outs[0], outs[1]).astype(BF16)
        return carry

    lax.fori_loop(0, pairs, long_pair, 0, unroll=2)
    for _, _, copy in part_copies():
        copy.wait_recv()
    norms = [part_l[own_rows]] + [from_l[step] for step in range(seq_count - 1)]
    outs = [part_o[own_rows]] + [from_o[step] for step in range(seq_count - 1)]
    top = functools.reduce(jnp.maximum, norms)
    shares = [jnp.exp(norm - top) for norm in norms]
    total = sum(shares)
    lq_ref[...] = top + jnp.log(total)
    shares = [share / total for share in shares]
    for at in range(pairs):
        lanes = slice(at * PAIR, (at + 1) * PAIR)
        mixed = 0.0
        for share, out in zip(shares, outs):
            spread = jnp.where(
                low_lanes, share[:, 2 * at : 2 * at + 1], share[:, 2 * at + 1 : 2 * at + 2]
            )
            mixed += spread * out[:, lanes].astype(F32)
        o_ref[block:, lanes] = mixed.astype(BF16)
    for _, _, copy in part_copies():
        copy.wait_send()
    for direction in range(2):

        @pl.when(neighbours[direction])
        def _(direction=direction):
            for copy in halo_copies(direction):
                copy.wait_send()


def attend(sizes, doc_len, rel_table, long_x, glob_x, *weights):
    block, count, quarter, seq_count, pairs = sizes
    width = long_x.shape[1]
    ext = block + 2 * HALO
    whole = pl.BlockSpec(memory_space=pltpu.VMEM)
    shape = jax.ShapeDtypeStruct
    others = seq_count - 1
    return pl.pallas_call(
        functools.partial(attend_kernel, sizes),
        in_specs=[pl.BlockSpec(memory_space=pltpu.SMEM)] + [whole] * 10,
        out_specs=[whole] * 10,
        out_shape=[
            shape((block + GP, width), BF16),
            shape((ext, width), BF16),
            shape((ext, width), BF16),
            shape((GP, width), BF16),
            shape((GP, width), BF16),
            shape((block + quarter, width), BF16),
            shape((block, PAIR), F32),
            shape((quarter, PAIR), F32),
            shape((GP, width), BF16),
            shape((pairs, 2, WINDOW), F32),
        ],
        scratch_shapes=[
            pltpu.VMEM(((2 * pairs + 7) // 8 * 8, WINDOW), F32),
            pltpu.VMEM((GP, width), F32),
            pltpu.VMEM((GP, width), BF16),
            pltpu.VMEM((GP, PAIR), F32),
            pltpu.VMEM((others, quarter, width), BF16),
            pltpu.VMEM((others, quarter, PAIR), F32),
            pltpu.SemaphoreType.DMA((2, 2)),
            pltpu.SemaphoreType.DMA((2, 2)),
            pltpu.SemaphoreType.DMA((2, others)),
            pltpu.SemaphoreType.DMA((2, others)),
        ],
        compiler_params=pltpu.CompilerParams(
            collective_id=3, has_side_effects=True, vmem_limit_bytes=56 * 2**20
        ),
        name="attend",
    )(doc_len, rel_table, long_x, glob_x, *weights)


class Reducer:
    def __init__(self, rows, split, scratch, pieces=None, order=None, parts=None):
        self.ids = mesh_ids()
        self.parts = parts
        self.order = order
        self.halves = (slice(0, split), slice(split, rows))
        held, self.from_core, self.from_one, self.from_two = scratch[:4]
        self.local, self.sends, self.recvs = scratch[4:7]
        if parts is None:
            self.from_z, self.z_sends, self.z_recvs = scratch[7:]
        self.pieces, self.held = pieces, held
        self.mine = held.at[self.ids[3]] if pieces is None else held.at[0]

    @staticmethod
    def scratch(rows, width, sides, with_z=False):
        buffers = [
            pltpu.VMEM((sides, 4, 2, 2, rows, width), BF16),
            pltpu.VMEM((4, 2, 2, rows, width), BF16),
            pltpu.VMEM((4, 2, rows, width), BF16),
            pltpu.VMEM((4, rows, width), BF16),
            pltpu.SemaphoreType.DMA((4,)),
            pltpu.SemaphoreType.DMA((5, 4)),
            pltpu.SemaphoreType.DMA((5, 4)),
        ]
        if with_z:
            buffers += [
                pltpu.VMEM((3, rows, width), BF16),
                pltpu.SemaphoreType.DMA((4,)),
                pltpu.SemaphoreType.DMA((3,)),
            ]
        return buffers

    def partners(self):
        z, y, x, core = self.ids
        dp, seq = z * 2 + y, x * 2 + core
        near = [(dp, x * 2 + 1 - core), (dp, (1 - x) * 2 + core), (z * 2 + 1 - y, seq)]
        return near + [(lax.rem(z + step, 4) * 2 + y, seq) for step in (1, 2, 3)]

    def target(self, chunk):
        return self.order(chunk) if self.order else lax.rem(self.ids[0] + 1 + chunk, 4)

    def remote(self, source, dest, kind, send_at, recv_at, device):
        return pltpu.make_async_remote_copy(
            src_ref=source,
            dst_ref=dest,
            send_sem=self.sends.at[kind, send_at],
            recv_sem=self.recvs.at[kind, recv_at],
            device_id=device,
            device_id_type=pl.DeviceIdType.MESH,
        )

    def own_copy(self, chunk):
        core, to = self.ids[3], self.target(chunk)
        return pltpu.make_async_copy(
            self.pieces.at[core, to], self.mine.at[to], self.local.at[chunk]
        )

    def core_copy(self, chunk):
        core, to = self.ids[3], self.target(chunk)
        source = (self.held if self.pieces is None else self.pieces).at[1 - core, to]
        return self.remote(source, self.from_core.at[to], 0, chunk, chunk, self.partners()[0])

    def first_copies(self, chunk):
        z, y, x, core = self.ids
        to = self.target(chunk)
        one, two = self.halves
        near = self.partners()
        return (
            self.remote(
                self.mine.at[to, :, 1 - x, one],
                self.from_one.at[to, :, one],
                1,
                chunk,
                chunk,
                near[1],
            ),
            self.remote(
                self.mine.at[to, 1 - y, :, two],
                self.from_one.at[to, :, two],
                2,
                chunk,
                chunk,
                near[2],
            ),
        )

    def second_copies(self, chunk):
        z, y, x, core = self.ids
        to = self.target(chunk)
        one, two = self.halves
        near = self.partners()
        return (
            self.remote(
                self.mine.at[to, 1 - y, x, one],
                self.from_two.at[to, one],
                3,
                chunk,
                chunk,
                near[2],
            ),
            self.remote(
                self.mine.at[to, y, 1 - x, two],
                self.from_two.at[to, two],
                4,
                chunk,
                chunk,
                near[1],
            ),
        )

    def last_copy(self, chunk):
        z, y, x, core = self.ids
        to = self.target(chunk)
        slot = lax.rem(z - to + 4, 4) - 1
        return pltpu.make_async_remote_copy(
            src_ref=self.mine.at[to, y, x],
            dst_ref=self.from_z.at[slot],
            send_sem=self.z_sends.at[chunk],
            recv_sem=self.z_recvs.at[slot],
            device_id=(to * 2 + y, x * 2 + core),
            device_id_type=pl.DeviceIdType.MESH,
        )

    def arrival(self, slot):
        z, y, x, core = self.ids
        return pltpu.make_async_remote_copy(
            src_ref=self.mine.at[z, y, x],
            dst_ref=self.from_z.at[slot],
            send_sem=self.z_sends.at[slot],
            recv_sem=self.z_recvs.at[slot],
            device_id=self.partners()[3],
            device_id_type=pl.DeviceIdType.MESH,
        )

    def leaves(self, chunk):
        return self.target(chunk) != self.ids[0]

    def fill(self, to, at, value):
        self.held[at % 2, to, at // 4, at // 2 % 2] = value.astype(BF16)

    def start(self, chunk):
        self.core_copy(chunk).start()
        if self.pieces is not None:
            self.own_copy(chunk).start()

    def add_core(self, chunk):
        to = self.target(chunk)
        if self.pieces is not None:
            self.own_copy(chunk).wait()
        self.core_copy(chunk).wait_recv()

        def add(index, carry):
            at = (to, lax.div(index, 2), lax.rem(index, 2))
            self.mine[at] = self.mine[at] + self.from_core[at]
            return carry

        lax.fori_loop(0, 4, add, 0)
        for copy in self.first_copies(chunk):
            copy.start()

    def add_first(self, chunk):
        z, y, x, core = self.ids
        one, two = self.halves
        to = self.target(chunk)
        for copy in self.first_copies(chunk):
            copy.wait_recv()

        def add(index, carry):
            for at, rows in (((to, index, x), one), ((to, y, index), two)):
                self.mine[at + (rows,)] = self.mine[at + (rows,)] + self.from_one[to, index, rows]
            return carry

        lax.fori_loop(0, 2, add, 0)
        for copy in self.second_copies(chunk):
            copy.start()

    def add_second(self, chunk):
        z, y, x, core = self.ids
        to = self.target(chunk)
        for copy in self.second_copies(chunk):
            copy.wait_recv()
        if self.parts is not None:
            self.parts[to] = self.mine[to, y, x] + self.from_two[to]
            return

        @pl.when(self.leaves(chunk))
        def _():
            self.mine[to, y, x] = self.mine[to, y, x] + self.from_two[to]
            self.last_copy(chunk).start()

    def finish(self, out=None):
        z, y, x, core = self.ids
        if self.parts is None:
            total = self.mine[z, y, x].astype(F32) + self.from_two[z].astype(F32)
            for slot in range(3):
                self.arrival(slot).wait_recv()
                total += self.from_z[slot].astype(F32)
            out[...] = total
        for chunk in range(4):
            self.core_copy(chunk).wait_send()
            for copy in self.first_copies(chunk) + self.second_copies(chunk):
                copy.wait_send()
            if self.parts is None:

                @pl.when(self.leaves(chunk))
                def _(chunk=chunk):
                    self.last_copy(chunk).wait_send()


class ZSum:
    def __init__(self, parts, scratch):
        self.ids = mesh_ids()
        self.parts = parts
        self.own, self.from_z, self.local, self.sends, self.recvs = scratch

    @staticmethod
    def scratch(rows, width):
        return [
            pltpu.VMEM((rows, width), BF16),
            pltpu.VMEM((3, rows, width), BF16),
            pltpu.SemaphoreType.DMA,
            pltpu.SemaphoreType.DMA((3,)),
            pltpu.SemaphoreType.DMA((3,)),
        ]

    def own_copy(self):
        return pltpu.make_async_copy(self.parts.at[self.ids[0]], self.own, self.local)

    def copies(self):
        z, y, x, core = self.ids
        for slot in range(3):
            to = lax.rem(z + 3 - slot, 4)
            yield pltpu.make_async_remote_copy(
                src_ref=self.parts.at[to],
                dst_ref=self.from_z.at[slot],
                send_sem=self.sends.at[slot],
                recv_sem=self.recvs.at[slot],
                device_id=(to * 2 + y, x * 2 + core),
                device_id_type=pl.DeviceIdType.MESH,
            )

    def start(self):
        self.own_copy().start()
        for copy in self.copies():
            copy.start()

    def finish(self, out):
        self.own_copy().wait()
        total = self.own[...].astype(F32)
        for slot, copy in enumerate(self.copies()):
            copy.wait_recv()
            total += self.from_z[slot].astype(F32)
        out[...] = total
        for copy in self.copies():
            copy.wait_send()


class EverySum:
    def __init__(self, scratch):
        self.kept, self.arrived, self.from_z, self.sends, self.recvs = scratch
        z, y, x, core = mesh_ids()
        seq = x * 2 + core
        self.z = z
        self.pairs = (
            (z * 2 + y, x * 2 + 1 - core),
            (z * 2 + y, (1 - x) * 2 + core),
            (z * 2 + 1 - y, seq),
        )
        self.along_z = [(lax.rem(z + step, 4) * 2 + y, seq) for step in (1, 2, 3)]

    @staticmethod
    def scratch(rows, width):
        return [
            pltpu.VMEM((3, rows, width), F32),
            pltpu.VMEM((3, rows, width), F32),
            pltpu.VMEM((4, rows, width), F32),
            pltpu.SemaphoreType.DMA((6,)),
            pltpu.SemaphoreType.DMA((6,)),
        ]

    def copy(self, stage):
        return pltpu.make_async_remote_copy(
            src_ref=self.kept.at[stage],
            dst_ref=self.arrived.at[stage],
            send_sem=self.sends.at[stage],
            recv_sem=self.recvs.at[stage],
            device_id=self.pairs[stage],
            device_id_type=pl.DeviceIdType.MESH,
        )

    def z_copies(self):
        for at, device in enumerate(self.along_z):
            yield pltpu.make_async_remote_copy(
                src_ref=self.from_z.at[self.z],
                dst_ref=self.from_z.at[self.z],
                send_sem=self.sends.at[3 + at],
                recv_sem=self.recvs.at[3 + at],
                device_id=device,
                device_id_type=pl.DeviceIdType.MESH,
            )

    def step(self, stage):
        if stage > 0:
            self.copy(stage - 1).wait_recv()
            total = self.kept[stage - 1] + self.arrived[stage - 1]
            if stage < 3:
                self.kept[stage] = total
            else:
                self.from_z[self.z] = total
        if stage < 3:
            self.copy(stage).start()
        else:
            for copy in self.z_copies():
                copy.start()

    def finish(self, out):
        for copy in self.z_copies():
            copy.wait_recv()
        out[...] = (self.from_z[0] + self.from_z[1]) + (self.from_z[2] + self.from_z[3])
        for copy in [self.copy(stage) for stage in range(3)] + list(self.z_copies()):
            copy.wait_send()


def mesh_ids():
    dp, seq = lax.axis_index("dp"), lax.axis_index("seq")
    return lax.div(dp, 2), lax.rem(dp, 2), lax.div(seq, 2), lax.rem(seq, 2)


def meet(devices):
    barrier = pltpu.get_barrier_semaphore()
    for device in devices:
        pl.semaphore_signal(barrier, inc=1, device_id=device, device_id_type=pl.DeviceIdType.MESH)
    pl.semaphore_wait(barrier, len(devices))


EARLY_PLAN = (
    (1, "add_core", 0),
    (1, "add_core", 1),
    (2, "add_core", 2),
    (2, "add_core", 3),
    (4, "add_first", 0),
    (4, "add_first", 1),
    (5, "add_first", 2),
    (5, "add_first", 3),
    (5, "add_second", 0),
    (6, "add_second", 1),
    (6, "add_second", 2),
    (6, "add_second", 3),
)


def late_kernel(
    sizes,
    planned,
    long_ref,
    glob_ref,
    dq_ref,
    dk_ref,
    dv_ref,
    dmid_ref,
    wq_ref,
    wk_ref,
    wv_ref,
    gain_ref,
    shift_ref,
    table_ref,
    *rest,
):
    block, count, quarter, seq_count, pairs = sizes
    rows = block + quarter
    width = long_ref.shape[1]
    if planned:
        early_parts, long_out, glob_out, late_ref, total_ref, scale_ref, early_ref, *rest = rest
    else:
        long_out, glob_out, gq_ref, gk_ref, gv_ref, total_ref, scale_ref, *rest = rest
    normed_t, every, gather_sends, gather_recvs, *rest = rest
    seq_index = lax.axis_index("seq")
    own_rows = pl.ds(pl.multiple_of(seq_index * quarter, quarter), quarter)
    others = [seq_device(step, seq_count) for step in range(1, seq_count)]

    def gathers():
        for step, device in enumerate(others):
            yield pltpu.make_async_remote_copy(
                src_ref=every.at[own_rows],
                dst_ref=every.at[own_rows],
                send_sem=gather_sends.at[step],
                recv_sem=gather_recvs.at[step],
                device_id=device,
                device_id_type=pl.DeviceIdType.MESH,
            )

    if planned:
        first_sum, second_sum = EverySum(rest[:5]), EverySum(rest[5:10])
        z_sum = ZSum(early_parts, rest[10:15])
        reducer = Reducer(rest[15].shape[-2], 32, rest[15:])

    meet(others + (reducer.partners()[2:] if planned else []))
    heads = 2 * pairs
    first = first_sum.kept.at[0] if planned else total_ref
    first[...] = jnp.zeros(first.shape, F32)
    for pair in range(pairs):
        first[2 * pair : 2 * pair + 2, :WINDOW] = table_ref[pair]
    for at, ref in enumerate((dq_ref, dv_ref)):
        first[heads + at : heads + at + 1] = column_sum(ref[...].astype(F32))
    if planned:
        first_sum.step(0)
        z_sum.start()
    everything = jnp.concatenate([long_ref[...], glob_ref[own_rows]], 0).astype(F32)
    hat, inverse = row_norm(everything)
    normed_t[...] = (hat * gain_ref[...] + shift_ref[...]).astype(BF16).T
    if planned:
        piece = width // 32
        blank = jnp.zeros((8, width), F32)
        def weight_rows(chunk):
            to = reducer.target(chunk)
            some = normed_t[pl.ds(pl.multiple_of(to * 8 * piece, 64), 8 * piece)]
            parts = [dot_n(some, ref[...]) for ref in (dq_ref, dk_ref, dv_ref)]
            for at in range(8):
                rows_at = slice(at * piece, (at + 1) * piece)
                reducer.fill(
                    to, at, jnp.concatenate([part[rows_at] for part in parts] + [blank], 0)
                )
            reducer.start(chunk)

        weight_rows(0)
        first_sum.step(1)
        weight_rows(1)
        first_sum.step(2)
        reducer.add_core(0)
        weight_rows(2)
        first_sum.step(3)
        reducer.add_core(1)
        weight_rows(3)
        grads = dot_t(dq_ref[...], wq_ref[...])
        grads += dot_t(dk_ref[...], wk_ref[...]) + dot_t(dv_ref[...], wv_ref[...])
        reducer.add_first(0)
        reducer.add_core(2)
    else:
        for ref, out in ((dq_ref, gq_ref), (dk_ref, gk_ref), (dv_ref, gv_ref)):
            out[...] = dot_n(normed_t[...], ref[...]).astype(BF16)
        grads = (
            dot_t(dq_ref[...], wq_ref[...])
            + dot_t(dk_ref[...], wk_ref[...])
            + dot_t(dv_ref[...], wv_ref[...])
        )
    scaled = grads * gain_ref[...]
    total = dmid_ref[...] + inverse * (
        scaled
        - jnp.mean(scaled, -1, keepdims=True)
        - hat * jnp.mean(scaled * hat, -1, keepdims=True)
    )
    every[own_rows] = total[block:].astype(BF16)
    for copy in gathers():
        copy.start()
    long_out[...] = total[:block]
    second = second_sum.kept.at[0] if planned else scale_ref
    second[...] = jnp.zeros(second.shape, F32)
    second[0:1] = column_sum(grads * hat)
    second[1:2] = column_sum(grads)
    if planned:
        second_sum.step(0)
        reducer.add_first(1)
        second_sum.step(1)
        reducer.add_core(3)
        reducer.add_second(0)
        reducer.add_first(2)
        second_sum.step(2)
        reducer.add_second(1)
        reducer.add_first(3)
        second_sum.step(3)
        reducer.add_second(2)
        reducer.add_second(3)
        first_sum.finish(total_ref)
        z_sum.finish(early_ref)
        reducer.finish(late_ref)
        second_sum.finish(scale_ref)
    for copy in gathers():
        copy.wait_recv()
    glob_out[...] = every[:count].astype(F32)
    for copy in gathers():
        copy.wait_send()


def last_part(sizes, planned, long_x, glob_x, dq, dk, dv, dmid, *weights):
    block, count, quarter, seq_count, pairs = sizes
    rows, width = dq.shape
    others = seq_count - 1
    whole = pl.BlockSpec(memory_space=pltpu.VMEM)
    shape = jax.ShapeDtypeStruct
    sums = [shape(((2 * pairs + 2 + 7) // 8 * 8, width), F32), shape((8, width), F32)]
    outs = [shape((block, width), F32), shape((count, width), F32)]
    scratch = [
        pltpu.VMEM((width, rows), BF16),
        pltpu.VMEM((GP, width), BF16),
        pltpu.SemaphoreType.DMA((others,)),
        pltpu.SemaphoreType.DMA((others,)),
    ]
    if planned:
        piece = width // 32
        part = 3 * piece + 8
        early = weights[-1].shape[1:]
        outs += [shape((part, width), F32), *sums, shape(early, F32)]
        for part_sums in sums:
            scratch += EverySum.scratch(*part_sums.shape)
        scratch += ZSum.scratch(*early) + Reducer.scratch(part, width, 2, with_z=True)
    else:
        outs += [shape((width, width), BF16)] * 3 + sums
    return pl.pallas_call(
        functools.partial(late_kernel, sizes, planned),
        in_specs=[whole] * 12 + [pl.BlockSpec(memory_space=pl.ANY)] * planned,
        out_specs=[whole] * len(outs),
        out_shape=outs,
        scratch_shapes=scratch,
        compiler_params=pltpu.CompilerParams(
            collective_id=2, has_side_effects=True, vmem_limit_bytes=60 * 2**20
        ),
        name="last_part",
    )(long_x, glob_x, dq, dk, dv, dmid, *weights)


def small_kernel(heads, early_ref, late_ref, outer_ref, inner_ref, sums_ref, scale_ref, *rest):
    outs = rest[4:-4]
    for source, out in zip(rest[:3], rest[-4:]):
        out[...] = source[...]
    rest[-1][...] = rest[3][...].reshape(rest[-1].shape)
    g_query, g_key, g_value, g_out, g_inner, g_outer, *vectors, table = outs
    device = lax.axis_index("dp") * lax.axis_size("seq") + lax.axis_index("seq")
    piece, width = g_query.shape
    for at, out in enumerate((g_query, g_key, g_value)):
        out[...] = late_ref[at * piece : (at + 1) * piece]
    g_out[...] = early_ref[2 * piece : 3 * piece]
    g_outer[...] = outer_ref[...]
    for source, first, chunk in (
        (inner_ref, 0, 0),
        (inner_ref, piece, 3),
        (early_ref, 0, 1),
        (early_ref, piece, 2),
    ):
        g_inner[:, chunk * width : (chunk + 1) * width] = source[first : first + piece]

    def entries(row, at, length):
        return pltpu.roll(row, width - at * length, 1)[0, :length]

    b_query, b_value, b_out, b_outer, gain_one, shift_one, gain_two, shift_two, b_inner = vectors
    for at, out in enumerate((b_query, b_value)):
        out[...] = entries(sums_ref[heads + at : heads + at + 1], device, piece)
    for at, out in enumerate((gain_one, shift_one)):
        out[...] = entries(scale_ref[at : at + 1], device, piece)
    for at, out in enumerate((b_out, b_outer, gain_two, shift_two)):
        row = 3 * piece + at
        out[...] = entries(early_ref[row : row + 1], device, piece)
    row = pl.ds(3 * piece + 4 + lax.div(device, 8), 1)
    b_inner[...] = entries(early_ref[row], lax.rem(device, 8), 4 * piece)
    labels = table.shape[1]
    turned = pltpu.roll(sums_ref[:, :WINDOW], WINDOW - HALO + R, 1)
    table[...] = turned[:heads, :labels]


def small_results(heads, early, late, outer, inner, sums, scales, *big):
    width = early.shape[1]
    piece = width // 32
    shape = jax.ShapeDtypeStruct
    whole = pl.BlockSpec(memory_space=pltpu.VMEM)
    outs = [shape((piece, width), F32)] * 4
    outs += [shape((piece, 4 * width), F32), shape((4 * piece, width), F32)]
    outs += [shape((piece,), F32)] * 8 + [shape((4 * piece,), F32)]
    outs += [shape((heads, 2 * R + 1), F32)]
    outs += [shape(part.shape, part.dtype) for part in big[:3]]
    outs.append(shape((big[3].shape[0], 1, width), F32))
    return pl.pallas_call(
        functools.partial(small_kernel, heads),
        in_specs=[whole] * 10,
        out_specs=[whole] * len(outs),
        out_shape=outs,
        name="small_results",
    )(early, late, outer, inner, sums, scales, *big)


def has_plan():
    return (lax.axis_size("dp"), lax.axis_size("seq")) == (8, 4)


GELU_A = 0.7978845608028654
GELU_B = 0.044715


def gate_both(u):
    square = u * u
    turned = jnp.tanh(GELU_A * u * (1.0 + GELU_B * square))
    half = 0.5 * (1.0 + turned)
    slope = half + 0.5 * u * (1.0 - turned * turned) * (
        GELU_A * (1.0 + 3.0 * GELU_B * square)
    )
    return u * half, slope


def column_sum(rows):
    return jnp.sum(rows, 0, keepdims=True)


def ffn_kernel(
    sizes,
    planned,
    len_ref,
    attn_ref,
    long_ref,
    glob_ref,
    dlong_ref,
    dglob_ref,
    lq_ref,
    wo_ref,
    bo_ref,
    gain_ref,
    shift_ref,
    wi_ref,
    bi_ref,
    wr_ref,
    br_ref,
    long_out,
    glob_out,
    dmid_ref,
    do_ref,
    dog_ref,
    ldg_ref,
    *rest,
):
    block, count, quarter, seq_count, pairs = sizes
    if planned:
        pieces_ref, outer_ref, inner_ref, *rest = rest
    else:
        g_outer_ref, g_inner_ref, g_out_ref, vec_ref, *rest = rest
    (
        mid,
        y_sum,
        df_sum,
        normed,
        normed_t,
        dy,
        vectors,
        biases,
        every_do,
        every_ld,
        gather_sends,
        gather_recvs,
        *rest,
    ) = rest
    if planned:
        even, *rest = rest
        outer = Reducer(rest[0].shape[-2], 48, rest[:7], order=chunk_of, parts=outer_ref)
        inner = Reducer(rest[7].shape[-2], 16, rest[7:], parts=inner_ref)
    step = pl.program_id(0)
    chunk = chunk_of(step)
    seq_index = lax.axis_index("seq")
    own_rows = pl.ds(pl.multiple_of(seq_index * quarter, quarter), quarter)
    width = mid.shape[1]
    piece = width // 32

    def rows_of(device):
        return pl.ds(pl.multiple_of(device[1] * quarter, quarter), quarter)

    def gather(owner, device, at):
        for kind, every in enumerate((every_do, every_ld)):
            yield pltpu.make_async_remote_copy(
                src_ref=every.at[rows_of(owner)],
                dst_ref=every.at[rows_of(owner)],
                send_sem=gather_sends.at[kind, at],
                recv_sem=gather_recvs.at[kind, at],
                device_id=device,
                device_id_type=pl.DeviceIdType.MESH,
            )

    me = seq_device(0, seq_count)
    if planned:
        sibling, across = outer.partners()[:2]
        first_gathers = [(me, across, 0), (me, sibling, 1)]
        second_gathers = [(across, sibling, 2)]
    else:
        first_gathers = [
            (me, seq_device(at + 1, seq_count), at) for at in range(seq_count - 1)
        ]
        second_gathers = []

    def act(now):
        if planned:
            for at, reducer, name, part in FFN_PLAN:
                if at == now:
                    getattr((outer, inner)[reducer], name)(part)

    def act_in_step(point):
        if planned:
            for now in range(4):
                if any(at == (now, point) for at, _, _, _ in FFN_PLAN):

                    @pl.when(step == now)
                    def _(now=now):
                        act((now, point))

    @pl.when(step == 0)
    def _():
        others = [seq_device(seq_step, seq_count) for seq_step in range(1, seq_count)]
        meet(others + (outer.partners()[2:] if planned else []))
        projected = dot_n(attn_ref[...], wo_ref[...]) + bo_ref[...]
        mid[:block] = long_ref[...].astype(F32) + projected[:block]
        mid[block:] = glob_ref[own_rows].astype(F32) + projected[block:]
        hat, _ = row_norm(mid[...])
        normed[...] = (hat * gain_ref[...] + shift_ref[...]).astype(BF16)
        normed_t[...] = normed[...].T
        position = seq_index * block + lax.broadcasted_iota(jnp.int32, (block, 1), 0)
        dy[:block] = jnp.where(
            position < len_ref[0], dlong_ref[...].astype(F32), 0.0
        ).astype(BF16)
        y_sum[:GP] = jnp.zeros((GP, width), F32)
        y_sum[:count] = dglob_ref[...].astype(F32)
        dy[block:] = y_sum[own_rows].astype(BF16)
        vectors[1:2] = column_sum(dy[...].astype(F32))
        y_sum[...] = mid[...] + br_ref[...]
        df_sum[...] = jnp.zeros_like(df_sum)
        for at in range(4):
            biases[at] = bi_ref[at * width : (at + 1) * width].reshape(1, width)

    act_in_step(0)
    active, slope = gate_both(dot_n(normed[...], wi_ref[...]) + biases[chunk])
    active = active.astype(BF16)
    g_outer = t_dot(active, dy[...])
    if planned:
        for at in range(8):
            outer.fill(chunk, at, g_outer[at * 4 * piece : (at + 1) * 4 * piece])
        outer.start(step)
    else:
        g_outer_ref[...] = g_outer.astype(BF16)
    y_sum[...] += dot_n(active, wr_ref[...])
    hidden = dot_t(dy[...], wr_ref[...]) * slope
    for at in range(4):

        @pl.when(chunk == at)
        def _(at=at):
            vectors[4 + at : 5 + at] = column_sum(hidden)

    hidden = hidden.astype(BF16)
    act_in_step(1)
    df_sum[...] += dot_t(hidden, wi_ref[...])
    g_inner = dot_n(normed_t[...], hidden)
    if planned:

        @pl.when(lax.rem(step, 2) == 0)
        def _():
            even[...] = g_inner

        def halves(at):
            part = slice(at * piece, (at + 1) * piece)
            return jnp.concatenate([even[part], g_inner[part]], 0)

        @pl.when(step == 1)
        def _():
            for at in range(32):
                inner.fill(at // 8, at % 8, halves(at))
            for part in range(4):
                inner.start(part)

        @pl.when(step == 3)
        def _():
            for at in range(32):
                pieces_ref[at % 2, at // 8, at // 4 % 2, at // 2 % 2, : 2 * piece] = halves(
                    at
                ).astype(BF16)

    else:
        g_inner_ref[...] = g_inner.astype(BF16)

    def norm_back(rows):
        hat, inverse = row_norm(mid[rows])
        df = df_sum[rows]
        scaled = df * gain_ref[...]
        dmid = dy[rows].astype(F32) + inverse * (
            scaled
            - jnp.mean(scaled, -1, keepdims=True)
            - hat * jnp.mean(scaled * hat, -1, keepdims=True)
        )
        dmid_ref[rows] = dmid
        low = dmid.astype(BF16)
        grad_o = dot_t(low, wo_ref[...]).astype(BF16)
        do_ref[rows] = grad_o
        return [column_sum(dmid), column_sum(df * hat), column_sum(df)], low, grad_o

    @pl.when(step == 3)
    def _():
        glob_sums, glob_low, grad_o = norm_back(slice(block, block + quarter))
        every_do[own_rows] = grad_o
        both = grad_o.astype(F32) * attn_ref[block:].astype(F32)
        stats = lq_ref[...]
        for head in range(2 * pairs):
            lanes = slice(head // 2 * PAIR, head // 2 * PAIR + PAIR)
            delta = jnp.sum(own_half(head % 2, both[:, lanes]), -1, keepdims=True)
            stats = jnp.where(lane_index() == HD + head, delta, stats)
        every_ld[own_rows] = stats
        for part in first_gathers:
            for copy in gather(*part):
                copy.start()
        glob_out[...] = y_sum[block:].astype(BF16)
        act((4, 0))
        position = seq_index * block + lax.broadcasted_iota(jnp.int32, (block, 1), 0)
        long_out[...] = jnp.where(position < len_ref[0], y_sum[:block], 0.0).astype(BF16)
        long_sums, long_low, _ = norm_back(slice(0, block))
        for at, one, two in zip((0, 2, 3), long_sums, glob_sums):
            vectors[at : at + 1] = one + two
        if planned:
            for copy in gather(*first_gathers[0]):
                copy.wait_recv()
            for copy in gather(*second_gathers[0]):
                copy.start()
        act((4, 1))
        g_out = t_dot(attn_ref[...], jnp.concatenate([long_low, glob_low], 0))
        if planned:
            for at in range(32):
                pieces_ref[at % 2, at // 8, at // 4 % 2, at // 2 % 2, 2 * piece :] = (
                    jnp.concatenate(
                        [g_out[at * piece : (at + 1) * piece], vectors[...]], 0
                    ).astype(BF16)
                )
            act((4, 2))
            outer.finish()
            inner.finish()
        else:
            g_out_ref[...] = g_out.astype(BF16)
            vec_ref[...] = vectors[...]
        for part in (first_gathers[1:] if planned else first_gathers) + second_gathers:
            for copy in gather(*part):
                copy.wait_recv()
        dog_ref[...] = every_do[...]
        ldg_ref[...] = every_ld[...]
        for part in first_gathers + second_gathers:
            for copy in gather(*part):
                copy.wait_send()


OUTER, INNER = 0, 1
FFN_PLAN = (
    ((1, 0), OUTER, "add_core", 0),
    ((2, 0), OUTER, "add_core", 1),
    ((2, 0), OUTER, "add_first", 0),
    ((2, 1), INNER, "add_core", 0),
    ((2, 1), INNER, "add_core", 1),
    ((2, 1), INNER, "add_core", 2),
    ((2, 1), INNER, "add_core", 3),
    ((3, 0), OUTER, "add_first", 1),
    ((3, 0), OUTER, "add_second", 0),
    ((3, 0), OUTER, "add_core", 2),
    ((4, 0), OUTER, "add_core", 3),
    ((4, 0), INNER, "add_first", 0),
    ((4, 0), INNER, "add_first", 1),
    ((4, 0), OUTER, "add_first", 2),
    ((4, 0), OUTER, "add_second", 1),
    ((4, 1), INNER, "add_first", 2),
    ((4, 1), INNER, "add_first", 3),
    ((4, 1), INNER, "add_second", 0),
    ((4, 1), INNER, "add_second", 1),
    ((4, 2), OUTER, "add_first", 3),
    ((4, 2), OUTER, "add_second", 2),
    ((4, 2), INNER, "add_second", 2),
    ((4, 2), INNER, "add_second", 3),
    ((4, 2), OUTER, "add_second", 3),
)


def chunk_of(step):
    return jnp.where(step == 0, 0, jnp.where(step == 1, 3, step - 1))


def feed_forward(sizes, planned, doc_len, attn, long_x, glob_x, dlong, dglob, lq, *weights):
    block, count, quarter, seq_count, pairs = sizes
    wo, bo, gain, shift, wi, bi, wr, br = weights
    width, hidden = wi.shape
    chunk = hidden // 4
    rows = block + quarter
    whole = pl.BlockSpec(memory_space=pltpu.VMEM)
    shape = jax.ShapeDtypeStruct
    in_specs = [pl.BlockSpec(memory_space=pltpu.SMEM)] + [whole] * 10
    in_specs += [
        pl.BlockSpec((width, chunk), lambda c: (0, chunk_of(c))),
        whole,
        pl.BlockSpec((chunk, width), lambda c: (chunk_of(c), 0)),
        whole,
    ]
    outs = [
        shape((block, width), BF16),
        shape((quarter, width), BF16),
        shape((rows, width), F32),
        shape((rows, width), BF16),
        shape((GP, width), BF16),
        shape((GP, PAIR), F32),
    ]
    out_specs = [whole] * 6
    others = seq_count - 1
    scratch = [
        pltpu.VMEM((rows, width), F32),
        pltpu.VMEM((rows, width), F32),
        pltpu.VMEM((rows, width), F32),
        pltpu.VMEM((rows, width), BF16),
        pltpu.VMEM((width, rows), BF16),
        pltpu.VMEM((rows, width), BF16),
        pltpu.VMEM((8, width), F32),
        pltpu.VMEM((4, 1, chunk), F32),
        pltpu.VMEM((GP, width), BF16),
        pltpu.VMEM((GP, PAIR), F32),
        pltpu.SemaphoreType.DMA((2, others)),
        pltpu.SemaphoreType.DMA((2, others)),
    ]
    if planned:
        part, piece = hidden // 32, width // 32
        outs += [
            shape((2, 4, 2, 2, 3 * piece + 8, width), BF16),
            shape((4, part, width), BF16),
            shape((4, 2 * piece, width), BF16),
        ]
        out_specs += [whole] * 3
        scratch += [
            pltpu.VMEM((width, chunk), F32),
        ]
        scratch += Reducer.scratch(part, width, 2) + Reducer.scratch(2 * piece, width, 2)
    else:
        outs += [
            shape((hidden, width), BF16),
            shape((width, hidden), BF16),
            shape((width, width), BF16),
            shape((8, width), F32),
        ]
        out_specs += [
            pl.BlockSpec((chunk, width), lambda c: (chunk_of(c), 0)),
            pl.BlockSpec((width, chunk), lambda c: (0, chunk_of(c))),
            whole,
            whole,
        ]
    return pl.pallas_call(
        functools.partial(ffn_kernel, sizes, planned),
        grid=(4,),
        in_specs=in_specs,
        out_specs=out_specs,
        out_shape=outs,
        scratch_shapes=scratch,
        compiler_params=pltpu.CompilerParams(
            collective_id=4, has_side_effects=True, vmem_limit_bytes=62 * 2**20
        ),
        name="feed_forward",
    )(doc_len, attn, long_x, glob_x, dlong, dglob, lq, wo, bo, gain, shift, wi, bi, wr, br)


def back_kernel(
    sizes,
    early_rows,
    len_ref,
    tab_ref,
    q_ref,
    kx_ref,
    vx_ref,
    kg_ref,
    vg_ref,
    o_ref,
    do_ref,
    l_ref,
    dog_ref,
    ldg_ref,
    yq_ref,
    *rest,
):
    block, count, quarter, seq_count, pairs = sizes
    reduces = early_rows > 0
    if reduces:
        pieces_ref, outer_parts, inner_parts, *rest = rest
    dq_ref, dk_ref, dv_ref, dtab_ref, glob_out, *rest = rest
    if reduces:
        early_parts, outer_ref, inner_ref, *rest = rest
    (
        dkx,
        dvx,
        dkg,
        dvg,
        q_send,
        q_recv,
        kv_send,
        kv_recv,
        halo_send,
        halo_recv,
        glob_sends,
        glob_recvs,
        halo_sends,
        halo_recvs,
        every,
        gather_sends,
        gather_recvs,
        *rest,
    ) = rest
    number = pl.program_id(0)
    steps = pairs // 2
    first_pair = 2 * lax.rem(number, steps)
    seq_index = lax.axis_index("seq")
    if reduces:
        reducer = Reducer(early_rows, 16, rest[:7], pieces=pieces_ref, parts=early_parts)
        z_sums = (
            (ZSum(outer_parts, rest[7:12]), outer_ref),
            (ZSum(inner_parts, rest[12:]), inner_ref),
        )
    scale = HD ** (-0.5)
    low_lanes = lane_index() < HD
    own_keys = slice(HALO, HALO + block)
    own_rows = pl.ds(pl.multiple_of(seq_index * quarter, quarter), quarter)

    def glob_copies(kind, at):
        source, dest = ((q_send, q_recv), (kv_send, kv_recv))[kind]
        for step in range(1, seq_count):
            device = seq_device(step, seq_count)
            yield pltpu.make_async_remote_copy(
                src_ref=source.at[device[1], at],
                dst_ref=dest.at[step - 1, at],
                send_sem=glob_sends.at[kind, step - 1, at],
                recv_sem=glob_recvs.at[kind, step - 1, at],
                device_id=device,
                device_id_type=pl.DeviceIdType.MESH,
            )

    def gathers():
        for step in range(1, seq_count):
            yield pltpu.make_async_remote_copy(
                src_ref=every.at[own_rows],
                dst_ref=every.at[own_rows],
                send_sem=gather_sends.at[step - 1],
                recv_sem=gather_recvs.at[step - 1],
                device_id=seq_device(step, seq_count),
                device_id_type=pl.DeviceIdType.MESH,
            )

    def halo_copy(direction, at):
        return pltpu.make_async_remote_copy(
            src_ref=halo_send.at[direction, at],
            dst_ref=halo_recv.at[direction, at],
            send_sem=halo_sends.at[direction, at],
            recv_sem=halo_recvs.at[direction, at],
            device_id=seq_device(2 * direction - 1, seq_count),
            device_id_type=pl.DeviceIdType.MESH,
        )

    has_low, has_high = seq_index > 0, seq_index < seq_count - 1
    sends_to = (has_low, has_high)
    gets_from = (has_high, has_low)

    def close_pair(at):
        lanes = lanes_of(at)
        for direction in range(2):

            @pl.when(gets_from[direction])
            def _(direction=direction):
                halo_copy(direction, at).wait_recv()

        for kind, (total, out) in enumerate(((dkx, dk_ref), (dvx, dv_ref))):
            first, last = HALO + REACH, HALO + block - REACH
            out[:REACH, lanes] = (
                total[at, HALO:first] + halo_recv[1, at, kind].astype(F32)
            ).astype(BF16)
            out[REACH : block - REACH, lanes] = total[at, first:last].astype(BF16)
            out[block - REACH : block, lanes] = (
                total[at, last : HALO + block] + halo_recv[0, at, kind].astype(F32)
            ).astype(BF16)
        sums = []
        for kind, (source, dest) in enumerate(((q_send, q_recv), (kv_send, kv_recv))):
            total = source[seq_index, at].astype(F32)
            for step, copy in enumerate(glob_copies(kind, at)):
                copy.wait_recv()
                total += dest[step, at].astype(F32)
            sums.append(total.astype(BF16))
        dq_ref[block:, lanes] = sums[0]
        dk_ref[block:, lanes] = sums[1][:, :PAIR]
        dv_ref[block:, lanes] = sums[1][:, PAIR:]

    def run_plan(now):
        for at, act, chunk in EARLY_PLAN:
            if now == at:
                getattr(reducer, act)(chunk)

    @pl.when(number == 0)
    def _():
        others = [seq_device(step, seq_count) for step in range(1, seq_count)]
        meet(others + (reducer.partners()[2:] if reduces else []))
        if reduces:
            for chunk in range(4):
                reducer.start(chunk)
            for z_sum, _ in z_sums:
                z_sum.start()
        every[own_rows] = yq_ref[...]
        for copy in gathers():
            copy.start()
        for direction in range(2):

            @pl.when(jnp.logical_not(gets_from[direction]))
            def _(direction=direction):
                halo_recv[direction] = jnp.zeros_like(halo_recv[direction])

    if reduces:
        for now in range(1, 2 * steps):
            if any(at == now for at, _, _ in EARLY_PLAN):

                @pl.when(number == now)
                def _(now=now):
                    run_plan(now)

    def glob_pair(pair, q_ref, kx_ref, vx_ref, kg_ref, vg_ref, dog_ref):
        long_bias = key_bias(seq_index * block, block, len_ref[0])
        near_bias = key_bias(seq_index * quarter, quarter, count)
        query = q_ref[block:] * jnp.asarray(scale, BF16)
        grad_o = dog_ref[...]
        far_k, far_v = kx_ref[own_keys], vx_ref[own_keys]
        near_k, near_v = kg_ref[own_rows], vg_ref[own_rows]
        outs, kept = [], []
        for head in range(2):
            norm = in_three(-pick_column(ldg_ref[...], 2 * pair + head))
            delta = in_three(-pick_column(ldg_ref[...], HD + 2 * pair + head))
            qa = with_lanes(head, query, (1.0,) + norm)
            doa = with_lanes(head, grad_o, delta)
            far = jnp.exp(dot_t(qa, key_side(head, far_k, long_bias)))
            near = jnp.exp(dot_t(qa, key_side(head, near_k, near_bias)))
            far_ds = (far * dot_t(doa, value_side(head, far_v))).astype(BF16)
            near_ds = (near * dot_t(doa, value_side(head, near_v))).astype(BF16)
            outs.append(dot_n(far_ds, far_k) + dot_n(near_ds, near_k))
            kept.append(
                (
                    own_half(head, query),
                    own_half(head, grad_o),
                    far.astype(BF16),
                    near.astype(BF16),
                    far_ds,
                    near_ds,
                )
            )
        own_q, own_do, far, near, far_ds, near_ds = (
            jnp.concatenate(part, 0) for part in zip(*kept)
        )
        for total, edge in ((dkx, own_keys), (dvx, own_keys)):
            total[pair, :HALO] = jnp.zeros((HALO, PAIR), F32)
            total[pair, HALO + block :] = jnp.zeros((HALO, PAIR), F32)
        dkx[pair, own_keys] = t_dot(far_ds, own_q)
        dvx[pair, own_keys] = t_dot(far, own_do)
        dkg[pair] = jnp.zeros((GP, PAIR), F32)
        dvg[pair] = jnp.zeros((GP, PAIR), F32)
        dkg[pair, own_rows] = t_dot(near_ds, own_q)
        dvg[pair, own_rows] = t_dot(near, own_do)
        glob_dq = (jnp.where(low_lanes, outs[0], outs[1]) * scale).astype(BF16)
        q_send[:, pair] = glob_dq.reshape(seq_count, quarter, PAIR)
        for copy in glob_copies(0, pair):
            copy.start()

    def long_pair(pair, q_ref, kx_ref, vx_ref, kg_ref, vg_ref, o_ref, do_ref, tab_ref):
        long_bias = key_bias(seq_index * block - HALO, block + 2 * HALO, len_ref[0])
        glob_bias = key_bias(0, GP, count)
        query = q_ref[:block] * jnp.asarray(scale, BF16)
        grad_o = do_ref[...]
        both = grad_o.astype(F32) * o_ref[...].astype(F32)
        heads = []
        for head in range(2):
            norm = in_three(-pick_column(l_ref[...], 2 * pair + head))
            delta = in_three(-jnp.sum(own_half(head, both), -1, keepdims=True))
            heads.append(
                dict(
                    q=own_half(head, query),
                    do=own_half(head, grad_o),
                    qa=with_lanes(head, query, (1.0,) + norm),
                    doa=with_lanes(head, grad_o, delta),
                    kxa=key_side(head, kx_ref[...], long_bias),
                    vxa=value_side(head, vx_ref[...]),
                    kga=key_side(head, kg_ref[...], glob_bias),
                    vga=value_side(head, vg_ref[...]),
                    bias=band_bias(tab_ref[0, head : head + 1]),
                )
            )
        table_sums = [0.0, 0.0]
        grads_q = []
        for start in range(0, block, SUB):
            rows, keys = slice(start, start + SUB), slice(start, start + WINDOW)
            outs, probs, grads = [], [], []
            for head, own in enumerate(heads):
                band = jnp.exp(dot_t(own["qa"][rows], own["kxa"][keys]) + own["bias"])
                band_ds = band * dot_t(own["doa"][rows], own["vxa"][keys])
                table_sums[head] += band_ds
                glob = jnp.exp(dot_t(own["qa"][rows], own["kga"]))
                glob_ds = (glob * dot_t(own["doa"][rows], own["vga"])).astype(BF16)
                band_ds = band_ds.astype(BF16)
                outs.append(dot_n(band_ds, kx_ref[keys]) + dot_n(glob_ds, kg_ref[...]))
                probs.append((band.astype(BF16), glob.astype(BF16)))
                grads.append((band_ds, glob_ds))
            grads_q.append(jnp.where(low_lanes, outs[0], outs[1]))
            own_q = jnp.concatenate([own["q"][rows] for own in heads], 0)
            own_do = jnp.concatenate([own["do"][rows] for own in heads], 0)
            band, glob = (jnp.concatenate(part, 0) for part in zip(*probs))
            band_ds, glob_ds = (jnp.concatenate(part, 0) for part in zip(*grads))
            dkx[pair, keys] += t_dot(band_ds, own_q)
            dvx[pair, keys] += t_dot(band, own_do)
            dkg[pair] += t_dot(glob_ds, own_q)
            dvg[pair] += t_dot(glob, own_do)
        for kind, total in enumerate((dkg, dvg)):
            kv_send[:, pair, :, kind * PAIR : (kind + 1) * PAIR] = (
                total[pair].astype(BF16).reshape(seq_count, quarter, PAIR)
            )
        for copy in glob_copies(1, pair):
            copy.start()
        for kind, total in enumerate((dkx, dvx)):
            for direction, first in enumerate((HALO - REACH, HALO + block)):
                halo_send[direction, pair, kind] = total[pair, first : first + REACH].astype(BF16)
        for direction in range(2):

            @pl.when(sends_to[direction])
            def _(direction=direction):
                halo_copy(direction, pair).start()

        dq_ref[:block, lanes_of(pair)] = (jnp.concatenate(grads_q, 0) * scale).astype(BF16)
        for head in range(2):
            dtab_ref[pair, head : head + 1] = diagonal_sums(table_sums[head])

    def part(at, *refs):
        return [ref.at[:, at * PAIR : (at + 1) * PAIR] for ref in refs]

    @pl.when(number < steps)
    def _():
        for at in range(2):
            glob_pair(
                first_pair + at, *part(at, q_ref, kx_ref, vx_ref, kg_ref, vg_ref, dog_ref)
            )

    @pl.when(number >= steps)
    def _():
        for at in range(2):
            long_pair(
                first_pair + at,
                *part(at, q_ref, kx_ref, vx_ref, kg_ref, vg_ref, o_ref, do_ref),
                tab_ref.at[at : at + 1],
            )

    @pl.when(number > steps)
    def _():
        close_pair(first_pair - 2)
        close_pair(first_pair - 1)

    @pl.when(number == 2 * steps - 1)
    def _():
        if reduces:
            run_plan(2 * steps)
        close_pair(pairs - 2)
        close_pair(pairs - 1)
        for at in range(pairs):
            for kind in range(2):
                for copy in glob_copies(kind, at):
                    copy.wait_send()
            for direction in range(2):

                @pl.when(sends_to[direction])
                def _(direction=direction, at=at):
                    halo_copy(direction, at).wait_send()

        for copy in gathers():
            copy.wait_recv()
        glob_out[...] = every[:count]
        for copy in gathers():
            copy.wait_send()
        if reduces:
            reducer.finish()
            for z_sum, out in z_sums:
                z_sum.finish(out)


def attend_back(sizes, doc_len, table, q, kx, vx, kg, vg, o, do, l, dog, ldg, yq, *sums):
    block, count, quarter, seq_count, pairs = sizes
    width = q.shape[1]
    early_rows = sums[0].shape[-2] if sums else 0
    ext = block + 2 * HALO
    steps = pairs // 2
    cols = lambda rows: pl.BlockSpec((rows, 2 * PAIR), lambda i: (0, lax.rem(i, steps)))
    whole = pl.BlockSpec(memory_space=pltpu.VMEM)
    shape = jax.ShapeDtypeStruct
    in_specs = [
        pl.BlockSpec(memory_space=pltpu.SMEM),
        pl.BlockSpec((2, 2, WINDOW), lambda i: (lax.rem(i, steps), 0, 0)),
        cols(block + GP),
        cols(ext),
        cols(ext),
        cols(GP),
        cols(GP),
        cols(block),
        cols(block),
        whole,
        cols(GP),
        whole,
        whole,
    ]
    rows = block + quarter
    outs = [shape((rows, width), BF16)] * 3 + [shape((pairs, 2, WINDOW), F32)]
    outs.append(shape((count, width), BF16))
    others = seq_count - 1
    scratch = [
        pltpu.VMEM((pairs, ext, PAIR), F32),
        pltpu.VMEM((pairs, ext, PAIR), F32),
        pltpu.VMEM((pairs, GP, PAIR), F32),
        pltpu.VMEM((pairs, GP, PAIR), F32),
        pltpu.VMEM((seq_count, pairs, quarter, PAIR), BF16),
        pltpu.VMEM((others, pairs, quarter, PAIR), BF16),
        pltpu.VMEM((seq_count, pairs, quarter, 2 * PAIR), BF16),
        pltpu.VMEM((others, pairs, quarter, 2 * PAIR), BF16),
        pltpu.VMEM((2, pairs, 2, REACH, PAIR), BF16),
        pltpu.VMEM((2, pairs, 2, REACH, PAIR), BF16),
        pltpu.SemaphoreType.DMA((2, others, pairs)),
        pltpu.SemaphoreType.DMA((2, others, pairs)),
        pltpu.SemaphoreType.DMA((2, pairs)),
        pltpu.SemaphoreType.DMA((2, pairs)),
        pltpu.VMEM((GP, width), BF16),
        pltpu.SemaphoreType.DMA((others,)),
        pltpu.SemaphoreType.DMA((others,)),
    ]
    args = [doc_len, table, q, kx, vx, kg, vg, o, do, l, dog, ldg, yq, *sums]
    if early_rows:
        in_specs += [pl.BlockSpec(memory_space=pl.ANY)] * 3
        outs.append(shape((4, early_rows, width), BF16))
        scratch += Reducer.scratch(early_rows, width, 1)
        for parts in sums[1:]:
            outs.append(shape(parts.shape[1:], F32))
            scratch += ZSum.scratch(*parts.shape[1:])
    return pl.pallas_call(
        functools.partial(back_kernel, sizes, early_rows),
        grid=(2 * steps,),
        in_specs=in_specs,
        out_specs=[whole] * len(outs),
        out_shape=outs,
        scratch_shapes=scratch,
        compiler_params=pltpu.CompilerParams(
            collective_id=1, has_side_effects=True, vmem_limit_bytes=60 * 2**20
        ),
        name="attend_back",
    )(*args)


def on_device(
    long_input,
    global_input,
    lengths,
    w_query,
    b_query,
    w_key,
    w_value,
    b_value,
    w_out,
    b_out,
    w_inner,
    b_inner,
    w_outer,
    b_outer,
    norm1_gain,
    norm1_shift,
    norm2_gain,
    norm2_shift,
    rel_table,
    long_cotangent,
    global_cotangent,
):
    seq_count = lax.axis_size("seq")
    data_count = lax.axis_size("dp")
    seq_index = lax.axis_index("seq")
    block = long_input.shape[1]
    count = global_input.shape[1]
    width = long_input.shape[2]
    heads = rel_table.shape[1]
    pairs = heads // 2
    labels = 2 * R + 1
    quarter = GP // seq_count
    sizes = Sizes(block, count, quarter, seq_count, pairs)
    queries, kx, vx, kg, vg, attn_low, long_l, glob_l, glob_x, table = attend(
        sizes,
        lengths,
        rel_table.T,
        long_input[0],
        global_input[0],
        w_query,
        w_key,
        w_value,
        b_query,
        b_value,
        norm1_gain,
        norm1_shift,
    )
    planned = has_plan()
    long_result, own_out, grad_mid, grad_attn, every_do, every_ld, *gradients = feed_forward(
        sizes,
        planned,
        lengths,
        attn_low,
        long_input[0],
        glob_x,
        long_cotangent[0],
        global_cotangent[0],
        glob_l,
        w_out,
        b_out,
        norm2_gain,
        norm2_shift,
        w_inner,
        b_inner,
        w_outer,
        b_outer,
    )
    query_low, key_low, value_low, dtab, glob_out, *early = attend_back(
        sizes,
        lengths,
        table,
        queries,
        kx,
        vx,
        kg,
        vg,
        attn_low,
        grad_attn,
        long_l,
        every_do,
        every_ld,
        own_out,
        *(gradients if planned else []),
    )
    long_grad, glob_grad, *late = last_part(
        sizes,
        planned,
        long_input[0],
        glob_x,
        query_low,
        key_low,
        value_low,
        grad_mid,
        w_query,
        w_key,
        w_value,
        norm1_gain,
        norm1_shift,
        dtab,
        *early[:1],
    )
    if planned:
        (
            g_query,
            g_key,
            g_value,
            g_out,
            g_inner,
            g_outer,
            g_b_query,
            g_b_value,
            g_b_out,
            g_b_outer,
            g_g1,
            g_s1,
            g_g2,
            g_s2,
            g_b_inner,
            table_total,
            long_grad,
            long_result,
            glob_out,
            glob_grad,
        ) = small_results(
            heads,
            late[3],
            late[0],
            early[1],
            early[2],
            late[1],
            late[2],
            long_grad,
            long_result,
            glob_out,
            glob_grad,
        )
        table_total = table_total.T
        glob_grad = glob_grad.reshape(count, width)
    else:
        devices = data_count * seq_count
        own_part = lambda vector: lax.dynamic_slice_in_dim(
            vector,
            (lax.axis_index("dp") * seq_count + seq_index) * (vector.shape[0] // devices),
            vector.shape[0] // devices,
        )
        g_outer, g_inner, g_out, vectors = gradients
        g_outer, g_inner, g_out, g_query, g_key, g_value = (
            lax.psum_scatter(g.astype(BF16), ("dp", "seq"), scatter_dimension=0, tiled=True).astype(
                F32
            )
            for g in (g_outer, g_inner, g_out, *late[:3])
        )
        vectors, sums, scales = lax.psum((vectors, *late[3:]), ("dp", "seq"))
        g_b_query, g_b_value = (own_part(sums[heads + i]) for i in range(2))
        g_g1, g_s1 = (own_part(scales[i]) for i in range(2))
        g_b_out, g_b_outer, g_g2, g_s2 = (own_part(vectors[i]) for i in range(4))
        g_b_inner = own_part(vectors[4:].reshape(-1))
        table_total = sums[:heads, HALO - R : HALO - R + labels].T
    return (
        long_result[None],
        glob_out[None],
        long_grad[None],
        glob_grad[None],
        g_query,
        g_b_query,
        g_key,
        g_value,
        g_b_value,
        g_out,
        g_b_out,
        g_inner,
        g_b_inner,
        g_outer,
        g_b_outer,
        g_g1,
        g_s1,
        g_g2,
        g_s2,
        table_total,
    )


def solution(mesh):
    rows, whole = P("dp", "seq", None), P("dp", None, None)
    matrix, vector = P(("dp", "seq"), None), P(("dp", "seq"))
    return jax.shard_map(
        on_device,
        mesh=mesh,
        in_specs=(rows, whole, P("dp")) + (P(),) * 16 + (rows, whole),
        out_specs=(
            rows,
            whole,
            rows,
            whole,
            matrix,
            vector,
            matrix,
            matrix,
            vector,
            matrix,
            vector,
            matrix,
            vector,
            matrix,
            vector,
            vector,
            vector,
            vector,
            vector,
            P(),
        ),
        check_vma=False,
    )
```

```python
import functools
from typing import NamedTuple

import jax
import jax.numpy as jnp
from jax import lax
from jax.experimental import pallas as pl
from jax.experimental.pallas import tpu as pltpu
from jax.sharding import PartitionSpec as P

HD = 64
R = 84
PAIR = 2 * HD
HALO = 128
REACH = 96
GP = 256
SUB = 256
WINDOW = SUB + 2 * HALO
EPSILON = 1e-05
MASKED = -1e30
F32 = jnp.float32
BF16 = jnp.bfloat16


def dot_t(left, right):
    return lax.dot_general(left, right, (((1,), (1,)), ((), ())), preferred_element_type=F32)


def dot_n(left, right):
    return lax.dot_general(left, right, (((1,), (0,)), ((), ())), preferred_element_type=F32)


def t_dot(left, right):
    return lax.dot_general(left, right, (((0,), (0,)), ((), ())), preferred_element_type=F32)


def band_bias(table_row):
    spread = jnp.broadcast_to(table_row, (SUB, WINDOW))
    return pltpu.roll(spread, 0, 1, stride=1, stride_axis=0)


def diagonal_sums(rows):
    height, width = rows.shape
    while height > 8:
        height //= 2
        rows = rows[:height] + pltpu.roll(rows[height:], width - height, 1)
    row = lax.broadcasted_iota(jnp.int32, rows.shape, 0)
    for bit in (1, 2, 4):
        rows = jnp.where((row & bit) != 0, pltpu.roll(rows, width - bit, 1), rows)
    return jnp.sum(rows, 0, keepdims=True)


def lane_index():
    return lax.broadcasted_iota(jnp.int32, (1, PAIR), 1)


def own_half(head, value):
    low_lanes = lane_index() < HD
    return jnp.where(low_lanes if head == 0 else ~low_lanes, value, jnp.zeros_like(value))


def other_lane(head):
    return HD * (1 - head)


def with_lanes(head, value, columns):
    wide = own_half(head, value.astype(F32))
    lane = lane_index()
    for offset, column in enumerate(columns):
        wide = jnp.where(lane == other_lane(head) + offset, column, wide)
    return wide.astype(BF16)


def in_three(column):
    high = column.astype(BF16).astype(F32)
    middle = (column - high).astype(BF16).astype(F32)
    return (high, middle, column - high - middle)


def key_bias(first, rows, end):
    position = first + lax.broadcasted_iota(jnp.int32, (rows, 1), 0)
    return jnp.where((position >= 0) & (position < end), 0.0, MASKED)


def pick_column(rows, index):
    return jnp.sum(jnp.where(lane_index() == index, rows, 0.0), -1, keepdims=True)


def key_side(head, keys, bias):
    return with_lanes(head, keys, (bias, 1.0, 1.0, 1.0))


def value_side(head, values):
    return with_lanes(head, values, (1.0, 1.0, 1.0))


def softmax_rows(parts, value_parts, head):
    top = functools.reduce(
        jnp.maximum, [jnp.max(part, -1, keepdims=True) for part in parts]
    )
    mixed = sum(
        dot_n(jnp.exp(part - top).astype(BF16), values)
        for part, values in zip(parts, value_parts)
    )
    at = other_lane(head)
    total = mixed[:, at : at + 1]
    return mixed / total, top + jnp.log(total)


def seq_device(steps, seq_count):
    return (lax.axis_index("dp"), lax.rem(lax.axis_index("seq") + steps + seq_count, seq_count))


def row_norm(rows):
    centred = rows - jnp.mean(rows, -1, keepdims=True)
    inverse = lax.rsqrt(jnp.mean(centred * centred, -1, keepdims=True) + EPSILON)
    return centred * inverse, inverse


def put_column(ref, rows, index, column):
    ref[rows] = jnp.where(lane_index() == index, column, ref[rows])


def lanes_of(at):
    return pl.ds(pl.multiple_of(at * PAIR, PAIR), PAIR)


class Sizes(NamedTuple):
    block: int
    count: int
    quarter: int
    seq_count: int
    pairs: int


def attend_kernel(
    sizes,
    len_ref,
    rel_ref,
    long_ref,
    raw_ref,
    wq_far,
    wk_far,
    wv_far,
    bq_ref,
    bv_ref,
    gain_ref,
    shift_ref,
    q_far,
    kx_far,
    vx_far,
    kg_far,
    vg_far,
    o_ref,
    l_ref,
    lq_ref,
    glob_ref,
    tab_ref,
    spread,
    wide,
    part_o,
    part_l,
    from_o,
    from_l,
    halo_sends,
    halo_recvs,
    part_sends,
    part_recvs,
    wq_ref,
    wk_ref,
    wv_ref,
    loads,
    q_ref,
    kx_ref,
    vx_ref,
    kg_ref,
    vg_ref,
    stores,
):
    block, count, quarter, seq_count, pairs = sizes
    ext = block + 2 * HALO
    seq_index = lax.axis_index("seq")
    scale = jnp.asarray(HD ** (-0.5), BF16)
    low_lanes = lane_index() < HD
    own_keys = slice(HALO, HALO + block)
    own_rows = pl.ds(pl.multiple_of(seq_index * quarter, quarter), quarter)
    neighbours = (seq_index > 0, seq_index < seq_count - 1)
    barrier = pltpu.get_barrier_semaphore()
    for step in range(1, seq_count):
        pl.semaphore_signal(
            barrier,
            inc=1,
            device_id=seq_device(step, seq_count),
            device_id_type=pl.DeviceIdType.MESH,
        )

    def halo_copies(direction):
        source = HALO if direction == 0 else HALO + block - REACH
        dest = HALO + block if direction == 0 else HALO - REACH
        for kind, ref in enumerate((kx_ref, vx_ref)):
            yield pltpu.make_async_remote_copy(
                src_ref=ref.at[source : source + REACH],
                dst_ref=ref.at[dest : dest + REACH],
                send_sem=halo_sends.at[direction, kind],
                recv_sem=halo_recvs.at[direction, kind],
                device_id=seq_device(2 * direction - 1, seq_count),
                device_id_type=pl.DeviceIdType.MESH,
            )

    def part_copies():
        for step in range(1, seq_count):
            device = seq_device(step, seq_count)
            rows = pl.ds(pl.multiple_of(device[1] * quarter, quarter), quarter)
            for kind, (source, dest) in enumerate(((part_o, from_o), (part_l, from_l))):
                yield step, kind, pltpu.make_async_remote_copy(
                    src_ref=source.at[rows],
                    dst_ref=dest.at[step - 1],
                    send_sem=part_sends.at[kind, step - 1],
                    recv_sem=part_recvs.at[kind, step - 1],
                    device_id=device,
                    device_id_type=pl.DeviceIdType.MESH,
                )

    loading = [
        pltpu.make_async_copy(source, dest, loads.at[at])
        for at, (source, dest) in enumerate(
            ((wk_far, wk_ref), (wv_far, wv_ref), (wq_far, wq_ref))
        )
    ]
    for copy in loading:
        copy.start()
    gain, shift = gain_ref[...], shift_ref[...]
    heads, labels = rel_ref.shape
    spread[...] = jnp.full(spread.shape, MASKED, F32)
    spread[:heads, :labels] = rel_ref[...]
    turned = pltpu.roll(spread[...], HALO - R, 1)
    for pair in range(pairs):
        tab_ref[pair] = turned[2 * pair : 2 * pair + 2]
    normed_long = (row_norm(long_ref[...].astype(F32))[0] * gain + shift).astype(BF16)
    loading[0].wait()
    kx_ref[own_keys] = dot_n(normed_long, wk_ref[...]).astype(BF16)
    loading[1].wait()
    vx_ref[own_keys] = (dot_n(normed_long, wv_ref[...]) + bv_ref[...]).astype(BF16)
    pl.semaphore_wait(barrier, seq_count - 1)
    for direction, first in enumerate((HALO - REACH, HALO + block)):

        @pl.when(neighbours[direction])
        def _(direction=direction):
            for copy in halo_copies(direction):
                copy.start()

        outer = slice(0, first) if direction == 0 else slice(first + REACH, ext)
        for ref in (kx_ref, vx_ref):
            ref[outer] = jnp.zeros((HALO - REACH, ref.shape[1]), BF16)

        @pl.when(jnp.logical_not(neighbours[direction]))
        def _(first=first):
            for ref in (kx_ref, vx_ref):
                ref[first : first + REACH] = jnp.zeros((REACH, ref.shape[1]), BF16)

    wide[...] = jnp.zeros_like(wide)
    wide[:count] = raw_ref[...].astype(F32)
    glob_ref[...] = wide[...].astype(BF16)
    normed_glob = (row_norm(wide[...])[0] * gain + shift).astype(BF16)
    kg_ref[...] = dot_n(normed_glob, wk_ref[...]).astype(BF16)
    vg_ref[...] = (dot_n(normed_glob, wv_ref[...]) + bv_ref[...]).astype(BF16)
    loading[2].wait()
    q_ref[block:] = (dot_n(normed_glob, wq_ref[...]) + bq_ref[...]).astype(BF16)
    q_ref[:block] = (dot_n(normed_long, wq_ref[...]) + bq_ref[...]).astype(BF16)
    part_l[...] = jnp.zeros_like(part_l)
    l_ref[...] = jnp.zeros_like(l_ref)

    def glob_pair(pair, carry):
        lanes = lanes_of(pair)
        far_bias = key_bias(seq_index * block, block, len_ref[0])
        near_bias = key_bias(seq_index * quarter, quarter, count)
        query = q_ref[block:, lanes] * scale
        outs = []
        for head in range(2):
            q = with_lanes(head, query, (1.0,))
            far = dot_t(q, with_lanes(head, kx_ref[own_keys, lanes], (far_bias,)))
            near = dot_t(q, with_lanes(head, kg_ref[own_rows, lanes], (near_bias,)))
            out, norm = softmax_rows(
                [far, near],
                [
                    with_lanes(head, vx_ref[own_keys, lanes], (1.0,)),
                    with_lanes(head, vg_ref[own_rows, lanes], (1.0,)),
                ],
                head,
            )
            outs.append(out)
            put_column(part_l, slice(None), 2 * pair + head, norm)
        part_o[:, lanes] = jnp.where(low_lanes, outs[0], outs[1]).astype(BF16)
        return carry

    lax.fori_loop(0, pairs, glob_pair, 0, unroll=2)
    for _, _, copy in part_copies():
        copy.start()
    for direction in range(2):

        @pl.when(neighbours[1 - direction])
        def _(direction=direction):
            for copy in halo_copies(direction):
                copy.wait_recv()

    storing = [
        pltpu.make_async_copy(source, dest, stores.at[at])
        for at, (source, dest) in enumerate(
            (
                (q_ref, q_far),
                (kx_ref, kx_far),
                (vx_ref, vx_far),
                (kg_ref, kg_far),
                (vg_ref, vg_far),
            )
        )
    ]
    for copy in storing:
        copy.start()

    def long_pair(pair, carry):
        lanes = lanes_of(pair)
        long_bias = key_bias(seq_index * block - HALO, ext, len_ref[0])
        glob_bias = key_bias(0, GP, count)
        query = q_ref[:block, lanes] * scale
        outs = []
        for head in range(2):
            q = with_lanes(head, query, (1.0,))
            kx = with_lanes(head, kx_ref[:, lanes], (long_bias,))
            kg = with_lanes(head, kg_ref[:, lanes], (glob_bias,))
            vx, vg = (with_lanes(head, ref[:, lanes], (1.0,)) for ref in (vx_ref, vg_ref))
            bias = band_bias(tab_ref[pair, head : head + 1])
            mixed = []
            for start in range(0, block, SUB):
                rows, keys = slice(start, start + SUB), slice(start, start + WINDOW)
                out, norm = softmax_rows(
                    [dot_t(q[rows], kx[keys]) + bias, dot_t(q[rows], kg)], [vx[keys], vg], head
                )
                mixed.append(out)
                put_column(l_ref, rows, 2 * pair + head, norm)
            outs.append(jnp.concatenate(mixed, 0))
        o_ref[:block, lanes] = jnp.where(low_lanes, outs[0], outs[1]).astype(BF16)
        return carry

    lax.fori_loop(0, pairs, long_pair, 0, unroll=2)
    for _, _, copy in part_copies():
        copy.wait_recv()
    norms = [part_l[own_rows]] + [from_l[step] for step in range(seq_count - 1)]
    outs = [part_o[own_rows]] + [from_o[step] for step in range(seq_count - 1)]
    top = functools.reduce(jnp.maximum, norms)
    shares = [jnp.exp(norm - top) for norm in norms]
    total = sum(shares)
    lq_ref[...] = top + jnp.log(total)
    shares = [share / total for share in shares]
    for at in range(pairs):
        lanes = slice(at * PAIR, (at + 1) * PAIR)
        mixed = 0.0
        for share, out in zip(shares, outs):
            spread = jnp.where(
                low_lanes, share[:, 2 * at : 2 * at + 1], share[:, 2 * at + 1 : 2 * at + 2]
            )
            mixed += spread * out[:, lanes].astype(F32)
        o_ref[block:, lanes] = mixed.astype(BF16)
    for copy in storing:
        copy.wait()
    for _, _, copy in part_copies():
        copy.wait_send()
    for direction in range(2):

        @pl.when(neighbours[direction])
        def _(direction=direction):
            for copy in halo_copies(direction):
                copy.wait_send()


def attend(sizes, doc_len, rel_table, long_x, glob_x, *weights):
    block, count, quarter, seq_count, pairs = sizes
    width = long_x.shape[1]
    ext = block + 2 * HALO
    whole = pl.BlockSpec(memory_space=pltpu.VMEM)
    shape = jax.ShapeDtypeStruct
    others = seq_count - 1
    return pl.pallas_call(
        functools.partial(attend_kernel, sizes),
        in_specs=[pl.BlockSpec(memory_space=pltpu.SMEM)]
        + [whole] * 3
        + [pl.BlockSpec(memory_space=pl.ANY)] * 3
        + [whole] * 4,
        out_specs=[pl.BlockSpec(memory_space=pl.ANY)] * 5 + [whole] * 5,
        out_shape=[
            shape((block + GP, width), BF16),
            shape((ext, width), BF16),
            shape((ext, width), BF16),
            shape((GP, width), BF16),
            shape((GP, width), BF16),
            shape((block + quarter, width), BF16),
            shape((block, PAIR), F32),
            shape((quarter, PAIR), F32),
            shape((GP, width), BF16),
            shape((pairs, 2, WINDOW), F32),
        ],
        scratch_shapes=[
            pltpu.VMEM(((2 * pairs + 7) // 8 * 8, WINDOW), F32),
            pltpu.VMEM((GP, width), F32),
            pltpu.VMEM((GP, width), BF16),
            pltpu.VMEM((GP, PAIR), F32),
            pltpu.VMEM((others, quarter, width), BF16),
            pltpu.VMEM((others, quarter, PAIR), F32),
            pltpu.SemaphoreType.DMA((2, 2)),
            pltpu.SemaphoreType.DMA((2, 2)),
            pltpu.SemaphoreType.DMA((2, others)),
            pltpu.SemaphoreType.DMA((2, others)),
            pltpu.VMEM((width, width), BF16),
            pltpu.VMEM((width, width), BF16),
            pltpu.VMEM((width, width), BF16),
            pltpu.SemaphoreType.DMA((3,)),
            pltpu.VMEM((block + GP, width), BF16),
            pltpu.VMEM((ext, width), BF16),
            pltpu.VMEM((ext, width), BF16),
            pltpu.VMEM((GP, width), BF16),
            pltpu.VMEM((GP, width), BF16),
            pltpu.SemaphoreType.DMA((5,)),
        ],
        compiler_params=pltpu.CompilerParams(
            collective_id=3, has_side_effects=True, vmem_limit_bytes=56 * 2**20
        ),
        name="attend",
    )(doc_len, rel_table, long_x, glob_x, *weights)


class Reducer:
    def __init__(self, rows, split, scratch, pieces=None, order=None, parts=None):
        self.ids = mesh_ids()
        self.parts = parts
        self.order = order
        self.halves = (slice(0, split), slice(split, rows))
        held, self.from_core, self.from_one, self.from_two = scratch[:4]
        self.local, self.sends, self.recvs = scratch[4:7]
        if parts is None:
            self.from_z, self.z_sends, self.z_recvs = scratch[7:]
        self.pieces, self.held = pieces, held
        self.mine = held.at[self.ids[3]] if pieces is None else held.at[0]

    @staticmethod
    def scratch(rows, width, sides, with_z=False):
        buffers = [
            pltpu.VMEM((sides, 4, 2, 2, rows, width), BF16),
            pltpu.VMEM((4, 2, 2, rows, width), BF16),
            pltpu.VMEM((4, 2, rows, width), BF16),
            pltpu.VMEM((4, rows, width), BF16),
            pltpu.SemaphoreType.DMA((4,)),
            pltpu.SemaphoreType.DMA((5, 4)),
            pltpu.SemaphoreType.DMA((5, 4)),
        ]
        if with_z:
            buffers += [
                pltpu.VMEM((3, rows, width), BF16),
                pltpu.SemaphoreType.DMA((4,)),
                pltpu.SemaphoreType.DMA((3,)),
            ]
        return buffers

    def partners(self):
        z, y, x, core = self.ids
        dp, seq = z * 2 + y, x * 2 + core
        near = [(dp, x * 2 + 1 - core), (dp, (1 - x) * 2 + core), (z * 2 + 1 - y, seq)]
        return near + [(lax.rem(z + step, 4) * 2 + y, seq) for step in (1, 2, 3)]

    def target(self, chunk):
        return self.order(chunk) if self.order else lax.rem(self.ids[0] + 1 + chunk, 4)

    def remote(self, source, dest, kind, send_at, recv_at, device):
        return pltpu.make_async_remote_copy(
            src_ref=source,
            dst_ref=dest,
            send_sem=self.sends.at[kind, send_at],
            recv_sem=self.recvs.at[kind, recv_at],
            device_id=device,
            device_id_type=pl.DeviceIdType.MESH,
        )

    def own_copy(self, chunk):
        core, to = self.ids[3], self.target(chunk)
        return pltpu.make_async_copy(
            self.pieces.at[core, to], self.mine.at[to], self.local.at[chunk]
        )

    def core_copy(self, chunk):
        core, to = self.ids[3], self.target(chunk)
        source = (self.held if self.pieces is None else self.pieces).at[1 - core, to]
        return self.remote(source, self.from_core.at[to], 0, chunk, chunk, self.partners()[0])

    def first_copies(self, chunk):
        z, y, x, core = self.ids
        to = self.target(chunk)
        one, two = self.halves
        near = self.partners()
        return (
            self.remote(
                self.mine.at[to, :, 1 - x, one],
                self.from_one.at[to, :, one],
                1,
                chunk,
                chunk,
                near[1],
            ),
            self.remote(
                self.mine.at[to, 1 - y, :, two],
                self.from_one.at[to, :, two],
                2,
                chunk,
                chunk,
                near[2],
            ),
        )

    def second_copies(self, chunk):
        z, y, x, core = self.ids
        to = self.target(chunk)
        one, two = self.halves
        near = self.partners()
        return (
            self.remote(
                self.mine.at[to, 1 - y, x, one],
                self.from_two.at[to, one],
                3,
                chunk,
                chunk,
                near[2],
            ),
            self.remote(
                self.mine.at[to, y, 1 - x, two],
                self.from_two.at[to, two],
                4,
                chunk,
                chunk,
                near[1],
            ),
        )

    def last_copy(self, chunk):
        z, y, x, core = self.ids
        to = self.target(chunk)
        slot = lax.rem(z - to + 4, 4) - 1
        return pltpu.make_async_remote_copy(
            src_ref=self.mine.at[to, y, x],
            dst_ref=self.from_z.at[slot],
            send_sem=self.z_sends.at[chunk],
            recv_sem=self.z_recvs.at[slot],
            device_id=(to * 2 + y, x * 2 + core),
            device_id_type=pl.DeviceIdType.MESH,
        )

    def arrival(self, slot):
        z, y, x, core = self.ids
        return pltpu.make_async_remote_copy(
            src_ref=self.mine.at[z, y, x],
            dst_ref=self.from_z.at[slot],
            send_sem=self.z_sends.at[slot],
            recv_sem=self.z_recvs.at[slot],
            device_id=self.partners()[3],
            device_id_type=pl.DeviceIdType.MESH,
        )

    def leaves(self, chunk):
        return self.target(chunk) != self.ids[0]

    def fill(self, to, at, value):
        self.held[at % 2, to, at // 4, at // 2 % 2] = value.astype(BF16)

    def start(self, chunk):
        self.core_copy(chunk).start()
        if self.pieces is not None:
            self.own_copy(chunk).start()

    def add_core(self, chunk):
        to = self.target(chunk)
        if self.pieces is not None:
            self.own_copy(chunk).wait()
        self.core_copy(chunk).wait_recv()

        def add(index, carry):
            at = (to, lax.div(index, 2), lax.rem(index, 2))
            self.mine[at] = self.mine[at] + self.from_core[at]
            return carry

        lax.fori_loop(0, 4, add, 0)
        for copy in self.first_copies(chunk):
            copy.start()

    def add_first(self, chunk):
        z, y, x, core = self.ids
        one, two = self.halves
        to = self.target(chunk)
        for copy in self.first_copies(chunk):
            copy.wait_recv()

        def add(index, carry):
            for at, rows in (((to, index, x), one), ((to, y, index), two)):
                self.mine[at + (rows,)] = self.mine[at + (rows,)] + self.from_one[to, index, rows]
            return carry

        lax.fori_loop(0, 2, add, 0)
        for copy in self.second_copies(chunk):
            copy.start()

    def add_second(self, chunk):
        z, y, x, core = self.ids
        to = self.target(chunk)
        for copy in self.second_copies(chunk):
            copy.wait_recv()
        if self.parts is not None:
            self.parts[to] = self.mine[to, y, x] + self.from_two[to]
            return

        @pl.when(self.leaves(chunk))
        def _():
            self.mine[to, y, x] = self.mine[to, y, x] + self.from_two[to]
            self.last_copy(chunk).start()

    def finish(self, out=None):
        z, y, x, core = self.ids
        if self.parts is None:
            total = self.mine[z, y, x].astype(F32) + self.from_two[z].astype(F32)
            for slot in range(3):
                self.arrival(slot).wait_recv()
                total += self.from_z[slot].astype(F32)
            out[...] = total
        for chunk in range(4):
            self.core_copy(chunk).wait_send()
            for copy in self.first_copies(chunk) + self.second_copies(chunk):
                copy.wait_send()
            if self.parts is None:

                @pl.when(self.leaves(chunk))
                def _(chunk=chunk):
                    self.last_copy(chunk).wait_send()


class ZSum:
    def __init__(self, parts, scratch):
        self.ids = mesh_ids()
        self.parts = parts
        self.own, self.from_z, self.local, self.sends, self.recvs = scratch

    @staticmethod
    def scratch(rows, width):
        return [
            pltpu.VMEM((rows, width), BF16),
            pltpu.VMEM((3, rows, width), BF16),
            pltpu.SemaphoreType.DMA,
            pltpu.SemaphoreType.DMA((3,)),
            pltpu.SemaphoreType.DMA((3,)),
        ]

    def own_copy(self):
        return pltpu.make_async_copy(self.parts.at[self.ids[0]], self.own, self.local)

    def copies(self):
        z, y, x, core = self.ids
        for slot in range(3):
            to = lax.rem(z + 3 - slot, 4)
            yield pltpu.make_async_remote_copy(
                src_ref=self.parts.at[to],
                dst_ref=self.from_z.at[slot],
                send_sem=self.sends.at[slot],
                recv_sem=self.recvs.at[slot],
                device_id=(to * 2 + y, x * 2 + core),
                device_id_type=pl.DeviceIdType.MESH,
            )

    def start(self):
        self.own_copy().start()
        for copy in self.copies():
            copy.start()

    def finish(self, out):
        self.own_copy().wait()
        total = self.own[...].astype(F32)
        for slot, copy in enumerate(self.copies()):
            copy.wait_recv()
            total += self.from_z[slot].astype(F32)
        out[...] = total
        for copy in self.copies():
            copy.wait_send()


class EverySum:
    def __init__(self, scratch):
        self.kept, self.arrived, self.from_z, self.sends, self.recvs = scratch
        z, y, x, core = mesh_ids()
        seq = x * 2 + core
        self.z = z
        self.pairs = (
            (z * 2 + y, x * 2 + 1 - core),
            (z * 2 + y, (1 - x) * 2 + core),
            (z * 2 + 1 - y, seq),
        )
        self.along_z = [(lax.rem(z + step, 4) * 2 + y, seq) for step in (1, 2, 3)]

    @staticmethod
    def scratch(rows, width):
        return [
            pltpu.VMEM((3, rows, width), F32),
            pltpu.VMEM((3, rows, width), F32),
            pltpu.VMEM((4, rows, width), F32),
            pltpu.SemaphoreType.DMA((6,)),
            pltpu.SemaphoreType.DMA((6,)),
        ]

    def copy(self, stage):
        return pltpu.make_async_remote_copy(
            src_ref=self.kept.at[stage],
            dst_ref=self.arrived.at[stage],
            send_sem=self.sends.at[stage],
            recv_sem=self.recvs.at[stage],
            device_id=self.pairs[stage],
            device_id_type=pl.DeviceIdType.MESH,
        )

    def z_copies(self):
        for at, device in enumerate(self.along_z):
            yield pltpu.make_async_remote_copy(
                src_ref=self.from_z.at[self.z],
                dst_ref=self.from_z.at[self.z],
                send_sem=self.sends.at[3 + at],
                recv_sem=self.recvs.at[3 + at],
                device_id=device,
                device_id_type=pl.DeviceIdType.MESH,
            )

    def step(self, stage):
        if stage > 0:
            self.copy(stage - 1).wait_recv()
            total = self.kept[stage - 1] + self.arrived[stage - 1]
            if stage < 3:
                self.kept[stage] = total
            else:
                self.from_z[self.z] = total
        if stage < 3:
            self.copy(stage).start()
        else:
            for copy in self.z_copies():
                copy.start()

    def finish(self, out):
        for copy in self.z_copies():
            copy.wait_recv()
        out[...] = (self.from_z[0] + self.from_z[1]) + (self.from_z[2] + self.from_z[3])
        for copy in [self.copy(stage) for stage in range(3)] + list(self.z_copies()):
            copy.wait_send()


def mesh_ids():
    dp, seq = lax.axis_index("dp"), lax.axis_index("seq")
    return lax.div(dp, 2), lax.rem(dp, 2), lax.div(seq, 2), lax.rem(seq, 2)


def meet(devices):
    barrier = pltpu.get_barrier_semaphore()
    for device in devices:
        pl.semaphore_signal(barrier, inc=1, device_id=device, device_id_type=pl.DeviceIdType.MESH)
    pl.semaphore_wait(barrier, len(devices))


EARLY_PLAN = (
    (1, "add_core", 0),
    (1, "add_core", 1),
    (2, "add_core", 2),
    (2, "add_core", 3),
    (4, "add_first", 0),
    (4, "add_first", 1),
    (5, "add_first", 2),
    (5, "add_first", 3),
    (5, "add_second", 0),
    (6, "add_second", 1),
    (6, "add_second", 2),
    (6, "add_second", 3),
)


def late_kernel(
    sizes,
    planned,
    long_ref,
    glob_ref,
    dq_ref,
    dk_ref,
    dv_ref,
    dmid_far,
    wq_far,
    wk_far,
    wv_far,
    gain_ref,
    shift_ref,
    table_ref,
    *rest,
):
    block, count, quarter, seq_count, pairs = sizes
    rows = block + quarter
    width = long_ref.shape[1]
    if planned:
        early_parts, long_far, glob_out, late_ref, total_ref, scale_ref, early_ref, *rest = rest
    else:
        long_far, glob_out, gq_ref, gk_ref, gv_ref, total_ref, scale_ref, *rest = rest
    normed_t, every, gather_sends, gather_recvs, *rest = rest
    dmid_ref, wq_ref, wk_ref, wv_ref, loads, long_out, store, *rest = rest
    storing = pltpu.make_async_copy(long_out, long_far, store)
    far = (wq_far, wk_far, wv_far, dmid_far)
    loading = [
        pltpu.make_async_copy(source, dest, loads.at[at])
        for at, (source, dest) in enumerate(zip(far, (wq_ref, wk_ref, wv_ref, dmid_ref)))
    ]
    for copy in loading:
        copy.start()
    seq_index = lax.axis_index("seq")
    own_rows = pl.ds(pl.multiple_of(seq_index * quarter, quarter), quarter)
    others = [seq_device(step, seq_count) for step in range(1, seq_count)]

    def gathers():
        for step, device in enumerate(others):
            yield pltpu.make_async_remote_copy(
                src_ref=every.at[own_rows],
                dst_ref=every.at[own_rows],
                send_sem=gather_sends.at[step],
                recv_sem=gather_recvs.at[step],
                device_id=device,
                device_id_type=pl.DeviceIdType.MESH,
            )

    if planned:
        first_sum, second_sum = EverySum(rest[:5]), EverySum(rest[5:10])
        z_sum = ZSum(early_parts, rest[10:15])
        reducer = Reducer(rest[15].shape[-2], 32, rest[15:])

    meet(others + (reducer.partners()[2:] if planned else []))
    heads = 2 * pairs
    first = first_sum.kept.at[0] if planned else total_ref
    first[...] = jnp.zeros(first.shape, F32)
    for pair in range(pairs):
        first[2 * pair : 2 * pair + 2, :WINDOW] = table_ref[pair]
    for at, ref in enumerate((dq_ref, dv_ref)):
        first[heads + at : heads + at + 1] = column_sum(ref[...].astype(F32))
    if planned:
        first_sum.step(0)
        z_sum.start()
    everything = jnp.concatenate([long_ref[...], glob_ref[own_rows]], 0).astype(F32)
    hat, inverse = row_norm(everything)
    normed_t[...] = (hat * gain_ref[...] + shift_ref[...]).astype(BF16).T
    if planned:
        piece = width // 32
        blank = jnp.zeros((8, width), F32)
        def weight_rows(chunk):
            to = reducer.target(chunk)
            some = normed_t[pl.ds(pl.multiple_of(to * 8 * piece, 64), 8 * piece)]
            parts = [dot_n(some, ref[...]) for ref in (dq_ref, dk_ref, dv_ref)]
            for at in range(8):
                rows_at = slice(at * piece, (at + 1) * piece)
                reducer.fill(
                    to, at, jnp.concatenate([part[rows_at] for part in parts] + [blank], 0)
                )
            reducer.start(chunk)

        weight_rows(0)
        first_sum.step(1)
        weight_rows(1)
        first_sum.step(2)
        reducer.add_core(0)
        weight_rows(2)
        first_sum.step(3)
        reducer.add_core(1)
        weight_rows(3)
        for copy in loading:
            copy.wait()
        grads = dot_t(dq_ref[...], wq_ref[...])
        grads += dot_t(dk_ref[...], wk_ref[...]) + dot_t(dv_ref[...], wv_ref[...])
        reducer.add_first(0)
        reducer.add_core(2)
    else:
        for ref, out in ((dq_ref, gq_ref), (dk_ref, gk_ref), (dv_ref, gv_ref)):
            out[...] = dot_n(normed_t[...], ref[...]).astype(BF16)
        for copy in loading:
            copy.wait()
        grads = (
            dot_t(dq_ref[...], wq_ref[...])
            + dot_t(dk_ref[...], wk_ref[...])
            + dot_t(dv_ref[...], wv_ref[...])
        )
    scaled = grads * gain_ref[...]
    total = dmid_ref[...] + inverse * (
        scaled
        - jnp.mean(scaled, -1, keepdims=True)
        - hat * jnp.mean(scaled * hat, -1, keepdims=True)
    )
    every[own_rows] = total[block:].astype(BF16)
    for copy in gathers():
        copy.start()
    long_out[...] = total[:block]
    storing.start()
    second = second_sum.kept.at[0] if planned else scale_ref
    second[...] = jnp.zeros(second.shape, F32)
    second[0:1] = column_sum(grads * hat)
    second[1:2] = column_sum(grads)
    if planned:
        second_sum.step(0)
        reducer.add_first(1)
        second_sum.step(1)
        reducer.add_core(3)
        reducer.add_second(0)
        reducer.add_first(2)
        second_sum.step(2)
        reducer.add_second(1)
        reducer.add_first(3)
        second_sum.step(3)
        reducer.add_second(2)
        reducer.add_second(3)
        first_sum.finish(total_ref)
        z_sum.finish(early_ref)
        reducer.finish(late_ref)
        second_sum.finish(scale_ref)
    for copy in gathers():
        copy.wait_recv()
    glob_out[...] = every[:count].astype(F32)
    storing.wait()
    for copy in gathers():
        copy.wait_send()


def last_part(sizes, planned, long_x, glob_x, dq, dk, dv, dmid, *weights):
    block, count, quarter, seq_count, pairs = sizes
    rows, width = dq.shape
    others = seq_count - 1
    whole = pl.BlockSpec(memory_space=pltpu.VMEM)
    there = pl.BlockSpec(memory_space=pl.ANY)
    shape = jax.ShapeDtypeStruct
    sums = [shape(((2 * pairs + 2 + 7) // 8 * 8, width), F32), shape((8, width), F32)]
    outs = [shape((block, width), F32), shape((count, width), F32)]
    scratch = [
        pltpu.VMEM((width, rows), BF16),
        pltpu.VMEM((GP, width), BF16),
        pltpu.SemaphoreType.DMA((others,)),
        pltpu.SemaphoreType.DMA((others,)),
        pltpu.VMEM((rows, width), F32),
        pltpu.VMEM((width, width), BF16),
        pltpu.VMEM((width, width), BF16),
        pltpu.VMEM((width, width), BF16),
        pltpu.SemaphoreType.DMA((4,)),
        pltpu.VMEM((block, width), F32),
        pltpu.SemaphoreType.DMA,
    ]
    if planned:
        piece = width // 32
        part = 3 * piece + 8
        early = weights[-1].shape[1:]
        outs += [shape((part, width), F32), *sums, shape(early, F32)]
        for part_sums in sums:
            scratch += EverySum.scratch(*part_sums.shape)
        scratch += ZSum.scratch(*early) + Reducer.scratch(part, width, 2, with_z=True)
    else:
        outs += [shape((width, width), BF16)] * 3 + sums
    return pl.pallas_call(
        functools.partial(late_kernel, sizes, planned),
        in_specs=[whole] * 5 + [there] * 4 + [whole] * 3 + [there] * planned,
        out_specs=[there] + [whole] * (len(outs) - 1),
        out_shape=outs,
        scratch_shapes=scratch,
        compiler_params=pltpu.CompilerParams(
            collective_id=2, has_side_effects=True, vmem_limit_bytes=60 * 2**20
        ),
        name="last_part",
    )(long_x, glob_x, dq, dk, dv, dmid, *weights)


def small_kernel(heads, early_ref, late_ref, outer_ref, inner_ref, sums_ref, scale_ref, *rest):
    outs = rest[4:-4]
    for source, out in zip(rest[:3], rest[-4:]):
        out[...] = source[...]
    rest[-1][...] = rest[3][...].reshape(rest[-1].shape)
    g_query, g_key, g_value, g_out, g_inner, g_outer, *vectors, table = outs
    device = lax.axis_index("dp") * lax.axis_size("seq") + lax.axis_index("seq")
    piece, width = g_query.shape
    for at, out in enumerate((g_query, g_key, g_value)):
        out[...] = late_ref[at * piece : (at + 1) * piece]
    g_out[...] = early_ref[2 * piece : 3 * piece]
    g_outer[...] = outer_ref[...]
    for source, first, chunk in (
        (inner_ref, 0, 0),
        (inner_ref, piece, 3),
        (early_ref, 0, 1),
        (early_ref, piece, 2),
    ):
        g_inner[:, chunk * width : (chunk + 1) * width] = source[first : first + piece]

    def entries(row, at, length):
        return pltpu.roll(row, width - at * length, 1)[0, :length]

    b_query, b_value, b_out, b_outer, gain_one, shift_one, gain_two, shift_two, b_inner = vectors
    for at, out in enumerate((b_query, b_value)):
        out[...] = entries(sums_ref[heads + at : heads + at + 1], device, piece)
    for at, out in enumerate((gain_one, shift_one)):
        out[...] = entries(scale_ref[at : at + 1], device, piece)
    for at, out in enumerate((b_out, b_outer, gain_two, shift_two)):
        row = 3 * piece + at
        out[...] = entries(early_ref[row : row + 1], device, piece)
    row = pl.ds(3 * piece + 4 + lax.div(device, 8), 1)
    b_inner[...] = entries(early_ref[row], lax.rem(device, 8), 4 * piece)
    labels = table.shape[1]
    turned = pltpu.roll(sums_ref[:, :WINDOW], WINDOW - HALO + R, 1)
    table[...] = turned[:heads, :labels]


def small_results(heads, early, late, outer, inner, sums, scales, *big):
    width = early.shape[1]
    piece = width // 32
    shape = jax.ShapeDtypeStruct
    whole = pl.BlockSpec(memory_space=pltpu.VMEM)
    outs = [shape((piece, width), F32)] * 4
    outs += [shape((piece, 4 * width), F32), shape((4 * piece, width), F32)]
    outs += [shape((piece,), F32)] * 8 + [shape((4 * piece,), F32)]
    outs += [shape((heads, 2 * R + 1), F32)]
    outs += [shape(part.shape, part.dtype) for part in big[:3]]
    outs.append(shape((big[3].shape[0], 1, width), F32))
    return pl.pallas_call(
        functools.partial(small_kernel, heads),
        in_specs=[whole] * 10,
        out_specs=[whole] * len(outs),
        out_shape=outs,
        name="small_results",
    )(early, late, outer, inner, sums, scales, *big)


def has_plan():
    return (lax.axis_size("dp"), lax.axis_size("seq")) == (8, 4)


GELU_A = 0.7978845608028654
GELU_B = 0.044715


def gate_both(u):
    square = u * u
    turned = jnp.tanh(GELU_A * u * (1.0 + GELU_B * square))
    half = 0.5 * (1.0 + turned)
    slope = half + 0.5 * u * (1.0 - turned * turned) * (
        GELU_A * (1.0 + 3.0 * GELU_B * square)
    )
    return u * half, slope


def column_sum(rows):
    return jnp.sum(rows, 0, keepdims=True)


def ffn_kernel(
    sizes,
    planned,
    len_ref,
    attn_ref,
    long_ref,
    glob_ref,
    dlong_ref,
    dglob_ref,
    lq_ref,
    wo_ref,
    bo_ref,
    gain_ref,
    shift_ref,
    wi_ref,
    bi_ref,
    wr_ref,
    br_ref,
    long_out,
    glob_out,
    dmid_far,
    do_far,
    dog_ref,
    ldg_ref,
    *rest,
):
    block, count, quarter, seq_count, pairs = sizes
    if planned:
        pieces_far, outer_ref, inner_ref, *rest = rest
    else:
        g_outer_ref, g_inner_ref, g_out_ref, vec_ref, *rest = rest
    (
        mid,
        y_sum,
        df_sum,
        normed,
        normed_t,
        dy,
        vectors,
        biases,
        every_do,
        every_ld,
        gather_sends,
        gather_recvs,
        dmid_ref,
        do_ref,
        stores,
        *rest,
    ) = rest
    storing = [
        pltpu.make_async_copy(dmid_ref, dmid_far, stores.at[0]),
        pltpu.make_async_copy(do_ref, do_far, stores.at[1]),
    ]
    if planned:
        even, pieces_ref, *rest = rest
        outer = Reducer(rest[0].shape[-2], 48, rest[:7], order=chunk_of, parts=outer_ref)
        inner = Reducer(rest[7].shape[-2], 16, rest[7:], parts=inner_ref)
    step = pl.program_id(0)
    chunk = chunk_of(step)
    seq_index = lax.axis_index("seq")
    own_rows = pl.ds(pl.multiple_of(seq_index * quarter, quarter), quarter)
    width = mid.shape[1]
    piece = width // 32

    def rows_of(device):
        return pl.ds(pl.multiple_of(device[1] * quarter, quarter), quarter)

    def gather(owner, device, at):
        for kind, every in enumerate((every_do, every_ld)):
            yield pltpu.make_async_remote_copy(
                src_ref=every.at[rows_of(owner)],
                dst_ref=every.at[rows_of(owner)],
                send_sem=gather_sends.at[kind, at],
                recv_sem=gather_recvs.at[kind, at],
                device_id=device,
                device_id_type=pl.DeviceIdType.MESH,
            )

    me = seq_device(0, seq_count)
    if planned:
        sibling, across = outer.partners()[:2]
        first_gathers = [(me, across, 0), (me, sibling, 1)]
        second_gathers = [(across, sibling, 2)]
    else:
        first_gathers = [
            (me, seq_device(at + 1, seq_count), at) for at in range(seq_count - 1)
        ]
        second_gathers = []

    def store_pieces(half):
        rows = (slice(0, 2 * piece), slice(2 * piece, 3 * piece + 8))[half]
        return pltpu.make_async_copy(
            pieces_ref.at[:, :, :, :, rows], pieces_far.at[:, :, :, :, rows], stores.at[2 + half]
        )

    def act(now):
        if planned:
            for at, reducer, name, part in FFN_PLAN:
                if at == now:
                    getattr((outer, inner)[reducer], name)(part)

    def act_in_step(point):
        if planned:
            for now in range(4):
                if any(at == (now, point) for at, _, _, _ in FFN_PLAN):

                    @pl.when(step == now)
                    def _(now=now):
                        act((now, point))

    @pl.when(step == 0)
    def _():
        others = [seq_device(seq_step, seq_count) for seq_step in range(1, seq_count)]
        meet(others + (outer.partners()[2:] if planned else []))
        projected = dot_n(attn_ref[...], wo_ref[...]) + bo_ref[...]
        mid[:block] = long_ref[...].astype(F32) + projected[:block]
        mid[block:] = glob_ref[own_rows].astype(F32) + projected[block:]
        hat, _ = row_norm(mid[...])
        normed[...] = (hat * gain_ref[...] + shift_ref[...]).astype(BF16)
        normed_t[...] = normed[...].T
        position = seq_index * block + lax.broadcasted_iota(jnp.int32, (block, 1), 0)
        dy[:block] = jnp.where(
            position < len_ref[0], dlong_ref[...].astype(F32), 0.0
        ).astype(BF16)
        y_sum[:GP] = jnp.zeros((GP, width), F32)
        y_sum[:count] = dglob_ref[...].astype(F32)
        dy[block:] = y_sum[own_rows].astype(BF16)
        vectors[1:2] = column_sum(dy[...].astype(F32))
        y_sum[...] = mid[...] + br_ref[...]
        df_sum[...] = jnp.zeros_like(df_sum)
        for at in range(4):
            biases[at] = bi_ref[at * width : (at + 1) * width].reshape(1, width)

    act_in_step(0)
    active, slope = gate_both(dot_n(normed[...], wi_ref[...]) + biases[chunk])
    active = active.astype(BF16)
    g_outer = t_dot(active, dy[...])
    if planned:
        for at in range(8):
            outer.fill(chunk, at, g_outer[at * 4 * piece : (at + 1) * 4 * piece])
        outer.start(step)
    else:
        g_outer_ref[...] = g_outer.astype(BF16)
    y_sum[...] += dot_n(active, wr_ref[...])
    hidden = dot_t(dy[...], wr_ref[...]) * slope
    for at in range(4):

        @pl.when(chunk == at)
        def _(at=at):
            vectors[4 + at : 5 + at] = column_sum(hidden)

    hidden = hidden.astype(BF16)
    act_in_step(1)
    df_sum[...] += dot_t(hidden, wi_ref[...])
    g_inner = dot_n(normed_t[...], hidden)
    if planned:

        @pl.when(lax.rem(step, 2) == 0)
        def _():
            even[...] = g_inner

        def halves(at):
            part = slice(at * piece, (at + 1) * piece)
            return jnp.concatenate([even[part], g_inner[part]], 0)

        @pl.when(step == 1)
        def _():
            for at in range(32):
                inner.fill(at // 8, at % 8, halves(at))
            for part in range(4):
                inner.start(part)

        @pl.when(step == 3)
        def _():
            for at in range(32):
                pieces_ref[at % 2, at // 8, at // 4 % 2, at // 2 % 2, : 2 * piece] = halves(
                    at
                ).astype(BF16)
            store_pieces(0).start()

    else:
        g_inner_ref[...] = g_inner.astype(BF16)

    def norm_back(rows):
        hat, inverse = row_norm(mid[rows])
        df = df_sum[rows]
        scaled = df * gain_ref[...]
        dmid = dy[rows].astype(F32) + inverse * (
            scaled
            - jnp.mean(scaled, -1, keepdims=True)
            - hat * jnp.mean(scaled * hat, -1, keepdims=True)
        )
        dmid_ref[rows] = dmid
        low = dmid.astype(BF16)
        grad_o = dot_t(low, wo_ref[...]).astype(BF16)
        do_ref[rows] = grad_o
        return [column_sum(dmid), column_sum(df * hat), column_sum(df)], low, grad_o

    @pl.when(step == 3)
    def _():
        glob_sums, glob_low, grad_o = norm_back(slice(block, block + quarter))
        every_do[own_rows] = grad_o
        both = grad_o.astype(F32) * attn_ref[block:].astype(F32)
        stats = lq_ref[...]
        for head in range(2 * pairs):
            lanes = slice(head // 2 * PAIR, head // 2 * PAIR + PAIR)
            delta = jnp.sum(own_half(head % 2, both[:, lanes]), -1, keepdims=True)
            stats = jnp.where(lane_index() == HD + head, delta, stats)
        every_ld[own_rows] = stats
        for part in first_gathers:
            for copy in gather(*part):
                copy.start()
        glob_out[...] = y_sum[block:].astype(BF16)
        act((4, 0))
        position = seq_index * block + lax.broadcasted_iota(jnp.int32, (block, 1), 0)
        long_out[...] = jnp.where(position < len_ref[0], y_sum[:block], 0.0).astype(BF16)
        long_sums, long_low, _ = norm_back(slice(0, block))
        for at, one, two in zip((0, 2, 3), long_sums, glob_sums):
            vectors[at : at + 1] = one + two
        for copy in storing:
            copy.start()
        if planned:
            for copy in gather(*first_gathers[0]):
                copy.wait_recv()
            for copy in gather(*second_gathers[0]):
                copy.start()
        act((4, 1))
        g_out = t_dot(attn_ref[...], jnp.concatenate([long_low, glob_low], 0))
        if planned:
            for at in range(32):
                pieces_ref[at % 2, at // 8, at // 4 % 2, at // 2 % 2, 2 * piece :] = (
                    jnp.concatenate(
                        [g_out[at * piece : (at + 1) * piece], vectors[...]], 0
                    ).astype(BF16)
                )
            store_pieces(1).start()
            act((4, 2))
            outer.finish()
            inner.finish()
            for half in range(2):
                store_pieces(half).wait()
        else:
            g_out_ref[...] = g_out.astype(BF16)
            vec_ref[...] = vectors[...]
        for part in (first_gathers[1:] if planned else first_gathers) + second_gathers:
            for copy in gather(*part):
                copy.wait_recv()
        for copy in storing:
            copy.wait()
        dog_ref[...] = every_do[...]
        ldg_ref[...] = every_ld[...]
        for part in first_gathers + second_gathers:
            for copy in gather(*part):
                copy.wait_send()


OUTER, INNER = 0, 1
FFN_PLAN = (
    ((1, 0), OUTER, "add_core", 0),
    ((2, 0), OUTER, "add_core", 1),
    ((2, 0), OUTER, "add_first", 0),
    ((2, 1), INNER, "add_core", 0),
    ((2, 1), INNER, "add_core", 1),
    ((2, 1), INNER, "add_core", 2),
    ((2, 1), INNER, "add_core", 3),
    ((3, 0), OUTER, "add_first", 1),
    ((3, 0), OUTER, "add_second", 0),
    ((3, 0), OUTER, "add_core", 2),
    ((3, 1), OUTER, "add_core", 3),
    ((4, 0), INNER, "add_first", 0),
    ((4, 0), INNER, "add_first", 1),
    ((4, 0), OUTER, "add_first", 2),
    ((4, 0), OUTER, "add_second", 1),
    ((4, 1), INNER, "add_first", 2),
    ((4, 1), INNER, "add_first", 3),
    ((4, 1), INNER, "add_second", 0),
    ((4, 1), INNER, "add_second", 1),
    ((4, 2), OUTER, "add_first", 3),
    ((4, 2), OUTER, "add_second", 2),
    ((4, 2), INNER, "add_second", 2),
    ((4, 2), INNER, "add_second", 3),
    ((4, 2), OUTER, "add_second", 3),
)


def chunk_of(step):
    return jnp.where(step == 0, 0, jnp.where(step == 1, 3, step - 1))


def feed_forward(sizes, planned, doc_len, attn, long_x, glob_x, dlong, dglob, lq, *weights):
    block, count, quarter, seq_count, pairs = sizes
    wo, bo, gain, shift, wi, bi, wr, br = weights
    width, hidden = wi.shape
    chunk = hidden // 4
    rows = block + quarter
    whole = pl.BlockSpec(memory_space=pltpu.VMEM)
    shape = jax.ShapeDtypeStruct
    in_specs = [pl.BlockSpec(memory_space=pltpu.SMEM)] + [whole] * 10
    in_specs += [
        pl.BlockSpec((width, chunk), lambda c: (0, chunk_of(c))),
        whole,
        pl.BlockSpec((chunk, width), lambda c: (chunk_of(c), 0)),
        whole,
    ]
    outs = [
        shape((block, width), BF16),
        shape((quarter, width), BF16),
        shape((rows, width), F32),
        shape((rows, width), BF16),
        shape((GP, width), BF16),
        shape((GP, PAIR), F32),
    ]
    there = pl.BlockSpec(memory_space=pl.ANY)
    out_specs = [whole] * 2 + [there] * 2 + [whole] * 2
    others = seq_count - 1
    scratch = [
        pltpu.VMEM((rows, width), F32),
        pltpu.VMEM((rows, width), F32),
        pltpu.VMEM((rows, width), F32),
        pltpu.VMEM((rows, width), BF16),
        pltpu.VMEM((width, rows), BF16),
        pltpu.VMEM((rows, width), BF16),
        pltpu.VMEM((8, width), F32),
        pltpu.VMEM((4, 1, chunk), F32),
        pltpu.VMEM((GP, width), BF16),
        pltpu.VMEM((GP, PAIR), F32),
        pltpu.SemaphoreType.DMA((2, others)),
        pltpu.SemaphoreType.DMA((2, others)),
        pltpu.VMEM((rows, width), F32),
        pltpu.VMEM((rows, width), BF16),
        pltpu.SemaphoreType.DMA((4,)),
    ]
    if planned:
        part, piece = hidden // 32, width // 32
        outs += [
            shape((2, 4, 2, 2, 3 * piece + 8, width), BF16),
            shape((4, part, width), BF16),
            shape((4, 2 * piece, width), BF16),
        ]
        out_specs += [there] + [whole] * 2
        scratch += [
            pltpu.VMEM((width, chunk), F32),
            pltpu.VMEM(outs[-3].shape, BF16),
        ]
        scratch += Reducer.scratch(part, width, 2) + Reducer.scratch(2 * piece, width, 2)
    else:
        outs += [
            shape((hidden, width), BF16),
            shape((width, hidden), BF16),
            shape((width, width), BF16),
            shape((8, width), F32),
        ]
        out_specs += [
            pl.BlockSpec((chunk, width), lambda c: (chunk_of(c), 0)),
            pl.BlockSpec((width, chunk), lambda c: (0, chunk_of(c))),
            whole,
            whole,
        ]
    return pl.pallas_call(
        functools.partial(ffn_kernel, sizes, planned),
        grid=(4,),
        in_specs=in_specs,
        out_specs=out_specs,
        out_shape=outs,
        scratch_shapes=scratch,
        compiler_params=pltpu.CompilerParams(
            collective_id=4, has_side_effects=True, vmem_limit_bytes=62 * 2**20
        ),
        name="feed_forward",
    )(doc_len, attn, long_x, glob_x, dlong, dglob, lq, wo, bo, gain, shift, wi, bi, wr, br)


def back_kernel(
    sizes,
    early_rows,
    len_ref,
    tab_ref,
    q_ref,
    kx_ref,
    vx_ref,
    kg_ref,
    vg_ref,
    o_ref,
    do_ref,
    l_ref,
    dog_ref,
    ldg_ref,
    yq_ref,
    *rest,
):
    block, count, quarter, seq_count, pairs = sizes
    reduces = early_rows > 0
    if reduces:
        pieces_ref, outer_parts, inner_parts, *rest = rest
    dq_ref, dk_ref, dv_ref, dtab_ref, glob_out, *rest = rest
    if reduces:
        early_parts, outer_ref, inner_ref, *rest = rest
    (
        dkx,
        dvx,
        dkg,
        dvg,
        q_send,
        q_recv,
        kv_send,
        kv_recv,
        halo_send,
        halo_recv,
        glob_sends,
        glob_recvs,
        halo_sends,
        halo_recvs,
        every,
        gather_sends,
        gather_recvs,
        *rest,
    ) = rest
    number = pl.program_id(0)
    steps = pairs // 2
    first_pair = 2 * lax.rem(number, steps)
    seq_index = lax.axis_index("seq")
    if reduces:
        reducer = Reducer(early_rows, 16, rest[:7], pieces=pieces_ref, parts=early_parts)
        z_sums = (
            (ZSum(outer_parts, rest[7:12]), outer_ref),
            (ZSum(inner_parts, rest[12:]), inner_ref),
        )
    scale = HD ** (-0.5)
    low_lanes = lane_index() < HD
    own_keys = slice(HALO, HALO + block)
    own_rows = pl.ds(pl.multiple_of(seq_index * quarter, quarter), quarter)

    def glob_copies(kind, at):
        source, dest = ((q_send, q_recv), (kv_send, kv_recv))[kind]
        for step in range(1, seq_count):
            device = seq_device(step, seq_count)
            yield pltpu.make_async_remote_copy(
                src_ref=source.at[device[1], at],
                dst_ref=dest.at[step - 1, at],
                send_sem=glob_sends.at[kind, step - 1, at],
                recv_sem=glob_recvs.at[kind, step - 1, at],
                device_id=device,
                device_id_type=pl.DeviceIdType.MESH,
            )

    def gathers():
        for step in range(1, seq_count):
            yield pltpu.make_async_remote_copy(
                src_ref=every.at[own_rows],
                dst_ref=every.at[own_rows],
                send_sem=gather_sends.at[step - 1],
                recv_sem=gather_recvs.at[step - 1],
                device_id=seq_device(step, seq_count),
                device_id_type=pl.DeviceIdType.MESH,
            )

    def halo_copy(direction, at):
        return pltpu.make_async_remote_copy(
            src_ref=halo_send.at[direction, at],
            dst_ref=halo_recv.at[direction, at],
            send_sem=halo_sends.at[direction, at],
            recv_sem=halo_recvs.at[direction, at],
            device_id=seq_device(2 * direction - 1, seq_count),
            device_id_type=pl.DeviceIdType.MESH,
        )

    has_low, has_high = seq_index > 0, seq_index < seq_count - 1
    sends_to = (has_low, has_high)
    gets_from = (has_high, has_low)

    def close_pair(at):
        lanes = lanes_of(at)
        for direction in range(2):

            @pl.when(gets_from[direction])
            def _(direction=direction):
                halo_copy(direction, at).wait_recv()

        for kind, (total, out) in enumerate(((dkx, dk_ref), (dvx, dv_ref))):
            first, last = HALO + REACH, HALO + block - REACH
            out[:REACH, lanes] = (
                total[at, HALO:first] + halo_recv[1, at, kind].astype(F32)
            ).astype(BF16)
            out[REACH : block - REACH, lanes] = total[at, first:last].astype(BF16)
            out[block - REACH : block, lanes] = (
                total[at, last : HALO + block] + halo_recv[0, at, kind].astype(F32)
            ).astype(BF16)
        sums = []
        for kind, (source, dest) in enumerate(((q_send, q_recv), (kv_send, kv_recv))):
            total = source[seq_index, at].astype(F32)
            for step, copy in enumerate(glob_copies(kind, at)):
                copy.wait_recv()
                total += dest[step, at].astype(F32)
            sums.append(total.astype(BF16))
        dq_ref[block:, lanes] = sums[0]
        dk_ref[block:, lanes] = sums[1][:, :PAIR]
        dv_ref[block:, lanes] = sums[1][:, PAIR:]

    def run_plan(now):
        for at, act, chunk in EARLY_PLAN:
            if now == at:
                getattr(reducer, act)(chunk)

    @pl.when(number == 0)
    def _():
        others = [seq_device(step, seq_count) for step in range(1, seq_count)]
        meet(others + (reducer.partners()[2:] if reduces else []))
        if reduces:
            for chunk in range(4):
                reducer.start(chunk)
            for z_sum, _ in z_sums:
                z_sum.start()
        every[own_rows] = yq_ref[...]
        for copy in gathers():
            copy.start()
        for direction in range(2):

            @pl.when(jnp.logical_not(gets_from[direction]))
            def _(direction=direction):
                halo_recv[direction] = jnp.zeros_like(halo_recv[direction])

    if reduces:
        for now in range(1, 2 * steps):
            if any(at == now for at, _, _ in EARLY_PLAN):

                @pl.when(number == now)
                def _(now=now):
                    run_plan(now)

    def glob_pair(pair, q_ref, kx_ref, vx_ref, kg_ref, vg_ref, dog_ref):
        long_bias = key_bias(seq_index * block, block, len_ref[0])
        near_bias = key_bias(seq_index * quarter, quarter, count)
        query = q_ref[block:] * jnp.asarray(scale, BF16)
        grad_o = dog_ref[...]
        far_k, far_v = kx_ref[own_keys], vx_ref[own_keys]
        near_k, near_v = kg_ref[own_rows], vg_ref[own_rows]
        outs, kept = [], []
        for head in range(2):
            norm = in_three(-pick_column(ldg_ref[...], 2 * pair + head))
            delta = in_three(-pick_column(ldg_ref[...], HD + 2 * pair + head))
            qa = with_lanes(head, query, (1.0,) + norm)
            doa = with_lanes(head, grad_o, delta)
            far = jnp.exp(dot_t(qa, key_side(head, far_k, long_bias)))
            near = jnp.exp(dot_t(qa, key_side(head, near_k, near_bias)))
            far_ds = (far * dot_t(doa, value_side(head, far_v))).astype(BF16)
            near_ds = (near * dot_t(doa, value_side(head, near_v))).astype(BF16)
            outs.append(dot_n(far_ds, far_k) + dot_n(near_ds, near_k))
            kept.append(
                (
                    own_half(head, query),
                    own_half(head, grad_o),
                    far.astype(BF16),
                    near.astype(BF16),
                    far_ds,
                    near_ds,
                )
            )
        own_q, own_do, far, near, far_ds, near_ds = (
            jnp.concatenate(part, 0) for part in zip(*kept)
        )
        for total, edge in ((dkx, own_keys), (dvx, own_keys)):
            total[pair, :HALO] = jnp.zeros((HALO, PAIR), F32)
            total[pair, HALO + block :] = jnp.zeros((HALO, PAIR), F32)
        dkx[pair, own_keys] = t_dot(far_ds, own_q)
        dvx[pair, own_keys] = t_dot(far, own_do)
        dkg[pair] = jnp.zeros((GP, PAIR), F32)
        dvg[pair] = jnp.zeros((GP, PAIR), F32)
        dkg[pair, own_rows] = t_dot(near_ds, own_q)
        dvg[pair, own_rows] = t_dot(near, own_do)
        glob_dq = (jnp.where(low_lanes, outs[0], outs[1]) * scale).astype(BF16)
        q_send[:, pair] = glob_dq.reshape(seq_count, quarter, PAIR)
        for copy in glob_copies(0, pair):
            copy.start()

    def long_pair(pair, q_ref, kx_ref, vx_ref, kg_ref, vg_ref, o_ref, do_ref, tab_ref):
        long_bias = key_bias(seq_index * block - HALO, block + 2 * HALO, len_ref[0])
        glob_bias = key_bias(0, GP, count)
        query = q_ref[:block] * jnp.asarray(scale, BF16)
        grad_o = do_ref[...]
        both = grad_o.astype(F32) * o_ref[...].astype(F32)
        heads = []
        for head in range(2):
            norm = in_three(-pick_column(l_ref[...], 2 * pair + head))
            delta = in_three(-jnp.sum(own_half(head, both), -1, keepdims=True))
            heads.append(
                dict(
                    q=own_half(head, query),
                    do=own_half(head, grad_o),
                    qa=with_lanes(head, query, (1.0,) + norm),
                    doa=with_lanes(head, grad_o, delta),
                    kxa=key_side(head, kx_ref[...], long_bias),
                    vxa=value_side(head, vx_ref[...]),
                    kga=key_side(head, kg_ref[...], glob_bias),
                    vga=value_side(head, vg_ref[...]),
                    bias=band_bias(tab_ref[0, head : head + 1]),
                )
            )
        table_sums = [0.0, 0.0]
        grads_q = []
        for start in range(0, block, SUB):
            rows, keys = slice(start, start + SUB), slice(start, start + WINDOW)
            outs, probs, grads = [], [], []
            for head, own in enumerate(heads):
                band = jnp.exp(dot_t(own["qa"][rows], own["kxa"][keys]) + own["bias"])
                band_ds = band * dot_t(own["doa"][rows], own["vxa"][keys])
                table_sums[head] += band_ds
                glob = jnp.exp(dot_t(own["qa"][rows], own["kga"]))
                glob_ds = (glob * dot_t(own["doa"][rows], own["vga"])).astype(BF16)
                band_ds = band_ds.astype(BF16)
                outs.append(dot_n(band_ds, kx_ref[keys]) + dot_n(glob_ds, kg_ref[...]))
                probs.append((band.astype(BF16), glob.astype(BF16)))
                grads.append((band_ds, glob_ds))
            grads_q.append(jnp.where(low_lanes, outs[0], outs[1]))
            own_q = jnp.concatenate([own["q"][rows] for own in heads], 0)
            own_do = jnp.concatenate([own["do"][rows] for own in heads], 0)
            band, glob = (jnp.concatenate(part, 0) for part in zip(*probs))
            band_ds, glob_ds = (jnp.concatenate(part, 0) for part in zip(*grads))
            dkx[pair, keys] += t_dot(band_ds, own_q)
            dvx[pair, keys] += t_dot(band, own_do)
            dkg[pair] += t_dot(glob_ds, own_q)
            dvg[pair] += t_dot(glob, own_do)
        for kind, total in enumerate((dkg, dvg)):
            kv_send[:, pair, :, kind * PAIR : (kind + 1) * PAIR] = (
                total[pair].astype(BF16).reshape(seq_count, quarter, PAIR)
            )
        for copy in glob_copies(1, pair):
            copy.start()
        for kind, total in enumerate((dkx, dvx)):
            for direction, first in enumerate((HALO - REACH, HALO + block)):
                halo_send[direction, pair, kind] = total[pair, first : first + REACH].astype(BF16)
        for direction in range(2):

            @pl.when(sends_to[direction])
            def _(direction=direction):
                halo_copy(direction, pair).start()

        dq_ref[:block, lanes_of(pair)] = (jnp.concatenate(grads_q, 0) * scale).astype(BF16)
        for head in range(2):
            dtab_ref[pair, head : head + 1] = diagonal_sums(table_sums[head])

    def part(at, *refs):
        return [ref.at[:, at * PAIR : (at + 1) * PAIR] for ref in refs]

    @pl.when(number < steps)
    def _():
        for at in range(2):
            glob_pair(
                first_pair + at, *part(at, q_ref, kx_ref, vx_ref, kg_ref, vg_ref, dog_ref)
            )

    @pl.when(number >= steps)
    def _():
        for at in range(2):
            long_pair(
                first_pair + at,
                *part(at, q_ref, kx_ref, vx_ref, kg_ref, vg_ref, o_ref, do_ref),
                tab_ref.at[at : at + 1],
            )

    @pl.when(number > steps)
    def _():
        close_pair(first_pair - 2)
        close_pair(first_pair - 1)

    @pl.when(number == 2 * steps - 1)
    def _():
        if reduces:
            run_plan(2 * steps)
        close_pair(pairs - 2)
        close_pair(pairs - 1)
        for at in range(pairs):
            for kind in range(2):
                for copy in glob_copies(kind, at):
                    copy.wait_send()
            for direction in range(2):

                @pl.when(sends_to[direction])
                def _(direction=direction, at=at):
                    halo_copy(direction, at).wait_send()

        for copy in gathers():
            copy.wait_recv()
        glob_out[...] = every[:count]
        for copy in gathers():
            copy.wait_send()
        if reduces:
            reducer.finish()
            for z_sum, out in z_sums:
                z_sum.finish(out)


def attend_back(sizes, doc_len, table, q, kx, vx, kg, vg, o, do, l, dog, ldg, yq, *sums):
    block, count, quarter, seq_count, pairs = sizes
    width = q.shape[1]
    early_rows = sums[0].shape[-2] if sums else 0
    ext = block + 2 * HALO
    steps = pairs // 2
    cols = lambda rows: pl.BlockSpec((rows, 2 * PAIR), lambda i: (0, lax.rem(i, steps)))
    whole = pl.BlockSpec(memory_space=pltpu.VMEM)
    shape = jax.ShapeDtypeStruct
    in_specs = [
        pl.BlockSpec(memory_space=pltpu.SMEM),
        pl.BlockSpec((2, 2, WINDOW), lambda i: (lax.rem(i, steps), 0, 0)),
        cols(block + GP),
        cols(ext),
        cols(ext),
        cols(GP),
        cols(GP),
        cols(block),
        cols(block),
        whole,
        cols(GP),
        whole,
        whole,
    ]
    rows = block + quarter
    outs = [shape((rows, width), BF16)] * 3 + [shape((pairs, 2, WINDOW), F32)]
    outs.append(shape((count, width), BF16))
    others = seq_count - 1
    scratch = [
        pltpu.VMEM((pairs, ext, PAIR), F32),
        pltpu.VMEM((pairs, ext, PAIR), F32),
        pltpu.VMEM((pairs, GP, PAIR), F32),
        pltpu.VMEM((pairs, GP, PAIR), F32),
        pltpu.VMEM((seq_count, pairs, quarter, PAIR), BF16),
        pltpu.VMEM((others, pairs, quarter, PAIR), BF16),
        pltpu.VMEM((seq_count, pairs, quarter, 2 * PAIR), BF16),
        pltpu.VMEM((others, pairs, quarter, 2 * PAIR), BF16),
        pltpu.VMEM((2, pairs, 2, REACH, PAIR), BF16),
        pltpu.VMEM((2, pairs, 2, REACH, PAIR), BF16),
        pltpu.SemaphoreType.DMA((2, others, pairs)),
        pltpu.SemaphoreType.DMA((2, others, pairs)),
        pltpu.SemaphoreType.DMA((2, pairs)),
        pltpu.SemaphoreType.DMA((2, pairs)),
        pltpu.VMEM((GP, width), BF16),
        pltpu.SemaphoreType.DMA((others,)),
        pltpu.SemaphoreType.DMA((others,)),
    ]
    args = [doc_len, table, q, kx, vx, kg, vg, o, do, l, dog, ldg, yq, *sums]
    if early_rows:
        in_specs += [pl.BlockSpec(memory_space=pl.ANY)] * 3
        outs.append(shape((4, early_rows, width), BF16))
        scratch += Reducer.scratch(early_rows, width, 1)
        for parts in sums[1:]:
            outs.append(shape(parts.shape[1:], F32))
            scratch += ZSum.scratch(*parts.shape[1:])
    return pl.pallas_call(
        functools.partial(back_kernel, sizes, early_rows),
        grid=(2 * steps,),
        in_specs=in_specs,
        out_specs=[whole] * len(outs),
        out_shape=outs,
        scratch_shapes=scratch,
        compiler_params=pltpu.CompilerParams(
            collective_id=1, has_side_effects=True, vmem_limit_bytes=60 * 2**20
        ),
        name="attend_back",
    )(*args)


def on_device(
    long_input,
    global_input,
    lengths,
    w_query,
    b_query,
    w_key,
    w_value,
    b_value,
    w_out,
    b_out,
    w_inner,
    b_inner,
    w_outer,
    b_outer,
    norm1_gain,
    norm1_shift,
    norm2_gain,
    norm2_shift,
    rel_table,
    long_cotangent,
    global_cotangent,
):
    seq_count = lax.axis_size("seq")
    data_count = lax.axis_size("dp")
    seq_index = lax.axis_index("seq")
    block = long_input.shape[1]
    count = global_input.shape[1]
    width = long_input.shape[2]
    heads = rel_table.shape[1]
    pairs = heads // 2
    labels = 2 * R + 1
    quarter = GP // seq_count
    sizes = Sizes(block, count, quarter, seq_count, pairs)
    queries, kx, vx, kg, vg, attn_low, long_l, glob_l, glob_x, table = attend(
        sizes,
        lengths,
        rel_table.T,
        long_input[0],
        global_input[0],
        w_query,
        w_key,
        w_value,
        b_query,
        b_value,
        norm1_gain,
        norm1_shift,
    )
    planned = has_plan()
    long_result, own_out, grad_mid, grad_attn, every_do, every_ld, *gradients = feed_forward(
        sizes,
        planned,
        lengths,
        attn_low,
        long_input[0],
        glob_x,
        long_cotangent[0],
        global_cotangent[0],
        glob_l,
        w_out,
        b_out,
        norm2_gain,
        norm2_shift,
        w_inner,
        b_inner,
        w_outer,
        b_outer,
    )
    query_low, key_low, value_low, dtab, glob_out, *early = attend_back(
        sizes,
        lengths,
        table,
        queries,
        kx,
        vx,
        kg,
        vg,
        attn_low,
        grad_attn,
        long_l,
        every_do,
        every_ld,
        own_out,
        *(gradients if planned else []),
    )
    long_grad, glob_grad, *late = last_part(
        sizes,
        planned,
        long_input[0],
        glob_x,
        query_low,
        key_low,
        value_low,
        grad_mid,
        w_query,
        w_key,
        w_value,
        norm1_gain,
        norm1_shift,
        dtab,
        *early[:1],
    )
    if planned:
        (
            g_query,
            g_key,
            g_value,
            g_out,
            g_inner,
            g_outer,
            g_b_query,
            g_b_value,
            g_b_out,
            g_b_outer,
            g_g1,
            g_s1,
            g_g2,
            g_s2,
            g_b_inner,
            table_total,
            long_grad,
            long_result,
            glob_out,
            glob_grad,
        ) = small_results(
            heads,
            late[3],
            late[0],
            early[1],
            early[2],
            late[1],
            late[2],
            long_grad,
            long_result,
            glob_out,
            glob_grad,
        )
        table_total = table_total.T
        glob_grad = glob_grad.reshape(count, width)
    else:
        devices = data_count * seq_count
        own_part = lambda vector: lax.dynamic_slice_in_dim(
            vector,
            (lax.axis_index("dp") * seq_count + seq_index) * (vector.shape[0] // devices),
            vector.shape[0] // devices,
        )
        g_outer, g_inner, g_out, vectors = gradients
        g_outer, g_inner, g_out, g_query, g_key, g_value = (
            lax.psum_scatter(g.astype(BF16), ("dp", "seq"), scatter_dimension=0, tiled=True).astype(
                F32
            )
            for g in (g_outer, g_inner, g_out, *late[:3])
        )
        vectors, sums, scales = lax.psum((vectors, *late[3:]), ("dp", "seq"))
        g_b_query, g_b_value = (own_part(sums[heads + i]) for i in range(2))
        g_g1, g_s1 = (own_part(scales[i]) for i in range(2))
        g_b_out, g_b_outer, g_g2, g_s2 = (own_part(vectors[i]) for i in range(4))
        g_b_inner = own_part(vectors[4:].reshape(-1))
        table_total = sums[:heads, HALO - R : HALO - R + labels].T
    return (
        long_result[None],
        glob_out[None],
        long_grad[None],
        glob_grad[None],
        g_query,
        g_b_query,
        g_key,
        g_value,
        g_b_value,
        g_out,
        g_b_out,
        g_inner,
        g_b_inner,
        g_outer,
        g_b_outer,
        g_g1,
        g_s1,
        g_g2,
        g_s2,
        table_total,
    )


def solution(mesh):
    rows, whole = P("dp", "seq", None), P("dp", None, None)
    matrix, vector = P(("dp", "seq"), None), P(("dp", "seq"))
    return jax.shard_map(
        on_device,
        mesh=mesh,
        in_specs=(rows, whole, P("dp")) + (P(),) * 16 + (rows, whole),
        out_specs=(
            rows,
            whole,
            rows,
            whole,
            matrix,
            vector,
            matrix,
            matrix,
            vector,
            matrix,
            vector,
            matrix,
            vector,
            matrix,
            vector,
            vector,
            vector,
            vector,
            vector,
            P(),
        ),
        check_vma=False,
    )
```

```python
import functools
from typing import NamedTuple

import jax
import jax.numpy as jnp
from jax import lax
from jax.experimental import pallas as pl
from jax.experimental.pallas import tpu as pltpu
from jax.sharding import PartitionSpec as P

HD = 64
R = 84
PAIR = 2 * HD
HALO = 128
REACH = 96
GP = 256
SUB = 256
WINDOW = SUB + 2 * HALO
EPSILON = 1e-05
MASKED = -1e30
F32 = jnp.float32
BF16 = jnp.bfloat16


def dot_t(left, right):
    return lax.dot_general(left, right, (((1,), (1,)), ((), ())), preferred_element_type=F32)


def dot_n(left, right):
    return lax.dot_general(left, right, (((1,), (0,)), ((), ())), preferred_element_type=F32)


def t_dot(left, right):
    return lax.dot_general(left, right, (((0,), (0,)), ((), ())), preferred_element_type=F32)


def band_bias(table_row):
    spread = jnp.broadcast_to(table_row, (SUB, WINDOW))
    return pltpu.roll(spread, 0, 1, stride=1, stride_axis=0)


def diagonal_sums(rows):
    height, width = rows.shape
    while height > 8:
        height //= 2
        rows = rows[:height] + pltpu.roll(rows[height:], width - height, 1)
    row = lax.broadcasted_iota(jnp.int32, rows.shape, 0)
    for bit in (1, 2, 4):
        rows = jnp.where((row & bit) != 0, pltpu.roll(rows, width - bit, 1), rows)
    return jnp.sum(rows, 0, keepdims=True)


def lane_index():
    return lax.broadcasted_iota(jnp.int32, (1, PAIR), 1)


def own_half(head, value):
    low_lanes = lane_index() < HD
    return jnp.where(low_lanes if head == 0 else ~low_lanes, value, jnp.zeros_like(value))


def other_lane(head):
    return HD * (1 - head)


def with_lanes(head, value, columns):
    wide = own_half(head, value.astype(F32))
    lane = lane_index()
    for offset, column in enumerate(columns):
        wide = jnp.where(lane == other_lane(head) + offset, column, wide)
    return wide.astype(BF16)


def in_three(column):
    high = column.astype(BF16).astype(F32)
    middle = (column - high).astype(BF16).astype(F32)
    return (high, middle, column - high - middle)


def key_bias(first, rows, end):
    position = first + lax.broadcasted_iota(jnp.int32, (rows, 1), 0)
    return jnp.where((position >= 0) & (position < end), 0.0, MASKED)


def pick_column(rows, index):
    return jnp.sum(jnp.where(lane_index() == index, rows, 0.0), -1, keepdims=True)


def key_side(head, keys, bias):
    return with_lanes(head, keys, (bias, 1.0, 1.0, 1.0))


def value_side(head, values):
    return with_lanes(head, values, (1.0, 1.0, 1.0))


def softmax_rows(parts, value_parts, head):
    top = functools.reduce(
        jnp.maximum, [jnp.max(part, -1, keepdims=True) for part in parts]
    )
    mixed = sum(
        dot_n(jnp.exp(part - top).astype(BF16), values)
        for part, values in zip(parts, value_parts)
    )
    at = other_lane(head)
    total = mixed[:, at : at + 1]
    return mixed / total, top + jnp.log(total)


def seq_device(steps, seq_count):
    return (lax.axis_index("dp"), lax.rem(lax.axis_index("seq") + steps + seq_count, seq_count))


def row_norm(rows):
    centred = rows - jnp.mean(rows, -1, keepdims=True)
    inverse = lax.rsqrt(jnp.mean(centred * centred, -1, keepdims=True) + EPSILON)
    return centred * inverse, inverse


def put_column(ref, rows, index, column):
    ref[rows] = jnp.where(lane_index() == index, column, ref[rows])


def lanes_of(at):
    return pl.ds(pl.multiple_of(at * PAIR, PAIR), PAIR)


class Sizes(NamedTuple):
    block: int
    count: int
    quarter: int
    seq_count: int
    pairs: int


def attend_kernel(
    sizes,
    len_ref,
    rel_ref,
    long_ref,
    raw_ref,
    wq_far,
    wk_far,
    wv_far,
    bq_ref,
    bv_ref,
    gain_ref,
    shift_ref,
    q_far,
    kx_far,
    vx_far,
    kg_far,
    vg_far,
    o_ref,
    l_ref,
    lq_ref,
    glob_ref,
    tab_ref,
    spread,
    wide,
    part_o,
    part_l,
    from_o,
    from_l,
    halo_sends,
    halo_recvs,
    part_sends,
    part_recvs,
    wq_ref,
    wk_ref,
    wv_ref,
    loads,
    q_ref,
    kx_ref,
    vx_ref,
    kg_ref,
    vg_ref,
    stores,
):
    block, count, quarter, seq_count, pairs = sizes
    ext = block + 2 * HALO
    seq_index = lax.axis_index("seq")
    scale = jnp.asarray(HD ** (-0.5), BF16)
    low_lanes = lane_index() < HD
    own_keys = slice(HALO, HALO + block)
    own_rows = pl.ds(pl.multiple_of(seq_index * quarter, quarter), quarter)
    neighbours = (seq_index > 0, seq_index < seq_count - 1)
    barrier = pltpu.get_barrier_semaphore()
    for step in range(1, seq_count):
        pl.semaphore_signal(
            barrier,
            inc=1,
            device_id=seq_device(step, seq_count),
            device_id_type=pl.DeviceIdType.MESH,
        )

    def halo_copies(direction):
        source = HALO if direction == 0 else HALO + block - REACH
        dest = HALO + block if direction == 0 else HALO - REACH
        for kind, ref in enumerate((kx_ref, vx_ref)):
            yield pltpu.make_async_remote_copy(
                src_ref=ref.at[source : source + REACH],
                dst_ref=ref.at[dest : dest + REACH],
                send_sem=halo_sends.at[direction, kind],
                recv_sem=halo_recvs.at[direction, kind],
                device_id=seq_device(2 * direction - 1, seq_count),
                device_id_type=pl.DeviceIdType.MESH,
            )

    def part_copies():
        for step in range(1, seq_count):
            device = seq_device(step, seq_count)
            rows = pl.ds(pl.multiple_of(device[1] * quarter, quarter), quarter)
            for kind, (source, dest) in enumerate(((part_o, from_o), (part_l, from_l))):
                yield step, kind, pltpu.make_async_remote_copy(
                    src_ref=source.at[rows],
                    dst_ref=dest.at[step - 1],
                    send_sem=part_sends.at[kind, step - 1],
                    recv_sem=part_recvs.at[kind, step - 1],
                    device_id=device,
                    device_id_type=pl.DeviceIdType.MESH,
                )

    loading = [
        pltpu.make_async_copy(source, dest, loads.at[at])
        for at, (source, dest) in enumerate(
            ((wk_far, wk_ref), (wv_far, wv_ref), (wq_far, wq_ref))
        )
    ]
    for copy in loading:
        copy.start()
    gain, shift = gain_ref[...], shift_ref[...]
    heads, labels = rel_ref.shape
    spread[...] = jnp.full(spread.shape, MASKED, F32)
    spread[:heads, :labels] = rel_ref[...]
    turned = pltpu.roll(spread[...], HALO - R, 1)
    for pair in range(pairs):
        tab_ref[pair] = turned[2 * pair : 2 * pair + 2]
    normed_long = (row_norm(long_ref[...].astype(F32))[0] * gain + shift).astype(BF16)
    loading[0].wait()
    kx_ref[own_keys] = dot_n(normed_long, wk_ref[...]).astype(BF16)
    loading[1].wait()
    vx_ref[own_keys] = (dot_n(normed_long, wv_ref[...]) + bv_ref[...]).astype(BF16)
    pl.semaphore_wait(barrier, seq_count - 1)
    for direction, first in enumerate((HALO - REACH, HALO + block)):

        @pl.when(neighbours[direction])
        def _(direction=direction):
            for copy in halo_copies(direction):
                copy.start()

        outer = slice(0, first) if direction == 0 else slice(first + REACH, ext)
        for ref in (kx_ref, vx_ref):
            ref[outer] = jnp.zeros((HALO - REACH, ref.shape[1]), BF16)

        @pl.when(jnp.logical_not(neighbours[direction]))
        def _(first=first):
            for ref in (kx_ref, vx_ref):
                ref[first : first + REACH] = jnp.zeros((REACH, ref.shape[1]), BF16)

    wide[...] = jnp.zeros_like(wide)
    wide[:count] = raw_ref[...].astype(F32)
    glob_ref[...] = wide[...].astype(BF16)
    normed_glob = (row_norm(wide[...])[0] * gain + shift).astype(BF16)
    kg_ref[...] = dot_n(normed_glob, wk_ref[...]).astype(BF16)
    vg_ref[...] = (dot_n(normed_glob, wv_ref[...]) + bv_ref[...]).astype(BF16)
    loading[2].wait()
    q_ref[block:] = (dot_n(normed_glob, wq_ref[...]) + bq_ref[...]).astype(BF16)
    q_ref[:block] = (dot_n(normed_long, wq_ref[...]) + bq_ref[...]).astype(BF16)
    part_l[...] = jnp.zeros_like(part_l)
    l_ref[...] = jnp.zeros_like(l_ref)

    def glob_pair(pair, carry):
        lanes = lanes_of(pair)
        far_bias = key_bias(seq_index * block, block, len_ref[0])
        near_bias = key_bias(seq_index * quarter, quarter, count)
        query = q_ref[block:, lanes] * scale
        outs = []
        for head in range(2):
            q = with_lanes(head, query, (1.0,))
            far = dot_t(q, with_lanes(head, kx_ref[own_keys, lanes], (far_bias,)))
            near = dot_t(q, with_lanes(head, kg_ref[own_rows, lanes], (near_bias,)))
            out, norm = softmax_rows(
                [far, near],
                [
                    with_lanes(head, vx_ref[own_keys, lanes], (1.0,)),
                    with_lanes(head, vg_ref[own_rows, lanes], (1.0,)),
                ],
                head,
            )
            outs.append(out)
            put_column(part_l, slice(None), 2 * pair + head, norm)
        part_o[:, lanes] = jnp.where(low_lanes, outs[0], outs[1]).astype(BF16)
        return carry

    lax.fori_loop(0, pairs, glob_pair, 0, unroll=2)
    for _, _, copy in part_copies():
        copy.start()
    for direction in range(2):

        @pl.when(neighbours[1 - direction])
        def _(direction=direction):
            for copy in halo_copies(direction):
                copy.wait_recv()

    storing = [
        pltpu.make_async_copy(source, dest, stores.at[at])
        for at, (source, dest) in enumerate(
            (
                (q_ref, q_far),
                (kx_ref, kx_far),
                (vx_ref, vx_far),
                (kg_ref, kg_far),
                (vg_ref, vg_far),
            )
        )
    ]
    for copy in storing:
        copy.start()

    def long_pair(pair, carry):
        lanes = lanes_of(pair)
        long_bias = key_bias(seq_index * block - HALO, ext, len_ref[0])
        glob_bias = key_bias(0, GP, count)
        query = q_ref[:block, lanes] * scale
        outs = []
        for head in range(2):
            q = with_lanes(head, query, (1.0,))
            kx = with_lanes(head, kx_ref[:, lanes], (long_bias,))
            kg = with_lanes(head, kg_ref[:, lanes], (glob_bias,))
            vx, vg = (with_lanes(head, ref[:, lanes], (1.0,)) for ref in (vx_ref, vg_ref))
            bias = band_bias(tab_ref[pair, head : head + 1])
            mixed = []
            for start in range(0, block, SUB):
                rows, keys = slice(start, start + SUB), slice(start, start + WINDOW)
                out, norm = softmax_rows(
                    [dot_t(q[rows], kx[keys]) + bias, dot_t(q[rows], kg)], [vx[keys], vg], head
                )
                mixed.append(out)
                put_column(l_ref, rows, 2 * pair + head, norm)
            outs.append(jnp.concatenate(mixed, 0))
        o_ref[:block, lanes] = jnp.where(low_lanes, outs[0], outs[1]).astype(BF16)
        return carry

    lax.fori_loop(0, pairs, long_pair, 0, unroll=2)
    for _, _, copy in part_copies():
        copy.wait_recv()
    norms = [part_l[own_rows]] + [from_l[step] for step in range(seq_count - 1)]
    outs = [part_o[own_rows]] + [from_o[step] for step in range(seq_count - 1)]
    top = functools.reduce(jnp.maximum, norms)
    shares = [jnp.exp(norm - top) for norm in norms]
    total = sum(shares)
    lq_ref[...] = top + jnp.log(total)
    shares = [share / total for share in shares]
    for at in range(pairs):
        lanes = slice(at * PAIR, (at + 1) * PAIR)
        mixed = 0.0
        for share, out in zip(shares, outs):
            spread = jnp.where(
                low_lanes, share[:, 2 * at : 2 * at + 1], share[:, 2 * at + 1 : 2 * at + 2]
            )
            mixed += spread * out[:, lanes].astype(F32)
        o_ref[block:, lanes] = mixed.astype(BF16)
    for copy in storing:
        copy.wait()
    for _, _, copy in part_copies():
        copy.wait_send()
    for direction in range(2):

        @pl.when(neighbours[direction])
        def _(direction=direction):
            for copy in halo_copies(direction):
                copy.wait_send()


def attend(sizes, doc_len, rel_table, long_x, glob_x, *weights):
    block, count, quarter, seq_count, pairs = sizes
    width = long_x.shape[1]
    ext = block + 2 * HALO
    whole = pl.BlockSpec(memory_space=pltpu.VMEM)
    shape = jax.ShapeDtypeStruct
    others = seq_count - 1
    return pl.pallas_call(
        functools.partial(attend_kernel, sizes),
        in_specs=[pl.BlockSpec(memory_space=pltpu.SMEM)]
        + [whole] * 3
        + [pl.BlockSpec(memory_space=pl.ANY)] * 3
        + [whole] * 4,
        out_specs=[pl.BlockSpec(memory_space=pl.ANY)] * 5 + [whole] * 5,
        out_shape=[
            shape((block + GP, width), BF16),
            shape((ext, width), BF16),
            shape((ext, width), BF16),
            shape((GP, width), BF16),
            shape((GP, width), BF16),
            shape((block + quarter, width), BF16),
            shape((block, PAIR), F32),
            shape((quarter, PAIR), F32),
            shape((GP, width), BF16),
            shape((pairs, 2, WINDOW), F32),
        ],
        scratch_shapes=[
            pltpu.VMEM(((2 * pairs + 7) // 8 * 8, WINDOW), F32),
            pltpu.VMEM((GP, width), F32),
            pltpu.VMEM((GP, width), BF16),
            pltpu.VMEM((GP, PAIR), F32),
            pltpu.VMEM((others, quarter, width), BF16),
            pltpu.VMEM((others, quarter, PAIR), F32),
            pltpu.SemaphoreType.DMA((2, 2)),
            pltpu.SemaphoreType.DMA((2, 2)),
            pltpu.SemaphoreType.DMA((2, others)),
            pltpu.SemaphoreType.DMA((2, others)),
            pltpu.VMEM((width, width), BF16),
            pltpu.VMEM((width, width), BF16),
            pltpu.VMEM((width, width), BF16),
            pltpu.SemaphoreType.DMA((3,)),
            pltpu.VMEM((block + GP, width), BF16),
            pltpu.VMEM((ext, width), BF16),
            pltpu.VMEM((ext, width), BF16),
            pltpu.VMEM((GP, width), BF16),
            pltpu.VMEM((GP, width), BF16),
            pltpu.SemaphoreType.DMA((5,)),
        ],
        compiler_params=pltpu.CompilerParams(
            collective_id=3, has_side_effects=True, vmem_limit_bytes=56 * 2**20
        ),
        name="attend",
    )(doc_len, rel_table, long_x, glob_x, *weights)


class Reducer:
    def __init__(self, rows, split, scratch, pieces=None, order=None, parts=None):
        self.ids = mesh_ids()
        self.parts = parts
        self.order = order
        self.halves = (slice(0, split), slice(split, rows))
        held, self.from_core, self.from_one, self.from_two = scratch[:4]
        self.local, self.sends, self.recvs = scratch[4:7]
        if parts is None:
            self.from_z, self.z_sends, self.z_recvs = scratch[7:]
        self.pieces, self.held = pieces, held
        self.mine = held.at[self.ids[3]] if pieces is None else held.at[0]

    @staticmethod
    def scratch(rows, width, sides, with_z=False):
        buffers = [
            pltpu.VMEM((sides, 4, 2, 2, rows, width), BF16),
            pltpu.VMEM((4, 2, 2, rows, width), BF16),
            pltpu.VMEM((4, 2, rows, width), BF16),
            pltpu.VMEM((4, rows, width), BF16),
            pltpu.SemaphoreType.DMA((4,)),
            pltpu.SemaphoreType.DMA((5, 4)),
            pltpu.SemaphoreType.DMA((5, 4)),
        ]
        if with_z:
            buffers += [
                pltpu.VMEM((3, rows, width), BF16),
                pltpu.SemaphoreType.DMA((4,)),
                pltpu.SemaphoreType.DMA((3,)),
            ]
        return buffers

    def partners(self):
        z, y, x, core = self.ids
        dp, seq = z * 2 + y, x * 2 + core
        near = [(dp, x * 2 + 1 - core), (dp, (1 - x) * 2 + core), (z * 2 + 1 - y, seq)]
        return near + [(lax.rem(z + step, 4) * 2 + y, seq) for step in (1, 2, 3)]

    def target(self, chunk):
        return self.order(chunk) if self.order else lax.rem(self.ids[0] + 1 + chunk, 4)

    def remote(self, source, dest, kind, send_at, recv_at, device):
        return pltpu.make_async_remote_copy(
            src_ref=source,
            dst_ref=dest,
            send_sem=self.sends.at[kind, send_at],
            recv_sem=self.recvs.at[kind, recv_at],
            device_id=device,
            device_id_type=pl.DeviceIdType.MESH,
        )

    def own_copy(self, chunk):
        core, to = self.ids[3], self.target(chunk)
        return pltpu.make_async_copy(
            self.pieces.at[core, to], self.mine.at[to], self.local.at[chunk]
        )

    def core_copy(self, chunk):
        core, to = self.ids[3], self.target(chunk)
        source = (self.held if self.pieces is None else self.pieces).at[1 - core, to]
        return self.remote(source, self.from_core.at[to], 0, chunk, chunk, self.partners()[0])

    def first_copies(self, chunk):
        z, y, x, core = self.ids
        to = self.target(chunk)
        one, two = self.halves
        near = self.partners()
        return (
            self.remote(
                self.mine.at[to, :, 1 - x, one],
                self.from_one.at[to, :, one],
                1,
                chunk,
                chunk,
                near[1],
            ),
            self.remote(
                self.mine.at[to, 1 - y, :, two],
                self.from_one.at[to, :, two],
                2,
                chunk,
                chunk,
                near[2],
            ),
        )

    def second_copies(self, chunk):
        z, y, x, core = self.ids
        to = self.target(chunk)
        one, two = self.halves
        near = self.partners()
        return (
            self.remote(
                self.mine.at[to, 1 - y, x, one],
                self.from_two.at[to, one],
                3,
                chunk,
                chunk,
                near[2],
            ),
            self.remote(
                self.mine.at[to, y, 1 - x, two],
                self.from_two.at[to, two],
                4,
                chunk,
                chunk,
                near[1],
            ),
        )

    def last_copy(self, chunk):
        z, y, x, core = self.ids
        to = self.target(chunk)
        slot = lax.rem(z - to + 4, 4) - 1
        return pltpu.make_async_remote_copy(
            src_ref=self.mine.at[to, y, x],
            dst_ref=self.from_z.at[slot],
            send_sem=self.z_sends.at[chunk],
            recv_sem=self.z_recvs.at[slot],
            device_id=(to * 2 + y, x * 2 + core),
            device_id_type=pl.DeviceIdType.MESH,
        )

    def arrival(self, slot):
        z, y, x, core = self.ids
        return pltpu.make_async_remote_copy(
            src_ref=self.mine.at[z, y, x],
            dst_ref=self.from_z.at[slot],
            send_sem=self.z_sends.at[slot],
            recv_sem=self.z_recvs.at[slot],
            device_id=self.partners()[3],
            device_id_type=pl.DeviceIdType.MESH,
        )

    def leaves(self, chunk):
        return self.target(chunk) != self.ids[0]

    def fill(self, to, at, value):
        self.held[at % 2, to, at // 4, at // 2 % 2] = value.astype(BF16)

    def start(self, chunk):
        self.core_copy(chunk).start()
        if self.pieces is not None:
            self.own_copy(chunk).start()

    def add_core(self, chunk):
        to = self.target(chunk)
        if self.pieces is not None:
            self.own_copy(chunk).wait()
        self.core_copy(chunk).wait_recv()

        def add(index, carry):
            at = (to, lax.div(index, 2), lax.rem(index, 2))
            self.mine[at] = self.mine[at] + self.from_core[at]
            return carry

        lax.fori_loop(0, 4, add, 0)
        for copy in self.first_copies(chunk):
            copy.start()

    def add_first(self, chunk):
        z, y, x, core = self.ids
        one, two = self.halves
        to = self.target(chunk)
        for copy in self.first_copies(chunk):
            copy.wait_recv()

        def add(index, carry):
            for at, rows in (((to, index, x), one), ((to, y, index), two)):
                self.mine[at + (rows,)] = self.mine[at + (rows,)] + self.from_one[to, index, rows]
            return carry

        lax.fori_loop(0, 2, add, 0)
        for copy in self.second_copies(chunk):
            copy.start()

    def add_second(self, chunk):
        z, y, x, core = self.ids
        to = self.target(chunk)
        for copy in self.second_copies(chunk):
            copy.wait_recv()
        if self.parts is not None:
            self.parts[to] = self.mine[to, y, x] + self.from_two[to]
            return

        @pl.when(self.leaves(chunk))
        def _():
            self.mine[to, y, x] = self.mine[to, y, x] + self.from_two[to]
            self.last_copy(chunk).start()

    def finish(self, out=None):
        z, y, x, core = self.ids
        if self.parts is None:
            total = self.mine[z, y, x].astype(F32) + self.from_two[z].astype(F32)
            for slot in range(3):
                self.arrival(slot).wait_recv()
                total += self.from_z[slot].astype(F32)
            out[...] = total
        for chunk in range(4):
            self.core_copy(chunk).wait_send()
            for copy in self.first_copies(chunk) + self.second_copies(chunk):
                copy.wait_send()
            if self.parts is None:

                @pl.when(self.leaves(chunk))
                def _(chunk=chunk):
                    self.last_copy(chunk).wait_send()


class ZSum:
    def __init__(self, parts, scratch):
        self.ids = mesh_ids()
        self.parts = parts
        self.own, self.from_z, self.local, self.sends, self.recvs = scratch

    @staticmethod
    def scratch(rows, width):
        return [
            pltpu.VMEM((rows, width), BF16),
            pltpu.VMEM((3, rows, width), BF16),
            pltpu.SemaphoreType.DMA,
            pltpu.SemaphoreType.DMA((3,)),
            pltpu.SemaphoreType.DMA((3,)),
        ]

    def own_copy(self):
        return pltpu.make_async_copy(self.parts.at[self.ids[0]], self.own, self.local)

    def copies(self):
        z, y, x, core = self.ids
        for slot in range(3):
            to = lax.rem(z + 3 - slot, 4)
            yield pltpu.make_async_remote_copy(
                src_ref=self.parts.at[to],
                dst_ref=self.from_z.at[slot],
                send_sem=self.sends.at[slot],
                recv_sem=self.recvs.at[slot],
                device_id=(to * 2 + y, x * 2 + core),
                device_id_type=pl.DeviceIdType.MESH,
            )

    def start(self):
        self.own_copy().start()
        for copy in self.copies():
            copy.start()

    def finish(self, out):
        self.own_copy().wait()
        total = self.own[...].astype(F32)
        for slot, copy in enumerate(self.copies()):
            copy.wait_recv()
            total += self.from_z[slot].astype(F32)
        out[...] = total
        for copy in self.copies():
            copy.wait_send()


class EverySum:
    def __init__(self, scratch):
        self.kept, self.arrived, self.from_z, self.sends, self.recvs = scratch
        z, y, x, core = mesh_ids()
        seq = x * 2 + core
        self.z = z
        self.pairs = (
            (z * 2 + y, x * 2 + 1 - core),
            (z * 2 + y, (1 - x) * 2 + core),
            (z * 2 + 1 - y, seq),
        )
        self.along_z = [(lax.rem(z + step, 4) * 2 + y, seq) for step in (1, 2, 3)]

    @staticmethod
    def scratch(rows, width):
        return [
            pltpu.VMEM((3, rows, width), F32),
            pltpu.VMEM((3, rows, width), F32),
            pltpu.VMEM((4, rows, width), F32),
            pltpu.SemaphoreType.DMA((6,)),
            pltpu.SemaphoreType.DMA((6,)),
        ]

    def copy(self, stage):
        return pltpu.make_async_remote_copy(
            src_ref=self.kept.at[stage],
            dst_ref=self.arrived.at[stage],
            send_sem=self.sends.at[stage],
            recv_sem=self.recvs.at[stage],
            device_id=self.pairs[stage],
            device_id_type=pl.DeviceIdType.MESH,
        )

    def z_copies(self):
        for at, device in enumerate(self.along_z):
            yield pltpu.make_async_remote_copy(
                src_ref=self.from_z.at[self.z],
                dst_ref=self.from_z.at[self.z],
                send_sem=self.sends.at[3 + at],
                recv_sem=self.recvs.at[3 + at],
                device_id=device,
                device_id_type=pl.DeviceIdType.MESH,
            )

    def step(self, stage):
        if stage > 0:
            self.copy(stage - 1).wait_recv()
            total = self.kept[stage - 1] + self.arrived[stage - 1]
            if stage < 3:
                self.kept[stage] = total
            else:
                self.from_z[self.z] = total
        if stage < 3:
            self.copy(stage).start()
        else:
            for copy in self.z_copies():
                copy.start()

    def finish(self, out):
        for copy in self.z_copies():
            copy.wait_recv()
        out[...] = (self.from_z[0] + self.from_z[1]) + (self.from_z[2] + self.from_z[3])
        for copy in [self.copy(stage) for stage in range(3)] + list(self.z_copies()):
            copy.wait_send()


def mesh_ids():
    dp, seq = lax.axis_index("dp"), lax.axis_index("seq")
    return lax.div(dp, 2), lax.rem(dp, 2), lax.div(seq, 2), lax.rem(seq, 2)


def meet(devices):
    barrier = pltpu.get_barrier_semaphore()
    for device in devices:
        pl.semaphore_signal(barrier, inc=1, device_id=device, device_id_type=pl.DeviceIdType.MESH)
    pl.semaphore_wait(barrier, len(devices))


EARLY_PLAN = (
    (1, "add_core", 0),
    (1, "add_core", 1),
    (2, "add_core", 2),
    (2, "add_core", 3),
    (4, "add_first", 0),
    (4, "add_first", 1),
    (5, "add_first", 2),
    (5, "add_first", 3),
    (5, "add_second", 0),
    (6, "add_second", 1),
    (6, "add_second", 2),
    (6, "add_second", 3),
)


def late_kernel(
    sizes,
    planned,
    long_ref,
    glob_ref,
    dq_ref,
    dk_ref,
    dv_ref,
    dmid_far,
    wq_far,
    wk_far,
    wv_far,
    gain_ref,
    shift_ref,
    table_ref,
    *rest,
):
    block, count, quarter, seq_count, pairs = sizes
    rows = block + quarter
    width = long_ref.shape[1]
    if planned:
        early_parts, long_far, glob_out, late_ref, total_ref, scale_ref, early_ref, *rest = rest
    else:
        long_far, glob_out, gq_ref, gk_ref, gv_ref, total_ref, scale_ref, *rest = rest
    normed_t, every, gather_sends, gather_recvs, *rest = rest
    dmid_ref, wq_ref, wk_ref, wv_ref, loads, long_out, store, *rest = rest
    storing = pltpu.make_async_copy(long_out, long_far, store)
    far = (wq_far, wk_far, wv_far, dmid_far)
    loading = [
        pltpu.make_async_copy(source, dest, loads.at[at])
        for at, (source, dest) in enumerate(zip(far, (wq_ref, wk_ref, wv_ref, dmid_ref)))
    ]
    for copy in loading:
        copy.start()
    seq_index = lax.axis_index("seq")
    own_rows = pl.ds(pl.multiple_of(seq_index * quarter, quarter), quarter)
    others = [seq_device(step, seq_count) for step in range(1, seq_count)]

    def gathers():
        for step, device in enumerate(others):
            yield pltpu.make_async_remote_copy(
                src_ref=every.at[own_rows],
                dst_ref=every.at[own_rows],
                send_sem=gather_sends.at[step],
                recv_sem=gather_recvs.at[step],
                device_id=device,
                device_id_type=pl.DeviceIdType.MESH,
            )

    if planned:
        first_sum, second_sum = EverySum(rest[:5]), EverySum(rest[5:10])
        z_sum = ZSum(early_parts, rest[10:15])
        reducer = Reducer(rest[15].shape[-2], 32, rest[15:])

    meet(others + (reducer.partners()[2:] if planned else []))
    heads = 2 * pairs
    first = first_sum.kept.at[0] if planned else total_ref
    first[...] = jnp.zeros(first.shape, F32)
    for pair in range(pairs):
        first[2 * pair : 2 * pair + 2, :WINDOW] = table_ref[pair]
    for at, ref in enumerate((dq_ref, dv_ref)):
        first[heads + at : heads + at + 1] = column_sum(ref[...].astype(F32))
    if planned:
        first_sum.step(0)
        z_sum.start()
    everything = jnp.concatenate([long_ref[...], glob_ref[own_rows]], 0).astype(F32)
    hat, inverse = row_norm(everything)
    normed_t[...] = (hat * gain_ref[...] + shift_ref[...]).astype(BF16).T
    if planned:
        piece = width // 32
        blank = jnp.zeros((8, width), F32)
        def weight_rows(chunk):
            to = reducer.target(chunk)
            some = normed_t[pl.ds(pl.multiple_of(to * 8 * piece, 64), 8 * piece)]
            parts = [dot_n(some, ref[...]) for ref in (dq_ref, dk_ref, dv_ref)]
            for at in range(8):
                rows_at = slice(at * piece, (at + 1) * piece)
                reducer.fill(
                    to, at, jnp.concatenate([part[rows_at] for part in parts] + [blank], 0)
                )
            reducer.start(chunk)

        weight_rows(0)
        first_sum.step(1)
        weight_rows(1)
        first_sum.step(2)
        reducer.add_core(0)
        weight_rows(2)
        first_sum.step(3)
        reducer.add_core(1)
        weight_rows(3)
        for copy in loading:
            copy.wait()
        grads = dot_t(dq_ref[...], wq_ref[...])
        grads += dot_t(dk_ref[...], wk_ref[...]) + dot_t(dv_ref[...], wv_ref[...])
        reducer.add_first(0)
        reducer.add_core(2)
    else:
        for ref, out in ((dq_ref, gq_ref), (dk_ref, gk_ref), (dv_ref, gv_ref)):
            out[...] = dot_n(normed_t[...], ref[...]).astype(BF16)
        for copy in loading:
            copy.wait()
        grads = (
            dot_t(dq_ref[...], wq_ref[...])
            + dot_t(dk_ref[...], wk_ref[...])
            + dot_t(dv_ref[...], wv_ref[...])
        )
    scaled = grads * gain_ref[...]
    total = dmid_ref[...] + inverse * (
        scaled
        - jnp.mean(scaled, -1, keepdims=True)
        - hat * jnp.mean(scaled * hat, -1, keepdims=True)
    )
    every[own_rows] = total[block:].astype(BF16)
    for copy in gathers():
        copy.start()
    long_out[...] = total[:block]
    storing.start()
    second = second_sum.kept.at[0] if planned else scale_ref
    second[...] = jnp.zeros(second.shape, F32)
    second[0:1] = column_sum(grads * hat)
    second[1:2] = column_sum(grads)
    if planned:
        second_sum.step(0)
        reducer.add_first(1)
        second_sum.step(1)
        reducer.add_core(3)
        reducer.add_second(0)
        reducer.add_first(2)
        second_sum.step(2)
        reducer.add_second(1)
        reducer.add_first(3)
        second_sum.step(3)
        reducer.add_second(2)
        reducer.add_second(3)
        first_sum.finish(total_ref)
        z_sum.finish(early_ref)
        reducer.finish(late_ref)
        second_sum.finish(scale_ref)
    for copy in gathers():
        copy.wait_recv()
    glob_out[...] = every[:count].astype(F32)
    storing.wait()
    for copy in gathers():
        copy.wait_send()


def last_part(sizes, planned, long_x, glob_x, dq, dk, dv, dmid, *weights):
    block, count, quarter, seq_count, pairs = sizes
    rows, width = dq.shape
    others = seq_count - 1
    whole = pl.BlockSpec(memory_space=pltpu.VMEM)
    there = pl.BlockSpec(memory_space=pl.ANY)
    shape = jax.ShapeDtypeStruct
    sums = [shape(((2 * pairs + 2 + 7) // 8 * 8, width), F32), shape((8, width), F32)]
    outs = [shape((block, width), F32), shape((count, width), F32)]
    scratch = [
        pltpu.VMEM((width, rows), BF16),
        pltpu.VMEM((GP, width), BF16),
        pltpu.SemaphoreType.DMA((others,)),
        pltpu.SemaphoreType.DMA((others,)),
        pltpu.VMEM((rows, width), F32),
        pltpu.VMEM((width, width), BF16),
        pltpu.VMEM((width, width), BF16),
        pltpu.VMEM((width, width), BF16),
        pltpu.SemaphoreType.DMA((4,)),
        pltpu.VMEM((block, width), F32),
        pltpu.SemaphoreType.DMA,
    ]
    if planned:
        piece = width // 32
        part = 3 * piece + 8
        early = weights[-1].shape[1:]
        outs += [shape((part, width), F32), *sums, shape(early, F32)]
        for part_sums in sums:
            scratch += EverySum.scratch(*part_sums.shape)
        scratch += ZSum.scratch(*early) + Reducer.scratch(part, width, 2, with_z=True)
    else:
        outs += [shape((width, width), BF16)] * 3 + sums
    return pl.pallas_call(
        functools.partial(late_kernel, sizes, planned),
        in_specs=[whole] * 5 + [there] * 4 + [whole] * 3 + [there] * planned,
        out_specs=[there] + [whole] * (len(outs) - 1),
        out_shape=outs,
        scratch_shapes=scratch,
        compiler_params=pltpu.CompilerParams(
            collective_id=2, has_side_effects=True, vmem_limit_bytes=60 * 2**20
        ),
        name="last_part",
    )(long_x, glob_x, dq, dk, dv, dmid, *weights)


def small_kernel(heads, early_ref, late_ref, outer_ref, inner_ref, sums_ref, scale_ref, *rest):
    outs = rest[3:-3]
    for source, out in zip(rest[:2], rest[-3:]):
        out[...] = source[...]
    rest[-1][...] = rest[2][...].reshape(rest[-1].shape)
    g_query, g_key, g_value, g_out, g_inner, g_outer, *vectors, table = outs
    device = lax.axis_index("dp") * lax.axis_size("seq") + lax.axis_index("seq")
    piece, width = g_query.shape
    for at, out in enumerate((g_query, g_key, g_value)):
        out[...] = late_ref[at * piece : (at + 1) * piece]
    g_out[...] = early_ref[2 * piece : 3 * piece]
    g_outer[...] = outer_ref[...]
    for source, first, chunk in (
        (inner_ref, 0, 0),
        (inner_ref, piece, 3),
        (early_ref, 0, 1),
        (early_ref, piece, 2),
    ):
        g_inner[:, chunk * width : (chunk + 1) * width] = source[first : first + piece]

    def entries(row, at, length):
        return pltpu.roll(row, width - at * length, 1)[0, :length]

    b_query, b_value, b_out, b_outer, gain_one, shift_one, gain_two, shift_two, b_inner = vectors
    for at, out in enumerate((b_query, b_value)):
        out[...] = entries(sums_ref[heads + at : heads + at + 1], device, piece)
    for at, out in enumerate((gain_one, shift_one)):
        out[...] = entries(scale_ref[at : at + 1], device, piece)
    for at, out in enumerate((b_out, b_outer, gain_two, shift_two)):
        row = 3 * piece + at
        out[...] = entries(early_ref[row : row + 1], device, piece)
    row = pl.ds(3 * piece + 4 + lax.div(device, 8), 1)
    b_inner[...] = entries(early_ref[row], lax.rem(device, 8), 4 * piece)
    labels = table.shape[1]
    turned = pltpu.roll(sums_ref[:, :WINDOW], WINDOW - HALO + R, 1)
    table[...] = turned[:heads, :labels]


def small_results(heads, early, late, outer, inner, sums, scales, *big):
    width = early.shape[1]
    piece = width // 32
    shape = jax.ShapeDtypeStruct
    whole = pl.BlockSpec(memory_space=pltpu.VMEM)
    outs = [shape((piece, width), F32)] * 4
    outs += [shape((piece, 4 * width), F32), shape((4 * piece, width), F32)]
    outs += [shape((piece,), F32)] * 8 + [shape((4 * piece,), F32)]
    outs += [shape((heads, 2 * R + 1), F32)]
    outs += [shape(part.shape, part.dtype) for part in big[:2]]
    outs.append(shape((big[2].shape[0], 1, width), F32))
    return pl.pallas_call(
        functools.partial(small_kernel, heads),
        in_specs=[whole] * 9,
        out_specs=[whole] * len(outs),
        out_shape=outs,
        name="small_results",
    )(early, late, outer, inner, sums, scales, *big)


def has_plan():
    return (lax.axis_size("dp"), lax.axis_size("seq")) == (8, 4)


GELU_A = 0.7978845608028654
GELU_B = 0.044715


def gate_both(u):
    square = u * u
    turned = jnp.tanh(GELU_A * u * (1.0 + GELU_B * square))
    half = 0.5 * (1.0 + turned)
    slope = half + 0.5 * u * (1.0 - turned * turned) * (
        GELU_A * (1.0 + 3.0 * GELU_B * square)
    )
    return u * half, slope


def column_sum(rows):
    return jnp.sum(rows, 0, keepdims=True)


def ffn_kernel(
    sizes,
    planned,
    len_ref,
    attn_ref,
    long_ref,
    glob_ref,
    dlong_ref,
    dglob_ref,
    lq_ref,
    wo_ref,
    bo_ref,
    gain_ref,
    shift_ref,
    wi_ref,
    bi_ref,
    wr_ref,
    br_ref,
    long_out,
    glob_out,
    dmid_far,
    do_far,
    dog_ref,
    ldg_ref,
    *rest,
):
    block, count, quarter, seq_count, pairs = sizes
    if planned:
        pieces_far, outer_ref, inner_ref, *rest = rest
    else:
        g_outer_ref, g_inner_ref, g_out_ref, vec_ref, *rest = rest
    (
        mid,
        y_sum,
        df_sum,
        normed,
        normed_t,
        dy,
        vectors,
        biases,
        every_do,
        every_ld,
        gather_sends,
        gather_recvs,
        dmid_ref,
        do_ref,
        stores,
        *rest,
    ) = rest
    storing = [
        pltpu.make_async_copy(dmid_ref, dmid_far, stores.at[0]),
        pltpu.make_async_copy(do_ref, do_far, stores.at[1]),
    ]
    if planned:
        even, pieces_ref, *rest = rest
        outer = Reducer(rest[0].shape[-2], 48, rest[:7], order=chunk_of, parts=outer_ref)
        inner = Reducer(rest[7].shape[-2], 16, rest[7:], parts=inner_ref)
    step = pl.program_id(0)
    chunk = chunk_of(step)
    seq_index = lax.axis_index("seq")
    own_rows = pl.ds(pl.multiple_of(seq_index * quarter, quarter), quarter)
    width = mid.shape[1]
    piece = width // 32

    def rows_of(device):
        return pl.ds(pl.multiple_of(device[1] * quarter, quarter), quarter)

    def gather(owner, device, at):
        for kind, every in enumerate((every_do, every_ld)):
            yield pltpu.make_async_remote_copy(
                src_ref=every.at[rows_of(owner)],
                dst_ref=every.at[rows_of(owner)],
                send_sem=gather_sends.at[kind, at],
                recv_sem=gather_recvs.at[kind, at],
                device_id=device,
                device_id_type=pl.DeviceIdType.MESH,
            )

    me = seq_device(0, seq_count)
    if planned:
        sibling, across = outer.partners()[:2]
        first_gathers = [(me, across, 0), (me, sibling, 1)]
        second_gathers = [(across, sibling, 2)]
    else:
        first_gathers = [
            (me, seq_device(at + 1, seq_count), at) for at in range(seq_count - 1)
        ]
        second_gathers = []

    def store_pieces(half):
        rows = (slice(0, 2 * piece), slice(2 * piece, 3 * piece + 8))[half]
        return pltpu.make_async_copy(
            pieces_ref.at[:, :, :, :, rows], pieces_far.at[:, :, :, :, rows], stores.at[2 + half]
        )

    def act(now):
        if planned:
            for at, reducer, name, part in FFN_PLAN:
                if at == now:
                    getattr((outer, inner)[reducer], name)(part)

    def act_in_step(point):
        if planned:
            for now in range(4):
                if any(at == (now, point) for at, _, _, _ in FFN_PLAN):

                    @pl.when(step == now)
                    def _(now=now):
                        act((now, point))

    @pl.when(step == 0)
    def _():
        others = [seq_device(seq_step, seq_count) for seq_step in range(1, seq_count)]
        meet(others + (outer.partners()[2:] if planned else []))
        projected = dot_n(attn_ref[...], wo_ref[...]) + bo_ref[...]
        mid[:block] = long_ref[...].astype(F32) + projected[:block]
        mid[block:] = glob_ref[own_rows].astype(F32) + projected[block:]
        hat, _ = row_norm(mid[...])
        normed[...] = (hat * gain_ref[...] + shift_ref[...]).astype(BF16)
        normed_t[...] = normed[...].T
        position = seq_index * block + lax.broadcasted_iota(jnp.int32, (block, 1), 0)
        dy[:block] = jnp.where(
            position < len_ref[0], dlong_ref[...].astype(F32), 0.0
        ).astype(BF16)
        y_sum[:GP] = jnp.zeros((GP, width), F32)
        y_sum[:count] = dglob_ref[...].astype(F32)
        dy[block:] = y_sum[own_rows].astype(BF16)
        vectors[1:2] = column_sum(dy[...].astype(F32))
        y_sum[...] = mid[...] + br_ref[...]
        df_sum[...] = jnp.zeros_like(df_sum)
        for at in range(4):
            biases[at] = bi_ref[at * width : (at + 1) * width].reshape(1, width)

    act_in_step(0)
    active, slope = gate_both(dot_n(normed[...], wi_ref[...]) + biases[chunk])
    active = active.astype(BF16)
    g_outer = t_dot(active, dy[...])
    if planned:
        for at in range(8):
            outer.fill(chunk, at, g_outer[at * 4 * piece : (at + 1) * 4 * piece])
        outer.start(step)
    else:
        g_outer_ref[...] = g_outer.astype(BF16)
    y_sum[...] += dot_n(active, wr_ref[...])
    hidden = dot_t(dy[...], wr_ref[...]) * slope
    for at in range(4):

        @pl.when(chunk == at)
        def _(at=at):
            vectors[4 + at : 5 + at] = column_sum(hidden)

    hidden = hidden.astype(BF16)
    act_in_step(1)
    df_sum[...] += dot_t(hidden, wi_ref[...])
    g_inner = dot_n(normed_t[...], hidden)
    if planned:

        @pl.when(lax.rem(step, 2) == 0)
        def _():
            even[...] = g_inner

        def halves(at):
            part = slice(at * piece, (at + 1) * piece)
            return jnp.concatenate([even[part], g_inner[part]], 0)

        @pl.when(step == 1)
        def _():
            for at in range(32):
                inner.fill(at // 8, at % 8, halves(at))
            for part in range(4):
                inner.start(part)

        @pl.when(step == 3)
        def _():
            for at in range(32):
                pieces_ref[at % 2, at // 8, at // 4 % 2, at // 2 % 2, : 2 * piece] = halves(
                    at
                ).astype(BF16)
            store_pieces(0).start()

    else:
        g_inner_ref[...] = g_inner.astype(BF16)

    def norm_back(rows):
        hat, inverse = row_norm(mid[rows])
        df = df_sum[rows]
        scaled = df * gain_ref[...]
        dmid = dy[rows].astype(F32) + inverse * (
            scaled
            - jnp.mean(scaled, -1, keepdims=True)
            - hat * jnp.mean(scaled * hat, -1, keepdims=True)
        )
        dmid_ref[rows] = dmid
        low = dmid.astype(BF16)
        grad_o = dot_t(low, wo_ref[...]).astype(BF16)
        do_ref[rows] = grad_o
        return [column_sum(dmid), column_sum(df * hat), column_sum(df)], low, grad_o

    @pl.when(step == 3)
    def _():
        glob_sums, glob_low, grad_o = norm_back(slice(block, block + quarter))
        every_do[own_rows] = grad_o
        both = grad_o.astype(F32) * attn_ref[block:].astype(F32)
        stats = lq_ref[...]
        for head in range(2 * pairs):
            lanes = slice(head // 2 * PAIR, head // 2 * PAIR + PAIR)
            delta = jnp.sum(own_half(head % 2, both[:, lanes]), -1, keepdims=True)
            stats = jnp.where(lane_index() == HD + head, delta, stats)
        every_ld[own_rows] = stats
        for part in first_gathers:
            for copy in gather(*part):
                copy.start()
        glob_out[...] = y_sum[block:].astype(BF16)
        act((4, 0))
        position = seq_index * block + lax.broadcasted_iota(jnp.int32, (block, 1), 0)
        long_out[...] = jnp.where(position < len_ref[0], y_sum[:block], 0.0).astype(BF16)
        long_sums, long_low, _ = norm_back(slice(0, block))
        for at, one, two in zip((0, 2, 3), long_sums, glob_sums):
            vectors[at : at + 1] = one + two
        for copy in storing:
            copy.start()
        if planned:
            for copy in gather(*first_gathers[0]):
                copy.wait_recv()
            for copy in gather(*second_gathers[0]):
                copy.start()
        act((4, 1))
        g_out = t_dot(attn_ref[...], jnp.concatenate([long_low, glob_low], 0))
        if planned:
            for at in range(32):
                pieces_ref[at % 2, at // 8, at // 4 % 2, at // 2 % 2, 2 * piece :] = (
                    jnp.concatenate(
                        [g_out[at * piece : (at + 1) * piece], vectors[...]], 0
                    ).astype(BF16)
                )
            store_pieces(1).start()
            act((4, 2))
            outer.finish()
            inner.finish()
            for half in range(2):
                store_pieces(half).wait()
        else:
            g_out_ref[...] = g_out.astype(BF16)
            vec_ref[...] = vectors[...]
        for part in (first_gathers[1:] if planned else first_gathers) + second_gathers:
            for copy in gather(*part):
                copy.wait_recv()
        for copy in storing:
            copy.wait()
        dog_ref[...] = every_do[...]
        ldg_ref[...] = every_ld[...]
        for part in first_gathers + second_gathers:
            for copy in gather(*part):
                copy.wait_send()


OUTER, INNER = 0, 1
FFN_PLAN = (
    ((1, 0), OUTER, "add_core", 0),
    ((2, 0), OUTER, "add_core", 1),
    ((2, 0), OUTER, "add_first", 0),
    ((2, 1), INNER, "add_core", 0),
    ((2, 1), INNER, "add_core", 1),
    ((2, 1), INNER, "add_core", 2),
    ((2, 1), INNER, "add_core", 3),
    ((3, 0), OUTER, "add_first", 1),
    ((3, 0), OUTER, "add_second", 0),
    ((3, 0), OUTER, "add_core", 2),
    ((3, 1), OUTER, "add_core", 3),
    ((4, 0), INNER, "add_first", 0),
    ((4, 0), INNER, "add_first", 1),
    ((4, 0), OUTER, "add_first", 2),
    ((4, 0), OUTER, "add_second", 1),
    ((4, 1), INNER, "add_first", 2),
    ((4, 1), INNER, "add_first", 3),
    ((4, 1), INNER, "add_second", 0),
    ((4, 1), INNER, "add_second", 1),
    ((4, 2), OUTER, "add_first", 3),
    ((4, 2), OUTER, "add_second", 2),
    ((4, 2), INNER, "add_second", 2),
    ((4, 2), INNER, "add_second", 3),
    ((4, 2), OUTER, "add_second", 3),
)


def chunk_of(step):
    return jnp.where(step == 0, 0, jnp.where(step == 1, 3, step - 1))


def feed_forward(sizes, planned, doc_len, attn, long_x, glob_x, dlong, dglob, lq, *weights):
    block, count, quarter, seq_count, pairs = sizes
    wo, bo, gain, shift, wi, bi, wr, br = weights
    width, hidden = wi.shape
    chunk = hidden // 4
    rows = block + quarter
    whole = pl.BlockSpec(memory_space=pltpu.VMEM)
    shape = jax.ShapeDtypeStruct
    in_specs = [pl.BlockSpec(memory_space=pltpu.SMEM)] + [whole] * 10
    in_specs += [
        pl.BlockSpec((width, chunk), lambda c: (0, chunk_of(c))),
        whole,
        pl.BlockSpec((chunk, width), lambda c: (chunk_of(c), 0)),
        whole,
    ]
    outs = [
        shape((block, width), BF16),
        shape((quarter, width), BF16),
        shape((rows, width), F32),
        shape((rows, width), BF16),
        shape((GP, width), BF16),
        shape((GP, PAIR), F32),
    ]
    there = pl.BlockSpec(memory_space=pl.ANY)
    out_specs = [whole] * 2 + [there] * 2 + [whole] * 2
    others = seq_count - 1
    scratch = [
        pltpu.VMEM((rows, width), F32),
        pltpu.VMEM((rows, width), F32),
        pltpu.VMEM((rows, width), F32),
        pltpu.VMEM((rows, width), BF16),
        pltpu.VMEM((width, rows), BF16),
        pltpu.VMEM((rows, width), BF16),
        pltpu.VMEM((8, width), F32),
        pltpu.VMEM((4, 1, chunk), F32),
        pltpu.VMEM((GP, width), BF16),
        pltpu.VMEM((GP, PAIR), F32),
        pltpu.SemaphoreType.DMA((2, others)),
        pltpu.SemaphoreType.DMA((2, others)),
        pltpu.VMEM((rows, width), F32),
        pltpu.VMEM((rows, width), BF16),
        pltpu.SemaphoreType.DMA((4,)),
    ]
    if planned:
        part, piece = hidden // 32, width // 32
        outs += [
            shape((2, 4, 2, 2, 3 * piece + 8, width), BF16),
            shape((4, part, width), BF16),
            shape((4, 2 * piece, width), BF16),
        ]
        out_specs += [there] + [whole] * 2
        scratch += [
            pltpu.VMEM((width, chunk), F32),
            pltpu.VMEM(outs[-3].shape, BF16),
        ]
        scratch += Reducer.scratch(part, width, 2) + Reducer.scratch(2 * piece, width, 2)
    else:
        outs += [
            shape((hidden, width), BF16),
            shape((width, hidden), BF16),
            shape((width, width), BF16),
            shape((8, width), F32),
        ]
        out_specs += [
            pl.BlockSpec((chunk, width), lambda c: (chunk_of(c), 0)),
            pl.BlockSpec((width, chunk), lambda c: (0, chunk_of(c))),
            whole,
            whole,
        ]
    return pl.pallas_call(
        functools.partial(ffn_kernel, sizes, planned),
        grid=(4,),
        in_specs=in_specs,
        out_specs=out_specs,
        out_shape=outs,
        scratch_shapes=scratch,
        compiler_params=pltpu.CompilerParams(
            collective_id=4, has_side_effects=True, vmem_limit_bytes=62 * 2**20
        ),
        name="feed_forward",
    )(doc_len, attn, long_x, glob_x, dlong, dglob, lq, wo, bo, gain, shift, wi, bi, wr, br)


def back_kernel(
    sizes,
    early_rows,
    len_ref,
    tab_ref,
    q_ref,
    kx_ref,
    vx_ref,
    kg_ref,
    vg_ref,
    o_ref,
    do_ref,
    l_ref,
    dog_ref,
    ldg_ref,
    yq_ref,
    *rest,
):
    block, count, quarter, seq_count, pairs = sizes
    reduces = early_rows > 0
    if reduces:
        pieces_ref, outer_parts, inner_parts, *rest = rest
    dq_ref, dk_ref, dv_ref, dtab_ref, glob_out, *rest = rest
    if reduces:
        early_parts, outer_ref, inner_ref, *rest = rest
    (
        dkx,
        dvx,
        dkg,
        dvg,
        q_send,
        q_recv,
        kv_send,
        kv_recv,
        halo_send,
        halo_recv,
        glob_sends,
        glob_recvs,
        halo_sends,
        halo_recvs,
        every,
        gather_sends,
        gather_recvs,
        *rest,
    ) = rest
    number = pl.program_id(0)
    steps = pairs // 2
    first_pair = 2 * lax.rem(number, steps)
    seq_index = lax.axis_index("seq")
    if reduces:
        reducer = Reducer(early_rows, 16, rest[:7], pieces=pieces_ref, parts=early_parts)
        z_sums = (
            (ZSum(outer_parts, rest[7:12]), outer_ref),
            (ZSum(inner_parts, rest[12:]), inner_ref),
        )
    scale = HD ** (-0.5)
    low_lanes = lane_index() < HD
    own_keys = slice(HALO, HALO + block)
    own_rows = pl.ds(pl.multiple_of(seq_index * quarter, quarter), quarter)

    def glob_copies(kind, at):
        source, dest = ((q_send, q_recv), (kv_send, kv_recv))[kind]
        for step in range(1, seq_count):
            device = seq_device(step, seq_count)
            yield pltpu.make_async_remote_copy(
                src_ref=source.at[device[1], at],
                dst_ref=dest.at[step - 1, at],
                send_sem=glob_sends.at[kind, step - 1, at],
                recv_sem=glob_recvs.at[kind, step - 1, at],
                device_id=device,
                device_id_type=pl.DeviceIdType.MESH,
            )

    def gathers():
        for step in range(1, seq_count):
            yield pltpu.make_async_remote_copy(
                src_ref=every.at[own_rows],
                dst_ref=every.at[own_rows],
                send_sem=gather_sends.at[step - 1],
                recv_sem=gather_recvs.at[step - 1],
                device_id=seq_device(step, seq_count),
                device_id_type=pl.DeviceIdType.MESH,
            )

    def halo_copy(direction, at):
        return pltpu.make_async_remote_copy(
            src_ref=halo_send.at[direction, at],
            dst_ref=halo_recv.at[direction, at],
            send_sem=halo_sends.at[direction, at],
            recv_sem=halo_recvs.at[direction, at],
            device_id=seq_device(2 * direction - 1, seq_count),
            device_id_type=pl.DeviceIdType.MESH,
        )

    has_low, has_high = seq_index > 0, seq_index < seq_count - 1
    sends_to = (has_low, has_high)
    gets_from = (has_high, has_low)

    def close_pair(at):
        lanes = lanes_of(at)
        for direction in range(2):

            @pl.when(gets_from[direction])
            def _(direction=direction):
                halo_copy(direction, at).wait_recv()

        for kind, (total, out) in enumerate(((dkx, dk_ref), (dvx, dv_ref))):
            first, last = HALO + REACH, HALO + block - REACH
            out[:REACH, lanes] = (
                total[at, HALO:first] + halo_recv[1, at, kind].astype(F32)
            ).astype(BF16)
            out[REACH : block - REACH, lanes] = total[at, first:last].astype(BF16)
            out[block - REACH : block, lanes] = (
                total[at, last : HALO + block] + halo_recv[0, at, kind].astype(F32)
            ).astype(BF16)
        sums = []
        for kind, (source, dest) in enumerate(((q_send, q_recv), (kv_send, kv_recv))):
            total = source[seq_index, at].astype(F32)
            for step, copy in enumerate(glob_copies(kind, at)):
                copy.wait_recv()
                total += dest[step, at].astype(F32)
            sums.append(total.astype(BF16))
        dq_ref[block:, lanes] = sums[0]
        dk_ref[block:, lanes] = sums[1][:, :PAIR]
        dv_ref[block:, lanes] = sums[1][:, PAIR:]

    def run_plan(now):
        for at, act, chunk in EARLY_PLAN:
            if now == at:
                getattr(reducer, act)(chunk)

    @pl.when(number == 0)
    def _():
        others = [seq_device(step, seq_count) for step in range(1, seq_count)]
        meet(others + (reducer.partners()[2:] if reduces else []))
        if reduces:
            for chunk in range(4):
                reducer.start(chunk)
            for z_sum, _ in z_sums:
                z_sum.start()
        every[own_rows] = yq_ref[...]
        for copy in gathers():
            copy.start()
        for direction in range(2):

            @pl.when(jnp.logical_not(gets_from[direction]))
            def _(direction=direction):
                halo_recv[direction] = jnp.zeros_like(halo_recv[direction])

    if reduces:
        for now in range(1, 2 * steps):
            if any(at == now for at, _, _ in EARLY_PLAN):

                @pl.when(number == now)
                def _(now=now):
                    run_plan(now)

    def glob_pair(pair, q_ref, kx_ref, vx_ref, kg_ref, vg_ref, dog_ref):
        long_bias = key_bias(seq_index * block, block, len_ref[0])
        near_bias = key_bias(seq_index * quarter, quarter, count)
        query = q_ref[block:] * jnp.asarray(scale, BF16)
        grad_o = dog_ref[...]
        far_k, far_v = kx_ref[own_keys], vx_ref[own_keys]
        near_k, near_v = kg_ref[own_rows], vg_ref[own_rows]
        outs, kept = [], []
        for head in range(2):
            norm = in_three(-pick_column(ldg_ref[...], 2 * pair + head))
            delta = in_three(-pick_column(ldg_ref[...], HD + 2 * pair + head))
            qa = with_lanes(head, query, (1.0,) + norm)
            doa = with_lanes(head, grad_o, delta)
            far = jnp.exp(dot_t(qa, key_side(head, far_k, long_bias)))
            near = jnp.exp(dot_t(qa, key_side(head, near_k, near_bias)))
            far_ds = (far * dot_t(doa, value_side(head, far_v))).astype(BF16)
            near_ds = (near * dot_t(doa, value_side(head, near_v))).astype(BF16)
            outs.append(dot_n(far_ds, far_k) + dot_n(near_ds, near_k))
            kept.append(
                (
                    own_half(head, query),
                    own_half(head, grad_o),
                    far.astype(BF16),
                    near.astype(BF16),
                    far_ds,
                    near_ds,
                )
            )
        own_q, own_do, far, near, far_ds, near_ds = (
            jnp.concatenate(part, 0) for part in zip(*kept)
        )
        for total, edge in ((dkx, own_keys), (dvx, own_keys)):
            total[pair, :HALO] = jnp.zeros((HALO, PAIR), F32)
            total[pair, HALO + block :] = jnp.zeros((HALO, PAIR), F32)
        dkx[pair, own_keys] = t_dot(far_ds, own_q)
        dvx[pair, own_keys] = t_dot(far, own_do)
        dkg[pair] = jnp.zeros((GP, PAIR), F32)
        dvg[pair] = jnp.zeros((GP, PAIR), F32)
        dkg[pair, own_rows] = t_dot(near_ds, own_q)
        dvg[pair, own_rows] = t_dot(near, own_do)
        glob_dq = (jnp.where(low_lanes, outs[0], outs[1]) * scale).astype(BF16)
        q_send[:, pair] = glob_dq.reshape(seq_count, quarter, PAIR)
        for copy in glob_copies(0, pair):
            copy.start()

    def long_pair(pair, q_ref, kx_ref, vx_ref, kg_ref, vg_ref, o_ref, do_ref, tab_ref):
        long_bias = key_bias(seq_index * block - HALO, block + 2 * HALO, len_ref[0])
        glob_bias = key_bias(0, GP, count)
        query = q_ref[:block] * jnp.asarray(scale, BF16)
        grad_o = do_ref[...]
        both = grad_o.astype(F32) * o_ref[...].astype(F32)
        heads = []
        for head in range(2):
            norm = in_three(-pick_column(l_ref[...], 2 * pair + head))
            delta = in_three(-jnp.sum(own_half(head, both), -1, keepdims=True))
            heads.append(
                dict(
                    q=own_half(head, query),
                    do=own_half(head, grad_o),
                    qa=with_lanes(head, query, (1.0,) + norm),
                    doa=with_lanes(head, grad_o, delta),
                    kxa=key_side(head, kx_ref[...], long_bias),
                    vxa=value_side(head, vx_ref[...]),
                    kga=key_side(head, kg_ref[...], glob_bias),
                    vga=value_side(head, vg_ref[...]),
                    bias=band_bias(tab_ref[0, head : head + 1]),
                )
            )
        table_sums = [0.0, 0.0]
        grads_q = []
        for start in range(0, block, SUB):
            rows, keys = slice(start, start + SUB), slice(start, start + WINDOW)
            outs, probs, grads = [], [], []
            for head, own in enumerate(heads):
                band = jnp.exp(dot_t(own["qa"][rows], own["kxa"][keys]) + own["bias"])
                band_ds = band * dot_t(own["doa"][rows], own["vxa"][keys])
                table_sums[head] += band_ds
                glob = jnp.exp(dot_t(own["qa"][rows], own["kga"]))
                glob_ds = (glob * dot_t(own["doa"][rows], own["vga"])).astype(BF16)
                band_ds = band_ds.astype(BF16)
                outs.append(dot_n(band_ds, kx_ref[keys]) + dot_n(glob_ds, kg_ref[...]))
                probs.append((band.astype(BF16), glob.astype(BF16)))
                grads.append((band_ds, glob_ds))
            grads_q.append(jnp.where(low_lanes, outs[0], outs[1]))
            own_q = jnp.concatenate([own["q"][rows] for own in heads], 0)
            own_do = jnp.concatenate([own["do"][rows] for own in heads], 0)
            band, glob = (jnp.concatenate(part, 0) for part in zip(*probs))
            band_ds, glob_ds = (jnp.concatenate(part, 0) for part in zip(*grads))
            dkx[pair, keys] += t_dot(band_ds, own_q)
            dvx[pair, keys] += t_dot(band, own_do)
            dkg[pair] += t_dot(glob_ds, own_q)
            dvg[pair] += t_dot(glob, own_do)
        for kind, total in enumerate((dkg, dvg)):
            kv_send[:, pair, :, kind * PAIR : (kind + 1) * PAIR] = (
                total[pair].astype(BF16).reshape(seq_count, quarter, PAIR)
            )
        for copy in glob_copies(1, pair):
            copy.start()
        for kind, total in enumerate((dkx, dvx)):
            for direction, first in enumerate((HALO - REACH, HALO + block)):
                halo_send[direction, pair, kind] = total[pair, first : first + REACH].astype(BF16)
        for direction in range(2):

            @pl.when(sends_to[direction])
            def _(direction=direction):
                halo_copy(direction, pair).start()

        dq_ref[:block, lanes_of(pair)] = (jnp.concatenate(grads_q, 0) * scale).astype(BF16)
        for head in range(2):
            dtab_ref[pair, head : head + 1] = diagonal_sums(table_sums[head])

    def part(at, *refs):
        return [ref.at[:, at * PAIR : (at + 1) * PAIR] for ref in refs]

    @pl.when(number < steps)
    def _():
        for at in range(2):
            glob_pair(
                first_pair + at, *part(at, q_ref, kx_ref, vx_ref, kg_ref, vg_ref, dog_ref)
            )

    @pl.when(number >= steps)
    def _():
        for at in range(2):
            long_pair(
                first_pair + at,
                *part(at, q_ref, kx_ref, vx_ref, kg_ref, vg_ref, o_ref, do_ref),
                tab_ref.at[at : at + 1],
            )

    @pl.when(number > steps)
    def _():
        close_pair(first_pair - 2)
        close_pair(first_pair - 1)

    @pl.when(number == 2 * steps - 1)
    def _():
        if reduces:
            run_plan(2 * steps)
        close_pair(pairs - 2)
        close_pair(pairs - 1)
        for at in range(pairs):
            for kind in range(2):
                for copy in glob_copies(kind, at):
                    copy.wait_send()
            for direction in range(2):

                @pl.when(sends_to[direction])
                def _(direction=direction, at=at):
                    halo_copy(direction, at).wait_send()

        for copy in gathers():
            copy.wait_recv()
        glob_out[...] = every[:count]
        for copy in gathers():
            copy.wait_send()
        if reduces:
            reducer.finish()
            for z_sum, out in z_sums:
                z_sum.finish(out)


def attend_back(sizes, doc_len, table, q, kx, vx, kg, vg, o, do, l, dog, ldg, yq, *sums):
    block, count, quarter, seq_count, pairs = sizes
    width = q.shape[1]
    early_rows = sums[0].shape[-2] if sums else 0
    ext = block + 2 * HALO
    steps = pairs // 2
    cols = lambda rows: pl.BlockSpec((rows, 2 * PAIR), lambda i: (0, lax.rem(i, steps)))
    whole = pl.BlockSpec(memory_space=pltpu.VMEM)
    shape = jax.ShapeDtypeStruct
    in_specs = [
        pl.BlockSpec(memory_space=pltpu.SMEM),
        pl.BlockSpec((2, 2, WINDOW), lambda i: (lax.rem(i, steps), 0, 0)),
        cols(block + GP),
        cols(ext),
        cols(ext),
        cols(GP),
        cols(GP),
        cols(block),
        cols(block),
        whole,
        cols(GP),
        whole,
        whole,
    ]
    rows = block + quarter
    outs = [shape((rows, width), BF16)] * 3 + [shape((pairs, 2, WINDOW), F32)]
    outs.append(shape((count, width), BF16))
    others = seq_count - 1
    scratch = [
        pltpu.VMEM((pairs, ext, PAIR), F32),
        pltpu.VMEM((pairs, ext, PAIR), F32),
        pltpu.VMEM((pairs, GP, PAIR), F32),
        pltpu.VMEM((pairs, GP, PAIR), F32),
        pltpu.VMEM((seq_count, pairs, quarter, PAIR), BF16),
        pltpu.VMEM((others, pairs, quarter, PAIR), BF16),
        pltpu.VMEM((seq_count, pairs, quarter, 2 * PAIR), BF16),
        pltpu.VMEM((others, pairs, quarter, 2 * PAIR), BF16),
        pltpu.VMEM((2, pairs, 2, REACH, PAIR), BF16),
        pltpu.VMEM((2, pairs, 2, REACH, PAIR), BF16),
        pltpu.SemaphoreType.DMA((2, others, pairs)),
        pltpu.SemaphoreType.DMA((2, others, pairs)),
        pltpu.SemaphoreType.DMA((2, pairs)),
        pltpu.SemaphoreType.DMA((2, pairs)),
        pltpu.VMEM((GP, width), BF16),
        pltpu.SemaphoreType.DMA((others,)),
        pltpu.SemaphoreType.DMA((others,)),
    ]
    args = [doc_len, table, q, kx, vx, kg, vg, o, do, l, dog, ldg, yq, *sums]
    if early_rows:
        in_specs += [pl.BlockSpec(memory_space=pl.ANY)] * 3
        outs.append(shape((4, early_rows, width), BF16))
        scratch += Reducer.scratch(early_rows, width, 1)
        for parts in sums[1:]:
            outs.append(shape(parts.shape[1:], F32))
            scratch += ZSum.scratch(*parts.shape[1:])
    return pl.pallas_call(
        functools.partial(back_kernel, sizes, early_rows),
        grid=(2 * steps,),
        in_specs=in_specs,
        out_specs=[whole] * len(outs),
        out_shape=outs,
        scratch_shapes=scratch,
        compiler_params=pltpu.CompilerParams(
            collective_id=1, has_side_effects=True, vmem_limit_bytes=60 * 2**20
        ),
        name="attend_back",
    )(*args)


def on_device(
    long_input,
    global_input,
    lengths,
    w_query,
    b_query,
    w_key,
    w_value,
    b_value,
    w_out,
    b_out,
    w_inner,
    b_inner,
    w_outer,
    b_outer,
    norm1_gain,
    norm1_shift,
    norm2_gain,
    norm2_shift,
    rel_table,
    long_cotangent,
    global_cotangent,
):
    seq_count = lax.axis_size("seq")
    data_count = lax.axis_size("dp")
    seq_index = lax.axis_index("seq")
    block = long_input.shape[1]
    count = global_input.shape[1]
    width = long_input.shape[2]
    heads = rel_table.shape[1]
    pairs = heads // 2
    labels = 2 * R + 1
    quarter = GP // seq_count
    sizes = Sizes(block, count, quarter, seq_count, pairs)
    queries, kx, vx, kg, vg, attn_low, long_l, glob_l, glob_x, table = attend(
        sizes,
        lengths,
        rel_table.T,
        long_input[0],
        global_input[0],
        w_query,
        w_key,
        w_value,
        b_query,
        b_value,
        norm1_gain,
        norm1_shift,
    )
    planned = has_plan()
    long_result, own_out, grad_mid, grad_attn, every_do, every_ld, *gradients = feed_forward(
        sizes,
        planned,
        lengths,
        attn_low,
        long_input[0],
        glob_x,
        long_cotangent[0],
        global_cotangent[0],
        glob_l,
        w_out,
        b_out,
        norm2_gain,
        norm2_shift,
        w_inner,
        b_inner,
        w_outer,
        b_outer,
    )
    query_low, key_low, value_low, dtab, glob_out, *early = attend_back(
        sizes,
        lengths,
        table,
        queries,
        kx,
        vx,
        kg,
        vg,
        attn_low,
        grad_attn,
        long_l,
        every_do,
        every_ld,
        own_out,
        *(gradients if planned else []),
    )
    long_grad, glob_grad, *late = last_part(
        sizes,
        planned,
        long_input[0],
        glob_x,
        query_low,
        key_low,
        value_low,
        grad_mid,
        w_query,
        w_key,
        w_value,
        norm1_gain,
        norm1_shift,
        dtab,
        *early[:1],
    )
    if planned:
        (
            g_query,
            g_key,
            g_value,
            g_out,
            g_inner,
            g_outer,
            g_b_query,
            g_b_value,
            g_b_out,
            g_b_outer,
            g_g1,
            g_s1,
            g_g2,
            g_s2,
            g_b_inner,
            table_total,
            long_grad,
            long_result,
            glob_grad,
        ) = small_results(
            heads,
            late[3],
            late[0],
            early[1],
            early[2],
            late[1],
            late[2],
            long_grad,
            long_result,
            glob_grad,
        )
        table_total = table_total.T
        glob_grad = glob_grad.reshape(count, width)
    else:
        devices = data_count * seq_count
        own_part = lambda vector: lax.dynamic_slice_in_dim(
            vector,
            (lax.axis_index("dp") * seq_count + seq_index) * (vector.shape[0] // devices),
            vector.shape[0] // devices,
        )
        g_outer, g_inner, g_out, vectors = gradients
        g_outer, g_inner, g_out, g_query, g_key, g_value = (
            lax.psum_scatter(g.astype(BF16), ("dp", "seq"), scatter_dimension=0, tiled=True).astype(
                F32
            )
            for g in (g_outer, g_inner, g_out, *late[:3])
        )
        vectors, sums, scales = lax.psum((vectors, *late[3:]), ("dp", "seq"))
        g_b_query, g_b_value = (own_part(sums[heads + i]) for i in range(2))
        g_g1, g_s1 = (own_part(scales[i]) for i in range(2))
        g_b_out, g_b_outer, g_g2, g_s2 = (own_part(vectors[i]) for i in range(4))
        g_b_inner = own_part(vectors[4:].reshape(-1))
        table_total = sums[:heads, HALO - R : HALO - R + labels].T
    return (
        long_result[None],
        glob_out[None],
        long_grad[None],
        glob_grad[None],
        g_query,
        g_b_query,
        g_key,
        g_value,
        g_b_value,
        g_out,
        g_b_out,
        g_inner,
        g_b_inner,
        g_outer,
        g_b_outer,
        g_g1,
        g_s1,
        g_g2,
        g_s2,
        table_total,
    )


def solution(mesh):
    rows, whole = P("dp", "seq", None), P("dp", None, None)
    matrix, vector = P(("dp", "seq"), None), P(("dp", "seq"))
    return jax.shard_map(
        on_device,
        mesh=mesh,
        in_specs=(rows, whole, P("dp")) + (P(),) * 16 + (rows, whole),
        out_specs=(
            rows,
            whole,
            rows,
            whole,
            matrix,
            vector,
            matrix,
            matrix,
            vector,
            matrix,
            vector,
            matrix,
            vector,
            matrix,
            vector,
            vector,
            vector,
            vector,
            vector,
            P(),
        ),
        check_vma=False,
    )
```

```python
import functools
from typing import NamedTuple

import jax
import jax.numpy as jnp
from jax import lax
from jax.experimental import pallas as pl
from jax.experimental.pallas import tpu as pltpu
from jax.sharding import PartitionSpec as P

HD = 64
R = 84
PAIR = 2 * HD
HALO = 128
REACH = 96
GP = 256
SUB = 256
WINDOW = SUB + 2 * HALO
EPSILON = 1e-05
MASKED = -1e30
F32 = jnp.float32
BF16 = jnp.bfloat16


def dot_t(left, right):
    return lax.dot_general(left, right, (((1,), (1,)), ((), ())), preferred_element_type=F32)


def dot_n(left, right):
    return lax.dot_general(left, right, (((1,), (0,)), ((), ())), preferred_element_type=F32)


def t_dot(left, right):
    return lax.dot_general(left, right, (((0,), (0,)), ((), ())), preferred_element_type=F32)


def band_bias(table_row):
    spread = jnp.broadcast_to(table_row, (SUB, WINDOW))
    return pltpu.roll(spread, 0, 1, stride=1, stride_axis=0)


def diagonal_sums(rows):
    height, width = rows.shape
    while height > 8:
        height //= 2
        rows = rows[:height] + pltpu.roll(rows[height:], width - height, 1)
    row = lax.broadcasted_iota(jnp.int32, rows.shape, 0)
    for bit in (1, 2, 4):
        rows = jnp.where((row & bit) != 0, pltpu.roll(rows, width - bit, 1), rows)
    return jnp.sum(rows, 0, keepdims=True)


def lane_index():
    return lax.broadcasted_iota(jnp.int32, (1, PAIR), 1)


def own_half(head, value):
    low_lanes = lane_index() < HD
    return jnp.where(low_lanes if head == 0 else ~low_lanes, value, jnp.zeros_like(value))


def other_lane(head):
    return HD * (1 - head)


def with_lanes(head, value, columns):
    wide = own_half(head, value.astype(F32))
    lane = lane_index()
    for offset, column in enumerate(columns):
        wide = jnp.where(lane == other_lane(head) + offset, column, wide)
    return wide.astype(BF16)


def in_three(column):
    high = column.astype(BF16).astype(F32)
    middle = (column - high).astype(BF16).astype(F32)
    return (high, middle, column - high - middle)


def key_bias(first, rows, end):
    position = first + lax.broadcasted_iota(jnp.int32, (rows, 1), 0)
    return jnp.where((position >= 0) & (position < end), 0.0, MASKED)


def pick_column(rows, index):
    return jnp.sum(jnp.where(lane_index() == index, rows, 0.0), -1, keepdims=True)


def key_side(head, keys, bias):
    return with_lanes(head, keys, (bias, 1.0, 1.0, 1.0))


def value_side(head, values):
    return with_lanes(head, values, (1.0, 1.0, 1.0))


def softmax_rows(parts, value_parts, head):
    top = functools.reduce(
        jnp.maximum, [jnp.max(part, -1, keepdims=True) for part in parts]
    )
    mixed = sum(
        dot_n(jnp.exp(part - top).astype(BF16), values)
        for part, values in zip(parts, value_parts)
    )
    at = other_lane(head)
    total = mixed[:, at : at + 1]
    return mixed / total, top + jnp.log(total)


def seq_device(steps, seq_count):
    return (lax.axis_index("dp"), lax.rem(lax.axis_index("seq") + steps + seq_count, seq_count))


def row_norm(rows):
    centred = rows - jnp.mean(rows, -1, keepdims=True)
    inverse = lax.rsqrt(jnp.mean(centred * centred, -1, keepdims=True) + EPSILON)
    return centred * inverse, inverse


def put_column(ref, rows, index, column):
    ref[rows] = jnp.where(lane_index() == index, column, ref[rows])


def lanes_of(at):
    return pl.ds(pl.multiple_of(at * PAIR, PAIR), PAIR)


class Sizes(NamedTuple):
    block: int
    count: int
    quarter: int
    seq_count: int
    pairs: int


def attend_kernel(
    sizes,
    len_ref,
    rel_ref,
    long_ref,
    raw_ref,
    wq_far,
    wk_far,
    wv_far,
    bq_ref,
    bv_ref,
    gain_ref,
    shift_ref,
    q_far,
    kx_far,
    vx_far,
    kg_far,
    vg_far,
    o_ref,
    l_ref,
    lq_ref,
    glob_ref,
    tab_ref,
    spread,
    wide,
    part_o,
    part_l,
    from_o,
    from_l,
    halo_sends,
    halo_recvs,
    part_sends,
    part_recvs,
    wq_ref,
    wk_ref,
    wv_ref,
    loads,
    q_ref,
    kx_ref,
    vx_ref,
    kg_ref,
    vg_ref,
    stores,
):
    block, count, quarter, seq_count, pairs = sizes
    ext = block + 2 * HALO
    seq_index = lax.axis_index("seq")
    scale = jnp.asarray(HD ** (-0.5), BF16)
    low_lanes = lane_index() < HD
    own_keys = slice(HALO, HALO + block)
    own_rows = pl.ds(pl.multiple_of(seq_index * quarter, quarter), quarter)
    neighbours = (seq_index > 0, seq_index < seq_count - 1)
    barrier = pltpu.get_barrier_semaphore()
    for step in range(1, seq_count):
        pl.semaphore_signal(
            barrier,
            inc=1,
            device_id=seq_device(step, seq_count),
            device_id_type=pl.DeviceIdType.MESH,
        )

    def halo_copies(direction):
        source = HALO if direction == 0 else HALO + block - REACH
        dest = HALO + block if direction == 0 else HALO - REACH
        for kind, ref in enumerate((kx_ref, vx_ref)):
            yield pltpu.make_async_remote_copy(
                src_ref=ref.at[source : source + REACH],
                dst_ref=ref.at[dest : dest + REACH],
                send_sem=halo_sends.at[direction, kind],
                recv_sem=halo_recvs.at[direction, kind],
                device_id=seq_device(2 * direction - 1, seq_count),
                device_id_type=pl.DeviceIdType.MESH,
            )

    def part_copies():
        for step in range(1, seq_count):
            device = seq_device(step, seq_count)
            rows = pl.ds(pl.multiple_of(device[1] * quarter, quarter), quarter)
            for kind, (source, dest) in enumerate(((part_o, from_o), (part_l, from_l))):
                yield step, kind, pltpu.make_async_remote_copy(
                    src_ref=source.at[rows],
                    dst_ref=dest.at[step - 1],
                    send_sem=part_sends.at[kind, step - 1],
                    recv_sem=part_recvs.at[kind, step - 1],
                    device_id=device,
                    device_id_type=pl.DeviceIdType.MESH,
                )

    loading = [
        pltpu.make_async_copy(source, dest, loads.at[at])
        for at, (source, dest) in enumerate(
            ((wk_far, wk_ref), (wv_far, wv_ref), (wq_far, wq_ref))
        )
    ]
    for copy in loading:
        copy.start()
    gain, shift = gain_ref[...], shift_ref[...]
    heads, labels = rel_ref.shape
    spread[...] = jnp.full(spread.shape, MASKED, F32)
    spread[:heads, :labels] = rel_ref[...]
    turned = pltpu.roll(spread[...], HALO - R, 1)
    for pair in range(pairs):
        tab_ref[pair] = turned[2 * pair : 2 * pair + 2]
    normed_long = (row_norm(long_ref[...].astype(F32))[0] * gain + shift).astype(BF16)
    loading[0].wait()
    kx_ref[own_keys] = dot_n(normed_long, wk_ref[...]).astype(BF16)
    loading[1].wait()
    vx_ref[own_keys] = (dot_n(normed_long, wv_ref[...]) + bv_ref[...]).astype(BF16)
    pl.semaphore_wait(barrier, seq_count - 1)
    for direction, first in enumerate((HALO - REACH, HALO + block)):

        @pl.when(neighbours[direction])
        def _(direction=direction):
            for copy in halo_copies(direction):
                copy.start()

        outer = slice(0, first) if direction == 0 else slice(first + REACH, ext)
        for ref in (kx_ref, vx_ref):
            ref[outer] = jnp.zeros((HALO - REACH, ref.shape[1]), BF16)

        @pl.when(jnp.logical_not(neighbours[direction]))
        def _(first=first):
            for ref in (kx_ref, vx_ref):
                ref[first : first + REACH] = jnp.zeros((REACH, ref.shape[1]), BF16)

    wide[...] = jnp.zeros_like(wide)
    wide[:count] = raw_ref[...].astype(F32)
    glob_ref[...] = wide[...].astype(BF16)
    normed_glob = (row_norm(wide[...])[0] * gain + shift).astype(BF16)
    kg_ref[...] = dot_n(normed_glob, wk_ref[...]).astype(BF16)
    vg_ref[...] = (dot_n(normed_glob, wv_ref[...]) + bv_ref[...]).astype(BF16)
    loading[2].wait()
    q_ref[block:] = (dot_n(normed_glob, wq_ref[...]) + bq_ref[...]).astype(BF16)
    q_ref[:block] = (dot_n(normed_long, wq_ref[...]) + bq_ref[...]).astype(BF16)
    part_l[...] = jnp.zeros_like(part_l)
    l_ref[...] = jnp.zeros_like(l_ref)

    def glob_pair(pair, carry):
        lanes = lanes_of(pair)
        far_bias = key_bias(seq_index * block, block, len_ref[0])
        near_bias = key_bias(seq_index * quarter, quarter, count)
        query = q_ref[block:, lanes] * scale
        outs = []
        for head in range(2):
            q = with_lanes(head, query, (1.0,))
            far = dot_t(q, with_lanes(head, kx_ref[own_keys, lanes], (far_bias,)))
            near = dot_t(q, with_lanes(head, kg_ref[own_rows, lanes], (near_bias,)))
            out, norm = softmax_rows(
                [far, near],
                [
                    with_lanes(head, vx_ref[own_keys, lanes], (1.0,)),
                    with_lanes(head, vg_ref[own_rows, lanes], (1.0,)),
                ],
                head,
            )
            outs.append(out)
            put_column(part_l, slice(None), 2 * pair + head, norm)
        part_o[:, lanes] = jnp.where(low_lanes, outs[0], outs[1]).astype(BF16)
        return carry

    lax.fori_loop(0, pairs, glob_pair, 0, unroll=2)
    for _, _, copy in part_copies():
        copy.start()
    for direction in range(2):

        @pl.when(neighbours[1 - direction])
        def _(direction=direction):
            for copy in halo_copies(direction):
                copy.wait_recv()

    storing = [
        pltpu.make_async_copy(source, dest, stores.at[at])
        for at, (source, dest) in enumerate(
            (
                (q_ref, q_far),
                (kx_ref, kx_far),
                (vx_ref, vx_far),
                (kg_ref, kg_far),
                (vg_ref, vg_far),
            )
        )
    ]
    for copy in storing:
        copy.start()

    def long_pair(pair, carry):
        lanes = lanes_of(pair)
        long_bias = key_bias(seq_index * block - HALO, ext, len_ref[0])
        glob_bias = key_bias(0, GP, count)
        query = q_ref[:block, lanes] * scale
        outs = []
        for head in range(2):
            q = with_lanes(head, query, (1.0,))
            kx = with_lanes(head, kx_ref[:, lanes], (long_bias,))
            kg = with_lanes(head, kg_ref[:, lanes], (glob_bias,))
            vx, vg = (with_lanes(head, ref[:, lanes], (1.0,)) for ref in (vx_ref, vg_ref))
            bias = band_bias(tab_ref[pair, head : head + 1])
            mixed = []
            for start in range(0, block, SUB):
                rows, keys = slice(start, start + SUB), slice(start, start + WINDOW)
                out, norm = softmax_rows(
                    [dot_t(q[rows], kx[keys]) + bias, dot_t(q[rows], kg)], [vx[keys], vg], head
                )
                mixed.append(out)
                put_column(l_ref, rows, 2 * pair + head, norm)
            outs.append(jnp.concatenate(mixed, 0))
        o_ref[:block, lanes] = jnp.where(low_lanes, outs[0], outs[1]).astype(BF16)
        return carry

    lax.fori_loop(0, pairs, long_pair, 0, unroll=2)
    for _, _, copy in part_copies():
        copy.wait_recv()
    norms = [part_l[own_rows]] + [from_l[step] for step in range(seq_count - 1)]
    outs = [part_o[own_rows]] + [from_o[step] for step in range(seq_count - 1)]
    top = functools.reduce(jnp.maximum, norms)
    shares = [jnp.exp(norm - top) for norm in norms]
    total = sum(shares)
    lq_ref[...] = top + jnp.log(total)
    shares = [share / total for share in shares]
    for at in range(pairs):
        lanes = slice(at * PAIR, (at + 1) * PAIR)
        mixed = 0.0
        for share, out in zip(shares, outs):
            spread = jnp.where(
                low_lanes, share[:, 2 * at : 2 * at + 1], share[:, 2 * at + 1 : 2 * at + 2]
            )
            mixed += spread * out[:, lanes].astype(F32)
        o_ref[block:, lanes] = mixed.astype(BF16)
    for copy in storing:
        copy.wait()
    for _, _, copy in part_copies():
        copy.wait_send()
    for direction in range(2):

        @pl.when(neighbours[direction])
        def _(direction=direction):
            for copy in halo_copies(direction):
                copy.wait_send()


def attend(sizes, doc_len, rel_table, long_x, glob_x, *weights):
    block, count, quarter, seq_count, pairs = sizes
    width = long_x.shape[1]
    ext = block + 2 * HALO
    whole = pl.BlockSpec(memory_space=pltpu.VMEM)
    shape = jax.ShapeDtypeStruct
    others = seq_count - 1
    return pl.pallas_call(
        functools.partial(attend_kernel, sizes),
        in_specs=[pl.BlockSpec(memory_space=pltpu.SMEM)]
        + [whole] * 3
        + [pl.BlockSpec(memory_space=pl.ANY)] * 3
        + [whole] * 4,
        out_specs=[pl.BlockSpec(memory_space=pl.ANY)] * 5 + [whole] * 5,
        out_shape=[
            shape((block + GP, width), BF16),
            shape((ext, width), BF16),
            shape((ext, width), BF16),
            shape((GP, width), BF16),
            shape((GP, width), BF16),
            shape((block + quarter, width), BF16),
            shape((block, PAIR), F32),
            shape((quarter, PAIR), F32),
            shape((GP, width), BF16),
            shape((pairs, 2, WINDOW), F32),
        ],
        scratch_shapes=[
            pltpu.VMEM(((2 * pairs + 7) // 8 * 8, WINDOW), F32),
            pltpu.VMEM((GP, width), F32),
            pltpu.VMEM((GP, width), BF16),
            pltpu.VMEM((GP, PAIR), F32),
            pltpu.VMEM((others, quarter, width), BF16),
            pltpu.VMEM((others, quarter, PAIR), F32),
            pltpu.SemaphoreType.DMA((2, 2)),
            pltpu.SemaphoreType.DMA((2, 2)),
            pltpu.SemaphoreType.DMA((2, others)),
            pltpu.SemaphoreType.DMA((2, others)),
            pltpu.VMEM((width, width), BF16),
            pltpu.VMEM((width, width), BF16),
            pltpu.VMEM((width, width), BF16),
            pltpu.SemaphoreType.DMA((3,)),
            pltpu.VMEM((block + GP, width), BF16),
            pltpu.VMEM((ext, width), BF16),
            pltpu.VMEM((ext, width), BF16),
            pltpu.VMEM((GP, width), BF16),
            pltpu.VMEM((GP, width), BF16),
            pltpu.SemaphoreType.DMA((5,)),
        ],
        compiler_params=pltpu.CompilerParams(
            collective_id=3, has_side_effects=True, vmem_limit_bytes=56 * 2**20
        ),
        name="attend",
    )(doc_len, rel_table, long_x, glob_x, *weights)


class Reducer:
    def __init__(self, rows, split, scratch, pieces=None, order=None, parts=None):
        self.ids = mesh_ids()
        self.parts = parts
        self.order = order
        self.halves = (slice(0, split), slice(split, rows))
        held, self.from_core, self.from_one, self.from_two = scratch[:4]
        self.local, self.sends, self.recvs = scratch[4:7]
        if parts is None:
            self.from_z, self.z_sends, self.z_recvs = scratch[7:]
        self.pieces, self.held = pieces, held
        self.mine = held.at[self.ids[3]] if pieces is None else held.at[0]

    @staticmethod
    def scratch(rows, width, sides, with_z=False):
        buffers = [
            pltpu.VMEM((sides, 4, 2, 2, rows, width), BF16),
            pltpu.VMEM((4, 2, 2, rows, width), BF16),
            pltpu.VMEM((4, 2, rows, width), BF16),
            pltpu.VMEM((4, rows, width), BF16),
            pltpu.SemaphoreType.DMA((4,)),
            pltpu.SemaphoreType.DMA((5, 4)),
            pltpu.SemaphoreType.DMA((5, 4)),
        ]
        if with_z:
            buffers += [
                pltpu.VMEM((3, rows, width), BF16),
                pltpu.SemaphoreType.DMA((4,)),
                pltpu.SemaphoreType.DMA((3,)),
            ]
        return buffers

    def partners(self):
        z, y, x, core = self.ids
        dp, seq = z * 2 + y, x * 2 + core
        near = [(dp, x * 2 + 1 - core), (dp, (1 - x) * 2 + core), (z * 2 + 1 - y, seq)]
        return near + [(lax.rem(z + step, 4) * 2 + y, seq) for step in (1, 2, 3)]

    def target(self, chunk):
        return self.order(chunk) if self.order else lax.rem(self.ids[0] + 1 + chunk, 4)

    def remote(self, source, dest, kind, send_at, recv_at, device):
        return pltpu.make_async_remote_copy(
            src_ref=source,
            dst_ref=dest,
            send_sem=self.sends.at[kind, send_at],
            recv_sem=self.recvs.at[kind, recv_at],
            device_id=device,
            device_id_type=pl.DeviceIdType.MESH,
        )

    def own_copy(self, chunk):
        core, to = self.ids[3], self.target(chunk)
        return pltpu.make_async_copy(
            self.pieces.at[core, to], self.mine.at[to], self.local.at[chunk]
        )

    def core_copy(self, chunk):
        core, to = self.ids[3], self.target(chunk)
        source = (self.held if self.pieces is None else self.pieces).at[1 - core, to]
        return self.remote(source, self.from_core.at[to], 0, chunk, chunk, self.partners()[0])

    def first_copies(self, chunk):
        z, y, x, core = self.ids
        to = self.target(chunk)
        one, two = self.halves
        near = self.partners()
        return (
            self.remote(
                self.mine.at[to, :, 1 - x, one],
                self.from_one.at[to, :, one],
                1,
                chunk,
                chunk,
                near[1],
            ),
            self.remote(
                self.mine.at[to, 1 - y, :, two],
                self.from_one.at[to, :, two],
                2,
                chunk,
                chunk,
                near[2],
            ),
        )

    def second_copies(self, chunk):
        z, y, x, core = self.ids
        to = self.target(chunk)
        one, two = self.halves
        near = self.partners()
        return (
            self.remote(
                self.mine.at[to, 1 - y, x, one],
                self.from_two.at[to, one],
                3,
                chunk,
                chunk,
                near[2],
            ),
            self.remote(
                self.mine.at[to, y, 1 - x, two],
                self.from_two.at[to, two],
                4,
                chunk,
                chunk,
                near[1],
            ),
        )

    def last_copy(self, chunk):
        z, y, x, core = self.ids
        to = self.target(chunk)
        slot = lax.rem(z - to + 4, 4) - 1
        return pltpu.make_async_remote_copy(
            src_ref=self.mine.at[to, y, x],
            dst_ref=self.from_z.at[slot],
            send_sem=self.z_sends.at[chunk],
            recv_sem=self.z_recvs.at[slot],
            device_id=(to * 2 + y, x * 2 + core),
            device_id_type=pl.DeviceIdType.MESH,
        )

    def arrival(self, slot):
        z, y, x, core = self.ids
        return pltpu.make_async_remote_copy(
            src_ref=self.mine.at[z, y, x],
            dst_ref=self.from_z.at[slot],
            send_sem=self.z_sends.at[slot],
            recv_sem=self.z_recvs.at[slot],
            device_id=self.partners()[3],
            device_id_type=pl.DeviceIdType.MESH,
        )

    def leaves(self, chunk):
        return self.target(chunk) != self.ids[0]

    def fill(self, to, at, value):
        self.held[at % 2, to, at // 4, at // 2 % 2] = value.astype(BF16)

    def start(self, chunk):
        self.core_copy(chunk).start()
        if self.pieces is not None:
            self.own_copy(chunk).start()

    def add_core(self, chunk):
        to = self.target(chunk)
        if self.pieces is not None:
            self.own_copy(chunk).wait()
        self.core_copy(chunk).wait_recv()

        def add(index, carry):
            at = (to, lax.div(index, 2), lax.rem(index, 2))
            self.mine[at] = self.mine[at] + self.from_core[at]
            return carry

        lax.fori_loop(0, 4, add, 0)
        for copy in self.first_copies(chunk):
            copy.start()

    def add_first(self, chunk):
        z, y, x, core = self.ids
        one, two = self.halves
        to = self.target(chunk)
        for copy in self.first_copies(chunk):
            copy.wait_recv()

        def add(index, carry):
            for at, rows in (((to, index, x), one), ((to, y, index), two)):
                self.mine[at + (rows,)] = self.mine[at + (rows,)] + self.from_one[to, index, rows]
            return carry

        lax.fori_loop(0, 2, add, 0)
        for copy in self.second_copies(chunk):
            copy.start()

    def add_second(self, chunk):
        z, y, x, core = self.ids
        to = self.target(chunk)
        for copy in self.second_copies(chunk):
            copy.wait_recv()
        if self.parts is not None:
            self.parts[to] = self.mine[to, y, x] + self.from_two[to]
            return

        @pl.when(self.leaves(chunk))
        def _():
            self.mine[to, y, x] = self.mine[to, y, x] + self.from_two[to]
            self.last_copy(chunk).start()

    def finish(self, out=None):
        z, y, x, core = self.ids
        if self.parts is None:
            total = self.mine[z, y, x].astype(F32) + self.from_two[z].astype(F32)
            for slot in range(3):
                self.arrival(slot).wait_recv()
                total += self.from_z[slot].astype(F32)
            out[...] = total
        for chunk in range(4):
            self.core_copy(chunk).wait_send()
            for copy in self.first_copies(chunk) + self.second_copies(chunk):
                copy.wait_send()
            if self.parts is None:

                @pl.when(self.leaves(chunk))
                def _(chunk=chunk):
                    self.last_copy(chunk).wait_send()


class ZSum:
    def __init__(self, parts, scratch):
        self.ids = mesh_ids()
        self.parts = parts
        self.own, self.from_z, self.local, self.sends, self.recvs = scratch

    @staticmethod
    def scratch(rows, width):
        return [
            pltpu.VMEM((rows, width), BF16),
            pltpu.VMEM((3, rows, width), BF16),
            pltpu.SemaphoreType.DMA,
            pltpu.SemaphoreType.DMA((3,)),
            pltpu.SemaphoreType.DMA((3,)),
        ]

    def own_copy(self):
        return pltpu.make_async_copy(self.parts.at[self.ids[0]], self.own, self.local)

    def copies(self):
        z, y, x, core = self.ids
        for slot in range(3):
            to = lax.rem(z + 3 - slot, 4)
            yield pltpu.make_async_remote_copy(
                src_ref=self.parts.at[to],
                dst_ref=self.from_z.at[slot],
                send_sem=self.sends.at[slot],
                recv_sem=self.recvs.at[slot],
                device_id=(to * 2 + y, x * 2 + core),
                device_id_type=pl.DeviceIdType.MESH,
            )

    def start(self):
        self.own_copy().start()
        for copy in self.copies():
            copy.start()

    def finish(self, out):
        self.own_copy().wait()
        total = self.own[...].astype(F32)
        for slot, copy in enumerate(self.copies()):
            copy.wait_recv()
            total += self.from_z[slot].astype(F32)
        out[...] = total
        for copy in self.copies():
            copy.wait_send()


class EverySum:
    def __init__(self, scratch):
        self.kept, self.arrived, self.from_z, self.sends, self.recvs = scratch
        z, y, x, core = mesh_ids()
        seq = x * 2 + core
        self.z = z
        self.pairs = (
            (z * 2 + y, x * 2 + 1 - core),
            (z * 2 + y, (1 - x) * 2 + core),
            (z * 2 + 1 - y, seq),
        )
        self.along_z = [(lax.rem(z + step, 4) * 2 + y, seq) for step in (1, 2, 3)]

    @staticmethod
    def scratch(rows, width):
        return [
            pltpu.VMEM((3, rows, width), F32),
            pltpu.VMEM((3, rows, width), F32),
            pltpu.VMEM((4, rows, width), F32),
            pltpu.SemaphoreType.DMA((6,)),
            pltpu.SemaphoreType.DMA((6,)),
        ]

    def copy(self, stage):
        return pltpu.make_async_remote_copy(
            src_ref=self.kept.at[stage],
            dst_ref=self.arrived.at[stage],
            send_sem=self.sends.at[stage],
            recv_sem=self.recvs.at[stage],
            device_id=self.pairs[stage],
            device_id_type=pl.DeviceIdType.MESH,
        )

    def z_copies(self):
        for at, device in enumerate(self.along_z):
            yield pltpu.make_async_remote_copy(
                src_ref=self.from_z.at[self.z],
                dst_ref=self.from_z.at[self.z],
                send_sem=self.sends.at[3 + at],
                recv_sem=self.recvs.at[3 + at],
                device_id=device,
                device_id_type=pl.DeviceIdType.MESH,
            )

    def step(self, stage):
        if stage > 0:
            self.copy(stage - 1).wait_recv()
            total = self.kept[stage - 1] + self.arrived[stage - 1]
            if stage < 3:
                self.kept[stage] = total
            else:
                self.from_z[self.z] = total
        if stage < 3:
            self.copy(stage).start()
        else:
            for copy in self.z_copies():
                copy.start()

    def finish(self, out):
        for copy in self.z_copies():
            copy.wait_recv()
        out[...] = (self.from_z[0] + self.from_z[1]) + (self.from_z[2] + self.from_z[3])
        for copy in [self.copy(stage) for stage in range(3)] + list(self.z_copies()):
            copy.wait_send()


def mesh_ids():
    dp, seq = lax.axis_index("dp"), lax.axis_index("seq")
    return lax.div(dp, 2), lax.rem(dp, 2), lax.div(seq, 2), lax.rem(seq, 2)


def meet(devices):
    barrier = pltpu.get_barrier_semaphore()
    for device in devices:
        pl.semaphore_signal(barrier, inc=1, device_id=device, device_id_type=pl.DeviceIdType.MESH)
    pl.semaphore_wait(barrier, len(devices))


EARLY_PLAN = (
    (1, "add_core", 0),
    (1, "add_core", 1),
    (2, "add_core", 2),
    (2, "add_core", 3),
    (4, "add_first", 0),
    (4, "add_first", 1),
    (5, "add_first", 2),
    (5, "add_first", 3),
    (5, "add_second", 0),
    (6, "add_second", 1),
    (6, "add_second", 2),
    (6, "add_second", 3),
)


def late_kernel(
    sizes,
    planned,
    long_ref,
    glob_ref,
    dq_ref,
    dk_ref,
    dv_ref,
    dmid_far,
    wq_far,
    wk_far,
    wv_far,
    gain_ref,
    shift_ref,
    table_ref,
    *rest,
):
    block, count, quarter, seq_count, pairs = sizes
    rows = block + quarter
    width = long_ref.shape[1]
    if planned:
        early_parts, long_far, glob_out, late_ref, total_ref, scale_ref, early_ref, *rest = rest
    else:
        long_far, glob_out, gq_ref, gk_ref, gv_ref, total_ref, scale_ref, *rest = rest
    normed_t, every, gather_sends, gather_recvs, *rest = rest
    dmid_ref, wq_ref, wk_ref, wv_ref, loads, long_out, store, *rest = rest
    storing = pltpu.make_async_copy(long_out, long_far, store)
    far = (wq_far, wk_far, wv_far, dmid_far)
    loading = [
        pltpu.make_async_copy(source, dest, loads.at[at])
        for at, (source, dest) in enumerate(zip(far, (wq_ref, wk_ref, wv_ref, dmid_ref)))
    ]
    for copy in loading:
        copy.start()
    seq_index = lax.axis_index("seq")
    own_rows = pl.ds(pl.multiple_of(seq_index * quarter, quarter), quarter)
    others = [seq_device(step, seq_count) for step in range(1, seq_count)]

    def gathers():
        for step, device in enumerate(others):
            yield pltpu.make_async_remote_copy(
                src_ref=every.at[own_rows],
                dst_ref=every.at[own_rows],
                send_sem=gather_sends.at[step],
                recv_sem=gather_recvs.at[step],
                device_id=device,
                device_id_type=pl.DeviceIdType.MESH,
            )

    if planned:
        first_sum, second_sum = EverySum(rest[:5]), EverySum(rest[5:10])
        z_sum = ZSum(early_parts, rest[10:15])
        reducer = Reducer(rest[15].shape[-2], 32, rest[15:])

    meet(others + (reducer.partners()[2:] if planned else []))
    heads = 2 * pairs
    first = first_sum.kept.at[0] if planned else total_ref
    first[...] = jnp.zeros(first.shape, F32)
    for pair in range(pairs):
        first[2 * pair : 2 * pair + 2, :WINDOW] = table_ref[pair]
    for at, ref in enumerate((dq_ref, dv_ref)):
        first[heads + at : heads + at + 1] = column_sum(ref[...].astype(F32))
    if planned:
        first_sum.step(0)
        z_sum.start()
    everything = jnp.concatenate([long_ref[...], glob_ref[own_rows]], 0).astype(F32)
    hat, inverse = row_norm(everything)
    normed_t[...] = (hat * gain_ref[...] + shift_ref[...]).astype(BF16).T
    if planned:
        piece = width // 32
        blank = jnp.zeros((8, width), F32)
        def weight_rows(chunk):
            to = reducer.target(chunk)
            some = normed_t[pl.ds(pl.multiple_of(to * 8 * piece, 64), 8 * piece)]
            parts = [dot_n(some, ref[...]) for ref in (dq_ref, dk_ref, dv_ref)]
            for at in range(8):
                rows_at = slice(at * piece, (at + 1) * piece)
                reducer.fill(
                    to, at, jnp.concatenate([part[rows_at] for part in parts] + [blank], 0)
                )
            reducer.start(chunk)

        weight_rows(0)
        first_sum.step(1)
        weight_rows(1)
        first_sum.step(2)
        reducer.add_core(0)
        weight_rows(2)
        first_sum.step(3)
        reducer.add_core(1)
        weight_rows(3)
        for copy in loading:
            copy.wait()
        grads = dot_t(dq_ref[...], wq_ref[...])
        grads += dot_t(dk_ref[...], wk_ref[...]) + dot_t(dv_ref[...], wv_ref[...])
        reducer.add_first(0)
        reducer.add_core(2)
    else:
        for ref, out in ((dq_ref, gq_ref), (dk_ref, gk_ref), (dv_ref, gv_ref)):
            out[...] = dot_n(normed_t[...], ref[...]).astype(BF16)
        for copy in loading:
            copy.wait()
        grads = (
            dot_t(dq_ref[...], wq_ref[...])
            + dot_t(dk_ref[...], wk_ref[...])
            + dot_t(dv_ref[...], wv_ref[...])
        )
    scaled = grads * gain_ref[...]
    total = dmid_ref[...] + inverse * (
        scaled
        - jnp.mean(scaled, -1, keepdims=True)
        - hat * jnp.mean(scaled * hat, -1, keepdims=True)
    )
    every[own_rows] = total[block:].astype(BF16)
    for copy in gathers():
        copy.start()
    long_out[...] = total[:block]
    storing.start()
    second = second_sum.kept.at[0] if planned else scale_ref
    second[...] = jnp.zeros(second.shape, F32)
    second[0:1] = column_sum(grads * hat)
    second[1:2] = column_sum(grads)
    if planned:
        second_sum.step(0)
        reducer.add_first(1)
        second_sum.step(1)
        reducer.add_core(3)
        reducer.add_second(0)
        reducer.add_first(2)
        second_sum.step(2)
        reducer.add_second(1)
        reducer.add_first(3)
        second_sum.step(3)
        reducer.add_second(2)
        reducer.add_second(3)
        first_sum.finish(total_ref)
        z_sum.finish(early_ref)
        reducer.finish(late_ref)
        second_sum.finish(scale_ref)
    for copy in gathers():
        copy.wait_recv()
    glob_out[...] = every[:count].astype(F32)
    storing.wait()
    for copy in gathers():
        copy.wait_send()


def last_part(sizes, planned, long_x, glob_x, dq, dk, dv, dmid, *weights):
    block, count, quarter, seq_count, pairs = sizes
    rows, width = dq.shape
    others = seq_count - 1
    whole = pl.BlockSpec(memory_space=pltpu.VMEM)
    there = pl.BlockSpec(memory_space=pl.ANY)
    shape = jax.ShapeDtypeStruct
    sums = [shape(((2 * pairs + 2 + 7) // 8 * 8, width), F32), shape((8, width), F32)]
    outs = [shape((block, width), F32), shape((count, width), F32)]
    scratch = [
        pltpu.VMEM((width, rows), BF16),
        pltpu.VMEM((GP, width), BF16),
        pltpu.SemaphoreType.DMA((others,)),
        pltpu.SemaphoreType.DMA((others,)),
        pltpu.VMEM((rows, width), F32),
        pltpu.VMEM((width, width), BF16),
        pltpu.VMEM((width, width), BF16),
        pltpu.VMEM((width, width), BF16),
        pltpu.SemaphoreType.DMA((4,)),
        pltpu.VMEM((block, width), F32),
        pltpu.SemaphoreType.DMA,
    ]
    if planned:
        piece = width // 32
        part = 3 * piece + 8
        early = weights[-1].shape[1:]
        outs += [shape((part, width), F32), *sums, shape(early, F32)]
        for part_sums in sums:
            scratch += EverySum.scratch(*part_sums.shape)
        scratch += ZSum.scratch(*early) + Reducer.scratch(part, width, 2, with_z=True)
    else:
        outs += [shape((width, width), BF16)] * 3 + sums
    return pl.pallas_call(
        functools.partial(late_kernel, sizes, planned),
        in_specs=[whole] * 5 + [there] * 4 + [whole] * 3 + [there] * planned,
        out_specs=[there] + [whole] * (len(outs) - 1),
        out_shape=outs,
        scratch_shapes=scratch,
        compiler_params=pltpu.CompilerParams(
            collective_id=2, has_side_effects=True, vmem_limit_bytes=60 * 2**20
        ),
        name="last_part",
    )(long_x, glob_x, dq, dk, dv, dmid, *weights)


def small_kernel(heads, early_ref, late_ref, outer_ref, inner_ref, sums_ref, scale_ref, *outs):
    g_query, g_key, g_value, g_out, g_inner, g_outer, *vectors, table = outs
    device = lax.axis_index("dp") * lax.axis_size("seq") + lax.axis_index("seq")
    piece, width = g_query.shape
    for at, out in enumerate((g_query, g_key, g_value)):
        out[...] = late_ref[at * piece : (at + 1) * piece]
    g_out[...] = early_ref[2 * piece : 3 * piece]
    g_outer[...] = outer_ref[...]
    for source, first, chunk in (
        (inner_ref, 0, 0),
        (inner_ref, piece, 3),
        (early_ref, 0, 1),
        (early_ref, piece, 2),
    ):
        g_inner[:, chunk * width : (chunk + 1) * width] = source[first : first + piece]

    def entries(row, at, length):
        return pltpu.roll(row, width - at * length, 1)[0, :length]

    b_query, b_value, b_out, b_outer, gain_one, shift_one, gain_two, shift_two, b_inner = vectors
    for at, out in enumerate((b_query, b_value)):
        out[...] = entries(sums_ref[heads + at : heads + at + 1], device, piece)
    for at, out in enumerate((gain_one, shift_one)):
        out[...] = entries(scale_ref[at : at + 1], device, piece)
    for at, out in enumerate((b_out, b_outer, gain_two, shift_two)):
        row = 3 * piece + at
        out[...] = entries(early_ref[row : row + 1], device, piece)
    row = pl.ds(3 * piece + 4 + lax.div(device, 8), 1)
    b_inner[...] = entries(early_ref[row], lax.rem(device, 8), 4 * piece)
    labels = table.shape[1]
    turned = pltpu.roll(sums_ref[:, :WINDOW], WINDOW - HALO + R, 1)
    table[...] = turned[:heads, :labels]


def small_results(heads, early, late, outer, inner, sums, scales):
    width = early.shape[1]
    piece = width // 32
    shape = jax.ShapeDtypeStruct
    whole = pl.BlockSpec(memory_space=pltpu.VMEM)
    outs = [shape((piece, width), F32)] * 4
    outs += [shape((piece, 4 * width), F32), shape((4 * piece, width), F32)]
    outs += [shape((piece,), F32)] * 8 + [shape((4 * piece,), F32)]
    outs += [shape((heads, 2 * R + 1), F32)]
    return pl.pallas_call(
        functools.partial(small_kernel, heads),
        in_specs=[whole] * 6,
        out_specs=[whole] * len(outs),
        out_shape=outs,
        name="small_results",
    )(early, late, outer, inner, sums, scales)


def has_plan():
    return (lax.axis_size("dp"), lax.axis_size("seq")) == (8, 4)


GELU_A = 0.7978845608028654
GELU_B = 0.044715


def gate_both(u):
    square = u * u
    turned = jnp.tanh(GELU_A * u * (1.0 + GELU_B * square))
    half = 0.5 * (1.0 + turned)
    slope = half + 0.5 * u * (1.0 - turned * turned) * (
        GELU_A * (1.0 + 3.0 * GELU_B * square)
    )
    return u * half, slope


def column_sum(rows):
    return jnp.sum(rows, 0, keepdims=True)


def ffn_kernel(
    sizes,
    planned,
    len_ref,
    attn_ref,
    long_ref,
    glob_ref,
    dlong_ref,
    dglob_ref,
    lq_ref,
    wo_ref,
    bo_ref,
    gain_ref,
    shift_ref,
    wi_ref,
    bi_ref,
    wr_ref,
    br_ref,
    long_out,
    glob_out,
    dmid_far,
    do_far,
    dog_ref,
    ldg_ref,
    *rest,
):
    block, count, quarter, seq_count, pairs = sizes
    if planned:
        pieces_far, outer_ref, inner_ref, *rest = rest
    else:
        g_outer_ref, g_inner_ref, g_out_ref, vec_ref, *rest = rest
    (
        mid,
        y_sum,
        df_sum,
        normed,
        normed_t,
        dy,
        vectors,
        biases,
        every_do,
        every_ld,
        gather_sends,
        gather_recvs,
        dmid_ref,
        do_ref,
        stores,
        *rest,
    ) = rest
    storing = [
        pltpu.make_async_copy(dmid_ref, dmid_far, stores.at[0]),
        pltpu.make_async_copy(do_ref, do_far, stores.at[1]),
    ]
    if planned:
        even, pieces_ref, *rest = rest
        outer = Reducer(rest[0].shape[-2], 48, rest[:7], order=chunk_of, parts=outer_ref)
        inner = Reducer(rest[7].shape[-2], 16, rest[7:], parts=inner_ref)
    step = pl.program_id(0)
    chunk = chunk_of(step)
    seq_index = lax.axis_index("seq")
    own_rows = pl.ds(pl.multiple_of(seq_index * quarter, quarter), quarter)
    width = mid.shape[1]
    piece = width // 32

    def rows_of(device):
        return pl.ds(pl.multiple_of(device[1] * quarter, quarter), quarter)

    def gather(owner, device, at):
        for kind, every in enumerate((every_do, every_ld)):
            yield pltpu.make_async_remote_copy(
                src_ref=every.at[rows_of(owner)],
                dst_ref=every.at[rows_of(owner)],
                send_sem=gather_sends.at[kind, at],
                recv_sem=gather_recvs.at[kind, at],
                device_id=device,
                device_id_type=pl.DeviceIdType.MESH,
            )

    me = seq_device(0, seq_count)
    if planned:
        sibling, across = outer.partners()[:2]
        first_gathers = [(me, across, 0), (me, sibling, 1)]
        second_gathers = [(across, sibling, 2)]
    else:
        first_gathers = [
            (me, seq_device(at + 1, seq_count), at) for at in range(seq_count - 1)
        ]
        second_gathers = []

    def store_pieces(half):
        rows = (slice(0, 2 * piece), slice(2 * piece, 3 * piece + 8))[half]
        return pltpu.make_async_copy(
            pieces_ref.at[:, :, :, :, rows], pieces_far.at[:, :, :, :, rows], stores.at[2 + half]
        )

    def act(now):
        if planned:
            for at, reducer, name, part in FFN_PLAN:
                if at == now:
                    getattr((outer, inner)[reducer], name)(part)

    def act_in_step(point):
        if planned:
            for now in range(4):
                if any(at == (now, point) for at, _, _, _ in FFN_PLAN):

                    @pl.when(step == now)
                    def _(now=now):
                        act((now, point))

    @pl.when(step == 0)
    def _():
        others = [seq_device(seq_step, seq_count) for seq_step in range(1, seq_count)]
        meet(others + (outer.partners()[2:] if planned else []))
        projected = dot_n(attn_ref[...], wo_ref[...]) + bo_ref[...]
        mid[:block] = long_ref[...].astype(F32) + projected[:block]
        mid[block:] = glob_ref[own_rows].astype(F32) + projected[block:]
        hat, _ = row_norm(mid[...])
        normed[...] = (hat * gain_ref[...] + shift_ref[...]).astype(BF16)
        normed_t[...] = normed[...].T
        position = seq_index * block + lax.broadcasted_iota(jnp.int32, (block, 1), 0)
        dy[:block] = jnp.where(
            position < len_ref[0], dlong_ref[...].astype(F32), 0.0
        ).astype(BF16)
        y_sum[:GP] = jnp.zeros((GP, width), F32)
        y_sum[:count] = dglob_ref[...].astype(F32)
        dy[block:] = y_sum[own_rows].astype(BF16)
        vectors[1:2] = column_sum(dy[...].astype(F32))
        y_sum[...] = mid[...] + br_ref[...]
        df_sum[...] = jnp.zeros_like(df_sum)
        for at in range(4):
            biases[at] = bi_ref[at * width : (at + 1) * width].reshape(1, width)

    act_in_step(0)
    active, slope = gate_both(dot_n(normed[...], wi_ref[...]) + biases[chunk])
    active = active.astype(BF16)
    g_outer = t_dot(active, dy[...])
    if planned:
        for at in range(8):
            outer.fill(chunk, at, g_outer[at * 4 * piece : (at + 1) * 4 * piece])
        outer.start(step)
    else:
        g_outer_ref[...] = g_outer.astype(BF16)
    y_sum[...] += dot_n(active, wr_ref[...])
    hidden = dot_t(dy[...], wr_ref[...]) * slope
    for at in range(4):

        @pl.when(chunk == at)
        def _(at=at):
            vectors[4 + at : 5 + at] = column_sum(hidden)

    hidden = hidden.astype(BF16)
    act_in_step(1)
    df_sum[...] += dot_t(hidden, wi_ref[...])
    g_inner = dot_n(normed_t[...], hidden)
    if planned:

        @pl.when(lax.rem(step, 2) == 0)
        def _():
            even[...] = g_inner

        def halves(at):
            part = slice(at * piece, (at + 1) * piece)
            return jnp.concatenate([even[part], g_inner[part]], 0)

        @pl.when(step == 1)
        def _():
            for at in range(32):
                inner.fill(at // 8, at % 8, halves(at))
            for part in range(4):
                inner.start(part)

        @pl.when(step == 3)
        def _():
            for at in range(32):
                pieces_ref[at % 2, at // 8, at // 4 % 2, at // 2 % 2, : 2 * piece] = halves(
                    at
                ).astype(BF16)
            store_pieces(0).start()

    else:
        g_inner_ref[...] = g_inner.astype(BF16)

    def norm_back(rows):
        hat, inverse = row_norm(mid[rows])
        df = df_sum[rows]
        scaled = df * gain_ref[...]
        dmid = dy[rows].astype(F32) + inverse * (
            scaled
            - jnp.mean(scaled, -1, keepdims=True)
            - hat * jnp.mean(scaled * hat, -1, keepdims=True)
        )
        dmid_ref[rows] = dmid
        low = dmid.astype(BF16)
        grad_o = dot_t(low, wo_ref[...]).astype(BF16)
        do_ref[rows] = grad_o
        return [column_sum(dmid), column_sum(df * hat), column_sum(df)], low, grad_o

    @pl.when(step == 3)
    def _():
        glob_sums, glob_low, grad_o = norm_back(slice(block, block + quarter))
        every_do[own_rows] = grad_o
        both = grad_o.astype(F32) * attn_ref[block:].astype(F32)
        stats = lq_ref[...]
        for head in range(2 * pairs):
            lanes = slice(head // 2 * PAIR, head // 2 * PAIR + PAIR)
            delta = jnp.sum(own_half(head % 2, both[:, lanes]), -1, keepdims=True)
            stats = jnp.where(lane_index() == HD + head, delta, stats)
        every_ld[own_rows] = stats
        for part in first_gathers:
            for copy in gather(*part):
                copy.start()
        glob_out[...] = y_sum[block:].astype(BF16)
        act((4, 0))
        position = seq_index * block + lax.broadcasted_iota(jnp.int32, (block, 1), 0)
        long_out[...] = jnp.where(position < len_ref[0], y_sum[:block], 0.0).astype(BF16)
        long_sums, long_low, _ = norm_back(slice(0, block))
        for at, one, two in zip((0, 2, 3), long_sums, glob_sums):
            vectors[at : at + 1] = one + two
        for copy in storing:
            copy.start()
        if planned:
            for copy in gather(*first_gathers[0]):
                copy.wait_recv()
            for copy in gather(*second_gathers[0]):
                copy.start()
        act((4, 1))
        g_out = t_dot(attn_ref[...], jnp.concatenate([long_low, glob_low], 0))
        if planned:
            for at in range(32):
                pieces_ref[at % 2, at // 8, at // 4 % 2, at // 2 % 2, 2 * piece :] = (
                    jnp.concatenate(
                        [g_out[at * piece : (at + 1) * piece], vectors[...]], 0
                    ).astype(BF16)
                )
            store_pieces(1).start()
            act((4, 2))
            outer.finish()
            inner.finish()
            for half in range(2):
                store_pieces(half).wait()
        else:
            g_out_ref[...] = g_out.astype(BF16)
            vec_ref[...] = vectors[...]
        for part in (first_gathers[1:] if planned else first_gathers) + second_gathers:
            for copy in gather(*part):
                copy.wait_recv()
        for copy in storing:
            copy.wait()
        dog_ref[...] = every_do[...]
        ldg_ref[...] = every_ld[...]
        for part in first_gathers + second_gathers:
            for copy in gather(*part):
                copy.wait_send()


OUTER, INNER = 0, 1
FFN_PLAN = (
    ((1, 0), OUTER, "add_core", 0),
    ((2, 0), OUTER, "add_core", 1),
    ((2, 0), OUTER, "add_first", 0),
    ((2, 1), INNER, "add_core", 0),
    ((2, 1), INNER, "add_core", 1),
    ((2, 1), INNER, "add_core", 2),
    ((2, 1), INNER, "add_core", 3),
    ((3, 0), OUTER, "add_first", 1),
    ((3, 0), OUTER, "add_second", 0),
    ((3, 0), OUTER, "add_core", 2),
    ((3, 1), OUTER, "add_core", 3),
    ((4, 0), INNER, "add_first", 0),
    ((4, 0), INNER, "add_first", 1),
    ((4, 0), OUTER, "add_first", 2),
    ((4, 0), OUTER, "add_second", 1),
    ((4, 1), INNER, "add_first", 2),
    ((4, 1), INNER, "add_first", 3),
    ((4, 1), INNER, "add_second", 0),
    ((4, 1), INNER, "add_second", 1),
    ((4, 2), OUTER, "add_first", 3),
    ((4, 2), OUTER, "add_second", 2),
    ((4, 2), INNER, "add_second", 2),
    ((4, 2), INNER, "add_second", 3),
    ((4, 2), OUTER, "add_second", 3),
)


def chunk_of(step):
    return jnp.where(step == 0, 0, jnp.where(step == 1, 3, step - 1))


def feed_forward(sizes, planned, doc_len, attn, long_x, glob_x, dlong, dglob, lq, *weights):
    block, count, quarter, seq_count, pairs = sizes
    wo, bo, gain, shift, wi, bi, wr, br = weights
    width, hidden = wi.shape
    chunk = hidden // 4
    rows = block + quarter
    whole = pl.BlockSpec(memory_space=pltpu.VMEM)
    shape = jax.ShapeDtypeStruct
    in_specs = [pl.BlockSpec(memory_space=pltpu.SMEM)] + [whole] * 10
    in_specs += [
        pl.BlockSpec((width, chunk), lambda c: (0, chunk_of(c))),
        whole,
        pl.BlockSpec((chunk, width), lambda c: (chunk_of(c), 0)),
        whole,
    ]
    outs = [
        shape((block, width), BF16),
        shape((quarter, width), BF16),
        shape((rows, width), F32),
        shape((rows, width), BF16),
        shape((GP, width), BF16),
        shape((GP, PAIR), F32),
    ]
    there = pl.BlockSpec(memory_space=pl.ANY)
    out_specs = [whole] * 2 + [there] * 2 + [whole] * 2
    others = seq_count - 1
    scratch = [
        pltpu.VMEM((rows, width), F32),
        pltpu.VMEM((rows, width), F32),
        pltpu.VMEM((rows, width), F32),
        pltpu.VMEM((rows, width), BF16),
        pltpu.VMEM((width, rows), BF16),
        pltpu.VMEM((rows, width), BF16),
        pltpu.VMEM((8, width), F32),
        pltpu.VMEM((4, 1, chunk), F32),
        pltpu.VMEM((GP, width), BF16),
        pltpu.VMEM((GP, PAIR), F32),
        pltpu.SemaphoreType.DMA((2, others)),
        pltpu.SemaphoreType.DMA((2, others)),
        pltpu.VMEM((rows, width), F32),
        pltpu.VMEM((rows, width), BF16),
        pltpu.SemaphoreType.DMA((4,)),
    ]
    if planned:
        part, piece = hidden // 32, width // 32
        outs += [
            shape((2, 4, 2, 2, 3 * piece + 8, width), BF16),
            shape((4, part, width), BF16),
            shape((4, 2 * piece, width), BF16),
        ]
        out_specs += [there] + [whole] * 2
        scratch += [
            pltpu.VMEM((width, chunk), F32),
            pltpu.VMEM(outs[-3].shape, BF16),
        ]
        scratch += Reducer.scratch(part, width, 2) + Reducer.scratch(2 * piece, width, 2)
    else:
        outs += [
            shape((hidden, width), BF16),
            shape((width, hidden), BF16),
            shape((width, width), BF16),
            shape((8, width), F32),
        ]
        out_specs += [
            pl.BlockSpec((chunk, width), lambda c: (chunk_of(c), 0)),
            pl.BlockSpec((width, chunk), lambda c: (0, chunk_of(c))),
            whole,
            whole,
        ]
    return pl.pallas_call(
        functools.partial(ffn_kernel, sizes, planned),
        grid=(4,),
        in_specs=in_specs,
        out_specs=out_specs,
        out_shape=outs,
        scratch_shapes=scratch,
        compiler_params=pltpu.CompilerParams(
            collective_id=4, has_side_effects=True, vmem_limit_bytes=62 * 2**20
        ),
        name="feed_forward",
    )(doc_len, attn, long_x, glob_x, dlong, dglob, lq, wo, bo, gain, shift, wi, bi, wr, br)


def back_kernel(
    sizes,
    early_rows,
    len_ref,
    tab_ref,
    q_ref,
    kx_ref,
    vx_ref,
    kg_ref,
    vg_ref,
    o_ref,
    do_ref,
    l_ref,
    dog_ref,
    ldg_ref,
    yq_ref,
    *rest,
):
    block, count, quarter, seq_count, pairs = sizes
    reduces = early_rows > 0
    if reduces:
        pieces_ref, outer_parts, inner_parts, *rest = rest
    dq_ref, dk_ref, dv_ref, dtab_ref, glob_out, *rest = rest
    if reduces:
        early_parts, outer_ref, inner_ref, *rest = rest
    (
        dkx,
        dvx,
        dkg,
        dvg,
        q_send,
        q_recv,
        kv_send,
        kv_recv,
        halo_send,
        halo_recv,
        glob_sends,
        glob_recvs,
        halo_sends,
        halo_recvs,
        every,
        gather_sends,
        gather_recvs,
        *rest,
    ) = rest
    number = pl.program_id(0)
    steps = pairs // 2
    first_pair = 2 * lax.rem(number, steps)
    seq_index = lax.axis_index("seq")
    if reduces:
        reducer = Reducer(early_rows, 16, rest[:7], pieces=pieces_ref, parts=early_parts)
        z_sums = (
            (ZSum(outer_parts, rest[7:12]), outer_ref),
            (ZSum(inner_parts, rest[12:]), inner_ref),
        )
    scale = HD ** (-0.5)
    low_lanes = lane_index() < HD
    own_keys = slice(HALO, HALO + block)
    own_rows = pl.ds(pl.multiple_of(seq_index * quarter, quarter), quarter)

    def glob_copies(kind, at):
        source, dest = ((q_send, q_recv), (kv_send, kv_recv))[kind]
        for step in range(1, seq_count):
            device = seq_device(step, seq_count)
            yield pltpu.make_async_remote_copy(
                src_ref=source.at[device[1], at],
                dst_ref=dest.at[step - 1, at],
                send_sem=glob_sends.at[kind, step - 1, at],
                recv_sem=glob_recvs.at[kind, step - 1, at],
                device_id=device,
                device_id_type=pl.DeviceIdType.MESH,
            )

    def gathers():
        for step in range(1, seq_count):
            yield pltpu.make_async_remote_copy(
                src_ref=every.at[own_rows],
                dst_ref=every.at[own_rows],
                send_sem=gather_sends.at[step - 1],
                recv_sem=gather_recvs.at[step - 1],
                device_id=seq_device(step, seq_count),
                device_id_type=pl.DeviceIdType.MESH,
            )

    def halo_copy(direction, at):
        return pltpu.make_async_remote_copy(
            src_ref=halo_send.at[direction, at],
            dst_ref=halo_recv.at[direction, at],
            send_sem=halo_sends.at[direction, at],
            recv_sem=halo_recvs.at[direction, at],
            device_id=seq_device(2 * direction - 1, seq_count),
            device_id_type=pl.DeviceIdType.MESH,
        )

    has_low, has_high = seq_index > 0, seq_index < seq_count - 1
    sends_to = (has_low, has_high)
    gets_from = (has_high, has_low)

    def close_pair(at):
        lanes = lanes_of(at)
        for direction in range(2):

            @pl.when(gets_from[direction])
            def _(direction=direction):
                halo_copy(direction, at).wait_recv()

        for kind, (total, out) in enumerate(((dkx, dk_ref), (dvx, dv_ref))):
            first, last = HALO + REACH, HALO + block - REACH
            out[:REACH, lanes] = (
                total[at, HALO:first] + halo_recv[1, at, kind].astype(F32)
            ).astype(BF16)
            out[REACH : block - REACH, lanes] = total[at, first:last].astype(BF16)
            out[block - REACH : block, lanes] = (
                total[at, last : HALO + block] + halo_recv[0, at, kind].astype(F32)
            ).astype(BF16)
        sums = []
        for kind, (source, dest) in enumerate(((q_send, q_recv), (kv_send, kv_recv))):
            total = source[seq_index, at].astype(F32)
            for step, copy in enumerate(glob_copies(kind, at)):
                copy.wait_recv()
                total += dest[step, at].astype(F32)
            sums.append(total.astype(BF16))
        dq_ref[block:, lanes] = sums[0]
        dk_ref[block:, lanes] = sums[1][:, :PAIR]
        dv_ref[block:, lanes] = sums[1][:, PAIR:]

    def run_plan(now):
        for at, act, chunk in EARLY_PLAN:
            if now == at:
                getattr(reducer, act)(chunk)

    @pl.when(number == 0)
    def _():
        others = [seq_device(step, seq_count) for step in range(1, seq_count)]
        meet(others + (reducer.partners()[2:] if reduces else []))
        if reduces:
            for chunk in range(4):
                reducer.start(chunk)
            for z_sum, _ in z_sums:
                z_sum.start()
        every[own_rows] = yq_ref[...]
        for copy in gathers():
            copy.start()
        for direction in range(2):

            @pl.when(jnp.logical_not(gets_from[direction]))
            def _(direction=direction):
                halo_recv[direction] = jnp.zeros_like(halo_recv[direction])

    if reduces:
        for now in range(1, 2 * steps):
            if any(at == now for at, _, _ in EARLY_PLAN):

                @pl.when(number == now)
                def _(now=now):
                    run_plan(now)

    def glob_pair(pair, q_ref, kx_ref, vx_ref, kg_ref, vg_ref, dog_ref):
        long_bias = key_bias(seq_index * block, block, len_ref[0])
        near_bias = key_bias(seq_index * quarter, quarter, count)
        query = q_ref[block:] * jnp.asarray(scale, BF16)
        grad_o = dog_ref[...]
        far_k, far_v = kx_ref[own_keys], vx_ref[own_keys]
        near_k, near_v = kg_ref[own_rows], vg_ref[own_rows]
        outs, kept = [], []
        for head in range(2):
            norm = in_three(-pick_column(ldg_ref[...], 2 * pair + head))
            delta = in_three(-pick_column(ldg_ref[...], HD + 2 * pair + head))
            qa = with_lanes(head, query, (1.0,) + norm)
            doa = with_lanes(head, grad_o, delta)
            far = jnp.exp(dot_t(qa, key_side(head, far_k, long_bias)))
            near = jnp.exp(dot_t(qa, key_side(head, near_k, near_bias)))
            far_ds = (far * dot_t(doa, value_side(head, far_v))).astype(BF16)
            near_ds = (near * dot_t(doa, value_side(head, near_v))).astype(BF16)
            outs.append(dot_n(far_ds, far_k) + dot_n(near_ds, near_k))
            kept.append(
                (
                    own_half(head, query),
                    own_half(head, grad_o),
                    far.astype(BF16),
                    near.astype(BF16),
                    far_ds,
                    near_ds,
                )
            )
        own_q, own_do, far, near, far_ds, near_ds = (
            jnp.concatenate(part, 0) for part in zip(*kept)
        )
        for total, edge in ((dkx, own_keys), (dvx, own_keys)):
            total[pair, :HALO] = jnp.zeros((HALO, PAIR), F32)
            total[pair, HALO + block :] = jnp.zeros((HALO, PAIR), F32)
        dkx[pair, own_keys] = t_dot(far_ds, own_q)
        dvx[pair, own_keys] = t_dot(far, own_do)
        dkg[pair] = jnp.zeros((GP, PAIR), F32)
        dvg[pair] = jnp.zeros((GP, PAIR), F32)
        dkg[pair, own_rows] = t_dot(near_ds, own_q)
        dvg[pair, own_rows] = t_dot(near, own_do)
        glob_dq = (jnp.where(low_lanes, outs[0], outs[1]) * scale).astype(BF16)
        q_send[:, pair] = glob_dq.reshape(seq_count, quarter, PAIR)
        for copy in glob_copies(0, pair):
            copy.start()

    def long_pair(pair, q_ref, kx_ref, vx_ref, kg_ref, vg_ref, o_ref, do_ref, tab_ref):
        long_bias = key_bias(seq_index * block - HALO, block + 2 * HALO, len_ref[0])
        glob_bias = key_bias(0, GP, count)
        query = q_ref[:block] * jnp.asarray(scale, BF16)
        grad_o = do_ref[...]
        both = grad_o.astype(F32) * o_ref[...].astype(F32)
        heads = []
        for head in range(2):
            norm = in_three(-pick_column(l_ref[...], 2 * pair + head))
            delta = in_three(-jnp.sum(own_half(head, both), -1, keepdims=True))
            heads.append(
                dict(
                    q=own_half(head, query),
                    do=own_half(head, grad_o),
                    qa=with_lanes(head, query, (1.0,) + norm),
                    doa=with_lanes(head, grad_o, delta),
                    kxa=key_side(head, kx_ref[...], long_bias),
                    vxa=value_side(head, vx_ref[...]),
                    kga=key_side(head, kg_ref[...], glob_bias),
                    vga=value_side(head, vg_ref[...]),
                    bias=band_bias(tab_ref[0, head : head + 1]),
                )
            )
        table_sums = [0.0, 0.0]
        grads_q = []
        for start in range(0, block, SUB):
            rows, keys = slice(start, start + SUB), slice(start, start + WINDOW)
            outs, probs, grads = [], [], []
            for head, own in enumerate(heads):
                band = jnp.exp(dot_t(own["qa"][rows], own["kxa"][keys]) + own["bias"])
                band_ds = band * dot_t(own["doa"][rows], own["vxa"][keys])
                table_sums[head] += band_ds
                glob = jnp.exp(dot_t(own["qa"][rows], own["kga"]))
                glob_ds = (glob * dot_t(own["doa"][rows], own["vga"])).astype(BF16)
                band_ds = band_ds.astype(BF16)
                outs.append(dot_n(band_ds, kx_ref[keys]) + dot_n(glob_ds, kg_ref[...]))
                probs.append((band.astype(BF16), glob.astype(BF16)))
                grads.append((band_ds, glob_ds))
            grads_q.append(jnp.where(low_lanes, outs[0], outs[1]))
            own_q = jnp.concatenate([own["q"][rows] for own in heads], 0)
            own_do = jnp.concatenate([own["do"][rows] for own in heads], 0)
            band, glob = (jnp.concatenate(part, 0) for part in zip(*probs))
            band_ds, glob_ds = (jnp.concatenate(part, 0) for part in zip(*grads))
            dkx[pair, keys] += t_dot(band_ds, own_q)
            dvx[pair, keys] += t_dot(band, own_do)
            dkg[pair] += t_dot(glob_ds, own_q)
            dvg[pair] += t_dot(glob, own_do)
        for kind, total in enumerate((dkg, dvg)):
            kv_send[:, pair, :, kind * PAIR : (kind + 1) * PAIR] = (
                total[pair].astype(BF16).reshape(seq_count, quarter, PAIR)
            )
        for copy in glob_copies(1, pair):
            copy.start()
        for kind, total in enumerate((dkx, dvx)):
            for direction, first in enumerate((HALO - REACH, HALO + block)):
                halo_send[direction, pair, kind] = total[pair, first : first + REACH].astype(BF16)
        for direction in range(2):

            @pl.when(sends_to[direction])
            def _(direction=direction):
                halo_copy(direction, pair).start()

        dq_ref[:block, lanes_of(pair)] = (jnp.concatenate(grads_q, 0) * scale).astype(BF16)
        for head in range(2):
            dtab_ref[pair, head : head + 1] = diagonal_sums(table_sums[head])

    def part(at, *refs):
        return [ref.at[:, at * PAIR : (at + 1) * PAIR] for ref in refs]

    @pl.when(number < steps)
    def _():
        for at in range(2):
            glob_pair(
                first_pair + at, *part(at, q_ref, kx_ref, vx_ref, kg_ref, vg_ref, dog_ref)
            )

    @pl.when(number >= steps)
    def _():
        for at in range(2):
            long_pair(
                first_pair + at,
                *part(at, q_ref, kx_ref, vx_ref, kg_ref, vg_ref, o_ref, do_ref),
                tab_ref.at[at : at + 1],
            )

    @pl.when(number > steps)
    def _():
        close_pair(first_pair - 2)
        close_pair(first_pair - 1)

    @pl.when(number == 2 * steps - 1)
    def _():
        if reduces:
            run_plan(2 * steps)
        close_pair(pairs - 2)
        close_pair(pairs - 1)
        for at in range(pairs):
            for kind in range(2):
                for copy in glob_copies(kind, at):
                    copy.wait_send()
            for direction in range(2):

                @pl.when(sends_to[direction])
                def _(direction=direction, at=at):
                    halo_copy(direction, at).wait_send()

        for copy in gathers():
            copy.wait_recv()
        glob_out[...] = every[:count]
        for copy in gathers():
            copy.wait_send()
        if reduces:
            reducer.finish()
            for z_sum, out in z_sums:
                z_sum.finish(out)


def attend_back(sizes, doc_len, table, q, kx, vx, kg, vg, o, do, l, dog, ldg, yq, *sums):
    block, count, quarter, seq_count, pairs = sizes
    width = q.shape[1]
    early_rows = sums[0].shape[-2] if sums else 0
    ext = block + 2 * HALO
    steps = pairs // 2
    cols = lambda rows: pl.BlockSpec((rows, 2 * PAIR), lambda i: (0, lax.rem(i, steps)))
    whole = pl.BlockSpec(memory_space=pltpu.VMEM)
    shape = jax.ShapeDtypeStruct
    in_specs = [
        pl.BlockSpec(memory_space=pltpu.SMEM),
        pl.BlockSpec((2, 2, WINDOW), lambda i: (lax.rem(i, steps), 0, 0)),
        cols(block + GP),
        cols(ext),
        cols(ext),
        cols(GP),
        cols(GP),
        cols(block),
        cols(block),
        whole,
        cols(GP),
        whole,
        whole,
    ]
    rows = block + quarter
    outs = [shape((rows, width), BF16)] * 3 + [shape((pairs, 2, WINDOW), F32)]
    outs.append(shape((count, width), BF16))
    others = seq_count - 1
    scratch = [
        pltpu.VMEM((pairs, ext, PAIR), F32),
        pltpu.VMEM((pairs, ext, PAIR), F32),
        pltpu.VMEM((pairs, GP, PAIR), F32),
        pltpu.VMEM((pairs, GP, PAIR), F32),
        pltpu.VMEM((seq_count, pairs, quarter, PAIR), BF16),
        pltpu.VMEM((others, pairs, quarter, PAIR), BF16),
        pltpu.VMEM((seq_count, pairs, quarter, 2 * PAIR), BF16),
        pltpu.VMEM((others, pairs, quarter, 2 * PAIR), BF16),
        pltpu.VMEM((2, pairs, 2, REACH, PAIR), BF16),
        pltpu.VMEM((2, pairs, 2, REACH, PAIR), BF16),
        pltpu.SemaphoreType.DMA((2, others, pairs)),
        pltpu.SemaphoreType.DMA((2, others, pairs)),
        pltpu.SemaphoreType.DMA((2, pairs)),
        pltpu.SemaphoreType.DMA((2, pairs)),
        pltpu.VMEM((GP, width), BF16),
        pltpu.SemaphoreType.DMA((others,)),
        pltpu.SemaphoreType.DMA((others,)),
    ]
    args = [doc_len, table, q, kx, vx, kg, vg, o, do, l, dog, ldg, yq, *sums]
    if early_rows:
        in_specs += [pl.BlockSpec(memory_space=pl.ANY)] * 3
        outs.append(shape((4, early_rows, width), BF16))
        scratch += Reducer.scratch(early_rows, width, 1)
        for parts in sums[1:]:
            outs.append(shape(parts.shape[1:], F32))
            scratch += ZSum.scratch(*parts.shape[1:])
    return pl.pallas_call(
        functools.partial(back_kernel, sizes, early_rows),
        grid=(2 * steps,),
        in_specs=in_specs,
        out_specs=[whole] * len(outs),
        out_shape=outs,
        scratch_shapes=scratch,
        compiler_params=pltpu.CompilerParams(
            collective_id=1, has_side_effects=True, vmem_limit_bytes=60 * 2**20
        ),
        name="attend_back",
    )(*args)


def on_device(
    long_input,
    global_input,
    lengths,
    w_query,
    b_query,
    w_key,
    w_value,
    b_value,
    w_out,
    b_out,
    w_inner,
    b_inner,
    w_outer,
    b_outer,
    norm1_gain,
    norm1_shift,
    norm2_gain,
    norm2_shift,
    rel_table,
    long_cotangent,
    global_cotangent,
):
    seq_count = lax.axis_size("seq")
    data_count = lax.axis_size("dp")
    seq_index = lax.axis_index("seq")
    block = long_input.shape[1]
    count = global_input.shape[1]
    width = long_input.shape[2]
    heads = rel_table.shape[1]
    pairs = heads // 2
    labels = 2 * R + 1
    quarter = GP // seq_count
    sizes = Sizes(block, count, quarter, seq_count, pairs)
    queries, kx, vx, kg, vg, attn_low, long_l, glob_l, glob_x, table = attend(
        sizes,
        lengths,
        rel_table.T,
        long_input[0],
        global_input[0],
        w_query,
        w_key,
        w_value,
        b_query,
        b_value,
        norm1_gain,
        norm1_shift,
    )
    planned = has_plan()
    long_result, own_out, grad_mid, grad_attn, every_do, every_ld, *gradients = feed_forward(
        sizes,
        planned,
        lengths,
        attn_low,
        long_input[0],
        glob_x,
        long_cotangent[0],
        global_cotangent[0],
        glob_l,
        w_out,
        b_out,
        norm2_gain,
        norm2_shift,
        w_inner,
        b_inner,
        w_outer,
        b_outer,
    )
    query_low, key_low, value_low, dtab, glob_out, *early = attend_back(
        sizes,
        lengths,
        table,
        queries,
        kx,
        vx,
        kg,
        vg,
        attn_low,
        grad_attn,
        long_l,
        every_do,
        every_ld,
        own_out,
        *(gradients if planned else []),
    )
    long_grad, glob_grad, *late = last_part(
        sizes,
        planned,
        long_input[0],
        glob_x,
        query_low,
        key_low,
        value_low,
        grad_mid,
        w_query,
        w_key,
        w_value,
        norm1_gain,
        norm1_shift,
        dtab,
        *early[:1],
    )
    if planned:
        (
            g_query,
            g_key,
            g_value,
            g_out,
            g_inner,
            g_outer,
            g_b_query,
            g_b_value,
            g_b_out,
            g_b_outer,
            g_g1,
            g_s1,
            g_g2,
            g_s2,
            g_b_inner,
            table_total,
        ) = small_results(
            heads,
            late[3],
            late[0],
            early[1],
            early[2],
            late[1],
            late[2],
        )
        table_total = table_total.T
    else:
        devices = data_count * seq_count
        own_part = lambda vector: lax.dynamic_slice_in_dim(
            vector,
            (lax.axis_index("dp") * seq_count + seq_index) * (vector.shape[0] // devices),
            vector.shape[0] // devices,
        )
        g_outer, g_inner, g_out, vectors = gradients
        g_outer, g_inner, g_out, g_query, g_key, g_value = (
            lax.psum_scatter(g.astype(BF16), ("dp", "seq"), scatter_dimension=0, tiled=True).astype(
                F32
            )
            for g in (g_outer, g_inner, g_out, *late[:3])
        )
        vectors, sums, scales = lax.psum((vectors, *late[3:]), ("dp", "seq"))
        g_b_query, g_b_value = (own_part(sums[heads + i]) for i in range(2))
        g_g1, g_s1 = (own_part(scales[i]) for i in range(2))
        g_b_out, g_b_outer, g_g2, g_s2 = (own_part(vectors[i]) for i in range(4))
        g_b_inner = own_part(vectors[4:].reshape(-1))
        table_total = sums[:heads, HALO - R : HALO - R + labels].T
    return (
        long_result[None],
        glob_out[None],
        long_grad[None],
        glob_grad[None],
        g_query,
        g_b_query,
        g_key,
        g_value,
        g_b_value,
        g_out,
        g_b_out,
        g_inner,
        g_b_inner,
        g_outer,
        g_b_outer,
        g_g1,
        g_s1,
        g_g2,
        g_s2,
        table_total,
    )


def solution(mesh):
    rows, whole = P("dp", "seq", None), P("dp", None, None)
    matrix, vector = P(("dp", "seq"), None), P(("dp", "seq"))
    return jax.shard_map(
        on_device,
        mesh=mesh,
        in_specs=(rows, whole, P("dp")) + (P(),) * 16 + (rows, whole),
        out_specs=(
            rows,
            whole,
            rows,
            whole,
            matrix,
            vector,
            matrix,
            matrix,
            vector,
            matrix,
            vector,
            matrix,
            vector,
            matrix,
            vector,
            vector,
            vector,
            vector,
            vector,
            P(),
        ),
        check_vma=False,
    )
```

```python
import functools
from typing import NamedTuple

import jax
import jax.numpy as jnp
from jax import lax
from jax.experimental import pallas as pl
from jax.experimental.pallas import tpu as pltpu
from jax.sharding import PartitionSpec as P

HD = 64
R = 84
PAIR = 2 * HD
HALO = 128
REACH = 96
GP = 256
SUB = 256
WINDOW = SUB + 2 * HALO
EPSILON = 1e-05
MASKED = -1e30
F32 = jnp.float32
BF16 = jnp.bfloat16


def dot_t(left, right):
    return lax.dot_general(left, right, (((1,), (1,)), ((), ())), preferred_element_type=F32)


def dot_n(left, right):
    return lax.dot_general(left, right, (((1,), (0,)), ((), ())), preferred_element_type=F32)


def t_dot(left, right):
    return lax.dot_general(left, right, (((0,), (0,)), ((), ())), preferred_element_type=F32)


def band_bias(table_row):
    spread = jnp.broadcast_to(table_row, (SUB, WINDOW))
    return pltpu.roll(spread, 0, 1, stride=1, stride_axis=0)


def diagonal_sums(rows):
    height, width = rows.shape
    while height > 8:
        height //= 2
        rows = rows[:height] + pltpu.roll(rows[height:], width - height, 1)
    row = lax.broadcasted_iota(jnp.int32, rows.shape, 0)
    for bit in (1, 2, 4):
        rows = jnp.where((row & bit) != 0, pltpu.roll(rows, width - bit, 1), rows)
    return jnp.sum(rows, 0, keepdims=True)


def lane_index():
    return lax.broadcasted_iota(jnp.int32, (1, PAIR), 1)


def own_half(head, value):
    low_lanes = lane_index() < HD
    return jnp.where(low_lanes if head == 0 else ~low_lanes, value, jnp.zeros_like(value))


def other_lane(head):
    return HD * (1 - head)


def with_lanes(head, value, columns):
    wide = own_half(head, value.astype(F32))
    lane = lane_index()
    for offset, column in enumerate(columns):
        wide = jnp.where(lane == other_lane(head) + offset, column, wide)
    return wide.astype(BF16)


def in_three(column):
    high = column.astype(BF16).astype(F32)
    middle = (column - high).astype(BF16).astype(F32)
    return (high, middle, column - high - middle)


def key_bias(first, rows, end):
    position = first + lax.broadcasted_iota(jnp.int32, (rows, 1), 0)
    return jnp.where((position >= 0) & (position < end), 0.0, MASKED)


def pick_column(rows, index):
    return jnp.sum(jnp.where(lane_index() == index, rows, 0.0), -1, keepdims=True)


def key_side(head, keys, bias):
    return with_lanes(head, keys, (bias, 1.0, 1.0, 1.0))


def value_side(head, values):
    return with_lanes(head, values, (1.0, 1.0, 1.0))


def softmax_rows(parts, value_parts, head):
    top = functools.reduce(
        jnp.maximum, [jnp.max(part, -1, keepdims=True) for part in parts]
    )
    mixed = sum(
        dot_n(jnp.exp(part - top).astype(BF16), values)
        for part, values in zip(parts, value_parts)
    )
    at = other_lane(head)
    total = mixed[:, at : at + 1]
    return mixed / total, top + jnp.log(total)


def seq_device(steps, seq_count):
    return (lax.axis_index("dp"), lax.rem(lax.axis_index("seq") + steps + seq_count, seq_count))


def row_norm(rows):
    centred = rows - jnp.mean(rows, -1, keepdims=True)
    inverse = lax.rsqrt(jnp.mean(centred * centred, -1, keepdims=True) + EPSILON)
    return centred * inverse, inverse


def put_column(ref, rows, index, column):
    ref[rows] = jnp.where(lane_index() == index, column, ref[rows])


def lanes_of(at):
    return pl.ds(pl.multiple_of(at * PAIR, PAIR), PAIR)


class Sizes(NamedTuple):
    block: int
    count: int
    quarter: int
    seq_count: int
    pairs: int


def attend_kernel(
    sizes,
    len_ref,
    rel_ref,
    long_ref,
    raw_ref,
    wq_far,
    wk_far,
    wv_far,
    bq_ref,
    bv_ref,
    gain_ref,
    shift_ref,
    q_far,
    kx_far,
    vx_far,
    kg_far,
    vg_far,
    o_ref,
    l_ref,
    lq_ref,
    glob_ref,
    tab_ref,
    spread,
    wide,
    part_o,
    part_l,
    from_o,
    from_l,
    halo_sends,
    halo_recvs,
    part_sends,
    part_recvs,
    wq_ref,
    wk_ref,
    wv_ref,
    loads,
    q_ref,
    kx_ref,
    vx_ref,
    kg_ref,
    vg_ref,
    stores,
):
    block, count, quarter, seq_count, pairs = sizes
    ext = block + 2 * HALO
    seq_index = lax.axis_index("seq")
    scale = jnp.asarray(HD ** (-0.5), BF16)
    low_lanes = lane_index() < HD
    own_keys = slice(HALO, HALO + block)
    own_rows = pl.ds(pl.multiple_of(seq_index * quarter, quarter), quarter)
    neighbours = (seq_index > 0, seq_index < seq_count - 1)
    barrier = pltpu.get_barrier_semaphore()
    for step in range(1, seq_count):
        pl.semaphore_signal(
            barrier,
            inc=1,
            device_id=seq_device(step, seq_count),
            device_id_type=pl.DeviceIdType.MESH,
        )

    def halo_copies(direction):
        source = HALO if direction == 0 else HALO + block - REACH
        dest = HALO + block if direction == 0 else HALO - REACH
        for kind, ref in enumerate((kx_ref, vx_ref)):
            yield pltpu.make_async_remote_copy(
                src_ref=ref.at[source : source + REACH],
                dst_ref=ref.at[dest : dest + REACH],
                send_sem=halo_sends.at[direction, kind],
                recv_sem=halo_recvs.at[direction, kind],
                device_id=seq_device(2 * direction - 1, seq_count),
                device_id_type=pl.DeviceIdType.MESH,
            )

    def part_copies():
        for step in range(1, seq_count):
            device = seq_device(step, seq_count)
            rows = pl.ds(pl.multiple_of(device[1] * quarter, quarter), quarter)
            for kind, (source, dest) in enumerate(((part_o, from_o), (part_l, from_l))):
                yield step, kind, pltpu.make_async_remote_copy(
                    src_ref=source.at[rows],
                    dst_ref=dest.at[step - 1],
                    send_sem=part_sends.at[kind, step - 1],
                    recv_sem=part_recvs.at[kind, step - 1],
                    device_id=device,
                    device_id_type=pl.DeviceIdType.MESH,
                )

    loading = [
        pltpu.make_async_copy(source, dest, loads.at[at])
        for at, (source, dest) in enumerate(
            ((wk_far, wk_ref), (wv_far, wv_ref), (wq_far, wq_ref))
        )
    ]
    for copy in loading:
        copy.start()
    gain, shift = gain_ref[...], shift_ref[...]
    labels, heads = rel_ref.shape
    spread[...] = jnp.full(spread.shape, MASKED, F32)
    spread[:labels, :heads] = rel_ref[...]
    turned = pltpu.roll(spread[...].T, HALO - R, 1)
    for pair in range(pairs):
        tab_ref[pair] = turned[2 * pair : 2 * pair + 2]
    normed_long = (row_norm(long_ref[...].astype(F32))[0] * gain + shift).astype(BF16)
    loading[0].wait()
    kx_ref[own_keys] = dot_n(normed_long, wk_ref[...]).astype(BF16)
    loading[1].wait()
    vx_ref[own_keys] = (dot_n(normed_long, wv_ref[...]) + bv_ref[...]).astype(BF16)
    pl.semaphore_wait(barrier, seq_count - 1)
    for direction, first in enumerate((HALO - REACH, HALO + block)):

        @pl.when(neighbours[direction])
        def _(direction=direction):
            for copy in halo_copies(direction):
                copy.start()

        outer = slice(0, first) if direction == 0 else slice(first + REACH, ext)
        for ref in (kx_ref, vx_ref):
            ref[outer] = jnp.zeros((HALO - REACH, ref.shape[1]), BF16)

        @pl.when(jnp.logical_not(neighbours[direction]))
        def _(first=first):
            for ref in (kx_ref, vx_ref):
                ref[first : first + REACH] = jnp.zeros((REACH, ref.shape[1]), BF16)

    wide[...] = jnp.zeros_like(wide)
    wide[:count] = raw_ref[...].astype(F32)
    glob_ref[...] = wide[...].astype(BF16)
    normed_glob = (row_norm(wide[...])[0] * gain + shift).astype(BF16)
    kg_ref[...] = dot_n(normed_glob, wk_ref[...]).astype(BF16)
    vg_ref[...] = (dot_n(normed_glob, wv_ref[...]) + bv_ref[...]).astype(BF16)
    loading[2].wait()
    q_ref[block:] = (dot_n(normed_glob, wq_ref[...]) + bq_ref[...]).astype(BF16)
    q_ref[:block] = (dot_n(normed_long, wq_ref[...]) + bq_ref[...]).astype(BF16)
    part_l[...] = jnp.zeros_like(part_l)
    l_ref[...] = jnp.zeros_like(l_ref)

    def glob_pair(pair, carry):
        lanes = lanes_of(pair)
        far_bias = key_bias(seq_index * block, block, len_ref[0])
        near_bias = key_bias(seq_index * quarter, quarter, count)
        query = q_ref[block:, lanes] * scale
        outs = []
        for head in range(2):
            q = with_lanes(head, query, (1.0,))
            far = dot_t(q, with_lanes(head, kx_ref[own_keys, lanes], (far_bias,)))
            near = dot_t(q, with_lanes(head, kg_ref[own_rows, lanes], (near_bias,)))
            out, norm = softmax_rows(
                [far, near],
                [
                    with_lanes(head, vx_ref[own_keys, lanes], (1.0,)),
                    with_lanes(head, vg_ref[own_rows, lanes], (1.0,)),
                ],
                head,
            )
            outs.append(out)
            put_column(part_l, slice(None), 2 * pair + head, norm)
        part_o[:, lanes] = jnp.where(low_lanes, outs[0], outs[1]).astype(BF16)
        return carry

    lax.fori_loop(0, pairs, glob_pair, 0, unroll=2)
    for _, _, copy in part_copies():
        copy.start()
    for direction in range(2):

        @pl.when(neighbours[1 - direction])
        def _(direction=direction):
            for copy in halo_copies(direction):
                copy.wait_recv()

    storing = [
        pltpu.make_async_copy(source, dest, stores.at[at])
        for at, (source, dest) in enumerate(
            (
                (q_ref, q_far),
                (kx_ref, kx_far),
                (vx_ref, vx_far),
                (kg_ref, kg_far),
                (vg_ref, vg_far),
            )
        )
    ]
    for copy in storing:
        copy.start()

    def long_pair(pair, carry):
        lanes = lanes_of(pair)
        long_bias = key_bias(seq_index * block - HALO, ext, len_ref[0])
        glob_bias = key_bias(0, GP, count)
        query = q_ref[:block, lanes] * scale
        outs = []
        for head in range(2):
            q = with_lanes(head, query, (1.0,))
            kx = with_lanes(head, kx_ref[:, lanes], (long_bias,))
            kg = with_lanes(head, kg_ref[:, lanes], (glob_bias,))
            vx, vg = (with_lanes(head, ref[:, lanes], (1.0,)) for ref in (vx_ref, vg_ref))
            bias = band_bias(tab_ref[pair, head : head + 1])
            mixed = []
            for start in range(0, block, SUB):
                rows, keys = slice(start, start + SUB), slice(start, start + WINDOW)
                out, norm = softmax_rows(
                    [dot_t(q[rows], kx[keys]) + bias, dot_t(q[rows], kg)], [vx[keys], vg], head
                )
                mixed.append(out)
                put_column(l_ref, rows, 2 * pair + head, norm)
            outs.append(jnp.concatenate(mixed, 0))
        o_ref[:block, lanes] = jnp.where(low_lanes, outs[0], outs[1]).astype(BF16)
        return carry

    lax.fori_loop(0, pairs, long_pair, 0, unroll=2)
    for _, _, copy in part_copies():
        copy.wait_recv()
    norms = [part_l[own_rows]] + [from_l[step] for step in range(seq_count - 1)]
    outs = [part_o[own_rows]] + [from_o[step] for step in range(seq_count - 1)]
    top = functools.reduce(jnp.maximum, norms)
    shares = [jnp.exp(norm - top) for norm in norms]
    total = sum(shares)
    lq_ref[...] = top + jnp.log(total)
    shares = [share / total for share in shares]
    for at in range(pairs):
        lanes = slice(at * PAIR, (at + 1) * PAIR)
        mixed = 0.0
        for share, out in zip(shares, outs):
            spread = jnp.where(
                low_lanes, share[:, 2 * at : 2 * at + 1], share[:, 2 * at + 1 : 2 * at + 2]
            )
            mixed += spread * out[:, lanes].astype(F32)
        o_ref[block:, lanes] = mixed.astype(BF16)
    for copy in storing:
        copy.wait()
    for _, _, copy in part_copies():
        copy.wait_send()
    for direction in range(2):

        @pl.when(neighbours[direction])
        def _(direction=direction):
            for copy in halo_copies(direction):
                copy.wait_send()


def attend(sizes, doc_len, rel_table, long_x, glob_x, *weights):
    block, count, quarter, seq_count, pairs = sizes
    width = long_x.shape[1]
    ext = block + 2 * HALO
    whole = pl.BlockSpec(memory_space=pltpu.VMEM)
    shape = jax.ShapeDtypeStruct
    others = seq_count - 1
    return pl.pallas_call(
        functools.partial(attend_kernel, sizes),
        in_specs=[pl.BlockSpec(memory_space=pltpu.SMEM)]
        + [whole] * 3
        + [pl.BlockSpec(memory_space=pl.ANY)] * 3
        + [whole] * 4,
        out_specs=[pl.BlockSpec(memory_space=pl.ANY)] * 5 + [whole] * 5,
        out_shape=[
            shape((block + GP, width), BF16),
            shape((ext, width), BF16),
            shape((ext, width), BF16),
            shape((GP, width), BF16),
            shape((GP, width), BF16),
            shape((block + quarter, width), BF16),
            shape((block, PAIR), F32),
            shape((quarter, PAIR), F32),
            shape((GP, width), BF16),
            shape((pairs, 2, WINDOW), F32),
        ],
        scratch_shapes=[
            pltpu.VMEM((WINDOW, PAIR), F32),
            pltpu.VMEM((GP, width), F32),
            pltpu.VMEM((GP, width), BF16),
            pltpu.VMEM((GP, PAIR), F32),
            pltpu.VMEM((others, quarter, width), BF16),
            pltpu.VMEM((others, quarter, PAIR), F32),
            pltpu.SemaphoreType.DMA((2, 2)),
            pltpu.SemaphoreType.DMA((2, 2)),
            pltpu.SemaphoreType.DMA((2, others)),
            pltpu.SemaphoreType.DMA((2, others)),
            pltpu.VMEM((width, width), BF16),
            pltpu.VMEM((width, width), BF16),
            pltpu.VMEM((width, width), BF16),
            pltpu.SemaphoreType.DMA((3,)),
            pltpu.VMEM((block + GP, width), BF16),
            pltpu.VMEM((ext, width), BF16),
            pltpu.VMEM((ext, width), BF16),
            pltpu.VMEM((GP, width), BF16),
            pltpu.VMEM((GP, width), BF16),
            pltpu.SemaphoreType.DMA((5,)),
        ],
        compiler_params=pltpu.CompilerParams(
            collective_id=3, has_side_effects=True, vmem_limit_bytes=56 * 2**20
        ),
        name="attend",
    )(doc_len, rel_table, long_x, glob_x, *weights)


class Reducer:
    def __init__(self, rows, split, scratch, pieces=None, order=None, parts=None):
        self.ids = mesh_ids()
        self.parts = parts
        self.order = order
        self.halves = (slice(0, split), slice(split, rows))
        held, self.from_core, self.from_one, self.from_two = scratch[:4]
        self.local, self.sends, self.recvs = scratch[4:7]
        if parts is None:
            self.from_z, self.z_sends, self.z_recvs = scratch[7:]
        self.pieces, self.held = pieces, held
        self.mine = held.at[self.ids[3]] if pieces is None else held.at[0]

    @staticmethod
    def scratch(rows, width, sides, with_z=False):
        buffers = [
            pltpu.VMEM((sides, 4, 2, 2, rows, width), BF16),
            pltpu.VMEM((4, 2, 2, rows, width), BF16),
            pltpu.VMEM((4, 2, rows, width), BF16),
            pltpu.VMEM((4, rows, width), BF16),
            pltpu.SemaphoreType.DMA((4,)),
            pltpu.SemaphoreType.DMA((5, 4)),
            pltpu.SemaphoreType.DMA((5, 4)),
        ]
        if with_z:
            buffers += [
                pltpu.VMEM((3, rows, width), BF16),
                pltpu.SemaphoreType.DMA((4,)),
                pltpu.SemaphoreType.DMA((3,)),
            ]
        return buffers

    def partners(self):
        z, y, x, core = self.ids
        dp, seq = z * 2 + y, x * 2 + core
        near = [(dp, x * 2 + 1 - core), (dp, (1 - x) * 2 + core), (z * 2 + 1 - y, seq)]
        return near + [(lax.rem(z + step, 4) * 2 + y, seq) for step in (1, 2, 3)]

    def target(self, chunk):
        return self.order(chunk) if self.order else lax.rem(self.ids[0] + 1 + chunk, 4)

    def remote(self, source, dest, kind, send_at, recv_at, device):
        return pltpu.make_async_remote_copy(
            src_ref=source,
            dst_ref=dest,
            send_sem=self.sends.at[kind, send_at],
            recv_sem=self.recvs.at[kind, recv_at],
            device_id=device,
            device_id_type=pl.DeviceIdType.MESH,
        )

    def own_copy(self, chunk):
        core, to = self.ids[3], self.target(chunk)
        return pltpu.make_async_copy(
            self.pieces.at[core, to], self.mine.at[to], self.local.at[chunk]
        )

    def core_copy(self, chunk):
        core, to = self.ids[3], self.target(chunk)
        source = (self.held if self.pieces is None else self.pieces).at[1 - core, to]
        return self.remote(source, self.from_core.at[to], 0, chunk, chunk, self.partners()[0])

    def first_copies(self, chunk):
        z, y, x, core = self.ids
        to = self.target(chunk)
        one, two = self.halves
        near = self.partners()
        return (
            self.remote(
                self.mine.at[to, :, 1 - x, one],
                self.from_one.at[to, :, one],
                1,
                chunk,
                chunk,
                near[1],
            ),
            self.remote(
                self.mine.at[to, 1 - y, :, two],
                self.from_one.at[to, :, two],
                2,
                chunk,
                chunk,
                near[2],
            ),
        )

    def second_copies(self, chunk):
        z, y, x, core = self.ids
        to = self.target(chunk)
        one, two = self.halves
        near = self.partners()
        return (
            self.remote(
                self.mine.at[to, 1 - y, x, one],
                self.from_two.at[to, one],
                3,
                chunk,
                chunk,
                near[2],
            ),
            self.remote(
                self.mine.at[to, y, 1 - x, two],
                self.from_two.at[to, two],
                4,
                chunk,
                chunk,
                near[1],
            ),
        )

    def last_copy(self, chunk):
        z, y, x, core = self.ids
        to = self.target(chunk)
        slot = lax.rem(z - to + 4, 4) - 1
        return pltpu.make_async_remote_copy(
            src_ref=self.mine.at[to, y, x],
            dst_ref=self.from_z.at[slot],
            send_sem=self.z_sends.at[chunk],
            recv_sem=self.z_recvs.at[slot],
            device_id=(to * 2 + y, x * 2 + core),
            device_id_type=pl.DeviceIdType.MESH,
        )

    def arrival(self, slot):
        z, y, x, core = self.ids
        return pltpu.make_async_remote_copy(
            src_ref=self.mine.at[z, y, x],
            dst_ref=self.from_z.at[slot],
            send_sem=self.z_sends.at[slot],
            recv_sem=self.z_recvs.at[slot],
            device_id=self.partners()[3],
            device_id_type=pl.DeviceIdType.MESH,
        )

    def leaves(self, chunk):
        return self.target(chunk) != self.ids[0]

    def fill(self, to, at, value):
        self.held[at % 2, to, at // 4, at // 2 % 2] = value.astype(BF16)

    def start(self, chunk):
        self.core_copy(chunk).start()
        if self.pieces is not None:
            self.own_copy(chunk).start()

    def add_core(self, chunk):
        to = self.target(chunk)
        if self.pieces is not None:
            self.own_copy(chunk).wait()
        self.core_copy(chunk).wait_recv()

        def add(index, carry):
            at = (to, lax.div(index, 2), lax.rem(index, 2))
            self.mine[at] = self.mine[at] + self.from_core[at]
            return carry

        lax.fori_loop(0, 4, add, 0)
        for copy in self.first_copies(chunk):
            copy.start()

    def add_first(self, chunk):
        z, y, x, core = self.ids
        one, two = self.halves
        to = self.target(chunk)
        for copy in self.first_copies(chunk):
            copy.wait_recv()

        def add(index, carry):
            for at, rows in (((to, index, x), one), ((to, y, index), two)):
                self.mine[at + (rows,)] = self.mine[at + (rows,)] + self.from_one[to, index, rows]
            return carry

        lax.fori_loop(0, 2, add, 0)
        for copy in self.second_copies(chunk):
            copy.start()

    def add_second(self, chunk):
        z, y, x, core = self.ids
        to = self.target(chunk)
        for copy in self.second_copies(chunk):
            copy.wait_recv()
        if self.parts is not None:
            self.parts[to] = self.mine[to, y, x] + self.from_two[to]
            return

        @pl.when(self.leaves(chunk))
        def _():
            self.mine[to, y, x] = self.mine[to, y, x] + self.from_two[to]
            self.last_copy(chunk).start()

    def finish(self, out=None):
        z, y, x, core = self.ids
        if self.parts is None:
            total = self.mine[z, y, x].astype(F32) + self.from_two[z].astype(F32)
            for slot in range(3):
                self.arrival(slot).wait_recv()
                total += self.from_z[slot].astype(F32)
            out[...] = total
        for chunk in range(4):
            self.core_copy(chunk).wait_send()
            for copy in self.first_copies(chunk) + self.second_copies(chunk):
                copy.wait_send()
            if self.parts is None:

                @pl.when(self.leaves(chunk))
                def _(chunk=chunk):
                    self.last_copy(chunk).wait_send()


class ZSum:
    def __init__(self, parts, scratch):
        self.ids = mesh_ids()
        self.parts = parts
        self.own, self.from_z, self.local, self.sends, self.recvs = scratch

    @staticmethod
    def scratch(rows, width):
        return [
            pltpu.VMEM((rows, width), BF16),
            pltpu.VMEM((3, rows, width), BF16),
            pltpu.SemaphoreType.DMA,
            pltpu.SemaphoreType.DMA((3,)),
            pltpu.SemaphoreType.DMA((3,)),
        ]

    def own_copy(self):
        return pltpu.make_async_copy(self.parts.at[self.ids[0]], self.own, self.local)

    def copies(self):
        z, y, x, core = self.ids
        for slot in range(3):
            to = lax.rem(z + 3 - slot, 4)
            yield pltpu.make_async_remote_copy(
                src_ref=self.parts.at[to],
                dst_ref=self.from_z.at[slot],
                send_sem=self.sends.at[slot],
                recv_sem=self.recvs.at[slot],
                device_id=(to * 2 + y, x * 2 + core),
                device_id_type=pl.DeviceIdType.MESH,
            )

    def start(self):
        self.own_copy().start()
        for copy in self.copies():
            copy.start()

    def finish(self, out):
        self.own_copy().wait()
        total = self.own[...].astype(F32)
        for slot, copy in enumerate(self.copies()):
            copy.wait_recv()
            total += self.from_z[slot].astype(F32)
        out[...] = total
        for copy in self.copies():
            copy.wait_send()


class EverySum:
    def __init__(self, scratch):
        self.kept, self.arrived, self.from_z, self.sends, self.recvs = scratch
        z, y, x, core = mesh_ids()
        seq = x * 2 + core
        self.z = z
        self.pairs = (
            (z * 2 + y, x * 2 + 1 - core),
            (z * 2 + y, (1 - x) * 2 + core),
            (z * 2 + 1 - y, seq),
        )
        self.along_z = [(lax.rem(z + step, 4) * 2 + y, seq) for step in (1, 2, 3)]

    @staticmethod
    def scratch(rows, width):
        return [
            pltpu.VMEM((3, rows, width), F32),
            pltpu.VMEM((3, rows, width), F32),
            pltpu.VMEM((4, rows, width), F32),
            pltpu.SemaphoreType.DMA((6,)),
            pltpu.SemaphoreType.DMA((6,)),
        ]

    def copy(self, stage):
        return pltpu.make_async_remote_copy(
            src_ref=self.kept.at[stage],
            dst_ref=self.arrived.at[stage],
            send_sem=self.sends.at[stage],
            recv_sem=self.recvs.at[stage],
            device_id=self.pairs[stage],
            device_id_type=pl.DeviceIdType.MESH,
        )

    def z_copies(self):
        for at, device in enumerate(self.along_z):
            yield pltpu.make_async_remote_copy(
                src_ref=self.from_z.at[self.z],
                dst_ref=self.from_z.at[self.z],
                send_sem=self.sends.at[3 + at],
                recv_sem=self.recvs.at[3 + at],
                device_id=device,
                device_id_type=pl.DeviceIdType.MESH,
            )

    def step(self, stage):
        if stage > 0:
            self.copy(stage - 1).wait_recv()
            total = self.kept[stage - 1] + self.arrived[stage - 1]
            if stage < 3:
                self.kept[stage] = total
            else:
                self.from_z[self.z] = total
        if stage < 3:
            self.copy(stage).start()
        else:
            for copy in self.z_copies():
                copy.start()

    def finish(self, out):
        for copy in self.z_copies():
            copy.wait_recv()
        out[...] = (self.from_z[0] + self.from_z[1]) + (self.from_z[2] + self.from_z[3])
        for copy in [self.copy(stage) for stage in range(3)] + list(self.z_copies()):
            copy.wait_send()


def mesh_ids():
    dp, seq = lax.axis_index("dp"), lax.axis_index("seq")
    return lax.div(dp, 2), lax.rem(dp, 2), lax.div(seq, 2), lax.rem(seq, 2)


def meet(devices):
    barrier = pltpu.get_barrier_semaphore()
    for device in devices:
        pl.semaphore_signal(barrier, inc=1, device_id=device, device_id_type=pl.DeviceIdType.MESH)
    pl.semaphore_wait(barrier, len(devices))


EARLY_PLAN = (
    (1, "add_core", 0),
    (1, "add_core", 1),
    (2, "add_core", 2),
    (2, "add_core", 3),
    (4, "add_first", 0),
    (4, "add_first", 1),
    (5, "add_first", 2),
    (5, "add_first", 3),
    (5, "add_second", 0),
    (6, "add_second", 1),
    (6, "add_second", 2),
    (6, "add_second", 3),
)


def late_kernel(
    sizes,
    planned,
    long_ref,
    glob_ref,
    dq_ref,
    dk_ref,
    dv_ref,
    dmid_far,
    wq_far,
    wk_far,
    wv_far,
    gain_ref,
    shift_ref,
    table_ref,
    *rest,
):
    block, count, quarter, seq_count, pairs = sizes
    rows = block + quarter
    width = long_ref.shape[1]
    if planned:
        early_parts, long_far, glob_out, late_ref, total_ref, scale_ref, early_ref, *rest = rest
    else:
        long_far, glob_out, gq_ref, gk_ref, gv_ref, total_ref, scale_ref, *rest = rest
    normed_t, every, gather_sends, gather_recvs, *rest = rest
    dmid_ref, wq_ref, wk_ref, wv_ref, loads, long_out, store, *rest = rest
    storing = pltpu.make_async_copy(long_out, long_far, store)
    far = (wq_far, wk_far, wv_far, dmid_far)
    loading = [
        pltpu.make_async_copy(source, dest, loads.at[at])
        for at, (source, dest) in enumerate(zip(far, (wq_ref, wk_ref, wv_ref, dmid_ref)))
    ]
    for copy in loading:
        copy.start()
    seq_index = lax.axis_index("seq")
    own_rows = pl.ds(pl.multiple_of(seq_index * quarter, quarter), quarter)
    others = [seq_device(step, seq_count) for step in range(1, seq_count)]

    def gathers():
        for step, device in enumerate(others):
            yield pltpu.make_async_remote_copy(
                src_ref=every.at[own_rows],
                dst_ref=every.at[own_rows],
                send_sem=gather_sends.at[step],
                recv_sem=gather_recvs.at[step],
                device_id=device,
                device_id_type=pl.DeviceIdType.MESH,
            )

    if planned:
        first_sum, second_sum = EverySum(rest[:5]), EverySum(rest[5:10])
        z_sum = ZSum(early_parts, rest[10:15])
        reducer = Reducer(rest[15].shape[-2], 32, rest[15:])

    meet(others + (reducer.partners()[2:] if planned else []))
    heads = 2 * pairs
    first = first_sum.kept.at[0] if planned else total_ref
    first[...] = jnp.zeros(first.shape, F32)
    for pair in range(pairs):
        first[2 * pair : 2 * pair + 2, :WINDOW] = table_ref[pair]
    for at, ref in enumerate((dq_ref, dv_ref)):
        first[heads + at : heads + at + 1] = column_sum(ref[...].astype(F32))
    if planned:
        first_sum.step(0)
        z_sum.start()
    everything = jnp.concatenate([long_ref[...], glob_ref[own_rows]], 0).astype(F32)
    hat, inverse = row_norm(everything)
    normed_t[...] = (hat * gain_ref[...] + shift_ref[...]).astype(BF16).T
    if planned:
        piece = width // 32
        blank = jnp.zeros((8, width), F32)
        def weight_rows(chunk):
            to = reducer.target(chunk)
            some = normed_t[pl.ds(pl.multiple_of(to * 8 * piece, 64), 8 * piece)]
            parts = [dot_n(some, ref[...]) for ref in (dq_ref, dk_ref, dv_ref)]
            for at in range(8):
                rows_at = slice(at * piece, (at + 1) * piece)
                reducer.fill(
                    to, at, jnp.concatenate([part[rows_at] for part in parts] + [blank], 0)
                )
            reducer.start(chunk)

        weight_rows(0)
        first_sum.step(1)
        weight_rows(1)
        first_sum.step(2)
        reducer.add_core(0)
        weight_rows(2)
        first_sum.step(3)
        reducer.add_core(1)
        weight_rows(3)
        for copy in loading:
            copy.wait()
        grads = dot_t(dq_ref[...], wq_ref[...])
        grads += dot_t(dk_ref[...], wk_ref[...]) + dot_t(dv_ref[...], wv_ref[...])
        reducer.add_first(0)
        reducer.add_core(2)
    else:
        for ref, out in ((dq_ref, gq_ref), (dk_ref, gk_ref), (dv_ref, gv_ref)):
            out[...] = dot_n(normed_t[...], ref[...]).astype(BF16)
        for copy in loading:
            copy.wait()
        grads = (
            dot_t(dq_ref[...], wq_ref[...])
            + dot_t(dk_ref[...], wk_ref[...])
            + dot_t(dv_ref[...], wv_ref[...])
        )
    scaled = grads * gain_ref[...]
    total = dmid_ref[...] + inverse * (
        scaled
        - jnp.mean(scaled, -1, keepdims=True)
        - hat * jnp.mean(scaled * hat, -1, keepdims=True)
    )
    every[own_rows] = total[block:].astype(BF16)
    for copy in gathers():
        copy.start()
    long_out[...] = total[:block]
    storing.start()
    second = second_sum.kept.at[0] if planned else scale_ref
    second[...] = jnp.zeros(second.shape, F32)
    second[0:1] = column_sum(grads * hat)
    second[1:2] = column_sum(grads)
    if planned:
        second_sum.step(0)
        reducer.add_first(1)
        second_sum.step(1)
        reducer.add_core(3)
        reducer.add_second(0)
        reducer.add_first(2)
        second_sum.step(2)
        reducer.add_second(1)
        reducer.add_first(3)
        second_sum.step(3)
        reducer.add_second(2)
        reducer.add_second(3)
        first_sum.finish(total_ref)
        z_sum.finish(early_ref)
        reducer.finish(late_ref)
        second_sum.finish(scale_ref)
    for copy in gathers():
        copy.wait_recv()
    glob_out[...] = every[:count].astype(F32)
    storing.wait()
    for copy in gathers():
        copy.wait_send()


def last_part(sizes, planned, long_x, glob_x, dq, dk, dv, dmid, *weights):
    block, count, quarter, seq_count, pairs = sizes
    rows, width = dq.shape
    others = seq_count - 1
    whole = pl.BlockSpec(memory_space=pltpu.VMEM)
    there = pl.BlockSpec(memory_space=pl.ANY)
    shape = jax.ShapeDtypeStruct
    sums = [shape(((2 * pairs + 2 + 7) // 8 * 8, width), F32), shape((8, width), F32)]
    outs = [shape((block, width), F32), shape((count, width), F32)]
    scratch = [
        pltpu.VMEM((width, rows), BF16),
        pltpu.VMEM((GP, width), BF16),
        pltpu.SemaphoreType.DMA((others,)),
        pltpu.SemaphoreType.DMA((others,)),
        pltpu.VMEM((rows, width), F32),
        pltpu.VMEM((width, width), BF16),
        pltpu.VMEM((width, width), BF16),
        pltpu.VMEM((width, width), BF16),
        pltpu.SemaphoreType.DMA((4,)),
        pltpu.VMEM((block, width), F32),
        pltpu.SemaphoreType.DMA,
    ]
    if planned:
        piece = width // 32
        part = 3 * piece + 8
        early = weights[-1].shape[1:]
        outs += [shape((part, width), F32), *sums, shape(early, F32)]
        for part_sums in sums:
            scratch += EverySum.scratch(*part_sums.shape)
        scratch += ZSum.scratch(*early) + Reducer.scratch(part, width, 2, with_z=True)
    else:
        outs += [shape((width, width), BF16)] * 3 + sums
    return pl.pallas_call(
        functools.partial(late_kernel, sizes, planned),
        in_specs=[whole] * 5 + [there] * 4 + [whole] * 3 + [there] * planned,
        out_specs=[there] + [whole] * (len(outs) - 1),
        out_shape=outs,
        scratch_shapes=scratch,
        compiler_params=pltpu.CompilerParams(
            collective_id=2, has_side_effects=True, vmem_limit_bytes=60 * 2**20
        ),
        name="last_part",
    )(long_x, glob_x, dq, dk, dv, dmid, *weights)


def small_kernel(heads, early_ref, late_ref, outer_ref, inner_ref, sums_ref, scale_ref, *rest):
    outs = rest[4:-4]
    for source, out in zip(rest[:3], rest[-4:]):
        out[...] = source[...]
    rest[-1][...] = rest[3][...].reshape(rest[-1].shape)
    g_query, g_key, g_value, g_out, g_inner, g_outer, *vectors, table = outs
    device = lax.axis_index("dp") * lax.axis_size("seq") + lax.axis_index("seq")
    piece, width = g_query.shape
    for at, out in enumerate((g_query, g_key, g_value)):
        out[...] = late_ref[at * piece : (at + 1) * piece]
    g_out[...] = early_ref[2 * piece : 3 * piece]
    g_outer[...] = outer_ref[...]
    for source, first, chunk in (
        (inner_ref, 0, 0),
        (inner_ref, piece, 3),
        (early_ref, 0, 1),
        (early_ref, piece, 2),
    ):
        g_inner[:, chunk * width : (chunk + 1) * width] = source[first : first + piece]

    def entries(row, at, length):
        return pltpu.roll(row, width - at * length, 1)[0, :length]

    b_query, b_value, b_out, b_outer, gain_one, shift_one, gain_two, shift_two, b_inner = vectors
    for at, out in enumerate((b_query, b_value)):
        out[...] = entries(sums_ref[heads + at : heads + at + 1], device, piece)
    for at, out in enumerate((gain_one, shift_one)):
        out[...] = entries(scale_ref[at : at + 1], device, piece)
    for at, out in enumerate((b_out, b_outer, gain_two, shift_two)):
        row = 3 * piece + at
        out[...] = entries(early_ref[row : row + 1], device, piece)
    row = pl.ds(3 * piece + 4 + lax.div(device, 8), 1)
    b_inner[...] = entries(early_ref[row], lax.rem(device, 8), 4 * piece)
    labels = table.shape[1]
    turned = pltpu.roll(sums_ref[:, :WINDOW], WINDOW - HALO + R, 1)
    table[...] = turned[:heads, :labels]


def small_results(heads, early, late, outer, inner, sums, scales, *big):
    width = early.shape[1]
    piece = width // 32
    shape = jax.ShapeDtypeStruct
    whole = pl.BlockSpec(memory_space=pltpu.VMEM)
    outs = [shape((piece, width), F32)] * 4
    outs += [shape((piece, 4 * width), F32), shape((4 * piece, width), F32)]
    outs += [shape((piece,), F32)] * 8 + [shape((4 * piece,), F32)]
    outs += [shape((heads, 2 * R + 1), F32)]
    outs += [shape(part.shape, part.dtype) for part in big[:3]]
    outs.append(shape((big[3].shape[0], 1, width), F32))
    return pl.pallas_call(
        functools.partial(small_kernel, heads),
        in_specs=[whole] * 10,
        out_specs=[whole] * len(outs),
        out_shape=outs,
        name="small_results",
    )(early, late, outer, inner, sums, scales, *big)


def has_plan():
    return (lax.axis_size("dp"), lax.axis_size("seq")) == (8, 4)


GELU_A = 0.7978845608028654
GELU_B = 0.044715


def gate_both(u):
    square = u * u
    turned = jnp.tanh(GELU_A * u * (1.0 + GELU_B * square))
    half = 0.5 * (1.0 + turned)
    slope = half + 0.5 * u * (1.0 - turned * turned) * (
        GELU_A * (1.0 + 3.0 * GELU_B * square)
    )
    return u * half, slope


def column_sum(rows):
    return jnp.sum(rows, 0, keepdims=True)


def ffn_kernel(
    sizes,
    planned,
    len_ref,
    attn_ref,
    long_ref,
    glob_ref,
    dlong_ref,
    dglob_ref,
    lq_ref,
    wo_ref,
    bo_ref,
    gain_ref,
    shift_ref,
    wi_ref,
    bi_ref,
    wr_ref,
    br_ref,
    long_out,
    glob_out,
    dmid_far,
    do_far,
    dog_ref,
    ldg_ref,
    *rest,
):
    block, count, quarter, seq_count, pairs = sizes
    if planned:
        pieces_far, outer_ref, inner_ref, *rest = rest
    else:
        g_outer_ref, g_inner_ref, g_out_ref, vec_ref, *rest = rest
    (
        mid,
        y_sum,
        df_sum,
        normed,
        normed_t,
        dy,
        vectors,
        biases,
        every_do,
        every_ld,
        gather_sends,
        gather_recvs,
        dmid_ref,
        do_ref,
        stores,
        *rest,
    ) = rest
    storing = [
        pltpu.make_async_copy(dmid_ref, dmid_far, stores.at[0]),
        pltpu.make_async_copy(do_ref, do_far, stores.at[1]),
    ]
    if planned:
        even, pieces_ref, *rest = rest
        outer = Reducer(rest[0].shape[-2], 48, rest[:7], order=chunk_of, parts=outer_ref)
        inner = Reducer(rest[7].shape[-2], 16, rest[7:], parts=inner_ref)
    step = pl.program_id(0)
    chunk = chunk_of(step)
    seq_index = lax.axis_index("seq")
    own_rows = pl.ds(pl.multiple_of(seq_index * quarter, quarter), quarter)
    width = mid.shape[1]
    piece = width // 32

    def rows_of(device):
        return pl.ds(pl.multiple_of(device[1] * quarter, quarter), quarter)

    def gather(owner, device, at):
        for kind, every in enumerate((every_do, every_ld)):
            yield pltpu.make_async_remote_copy(
                src_ref=every.at[rows_of(owner)],
                dst_ref=every.at[rows_of(owner)],
                send_sem=gather_sends.at[kind, at],
                recv_sem=gather_recvs.at[kind, at],
                device_id=device,
                device_id_type=pl.DeviceIdType.MESH,
            )

    me = seq_device(0, seq_count)
    if planned:
        sibling, across = outer.partners()[:2]
        first_gathers = [(me, across, 0), (me, sibling, 1)]
        second_gathers = [(across, sibling, 2)]
    else:
        first_gathers = [
            (me, seq_device(at + 1, seq_count), at) for at in range(seq_count - 1)
        ]
        second_gathers = []

    def store_pieces(half):
        rows = (slice(0, 2 * piece), slice(2 * piece, 3 * piece + 8))[half]
        return pltpu.make_async_copy(
            pieces_ref.at[:, :, :, :, rows], pieces_far.at[:, :, :, :, rows], stores.at[2 + half]
        )

    def act(now):
        if planned:
            for at, reducer, name, part in FFN_PLAN:
                if at == now:
                    getattr((outer, inner)[reducer], name)(part)

    def act_in_step(point):
        if planned:
            for now in range(4):
                if any(at == (now, point) for at, _, _, _ in FFN_PLAN):

                    @pl.when(step == now)
                    def _(now=now):
                        act((now, point))

    @pl.when(step == 0)
    def _():
        others = [seq_device(seq_step, seq_count) for seq_step in range(1, seq_count)]
        meet(others + (outer.partners()[2:] if planned else []))
        projected = dot_n(attn_ref[...], wo_ref[...]) + bo_ref[...]
        mid[:block] = long_ref[...].astype(F32) + projected[:block]
        mid[block:] = glob_ref[own_rows].astype(F32) + projected[block:]
        hat, _ = row_norm(mid[...])
        normed[...] = (hat * gain_ref[...] + shift_ref[...]).astype(BF16)
        normed_t[...] = normed[...].T
        position = seq_index * block + lax.broadcasted_iota(jnp.int32, (block, 1), 0)
        dy[:block] = jnp.where(
            position < len_ref[0], dlong_ref[...].astype(F32), 0.0
        ).astype(BF16)
        y_sum[:GP] = jnp.zeros((GP, width), F32)
        y_sum[:count] = dglob_ref[...].astype(F32)
        dy[block:] = y_sum[own_rows].astype(BF16)
        vectors[1:2] = column_sum(dy[...].astype(F32))
        y_sum[...] = mid[...] + br_ref[...]
        df_sum[...] = jnp.zeros_like(df_sum)
        for at in range(4):
            biases[at] = bi_ref[at * width : (at + 1) * width].reshape(1, width)

    act_in_step(0)
    active, slope = gate_both(dot_n(normed[...], wi_ref[...]) + biases[chunk])
    active = active.astype(BF16)
    g_outer = t_dot(active, dy[...])
    if planned:
        for at in range(8):
            outer.fill(chunk, at, g_outer[at * 4 * piece : (at + 1) * 4 * piece])
        outer.start(step)
    else:
        g_outer_ref[...] = g_outer.astype(BF16)
    y_sum[...] += dot_n(active, wr_ref[...])
    hidden = dot_t(dy[...], wr_ref[...]) * slope
    for at in range(4):

        @pl.when(chunk == at)
        def _(at=at):
            vectors[4 + at : 5 + at] = column_sum(hidden)

    hidden = hidden.astype(BF16)
    act_in_step(1)
    df_sum[...] += dot_t(hidden, wi_ref[...])
    g_inner = dot_n(normed_t[...], hidden)
    if planned:

        @pl.when(lax.rem(step, 2) == 0)
        def _():
            even[...] = g_inner

        def halves(at):
            part = slice(at * piece, (at + 1) * piece)
            return jnp.concatenate([even[part], g_inner[part]], 0)

        @pl.when(step == 1)
        def _():
            for at in range(32):
                inner.fill(at // 8, at % 8, halves(at))
            for part in range(4):
                inner.start(part)

        @pl.when(step == 3)
        def _():
            for at in range(32):
                pieces_ref[at % 2, at // 8, at // 4 % 2, at // 2 % 2, : 2 * piece] = halves(
                    at
                ).astype(BF16)
            store_pieces(0).start()

    else:
        g_inner_ref[...] = g_inner.astype(BF16)

    def norm_back(rows):
        hat, inverse = row_norm(mid[rows])
        df = df_sum[rows]
        scaled = df * gain_ref[...]
        dmid = dy[rows].astype(F32) + inverse * (
            scaled
            - jnp.mean(scaled, -1, keepdims=True)
            - hat * jnp.mean(scaled * hat, -1, keepdims=True)
        )
        dmid_ref[rows] = dmid
        low = dmid.astype(BF16)
        grad_o = dot_t(low, wo_ref[...]).astype(BF16)
        do_ref[rows] = grad_o
        return [column_sum(dmid), column_sum(df * hat), column_sum(df)], low, grad_o

    @pl.when(step == 3)
    def _():
        glob_sums, glob_low, grad_o = norm_back(slice(block, block + quarter))
        every_do[own_rows] = grad_o
        both = grad_o.astype(F32) * attn_ref[block:].astype(F32)
        stats = lq_ref[...]
        for head in range(2 * pairs):
            lanes = slice(head // 2 * PAIR, head // 2 * PAIR + PAIR)
            delta = jnp.sum(own_half(head % 2, both[:, lanes]), -1, keepdims=True)
            stats = jnp.where(lane_index() == HD + head, delta, stats)
        every_ld[own_rows] = stats
        for part in first_gathers:
            for copy in gather(*part):
                copy.start()
        glob_out[...] = y_sum[block:].astype(BF16)
        act((4, 0))
        position = seq_index * block + lax.broadcasted_iota(jnp.int32, (block, 1), 0)
        long_out[...] = jnp.where(position < len_ref[0], y_sum[:block], 0.0).astype(BF16)
        long_sums, long_low, _ = norm_back(slice(0, block))
        for at, one, two in zip((0, 2, 3), long_sums, glob_sums):
            vectors[at : at + 1] = one + two
        for copy in storing:
            copy.start()
        if planned:
            for copy in gather(*first_gathers[0]):
                copy.wait_recv()
            for copy in gather(*second_gathers[0]):
                copy.start()
        act((4, 1))
        g_out = t_dot(attn_ref[...], jnp.concatenate([long_low, glob_low], 0))
        if planned:
            for at in range(32):
                pieces_ref[at % 2, at // 8, at // 4 % 2, at // 2 % 2, 2 * piece :] = (
                    jnp.concatenate(
                        [g_out[at * piece : (at + 1) * piece], vectors[...]], 0
                    ).astype(BF16)
                )
            store_pieces(1).start()
            act((4, 2))
            outer.finish()
            inner.finish()
            for half in range(2):
                store_pieces(half).wait()
        else:
            g_out_ref[...] = g_out.astype(BF16)
            vec_ref[...] = vectors[...]
        for part in (first_gathers[1:] if planned else first_gathers) + second_gathers:
            for copy in gather(*part):
                copy.wait_recv()
        for copy in storing:
            copy.wait()
        dog_ref[...] = every_do[...]
        ldg_ref[...] = every_ld[...]
        for part in first_gathers + second_gathers:
            for copy in gather(*part):
                copy.wait_send()


OUTER, INNER = 0, 1
FFN_PLAN = (
    ((1, 0), OUTER, "add_core", 0),
    ((2, 0), OUTER, "add_core", 1),
    ((2, 0), OUTER, "add_first", 0),
    ((2, 1), INNER, "add_core", 0),
    ((2, 1), INNER, "add_core", 1),
    ((2, 1), INNER, "add_core", 2),
    ((2, 1), INNER, "add_core", 3),
    ((3, 0), OUTER, "add_first", 1),
    ((3, 0), OUTER, "add_second", 0),
    ((3, 0), OUTER, "add_core", 2),
    ((3, 1), OUTER, "add_core", 3),
    ((4, 0), INNER, "add_first", 0),
    ((4, 0), INNER, "add_first", 1),
    ((4, 0), OUTER, "add_first", 2),
    ((4, 0), OUTER, "add_second", 1),
    ((4, 1), INNER, "add_first", 2),
    ((4, 1), INNER, "add_first", 3),
    ((4, 1), INNER, "add_second", 0),
    ((4, 1), INNER, "add_second", 1),
    ((4, 2), OUTER, "add_first", 3),
    ((4, 2), OUTER, "add_second", 2),
    ((4, 2), INNER, "add_second", 2),
    ((4, 2), INNER, "add_second", 3),
    ((4, 2), OUTER, "add_second", 3),
)


def chunk_of(step):
    return jnp.where(step == 0, 0, jnp.where(step == 1, 3, step - 1))


def feed_forward(sizes, planned, doc_len, attn, long_x, glob_x, dlong, dglob, lq, *weights):
    block, count, quarter, seq_count, pairs = sizes
    wo, bo, gain, shift, wi, bi, wr, br = weights
    width, hidden = wi.shape
    chunk = hidden // 4
    rows = block + quarter
    whole = pl.BlockSpec(memory_space=pltpu.VMEM)
    shape = jax.ShapeDtypeStruct
    in_specs = [pl.BlockSpec(memory_space=pltpu.SMEM)] + [whole] * 10
    in_specs += [
        pl.BlockSpec((width, chunk), lambda c: (0, chunk_of(c))),
        whole,
        pl.BlockSpec((chunk, width), lambda c: (chunk_of(c), 0)),
        whole,
    ]
    outs = [
        shape((block, width), BF16),
        shape((quarter, width), BF16),
        shape((rows, width), F32),
        shape((rows, width), BF16),
        shape((GP, width), BF16),
        shape((GP, PAIR), F32),
    ]
    there = pl.BlockSpec(memory_space=pl.ANY)
    out_specs = [whole] * 2 + [there] * 2 + [whole] * 2
    others = seq_count - 1
    scratch = [
        pltpu.VMEM((rows, width), F32),
        pltpu.VMEM((rows, width), F32),
        pltpu.VMEM((rows, width), F32),
        pltpu.VMEM((rows, width), BF16),
        pltpu.VMEM((width, rows), BF16),
        pltpu.VMEM((rows, width), BF16),
        pltpu.VMEM((8, width), F32),
        pltpu.VMEM((4, 1, chunk), F32),
        pltpu.VMEM((GP, width), BF16),
        pltpu.VMEM((GP, PAIR), F32),
        pltpu.SemaphoreType.DMA((2, others)),
        pltpu.SemaphoreType.DMA((2, others)),
        pltpu.VMEM((rows, width), F32),
        pltpu.VMEM((rows, width), BF16),
        pltpu.SemaphoreType.DMA((4,)),
    ]
    if planned:
        part, piece = hidden // 32, width // 32
        outs += [
            shape((2, 4, 2, 2, 3 * piece + 8, width), BF16),
            shape((4, part, width), BF16),
            shape((4, 2 * piece, width), BF16),
        ]
        out_specs += [there] + [whole] * 2
        scratch += [
            pltpu.VMEM((width, chunk), F32),
            pltpu.VMEM(outs[-3].shape, BF16),
        ]
        scratch += Reducer.scratch(part, width, 2) + Reducer.scratch(2 * piece, width, 2)
    else:
        outs += [
            shape((hidden, width), BF16),
            shape((width, hidden), BF16),
            shape((width, width), BF16),
            shape((8, width), F32),
        ]
        out_specs += [
            pl.BlockSpec((chunk, width), lambda c: (chunk_of(c), 0)),
            pl.BlockSpec((width, chunk), lambda c: (0, chunk_of(c))),
            whole,
            whole,
        ]
    return pl.pallas_call(
        functools.partial(ffn_kernel, sizes, planned),
        grid=(4,),
        in_specs=in_specs,
        out_specs=out_specs,
        out_shape=outs,
        scratch_shapes=scratch,
        compiler_params=pltpu.CompilerParams(
            collective_id=4, has_side_effects=True, vmem_limit_bytes=62 * 2**20
        ),
        name="feed_forward",
    )(doc_len, attn, long_x, glob_x, dlong, dglob, lq, wo, bo, gain, shift, wi, bi, wr, br)


def back_kernel(
    sizes,
    early_rows,
    len_ref,
    tab_ref,
    q_ref,
    kx_ref,
    vx_ref,
    kg_ref,
    vg_ref,
    o_ref,
    do_ref,
    l_ref,
    dog_ref,
    ldg_ref,
    yq_ref,
    *rest,
):
    block, count, quarter, seq_count, pairs = sizes
    reduces = early_rows > 0
    if reduces:
        pieces_ref, outer_parts, inner_parts, *rest = rest
    dq_ref, dk_ref, dv_ref, dtab_ref, glob_out, *rest = rest
    if reduces:
        early_parts, outer_ref, inner_ref, *rest = rest
    (
        dkx,
        dvx,
        dkg,
        dvg,
        q_send,
        q_recv,
        kv_send,
        kv_recv,
        halo_send,
        halo_recv,
        glob_sends,
        glob_recvs,
        halo_sends,
        halo_recvs,
        every,
        gather_sends,
        gather_recvs,
        *rest,
    ) = rest
    number = pl.program_id(0)
    steps = pairs // 2
    first_pair = 2 * lax.rem(number, steps)
    seq_index = lax.axis_index("seq")
    if reduces:
        reducer = Reducer(early_rows, 16, rest[:7], pieces=pieces_ref, parts=early_parts)
        z_sums = (
            (ZSum(outer_parts, rest[7:12]), outer_ref),
            (ZSum(inner_parts, rest[12:]), inner_ref),
        )
    scale = HD ** (-0.5)
    low_lanes = lane_index() < HD
    own_keys = slice(HALO, HALO + block)
    own_rows = pl.ds(pl.multiple_of(seq_index * quarter, quarter), quarter)

    def glob_copies(kind, at):
        source, dest = ((q_send, q_recv), (kv_send, kv_recv))[kind]
        for step in range(1, seq_count):
            device = seq_device(step, seq_count)
            yield pltpu.make_async_remote_copy(
                src_ref=source.at[device[1], at],
                dst_ref=dest.at[step - 1, at],
                send_sem=glob_sends.at[kind, step - 1, at],
                recv_sem=glob_recvs.at[kind, step - 1, at],
                device_id=device,
                device_id_type=pl.DeviceIdType.MESH,
            )

    def gathers():
        for step in range(1, seq_count):
            yield pltpu.make_async_remote_copy(
                src_ref=every.at[own_rows],
                dst_ref=every.at[own_rows],
                send_sem=gather_sends.at[step - 1],
                recv_sem=gather_recvs.at[step - 1],
                device_id=seq_device(step, seq_count),
                device_id_type=pl.DeviceIdType.MESH,
            )

    def halo_copy(direction, at):
        return pltpu.make_async_remote_copy(
            src_ref=halo_send.at[direction, at],
            dst_ref=halo_recv.at[direction, at],
            send_sem=halo_sends.at[direction, at],
            recv_sem=halo_recvs.at[direction, at],
            device_id=seq_device(2 * direction - 1, seq_count),
            device_id_type=pl.DeviceIdType.MESH,
        )

    has_low, has_high = seq_index > 0, seq_index < seq_count - 1
    sends_to = (has_low, has_high)
    gets_from = (has_high, has_low)

    def close_pair(at):
        lanes = lanes_of(at)
        for direction in range(2):

            @pl.when(gets_from[direction])
            def _(direction=direction):
                halo_copy(direction, at).wait_recv()

        for kind, (total, out) in enumerate(((dkx, dk_ref), (dvx, dv_ref))):
            first, last = HALO + REACH, HALO + block - REACH
            out[:REACH, lanes] = (
                total[at, HALO:first] + halo_recv[1, at, kind].astype(F32)
            ).astype(BF16)
            out[REACH : block - REACH, lanes] = total[at, first:last].astype(BF16)
            out[block - REACH : block, lanes] = (
                total[at, last : HALO + block] + halo_recv[0, at, kind].astype(F32)
            ).astype(BF16)
        sums = []
        for kind, (source, dest) in enumerate(((q_send, q_recv), (kv_send, kv_recv))):
            total = source[seq_index, at].astype(F32)
            for step, copy in enumerate(glob_copies(kind, at)):
                copy.wait_recv()
                total += dest[step, at].astype(F32)
            sums.append(total.astype(BF16))
        dq_ref[block:, lanes] = sums[0]
        dk_ref[block:, lanes] = sums[1][:, :PAIR]
        dv_ref[block:, lanes] = sums[1][:, PAIR:]

    def run_plan(now):
        for at, act, chunk in EARLY_PLAN:
            if now == at:
                getattr(reducer, act)(chunk)

    @pl.when(number == 0)
    def _():
        others = [seq_device(step, seq_count) for step in range(1, seq_count)]
        meet(others + (reducer.partners()[2:] if reduces else []))
        if reduces:
            for chunk in range(4):
                reducer.start(chunk)
            for z_sum, _ in z_sums:
                z_sum.start()
        every[own_rows] = yq_ref[...]
        for copy in gathers():
            copy.start()
        for direction in range(2):

            @pl.when(jnp.logical_not(gets_from[direction]))
            def _(direction=direction):
                halo_recv[direction] = jnp.zeros_like(halo_recv[direction])

    if reduces:
        for now in range(1, 2 * steps):
            if any(at == now for at, _, _ in EARLY_PLAN):

                @pl.when(number == now)
                def _(now=now):
                    run_plan(now)

    def glob_pair(pair, q_ref, kx_ref, vx_ref, kg_ref, vg_ref, dog_ref):
        long_bias = key_bias(seq_index * block, block, len_ref[0])
        near_bias = key_bias(seq_index * quarter, quarter, count)
        query = q_ref[block:] * jnp.asarray(scale, BF16)
        grad_o = dog_ref[...]
        far_k, far_v = kx_ref[own_keys], vx_ref[own_keys]
        near_k, near_v = kg_ref[own_rows], vg_ref[own_rows]
        outs, kept = [], []
        for head in range(2):
            norm = in_three(-pick_column(ldg_ref[...], 2 * pair + head))
            delta = in_three(-pick_column(ldg_ref[...], HD + 2 * pair + head))
            qa = with_lanes(head, query, (1.0,) + norm)
            doa = with_lanes(head, grad_o, delta)
            far = jnp.exp(dot_t(qa, key_side(head, far_k, long_bias)))
            near = jnp.exp(dot_t(qa, key_side(head, near_k, near_bias)))
            far_ds = (far * dot_t(doa, value_side(head, far_v))).astype(BF16)
            near_ds = (near * dot_t(doa, value_side(head, near_v))).astype(BF16)
            outs.append(dot_n(far_ds, far_k) + dot_n(near_ds, near_k))
            kept.append(
                (
                    own_half(head, query),
                    own_half(head, grad_o),
                    far.astype(BF16),
                    near.astype(BF16),
                    far_ds,
                    near_ds,
                )
            )
        own_q, own_do, far, near, far_ds, near_ds = (
            jnp.concatenate(part, 0) for part in zip(*kept)
        )
        for total, edge in ((dkx, own_keys), (dvx, own_keys)):
            total[pair, :HALO] = jnp.zeros((HALO, PAIR), F32)
            total[pair, HALO + block :] = jnp.zeros((HALO, PAIR), F32)
        dkx[pair, own_keys] = t_dot(far_ds, own_q)
        dvx[pair, own_keys] = t_dot(far, own_do)
        dkg[pair] = jnp.zeros((GP, PAIR), F32)
        dvg[pair] = jnp.zeros((GP, PAIR), F32)
        dkg[pair, own_rows] = t_dot(near_ds, own_q)
        dvg[pair, own_rows] = t_dot(near, own_do)
        glob_dq = (jnp.where(low_lanes, outs[0], outs[1]) * scale).astype(BF16)
        q_send[:, pair] = glob_dq.reshape(seq_count, quarter, PAIR)
        for copy in glob_copies(0, pair):
            copy.start()

    def long_pair(pair, q_ref, kx_ref, vx_ref, kg_ref, vg_ref, o_ref, do_ref, tab_ref):
        long_bias = key_bias(seq_index * block - HALO, block + 2 * HALO, len_ref[0])
        glob_bias = key_bias(0, GP, count)
        query = q_ref[:block] * jnp.asarray(scale, BF16)
        grad_o = do_ref[...]
        both = grad_o.astype(F32) * o_ref[...].astype(F32)
        heads = []
        for head in range(2):
            norm = in_three(-pick_column(l_ref[...], 2 * pair + head))
            delta = in_three(-jnp.sum(own_half(head, both), -1, keepdims=True))
            heads.append(
                dict(
                    q=own_half(head, query),
                    do=own_half(head, grad_o),
                    qa=with_lanes(head, query, (1.0,) + norm),
                    doa=with_lanes(head, grad_o, delta),
                    kxa=key_side(head, kx_ref[...], long_bias),
                    vxa=value_side(head, vx_ref[...]),
                    kga=key_side(head, kg_ref[...], glob_bias),
                    vga=value_side(head, vg_ref[...]),
                    bias=band_bias(tab_ref[0, head : head + 1]),
                )
            )
        table_sums = [0.0, 0.0]
        grads_q = []
        for start in range(0, block, SUB):
            rows, keys = slice(start, start + SUB), slice(start, start + WINDOW)
            outs, probs, grads = [], [], []
            for head, own in enumerate(heads):
                band = jnp.exp(dot_t(own["qa"][rows], own["kxa"][keys]) + own["bias"])
                band_ds = band * dot_t(own["doa"][rows], own["vxa"][keys])
                table_sums[head] += band_ds
                glob = jnp.exp(dot_t(own["qa"][rows], own["kga"]))
                glob_ds = (glob * dot_t(own["doa"][rows], own["vga"])).astype(BF16)
                band_ds = band_ds.astype(BF16)
                outs.append(dot_n(band_ds, kx_ref[keys]) + dot_n(glob_ds, kg_ref[...]))
                probs.append((band.astype(BF16), glob.astype(BF16)))
                grads.append((band_ds, glob_ds))
            grads_q.append(jnp.where(low_lanes, outs[0], outs[1]))
            own_q = jnp.concatenate([own["q"][rows] for own in heads], 0)
            own_do = jnp.concatenate([own["do"][rows] for own in heads], 0)
            band, glob = (jnp.concatenate(part, 0) for part in zip(*probs))
            band_ds, glob_ds = (jnp.concatenate(part, 0) for part in zip(*grads))
            dkx[pair, keys] += t_dot(band_ds, own_q)
            dvx[pair, keys] += t_dot(band, own_do)
            dkg[pair] += t_dot(glob_ds, own_q)
            dvg[pair] += t_dot(glob, own_do)
        for kind, total in enumerate((dkg, dvg)):
            kv_send[:, pair, :, kind * PAIR : (kind + 1) * PAIR] = (
                total[pair].astype(BF16).reshape(seq_count, quarter, PAIR)
            )
        for copy in glob_copies(1, pair):
            copy.start()
        for kind, total in enumerate((dkx, dvx)):
            for direction, first in enumerate((HALO - REACH, HALO + block)):
                halo_send[direction, pair, kind] = total[pair, first : first + REACH].astype(BF16)
        for direction in range(2):

            @pl.when(sends_to[direction])
            def _(direction=direction):
                halo_copy(direction, pair).start()

        dq_ref[:block, lanes_of(pair)] = (jnp.concatenate(grads_q, 0) * scale).astype(BF16)
        for head in range(2):
            dtab_ref[pair, head : head + 1] = diagonal_sums(table_sums[head])

    def part(at, *refs):
        return [ref.at[:, at * PAIR : (at + 1) * PAIR] for ref in refs]

    @pl.when(number < steps)
    def _():
        for at in range(2):
            glob_pair(
                first_pair + at, *part(at, q_ref, kx_ref, vx_ref, kg_ref, vg_ref, dog_ref)
            )

    @pl.when(number >= steps)
    def _():
        for at in range(2):
            long_pair(
                first_pair + at,
                *part(at, q_ref, kx_ref, vx_ref, kg_ref, vg_ref, o_ref, do_ref),
                tab_ref.at[at : at + 1],
            )

    @pl.when(number > steps)
    def _():
        close_pair(first_pair - 2)
        close_pair(first_pair - 1)

    @pl.when(number == 2 * steps - 1)
    def _():
        if reduces:
            run_plan(2 * steps)
        close_pair(pairs - 2)
        close_pair(pairs - 1)
        for at in range(pairs):
            for kind in range(2):
                for copy in glob_copies(kind, at):
                    copy.wait_send()
            for direction in range(2):

                @pl.when(sends_to[direction])
                def _(direction=direction, at=at):
                    halo_copy(direction, at).wait_send()

        for copy in gathers():
            copy.wait_recv()
        glob_out[...] = every[:count]
        for copy in gathers():
            copy.wait_send()
        if reduces:
            reducer.finish()
            for z_sum, out in z_sums:
                z_sum.finish(out)


def attend_back(sizes, doc_len, table, q, kx, vx, kg, vg, o, do, l, dog, ldg, yq, *sums):
    block, count, quarter, seq_count, pairs = sizes
    width = q.shape[1]
    early_rows = sums[0].shape[-2] if sums else 0
    ext = block + 2 * HALO
    steps = pairs // 2
    cols = lambda rows: pl.BlockSpec((rows, 2 * PAIR), lambda i: (0, lax.rem(i, steps)))
    whole = pl.BlockSpec(memory_space=pltpu.VMEM)
    shape = jax.ShapeDtypeStruct
    in_specs = [
        pl.BlockSpec(memory_space=pltpu.SMEM),
        pl.BlockSpec((2, 2, WINDOW), lambda i: (lax.rem(i, steps), 0, 0)),
        cols(block + GP),
        cols(ext),
        cols(ext),
        cols(GP),
        cols(GP),
        cols(block),
        cols(block),
        whole,
        cols(GP),
        whole,
        whole,
    ]
    rows = block + quarter
    outs = [shape((rows, width), BF16)] * 3 + [shape((pairs, 2, WINDOW), F32)]
    outs.append(shape((count, width), BF16))
    others = seq_count - 1
    scratch = [
        pltpu.VMEM((pairs, ext, PAIR), F32),
        pltpu.VMEM((pairs, ext, PAIR), F32),
        pltpu.VMEM((pairs, GP, PAIR), F32),
        pltpu.VMEM((pairs, GP, PAIR), F32),
        pltpu.VMEM((seq_count, pairs, quarter, PAIR), BF16),
        pltpu.VMEM((others, pairs, quarter, PAIR), BF16),
        pltpu.VMEM((seq_count, pairs, quarter, 2 * PAIR), BF16),
        pltpu.VMEM((others, pairs, quarter, 2 * PAIR), BF16),
        pltpu.VMEM((2, pairs, 2, REACH, PAIR), BF16),
        pltpu.VMEM((2, pairs, 2, REACH, PAIR), BF16),
        pltpu.SemaphoreType.DMA((2, others, pairs)),
        pltpu.SemaphoreType.DMA((2, others, pairs)),
        pltpu.SemaphoreType.DMA((2, pairs)),
        pltpu.SemaphoreType.DMA((2, pairs)),
        pltpu.VMEM((GP, width), BF16),
        pltpu.SemaphoreType.DMA((others,)),
        pltpu.SemaphoreType.DMA((others,)),
    ]
    args = [doc_len, table, q, kx, vx, kg, vg, o, do, l, dog, ldg, yq, *sums]
    if early_rows:
        in_specs += [pl.BlockSpec(memory_space=pl.ANY)] * 3
        outs.append(shape((4, early_rows, width), BF16))
        scratch += Reducer.scratch(early_rows, width, 1)
        for parts in sums[1:]:
            outs.append(shape(parts.shape[1:], F32))
            scratch += ZSum.scratch(*parts.shape[1:])
    return pl.pallas_call(
        functools.partial(back_kernel, sizes, early_rows),
        grid=(2 * steps,),
        in_specs=in_specs,
        out_specs=[whole] * len(outs),
        out_shape=outs,
        scratch_shapes=scratch,
        compiler_params=pltpu.CompilerParams(
            collective_id=1, has_side_effects=True, vmem_limit_bytes=60 * 2**20
        ),
        name="attend_back",
    )(*args)


def on_device(
    long_input,
    global_input,
    lengths,
    w_query,
    b_query,
    w_key,
    w_value,
    b_value,
    w_out,
    b_out,
    w_inner,
    b_inner,
    w_outer,
    b_outer,
    norm1_gain,
    norm1_shift,
    norm2_gain,
    norm2_shift,
    rel_table,
    long_cotangent,
    global_cotangent,
):
    seq_count = lax.axis_size("seq")
    data_count = lax.axis_size("dp")
    seq_index = lax.axis_index("seq")
    block = long_input.shape[1]
    count = global_input.shape[1]
    width = long_input.shape[2]
    heads = rel_table.shape[1]
    pairs = heads // 2
    labels = 2 * R + 1
    quarter = GP // seq_count
    sizes = Sizes(block, count, quarter, seq_count, pairs)
    queries, kx, vx, kg, vg, attn_low, long_l, glob_l, glob_x, table = attend(
        sizes,
        lengths,
        rel_table,
        long_input[0],
        global_input[0],
        w_query,
        w_key,
        w_value,
        b_query,
        b_value,
        norm1_gain,
        norm1_shift,
    )
    planned = has_plan()
    long_result, own_out, grad_mid, grad_attn, every_do, every_ld, *gradients = feed_forward(
        sizes,
        planned,
        lengths,
        attn_low,
        long_input[0],
        glob_x,
        long_cotangent[0],
        global_cotangent[0],
        glob_l,
        w_out,
        b_out,
        norm2_gain,
        norm2_shift,
        w_inner,
        b_inner,
        w_outer,
        b_outer,
    )
    query_low, key_low, value_low, dtab, glob_out, *early = attend_back(
        sizes,
        lengths,
        table,
        queries,
        kx,
        vx,
        kg,
        vg,
        attn_low,
        grad_attn,
        long_l,
        every_do,
        every_ld,
        own_out,
        *(gradients if planned else []),
    )
    long_grad, glob_grad, *late = last_part(
        sizes,
        planned,
        long_input[0],
        glob_x,
        query_low,
        key_low,
        value_low,
        grad_mid,
        w_query,
        w_key,
        w_value,
        norm1_gain,
        norm1_shift,
        dtab,
        *early[:1],
    )
    if planned:
        (
            g_query,
            g_key,
            g_value,
            g_out,
            g_inner,
            g_outer,
            g_b_query,
            g_b_value,
            g_b_out,
            g_b_outer,
            g_g1,
            g_s1,
            g_g2,
            g_s2,
            g_b_inner,
            table_total,
            long_grad,
            long_result,
            glob_out,
            glob_grad,
        ) = small_results(
            heads,
            late[3],
            late[0],
            early[1],
            early[2],
            late[1],
            late[2],
            long_grad,
            long_result,
            glob_out,
            glob_grad,
        )
        table_total = table_total.T
        glob_grad = glob_grad.reshape(count, width)
    else:
        devices = data_count * seq_count
        own_part = lambda vector: lax.dynamic_slice_in_dim(
            vector,
            (lax.axis_index("dp") * seq_count + seq_index) * (vector.shape[0] // devices),
            vector.shape[0] // devices,
        )
        g_outer, g_inner, g_out, vectors = gradients
        g_outer, g_inner, g_out, g_query, g_key, g_value = (
            lax.psum_scatter(g.astype(BF16), ("dp", "seq"), scatter_dimension=0, tiled=True).astype(
                F32
            )
            for g in (g_outer, g_inner, g_out, *late[:3])
        )
        vectors, sums, scales = lax.psum((vectors, *late[3:]), ("dp", "seq"))
        g_b_query, g_b_value = (own_part(sums[heads + i]) for i in range(2))
        g_g1, g_s1 = (own_part(scales[i]) for i in range(2))
        g_b_out, g_b_outer, g_g2, g_s2 = (own_part(vectors[i]) for i in range(4))
        g_b_inner = own_part(vectors[4:].reshape(-1))
        table_total = sums[:heads, HALO - R : HALO - R + labels].T
    return (
        long_result[None],
        glob_out[None],
        long_grad[None],
        glob_grad[None],
        g_query,
        g_b_query,
        g_key,
        g_value,
        g_b_value,
        g_out,
        g_b_out,
        g_inner,
        g_b_inner,
        g_outer,
        g_b_outer,
        g_g1,
        g_s1,
        g_g2,
        g_s2,
        table_total,
    )


def solution(mesh):
    rows, whole = P("dp", "seq", None), P("dp", None, None)
    matrix, vector = P(("dp", "seq"), None), P(("dp", "seq"))
    return jax.shard_map(
        on_device,
        mesh=mesh,
        in_specs=(rows, whole, P("dp")) + (P(),) * 16 + (rows, whole),
        out_specs=(
            rows,
            whole,
            rows,
            whole,
            matrix,
            vector,
            matrix,
            matrix,
            vector,
            matrix,
            vector,
            matrix,
            vector,
            matrix,
            vector,
            vector,
            vector,
            vector,
            vector,
            P(),
        ),
        check_vma=False,
    )
```

```python
import functools
from typing import NamedTuple

import jax
import jax.numpy as jnp
from jax import lax
from jax.experimental import pallas as pl
from jax.experimental.pallas import tpu as pltpu
from jax.sharding import PartitionSpec as P

HD = 64
R = 84
PAIR = 2 * HD
HALO = 128
REACH = 96
GP = 256
SUB = 256
WINDOW = SUB + 2 * HALO
EPSILON = 1e-05
MASKED = -1e30
F32 = jnp.float32
BF16 = jnp.bfloat16


def dot_t(left, right):
    return lax.dot_general(left, right, (((1,), (1,)), ((), ())), preferred_element_type=F32)


def dot_n(left, right):
    return lax.dot_general(left, right, (((1,), (0,)), ((), ())), preferred_element_type=F32)


def t_dot(left, right):
    return lax.dot_general(left, right, (((0,), (0,)), ((), ())), preferred_element_type=F32)


def band_bias(table_row):
    spread = jnp.broadcast_to(table_row, (SUB, WINDOW))
    return pltpu.roll(spread, 0, 1, stride=1, stride_axis=0)


def diagonal_sums(rows):
    height, width = rows.shape
    while height > 8:
        height //= 2
        rows = rows[:height] + pltpu.roll(rows[height:], width - height, 1)
    row = lax.broadcasted_iota(jnp.int32, rows.shape, 0)
    for bit in (1, 2, 4):
        rows = jnp.where((row & bit) != 0, pltpu.roll(rows, width - bit, 1), rows)
    return jnp.sum(rows, 0, keepdims=True)


def lane_index():
    return lax.broadcasted_iota(jnp.int32, (1, PAIR), 1)


def own_half(head, value):
    low_lanes = lane_index() < HD
    return jnp.where(low_lanes if head == 0 else ~low_lanes, value, jnp.zeros_like(value))


def other_lane(head):
    return HD * (1 - head)


def with_lanes(head, value, columns):
    wide = own_half(head, value.astype(F32))
    lane = lane_index()
    for offset, column in enumerate(columns):
        wide = jnp.where(lane == other_lane(head) + offset, column, wide)
    return wide.astype(BF16)


def in_three(column):
    high = column.astype(BF16).astype(F32)
    middle = (column - high).astype(BF16).astype(F32)
    return (high, middle, column - high - middle)


def key_bias(first, rows, end):
    position = first + lax.broadcasted_iota(jnp.int32, (rows, 1), 0)
    return jnp.where((position >= 0) & (position < end), 0.0, MASKED)


def pick_column(rows, index):
    return jnp.sum(jnp.where(lane_index() == index, rows, 0.0), -1, keepdims=True)


def key_side(head, keys, bias):
    return with_lanes(head, keys, (bias, 1.0, 1.0, 1.0))


def value_side(head, values):
    return with_lanes(head, values, (1.0, 1.0, 1.0))


def softmax_rows(parts, value_parts, head):
    top = functools.reduce(
        jnp.maximum, [jnp.max(part, -1, keepdims=True) for part in parts]
    )
    mixed = sum(
        dot_n(jnp.exp(part - top).astype(BF16), values)
        for part, values in zip(parts, value_parts)
    )
    at = other_lane(head)
    total = mixed[:, at : at + 1]
    return mixed / total, top + jnp.log(total)


def seq_device(steps, seq_count):
    return (lax.axis_index("dp"), lax.rem(lax.axis_index("seq") + steps + seq_count, seq_count))


def row_norm(rows):
    centred = rows - jnp.mean(rows, -1, keepdims=True)
    inverse = lax.rsqrt(jnp.mean(centred * centred, -1, keepdims=True) + EPSILON)
    return centred * inverse, inverse


def put_column(ref, rows, index, column):
    ref[rows] = jnp.where(lane_index() == index, column, ref[rows])


def lanes_of(at):
    return pl.ds(pl.multiple_of(at * PAIR, PAIR), PAIR)


class Sizes(NamedTuple):
    block: int
    count: int
    quarter: int
    seq_count: int
    pairs: int


def attend_kernel(
    sizes,
    len_ref,
    rel_ref,
    long_ref,
    raw_ref,
    wq_far,
    wk_far,
    wv_far,
    bq_ref,
    bv_ref,
    gain_ref,
    shift_ref,
    q_far,
    kx_far,
    vx_far,
    kg_far,
    vg_far,
    o_ref,
    l_ref,
    lq_ref,
    glob_ref,
    tab_ref,
    spread,
    wide,
    part_o,
    part_l,
    from_o,
    from_l,
    halo_sends,
    halo_recvs,
    part_sends,
    part_recvs,
    wq_ref,
    wk_ref,
    wv_ref,
    loads,
    q_ref,
    kx_ref,
    vx_ref,
    kg_ref,
    vg_ref,
    stores,
):
    block, count, quarter, seq_count, pairs = sizes
    ext = block + 2 * HALO
    seq_index = lax.axis_index("seq")
    scale = jnp.asarray(HD ** (-0.5), BF16)
    low_lanes = lane_index() < HD
    own_keys = slice(HALO, HALO + block)
    own_rows = pl.ds(pl.multiple_of(seq_index * quarter, quarter), quarter)
    neighbours = (seq_index > 0, seq_index < seq_count - 1)
    barrier = pltpu.get_barrier_semaphore()
    for step in range(1, seq_count):
        pl.semaphore_signal(
            barrier,
            inc=1,
            device_id=seq_device(step, seq_count),
            device_id_type=pl.DeviceIdType.MESH,
        )

    def halo_copies(direction):
        source = HALO if direction == 0 else HALO + block - REACH
        dest = HALO + block if direction == 0 else HALO - REACH
        for kind, ref in enumerate((kx_ref, vx_ref)):
            yield pltpu.make_async_remote_copy(
                src_ref=ref.at[source : source + REACH],
                dst_ref=ref.at[dest : dest + REACH],
                send_sem=halo_sends.at[direction, kind],
                recv_sem=halo_recvs.at[direction, kind],
                device_id=seq_device(2 * direction - 1, seq_count),
                device_id_type=pl.DeviceIdType.MESH,
            )

    def part_copies():
        for step in range(1, seq_count):
            device = seq_device(step, seq_count)
            rows = pl.ds(pl.multiple_of(device[1] * quarter, quarter), quarter)
            for kind, (source, dest) in enumerate(((part_o, from_o), (part_l, from_l))):
                yield step, kind, pltpu.make_async_remote_copy(
                    src_ref=source.at[rows],
                    dst_ref=dest.at[step - 1],
                    send_sem=part_sends.at[kind, step - 1],
                    recv_sem=part_recvs.at[kind, step - 1],
                    device_id=device,
                    device_id_type=pl.DeviceIdType.MESH,
                )

    loading = [
        pltpu.make_async_copy(source, dest, loads.at[at])
        for at, (source, dest) in enumerate(
            ((wk_far, wk_ref), (wv_far, wv_ref), (wq_far, wq_ref))
        )
    ]
    for copy in loading:
        copy.start()
    gain, shift = gain_ref[...], shift_ref[...]
    heads, labels = rel_ref.shape
    spread[...] = jnp.full(spread.shape, MASKED, F32)
    spread[:heads, :labels] = rel_ref[...]
    turned = pltpu.roll(spread[...], HALO - R, 1)
    for pair in range(pairs):
        tab_ref[pair] = turned[2 * pair : 2 * pair + 2]
    normed_long = (row_norm(long_ref[...].astype(F32))[0] * gain + shift).astype(BF16)
    loading[0].wait()
    kx_ref[own_keys] = dot_n(normed_long, wk_ref[...]).astype(BF16)
    loading[1].wait()
    vx_ref[own_keys] = (dot_n(normed_long, wv_ref[...]) + bv_ref[...]).astype(BF16)
    pl.semaphore_wait(barrier, seq_count - 1)
    for direction, first in enumerate((HALO - REACH, HALO + block)):

        @pl.when(neighbours[direction])
        def _(direction=direction):
            for copy in halo_copies(direction):
                copy.start()

        outer = slice(0, first) if direction == 0 else slice(first + REACH, ext)
        for ref in (kx_ref, vx_ref):
            ref[outer] = jnp.zeros((HALO - REACH, ref.shape[1]), BF16)

        @pl.when(jnp.logical_not(neighbours[direction]))
        def _(first=first):
            for ref in (kx_ref, vx_ref):
                ref[first : first + REACH] = jnp.zeros((REACH, ref.shape[1]), BF16)

    wide[...] = jnp.zeros_like(wide)
    wide[:count] = raw_ref[...].astype(F32)
    glob_ref[...] = wide[...].astype(BF16)
    normed_glob = (row_norm(wide[...])[0] * gain + shift).astype(BF16)
    kg_ref[...] = dot_n(normed_glob, wk_ref[...]).astype(BF16)
    vg_ref[...] = (dot_n(normed_glob, wv_ref[...]) + bv_ref[...]).astype(BF16)
    loading[2].wait()
    q_ref[block:] = (dot_n(normed_glob, wq_ref[...]) + bq_ref[...]).astype(BF16)
    q_ref[:block] = (dot_n(normed_long, wq_ref[...]) + bq_ref[...]).astype(BF16)
    part_l[...] = jnp.zeros_like(part_l)
    l_ref[...] = jnp.zeros_like(l_ref)

    def glob_pair(pair, carry):
        lanes = lanes_of(pair)
        far_bias = key_bias(seq_index * block, block, len_ref[0])
        near_bias = key_bias(seq_index * quarter, quarter, count)
        query = q_ref[block:, lanes] * scale
        outs = []
        for head in range(2):
            q = with_lanes(head, query, (1.0,))
            far = dot_t(q, with_lanes(head, kx_ref[own_keys, lanes], (far_bias,)))
            near = dot_t(q, with_lanes(head, kg_ref[own_rows, lanes], (near_bias,)))
            out, norm = softmax_rows(
                [far, near],
                [
                    with_lanes(head, vx_ref[own_keys, lanes], (1.0,)),
                    with_lanes(head, vg_ref[own_rows, lanes], (1.0,)),
                ],
                head,
            )
            outs.append(out)
            put_column(part_l, slice(None), 2 * pair + head, norm)
        part_o[:, lanes] = jnp.where(low_lanes, outs[0], outs[1]).astype(BF16)
        return carry

    lax.fori_loop(0, pairs, glob_pair, 0, unroll=2)
    for _, _, copy in part_copies():
        copy.start()
    for direction in range(2):

        @pl.when(neighbours[1 - direction])
        def _(direction=direction):
            for copy in halo_copies(direction):
                copy.wait_recv()

    storing = [
        pltpu.make_async_copy(source, dest, stores.at[at])
        for at, (source, dest) in enumerate(
            (
                (q_ref, q_far),
                (kx_ref, kx_far),
                (vx_ref, vx_far),
                (kg_ref, kg_far),
                (vg_ref, vg_far),
            )
        )
    ]
    for copy in storing:
        copy.start()

    def long_pair(pair, carry):
        lanes = lanes_of(pair)
        long_bias = key_bias(seq_index * block - HALO, ext, len_ref[0])
        glob_bias = key_bias(0, GP, count)
        query = q_ref[:block, lanes] * scale
        outs = []
        for head in range(2):
            q = with_lanes(head, query, (1.0,))
            kx = with_lanes(head, kx_ref[:, lanes], (long_bias,))
            kg = with_lanes(head, kg_ref[:, lanes], (glob_bias,))
            vx, vg = (with_lanes(head, ref[:, lanes], (1.0,)) for ref in (vx_ref, vg_ref))
            bias = band_bias(tab_ref[pair, head : head + 1])
            mixed = []
            for start in range(0, block, SUB):
                rows, keys = slice(start, start + SUB), slice(start, start + WINDOW)
                out, norm = softmax_rows(
                    [dot_t(q[rows], kx[keys]) + bias, dot_t(q[rows], kg)], [vx[keys], vg], head
                )
                mixed.append(out)
                put_column(l_ref, rows, 2 * pair + head, norm)
            outs.append(jnp.concatenate(mixed, 0))
        o_ref[:block, lanes] = jnp.where(low_lanes, outs[0], outs[1]).astype(BF16)
        return carry

    lax.fori_loop(0, pairs, long_pair, 0, unroll=2)
    for _, _, copy in part_copies():
        copy.wait_recv()
    norms = [part_l[own_rows]] + [from_l[step] for step in range(seq_count - 1)]
    outs = [part_o[own_rows]] + [from_o[step] for step in range(seq_count - 1)]
    top = functools.reduce(jnp.maximum, norms)
    shares = [jnp.exp(norm - top) for norm in norms]
    total = sum(shares)
    lq_ref[...] = top + jnp.log(total)
    shares = [share / total for share in shares]
    for at in range(pairs):
        lanes = slice(at * PAIR, (at + 1) * PAIR)
        mixed = 0.0
        for share, out in zip(shares, outs):
            spread = jnp.where(
                low_lanes, share[:, 2 * at : 2 * at + 1], share[:, 2 * at + 1 : 2 * at + 2]
            )
            mixed += spread * out[:, lanes].astype(F32)
        o_ref[block:, lanes] = mixed.astype(BF16)
    for copy in storing:
        copy.wait()
    for _, _, copy in part_copies():
        copy.wait_send()
    for direction in range(2):

        @pl.when(neighbours[direction])
        def _(direction=direction):
            for copy in halo_copies(direction):
                copy.wait_send()


def attend(sizes, doc_len, rel_table, long_x, glob_x, *weights):
    block, count, quarter, seq_count, pairs = sizes
    width = long_x.shape[1]
    ext = block + 2 * HALO
    whole = pl.BlockSpec(memory_space=pltpu.VMEM)
    shape = jax.ShapeDtypeStruct
    others = seq_count - 1
    return pl.pallas_call(
        functools.partial(attend_kernel, sizes),
        in_specs=[pl.BlockSpec(memory_space=pltpu.SMEM)]
        + [whole] * 3
        + [pl.BlockSpec(memory_space=pl.ANY)] * 3
        + [whole] * 4,
        out_specs=[pl.BlockSpec(memory_space=pl.ANY)] * 5 + [whole] * 5,
        out_shape=[
            shape((block + GP, width), BF16),
            shape((ext, width), BF16),
            shape((ext, width), BF16),
            shape((GP, width), BF16),
            shape((GP, width), BF16),
            shape((block + quarter, width), BF16),
            shape((block, PAIR), F32),
            shape((quarter, PAIR), F32),
            shape((GP, width), BF16),
            shape((pairs, 2, WINDOW), F32),
        ],
        scratch_shapes=[
            pltpu.VMEM(((2 * pairs + 7) // 8 * 8, WINDOW), F32),
            pltpu.VMEM((GP, width), F32),
            pltpu.VMEM((GP, width), BF16),
            pltpu.VMEM((GP, PAIR), F32),
            pltpu.VMEM((others, quarter, width), BF16),
            pltpu.VMEM((others, quarter, PAIR), F32),
            pltpu.SemaphoreType.DMA((2, 2)),
            pltpu.SemaphoreType.DMA((2, 2)),
            pltpu.SemaphoreType.DMA((2, others)),
            pltpu.SemaphoreType.DMA((2, others)),
            pltpu.VMEM((width, width), BF16),
            pltpu.VMEM((width, width), BF16),
            pltpu.VMEM((width, width), BF16),
            pltpu.SemaphoreType.DMA((3,)),
            pltpu.VMEM((block + GP, width), BF16),
            pltpu.VMEM((ext, width), BF16),
            pltpu.VMEM((ext, width), BF16),
            pltpu.VMEM((GP, width), BF16),
            pltpu.VMEM((GP, width), BF16),
            pltpu.SemaphoreType.DMA((5,)),
        ],
        compiler_params=pltpu.CompilerParams(
            collective_id=3, has_side_effects=True, vmem_limit_bytes=56 * 2**20
        ),
        name="attend",
    )(doc_len, rel_table, long_x, glob_x, *weights)


class Reducer:
    def __init__(self, rows, split, scratch, pieces=None, order=None, parts=None):
        self.ids = mesh_ids()
        self.parts = parts
        self.order = order
        self.halves = (slice(0, split), slice(split, rows))
        held, self.from_core, self.from_one, self.from_two = scratch[:4]
        self.local, self.sends, self.recvs = scratch[4:7]
        if parts is None:
            self.from_z, self.z_sends, self.z_recvs = scratch[7:]
        self.pieces, self.held = pieces, held
        self.mine = held.at[self.ids[3]] if pieces is None else held.at[0]

    @staticmethod
    def scratch(rows, width, sides, with_z=False):
        buffers = [
            pltpu.VMEM((sides, 4, 2, 2, rows, width), BF16),
            pltpu.VMEM((4, 2, 2, rows, width), BF16),
            pltpu.VMEM((4, 2, rows, width), BF16),
            pltpu.VMEM((4, rows, width), BF16),
            pltpu.SemaphoreType.DMA((4,)),
            pltpu.SemaphoreType.DMA((5, 4)),
            pltpu.SemaphoreType.DMA((5, 4)),
        ]
        if with_z:
            buffers += [
                pltpu.VMEM((3, rows, width), BF16),
                pltpu.SemaphoreType.DMA((4,)),
                pltpu.SemaphoreType.DMA((3,)),
            ]
        return buffers

    def partners(self):
        z, y, x, core = self.ids
        dp, seq = z * 2 + y, x * 2 + core
        near = [(dp, x * 2 + 1 - core), (dp, (1 - x) * 2 + core), (z * 2 + 1 - y, seq)]
        return near + [(lax.rem(z + step, 4) * 2 + y, seq) for step in (1, 2, 3)]

    def target(self, chunk):
        return self.order(chunk) if self.order else lax.rem(self.ids[0] + 1 + chunk, 4)

    def remote(self, source, dest, kind, send_at, recv_at, device):
        return pltpu.make_async_remote_copy(
            src_ref=source,
            dst_ref=dest,
            send_sem=self.sends.at[kind, send_at],
            recv_sem=self.recvs.at[kind, recv_at],
            device_id=device,
            device_id_type=pl.DeviceIdType.MESH,
        )

    def own_copy(self, chunk):
        core, to = self.ids[3], self.target(chunk)
        return pltpu.make_async_copy(
            self.pieces.at[core, to], self.mine.at[to], self.local.at[chunk]
        )

    def core_copy(self, chunk):
        core, to = self.ids[3], self.target(chunk)
        source = (self.held if self.pieces is None else self.pieces).at[1 - core, to]
        return self.remote(source, self.from_core.at[to], 0, chunk, chunk, self.partners()[0])

    def first_copies(self, chunk):
        z, y, x, core = self.ids
        to = self.target(chunk)
        one, two = self.halves
        near = self.partners()
        return (
            self.remote(
                self.mine.at[to, :, 1 - x, one],
                self.from_one.at[to, :, one],
                1,
                chunk,
                chunk,
                near[1],
            ),
            self.remote(
                self.mine.at[to, 1 - y, :, two],
                self.from_one.at[to, :, two],
                2,
                chunk,
                chunk,
                near[2],
            ),
        )

    def second_copies(self, chunk):
        z, y, x, core = self.ids
        to = self.target(chunk)
        one, two = self.halves
        near = self.partners()
        return (
            self.remote(
                self.mine.at[to, 1 - y, x, one],
                self.from_two.at[to, one],
                3,
                chunk,
                chunk,
                near[2],
            ),
            self.remote(
                self.mine.at[to, y, 1 - x, two],
                self.from_two.at[to, two],
                4,
                chunk,
                chunk,
                near[1],
            ),
        )

    def last_copy(self, chunk):
        z, y, x, core = self.ids
        to = self.target(chunk)
        slot = lax.rem(z - to + 4, 4) - 1
        return pltpu.make_async_remote_copy(
            src_ref=self.mine.at[to, y, x],
            dst_ref=self.from_z.at[slot],
            send_sem=self.z_sends.at[chunk],
            recv_sem=self.z_recvs.at[slot],
            device_id=(to * 2 + y, x * 2 + core),
            device_id_type=pl.DeviceIdType.MESH,
        )

    def arrival(self, slot):
        z, y, x, core = self.ids
        return pltpu.make_async_remote_copy(
            src_ref=self.mine.at[z, y, x],
            dst_ref=self.from_z.at[slot],
            send_sem=self.z_sends.at[slot],
            recv_sem=self.z_recvs.at[slot],
            device_id=self.partners()[3],
            device_id_type=pl.DeviceIdType.MESH,
        )

    def leaves(self, chunk):
        return self.target(chunk) != self.ids[0]

    def fill(self, to, at, value):
        self.held[at % 2, to, at // 4, at // 2 % 2] = value.astype(BF16)

    def start(self, chunk):
        self.core_copy(chunk).start()
        if self.pieces is not None:
            self.own_copy(chunk).start()

    def add_core(self, chunk):
        to = self.target(chunk)
        if self.pieces is not None:
            self.own_copy(chunk).wait()
        self.core_copy(chunk).wait_recv()

        def add(index, carry):
            at = (to, lax.div(index, 2), lax.rem(index, 2))
            self.mine[at] = self.mine[at] + self.from_core[at]
            return carry

        lax.fori_loop(0, 4, add, 0)
        for copy in self.first_copies(chunk):
            copy.start()

    def add_first(self, chunk):
        z, y, x, core = self.ids
        one, two = self.halves
        to = self.target(chunk)
        for copy in self.first_copies(chunk):
            copy.wait_recv()

        def add(index, carry):
            for at, rows in (((to, index, x), one), ((to, y, index), two)):
                self.mine[at + (rows,)] = self.mine[at + (rows,)] + self.from_one[to, index, rows]
            return carry

        lax.fori_loop(0, 2, add, 0)
        for copy in self.second_copies(chunk):
            copy.start()

    def add_second(self, chunk):
        z, y, x, core = self.ids
        to = self.target(chunk)
        for copy in self.second_copies(chunk):
            copy.wait_recv()
        if self.parts is not None:
            self.parts[to] = self.mine[to, y, x] + self.from_two[to]
            return

        @pl.when(self.leaves(chunk))
        def _():
            self.mine[to, y, x] = self.mine[to, y, x] + self.from_two[to]
            self.last_copy(chunk).start()

    def finish(self, out=None):
        z, y, x, core = self.ids
        if self.parts is None:
            total = self.mine[z, y, x].astype(F32) + self.from_two[z].astype(F32)
            for slot in range(3):
                self.arrival(slot).wait_recv()
                total += self.from_z[slot].astype(F32)
            out[...] = total
        for chunk in range(4):
            self.core_copy(chunk).wait_send()
            for copy in self.first_copies(chunk) + self.second_copies(chunk):
                copy.wait_send()
            if self.parts is None:

                @pl.when(self.leaves(chunk))
                def _(chunk=chunk):
                    self.last_copy(chunk).wait_send()


class ZSum:
    def __init__(self, parts, scratch):
        self.ids = mesh_ids()
        self.parts = parts
        self.own, self.from_z, self.local, self.sends, self.recvs = scratch

    @staticmethod
    def scratch(rows, width):
        return [
            pltpu.VMEM((rows, width), BF16),
            pltpu.VMEM((3, rows, width), BF16),
            pltpu.SemaphoreType.DMA,
            pltpu.SemaphoreType.DMA((3,)),
            pltpu.SemaphoreType.DMA((3,)),
        ]

    def own_copy(self):
        return pltpu.make_async_copy(self.parts.at[self.ids[0]], self.own, self.local)

    def copies(self):
        z, y, x, core = self.ids
        for slot in range(3):
            to = lax.rem(z + 3 - slot, 4)
            yield pltpu.make_async_remote_copy(
                src_ref=self.parts.at[to],
                dst_ref=self.from_z.at[slot],
                send_sem=self.sends.at[slot],
                recv_sem=self.recvs.at[slot],
                device_id=(to * 2 + y, x * 2 + core),
                device_id_type=pl.DeviceIdType.MESH,
            )

    def start(self):
        self.own_copy().start()
        for copy in self.copies():
            copy.start()

    def finish(self, out):
        self.own_copy().wait()
        total = self.own[...].astype(F32)
        for slot, copy in enumerate(self.copies()):
            copy.wait_recv()
            total += self.from_z[slot].astype(F32)
        out[...] = total
        for copy in self.copies():
            copy.wait_send()


class EverySum:
    def __init__(self, scratch):
        self.kept, self.arrived, self.from_z, self.sends, self.recvs = scratch
        z, y, x, core = mesh_ids()
        seq = x * 2 + core
        self.z = z
        self.pairs = (
            (z * 2 + y, x * 2 + 1 - core),
            (z * 2 + y, (1 - x) * 2 + core),
            (z * 2 + 1 - y, seq),
        )
        self.along_z = [(lax.rem(z + step, 4) * 2 + y, seq) for step in (1, 2, 3)]

    @staticmethod
    def scratch(rows, width):
        return [
            pltpu.VMEM((3, rows, width), F32),
            pltpu.VMEM((3, rows, width), F32),
            pltpu.VMEM((4, rows, width), F32),
            pltpu.SemaphoreType.DMA((6,)),
            pltpu.SemaphoreType.DMA((6,)),
        ]

    def copy(self, stage):
        return pltpu.make_async_remote_copy(
            src_ref=self.kept.at[stage],
            dst_ref=self.arrived.at[stage],
            send_sem=self.sends.at[stage],
            recv_sem=self.recvs.at[stage],
            device_id=self.pairs[stage],
            device_id_type=pl.DeviceIdType.MESH,
        )

    def z_copies(self):
        for at, device in enumerate(self.along_z):
            yield pltpu.make_async_remote_copy(
                src_ref=self.from_z.at[self.z],
                dst_ref=self.from_z.at[self.z],
                send_sem=self.sends.at[3 + at],
                recv_sem=self.recvs.at[3 + at],
                device_id=device,
                device_id_type=pl.DeviceIdType.MESH,
            )

    def step(self, stage):
        if stage > 0:
            self.copy(stage - 1).wait_recv()
            total = self.kept[stage - 1] + self.arrived[stage - 1]
            if stage < 3:
                self.kept[stage] = total
            else:
                self.from_z[self.z] = total
        if stage < 3:
            self.copy(stage).start()
        else:
            for copy in self.z_copies():
                copy.start()

    def finish(self, out):
        for copy in self.z_copies():
            copy.wait_recv()
        out[...] = (self.from_z[0] + self.from_z[1]) + (self.from_z[2] + self.from_z[3])
        for copy in [self.copy(stage) for stage in range(3)] + list(self.z_copies()):
            copy.wait_send()


def mesh_ids():
    dp, seq = lax.axis_index("dp"), lax.axis_index("seq")
    return lax.div(dp, 2), lax.rem(dp, 2), lax.div(seq, 2), lax.rem(seq, 2)


def meet(devices):
    barrier = pltpu.get_barrier_semaphore()
    for device in devices:
        pl.semaphore_signal(barrier, inc=1, device_id=device, device_id_type=pl.DeviceIdType.MESH)
    pl.semaphore_wait(barrier, len(devices))


EARLY_PLAN = (
    (2, "add_core", 0),
    (3, "add_core", 1),
    (4, "add_core", 2),
    (5, "add_core", 3),
    (7, "add_first", 0),
    (8, "add_first", 1),
    (9, "add_second", 0),
    (9, "add_first", 2),
    (10, "add_second", 1),
    (10, "add_first", 3),
    (11, "add_second", 2),
    (12, "add_second", 3),
)


def late_kernel(
    sizes,
    planned,
    long_ref,
    glob_ref,
    dq_ref,
    dk_ref,
    dv_ref,
    dmid_far,
    wq_far,
    wk_far,
    wv_far,
    gain_ref,
    shift_ref,
    table_ref,
    *rest,
):
    block, count, quarter, seq_count, pairs = sizes
    rows = block + quarter
    width = long_ref.shape[1]
    if planned:
        early_parts, long_far, glob_out, late_ref, total_ref, scale_ref, early_ref, *rest = rest
    else:
        long_far, glob_out, gq_ref, gk_ref, gv_ref, total_ref, scale_ref, *rest = rest
    normed_t, every, gather_sends, gather_recvs, *rest = rest
    dmid_ref, wq_ref, wk_ref, wv_ref, loads, long_out, store, *rest = rest
    storing = pltpu.make_async_copy(long_out, long_far, store)
    far = (wq_far, wk_far, wv_far, dmid_far)
    loading = [
        pltpu.make_async_copy(source, dest, loads.at[at])
        for at, (source, dest) in enumerate(zip(far, (wq_ref, wk_ref, wv_ref, dmid_ref)))
    ]
    for copy in loading:
        copy.start()
    seq_index = lax.axis_index("seq")
    own_rows = pl.ds(pl.multiple_of(seq_index * quarter, quarter), quarter)
    others = [seq_device(step, seq_count) for step in range(1, seq_count)]

    def gathers():
        for step, device in enumerate(others):
            yield pltpu.make_async_remote_copy(
                src_ref=every.at[own_rows],
                dst_ref=every.at[own_rows],
                send_sem=gather_sends.at[step],
                recv_sem=gather_recvs.at[step],
                device_id=device,
                device_id_type=pl.DeviceIdType.MESH,
            )

    if planned:
        first_sum, second_sum = EverySum(rest[:5]), EverySum(rest[5:10])
        z_sum = ZSum(early_parts, rest[10:15])
        reducer = Reducer(rest[15].shape[-2], 32, rest[15:])

    meet(others + (reducer.partners()[2:] if planned else []))
    heads = 2 * pairs
    first = first_sum.kept.at[0] if planned else total_ref
    first[...] = jnp.zeros(first.shape, F32)
    for pair in range(pairs):
        first[2 * pair : 2 * pair + 2, :WINDOW] = table_ref[pair]
    for at, ref in enumerate((dq_ref, dv_ref)):
        first[heads + at : heads + at + 1] = column_sum(ref[...].astype(F32))
    if planned:
        first_sum.step(0)
        z_sum.start()
    everything = jnp.concatenate([long_ref[...], glob_ref[own_rows]], 0).astype(F32)
    hat, inverse = row_norm(everything)
    normed_t[...] = (hat * gain_ref[...] + shift_ref[...]).astype(BF16).T
    if planned:
        piece = width // 32
        blank = jnp.zeros((8, width), F32)
        def weight_rows(chunk):
            to = reducer.target(chunk)
            some = normed_t[pl.ds(pl.multiple_of(to * 8 * piece, 64), 8 * piece)]
            parts = [dot_n(some, ref[...]) for ref in (dq_ref, dk_ref, dv_ref)]
            for at in range(8):
                rows_at = slice(at * piece, (at + 1) * piece)
                reducer.fill(
                    to, at, jnp.concatenate([part[rows_at] for part in parts] + [blank], 0)
                )
            reducer.start(chunk)

        weight_rows(0)
        first_sum.step(1)
        weight_rows(1)
        first_sum.step(2)
        reducer.add_core(0)
        weight_rows(2)
        first_sum.step(3)
        reducer.add_core(1)
        weight_rows(3)
        for copy in loading:
            copy.wait()
        grads = dot_t(dq_ref[...], wq_ref[...])
        grads += dot_t(dk_ref[...], wk_ref[...]) + dot_t(dv_ref[...], wv_ref[...])
        reducer.add_first(0)
        reducer.add_core(2)
    else:
        for ref, out in ((dq_ref, gq_ref), (dk_ref, gk_ref), (dv_ref, gv_ref)):
            out[...] = dot_n(normed_t[...], ref[...]).astype(BF16)
        for copy in loading:
            copy.wait()
        grads = (
            dot_t(dq_ref[...], wq_ref[...])
            + dot_t(dk_ref[...], wk_ref[...])
            + dot_t(dv_ref[...], wv_ref[...])
        )
    scaled = grads * gain_ref[...]
    total = dmid_ref[...] + inverse * (
        scaled
        - jnp.mean(scaled, -1, keepdims=True)
        - hat * jnp.mean(scaled * hat, -1, keepdims=True)
    )
    every[own_rows] = total[block:].astype(BF16)
    for copy in gathers():
        copy.start()
    long_out[...] = total[:block]
    storing.start()
    second = second_sum.kept.at[0] if planned else scale_ref
    second[...] = jnp.zeros(second.shape, F32)
    second[0:1] = column_sum(grads * hat)
    second[1:2] = column_sum(grads)
    if planned:
        second_sum.step(0)
        reducer.add_first(1)
        second_sum.step(1)
        reducer.add_core(3)
        reducer.add_second(0)
        reducer.add_first(2)
        second_sum.step(2)
        reducer.add_second(1)
        reducer.add_first(3)
        second_sum.step(3)
        reducer.add_second(2)
        reducer.add_second(3)
        first_sum.finish(total_ref)
        z_sum.finish(early_ref)
        reducer.finish(late_ref)
        second_sum.finish(scale_ref)
    for copy in gathers():
        copy.wait_recv()
    glob_out[...] = every[:count].astype(F32)
    storing.wait()
    for copy in gathers():
        copy.wait_send()


def last_part(sizes, planned, long_x, glob_x, dq, dk, dv, dmid, *weights):
    block, count, quarter, seq_count, pairs = sizes
    rows, width = dq.shape
    others = seq_count - 1
    whole = pl.BlockSpec(memory_space=pltpu.VMEM)
    there = pl.BlockSpec(memory_space=pl.ANY)
    shape = jax.ShapeDtypeStruct
    sums = [shape(((2 * pairs + 2 + 7) // 8 * 8, width), F32), shape((8, width), F32)]
    outs = [shape((block, width), F32), shape((count, width), F32)]
    scratch = [
        pltpu.VMEM((width, rows), BF16),
        pltpu.VMEM((GP, width), BF16),
        pltpu.SemaphoreType.DMA((others,)),
        pltpu.SemaphoreType.DMA((others,)),
        pltpu.VMEM((rows, width), F32),
        pltpu.VMEM((width, width), BF16),
        pltpu.VMEM((width, width), BF16),
        pltpu.VMEM((width, width), BF16),
        pltpu.SemaphoreType.DMA((4,)),
        pltpu.VMEM((block, width), F32),
        pltpu.SemaphoreType.DMA,
    ]
    if planned:
        piece = width // 32
        part = 3 * piece + 8
        early = weights[-1].shape[1:]
        outs += [shape((part, width), F32), *sums, shape(early, F32)]
        for part_sums in sums:
            scratch += EverySum.scratch(*part_sums.shape)
        scratch += ZSum.scratch(*early) + Reducer.scratch(part, width, 2, with_z=True)
    else:
        outs += [shape((width, width), BF16)] * 3 + sums
    return pl.pallas_call(
        functools.partial(late_kernel, sizes, planned),
        in_specs=[whole] * 5 + [there] * 4 + [whole] * 3 + [there] * planned,
        out_specs=[there] + [whole] * (len(outs) - 1),
        out_shape=outs,
        scratch_shapes=scratch,
        compiler_params=pltpu.CompilerParams(
            collective_id=2, has_side_effects=True, vmem_limit_bytes=60 * 2**20
        ),
        name="last_part",
    )(long_x, glob_x, dq, dk, dv, dmid, *weights)


def small_kernel(heads, early_ref, late_ref, outer_ref, inner_ref, sums_ref, scale_ref, *rest):
    outs = rest[4:-4]
    for source, out in zip(rest[:3], rest[-4:]):
        out[...] = source[...]
    rest[-1][...] = rest[3][...].reshape(rest[-1].shape)
    g_query, g_key, g_value, g_out, g_inner, g_outer, *vectors, table = outs
    device = lax.axis_index("dp") * lax.axis_size("seq") + lax.axis_index("seq")
    piece, width = g_query.shape
    for at, out in enumerate((g_query, g_key, g_value)):
        out[...] = late_ref[at * piece : (at + 1) * piece]
    g_out[...] = early_ref[2 * piece : 3 * piece]
    g_outer[...] = outer_ref[...]
    for source, first, chunk in (
        (inner_ref, 0, 0),
        (inner_ref, piece, 3),
        (early_ref, 0, 1),
        (early_ref, piece, 2),
    ):
        g_inner[:, chunk * width : (chunk + 1) * width] = source[first : first + piece]

    def entries(row, at, length):
        return pltpu.roll(row, width - at * length, 1)[0, :length]

    b_query, b_value, b_out, b_outer, gain_one, shift_one, gain_two, shift_two, b_inner = vectors
    for at, out in enumerate((b_query, b_value)):
        out[...] = entries(sums_ref[heads + at : heads + at + 1], device, piece)
    for at, out in enumerate((gain_one, shift_one)):
        out[...] = entries(scale_ref[at : at + 1], device, piece)
    for at, out in enumerate((b_out, b_outer, gain_two, shift_two)):
        row = 3 * piece + at
        out[...] = entries(early_ref[row : row + 1], device, piece)
    row = pl.ds(3 * piece + 4 + lax.div(device, 8), 1)
    b_inner[...] = entries(early_ref[row], lax.rem(device, 8), 4 * piece)
    labels = table.shape[1]
    turned = pltpu.roll(sums_ref[:, :WINDOW], WINDOW - HALO + R, 1)
    table[...] = turned[:heads, :labels]


def small_results(heads, early, late, outer, inner, sums, scales, *big):
    width = early.shape[1]
    piece = width // 32
    shape = jax.ShapeDtypeStruct
    whole = pl.BlockSpec(memory_space=pltpu.VMEM)
    outs = [shape((piece, width), F32)] * 4
    outs += [shape((piece, 4 * width), F32), shape((4 * piece, width), F32)]
    outs += [shape((piece,), F32)] * 8 + [shape((4 * piece,), F32)]
    outs += [shape((heads, 2 * R + 1), F32)]
    outs += [shape(part.shape, part.dtype) for part in big[:3]]
    outs.append(shape((big[3].shape[0], 1, width), F32))
    return pl.pallas_call(
        functools.partial(small_kernel, heads),
        in_specs=[whole] * 10,
        out_specs=[whole] * len(outs),
        out_shape=outs,
        name="small_results",
    )(early, late, outer, inner, sums, scales, *big)


def has_plan():
    return (lax.axis_size("dp"), lax.axis_size("seq")) == (8, 4)


GELU_A = 0.7978845608028654
GELU_B = 0.044715


def gate_both(u):
    square = u * u
    turned = jnp.tanh(GELU_A * u * (1.0 + GELU_B * square))
    half = 0.5 * (1.0 + turned)
    slope = half + 0.5 * u * (1.0 - turned * turned) * (
        GELU_A * (1.0 + 3.0 * GELU_B * square)
    )
    return u * half, slope


def column_sum(rows):
    return jnp.sum(rows, 0, keepdims=True)


def ffn_kernel(
    sizes,
    planned,
    len_ref,
    attn_ref,
    long_ref,
    glob_ref,
    dlong_ref,
    dglob_ref,
    lq_ref,
    wo_ref,
    bo_ref,
    gain_ref,
    shift_ref,
    wi_ref,
    bi_ref,
    wr_ref,
    br_ref,
    long_out,
    glob_out,
    dmid_far,
    do_far,
    dog_ref,
    ldg_ref,
    *rest,
):
    block, count, quarter, seq_count, pairs = sizes
    if planned:
        pieces_far, outer_ref, inner_ref, *rest = rest
    else:
        g_outer_ref, g_inner_ref, g_out_ref, vec_ref, *rest = rest
    (
        mid,
        y_sum,
        df_sum,
        normed,
        normed_t,
        dy,
        vectors,
        biases,
        every_do,
        every_ld,
        gather_sends,
        gather_recvs,
        dmid_ref,
        do_ref,
        stores,
        *rest,
    ) = rest
    storing = [
        pltpu.make_async_copy(dmid_ref, dmid_far, stores.at[0]),
        pltpu.make_async_copy(do_ref, do_far, stores.at[1]),
    ]
    if planned:
        even, pieces_ref, *rest = rest
        outer = Reducer(rest[0].shape[-2], 48, rest[:7], order=chunk_of, parts=outer_ref)
        inner = Reducer(rest[7].shape[-2], 16, rest[7:], parts=inner_ref)
    step = pl.program_id(0)
    chunk = chunk_of(step)
    seq_index = lax.axis_index("seq")
    own_rows = pl.ds(pl.multiple_of(seq_index * quarter, quarter), quarter)
    width = mid.shape[1]
    piece = width // 32

    def rows_of(device):
        return pl.ds(pl.multiple_of(device[1] * quarter, quarter), quarter)

    def gather(owner, device, at):
        for kind, every in enumerate((every_do, every_ld)):
            yield pltpu.make_async_remote_copy(
                src_ref=every.at[rows_of(owner)],
                dst_ref=every.at[rows_of(owner)],
                send_sem=gather_sends.at[kind, at],
                recv_sem=gather_recvs.at[kind, at],
                device_id=device,
                device_id_type=pl.DeviceIdType.MESH,
            )

    me = seq_device(0, seq_count)
    if planned:
        sibling, across = outer.partners()[:2]
        first_gathers = [(me, across, 0), (me, sibling, 1)]
        second_gathers = [(across, sibling, 2)]
    else:
        first_gathers = [
            (me, seq_device(at + 1, seq_count), at) for at in range(seq_count - 1)
        ]
        second_gathers = []

    def store_pieces(half):
        rows = (slice(0, 2 * piece), slice(2 * piece, 3 * piece + 8))[half]
        return pltpu.make_async_copy(
            pieces_ref.at[:, :, :, :, rows], pieces_far.at[:, :, :, :, rows], stores.at[2 + half]
        )

    def act(now):
        if planned:
            for at, reducer, name, part in FFN_PLAN:
                if at == now:
                    getattr((outer, inner)[reducer], name)(part)

    def act_in_step(point):
        if planned:
            for now in range(4):
                if any(at == (now, point) for at, _, _, _ in FFN_PLAN):

                    @pl.when(step == now)
                    def _(now=now):
                        act((now, point))

    @pl.when(step == 0)
    def _():
        others = [seq_device(seq_step, seq_count) for seq_step in range(1, seq_count)]
        meet(others + (outer.partners()[2:] if planned else []))
        projected = dot_n(attn_ref[...], wo_ref[...]) + bo_ref[...]
        mid[:block] = long_ref[...].astype(F32) + projected[:block]
        mid[block:] = glob_ref[own_rows].astype(F32) + projected[block:]
        hat, _ = row_norm(mid[...])
        normed[...] = (hat * gain_ref[...] + shift_ref[...]).astype(BF16)
        normed_t[...] = normed[...].T
        position = seq_index * block + lax.broadcasted_iota(jnp.int32, (block, 1), 0)
        dy[:block] = jnp.where(
            position < len_ref[0], dlong_ref[...].astype(F32), 0.0
        ).astype(BF16)
        y_sum[:GP] = jnp.zeros((GP, width), F32)
        y_sum[:count] = dglob_ref[...].astype(F32)
        dy[block:] = y_sum[own_rows].astype(BF16)
        vectors[1:2] = column_sum(dy[...].astype(F32))
        y_sum[...] = mid[...] + br_ref[...]
        df_sum[...] = jnp.zeros_like(df_sum)
        for at in range(4):
            biases[at] = bi_ref[at * width : (at + 1) * width].reshape(1, width)

    act_in_step(0)
    active, slope = gate_both(dot_n(normed[...], wi_ref[...]) + biases[chunk])
    active = active.astype(BF16)
    g_outer = t_dot(active, dy[...])
    if planned:
        for at in range(8):
            outer.fill(chunk, at, g_outer[at * 4 * piece : (at + 1) * 4 * piece])
        outer.start(step)
    else:
        g_outer_ref[...] = g_outer.astype(BF16)
    y_sum[...] += dot_n(active, wr_ref[...])
    hidden = dot_t(dy[...], wr_ref[...]) * slope
    for at in range(4):

        @pl.when(chunk == at)
        def _(at=at):
            vectors[4 + at : 5 + at] = column_sum(hidden)

    hidden = hidden.astype(BF16)
    act_in_step(1)
    df_sum[...] += dot_t(hidden, wi_ref[...])
    g_inner = dot_n(normed_t[...], hidden)
    if planned:

        @pl.when(lax.rem(step, 2) == 0)
        def _():
            even[...] = g_inner

        def halves(at):
            part = slice(at * piece, (at + 1) * piece)
            return jnp.concatenate([even[part], g_inner[part]], 0)

        @pl.when(step == 1)
        def _():
            for at in range(32):
                inner.fill(at // 8, at % 8, halves(at))
            for part in range(4):
                inner.start(part)

        @pl.when(step == 3)
        def _():
            for at in range(32):
                pieces_ref[at % 2, at // 8, at // 4 % 2, at // 2 % 2, : 2 * piece] = halves(
                    at
                ).astype(BF16)
            store_pieces(0).start()

    else:
        g_inner_ref[...] = g_inner.astype(BF16)

    def norm_back(rows):
        hat, inverse = row_norm(mid[rows])
        df = df_sum[rows]
        scaled = df * gain_ref[...]
        dmid = dy[rows].astype(F32) + inverse * (
            scaled
            - jnp.mean(scaled, -1, keepdims=True)
            - hat * jnp.mean(scaled * hat, -1, keepdims=True)
        )
        dmid_ref[rows] = dmid
        low = dmid.astype(BF16)
        grad_o = dot_t(low, wo_ref[...]).astype(BF16)
        do_ref[rows] = grad_o
        return [column_sum(dmid), column_sum(df * hat), column_sum(df)], low, grad_o

    @pl.when(step == 3)
    def _():
        glob_sums, glob_low, grad_o = norm_back(slice(block, block + quarter))
        every_do[own_rows] = grad_o
        both = grad_o.astype(F32) * attn_ref[block:].astype(F32)
        stats = lq_ref[...]
        for head in range(2 * pairs):
            lanes = slice(head // 2 * PAIR, head // 2 * PAIR + PAIR)
            delta = jnp.sum(own_half(head % 2, both[:, lanes]), -1, keepdims=True)
            stats = jnp.where(lane_index() == HD + head, delta, stats)
        every_ld[own_rows] = stats
        for part in first_gathers:
            for copy in gather(*part):
                copy.start()
        glob_out[...] = y_sum[block:].astype(BF16)
        act((4, 0))
        position = seq_index * block + lax.broadcasted_iota(jnp.int32, (block, 1), 0)
        long_out[...] = jnp.where(position < len_ref[0], y_sum[:block], 0.0).astype(BF16)
        long_sums, long_low, _ = norm_back(slice(0, block))
        for at, one, two in zip((0, 2, 3), long_sums, glob_sums):
            vectors[at : at + 1] = one + two
        for copy in storing:
            copy.start()
        if planned:
            for copy in gather(*first_gathers[0]):
                copy.wait_recv()
            for copy in gather(*second_gathers[0]):
                copy.start()
        act((4, 1))
        g_out = t_dot(attn_ref[...], jnp.concatenate([long_low, glob_low], 0))
        if planned:
            for at in range(32):
                pieces_ref[at % 2, at // 8, at // 4 % 2, at // 2 % 2, 2 * piece :] = (
                    jnp.concatenate(
                        [g_out[at * piece : (at + 1) * piece], vectors[...]], 0
                    ).astype(BF16)
                )
            store_pieces(1).start()
            act((4, 2))
            outer.finish()
            inner.finish()
            for half in range(2):
                store_pieces(half).wait()
        else:
            g_out_ref[...] = g_out.astype(BF16)
            vec_ref[...] = vectors[...]
        for part in (first_gathers[1:] if planned else first_gathers) + second_gathers:
            for copy in gather(*part):
                copy.wait_recv()
        for copy in storing:
            copy.wait()
        dog_ref[...] = every_do[...]
        ldg_ref[...] = every_ld[...]
        for part in first_gathers + second_gathers:
            for copy in gather(*part):
                copy.wait_send()


OUTER, INNER = 0, 1
FFN_PLAN = (
    ((1, 0), OUTER, "add_core", 0),
    ((2, 0), OUTER, "add_core", 1),
    ((2, 0), OUTER, "add_first", 0),
    ((2, 1), INNER, "add_core", 0),
    ((2, 1), INNER, "add_core", 1),
    ((2, 1), INNER, "add_core", 2),
    ((2, 1), INNER, "add_core", 3),
    ((3, 0), OUTER, "add_first", 1),
    ((3, 0), OUTER, "add_second", 0),
    ((3, 0), OUTER, "add_core", 2),
    ((3, 1), OUTER, "add_core", 3),
    ((4, 0), INNER, "add_first", 0),
    ((4, 0), INNER, "add_first", 1),
    ((4, 0), OUTER, "add_first", 2),
    ((4, 0), OUTER, "add_second", 1),
    ((4, 1), INNER, "add_first", 2),
    ((4, 1), INNER, "add_first", 3),
    ((4, 1), INNER, "add_second", 0),
    ((4, 1), INNER, "add_second", 1),
    ((4, 2), OUTER, "add_first", 3),
    ((4, 2), OUTER, "add_second", 2),
    ((4, 2), INNER, "add_second", 2),
    ((4, 2), INNER, "add_second", 3),
    ((4, 2), OUTER, "add_second", 3),
)


def chunk_of(step):
    return jnp.where(step == 0, 0, jnp.where(step == 1, 3, step - 1))


def feed_forward(sizes, planned, doc_len, attn, long_x, glob_x, dlong, dglob, lq, *weights):
    block, count, quarter, seq_count, pairs = sizes
    wo, bo, gain, shift, wi, bi, wr, br = weights
    width, hidden = wi.shape
    chunk = hidden // 4
    rows = block + quarter
    whole = pl.BlockSpec(memory_space=pltpu.VMEM)
    shape = jax.ShapeDtypeStruct
    in_specs = [pl.BlockSpec(memory_space=pltpu.SMEM)] + [whole] * 10
    in_specs += [
        pl.BlockSpec((width, chunk), lambda c: (0, chunk_of(c))),
        whole,
        pl.BlockSpec((chunk, width), lambda c: (chunk_of(c), 0)),
        whole,
    ]
    outs = [
        shape((block, width), BF16),
        shape((quarter, width), BF16),
        shape((rows, width), F32),
        shape((rows, width), BF16),
        shape((GP, width), BF16),
        shape((GP, PAIR), F32),
    ]
    there = pl.BlockSpec(memory_space=pl.ANY)
    out_specs = [whole] * 2 + [there] * 2 + [whole] * 2
    others = seq_count - 1
    scratch = [
        pltpu.VMEM((rows, width), F32),
        pltpu.VMEM((rows, width), F32),
        pltpu.VMEM((rows, width), F32),
        pltpu.VMEM((rows, width), BF16),
        pltpu.VMEM((width, rows), BF16),
        pltpu.VMEM((rows, width), BF16),
        pltpu.VMEM((8, width), F32),
        pltpu.VMEM((4, 1, chunk), F32),
        pltpu.VMEM((GP, width), BF16),
        pltpu.VMEM((GP, PAIR), F32),
        pltpu.SemaphoreType.DMA((2, others)),
        pltpu.SemaphoreType.DMA((2, others)),
        pltpu.VMEM((rows, width), F32),
        pltpu.VMEM((rows, width), BF16),
        pltpu.SemaphoreType.DMA((4,)),
    ]
    if planned:
        part, piece = hidden // 32, width // 32
        outs += [
            shape((2, 4, 2, 2, 3 * piece + 8, width), BF16),
            shape((4, part, width), BF16),
            shape((4, 2 * piece, width), BF16),
        ]
        out_specs += [there] + [whole] * 2
        scratch += [
            pltpu.VMEM((width, chunk), F32),
            pltpu.VMEM(outs[-3].shape, BF16),
        ]
        scratch += Reducer.scratch(part, width, 2) + Reducer.scratch(2 * piece, width, 2)
    else:
        outs += [
            shape((hidden, width), BF16),
            shape((width, hidden), BF16),
            shape((width, width), BF16),
            shape((8, width), F32),
        ]
        out_specs += [
            pl.BlockSpec((chunk, width), lambda c: (chunk_of(c), 0)),
            pl.BlockSpec((width, chunk), lambda c: (0, chunk_of(c))),
            whole,
            whole,
        ]
    return pl.pallas_call(
        functools.partial(ffn_kernel, sizes, planned),
        grid=(4,),
        in_specs=in_specs,
        out_specs=out_specs,
        out_shape=outs,
        scratch_shapes=scratch,
        compiler_params=pltpu.CompilerParams(
            collective_id=4, has_side_effects=True, vmem_limit_bytes=62 * 2**20
        ),
        name="feed_forward",
    )(doc_len, attn, long_x, glob_x, dlong, dglob, lq, wo, bo, gain, shift, wi, bi, wr, br)


def back_kernel(
    sizes,
    early_rows,
    len_ref,
    tab_ref,
    q_ref,
    kx_ref,
    vx_ref,
    kg_ref,
    vg_ref,
    o_ref,
    do_ref,
    l_ref,
    dog_ref,
    ldg_ref,
    yq_ref,
    *rest,
):
    block, count, quarter, seq_count, pairs = sizes
    reduces = early_rows > 0
    if reduces:
        pieces_ref, outer_parts, inner_parts, *rest = rest
    dq_ref, dk_ref, dv_ref, dtab_ref, glob_out, *rest = rest
    if reduces:
        early_parts, outer_ref, inner_ref, *rest = rest
    (
        dkx,
        dvx,
        dkg,
        dvg,
        q_send,
        q_recv,
        kv_send,
        kv_recv,
        halo_send,
        halo_recv,
        glob_sends,
        glob_recvs,
        halo_sends,
        halo_recvs,
        every,
        gather_sends,
        gather_recvs,
        *rest,
    ) = rest
    number = pl.program_id(0)
    pair = lax.rem(number, pairs)
    seq_index = lax.axis_index("seq")
    if reduces:
        reducer = Reducer(early_rows, 16, rest[:7], pieces=pieces_ref, parts=early_parts)
        z_sums = (
            (ZSum(outer_parts, rest[7:12]), outer_ref),
            (ZSum(inner_parts, rest[12:]), inner_ref),
        )
    scale = HD ** (-0.5)
    low_lanes = lane_index() < HD
    own_keys = slice(HALO, HALO + block)
    own_rows = pl.ds(pl.multiple_of(seq_index * quarter, quarter), quarter)

    def glob_copies(kind, at):
        source, dest = ((q_send, q_recv), (kv_send, kv_recv))[kind]
        for step in range(1, seq_count):
            device = seq_device(step, seq_count)
            yield pltpu.make_async_remote_copy(
                src_ref=source.at[device[1], at],
                dst_ref=dest.at[step - 1, at],
                send_sem=glob_sends.at[kind, step - 1, at],
                recv_sem=glob_recvs.at[kind, step - 1, at],
                device_id=device,
                device_id_type=pl.DeviceIdType.MESH,
            )

    def gathers():
        for step in range(1, seq_count):
            yield pltpu.make_async_remote_copy(
                src_ref=every.at[own_rows],
                dst_ref=every.at[own_rows],
                send_sem=gather_sends.at[step - 1],
                recv_sem=gather_recvs.at[step - 1],
                device_id=seq_device(step, seq_count),
                device_id_type=pl.DeviceIdType.MESH,
            )

    def halo_copy(direction, at):
        return pltpu.make_async_remote_copy(
            src_ref=halo_send.at[direction, at],
            dst_ref=halo_recv.at[direction, at],
            send_sem=halo_sends.at[direction, at],
            recv_sem=halo_recvs.at[direction, at],
            device_id=seq_device(2 * direction - 1, seq_count),
            device_id_type=pl.DeviceIdType.MESH,
        )

    has_low, has_high = seq_index > 0, seq_index < seq_count - 1
    sends_to = (has_low, has_high)
    gets_from = (has_high, has_low)

    def close_pair(at):
        lanes = lanes_of(at)
        for direction in range(2):

            @pl.when(gets_from[direction])
            def _(direction=direction):
                halo_copy(direction, at).wait_recv()

        for kind, (total, out) in enumerate(((dkx, dk_ref), (dvx, dv_ref))):
            first, last = HALO + REACH, HALO + block - REACH
            out[:REACH, lanes] = (
                total[at, HALO:first] + halo_recv[1, at, kind].astype(F32)
            ).astype(BF16)
            out[REACH : block - REACH, lanes] = total[at, first:last].astype(BF16)
            out[block - REACH : block, lanes] = (
                total[at, last : HALO + block] + halo_recv[0, at, kind].astype(F32)
            ).astype(BF16)
        sums = []
        for kind, (source, dest) in enumerate(((q_send, q_recv), (kv_send, kv_recv))):
            total = source[seq_index, at].astype(F32)
            for step, copy in enumerate(glob_copies(kind, at)):
                copy.wait_recv()
                total += dest[step, at].astype(F32)
            sums.append(total.astype(BF16))
        dq_ref[block:, lanes] = sums[0]
        dk_ref[block:, lanes] = sums[1][:, :PAIR]
        dv_ref[block:, lanes] = sums[1][:, PAIR:]

    def run_plan(now):
        for at, act, chunk in EARLY_PLAN:
            if now == at:
                getattr(reducer, act)(chunk)

    @pl.when(number == 0)
    def _():
        others = [seq_device(step, seq_count) for step in range(1, seq_count)]
        meet(others + (reducer.partners()[2:] if reduces else []))
        if reduces:
            for chunk in range(4):
                reducer.start(chunk)
            for z_sum, _ in z_sums:
                z_sum.start()
        every[own_rows] = yq_ref[...]
        for copy in gathers():
            copy.start()
        for direction in range(2):

            @pl.when(jnp.logical_not(gets_from[direction]))
            def _(direction=direction):
                halo_recv[direction] = jnp.zeros_like(halo_recv[direction])

    if reduces:
        for now in range(1, 2 * pairs):
            if any(at == now for at, _, _ in EARLY_PLAN):

                @pl.when(number == now)
                def _(now=now):
                    run_plan(now)

    @pl.when(number < pairs)
    def _():
        long_bias = key_bias(seq_index * block, block, len_ref[0])
        near_bias = key_bias(seq_index * quarter, quarter, count)
        query = q_ref[block:] * jnp.asarray(scale, BF16)
        grad_o = dog_ref[...]
        far_k, far_v = kx_ref[own_keys], vx_ref[own_keys]
        near_k, near_v = kg_ref[own_rows], vg_ref[own_rows]
        outs, kept = [], []
        for head in range(2):
            norm = in_three(-pick_column(ldg_ref[...], 2 * pair + head))
            delta = in_three(-pick_column(ldg_ref[...], HD + 2 * pair + head))
            qa = with_lanes(head, query, (1.0,) + norm)
            doa = with_lanes(head, grad_o, delta)
            far = jnp.exp(dot_t(qa, key_side(head, far_k, long_bias)))
            near = jnp.exp(dot_t(qa, key_side(head, near_k, near_bias)))
            far_ds = (far * dot_t(doa, value_side(head, far_v))).astype(BF16)
            near_ds = (near * dot_t(doa, value_side(head, near_v))).astype(BF16)
            outs.append(dot_n(far_ds, far_k) + dot_n(near_ds, near_k))
            kept.append(
                (
                    own_half(head, query),
                    own_half(head, grad_o),
                    far.astype(BF16),
                    near.astype(BF16),
                    far_ds,
                    near_ds,
                )
            )
        own_q, own_do, far, near, far_ds, near_ds = (
            jnp.concatenate(part, 0) for part in zip(*kept)
        )
        for total, edge in ((dkx, own_keys), (dvx, own_keys)):
            total[pair, :HALO] = jnp.zeros((HALO, PAIR), F32)
            total[pair, HALO + block :] = jnp.zeros((HALO, PAIR), F32)
        dkx[pair, own_keys] = t_dot(far_ds, own_q)
        dvx[pair, own_keys] = t_dot(far, own_do)
        dkg[pair] = jnp.zeros((GP, PAIR), F32)
        dvg[pair] = jnp.zeros((GP, PAIR), F32)
        dkg[pair, own_rows] = t_dot(near_ds, own_q)
        dvg[pair, own_rows] = t_dot(near, own_do)
        glob_dq = (jnp.where(low_lanes, outs[0], outs[1]) * scale).astype(BF16)
        q_send[:, pair] = glob_dq.reshape(seq_count, quarter, PAIR)
        for copy in glob_copies(0, pair):
            copy.start()

    @pl.when(number >= pairs)
    def _():
        long_bias = key_bias(seq_index * block - HALO, block + 2 * HALO, len_ref[0])
        glob_bias = key_bias(0, GP, count)
        query = q_ref[:block] * jnp.asarray(scale, BF16)
        grad_o = do_ref[...]
        both = grad_o.astype(F32) * o_ref[...].astype(F32)
        heads = []
        for head in range(2):
            norm = in_three(-pick_column(l_ref[...], 2 * pair + head))
            delta = in_three(-jnp.sum(own_half(head, both), -1, keepdims=True))
            heads.append(
                dict(
                    q=own_half(head, query),
                    do=own_half(head, grad_o),
                    qa=with_lanes(head, query, (1.0,) + norm),
                    doa=with_lanes(head, grad_o, delta),
                    kxa=key_side(head, kx_ref[...], long_bias),
                    vxa=value_side(head, vx_ref[...]),
                    kga=key_side(head, kg_ref[...], glob_bias),
                    vga=value_side(head, vg_ref[...]),
                    bias=band_bias(tab_ref[0, head : head + 1]),
                )
            )
        table_sums = [0.0, 0.0]
        grads_q = []
        for start in range(0, block, SUB):
            rows, keys = slice(start, start + SUB), slice(start, start + WINDOW)
            outs, probs, grads = [], [], []
            for head, own in enumerate(heads):
                band = jnp.exp(dot_t(own["qa"][rows], own["kxa"][keys]) + own["bias"])
                band_ds = band * dot_t(own["doa"][rows], own["vxa"][keys])
                table_sums[head] += band_ds
                glob = jnp.exp(dot_t(own["qa"][rows], own["kga"]))
                glob_ds = (glob * dot_t(own["doa"][rows], own["vga"])).astype(BF16)
                band_ds = band_ds.astype(BF16)
                outs.append(dot_n(band_ds, kx_ref[keys]) + dot_n(glob_ds, kg_ref[...]))
                probs.append((band.astype(BF16), glob.astype(BF16)))
                grads.append((band_ds, glob_ds))
            grads_q.append(jnp.where(low_lanes, outs[0], outs[1]))
            own_q = jnp.concatenate([own["q"][rows] for own in heads], 0)
            own_do = jnp.concatenate([own["do"][rows] for own in heads], 0)
            band, glob = (jnp.concatenate(part, 0) for part in zip(*probs))
            band_ds, glob_ds = (jnp.concatenate(part, 0) for part in zip(*grads))
            dkx[pair, keys] += t_dot(band_ds, own_q)
            dvx[pair, keys] += t_dot(band, own_do)
            dkg[pair] += t_dot(glob_ds, own_q)
            dvg[pair] += t_dot(glob, own_do)
        for kind, total in enumerate((dkg, dvg)):
            kv_send[:, pair, :, kind * PAIR : (kind + 1) * PAIR] = (
                total[pair].astype(BF16).reshape(seq_count, quarter, PAIR)
            )
        for copy in glob_copies(1, pair):
            copy.start()
        for kind, total in enumerate((dkx, dvx)):
            for direction, first in enumerate((HALO - REACH, HALO + block)):
                halo_send[direction, pair, kind] = total[pair, first : first + REACH].astype(BF16)
        for direction in range(2):

            @pl.when(sends_to[direction])
            def _(direction=direction):
                halo_copy(direction, pair).start()

        dq_ref[:block, lanes_of(pair)] = (jnp.concatenate(grads_q, 0) * scale).astype(BF16)
        for head in range(2):
            dtab_ref[pair, head : head + 1] = diagonal_sums(table_sums[head])

    @pl.when(number > pairs)
    def _():
        close_pair(pair - 1)

    @pl.when(number == 2 * pairs - 1)
    def _():
        if reduces:
            run_plan(2 * pairs)
        close_pair(pairs - 1)
        for at in range(pairs):
            for kind in range(2):
                for copy in glob_copies(kind, at):
                    copy.wait_send()
            for direction in range(2):

                @pl.when(sends_to[direction])
                def _(direction=direction, at=at):
                    halo_copy(direction, at).wait_send()

        for copy in gathers():
            copy.wait_recv()
        glob_out[...] = every[:count]
        for copy in gathers():
            copy.wait_send()
        if reduces:
            reducer.finish()
            for z_sum, out in z_sums:
                z_sum.finish(out)


def attend_back(sizes, doc_len, table, q, kx, vx, kg, vg, o, do, l, dog, ldg, yq, *sums):
    block, count, quarter, seq_count, pairs = sizes
    width = q.shape[1]
    early_rows = sums[0].shape[-2] if sums else 0
    ext = block + 2 * HALO
    cols = lambda rows: pl.BlockSpec((rows, PAIR), lambda i: (0, lax.rem(i, pairs)))
    whole = pl.BlockSpec(memory_space=pltpu.VMEM)
    shape = jax.ShapeDtypeStruct
    in_specs = [
        pl.BlockSpec(memory_space=pltpu.SMEM),
        pl.BlockSpec((1, 2, WINDOW), lambda i: (lax.rem(i, pairs), 0, 0)),
        cols(block + GP),
        cols(ext),
        cols(ext),
        cols(GP),
        cols(GP),
        cols(block),
        cols(block),
        whole,
        cols(GP),
        whole,
        whole,
    ]
    rows = block + quarter
    outs = [shape((rows, width), BF16)] * 3 + [shape((pairs, 2, WINDOW), F32)]
    outs.append(shape((count, width), BF16))
    others = seq_count - 1
    scratch = [
        pltpu.VMEM((pairs, ext, PAIR), F32),
        pltpu.VMEM((pairs, ext, PAIR), F32),
        pltpu.VMEM((pairs, GP, PAIR), F32),
        pltpu.VMEM((pairs, GP, PAIR), F32),
        pltpu.VMEM((seq_count, pairs, quarter, PAIR), BF16),
        pltpu.VMEM((others, pairs, quarter, PAIR), BF16),
        pltpu.VMEM((seq_count, pairs, quarter, 2 * PAIR), BF16),
        pltpu.VMEM((others, pairs, quarter, 2 * PAIR), BF16),
        pltpu.VMEM((2, pairs, 2, REACH, PAIR), BF16),
        pltpu.VMEM((2, pairs, 2, REACH, PAIR), BF16),
        pltpu.SemaphoreType.DMA((2, others, pairs)),
        pltpu.SemaphoreType.DMA((2, others, pairs)),
        pltpu.SemaphoreType.DMA((2, pairs)),
        pltpu.SemaphoreType.DMA((2, pairs)),
        pltpu.VMEM((GP, width), BF16),
        pltpu.SemaphoreType.DMA((others,)),
        pltpu.SemaphoreType.DMA((others,)),
    ]
    args = [doc_len, table, q, kx, vx, kg, vg, o, do, l, dog, ldg, yq, *sums]
    if early_rows:
        in_specs += [pl.BlockSpec(memory_space=pl.ANY)] * 3
        outs.append(shape((4, early_rows, width), BF16))
        scratch += Reducer.scratch(early_rows, width, 1)
        for parts in sums[1:]:
            outs.append(shape(parts.shape[1:], F32))
            scratch += ZSum.scratch(*parts.shape[1:])
    return pl.pallas_call(
        functools.partial(back_kernel, sizes, early_rows),
        grid=(2 * pairs,),
        in_specs=in_specs,
        out_specs=[whole] * len(outs),
        out_shape=outs,
        scratch_shapes=scratch,
        compiler_params=pltpu.CompilerParams(
            collective_id=1, has_side_effects=True, vmem_limit_bytes=60 * 2**20
        ),
        name="attend_back",
    )(*args)


def on_device(
    long_input,
    global_input,
    lengths,
    w_query,
    b_query,
    w_key,
    w_value,
    b_value,
    w_out,
    b_out,
    w_inner,
    b_inner,
    w_outer,
    b_outer,
    norm1_gain,
    norm1_shift,
    norm2_gain,
    norm2_shift,
    rel_table,
    long_cotangent,
    global_cotangent,
):
    seq_count = lax.axis_size("seq")
    data_count = lax.axis_size("dp")
    seq_index = lax.axis_index("seq")
    block = long_input.shape[1]
    count = global_input.shape[1]
    width = long_input.shape[2]
    heads = rel_table.shape[1]
    pairs = heads // 2
    labels = 2 * R + 1
    quarter = GP // seq_count
    sizes = Sizes(block, count, quarter, seq_count, pairs)
    queries, kx, vx, kg, vg, attn_low, long_l, glob_l, glob_x, table = attend(
        sizes,
        lengths,
        rel_table.T,
        long_input[0],
        global_input[0],
        w_query,
        w_key,
        w_value,
        b_query,
        b_value,
        norm1_gain,
        norm1_shift,
    )
    planned = has_plan()
    long_result, own_out, grad_mid, grad_attn, every_do, every_ld, *gradients = feed_forward(
        sizes,
        planned,
        lengths,
        attn_low,
        long_input[0],
        glob_x,
        long_cotangent[0],
        global_cotangent[0],
        glob_l,
        w_out,
        b_out,
        norm2_gain,
        norm2_shift,
        w_inner,
        b_inner,
        w_outer,
        b_outer,
    )
    query_low, key_low, value_low, dtab, glob_out, *early = attend_back(
        sizes,
        lengths,
        table,
        queries,
        kx,
        vx,
        kg,
        vg,
        attn_low,
        grad_attn,
        long_l,
        every_do,
        every_ld,
        own_out,
        *(gradients if planned else []),
    )
    long_grad, glob_grad, *late = last_part(
        sizes,
        planned,
        long_input[0],
        glob_x,
        query_low,
        key_low,
        value_low,
        grad_mid,
        w_query,
        w_key,
        w_value,
        norm1_gain,
        norm1_shift,
        dtab,
        *early[:1],
    )
    if planned:
        (
            g_query,
            g_key,
            g_value,
            g_out,
            g_inner,
            g_outer,
            g_b_query,
            g_b_value,
            g_b_out,
            g_b_outer,
            g_g1,
            g_s1,
            g_g2,
            g_s2,
            g_b_inner,
            table_total,
            long_grad,
            long_result,
            glob_out,
            glob_grad,
        ) = small_results(
            heads,
            late[3],
            late[0],
            early[1],
            early[2],
            late[1],
            late[2],
            long_grad,
            long_result,
            glob_out,
            glob_grad,
        )
        table_total = table_total.T
        glob_grad = glob_grad.reshape(count, width)
    else:
        devices = data_count * seq_count
        own_part = lambda vector: lax.dynamic_slice_in_dim(
            vector,
            (lax.axis_index("dp") * seq_count + seq_index) * (vector.shape[0] // devices),
            vector.shape[0] // devices,
        )
        g_outer, g_inner, g_out, vectors = gradients
        g_outer, g_inner, g_out, g_query, g_key, g_value = (
            lax.psum_scatter(g.astype(BF16), ("dp", "seq"), scatter_dimension=0, tiled=True).astype(
                F32
            )
            for g in (g_outer, g_inner, g_out, *late[:3])
        )
        vectors, sums, scales = lax.psum((vectors, *late[3:]), ("dp", "seq"))
        g_b_query, g_b_value = (own_part(sums[heads + i]) for i in range(2))
        g_g1, g_s1 = (own_part(scales[i]) for i in range(2))
        g_b_out, g_b_outer, g_g2, g_s2 = (own_part(vectors[i]) for i in range(4))
        g_b_inner = own_part(vectors[4:].reshape(-1))
        table_total = sums[:heads, HALO - R : HALO - R + labels].T
    return (
        long_result[None],
        glob_out[None],
        long_grad[None],
        glob_grad[None],
        g_query,
        g_b_query,
        g_key,
        g_value,
        g_b_value,
        g_out,
        g_b_out,
        g_inner,
        g_b_inner,
        g_outer,
        g_b_outer,
        g_g1,
        g_s1,
        g_g2,
        g_s2,
        table_total,
    )


def solution(mesh):
    rows, whole = P("dp", "seq", None), P("dp", None, None)
    matrix, vector = P(("dp", "seq"), None), P(("dp", "seq"))
    return jax.shard_map(
        on_device,
        mesh=mesh,
        in_specs=(rows, whole, P("dp")) + (P(),) * 16 + (rows, whole),
        out_specs=(
            rows,
            whole,
            rows,
            whole,
            matrix,
            vector,
            matrix,
            matrix,
            vector,
            matrix,
            vector,
            matrix,
            vector,
            matrix,
            vector,
            vector,
            vector,
            vector,
            vector,
            P(),
        ),
        check_vma=False,
    )
```
